32 devices in a mesh: dp: 2 (over x), blk: 4 (over z), uly: 4 (over y, core).
Axes of the slice: x: 2, y: 2, z: 4, core: 2. Of those that a mesh axis runs over, the one named last changes fastest.
Arguments:
- hidden: bfloat16 [4, 1024, 2048], P('dp', ('blk', 'uly')), may hold values from -6 to 6
- span_order: int32 [8], replicated, may hold values from 0 to 7, each once
- attn_gain: bfloat16 [2048], P(('dp', 'blk', 'uly')), may hold values from 0.5 to 1.5
- w_query: bfloat16 [2048, 2048], P(('dp', 'blk', 'uly')), may hold values from -0.125 to 0.125
- key_weight: bfloat16 [2048, 1024], P(('dp', 'blk', 'uly')), may hold values from -0.125 to 0.125
- value_weight: bfloat16 [2048, 1024], P(('dp', 'blk', 'uly')), may hold values from -0.125 to 0.125
- w_out: bfloat16 [2048, 2048], P(('dp', 'blk', 'uly')), may hold values from -0.75 to 0.75
- q_gain: bfloat16 [128], replicated, may hold values from 0.5 to 1.5
- k_gain: bfloat16 [128], replicated, may hold values from 0.5 to 1.5
- mlp_gain: bfloat16 [2048], P(('dp', 'blk', 'uly')), may hold values from 0.5 to 1.5
- w_gate: bfloat16 [2048, 6144], P(('dp', 'blk', 'uly')), may hold values from -0.125 to 0.125
- w_up: bfloat16 [2048, 6144], P(('dp', 'blk', 'uly')), may hold values from -0.125 to 0.125
- w_down: bfloat16 [6144, 2048], P(('dp', 'blk', 'uly')), may hold values from -0.078125 to 0.078125
- cotangent: bfloat16 [4, 1024, 2048], P('dp', ('blk', 'uly')), may hold values from -6 to 6
Outputs:
- output: bfloat16 [4, 1024, 2048], P('dp', ('blk', 'uly'))
- grad_hidden: float32 [4, 1024, 2048], P('dp', ('blk', 'uly'))
- grad_attn_gain: float32 [2048], P(('dp', 'blk', 'uly'))
- grad_query: float32 [2048, 2048], P(('dp', 'blk', 'uly'))
- grad_key: float32 [2048, 1024], P(('dp', 'blk', 'uly'))
- grad_value: float32 [2048, 1024], P(('dp', 'blk', 'uly'))
- grad_out: float32 [2048, 2048], P(('dp', 'blk', 'uly'))
- grad_q_gain: float32 [128], replicated
- grad_k_gain: float32 [128], replicated
- grad_mlp_gain: float32 [2048], P(('dp', 'blk', 'uly'))
- grad_gate: float32 [2048, 6144], P(('dp', 'blk', 'uly'))
- grad_up: float32 [2048, 6144], P(('dp', 'blk', 'uly'))
- grad_down: float32 [6144, 2048], P(('dp', 'blk', 'uly'))
The draws below stay inside these ranges and needn't reach their ends.
Inputs may be any that keep to these rules, and one draw needn't show every extreme that they name: `span_order`: every half-block index appears exactly once.
All inputs are finite; a program needn't handle non-finite values.
Results may differ from the reference program's by a relative error of at most 0.02.
Values may be sent and summed in bfloat16 or wider, within the bound.
A program may use at most 384 MiB of HBM per device.

```python
import math
import jax
import jax.numpy as jnp
from jax import lax

MODEL_WIDTH = 2048
QUERY_HEADS = 16
KEY_VALUE_HEADS = 8
HEAD_SIZE = 128
FF = 6144
SEQUENCE_LENGTH = 1024
HALF = 128
BATCH_TOTAL = 4
N_BLK = 4


def levels(key, shape, shards, low, largest):
    loudness = 1.0
    for axis_at, parts in shards:
        draws = jax.random.uniform(jax.random.fold_in(jax.random.fold_in(key, 6), axis_at), (parts,), jnp.float32, low / len(shards), largest / len(shards))
        loudness = loudness * jnp.repeat(jnp.exp(draws), shape[axis_at] // parts).reshape((-1,) + (1,) * (len(shape) - 1 - axis_at))
    return loudness


def scatter_about(key, extent, width, bound, shards=(), kind=jnp.bfloat16):
    entries = jax.random.normal(key, extent, jnp.float32) * width
    if len(shards) > 0:
        entries = levels(key, extent, shards, -0.22, 0.18) * entries
    return jnp.clip(entries, min=-bound, max=bound).astype(kind)


def setup_inputs(seed: int = 0) -> dict:
    seeds = jax.random.split(jax.random.key(seed), 15)
    hidden = scatter_about(seeds[0], (BATCH_TOTAL, SEQUENCE_LENGTH, MODEL_WIDTH), 1.0, 6.0, ((0, 2), (1, 16)))
    span_order = jax.random.permutation(seeds[1], 2 * N_BLK).astype(jnp.int32)
    attn_gain = jnp.clip(1.0 + 0.1 * jax.random.normal(seeds[2], (MODEL_WIDTH,), jnp.float32), 0.5, 1.5).astype(jnp.bfloat16)
    w_query = scatter_about(seeds[3], (MODEL_WIDTH, QUERY_HEADS * HEAD_SIZE), MODEL_WIDTH ** -0.5, 0.125, ((0, 32),))
    key_weight = scatter_about(seeds[4], (MODEL_WIDTH, KEY_VALUE_HEADS * HEAD_SIZE), MODEL_WIDTH ** -0.5, 0.125, ((0, 32),))
    value_weight = scatter_about(seeds[5], (MODEL_WIDTH, KEY_VALUE_HEADS * HEAD_SIZE), MODEL_WIDTH ** -0.5, 0.125, ((0, 32),))
    w_out = scatter_about(seeds[6], (QUERY_HEADS * HEAD_SIZE, MODEL_WIDTH), 64 ** -0.5, 0.75, ((0, 32),))
    q_gain = jnp.clip(1.0 + 0.1 * jax.random.normal(seeds[7], (HEAD_SIZE,), jnp.float32), 0.5, 1.5).astype(jnp.bfloat16)
    k_gain = jnp.clip(1.0 + 0.1 * jax.random.normal(seeds[8], (HEAD_SIZE,), jnp.float32), 0.5, 1.5).astype(jnp.bfloat16)
    mlp_gain = jnp.clip(1.0 + 0.1 * jax.random.normal(seeds[9], (MODEL_WIDTH,), jnp.float32), 0.5, 1.5).astype(jnp.bfloat16)
    w_gate = scatter_about(seeds[10], (MODEL_WIDTH, FF), MODEL_WIDTH ** -0.5, 0.125, ((0, 32),))
    w_up = scatter_about(seeds[11], (MODEL_WIDTH, FF), MODEL_WIDTH ** -0.5, 0.125, ((0, 32),))
    w_down = scatter_about(seeds[12], (FF, MODEL_WIDTH), FF ** -0.5, 0.078125, ((0, 32),))
    cotangent = scatter_about(seeds[13], (BATCH_TOTAL, SEQUENCE_LENGTH, MODEL_WIDTH), 1.0, 6.0, ((0, 2), (1, 16)))
    return dict(hidden=hidden, span_order=span_order, attn_gain=attn_gain, w_query=w_query, key_weight=key_weight, value_weight=value_weight, w_out=w_out, q_gain=q_gain, k_gain=k_gain, mlp_gain=mlp_gain, w_gate=w_gate, w_up=w_up, w_down=w_down, cotangent=cotangent)


EPSILON = 1e-06
ROPE_BASE = 1000000.0
BEST_PRECISION = lax.Precision.HIGHEST

@jax.custom_vjp
def low(v):
    return lax.optimization_barrier(v.astype(jnp.bfloat16)).astype(jnp.float32)

@jax.custom_vjp
def lower_backward(v):
    return v

def low_keep(v):
    return (low(v), None)

def low_pass(kept, grad):
    return (grad,)

def back_keep(v):
    return (v, None)

def back_low(kept, grad):
    return (low(grad),)
low.defvjp(low_keep, low_pass)
lower_backward.defvjp(back_keep, back_low)

def rms_scale(source):
    return lax.rsqrt(lax.optimization_barrier(jnp.mean(source * source, axis=-1, keepdims=True)) + EPSILON)

def angles_of(positions, head_dim):
    freq_steps = jnp.arange(head_dim // 2, dtype=jnp.float32)
    inverse = jnp.exp(freq_steps * (-2.0 * math.log(ROPE_BASE) / head_dim))
    return positions.astype(jnp.float32)[:, None] * inverse[None, :]

def rotate(source, angles):
    half_dim = source.shape[-1] // 2
    cosine = jnp.cos(angles)[:, None, :]
    sine_part = jnp.sin(angles)[:, None, :]
    first_half = source[..., :half_dim]
    second_half = source[..., half_dim:]
    return jnp.concatenate([first_half * cosine - second_half * sine_part, second_half * cosine + first_half * sine_part], axis=-1)

def attend_block(query_block, query_pos, key_rows, value_rows, key_pos):
    scale_factor = 1.0 / math.sqrt(HEAD_SIZE)
    scores = jnp.einsum('qkgd,nkd->kgqn', query_block, key_rows, precision=BEST_PRECISION) * scale_factor
    scores = lower_backward(scores)
    allowed = query_pos[:, None] >= key_pos[None, :]
    scores = jnp.where(allowed, scores, -jnp.inf)
    row_top = lax.optimization_barrier(jnp.max(scores, axis=-1, keepdims=True))
    log_total = jnp.log(lax.optimization_barrier(jnp.sum(jnp.exp(scores - row_top), axis=-1, keepdims=True))) + row_top
    weights = low(jnp.exp(scores - log_total))
    return jnp.einsum('kgqn,nkd->qkgd', weights, value_rows, precision=BEST_PRECISION)

def reference(hidden, span_order, attn_gain, w_query, key_weight, value_weight, w_out, q_gain, k_gain, mlp_gain, w_gate, w_up, w_down, cotangent):
    query_group_width = QUERY_HEADS // KEY_VALUE_HEADS
    places = jnp.arange(SEQUENCE_LENGTH, dtype=jnp.int32)
    positions = (span_order[places // HALF] * HALF + places % HALF).astype(jnp.int32)
    angles = angles_of(positions, HEAD_SIZE)
    rows_per_block = math.gcd(SEQUENCE_LENGTH, 512)
    count_of_blocks = SEQUENCE_LENGTH // rows_per_block
    checked = jax.checkpoint(attend_block)
    position_blocks = positions.reshape(count_of_blocks, rows_per_block)

    def attend_full_sequence(members):
        query_sequence, key_seq, value_seq = members

        def single_block(block_members):
            return checked(block_members[0], block_members[1], key_seq, value_seq, positions)
        block_outputs = lax.map(single_block, (query_sequence.reshape(count_of_blocks, rows_per_block, KEY_VALUE_HEADS, query_group_width, HEAD_SIZE), position_blocks))
        return block_outputs.reshape(SEQUENCE_LENGTH, QUERY_HEADS, HEAD_SIZE)

    def forward(source, g_attn, wq_full, key_weight_complete, value_weight_complete, wo_full, gain_q, gain_k, g_mlp, wg_full, wu_full, wd_full):
        normalized_input = low(source * rms_scale(source) * g_attn)
        q_pre = lower_backward(jnp.einsum('nwu,uq->nwq', normalized_input, wq_full, precision=BEST_PRECISION)).reshape(BATCH_TOTAL, SEQUENCE_LENGTH, QUERY_HEADS, HEAD_SIZE)
        key_before_norm = lower_backward(jnp.einsum('nwu,uq->nwq', normalized_input, key_weight_complete, precision=BEST_PRECISION)).reshape(BATCH_TOTAL, SEQUENCE_LENGTH, KEY_VALUE_HEADS, HEAD_SIZE)
        value_before_norm = lower_backward(jnp.einsum('nwu,uq->nwq', normalized_input, value_weight_complete, precision=BEST_PRECISION)).reshape(BATCH_TOTAL, SEQUENCE_LENGTH, KEY_VALUE_HEADS, HEAD_SIZE)
        query_rows = low(rotate(q_pre * rms_scale(q_pre) * gain_q, angles))
        gathered_keys = low(rotate(key_before_norm * rms_scale(key_before_norm) * gain_k, angles))
        gathered_values = low(value_before_norm)
        attention_output = lax.map(attend_full_sequence, (query_rows.reshape(BATCH_TOTAL, SEQUENCE_LENGTH, KEY_VALUE_HEADS, query_group_width, HEAD_SIZE), gathered_keys, gathered_values))
        heads = lower_backward(low(attention_output)).reshape(BATCH_TOTAL, SEQUENCE_LENGTH, QUERY_HEADS * HEAD_SIZE)
        branch = lower_backward(jnp.einsum('ble,ed->bld', heads, wo_full, precision=BEST_PRECISION))
        middle = source + branch
        normed2 = low(middle * rms_scale(middle) * g_mlp)
        gate_pre = lower_backward(jnp.einsum('bld,df->blf', normed2, wg_full, precision=BEST_PRECISION))
        up_pre = lower_backward(jnp.einsum('bld,df->blf', normed2, wu_full, precision=BEST_PRECISION))
        activated = low(jax.nn.silu(gate_pre) * up_pre)
        return middle + jnp.einsum('blf,fd->bld', activated, wd_full, precision=BEST_PRECISION)
    params = tuple((item.astype(jnp.float32) for item in (hidden, attn_gain, w_query, key_weight, value_weight, w_out, q_gain, k_gain, mlp_gain, w_gate, w_up, w_down)))
    result, pullback = jax.vjp(forward, *params)
    grads = pullback(cotangent.astype(jnp.float32))
    return (result.astype(jnp.bfloat16), grads[0], grads[1], grads[2], grads[3], grads[4], grads[5], grads[6], grads[7], grads[8], grads[9], grads[10], grads[11])
```

```python
import math

import jax
import jax.numpy as jnp
from jax import lax
from jax.sharding import PartitionSpec as P

QUERY_HEADS = 16
KEY_VALUE_HEADS = 8
HEAD_SIZE = 128


DP, BLK, ULY = "dp", "blk", "uly"
EVERY = (DP, BLK, ULY)
PLANE = (DP, ULY)
TOKENS = P(DP, (BLK, ULY), None)
EQ_KGQD_NKD_TO_KGQN = "kgqd,nkd->kgqn"
EQ_KGQN_KGQD_TO_NKD = "kgqn,kgqd->nkd"
EQ_KGQN_NKD_TO_KGQD = "kgqn,nkd->kgqd"
EQ_KGQN_QKGD_TO_NKD = "kgqn,qkgd->nkd"
EQ_QKGD_NKD_TO_KGQN = "qkgd,nkd->kgqn"
EQ_SKGQD_SKND_TO_SKGQN = "skgqd,sknd->skgqn"
EQ_SKGQN_SKGQD_TO_SKND = "skgqn,skgqd->sknd"
EQ_SKGQN_SKND_TO_SKGQD = "skgqn,sknd->skgqd"
EQ_STD_DE_TO_STE = "std,de->ste"
EQ_STD_DF_TO_STF = "std,df->stf"
EQ_STD_ED_TO_STE = "std,ed->ste"
EQ_STD_FD_TO_STF = "std,fd->stf"
EQ_STD_STE_TO_DE = "std,ste->de"
EQ_STD_STF_TO_DF = "std,stf->df"
EQ_STE_DE_TO_STD = "ste,de->std"
EQ_STE_ED_TO_STD = "ste,ed->std"
EQ_STE_STD_TO_ED = "ste,std->ed"
EQ_STF_DF_TO_STD = "stf,df->std"
EQ_STF_FD_TO_STD = "stf,fd->std"
EQ_STF_STD_TO_FD = "stf,std->fd"
EQ_TD_ED_TO_TE = "td,ed->te"
EQ_TD_FD_TO_TF = "td,fd->tf"
EQ_TD_TE_TO_DE = "td,te->de"
EQ_TD_TF_TO_DF = "td,tf->df"
EQ_TE_DE_TO_TD = "te,de->td"
EQ_TE_TD_TO_ED = "te,td->ed"
EQ_TF_DF_TO_TD = "tf,df->td"
EQ_TF_TD_TO_FD = "tf,td->fd"

EPSILON = 1e-06
ROPE_BASE = 1000000.0


def rms_scale(source):
    return lax.rsqrt(jnp.mean(source * source, axis=-1, keepdims=True) + EPSILON)


def norm_back(grad_normed, source, norm_scale, gain):
    unit_rows = source * norm_scale
    scaled = grad_normed * gain
    return norm_scale * (scaled - unit_rows * jnp.mean(scaled * unit_rows, axis=-1, keepdims=True))


def angles_of(positions, head_dim):
    freq_steps = jnp.arange(head_dim // 2, dtype=jnp.float32)
    inverse = jnp.exp(freq_steps * (-2.0 * math.log(ROPE_BASE) / head_dim))
    return positions.astype(jnp.float32)[:, None] * inverse[None, :]


def rotate(source, angles, direction):
    half_dim = source.shape[-1] // 2
    cosine = jnp.cos(angles)[:, None, :]
    sine_part = direction * jnp.sin(angles)[:, None, :]
    first_half = source[..., :half_dim]
    second_half = source[..., half_dim:]
    return jnp.concatenate(
        [
            first_half * cosine - second_half * sine_part,
            second_half * cosine + first_half * sine_part,
        ],
        axis=-1,
    )


def positions_of(places, span_order, half_len):
    blocks_of = places // half_len
    block_ids = jnp.arange(span_order.shape[0], dtype=jnp.int32)
    chosen = jnp.sum(
        jnp.where(blocks_of[:, None] == block_ids[None, :], span_order[None, :], 0), axis=1
    )
    return chosen * half_len + places % half_len


def add_rows(buffer, new_rows):
    return buffer + new_rows


def shards_general(
    hidden,
    span_order,
    attn_gain,
    w_query,
    key_weight,
    value_weight,
    w_out,
    q_gain,
    k_gain,
    mlp_gain,
    w_gate,
    w_up,
    w_down,
    cotangent,
):
    sequence_count = hidden.shape[0]
    token_count = hidden.shape[1]
    ulysses_group_size = lax.axis_size(ULY)
    local_q = QUERY_HEADS // ulysses_group_size
    local_key_value = KEY_VALUE_HEADS // ulysses_group_size
    query_group_width = QUERY_HEADS // KEY_VALUE_HEADS
    block_len = token_count * ulysses_group_size
    half_len = block_len // 2
    score_scale = 1.0 / math.sqrt(HEAD_SIZE)
    blk_index = lax.axis_index(BLK)
    uly_index = lax.axis_index(ULY)
    first_place = (blk_index * ulysses_group_size + uly_index) * token_count
    local_angles = angles_of(
        positions_of(first_place + jnp.arange(token_count, dtype=jnp.int32), span_order, half_len),
        HEAD_SIZE,
    )
    query_pos = positions_of(
        blk_index * block_len + jnp.arange(block_len, dtype=jnp.int32), span_order, half_len
    )
    g_attn, wq_all, wk_all, wv_all, wo_all = (
        lax.all_gather(attn_gain, EVERY, axis=0, tiled=True),
        lax.all_gather(w_query, EVERY, axis=0, tiled=True),
        lax.all_gather(key_weight, EVERY, axis=0, tiled=True),
        lax.all_gather(value_weight, EVERY, axis=0, tiled=True),
        lax.all_gather(w_out, EVERY, axis=0, tiled=True),
    )
    source = hidden.astype(jnp.float32)
    first_scale = rms_scale(source)
    normalized_input = (source * first_scale * g_attn.astype(jnp.float32)).astype(jnp.bfloat16)
    q_pre = jnp.einsum(
        EQ_STD_DE_TO_STE, normalized_input, wq_all, preferred_element_type=jnp.float32
    ).reshape(sequence_count, token_count, QUERY_HEADS, HEAD_SIZE)
    key_before_norm = jnp.einsum(
        EQ_STD_DE_TO_STE, normalized_input, wk_all, preferred_element_type=jnp.float32
    ).reshape(sequence_count, token_count, KEY_VALUE_HEADS, HEAD_SIZE)
    value_before_norm = jnp.einsum(
        EQ_STD_DE_TO_STE, normalized_input, wv_all, preferred_element_type=jnp.float32
    ).reshape(sequence_count, token_count, KEY_VALUE_HEADS, HEAD_SIZE)
    q_scale = rms_scale(q_pre)
    k_scale = rms_scale(key_before_norm)
    gain_q = q_gain.astype(jnp.float32)
    gain_k = k_gain.astype(jnp.float32)
    q_rot = rotate(q_pre * q_scale * gain_q, local_angles, 1.0).astype(jnp.bfloat16)
    k_rot = rotate(key_before_norm * k_scale * gain_k, local_angles, 1.0).astype(jnp.bfloat16)
    v_low = value_before_norm.astype(jnp.bfloat16)
    q_heads, k_heads, v_heads = (
        lax.all_to_all(q_rot, ULY, split_axis=2, concat_axis=1, tiled=True),
        lax.all_to_all(k_rot, ULY, split_axis=2, concat_axis=1, tiled=True),
        lax.all_to_all(v_low, ULY, split_axis=2, concat_axis=1, tiled=True),
    )
    q_group = q_heads.reshape(
        sequence_count, block_len, local_key_value, query_group_width, HEAD_SIZE
    )
    stat_shape = (sequence_count, local_key_value, query_group_width, block_len)
    start_state = (
        jnp.full(stat_shape, -1e30, jnp.float32),
        jnp.zeros(stat_shape, jnp.float32),
        jnp.zeros(stat_shape + (HEAD_SIZE,), jnp.float32),
    )
    key_piece = lax.all_gather(k_heads, BLK, axis=1, tiled=True)
    value_piece = lax.all_gather(v_heads, BLK, axis=1, tiled=True)
    key_pos = positions_of(jnp.arange(key_piece.shape[1], dtype=jnp.int32), span_order, half_len)
    allowed = query_pos[:, None] >= key_pos[None, :]

    def attend_one_sequence(members):
        query_rows, key_rows, value_rows, top_seq, total_seq, accum_seq = members
        scores = (
            jnp.einsum(EQ_QKGD_NKD_TO_KGQN, query_rows, key_rows, preferred_element_type=jnp.float32)
            * score_scale
        )
        scores = jnp.where(allowed, scores, -jnp.inf)
        new_top = jnp.maximum(top_seq, jnp.max(scores, axis=-1))
        fading = jnp.exp(top_seq - new_top)
        weights = jnp.exp(scores - new_top[..., None])
        total_seq = total_seq * fading + jnp.sum(weights, axis=-1)
        accum_seq = accum_seq * fading[..., None] + jnp.einsum(
            EQ_KGQN_NKD_TO_KGQD,
            weights.astype(jnp.bfloat16),
            value_rows,
            preferred_element_type=jnp.float32,
        )
        return (new_top, total_seq, accum_seq)

    row_top, row_total, accum = lax.map(
        attend_one_sequence,
        (q_group, key_piece, value_piece, start_state[0], start_state[1], start_state[2]),
    )
    log_total = row_top + jnp.log(row_total)
    attention_output = jnp.transpose(accum / row_total[..., None], (0, 3, 1, 2, 4)).reshape(
        sequence_count, block_len, local_q, HEAD_SIZE
    )
    heads_seq = lax.all_to_all(
        attention_output.astype(jnp.bfloat16), ULY, split_axis=1, concat_axis=2, tiled=True
    )
    heads_flat = heads_seq.reshape(sequence_count, token_count, QUERY_HEADS * HEAD_SIZE)
    middle = source + jnp.einsum(
        EQ_STE_ED_TO_STD, heads_flat, wo_all, preferred_element_type=jnp.float32
    )
    g_mlp, wg_all, wu_all, wd_all = (
        lax.all_gather(mlp_gain, EVERY, axis=0, tiled=True),
        lax.all_gather(w_gate, EVERY, axis=0, tiled=True),
        lax.all_gather(w_up, EVERY, axis=0, tiled=True),
        lax.all_gather(w_down, EVERY, axis=0, tiled=True),
    )
    second_scale = rms_scale(middle)
    gain_mlp = g_mlp.astype(jnp.float32)
    normed2 = (middle * second_scale * gain_mlp).astype(jnp.bfloat16)
    gate_pre = jnp.einsum(EQ_STD_DF_TO_STF, normed2, wg_all, preferred_element_type=jnp.float32)
    up_pre = jnp.einsum(EQ_STD_DF_TO_STF, normed2, wu_all, preferred_element_type=jnp.float32)
    sigmoid_gate = jax.nn.sigmoid(gate_pre)
    activated = (gate_pre * sigmoid_gate * up_pre).astype(jnp.bfloat16)
    result = middle + jnp.einsum(
        EQ_STF_FD_TO_STD, activated, wd_all, preferred_element_type=jnp.float32
    )
    output = result.astype(jnp.bfloat16)
    g_mlp, wg_all, wu_all, wd_all = (
        lax.all_gather(mlp_gain, EVERY, axis=0, tiled=True),
        lax.all_gather(w_gate, EVERY, axis=0, tiled=True),
        lax.all_gather(w_up, EVERY, axis=0, tiled=True),
        lax.all_gather(w_down, EVERY, axis=0, tiled=True),
    )
    gain_mlp = g_mlp.astype(jnp.float32)
    grad_act = jnp.einsum(EQ_STD_FD_TO_STF, cotangent, wd_all, preferred_element_type=jnp.float32)
    grad_gate_pre = (
        grad_act * up_pre * sigmoid_gate * (1.0 + gate_pre * (1.0 - sigmoid_gate))
    ).astype(jnp.bfloat16)
    grad_up_pre = (grad_act * gate_pre * sigmoid_gate).astype(jnp.bfloat16)
    grad_gate = jnp.einsum(
        EQ_STD_STF_TO_DF, normed2, grad_gate_pre, preferred_element_type=jnp.float32
    )
    grad_up = jnp.einsum(EQ_STD_STF_TO_DF, normed2, grad_up_pre, preferred_element_type=jnp.float32)
    grad_normed2 = jnp.einsum(
        EQ_STF_DF_TO_STD, grad_gate_pre, wg_all, preferred_element_type=jnp.float32
    ) + jnp.einsum(EQ_STF_DF_TO_STD, grad_up_pre, wu_all, preferred_element_type=jnp.float32)
    mlp_gain_term = jnp.sum(grad_normed2 * middle * second_scale, axis=(0, 1))
    grad_middle = cotangent.astype(jnp.float32) + norm_back(
        grad_normed2, middle, second_scale, gain_mlp
    )
    grad_mlp_gain, grad_gate, grad_up = (
        lax.psum_scatter(mlp_gain_term, EVERY, scatter_dimension=0, tiled=True),
        lax.psum_scatter(grad_gate, EVERY, scatter_dimension=0, tiled=True),
        lax.psum_scatter(grad_up, EVERY, scatter_dimension=0, tiled=True),
    )
    g_attn, wq_all, wk_all, wv_all, wo_all = (
        lax.all_gather(attn_gain, EVERY, axis=0, tiled=True),
        lax.all_gather(w_query, EVERY, axis=0, tiled=True),
        lax.all_gather(key_weight, EVERY, axis=0, tiled=True),
        lax.all_gather(value_weight, EVERY, axis=0, tiled=True),
        lax.all_gather(w_out, EVERY, axis=0, tiled=True),
    )
    middle_low = grad_middle.astype(jnp.bfloat16)
    grad_out = jnp.einsum(EQ_STE_STD_TO_ED, heads_flat, middle_low, preferred_element_type=jnp.float32)
    grad_heads = (
        jnp.einsum(EQ_STD_ED_TO_STE, middle_low, wo_all, preferred_element_type=jnp.float32)
        .astype(jnp.bfloat16)
        .reshape(sequence_count, token_count, QUERY_HEADS, HEAD_SIZE)
    )
    grad_heads_local = lax.all_to_all(grad_heads, ULY, split_axis=2, concat_axis=1, tiled=True)
    grad_group = jnp.transpose(
        grad_heads_local.reshape(
            sequence_count, block_len, local_key_value, query_group_width, HEAD_SIZE
        ),
        (0, 2, 3, 1, 4),
    )
    delta = jnp.sum(grad_heads_local.astype(jnp.float32) * attention_output, axis=-1)
    delta = jnp.transpose(
        delta.reshape(sequence_count, block_len, local_key_value, query_group_width), (0, 2, 3, 1)
    )
    seq_length = block_len * lax.axis_size(BLK)
    zero_keys = jnp.zeros((sequence_count, seq_length, local_key_value, HEAD_SIZE), jnp.float32)
    back_state = (jnp.zeros(stat_shape + (HEAD_SIZE,), jnp.float32), zero_keys, zero_keys)
    key_piece = lax.all_gather(k_heads, BLK, axis=1, tiled=True)
    value_piece = lax.all_gather(v_heads, BLK, axis=1, tiled=True)
    key_pos = positions_of(jnp.arange(key_piece.shape[1], dtype=jnp.int32), span_order, half_len)
    back_allowed = query_pos[:, None] >= key_pos[None, :]

    def back_one_sequence(members):
        query_rows, grad_rows, lse_seq, delta_seq, key_rows, value_rows, dq_seq, dk_seq, dv_seq = (
            members
        )
        scores = (
            jnp.einsum(EQ_QKGD_NKD_TO_KGQN, query_rows, key_rows, preferred_element_type=jnp.float32)
            * score_scale
        )
        scores = jnp.where(back_allowed, scores, -jnp.inf)
        probs = jnp.exp(scores - lse_seq[..., None])
        grad_values = jnp.einsum(
            EQ_KGQN_KGQD_TO_NKD,
            probs.astype(jnp.bfloat16),
            grad_rows,
            preferred_element_type=jnp.float32,
        )
        grad_probs = jnp.einsum(
            EQ_KGQD_NKD_TO_KGQN, grad_rows, value_rows, preferred_element_type=jnp.float32
        )
        grad_scores = (probs * (grad_probs - delta_seq[..., None])).astype(jnp.bfloat16)
        dq_seq = dq_seq + score_scale * jnp.einsum(
            EQ_KGQN_NKD_TO_KGQD, grad_scores, key_rows, preferred_element_type=jnp.float32
        )
        grad_keys = score_scale * jnp.einsum(
            EQ_KGQN_QKGD_TO_NKD, grad_scores, query_rows, preferred_element_type=jnp.float32
        )
        return (dq_seq, add_rows(dk_seq, grad_keys), add_rows(dv_seq, grad_values))

    grad_q_group, grad_k_whole, grad_v_whole = lax.map(
        back_one_sequence,
        (
            q_group,
            grad_group,
            log_total,
            delta,
            key_piece,
            value_piece,
            back_state[0],
            back_state[1],
            back_state[2],
        ),
    )
    grad_k_block, grad_v_block = (
        lax.psum_scatter(
            grad_k_whole.astype(jnp.bfloat16), BLK, scatter_dimension=1, tiled=True
        ).astype(jnp.float32),
        lax.psum_scatter(
            grad_v_whole.astype(jnp.bfloat16), BLK, scatter_dimension=1, tiled=True
        ).astype(jnp.float32),
    )
    grad_q_block = jnp.transpose(grad_q_group, (0, 3, 1, 2, 4)).reshape(
        sequence_count, block_len, local_q, HEAD_SIZE
    )
    grad_q_seq, grad_k_seq, value_sequence_gradient = (
        lax.all_to_all(
            grad_q_block.astype(jnp.bfloat16), ULY, split_axis=1, concat_axis=2, tiled=True
        ).astype(grad_q_block.dtype),
        lax.all_to_all(
            grad_k_block.astype(jnp.bfloat16), ULY, split_axis=1, concat_axis=2, tiled=True
        ).astype(grad_k_block.dtype),
        lax.all_to_all(
            grad_v_block.astype(jnp.bfloat16), ULY, split_axis=1, concat_axis=2, tiled=True
        ).astype(grad_v_block.dtype),
    )
    grad_q_normed = rotate(grad_q_seq, local_angles, -1.0)
    grad_k_normed = rotate(grad_k_seq, local_angles, -1.0)
    q_gain_term = jnp.sum(grad_q_normed * q_pre * q_scale, axis=(0, 1, 2))
    k_gain_term = jnp.sum(grad_k_normed * key_before_norm * k_scale, axis=(0, 1, 2))
    grad_q_pre = (
        norm_back(grad_q_normed, q_pre, q_scale, gain_q)
        .astype(jnp.bfloat16)
        .reshape(sequence_count, token_count, QUERY_HEADS * HEAD_SIZE)
    )
    grad_k_pre = (
        norm_back(grad_k_normed, key_before_norm, k_scale, gain_k)
        .astype(jnp.bfloat16)
        .reshape(sequence_count, token_count, KEY_VALUE_HEADS * HEAD_SIZE)
    )
    value_pre_gradient = value_sequence_gradient.astype(jnp.bfloat16).reshape(
        sequence_count, token_count, KEY_VALUE_HEADS * HEAD_SIZE
    )
    grad_query = jnp.einsum(
        EQ_STD_STE_TO_DE, normalized_input, grad_q_pre, preferred_element_type=jnp.float32
    )
    grad_key = jnp.einsum(
        EQ_STD_STE_TO_DE, normalized_input, grad_k_pre, preferred_element_type=jnp.float32
    )
    grad_value = jnp.einsum(
        EQ_STD_STE_TO_DE, normalized_input, value_pre_gradient, preferred_element_type=jnp.float32
    )
    grad_normed = jnp.einsum(EQ_STE_DE_TO_STD, grad_q_pre, wq_all, preferred_element_type=jnp.float32)
    grad_normed = grad_normed + jnp.einsum(
        EQ_STE_DE_TO_STD, grad_k_pre, wk_all, preferred_element_type=jnp.float32
    )
    grad_normed = grad_normed + jnp.einsum(
        EQ_STE_DE_TO_STD, value_pre_gradient, wv_all, preferred_element_type=jnp.float32
    )
    attn_gain_term = jnp.sum(grad_normed * source * first_scale, axis=(0, 1))
    grad_hidden = grad_middle + norm_back(
        grad_normed, source, first_scale, g_attn.astype(jnp.float32)
    )
    grad_down = jnp.einsum(EQ_STF_STD_TO_FD, activated, cotangent, preferred_element_type=jnp.float32)
    grad_attn_gain, grad_query, grad_key, grad_value, grad_out, grad_down = (
        lax.psum_scatter(attn_gain_term, EVERY, scatter_dimension=0, tiled=True),
        lax.psum_scatter(grad_query, EVERY, scatter_dimension=0, tiled=True),
        lax.psum_scatter(grad_key, EVERY, scatter_dimension=0, tiled=True),
        lax.psum_scatter(grad_value, EVERY, scatter_dimension=0, tiled=True),
        lax.psum_scatter(grad_out, EVERY, scatter_dimension=0, tiled=True),
        lax.psum_scatter(grad_down, EVERY, scatter_dimension=0, tiled=True),
    )
    grad_q_gain, grad_k_gain = lax.psum((q_gain_term, k_gain_term), EVERY)
    return (
        output,
        grad_hidden,
        grad_attn_gain,
        grad_query,
        grad_key,
        grad_value,
        grad_out,
        grad_q_gain,
        grad_k_gain,
        grad_mlp_gain,
        grad_gate,
        grad_up,
        grad_down,
    )


def permute_features(rows, n_dp, n_blk, n_uly):
    lead = rows.shape[:-1]
    split = rows.reshape(lead + (n_dp, n_blk, n_uly, -1))
    return jnp.swapaxes(split, -3, -2).reshape(rows.shape)


def restore_features(rows, n_dp, n_blk, n_uly):
    lead = rows.shape[:-1]
    split = rows.reshape(lead + (n_dp, n_uly, n_blk, -1))
    return jnp.swapaxes(split, -3, -2).reshape(rows.shape)


def take_columns(weight, n_dp, n_blk):
    rows, width = weight.shape
    split = jnp.transpose(weight.reshape(rows, n_dp, n_blk, -1), (2, 0, 1, 3))
    swapped = lax.all_to_all(split, BLK, split_axis=0, concat_axis=0)
    swapped = jnp.transpose(swapped, (0, 1, 2, 3)).reshape(n_blk * rows, width // n_blk)
    return lax.all_gather(swapped, PLANE, axis=0, tiled=True)


def give_columns(grad, n_dp, n_blk):
    summed = lax.psum_scatter(
        grad.astype(jnp.bfloat16), PLANE, scatter_dimension=0, tiled=True
    )
    rows = summed.shape[0] // n_blk
    split = summed.reshape(n_blk, rows, n_dp, -1)
    swapped = lax.all_to_all(split, BLK, split_axis=0, concat_axis=0)
    return jnp.transpose(swapped, (1, 2, 0, 3)).reshape(rows, -1).astype(jnp.float32)


def shards(
    hidden,
    span_order,
    attn_gain,
    w_query,
    key_weight,
    value_weight,
    w_out,
    q_gain,
    k_gain,
    mlp_gain,
    w_gate,
    w_up,
    w_down,
    cotangent,
):
    seqs, toks, width = hidden.shape
    n_dp, n_blk, n_uly = (lax.axis_size(a) for a in EVERY)
    blk_index = lax.axis_index(BLK)
    uly_index = lax.axis_index(ULY)
    local_q = QUERY_HEADS // n_blk
    local_kv = KEY_VALUE_HEADS // n_blk
    group = QUERY_HEADS // KEY_VALUE_HEADS
    half_len = toks * n_uly // 2
    score_scale = 1.0 / math.sqrt(HEAD_SIZE)
    rows = n_blk * seqs * toks
    f32, bf16 = jnp.float32, jnp.bfloat16

    def places(u):
        return (
            (jnp.arange(n_blk, dtype=jnp.int32)[:, None] * n_uly + u) * toks
            + jnp.arange(toks, dtype=jnp.int32)[None, :]
        )

    query_pos = positions_of(places(uly_index).reshape(-1), span_order, half_len)
    key_pos = jnp.concatenate(
        [positions_of(places(u).reshape(-1), span_order, half_len) for u in range(n_uly)]
    )
    angles = angles_of(query_pos, HEAD_SIZE).reshape(n_blk, 1, toks, HEAD_SIZE // 2)
    angles = jnp.broadcast_to(angles, (n_blk, seqs, toks, HEAD_SIZE // 2)).reshape(rows, -1)

    gains = lax.all_gather(
        jnp.stack([attn_gain, mlp_gain]), EVERY, axis=1, tiled=True
    ).astype(f32)
    g_attn, g_mlp = gains[0], gains[1]

    qkv_local = jnp.concatenate(
        [
            w.reshape(w.shape[0], n_dp, n_blk, -1)
            for w in (w_query, key_weight, value_weight)
        ],
        axis=-1,
    ).reshape(w_query.shape[0], -1)
    per_dp = qkv_local.shape[1] // (n_dp * n_blk)
    wq_per, wk_per = w_query.shape[1] // (n_dp * n_blk), key_weight.shape[1] // (n_dp * n_blk)
    w_qkv = take_columns(qkv_local, n_dp, n_blk)
    wo = lax.all_gather(w_out, PLANE, axis=0, tiled=True)

    source_own = hidden.astype(f32)
    source_gathered = lax.all_gather(hidden, BLK, axis=0)
    source = source_gathered.reshape(rows, width).astype(f32)
    first_scale = rms_scale(source)
    normed = permute_features(
        (source * first_scale * g_attn).astype(bf16), n_dp, n_blk, n_uly
    )
    qkv = jnp.dot(normed, w_qkv, preferred_element_type=f32).reshape(rows, n_dp, per_dp)
    q_pre = qkv[:, :, :wq_per].reshape(rows, local_q, HEAD_SIZE)
    k_pre = qkv[:, :, wq_per : wq_per + wk_per].reshape(rows, local_kv, HEAD_SIZE)
    v_pre = qkv[:, :, wq_per + wk_per :].reshape(rows, local_kv, HEAD_SIZE)
    q_scale, k_scale = rms_scale(q_pre), rms_scale(k_pre)
    gain_q, gain_k = q_gain.astype(f32), k_gain.astype(f32)
    q_rot = rotate(q_pre * q_scale * gain_q, angles, 1.0).astype(bf16)
    k_rot = rotate(k_pre * k_scale * gain_k, angles, 1.0).astype(bf16)
    v_low = v_pre.astype(bf16)

    def by_head(x):
        heads = x.shape[1]
        x = x.reshape(n_blk, seqs, toks, heads, HEAD_SIZE)
        return jnp.transpose(x, (1, 3, 0, 2, 4)).reshape(seqs, heads, n_blk * toks, HEAD_SIZE)

    def from_head(x):
        heads = x.shape[1]
        x = x.reshape(seqs, heads, n_blk, toks, HEAD_SIZE)
        return jnp.transpose(x, (2, 0, 3, 1, 4)).reshape(rows, heads, HEAD_SIZE)

    q_len = n_blk * toks
    k_len = n_uly * q_len
    kv = jnp.stack([by_head(k_rot), by_head(v_low)])
    kv_all = lax.all_gather(kv, ULY, axis=3, tiled=True)
    keys, values = kv_all[0], kv_all[1]
    queries = by_head(q_rot).reshape(seqs, local_kv, group, q_len, HEAD_SIZE)
    allowed = query_pos[:, None] >= key_pos[None, :]
    scores = (
        jnp.einsum(EQ_SKGQD_SKND_TO_SKGQN, queries, keys, preferred_element_type=f32) * score_scale
    )
    scores = jnp.where(allowed, scores, -jnp.inf)
    top = jnp.max(scores, axis=-1, keepdims=True)
    weights = jnp.exp(scores - top)
    total = jnp.sum(weights, axis=-1, keepdims=True)
    lse = top + jnp.log(total)
    attended = (
        jnp.einsum(EQ_SKGQN_SKND_TO_SKGQD, weights.astype(bf16), values, preferred_element_type=f32)
        / total
    )
    heads_flat = from_head(
        attended.astype(bf16).reshape(seqs, local_q, q_len, HEAD_SIZE)
    ).reshape(rows, local_q * HEAD_SIZE)

    def scatter_tokens(partial):
        partial = partial.astype(bf16).reshape(n_blk, seqs, toks, width)
        return lax.psum_scatter(partial, BLK, scatter_dimension=0, tiled=True)[0].astype(f32)

    def gather_tokens(own):
        return lax.all_gather(own, BLK, axis=0).reshape(rows, -1)

    middle = source_own + scatter_tokens(jnp.dot(heads_flat, wo, preferred_element_type=f32))
    second_scale = rms_scale(middle)
    normed2_own = permute_features(
        (middle * second_scale * g_mlp).astype(bf16), n_dp, n_blk, n_uly
    )
    normed2 = gather_tokens(normed2_own)
    wg = take_columns(w_gate, n_dp, n_blk)
    wu = take_columns(w_up, n_dp, n_blk)
    wd = lax.all_gather(w_down, PLANE, axis=0, tiled=True)
    cot = gather_tokens(cotangent)
    gate_pre = jnp.dot(normed2, wg, preferred_element_type=f32)
    up_pre = jnp.dot(normed2, wu, preferred_element_type=f32)
    sigmoid_gate = jax.nn.sigmoid(gate_pre)
    activated = (gate_pre * sigmoid_gate * up_pre).astype(bf16)
    output = (
        middle + scatter_tokens(jnp.dot(activated, wd, preferred_element_type=f32))
    ).astype(bf16)
    grad_act = jnp.einsum(EQ_TD_FD_TO_TF, cot, wd, preferred_element_type=f32)
    grad_gate_pre = (
        grad_act * up_pre * sigmoid_gate * (1.0 + gate_pre * (1.0 - sigmoid_gate))
    ).astype(bf16)
    grad_up_pre = (grad_act * gate_pre * sigmoid_gate).astype(bf16)
    grad_normed2_part = jnp.einsum(
        EQ_TF_DF_TO_TD, grad_gate_pre, wg, preferred_element_type=f32
    ) + jnp.einsum(EQ_TF_DF_TO_TD, grad_up_pre, wu, preferred_element_type=f32)
    grad_normed2 = restore_features(scatter_tokens(grad_normed2_part), n_dp, n_blk, n_uly)
    grad_gate = give_columns(
        jnp.einsum(EQ_TD_TF_TO_DF, normed2, grad_gate_pre, preferred_element_type=f32), n_dp, n_blk
    )
    grad_up = give_columns(
        jnp.einsum(EQ_TD_TF_TO_DF, normed2, grad_up_pre, preferred_element_type=f32), n_dp, n_blk
    )
    grad_down = lax.psum_scatter(
        jnp.einsum(EQ_TF_TD_TO_FD, activated, cot, preferred_element_type=f32).astype(bf16),
        PLANE,
        scatter_dimension=0,
        tiled=True,
    ).astype(f32)
    mlp_gain_term = jnp.sum(grad_normed2 * middle * second_scale, axis=(0, 1))
    grad_middle = cotangent.astype(f32) + norm_back(grad_normed2, middle, second_scale, g_mlp)
    middle_low = gather_tokens(grad_middle.astype(bf16))
    grad_out = lax.psum_scatter(
        jnp.einsum(EQ_TE_TD_TO_ED, heads_flat, middle_low, preferred_element_type=f32).astype(bf16),
        PLANE,
        scatter_dimension=0,
        tiled=True,
    ).astype(f32)
    grad_heads = by_head(
        jnp.einsum(EQ_TD_ED_TO_TE, middle_low, wo, preferred_element_type=f32)
        .astype(bf16)
        .reshape(rows, local_q, HEAD_SIZE)
    ).reshape(seqs, local_kv, group, q_len, HEAD_SIZE)
    delta = jnp.sum(grad_heads.astype(f32) * attended, axis=-1, keepdims=True)
    probs = jnp.exp(scores - lse)
    grad_values = jnp.einsum(
        EQ_SKGQN_SKGQD_TO_SKND, probs.astype(bf16), grad_heads, preferred_element_type=f32
    )
    grad_probs = jnp.einsum(EQ_SKGQD_SKND_TO_SKGQN, grad_heads, values, preferred_element_type=f32)
    grad_scores = (probs * (grad_probs - delta)).astype(bf16)
    grad_queries = score_scale * jnp.einsum(
        EQ_SKGQN_SKND_TO_SKGQD, grad_scores, keys, preferred_element_type=f32
    )
    grad_keys = score_scale * jnp.einsum(
        EQ_SKGQN_SKGQD_TO_SKND, grad_scores, queries, preferred_element_type=f32
    )
    grad_kv = lax.psum_scatter(
        jnp.stack([grad_keys, grad_values]).astype(bf16),
        ULY,
        scatter_dimension=3,
        tiled=True,
    ).astype(f32)
    grad_q_normed = rotate(
        from_head(grad_queries.reshape(seqs, local_q, q_len, HEAD_SIZE)), angles, -1.0
    )
    grad_k_normed = rotate(from_head(grad_kv[0]), angles, -1.0)
    q_gain_term = jnp.sum(grad_q_normed * q_pre * q_scale, axis=(0, 1))
    k_gain_term = jnp.sum(grad_k_normed * k_pre * k_scale, axis=(0, 1))
    grad_q_pre = norm_back(grad_q_normed, q_pre, q_scale, gain_q).astype(bf16)
    grad_k_pre = norm_back(grad_k_normed, k_pre, k_scale, gain_k).astype(bf16)
    grad_v_pre = from_head(grad_kv[1]).astype(bf16)
    grad_qkv = jnp.concatenate(
        [g.reshape(rows, n_dp, -1) for g in (grad_q_pre, grad_k_pre, grad_v_pre)], axis=-1
    ).reshape(rows, n_dp * per_dp)
    grad_normed = restore_features(
        scatter_tokens(jnp.einsum(EQ_TE_DE_TO_TD, grad_qkv, w_qkv, preferred_element_type=f32)),
        n_dp,
        n_blk,
        n_uly,
    )
    grad_w_qkv = give_columns(
        jnp.einsum(EQ_TD_TE_TO_DE, normed, grad_qkv, preferred_element_type=f32), n_dp, n_blk
    ).reshape(-1, n_dp, n_blk, per_dp)
    grad_query = grad_w_qkv[..., :wq_per].reshape(w_query.shape)
    grad_key = grad_w_qkv[..., wq_per : wq_per + wk_per].reshape(key_weight.shape)
    grad_value = grad_w_qkv[..., wq_per + wk_per :].reshape(value_weight.shape)
    own_scale = rms_scale(source_own)
    attn_gain_term = jnp.sum(grad_normed * source_own * own_scale, axis=(0, 1))
    grad_hidden = grad_middle + norm_back(grad_normed, source_own, own_scale, g_attn)
    small = lax.psum(
        jnp.concatenate([attn_gain_term, mlp_gain_term, q_gain_term, k_gain_term]),
        EVERY,
    )
    gain_rows = attn_gain.shape[0]
    gain_at = ((lax.axis_index(DP) * n_blk + blk_index) * n_uly + uly_index) * gain_rows
    grad_attn_gain = lax.dynamic_slice(small, (gain_at,), (gain_rows,))
    grad_mlp_gain = lax.dynamic_slice(small, (width + gain_at,), (gain_rows,))
    grad_q_gain = small[2 * width : 2 * width + HEAD_SIZE]
    grad_k_gain = small[2 * width + HEAD_SIZE :]
    return (
        output,
        grad_hidden,
        grad_attn_gain,
        grad_query,
        grad_key,
        grad_value,
        grad_out,
        grad_q_gain,
        grad_k_gain,
        grad_mlp_gain,
        grad_gate,
        grad_up,
        grad_down,
    )


def solution(mesh):
    parts = mesh.shape[DP] * mesh.shape[BLK]
    aligned = KEY_VALUE_HEADS % parts == 0
    in_specs = (
        TOKENS,
        P(),
        P(EVERY),
        P(EVERY, None),
        P(EVERY, None),
        P(EVERY, None),
        P(EVERY, None),
        P(),
        P(),
        P(EVERY),
        P(EVERY, None),
        P(EVERY, None),
        P(EVERY, None),
        TOKENS,
    )
    out_specs = (
        TOKENS,
        TOKENS,
        P(EVERY),
        P(EVERY, None),
        P(EVERY, None),
        P(EVERY, None),
        P(EVERY, None),
        P(),
        P(),
        P(EVERY),
        P(EVERY, None),
        P(EVERY, None),
        P(EVERY, None),
    )
    return jax.shard_map(
        shards if aligned else shards_general,
        mesh=mesh, in_specs=in_specs, out_specs=out_specs, check_vma=False)
```

```python
import math

import jax
import jax.numpy as jnp
from jax import lax
from jax.experimental import pallas as pl
from jax.experimental.pallas import tpu as pltpu
from jax.sharding import PartitionSpec as P

QUERY_HEADS = 16
KEY_VALUE_HEADS = 8
HEAD_SIZE = 128


DP, BLK, ULY = "dp", "blk", "uly"
EVERY = (DP, BLK, ULY)
PLANE = (DP, ULY)
TOKENS = P(DP, (BLK, ULY), None)
EQ_SCORES = "skgqd,sknd->skgqn"
EQ_ATTEND = "skgqn,sknd->skgqd"
EQ_TO_KEYS = "skgqn,skgqd->sknd"
EQ_KGQD_NKD_TO_KGQN = "kgqd,nkd->kgqn"
EQ_KGQN_KGQD_TO_NKD = "kgqn,kgqd->nkd"
EQ_KGQN_NKD_TO_KGQD = "kgqn,nkd->kgqd"
EQ_KGQN_QKGD_TO_NKD = "kgqn,qkgd->nkd"
EQ_QKGD_NKD_TO_KGQN = "qkgd,nkd->kgqn"
EQ_STD_DE_TO_STE = "std,de->ste"
EQ_STD_DF_TO_STF = "std,df->stf"
EQ_STD_ED_TO_STE = "std,ed->ste"
EQ_STD_FD_TO_STF = "std,fd->stf"
EQ_STD_STE_TO_DE = "std,ste->de"
EQ_STD_STF_TO_DF = "std,stf->df"
EQ_STE_DE_TO_STD = "ste,de->std"
EQ_STE_ED_TO_STD = "ste,ed->std"
EQ_STE_STD_TO_ED = "ste,std->ed"
EQ_STF_DF_TO_STD = "stf,df->std"
EQ_STF_FD_TO_STD = "stf,fd->std"
EQ_STF_STD_TO_FD = "stf,std->fd"

EPSILON = 1e-06
ROPE_BASE = 1000000.0


def rms_scale(source):
    return lax.rsqrt(jnp.mean(source * source, axis=-1, keepdims=True) + EPSILON)


def norm_back(grad_normed, source, norm_scale, gain):
    unit_rows = source * norm_scale
    scaled = grad_normed * gain
    return norm_scale * (scaled - unit_rows * jnp.mean(scaled * unit_rows, axis=-1, keepdims=True))


def angles_of(positions, head_dim):
    freq_steps = jnp.arange(head_dim // 2, dtype=jnp.float32)
    inverse = jnp.exp(freq_steps * (-2.0 * math.log(ROPE_BASE) / head_dim))
    return positions.astype(jnp.float32)[:, None] * inverse[None, :]


def rotate(source, angles, direction):
    half_dim = source.shape[-1] // 2
    cosine = jnp.cos(angles)[:, None, :]
    sine_part = direction * jnp.sin(angles)[:, None, :]
    first_half = source[..., :half_dim]
    second_half = source[..., half_dim:]
    return jnp.concatenate(
        [
            first_half * cosine - second_half * sine_part,
            second_half * cosine + first_half * sine_part,
        ],
        axis=-1,
    )


def positions_of(places, span_order, half_len):
    blocks_of = places // half_len
    block_ids = jnp.arange(span_order.shape[0], dtype=jnp.int32)
    chosen = jnp.sum(
        jnp.where(blocks_of[:, None] == block_ids[None, :], span_order[None, :], 0), axis=1
    )
    return chosen * half_len + places % half_len


def add_rows(buffer, new_rows):
    return buffer + new_rows


def shards_general(
    hidden,
    span_order,
    attn_gain,
    w_query,
    key_weight,
    value_weight,
    w_out,
    q_gain,
    k_gain,
    mlp_gain,
    w_gate,
    w_up,
    w_down,
    cotangent,
):
    sequence_count = hidden.shape[0]
    token_count = hidden.shape[1]
    ulysses_group_size = lax.axis_size(ULY)
    local_q = QUERY_HEADS // ulysses_group_size
    local_key_value = KEY_VALUE_HEADS // ulysses_group_size
    query_group_width = QUERY_HEADS // KEY_VALUE_HEADS
    block_len = token_count * ulysses_group_size
    half_len = block_len // 2
    score_scale = 1.0 / math.sqrt(HEAD_SIZE)
    blk_index = lax.axis_index(BLK)
    uly_index = lax.axis_index(ULY)
    first_place = (blk_index * ulysses_group_size + uly_index) * token_count
    local_angles = angles_of(
        positions_of(first_place + jnp.arange(token_count, dtype=jnp.int32), span_order, half_len),
        HEAD_SIZE,
    )
    query_pos = positions_of(
        blk_index * block_len + jnp.arange(block_len, dtype=jnp.int32), span_order, half_len
    )
    g_attn, wq_all, wk_all, wv_all, wo_all = (
        lax.all_gather(attn_gain, EVERY, axis=0, tiled=True),
        lax.all_gather(w_query, EVERY, axis=0, tiled=True),
        lax.all_gather(key_weight, EVERY, axis=0, tiled=True),
        lax.all_gather(value_weight, EVERY, axis=0, tiled=True),
        lax.all_gather(w_out, EVERY, axis=0, tiled=True),
    )
    source = hidden.astype(jnp.float32)
    first_scale = rms_scale(source)
    normalized_input = (source * first_scale * g_attn.astype(jnp.float32)).astype(jnp.bfloat16)
    q_pre = jnp.einsum(
        EQ_STD_DE_TO_STE, normalized_input, wq_all, preferred_element_type=jnp.float32
    ).reshape(sequence_count, token_count, QUERY_HEADS, HEAD_SIZE)
    key_before_norm = jnp.einsum(
        EQ_STD_DE_TO_STE, normalized_input, wk_all, preferred_element_type=jnp.float32
    ).reshape(sequence_count, token_count, KEY_VALUE_HEADS, HEAD_SIZE)
    value_before_norm = jnp.einsum(
        EQ_STD_DE_TO_STE, normalized_input, wv_all, preferred_element_type=jnp.float32
    ).reshape(sequence_count, token_count, KEY_VALUE_HEADS, HEAD_SIZE)
    q_scale = rms_scale(q_pre)
    k_scale = rms_scale(key_before_norm)
    gain_q = q_gain.astype(jnp.float32)
    gain_k = k_gain.astype(jnp.float32)
    q_rot = rotate(q_pre * q_scale * gain_q, local_angles, 1.0).astype(jnp.bfloat16)
    k_rot = rotate(key_before_norm * k_scale * gain_k, local_angles, 1.0).astype(jnp.bfloat16)
    v_low = value_before_norm.astype(jnp.bfloat16)
    q_heads, k_heads, v_heads = (
        lax.all_to_all(q_rot, ULY, split_axis=2, concat_axis=1, tiled=True),
        lax.all_to_all(k_rot, ULY, split_axis=2, concat_axis=1, tiled=True),
        lax.all_to_all(v_low, ULY, split_axis=2, concat_axis=1, tiled=True),
    )
    q_group = q_heads.reshape(
        sequence_count, block_len, local_key_value, query_group_width, HEAD_SIZE
    )
    stat_shape = (sequence_count, local_key_value, query_group_width, block_len)
    start_state = (
        jnp.full(stat_shape, -1e30, jnp.float32),
        jnp.zeros(stat_shape, jnp.float32),
        jnp.zeros(stat_shape + (HEAD_SIZE,), jnp.float32),
    )
    key_piece = lax.all_gather(k_heads, BLK, axis=1, tiled=True)
    value_piece = lax.all_gather(v_heads, BLK, axis=1, tiled=True)
    key_pos = positions_of(jnp.arange(key_piece.shape[1], dtype=jnp.int32), span_order, half_len)
    allowed = query_pos[:, None] >= key_pos[None, :]

    def attend_one_sequence(members):
        query_rows, key_rows, value_rows, top_seq, total_seq, accum_seq = members
        scores = (
            jnp.einsum(EQ_QKGD_NKD_TO_KGQN, query_rows, key_rows, preferred_element_type=jnp.float32)
            * score_scale
        )
        scores = jnp.where(allowed, scores, -jnp.inf)
        new_top = jnp.maximum(top_seq, jnp.max(scores, axis=-1))
        fading = jnp.exp(top_seq - new_top)
        weights = jnp.exp(scores - new_top[..., None])
        total_seq = total_seq * fading + jnp.sum(weights, axis=-1)
        accum_seq = accum_seq * fading[..., None] + jnp.einsum(
            EQ_KGQN_NKD_TO_KGQD,
            weights.astype(jnp.bfloat16),
            value_rows,
            preferred_element_type=jnp.float32,
        )
        return (new_top, total_seq, accum_seq)

    row_top, row_total, accum = lax.map(
        attend_one_sequence,
        (q_group, key_piece, value_piece, start_state[0], start_state[1], start_state[2]),
    )
    log_total = row_top + jnp.log(row_total)
    attention_output = jnp.transpose(accum / row_total[..., None], (0, 3, 1, 2, 4)).reshape(
        sequence_count, block_len, local_q, HEAD_SIZE
    )
    heads_seq = lax.all_to_all(
        attention_output.astype(jnp.bfloat16), ULY, split_axis=1, concat_axis=2, tiled=True
    )
    heads_flat = heads_seq.reshape(sequence_count, token_count, QUERY_HEADS * HEAD_SIZE)
    middle = source + jnp.einsum(
        EQ_STE_ED_TO_STD, heads_flat, wo_all, preferred_element_type=jnp.float32
    )
    g_mlp, wg_all, wu_all, wd_all = (
        lax.all_gather(mlp_gain, EVERY, axis=0, tiled=True),
        lax.all_gather(w_gate, EVERY, axis=0, tiled=True),
        lax.all_gather(w_up, EVERY, axis=0, tiled=True),
        lax.all_gather(w_down, EVERY, axis=0, tiled=True),
    )
    second_scale = rms_scale(middle)
    gain_mlp = g_mlp.astype(jnp.float32)
    normed2 = (middle * second_scale * gain_mlp).astype(jnp.bfloat16)
    gate_pre = jnp.einsum(EQ_STD_DF_TO_STF, normed2, wg_all, preferred_element_type=jnp.float32)
    up_pre = jnp.einsum(EQ_STD_DF_TO_STF, normed2, wu_all, preferred_element_type=jnp.float32)
    sigmoid_gate = jax.nn.sigmoid(gate_pre)
    activated = (gate_pre * sigmoid_gate * up_pre).astype(jnp.bfloat16)
    result = middle + jnp.einsum(
        EQ_STF_FD_TO_STD, activated, wd_all, preferred_element_type=jnp.float32
    )
    output = result.astype(jnp.bfloat16)
    g_mlp, wg_all, wu_all, wd_all = (
        lax.all_gather(mlp_gain, EVERY, axis=0, tiled=True),
        lax.all_gather(w_gate, EVERY, axis=0, tiled=True),
        lax.all_gather(w_up, EVERY, axis=0, tiled=True),
        lax.all_gather(w_down, EVERY, axis=0, tiled=True),
    )
    gain_mlp = g_mlp.astype(jnp.float32)
    grad_act = jnp.einsum(EQ_STD_FD_TO_STF, cotangent, wd_all, preferred_element_type=jnp.float32)
    grad_gate_pre = (
        grad_act * up_pre * sigmoid_gate * (1.0 + gate_pre * (1.0 - sigmoid_gate))
    ).astype(jnp.bfloat16)
    grad_up_pre = (grad_act * gate_pre * sigmoid_gate).astype(jnp.bfloat16)
    grad_gate = jnp.einsum(
        EQ_STD_STF_TO_DF, normed2, grad_gate_pre, preferred_element_type=jnp.float32
    )
    grad_up = jnp.einsum(EQ_STD_STF_TO_DF, normed2, grad_up_pre, preferred_element_type=jnp.float32)
    grad_normed2 = jnp.einsum(
        EQ_STF_DF_TO_STD, grad_gate_pre, wg_all, preferred_element_type=jnp.float32
    ) + jnp.einsum(EQ_STF_DF_TO_STD, grad_up_pre, wu_all, preferred_element_type=jnp.float32)
    mlp_gain_term = jnp.sum(grad_normed2 * middle * second_scale, axis=(0, 1))
    grad_middle = cotangent.astype(jnp.float32) + norm_back(
        grad_normed2, middle, second_scale, gain_mlp
    )
    grad_mlp_gain, grad_gate, grad_up = (
        lax.psum_scatter(mlp_gain_term, EVERY, scatter_dimension=0, tiled=True),
        lax.psum_scatter(grad_gate, EVERY, scatter_dimension=0, tiled=True),
        lax.psum_scatter(grad_up, EVERY, scatter_dimension=0, tiled=True),
    )
    g_attn, wq_all, wk_all, wv_all, wo_all = (
        lax.all_gather(attn_gain, EVERY, axis=0, tiled=True),
        lax.all_gather(w_query, EVERY, axis=0, tiled=True),
        lax.all_gather(key_weight, EVERY, axis=0, tiled=True),
        lax.all_gather(value_weight, EVERY, axis=0, tiled=True),
        lax.all_gather(w_out, EVERY, axis=0, tiled=True),
    )
    middle_low = grad_middle.astype(jnp.bfloat16)
    grad_out = jnp.einsum(EQ_STE_STD_TO_ED, heads_flat, middle_low, preferred_element_type=jnp.float32)
    grad_heads = (
        jnp.einsum(EQ_STD_ED_TO_STE, middle_low, wo_all, preferred_element_type=jnp.float32)
        .astype(jnp.bfloat16)
        .reshape(sequence_count, token_count, QUERY_HEADS, HEAD_SIZE)
    )
    grad_heads_local = lax.all_to_all(grad_heads, ULY, split_axis=2, concat_axis=1, tiled=True)
    grad_group = jnp.transpose(
        grad_heads_local.reshape(
            sequence_count, block_len, local_key_value, query_group_width, HEAD_SIZE
        ),
        (0, 2, 3, 1, 4),
    )
    delta = jnp.sum(grad_heads_local.astype(jnp.float32) * attention_output, axis=-1)
    delta = jnp.transpose(
        delta.reshape(sequence_count, block_len, local_key_value, query_group_width), (0, 2, 3, 1)
    )
    seq_length = block_len * lax.axis_size(BLK)
    zero_keys = jnp.zeros((sequence_count, seq_length, local_key_value, HEAD_SIZE), jnp.float32)
    back_state = (jnp.zeros(stat_shape + (HEAD_SIZE,), jnp.float32), zero_keys, zero_keys)
    key_piece = lax.all_gather(k_heads, BLK, axis=1, tiled=True)
    value_piece = lax.all_gather(v_heads, BLK, axis=1, tiled=True)
    key_pos = positions_of(jnp.arange(key_piece.shape[1], dtype=jnp.int32), span_order, half_len)
    back_allowed = query_pos[:, None] >= key_pos[None, :]

    def back_one_sequence(members):
        query_rows, grad_rows, lse_seq, delta_seq, key_rows, value_rows, dq_seq, dk_seq, dv_seq = (
            members
        )
        scores = (
            jnp.einsum(EQ_QKGD_NKD_TO_KGQN, query_rows, key_rows, preferred_element_type=jnp.float32)
            * score_scale
        )
        scores = jnp.where(back_allowed, scores, -jnp.inf)
        probs = jnp.exp(scores - lse_seq[..., None])
        grad_values = jnp.einsum(
            EQ_KGQN_KGQD_TO_NKD,
            probs.astype(jnp.bfloat16),
            grad_rows,
            preferred_element_type=jnp.float32,
        )
        grad_probs = jnp.einsum(
            EQ_KGQD_NKD_TO_KGQN, grad_rows, value_rows, preferred_element_type=jnp.float32
        )
        grad_scores = (probs * (grad_probs - delta_seq[..., None])).astype(jnp.bfloat16)
        dq_seq = dq_seq + score_scale * jnp.einsum(
            EQ_KGQN_NKD_TO_KGQD, grad_scores, key_rows, preferred_element_type=jnp.float32
        )
        grad_keys = score_scale * jnp.einsum(
            EQ_KGQN_QKGD_TO_NKD, grad_scores, query_rows, preferred_element_type=jnp.float32
        )
        return (dq_seq, add_rows(dk_seq, grad_keys), add_rows(dv_seq, grad_values))

    grad_q_group, grad_k_whole, grad_v_whole = lax.map(
        back_one_sequence,
        (
            q_group,
            grad_group,
            log_total,
            delta,
            key_piece,
            value_piece,
            back_state[0],
            back_state[1],
            back_state[2],
        ),
    )
    grad_k_block, grad_v_block = (
        lax.psum_scatter(
            grad_k_whole.astype(jnp.bfloat16), BLK, scatter_dimension=1, tiled=True
        ).astype(jnp.float32),
        lax.psum_scatter(
            grad_v_whole.astype(jnp.bfloat16), BLK, scatter_dimension=1, tiled=True
        ).astype(jnp.float32),
    )
    grad_q_block = jnp.transpose(grad_q_group, (0, 3, 1, 2, 4)).reshape(
        sequence_count, block_len, local_q, HEAD_SIZE
    )
    grad_q_seq, grad_k_seq, value_sequence_gradient = (
        lax.all_to_all(
            grad_q_block.astype(jnp.bfloat16), ULY, split_axis=1, concat_axis=2, tiled=True
        ).astype(grad_q_block.dtype),
        lax.all_to_all(
            grad_k_block.astype(jnp.bfloat16), ULY, split_axis=1, concat_axis=2, tiled=True
        ).astype(grad_k_block.dtype),
        lax.all_to_all(
            grad_v_block.astype(jnp.bfloat16), ULY, split_axis=1, concat_axis=2, tiled=True
        ).astype(grad_v_block.dtype),
    )
    grad_q_normed = rotate(grad_q_seq, local_angles, -1.0)
    grad_k_normed = rotate(grad_k_seq, local_angles, -1.0)
    q_gain_term = jnp.sum(grad_q_normed * q_pre * q_scale, axis=(0, 1, 2))
    k_gain_term = jnp.sum(grad_k_normed * key_before_norm * k_scale, axis=(0, 1, 2))
    grad_q_pre = (
        norm_back(grad_q_normed, q_pre, q_scale, gain_q)
        .astype(jnp.bfloat16)
        .reshape(sequence_count, token_count, QUERY_HEADS * HEAD_SIZE)
    )
    grad_k_pre = (
        norm_back(grad_k_normed, key_before_norm, k_scale, gain_k)
        .astype(jnp.bfloat16)
        .reshape(sequence_count, token_count, KEY_VALUE_HEADS * HEAD_SIZE)
    )
    value_pre_gradient = value_sequence_gradient.astype(jnp.bfloat16).reshape(
        sequence_count, token_count, KEY_VALUE_HEADS * HEAD_SIZE
    )
    grad_query = jnp.einsum(
        EQ_STD_STE_TO_DE, normalized_input, grad_q_pre, preferred_element_type=jnp.float32
    )
    grad_key = jnp.einsum(
        EQ_STD_STE_TO_DE, normalized_input, grad_k_pre, preferred_element_type=jnp.float32
    )
    grad_value = jnp.einsum(
        EQ_STD_STE_TO_DE, normalized_input, value_pre_gradient, preferred_element_type=jnp.float32
    )
    grad_normed = jnp.einsum(EQ_STE_DE_TO_STD, grad_q_pre, wq_all, preferred_element_type=jnp.float32)
    grad_normed = grad_normed + jnp.einsum(
        EQ_STE_DE_TO_STD, grad_k_pre, wk_all, preferred_element_type=jnp.float32
    )
    grad_normed = grad_normed + jnp.einsum(
        EQ_STE_DE_TO_STD, value_pre_gradient, wv_all, preferred_element_type=jnp.float32
    )
    attn_gain_term = jnp.sum(grad_normed * source * first_scale, axis=(0, 1))
    grad_hidden = grad_middle + norm_back(
        grad_normed, source, first_scale, g_attn.astype(jnp.float32)
    )
    grad_down = jnp.einsum(EQ_STF_STD_TO_FD, activated, cotangent, preferred_element_type=jnp.float32)
    grad_attn_gain, grad_query, grad_key, grad_value, grad_out, grad_down = (
        lax.psum_scatter(attn_gain_term, EVERY, scatter_dimension=0, tiled=True),
        lax.psum_scatter(grad_query, EVERY, scatter_dimension=0, tiled=True),
        lax.psum_scatter(grad_key, EVERY, scatter_dimension=0, tiled=True),
        lax.psum_scatter(grad_value, EVERY, scatter_dimension=0, tiled=True),
        lax.psum_scatter(grad_out, EVERY, scatter_dimension=0, tiled=True),
        lax.psum_scatter(grad_down, EVERY, scatter_dimension=0, tiled=True),
    )
    grad_q_gain, grad_k_gain = lax.psum((q_gain_term, k_gain_term), EVERY)
    return (
        output,
        grad_hidden,
        grad_attn_gain,
        grad_query,
        grad_key,
        grad_value,
        grad_out,
        grad_q_gain,
        grad_k_gain,
        grad_mlp_gain,
        grad_gate,
        grad_up,
        grad_down,
    )


MESH = pl.DeviceIdType.MESH
HBM = pl.BlockSpec(memory_space=pl.ANY)
VMEM = pl.BlockSpec(memory_space=pltpu.VMEM)
MIB = 1 << 20


def kernel_params(collective_id, vmem_mib=48):
    return pltpu.CompilerParams(
        collective_id=collective_id, has_side_effects=True, vmem_limit_bytes=vmem_mib * MIB
    )


def semaphores(count, local=16):
    return [
        pltpu.SemaphoreType.DMA((count,)),
        pltpu.SemaphoreType.DMA((count,)),
        pltpu.SemaphoreType.DMA((local,)),
    ]


class Copy:
    def __init__(self, descriptor, sends, receives):
        self.descriptor, self.sends, self.receives = descriptor, sends, receives

    def under(self, condition, action):
        if condition is None:
            action()
        else:
            pl.when(condition)(action)

    def start(self):
        self.under(self.sends, lambda: self.descriptor().start())
        return self

    def sent(self):
        self.under(self.sends, lambda: self.descriptor().wait_send())

    def arrived(self):
        self.under(self.receives, lambda: self.descriptor().wait_recv())


class Links:
    def __init__(self, send, recv, here):
        self.send, self.recv, self.here = send, recv, here
        self.used, self.used_here = 0, 0
        self.copies, self.local_copies = [], []
        self.n_dp, self.n_blk, self.n_uly = (lax.axis_size(a) for a in EVERY)
        self.dp, self.blk, self.uly = (lax.axis_index(a) for a in EVERY)
        self.other_dp = 1 - self.dp
        self.across = lax.rem(self.uly + 2, 4)
        self.twin = self.uly + 1 - 2 * lax.rem(self.uly, 2)
        self.x_way = (self.other_dp, self.blk, self.uly)
        self.y_way = (self.dp, self.blk, self.across)
        self.core_way = (self.dp, self.blk, self.twin)

    def peer(self, step):
        return lax.rem(self.blk + step, self.n_blk)

    def peers(self):
        return [(self.dp, self.peer(k), self.uly) for k in range(1, self.n_blk)]

    def greet(self, devices):
        barrier = pltpu.get_barrier_semaphore()
        for device in devices:
            pl.semaphore_signal(barrier, inc=1, device_id=device, device_id_type=MESH)
        pl.semaphore_wait(barrier, len(devices))

    def remote(self, source, target, device, sends=None, receives=None):
        slot = self.used
        self.used += 1

        def descriptor():
            return pltpu.make_async_remote_copy(
                src_ref=source(),
                dst_ref=target(),
                send_sem=self.send.at[slot],
                recv_sem=self.recv.at[slot],
                device_id=device,
                device_id_type=MESH,
            )

        copy = Copy(descriptor, sends, receives)
        self.copies.append(copy)
        return copy.start()

    def to(self, source, target, device):
        return self.remote(lambda: source, lambda: target, device)

    def local(self, source, target):
        copy = pltpu.make_async_copy(source, target, self.here.at[self.used_here])
        self.used_here += 1
        copy.start()
        self.local_copies.append(copy)
        return copy

    def finish(self):
        for copy in self.copies:
            copy.sent()


class LineGather:
    def __init__(self, links, own, whole):
        self.links, self.own, self.whole = links, own, whole
        self.waiting = []

    def send(self, step):
        links, whole = self.links, self.whole
        blk, last = links.blk, links.n_blk - 1

        def block(index):
            if step == 0:
                return lambda: self.own
            return lambda: whole.at[index]

        self.waiting = [
            links.remote(
                block(blk - step),
                lambda: whole.at[blk - step],
                (links.dp, blk + 1, links.uly),
                jnp.logical_and(blk >= step, blk < last),
                blk >= step + 1,
            ),
            links.remote(
                block(blk + step),
                lambda: whole.at[blk + step],
                (links.dp, blk - 1, links.uly),
                jnp.logical_and(blk + step <= last, blk > 0),
                blk + step + 1 <= last,
            ),
        ]

    def arrived(self):
        for copy in self.waiting:
            copy.arrived()


class PlaneGather:
    def __init__(self, links, at):
        self.links, self.at = links, at

    def start(self, own=None):
        links, at = self.links, self.at
        mine = at(links.dp, links.uly)
        own = mine if own is None else own
        self.from_x = links.to(own, mine, links.x_way)
        self.from_y = links.to(own, mine, links.y_way)
        self.from_core = [links.to(own, mine, links.core_way)]

    def hand_on(self):
        links, at = self.links, self.at
        self.from_x.arrived()
        half = at(links.other_dp, links.uly, 0)
        self.second_y = links.to(half, half, links.y_way)
        self.from_y.arrived()
        half = at(links.dp, links.across, 1)
        self.second_x = links.to(half, half, links.x_way)
        for chunk in (at(links.other_dp, links.uly), at(links.dp, links.across)):
            self.from_core.append(links.to(chunk, chunk, links.core_way))

    def last(self):
        links = self.links
        self.second_y.arrived()
        self.second_x.arrived()
        chunk = self.at(links.other_dp, links.across)
        self.from_core.append(links.to(chunk, chunk, links.core_way))

    def arrived(self):
        for copy in self.from_core:
            copy.arrived()


def rows_of(whole, blocked):
    def at(dp, uly, half=None):
        part = whole.at[dp, :, uly] if blocked else whole.at[dp, uly]
        if half is None:
            return part
        depth = whole.shape[-2] // 2
        rows = pl.ds(half * depth, depth)
        return part.at[:, rows] if blocked else part.at[rows]

    return at


class ColumnSwap:
    def __init__(self, links, pieces):
        self.links, self.pieces = links, pieces
        self.incoming, self.kept = [], []

    def parts(self, blk):
        links = self.links
        for weight, whole, offset in self.pieces:
            width = weight.shape[-1] // links.n_dp // links.n_blk
            for group in range(links.n_dp):
                start = (group * links.n_blk + blk) * width
                yield (
                    weight.at[:, pl.ds(pl.multiple_of(start, 128), width)],
                    whole.at[
                        links.dp, links.blk, links.uly, :, pl.ds(offset + group * width, width)
                    ],
                )

    def start(self):
        links = self.links
        for step in range(1, links.n_blk):
            device = (links.dp, links.peer(step), links.uly)
            for source, target in self.parts(links.peer(step)):
                self.incoming.append(links.to(source, target, device))
        for source, target in self.parts(links.blk):
            self.kept.append(links.local(source, target))

    def arrived(self):
        for copy in self.kept:
            copy.wait()
        for copy in self.incoming:
            copy.arrived()


def front_kernel(
    hidden, wq, wk, wv, wo, gains, all_hidden, w_qkv, all_wo, all_gains, send, recv, here
):
    links = Links(send, recv, here)
    links.greet(links.peers() + [links.x_way, links.y_way, links.core_way])
    q_width, k_width = wq.shape[1] // links.n_blk, wk.shape[1] // links.n_blk
    swap = ColumnSwap(
        links, [(wq, w_qkv, 0), (wk, w_qkv, q_width), (wv, w_qkv, q_width + k_width)]
    )
    swap.start()
    gain_swap = []
    my_gains = all_gains.at[links.dp, links.blk, links.uly]
    for device in links.peers():
        gain_swap.append(links.to(gains, my_gains, device))
    keep = [
        links.local(gains, my_gains),
        links.local(hidden, all_hidden.at[links.blk]),
        links.local(wo, all_wo.at[links.dp, links.uly]),
    ]
    line = LineGather(links, hidden, all_hidden)
    line.send(0)
    plane_wo = PlaneGather(links, rows_of(all_wo, False))
    plane_wo.start(wo)
    plane_qkv = PlaneGather(links, rows_of(w_qkv, True))
    plane_gain = PlaneGather(links, rows_of(all_gains, True))
    swap.arrived()
    plane_qkv.start()
    keep[0].wait()
    for copy in gain_swap:
        copy.arrived()
    plane_gain.start()
    for step in range(1, links.n_blk - 1):
        line.arrived()
        line.send(step)
        if step == 1:
            plane_wo.hand_on()
    plane_qkv.hand_on()
    plane_gain.hand_on()
    plane_wo.last()
    plane_qkv.last()
    plane_gain.last()
    line.arrived()
    for plane in (plane_wo, plane_qkv, plane_gain):
        plane.arrived()
    for copy in keep[1:]:
        copy.wait()
    links.finish()


def gather_front(hidden, wq, wk, wv, wo, gains):
    n_dp, n_blk, n_uly = (lax.axis_size(a) for a in EVERY)
    qkv_width = (wq.shape[1] + wk.shape[1] + wv.shape[1]) // n_blk
    shapes = [
        (n_blk,) + hidden.shape,
        (n_dp, n_blk, n_uly, wq.shape[0], qkv_width),
        (n_dp, n_uly) + wo.shape,
        (n_dp, n_blk, n_uly) + gains.shape,
    ]
    return pl.pallas_call(
        front_kernel,
        out_shape=[jax.ShapeDtypeStruct(s, jnp.bfloat16) for s in shapes],
        in_specs=[HBM] * 6,
        out_specs=[HBM] * 4,
        scratch_shapes=semaphores(72),
        compiler_params=kernel_params(0),
    )(hidden, wq, wk, wv, wo, gains)


def feed_forward_kernel(
    wg, wu, wd, cotangent, all_wg, all_wu, all_wd, all_cot, send, recv, here
):
    links = Links(send, recv, here)
    links.greet(links.peers() + [links.x_way, links.y_way, links.core_way])
    swaps = [ColumnSwap(links, [(wg, all_wg, 0)]), ColumnSwap(links, [(wu, all_wu, 0)])]
    swaps[0].start()
    plane_wd = PlaneGather(links, rows_of(all_wd, False))
    plane_wd.start(wd)
    swaps[1].start()
    keep = [
        links.local(wd, all_wd.at[links.dp, links.uly]),
        links.local(cotangent, all_cot.at[links.blk]),
    ]
    planes = [PlaneGather(links, rows_of(w, True)) for w in (all_wg, all_wu)]
    swaps[0].arrived()
    planes[0].start()
    swaps[1].arrived()
    line = LineGather(links, cotangent, all_cot)
    line.send(0)
    planes[1].start()
    plane_wd.hand_on()
    planes[0].hand_on()
    for step in range(1, links.n_blk - 1):
        line.arrived()
        line.send(step)
        if step == 1:
            plane_wd.last()
            planes[1].hand_on()
            planes[0].last()
    planes[1].last()
    line.arrived()
    for plane in [plane_wd] + planes:
        plane.arrived()
    for copy in keep:
        copy.wait()
    links.finish()


def gather_feed_forward(wg, wu, wd, cotangent):
    n_dp, n_blk, n_uly = (lax.axis_size(a) for a in EVERY)
    shapes = [
        (n_dp, n_blk, n_uly, wg.shape[0], wg.shape[1] // n_blk),
        (n_dp, n_blk, n_uly, wu.shape[0], wu.shape[1] // n_blk),
        (n_dp, n_uly) + wd.shape,
        (n_blk,) + cotangent.shape,
    ]
    return pl.pallas_call(
        feed_forward_kernel,
        out_shape=[jax.ShapeDtypeStruct(s, jnp.bfloat16) for s in shapes],
        in_specs=[HBM] * 4,
        out_specs=[HBM] * 4,
        scratch_shapes=semaphores(56),
        compiler_params=kernel_params(1),
    )(wg, wu, wd, cotangent)


ROWS = 32


def each_block(count, body):
    def step(index, carry):
        body(pl.ds(pl.multiple_of(index * ROWS, ROWS), ROWS))
        return carry

    lax.fori_loop(0, count // ROWS, step, 0)


def middle_kernel(
    heads, wo, source, gain, middle, all_normed, parts, incoming, normed, send, recv, here
):
    links = Links(send, recv, here)
    links.greet(links.peers())
    tokens = source.shape[0]
    copies = []
    for step in range(1, links.n_blk):
        parts[step - 1] = jnp.dot(
            heads[links.peer(step)], wo[...], preferred_element_type=jnp.float32
        ).astype(jnp.bfloat16)
        copies.append(
            links.to(
                parts.at[step - 1],
                incoming.at[step - 1],
                (links.dp, links.peer(step), links.uly),
            )
        )
    middle[...] = jnp.dot(heads[links.blk], wo[...], preferred_element_type=jnp.float32)
    for copy in copies:
        copy.arrived()

    def body(rows):
        total = middle[rows, :] + source[rows, :].astype(jnp.float32)
        for step in range(links.n_blk - 1):
            total = total + incoming[step, rows, :].astype(jnp.float32)
        middle[rows, :] = total
        scale = rms_scale(total)
        normed[rows, :] = (total * scale * gain[...]).astype(jnp.bfloat16)

    each_block(tokens, body)
    keep = links.local(normed, all_normed.at[links.blk])
    line = LineGather(links, normed, all_normed)
    for step in range(links.n_blk - 1):
        line.send(step)
        line.arrived()
    keep.wait()
    links.finish()


def exchange_middle(heads, wo, source, gain):
    n_blk = lax.axis_size(BLK)
    tokens, width = source.shape
    return pl.pallas_call(
        middle_kernel,
        out_shape=[
            jax.ShapeDtypeStruct((tokens, width), jnp.float32),
            jax.ShapeDtypeStruct((n_blk, tokens, width), jnp.bfloat16),
        ],
        in_specs=[VMEM] * 4,
        out_specs=[VMEM, HBM],
        scratch_shapes=[
            pltpu.VMEM((n_blk - 1, tokens, width), jnp.bfloat16),
            pltpu.VMEM((n_blk - 1, tokens, width), jnp.bfloat16),
            pltpu.VMEM((tokens, width), jnp.bfloat16),
        ]
        + semaphores(16),
        compiler_params=kernel_params(2),
    )(heads, wo, source, gain)


def back_rows(grad_normed, source, gain, gain_term):
    scale = rms_scale(source)
    unit = source * scale
    gain_term[...] += jnp.sum(grad_normed * unit, axis=0, keepdims=True)
    scaled = grad_normed * gain
    return scale * (scaled - unit * jnp.mean(scaled * unit, axis=-1, keepdims=True))


def back_kernel(
    grad_parts,
    out_parts,
    middle,
    cotangent,
    gain,
    output,
    grad_middle,
    gain_term,
    all_low,
    grad_in,
    out_in,
    own_grad,
    own_out,
    low,
    send,
    recv,
    here,
):
    links = Links(send, recv, here)
    links.greet(links.peers())
    tokens = middle.shape[0]
    copies, out_copies = [], []
    for parts, target, log in ((grad_parts, grad_in, copies), (out_parts, out_in, out_copies)):
        for step in range(1, links.n_blk):
            peer = links.peer(step)
            log.append(
                links.to(parts.at[peer], target.at[step - 1], (links.dp, peer, links.uly))
            )
    keep = [
        links.local(grad_parts.at[links.blk], own_grad),
        links.local(out_parts.at[links.blk], own_out),
    ]
    gain_term[...] = jnp.zeros_like(gain_term)
    keep[0].wait()
    for copy in copies:
        copy.arrived()

    def body(rows):
        total = own_grad[rows, :].astype(jnp.float32)
        for step in range(links.n_blk - 1):
            total = total + grad_in[step, rows, :].astype(jnp.float32)
        grad = cotangent[rows, :].astype(jnp.float32) + back_rows(
            total, middle[rows, :], gain[...], gain_term
        )
        grad_middle[rows, :] = grad
        low[rows, :] = grad.astype(jnp.bfloat16)

    each_block(tokens, body)
    keep.append(links.local(low, all_low.at[links.blk]))
    line = LineGather(links, low, all_low)
    line.send(0)
    keep[1].wait()
    for copy in out_copies:
        copy.arrived()

    def add_output(rows):
        total = middle[rows, :] + own_out[rows, :].astype(jnp.float32)
        for step in range(links.n_blk - 1):
            total = total + out_in[step, rows, :].astype(jnp.float32)
        output[rows, :] = total.astype(jnp.bfloat16)

    each_block(tokens, add_output)
    line.arrived()
    for step in range(1, links.n_blk - 1):
        line.send(step)
        line.arrived()
    keep[2].wait()
    links.finish()


def exchange_back(grad_parts, out_parts, middle, cotangent, gain):
    n_blk, tokens, width = grad_parts.shape
    several = pltpu.VMEM((n_blk - 1, tokens, width), jnp.bfloat16)
    one = pltpu.VMEM((tokens, width), jnp.bfloat16)
    return pl.pallas_call(
        back_kernel,
        out_shape=[
            jax.ShapeDtypeStruct((tokens, width), jnp.bfloat16),
            jax.ShapeDtypeStruct((tokens, width), jnp.float32),
            jax.ShapeDtypeStruct((1, width), jnp.float32),
            jax.ShapeDtypeStruct((n_blk, tokens, width), jnp.bfloat16),
        ],
        in_specs=[HBM, HBM, VMEM, VMEM, VMEM],
        out_specs=[VMEM, VMEM, VMEM, HBM],
        scratch_shapes=[several, several, one, one, one] + semaphores(16),
        compiler_params=kernel_params(3),
    )(grad_parts, out_parts, middle, cotangent, gain)


def last_kernel(
    grad_parts, source, grad_middle, gain, grad_hidden, gain_term, grad_in, own, send, recv, here
):
    links = Links(send, recv, here)
    links.greet(links.peers())
    copies = []
    for step in range(1, links.n_blk):
        peer = links.peer(step)
        copies.append(
            links.to(grad_parts.at[peer], grad_in.at[step - 1], (links.dp, peer, links.uly))
        )
    keep = links.local(grad_parts.at[links.blk], own)
    gain_term[...] = jnp.zeros_like(gain_term)
    keep.wait()
    for copy in copies:
        copy.arrived()

    def body(rows):
        total = own[rows, :].astype(jnp.float32)
        for step in range(links.n_blk - 1):
            total = total + grad_in[step, rows, :].astype(jnp.float32)
        grad_hidden[rows, :] = grad_middle[rows, :] + back_rows(
            total, source[rows, :].astype(jnp.float32), gain[...], gain_term
        )

    each_block(source.shape[0], body)
    links.finish()


def exchange_last(grad_parts, source, grad_middle, gain):
    n_blk, tokens, width = grad_parts.shape
    return pl.pallas_call(
        last_kernel,
        out_shape=[
            jax.ShapeDtypeStruct((tokens, width), jnp.float32),
            jax.ShapeDtypeStruct((1, width), jnp.float32),
        ],
        in_specs=[HBM, VMEM, VMEM, VMEM],
        out_specs=[VMEM, VMEM],
        scratch_shapes=[
            pltpu.VMEM((n_blk - 1, tokens, width), jnp.bfloat16),
            pltpu.VMEM((tokens, width), jnp.bfloat16),
        ]
        + semaphores(8),
        compiler_params=kernel_params(4),
    )(grad_parts, source, grad_middle, gain)


def permute_features(rows):
    n_dp, n_blk, n_uly = (lax.axis_size(a) for a in EVERY)
    split = rows.reshape(rows.shape[0], n_dp, n_blk, n_uly, -1)
    return jnp.swapaxes(split, 2, 3).reshape(rows.shape)


def give_columns(grad):
    n_blk = lax.axis_size(BLK)
    summed = lax.psum_scatter(grad.astype(jnp.bfloat16), PLANE, scatter_dimension=0, tiled=True)
    split = summed.reshape(n_blk, -1, grad.shape[1])
    return lax.all_to_all(split, BLK, split_axis=0, concat_axis=0)


def place_columns(blocks, n_dp):
    n_blk, rows, _ = blocks.shape
    split = blocks.reshape(n_blk, rows, n_dp, -1)
    return jnp.transpose(split, (1, 2, 0, 3)).reshape(rows, -1).astype(jnp.float32)


def give_rows(grad):
    return lax.psum_scatter(
        grad.astype(jnp.bfloat16), PLANE, scatter_dimension=0, tiled=True
    ).astype(jnp.float32)


def product(left, right):
    return jnp.dot(left, right, preferred_element_type=jnp.float32)


def product_right(left, right):
    return lax.dot_general(
        left, right, (((1,), (1,)), ((), ())), preferred_element_type=jnp.float32
    )


def product_left(left, right):
    return lax.dot_general(
        left, right, (((0,), (0,)), ((), ())), preferred_element_type=jnp.float32
    )


def shards(
    hidden,
    span_order,
    attn_gain,
    w_query,
    key_weight,
    value_weight,
    w_out,
    q_gain,
    k_gain,
    mlp_gain,
    w_gate,
    w_up,
    w_down,
    cotangent,
):
    seqs, toks, width = hidden.shape
    n_dp, n_blk, n_uly = (lax.axis_size(a) for a in EVERY)
    blk_index = lax.axis_index(BLK)
    uly_index = lax.axis_index(ULY)
    local_q = QUERY_HEADS // n_blk
    local_kv = KEY_VALUE_HEADS // n_blk
    group = QUERY_HEADS // KEY_VALUE_HEADS
    half_len = toks * n_uly // 2
    score_scale = 1.0 / math.sqrt(HEAD_SIZE)
    rows = n_blk * seqs * toks
    f32, bf16 = jnp.float32, jnp.bfloat16
    own_hidden = hidden.reshape(seqs * toks, width)
    own_cotangent = cotangent.reshape(seqs * toks, width)

    def places(u):
        return (
            (jnp.arange(n_blk, dtype=jnp.int32)[:, None] * n_uly + u) * toks
            + jnp.arange(toks, dtype=jnp.int32)[None, :]
        )

    query_pos = positions_of(places(uly_index).reshape(-1), span_order, half_len)
    key_pos = jnp.concatenate(
        [positions_of(places(u).reshape(-1), span_order, half_len) for u in range(n_uly)]
    )
    angles = angles_of(query_pos, HEAD_SIZE).reshape(n_blk, 1, toks, HEAD_SIZE // 2)
    angles = jnp.broadcast_to(angles, (n_blk, seqs, toks, HEAD_SIZE // 2)).reshape(rows, -1)

    gain_rows = attn_gain.shape[0]
    own_gains = jnp.pad(jnp.stack([attn_gain, mlp_gain]), ((0, 14), (0, 128 - gain_rows)))
    all_hidden, w_qkv, wo, all_gains = gather_front(
        own_hidden, w_query, key_weight, value_weight, w_out, own_gains
    )
    all_wg, all_wu, all_wd, cot = gather_feed_forward(w_gate, w_up, w_down, own_cotangent)
    gains = all_gains[..., :2, :gain_rows].astype(f32)
    g_attn = gains[..., 0, :].reshape(1, width)
    g_mlp = gains[..., 1, :].reshape(1, width)
    w_qkv = w_qkv.reshape(width, -1)
    wo = wo.reshape(-1, width)
    wg, wu = all_wg.reshape(width, -1), all_wu.reshape(width, -1)
    wd = all_wd.reshape(-1, width)
    cot = cot.reshape(rows, width)

    source = all_hidden.reshape(rows, width).astype(f32)
    first_scale = rms_scale(source)
    normed = (source * first_scale * g_attn).astype(bf16)
    qkv = product(normed, w_qkv)
    q_end = local_q * HEAD_SIZE
    k_end = q_end + local_kv * HEAD_SIZE
    q_pre = qkv[:, :q_end].reshape(rows, local_q, HEAD_SIZE)
    k_pre = qkv[:, q_end:k_end].reshape(rows, local_kv, HEAD_SIZE)
    v_pre = qkv[:, k_end:].reshape(rows, local_kv, HEAD_SIZE)
    q_scale, k_scale = rms_scale(q_pre), rms_scale(k_pre)
    gain_q, gain_k = q_gain.astype(f32), k_gain.astype(f32)
    q_rot = rotate(q_pre * q_scale * gain_q, angles, 1.0).astype(bf16)
    k_rot = rotate(k_pre * k_scale * gain_k, angles, 1.0).astype(bf16)
    v_low = v_pre.astype(bf16)

    def by_head(x):
        heads = x.shape[1]
        x = x.reshape(n_blk, seqs, toks, heads, HEAD_SIZE)
        return jnp.transpose(x, (1, 3, 0, 2, 4)).reshape(seqs, heads, n_blk * toks, HEAD_SIZE)

    def from_head(x):
        heads = x.shape[1]
        x = x.reshape(seqs, heads, n_blk, toks, HEAD_SIZE)
        return jnp.transpose(x, (2, 0, 3, 1, 4)).reshape(rows, heads, HEAD_SIZE)

    q_len = n_blk * toks
    kv = jnp.stack([by_head(k_rot), by_head(v_low)])
    kv_all = lax.all_gather(kv, ULY, axis=3, tiled=True)
    keys, values = kv_all[0], kv_all[1]
    queries = by_head(q_rot).reshape(seqs, local_kv, group, q_len, HEAD_SIZE)
    allowed = query_pos[:, None] >= key_pos[None, :]
    scores = (
        jnp.einsum(EQ_SCORES, queries, keys, preferred_element_type=f32) * score_scale
    )
    scores = jnp.where(allowed, scores, -jnp.inf)
    top = jnp.max(scores, axis=-1, keepdims=True)
    weights = jnp.exp(scores - top)
    total = jnp.sum(weights, axis=-1, keepdims=True)
    lse = top + jnp.log(total)
    attended = (
        jnp.einsum(EQ_ATTEND, weights.astype(bf16), values, preferred_element_type=f32) / total
    )
    heads_flat = from_head(
        attended.astype(bf16).reshape(seqs, local_q, q_len, HEAD_SIZE)
    ).reshape(rows, local_q * HEAD_SIZE)

    middle, normed2 = exchange_middle(
        heads_flat.reshape(n_blk, seqs * toks, -1), wo, own_hidden, g_mlp
    )
    normed2 = normed2.reshape(rows, width)
    gate_pre = product(normed2, wg)
    up_pre = product(normed2, wu)
    sigmoid_gate = jax.nn.sigmoid(gate_pre)
    activated = (gate_pre * sigmoid_gate * up_pre).astype(bf16)
    out_parts = product(activated, wd).astype(bf16)
    grad_act = product_right(cot, wd)
    grad_gate_pre = (
        grad_act * up_pre * sigmoid_gate * (1.0 + gate_pre * (1.0 - sigmoid_gate))
    ).astype(bf16)
    grad_up_pre = (grad_act * gate_pre * sigmoid_gate).astype(bf16)
    grad_parts = (product_right(grad_gate_pre, wg) + product_right(grad_up_pre, wu)).astype(bf16)
    blocks = (n_blk, seqs * toks, width)
    output, grad_middle, mlp_gain_term, middle_low = exchange_back(
        grad_parts.reshape(blocks), out_parts.reshape(blocks), middle, own_cotangent, g_mlp
    )
    normed2_swapped = permute_features(normed2)
    grad_gate = place_columns(give_columns(product_left(normed2_swapped, grad_gate_pre)), n_dp)
    grad_up = place_columns(give_columns(product_left(normed2_swapped, grad_up_pre)), n_dp)
    grad_down = give_rows(product_left(activated, cot))
    middle_low = middle_low.reshape(rows, width)
    grad_out = give_rows(product_left(heads_flat, middle_low))
    grad_heads = by_head(
        product_right(middle_low, wo).astype(bf16).reshape(rows, local_q, HEAD_SIZE)
    ).reshape(seqs, local_kv, group, q_len, HEAD_SIZE)
    delta = jnp.sum(grad_heads.astype(f32) * attended, axis=-1, keepdims=True)
    probs = jnp.exp(scores - lse)
    grad_values = jnp.einsum(EQ_TO_KEYS, probs.astype(bf16), grad_heads, preferred_element_type=f32)
    grad_probs = jnp.einsum(EQ_SCORES, grad_heads, values, preferred_element_type=f32)
    grad_scores = (probs * (grad_probs - delta)).astype(bf16)
    grad_queries = score_scale * jnp.einsum(
        EQ_ATTEND, grad_scores, keys, preferred_element_type=f32
    )
    grad_keys = score_scale * jnp.einsum(
        EQ_TO_KEYS, grad_scores, queries, preferred_element_type=f32
    )
    grad_kv = lax.psum_scatter(
        jnp.stack([grad_keys, grad_values]).astype(bf16), ULY, scatter_dimension=3, tiled=True
    ).astype(f32)
    grad_q_normed = rotate(
        from_head(grad_queries.reshape(seqs, local_q, q_len, HEAD_SIZE)), angles, -1.0
    )
    grad_k_normed = rotate(from_head(grad_kv[0]), angles, -1.0)
    q_gain_term = jnp.sum(grad_q_normed * q_pre * q_scale, axis=(0, 1))
    k_gain_term = jnp.sum(grad_k_normed * k_pre * k_scale, axis=(0, 1))
    grad_q_pre = norm_back(grad_q_normed, q_pre, q_scale, gain_q).astype(bf16)
    grad_k_pre = norm_back(grad_k_normed, k_pre, k_scale, gain_k).astype(bf16)
    grad_v_pre = from_head(grad_kv[1]).astype(bf16)
    grad_qkv = jnp.concatenate(
        [g.reshape(rows, -1) for g in (grad_q_pre, grad_k_pre, grad_v_pre)], axis=-1
    )
    last_parts = product_right(grad_qkv, w_qkv).astype(bf16)
    grad_hidden, attn_gain_term = exchange_last(
        last_parts.reshape(blocks), own_hidden, grad_middle, g_attn
    )
    grad_w_qkv = give_columns(product_left(permute_features(normed), grad_qkv))
    grad_query = place_columns(grad_w_qkv[..., :q_end], n_dp)
    grad_key = place_columns(grad_w_qkv[..., q_end:k_end], n_dp)
    grad_value = place_columns(grad_w_qkv[..., k_end:], n_dp)
    small = lax.psum(
        jnp.concatenate([attn_gain_term[0], mlp_gain_term[0], q_gain_term, k_gain_term]), EVERY
    )
    gain_at = ((lax.axis_index(DP) * n_blk + blk_index) * n_uly + uly_index) * gain_rows
    grad_attn_gain = lax.dynamic_slice(small, (gain_at,), (gain_rows,))
    grad_mlp_gain = lax.dynamic_slice(small, (width + gain_at,), (gain_rows,))
    grad_q_gain = small[2 * width : 2 * width + HEAD_SIZE]
    grad_k_gain = small[2 * width + HEAD_SIZE :]
    return (
        output.reshape(hidden.shape),
        grad_hidden.reshape(hidden.shape),
        grad_attn_gain,
        grad_query,
        grad_key,
        grad_value,
        grad_out,
        grad_q_gain,
        grad_k_gain,
        grad_mlp_gain,
        grad_gate,
        grad_up,
        grad_down,
    )


def solution(mesh):
    n_dp, n_blk, n_uly = (mesh.shape[a] for a in EVERY)
    aligned = (n_dp, n_uly) == (2, 4) and KEY_VALUE_HEADS % (n_dp * n_blk) == 0
    in_specs = (
        TOKENS,
        P(),
        P(EVERY),
        P(EVERY, None),
        P(EVERY, None),
        P(EVERY, None),
        P(EVERY, None),
        P(),
        P(),
        P(EVERY),
        P(EVERY, None),
        P(EVERY, None),
        P(EVERY, None),
        TOKENS,
    )
    out_specs = (
        TOKENS,
        TOKENS,
        P(EVERY),
        P(EVERY, None),
        P(EVERY, None),
        P(EVERY, None),
        P(EVERY, None),
        P(),
        P(),
        P(EVERY),
        P(EVERY, None),
        P(EVERY, None),
        P(EVERY, None),
    )
    return jax.shard_map(
        shards if aligned else shards_general,
        mesh=mesh, in_specs=in_specs, out_specs=out_specs, check_vma=False)
```

```python
import math

import jax
import jax.numpy as jnp
from jax import lax
from jax.experimental import pallas as pl
from jax.experimental.pallas import tpu as pltpu
from jax.sharding import PartitionSpec as P

QUERY_HEADS = 16
KEY_VALUE_HEADS = 8
HEAD_SIZE = 128


DP, BLK, ULY = "dp", "blk", "uly"
EVERY = (DP, BLK, ULY)
PLANE = (DP, ULY)
TOKENS = P(DP, (BLK, ULY), None)
EQ_SCORES = "skgqd,sknd->skgqn"
EQ_ATTEND = "skgqn,sknd->skgqd"
EQ_TO_KEYS = "skgqn,skgqd->sknd"
EQ_KGQD_NKD_TO_KGQN = "kgqd,nkd->kgqn"
EQ_KGQN_KGQD_TO_NKD = "kgqn,kgqd->nkd"
EQ_KGQN_NKD_TO_KGQD = "kgqn,nkd->kgqd"
EQ_KGQN_QKGD_TO_NKD = "kgqn,qkgd->nkd"
EQ_QKGD_NKD_TO_KGQN = "qkgd,nkd->kgqn"
EQ_STD_DE_TO_STE = "std,de->ste"
EQ_STD_DF_TO_STF = "std,df->stf"
EQ_STD_ED_TO_STE = "std,ed->ste"
EQ_STD_FD_TO_STF = "std,fd->stf"
EQ_STD_STE_TO_DE = "std,ste->de"
EQ_STD_STF_TO_DF = "std,stf->df"
EQ_STE_DE_TO_STD = "ste,de->std"
EQ_STE_ED_TO_STD = "ste,ed->std"
EQ_STE_STD_TO_ED = "ste,std->ed"
EQ_STF_DF_TO_STD = "stf,df->std"
EQ_STF_FD_TO_STD = "stf,fd->std"
EQ_STF_STD_TO_FD = "stf,std->fd"

EPSILON = 1e-06
ROPE_BASE = 1000000.0


def rms_scale(source):
    return lax.rsqrt(jnp.mean(source * source, axis=-1, keepdims=True) + EPSILON)


def norm_back(grad_normed, source, norm_scale, gain):
    unit_rows = source * norm_scale
    scaled = grad_normed * gain
    return norm_scale * (scaled - unit_rows * jnp.mean(scaled * unit_rows, axis=-1, keepdims=True))


def angles_of(positions, head_dim):
    freq_steps = jnp.arange(head_dim // 2, dtype=jnp.float32)
    inverse = jnp.exp(freq_steps * (-2.0 * math.log(ROPE_BASE) / head_dim))
    return positions.astype(jnp.float32)[:, None] * inverse[None, :]


def rotate(source, angles, direction):
    half_dim = source.shape[-1] // 2
    cosine = jnp.cos(angles)[:, None, :]
    sine_part = direction * jnp.sin(angles)[:, None, :]
    first_half = source[..., :half_dim]
    second_half = source[..., half_dim:]
    return jnp.concatenate(
        [
            first_half * cosine - second_half * sine_part,
            second_half * cosine + first_half * sine_part,
        ],
        axis=-1,
    )


def positions_of(places, span_order, half_len):
    blocks_of = places // half_len
    block_ids = jnp.arange(span_order.shape[0], dtype=jnp.int32)
    chosen = jnp.sum(
        jnp.where(blocks_of[:, None] == block_ids[None, :], span_order[None, :], 0), axis=1
    )
    return chosen * half_len + places % half_len


def add_rows(buffer, new_rows):
    return buffer + new_rows


def shards_general(
    hidden,
    span_order,
    attn_gain,
    w_query,
    key_weight,
    value_weight,
    w_out,
    q_gain,
    k_gain,
    mlp_gain,
    w_gate,
    w_up,
    w_down,
    cotangent,
):
    sequence_count = hidden.shape[0]
    token_count = hidden.shape[1]
    ulysses_group_size = lax.axis_size(ULY)
    local_q = QUERY_HEADS // ulysses_group_size
    local_key_value = KEY_VALUE_HEADS // ulysses_group_size
    query_group_width = QUERY_HEADS // KEY_VALUE_HEADS
    block_len = token_count * ulysses_group_size
    half_len = block_len // 2
    score_scale = 1.0 / math.sqrt(HEAD_SIZE)
    blk_index = lax.axis_index(BLK)
    uly_index = lax.axis_index(ULY)
    first_place = (blk_index * ulysses_group_size + uly_index) * token_count
    local_angles = angles_of(
        positions_of(first_place + jnp.arange(token_count, dtype=jnp.int32), span_order, half_len),
        HEAD_SIZE,
    )
    query_pos = positions_of(
        blk_index * block_len + jnp.arange(block_len, dtype=jnp.int32), span_order, half_len
    )
    g_attn, wq_all, wk_all, wv_all, wo_all = (
        lax.all_gather(attn_gain, EVERY, axis=0, tiled=True),
        lax.all_gather(w_query, EVERY, axis=0, tiled=True),
        lax.all_gather(key_weight, EVERY, axis=0, tiled=True),
        lax.all_gather(value_weight, EVERY, axis=0, tiled=True),
        lax.all_gather(w_out, EVERY, axis=0, tiled=True),
    )
    source = hidden.astype(jnp.float32)
    first_scale = rms_scale(source)
    normalized_input = (source * first_scale * g_attn.astype(jnp.float32)).astype(jnp.bfloat16)
    q_pre = jnp.einsum(
        EQ_STD_DE_TO_STE, normalized_input, wq_all, preferred_element_type=jnp.float32
    ).reshape(sequence_count, token_count, QUERY_HEADS, HEAD_SIZE)
    key_before_norm = jnp.einsum(
        EQ_STD_DE_TO_STE, normalized_input, wk_all, preferred_element_type=jnp.float32
    ).reshape(sequence_count, token_count, KEY_VALUE_HEADS, HEAD_SIZE)
    value_before_norm = jnp.einsum(
        EQ_STD_DE_TO_STE, normalized_input, wv_all, preferred_element_type=jnp.float32
    ).reshape(sequence_count, token_count, KEY_VALUE_HEADS, HEAD_SIZE)
    q_scale = rms_scale(q_pre)
    k_scale = rms_scale(key_before_norm)
    gain_q = q_gain.astype(jnp.float32)
    gain_k = k_gain.astype(jnp.float32)
    q_rot = rotate(q_pre * q_scale * gain_q, local_angles, 1.0).astype(jnp.bfloat16)
    k_rot = rotate(key_before_norm * k_scale * gain_k, local_angles, 1.0).astype(jnp.bfloat16)
    v_low = value_before_norm.astype(jnp.bfloat16)
    q_heads, k_heads, v_heads = (
        lax.all_to_all(q_rot, ULY, split_axis=2, concat_axis=1, tiled=True),
        lax.all_to_all(k_rot, ULY, split_axis=2, concat_axis=1, tiled=True),
        lax.all_to_all(v_low, ULY, split_axis=2, concat_axis=1, tiled=True),
    )
    q_group = q_heads.reshape(
        sequence_count, block_len, local_key_value, query_group_width, HEAD_SIZE
    )
    stat_shape = (sequence_count, local_key_value, query_group_width, block_len)
    start_state = (
        jnp.full(stat_shape, -1e30, jnp.float32),
        jnp.zeros(stat_shape, jnp.float32),
        jnp.zeros(stat_shape + (HEAD_SIZE,), jnp.float32),
    )
    key_piece = lax.all_gather(k_heads, BLK, axis=1, tiled=True)
    value_piece = lax.all_gather(v_heads, BLK, axis=1, tiled=True)
    key_pos = positions_of(jnp.arange(key_piece.shape[1], dtype=jnp.int32), span_order, half_len)
    allowed = query_pos[:, None] >= key_pos[None, :]

    def attend_one_sequence(members):
        query_rows, key_rows, value_rows, top_seq, total_seq, accum_seq = members
        scores = (
            jnp.einsum(EQ_QKGD_NKD_TO_KGQN, query_rows, key_rows, preferred_element_type=jnp.float32)
            * score_scale
        )
        scores = jnp.where(allowed, scores, -jnp.inf)
        new_top = jnp.maximum(top_seq, jnp.max(scores, axis=-1))
        fading = jnp.exp(top_seq - new_top)
        weights = jnp.exp(scores - new_top[..., None])
        total_seq = total_seq * fading + jnp.sum(weights, axis=-1)
        accum_seq = accum_seq * fading[..., None] + jnp.einsum(
            EQ_KGQN_NKD_TO_KGQD,
            weights.astype(jnp.bfloat16),
            value_rows,
            preferred_element_type=jnp.float32,
        )
        return (new_top, total_seq, accum_seq)

    row_top, row_total, accum = lax.map(
        attend_one_sequence,
        (q_group, key_piece, value_piece, start_state[0], start_state[1], start_state[2]),
    )
    log_total = row_top + jnp.log(row_total)
    attention_output = jnp.transpose(accum / row_total[..., None], (0, 3, 1, 2, 4)).reshape(
        sequence_count, block_len, local_q, HEAD_SIZE
    )
    heads_seq = lax.all_to_all(
        attention_output.astype(jnp.bfloat16), ULY, split_axis=1, concat_axis=2, tiled=True
    )
    heads_flat = heads_seq.reshape(sequence_count, token_count, QUERY_HEADS * HEAD_SIZE)
    middle = source + jnp.einsum(
        EQ_STE_ED_TO_STD, heads_flat, wo_all, preferred_element_type=jnp.float32
    )
    g_mlp, wg_all, wu_all, wd_all = (
        lax.all_gather(mlp_gain, EVERY, axis=0, tiled=True),
        lax.all_gather(w_gate, EVERY, axis=0, tiled=True),
        lax.all_gather(w_up, EVERY, axis=0, tiled=True),
        lax.all_gather(w_down, EVERY, axis=0, tiled=True),
    )
    second_scale = rms_scale(middle)
    gain_mlp = g_mlp.astype(jnp.float32)
    normed2 = (middle * second_scale * gain_mlp).astype(jnp.bfloat16)
    gate_pre = jnp.einsum(EQ_STD_DF_TO_STF, normed2, wg_all, preferred_element_type=jnp.float32)
    up_pre = jnp.einsum(EQ_STD_DF_TO_STF, normed2, wu_all, preferred_element_type=jnp.float32)
    sigmoid_gate = jax.nn.sigmoid(gate_pre)
    activated = (gate_pre * sigmoid_gate * up_pre).astype(jnp.bfloat16)
    result = middle + jnp.einsum(
        EQ_STF_FD_TO_STD, activated, wd_all, preferred_element_type=jnp.float32
    )
    output = result.astype(jnp.bfloat16)
    g_mlp, wg_all, wu_all, wd_all = (
        lax.all_gather(mlp_gain, EVERY, axis=0, tiled=True),
        lax.all_gather(w_gate, EVERY, axis=0, tiled=True),
        lax.all_gather(w_up, EVERY, axis=0, tiled=True),
        lax.all_gather(w_down, EVERY, axis=0, tiled=True),
    )
    gain_mlp = g_mlp.astype(jnp.float32)
    grad_act = jnp.einsum(EQ_STD_FD_TO_STF, cotangent, wd_all, preferred_element_type=jnp.float32)
    grad_gate_pre = (
        grad_act * up_pre * sigmoid_gate * (1.0 + gate_pre * (1.0 - sigmoid_gate))
    ).astype(jnp.bfloat16)
    grad_up_pre = (grad_act * gate_pre * sigmoid_gate).astype(jnp.bfloat16)
    grad_gate = jnp.einsum(
        EQ_STD_STF_TO_DF, normed2, grad_gate_pre, preferred_element_type=jnp.float32
    )
    grad_up = jnp.einsum(EQ_STD_STF_TO_DF, normed2, grad_up_pre, preferred_element_type=jnp.float32)
    grad_normed2 = jnp.einsum(
        EQ_STF_DF_TO_STD, grad_gate_pre, wg_all, preferred_element_type=jnp.float32
    ) + jnp.einsum(EQ_STF_DF_TO_STD, grad_up_pre, wu_all, preferred_element_type=jnp.float32)
    mlp_gain_term = jnp.sum(grad_normed2 * middle * second_scale, axis=(0, 1))
    grad_middle = cotangent.astype(jnp.float32) + norm_back(
        grad_normed2, middle, second_scale, gain_mlp
    )
    grad_mlp_gain, grad_gate, grad_up = (
        lax.psum_scatter(mlp_gain_term, EVERY, scatter_dimension=0, tiled=True),
        lax.psum_scatter(grad_gate, EVERY, scatter_dimension=0, tiled=True),
        lax.psum_scatter(grad_up, EVERY, scatter_dimension=0, tiled=True),
    )
    g_attn, wq_all, wk_all, wv_all, wo_all = (
        lax.all_gather(attn_gain, EVERY, axis=0, tiled=True),
        lax.all_gather(w_query, EVERY, axis=0, tiled=True),
        lax.all_gather(key_weight, EVERY, axis=0, tiled=True),
        lax.all_gather(value_weight, EVERY, axis=0, tiled=True),
        lax.all_gather(w_out, EVERY, axis=0, tiled=True),
    )
    middle_low = grad_middle.astype(jnp.bfloat16)
    grad_out = jnp.einsum(EQ_STE_STD_TO_ED, heads_flat, middle_low, preferred_element_type=jnp.float32)
    grad_heads = (
        jnp.einsum(EQ_STD_ED_TO_STE, middle_low, wo_all, preferred_element_type=jnp.float32)
        .astype(jnp.bfloat16)
        .reshape(sequence_count, token_count, QUERY_HEADS, HEAD_SIZE)
    )
    grad_heads_local = lax.all_to_all(grad_heads, ULY, split_axis=2, concat_axis=1, tiled=True)
    grad_group = jnp.transpose(
        grad_heads_local.reshape(
            sequence_count, block_len, local_key_value, query_group_width, HEAD_SIZE
        ),
        (0, 2, 3, 1, 4),
    )
    delta = jnp.sum(grad_heads_local.astype(jnp.float32) * attention_output, axis=-1)
    delta = jnp.transpose(
        delta.reshape(sequence_count, block_len, local_key_value, query_group_width), (0, 2, 3, 1)
    )
    seq_length = block_len * lax.axis_size(BLK)
    zero_keys = jnp.zeros((sequence_count, seq_length, local_key_value, HEAD_SIZE), jnp.float32)
    back_state = (jnp.zeros(stat_shape + (HEAD_SIZE,), jnp.float32), zero_keys, zero_keys)
    key_piece = lax.all_gather(k_heads, BLK, axis=1, tiled=True)
    value_piece = lax.all_gather(v_heads, BLK, axis=1, tiled=True)
    key_pos = positions_of(jnp.arange(key_piece.shape[1], dtype=jnp.int32), span_order, half_len)
    back_allowed = query_pos[:, None] >= key_pos[None, :]

    def back_one_sequence(members):
        query_rows, grad_rows, lse_seq, delta_seq, key_rows, value_rows, dq_seq, dk_seq, dv_seq = (
            members
        )
        scores = (
            jnp.einsum(EQ_QKGD_NKD_TO_KGQN, query_rows, key_rows, preferred_element_type=jnp.float32)
            * score_scale
        )
        scores = jnp.where(back_allowed, scores, -jnp.inf)
        probs = jnp.exp(scores - lse_seq[..., None])
        grad_values = jnp.einsum(
            EQ_KGQN_KGQD_TO_NKD,
            probs.astype(jnp.bfloat16),
            grad_rows,
            preferred_element_type=jnp.float32,
        )
        grad_probs = jnp.einsum(
            EQ_KGQD_NKD_TO_KGQN, grad_rows, value_rows, preferred_element_type=jnp.float32
        )
        grad_scores = (probs * (grad_probs - delta_seq[..., None])).astype(jnp.bfloat16)
        dq_seq = dq_seq + score_scale * jnp.einsum(
            EQ_KGQN_NKD_TO_KGQD, grad_scores, key_rows, preferred_element_type=jnp.float32
        )
        grad_keys = score_scale * jnp.einsum(
            EQ_KGQN_QKGD_TO_NKD, grad_scores, query_rows, preferred_element_type=jnp.float32
        )
        return (dq_seq, add_rows(dk_seq, grad_keys), add_rows(dv_seq, grad_values))

    grad_q_group, grad_k_whole, grad_v_whole = lax.map(
        back_one_sequence,
        (
            q_group,
            grad_group,
            log_total,
            delta,
            key_piece,
            value_piece,
            back_state[0],
            back_state[1],
            back_state[2],
        ),
    )
    grad_k_block, grad_v_block = (
        lax.psum_scatter(
            grad_k_whole.astype(jnp.bfloat16), BLK, scatter_dimension=1, tiled=True
        ).astype(jnp.float32),
        lax.psum_scatter(
            grad_v_whole.astype(jnp.bfloat16), BLK, scatter_dimension=1, tiled=True
        ).astype(jnp.float32),
    )
    grad_q_block = jnp.transpose(grad_q_group, (0, 3, 1, 2, 4)).reshape(
        sequence_count, block_len, local_q, HEAD_SIZE
    )
    grad_q_seq, grad_k_seq, value_sequence_gradient = (
        lax.all_to_all(
            grad_q_block.astype(jnp.bfloat16), ULY, split_axis=1, concat_axis=2, tiled=True
        ).astype(grad_q_block.dtype),
        lax.all_to_all(
            grad_k_block.astype(jnp.bfloat16), ULY, split_axis=1, concat_axis=2, tiled=True
        ).astype(grad_k_block.dtype),
        lax.all_to_all(
            grad_v_block.astype(jnp.bfloat16), ULY, split_axis=1, concat_axis=2, tiled=True
        ).astype(grad_v_block.dtype),
    )
    grad_q_normed = rotate(grad_q_seq, local_angles, -1.0)
    grad_k_normed = rotate(grad_k_seq, local_angles, -1.0)
    q_gain_term = jnp.sum(grad_q_normed * q_pre * q_scale, axis=(0, 1, 2))
    k_gain_term = jnp.sum(grad_k_normed * key_before_norm * k_scale, axis=(0, 1, 2))
    grad_q_pre = (
        norm_back(grad_q_normed, q_pre, q_scale, gain_q)
        .astype(jnp.bfloat16)
        .reshape(sequence_count, token_count, QUERY_HEADS * HEAD_SIZE)
    )
    grad_k_pre = (
        norm_back(grad_k_normed, key_before_norm, k_scale, gain_k)
        .astype(jnp.bfloat16)
        .reshape(sequence_count, token_count, KEY_VALUE_HEADS * HEAD_SIZE)
    )
    value_pre_gradient = value_sequence_gradient.astype(jnp.bfloat16).reshape(
        sequence_count, token_count, KEY_VALUE_HEADS * HEAD_SIZE
    )
    grad_query = jnp.einsum(
        EQ_STD_STE_TO_DE, normalized_input, grad_q_pre, preferred_element_type=jnp.float32
    )
    grad_key = jnp.einsum(
        EQ_STD_STE_TO_DE, normalized_input, grad_k_pre, preferred_element_type=jnp.float32
    )
    grad_value = jnp.einsum(
        EQ_STD_STE_TO_DE, normalized_input, value_pre_gradient, preferred_element_type=jnp.float32
    )
    grad_normed = jnp.einsum(EQ_STE_DE_TO_STD, grad_q_pre, wq_all, preferred_element_type=jnp.float32)
    grad_normed = grad_normed + jnp.einsum(
        EQ_STE_DE_TO_STD, grad_k_pre, wk_all, preferred_element_type=jnp.float32
    )
    grad_normed = grad_normed + jnp.einsum(
        EQ_STE_DE_TO_STD, value_pre_gradient, wv_all, preferred_element_type=jnp.float32
    )
    attn_gain_term = jnp.sum(grad_normed * source * first_scale, axis=(0, 1))
    grad_hidden = grad_middle + norm_back(
        grad_normed, source, first_scale, g_attn.astype(jnp.float32)
    )
    grad_down = jnp.einsum(EQ_STF_STD_TO_FD, activated, cotangent, preferred_element_type=jnp.float32)
    grad_attn_gain, grad_query, grad_key, grad_value, grad_out, grad_down = (
        lax.psum_scatter(attn_gain_term, EVERY, scatter_dimension=0, tiled=True),
        lax.psum_scatter(grad_query, EVERY, scatter_dimension=0, tiled=True),
        lax.psum_scatter(grad_key, EVERY, scatter_dimension=0, tiled=True),
        lax.psum_scatter(grad_value, EVERY, scatter_dimension=0, tiled=True),
        lax.psum_scatter(grad_out, EVERY, scatter_dimension=0, tiled=True),
        lax.psum_scatter(grad_down, EVERY, scatter_dimension=0, tiled=True),
    )
    grad_q_gain, grad_k_gain = lax.psum((q_gain_term, k_gain_term), EVERY)
    return (
        output,
        grad_hidden,
        grad_attn_gain,
        grad_query,
        grad_key,
        grad_value,
        grad_out,
        grad_q_gain,
        grad_k_gain,
        grad_mlp_gain,
        grad_gate,
        grad_up,
        grad_down,
    )


MESH = pl.DeviceIdType.MESH
HBM = pl.BlockSpec(memory_space=pl.ANY)
VMEM = pl.BlockSpec(memory_space=pltpu.VMEM)
MIB = 1 << 20


def kernel_params(collective_id, vmem_mib=48):
    return pltpu.CompilerParams(
        collective_id=collective_id, has_side_effects=True, vmem_limit_bytes=vmem_mib * MIB
    )


def semaphores(count, local=16):
    return [
        pltpu.SemaphoreType.DMA((count,)),
        pltpu.SemaphoreType.DMA((count,)),
        pltpu.SemaphoreType.DMA((local,)),
    ]


class Copy:
    def __init__(self, descriptor, sends, receives):
        self.descriptor, self.sends, self.receives = descriptor, sends, receives

    def under(self, condition, action):
        if condition is None:
            action()
        else:
            pl.when(condition)(action)

    def start(self):
        self.under(self.sends, lambda: self.descriptor().start())
        return self

    def sent(self):
        self.under(self.sends, lambda: self.descriptor().wait_send())

    def arrived(self):
        self.under(self.receives, lambda: self.descriptor().wait_recv())


class Links:
    def __init__(self, send, recv, here):
        self.send, self.recv, self.here = send, recv, here
        self.used, self.used_here = 0, 0
        self.copies, self.local_copies = [], []
        self.n_dp, self.n_blk, self.n_uly = (lax.axis_size(a) for a in EVERY)
        self.dp, self.blk, self.uly = (lax.axis_index(a) for a in EVERY)
        self.other_dp = 1 - self.dp
        self.across = lax.rem(self.uly + 2, 4)
        self.twin = self.uly + 1 - 2 * lax.rem(self.uly, 2)
        self.x_way = (self.other_dp, self.blk, self.uly)
        self.y_way = (self.dp, self.blk, self.across)
        self.core_way = (self.dp, self.blk, self.twin)

    def peer(self, step):
        return lax.rem(self.blk + step, self.n_blk)

    def peers(self):
        return [(self.dp, self.peer(k), self.uly) for k in range(1, self.n_blk)]

    def greet(self, devices):
        barrier = pltpu.get_barrier_semaphore()
        for device in devices:
            pl.semaphore_signal(barrier, inc=1, device_id=device, device_id_type=MESH)
        pl.semaphore_wait(barrier, len(devices))

    def remote(self, source, target, device, sends=None, receives=None):
        slot = self.used
        self.used += 1

        def descriptor():
            return pltpu.make_async_remote_copy(
                src_ref=source(),
                dst_ref=target(),
                send_sem=self.send.at[slot],
                recv_sem=self.recv.at[slot],
                device_id=device,
                device_id_type=MESH,
            )

        copy = Copy(descriptor, sends, receives)
        self.copies.append(copy)
        return copy.start()

    def to(self, source, target, device):
        return self.remote(lambda: source, lambda: target, device)

    def local(self, source, target):
        copy = pltpu.make_async_copy(source, target, self.here.at[self.used_here])
        self.used_here += 1
        copy.start()
        self.local_copies.append(copy)
        return copy

    def finish(self):
        for copy in self.copies:
            copy.sent()


class LineGather:
    def __init__(self, links, own, whole):
        self.links, self.own, self.whole = links, own, whole
        self.waiting = []

    def send(self, step):
        links, whole = self.links, self.whole
        blk, last = links.blk, links.n_blk - 1

        def block(index):
            if step == 0:
                return lambda: self.own
            return lambda: whole.at[index]

        self.waiting = [
            links.remote(
                block(blk - step),
                lambda: whole.at[blk - step],
                (links.dp, blk + 1, links.uly),
                jnp.logical_and(blk >= step, blk < last),
                blk >= step + 1,
            ),
            links.remote(
                block(blk + step),
                lambda: whole.at[blk + step],
                (links.dp, blk - 1, links.uly),
                jnp.logical_and(blk + step <= last, blk > 0),
                blk + step + 1 <= last,
            ),
        ]

    def arrived(self):
        for copy in self.waiting:
            copy.arrived()


class PlaneGather:
    def __init__(self, links, at):
        self.links, self.at = links, at

    def start(self, own=None):
        links, at = self.links, self.at
        mine = at(links.dp, links.uly)
        own = mine if own is None else own
        self.from_x = links.to(own, mine, links.x_way)
        self.from_y = links.to(own, mine, links.y_way)
        self.from_core = [links.to(own, mine, links.core_way)]

    def hand_on(self):
        links, at = self.links, self.at
        self.from_x.arrived()
        half = at(links.other_dp, links.uly, 0)
        self.second_y = links.to(half, half, links.y_way)
        self.from_y.arrived()
        half = at(links.dp, links.across, 1)
        self.second_x = links.to(half, half, links.x_way)
        for chunk in (at(links.other_dp, links.uly), at(links.dp, links.across)):
            self.from_core.append(links.to(chunk, chunk, links.core_way))

    def last(self):
        links = self.links
        self.second_y.arrived()
        self.second_x.arrived()
        chunk = self.at(links.other_dp, links.across)
        self.from_core.append(links.to(chunk, chunk, links.core_way))

    def arrived(self):
        for copy in self.from_core:
            copy.arrived()


def rows_of(whole, blocked):
    def at(dp, uly, half=None):
        part = whole.at[dp, :, uly] if blocked else whole.at[dp, uly]
        if half is None:
            return part
        depth = whole.shape[-2] // 2
        rows = pl.ds(half * depth, depth)
        return part.at[:, rows] if blocked else part.at[rows]

    return at


class ColumnSwap:
    def __init__(self, links, pieces):
        self.links, self.pieces = links, pieces
        self.incoming, self.kept = [], []

    def parts(self, blk):
        links = self.links
        for weight, whole, offset in self.pieces:
            width = weight.shape[-1] // links.n_dp // links.n_blk
            for group in range(links.n_dp):
                start = (group * links.n_blk + blk) * width
                yield (
                    weight.at[:, pl.ds(pl.multiple_of(start, 128), width)],
                    whole.at[
                        links.dp, links.blk, links.uly, :, pl.ds(offset + group * width, width)
                    ],
                )

    def start(self):
        links = self.links
        for step in range(1, links.n_blk):
            device = (links.dp, links.peer(step), links.uly)
            for source, target in self.parts(links.peer(step)):
                self.incoming.append(links.to(source, target, device))
        for source, target in self.parts(links.blk):
            self.kept.append(links.local(source, target))

    def arrived(self):
        for copy in self.kept:
            copy.wait()
        for copy in self.incoming:
            copy.arrived()


def front_kernel(
    hidden,
    wq,
    wk,
    wv,
    wo,
    wd,
    gains,
    all_hidden,
    w_qkv,
    all_wo,
    all_wd,
    all_gains,
    send,
    recv,
    here,
):
    links = Links(send, recv, here)
    links.greet(links.peers() + [links.x_way, links.y_way, links.core_way])
    q_width, k_width = wq.shape[1] // links.n_blk, wk.shape[1] // links.n_blk
    swap = ColumnSwap(
        links, [(wq, w_qkv, 0), (wk, w_qkv, q_width), (wv, w_qkv, q_width + k_width)]
    )
    swap.start()
    gain_swap = []
    my_gains = all_gains.at[links.dp, links.blk, links.uly]
    for device in links.peers():
        gain_swap.append(links.to(gains, my_gains, device))
    keep = [
        links.local(gains, my_gains),
        links.local(hidden, all_hidden.at[links.blk]),
        links.local(wo, all_wo.at[links.dp, links.uly]),
        links.local(wd, all_wd.at[links.dp, links.uly]),
    ]
    line = LineGather(links, hidden, all_hidden)
    line.send(0)
    plane_wo = PlaneGather(links, rows_of(all_wo, False))
    plane_wo.start(wo)
    plane_qkv = PlaneGather(links, rows_of(w_qkv, True))
    plane_gain = PlaneGather(links, rows_of(all_gains, True))
    plane_wd = PlaneGather(links, rows_of(all_wd, False))
    swap.arrived()
    plane_qkv.start()
    keep[0].wait()
    for copy in gain_swap:
        copy.arrived()
    plane_gain.start()
    plane_wd.start(wd)
    for step in range(1, links.n_blk - 1):
        line.arrived()
        line.send(step)
        if step == 1:
            plane_wo.hand_on()
            plane_qkv.hand_on()
            plane_gain.hand_on()
    plane_wd.hand_on()
    plane_wo.last()
    plane_qkv.last()
    plane_gain.last()
    plane_wd.last()
    line.arrived()
    for plane in (plane_wo, plane_qkv, plane_gain, plane_wd):
        plane.arrived()
    for copy in keep[1:]:
        copy.wait()
    links.finish()


def gather_front(hidden, wq, wk, wv, wo, wd, gains):
    n_dp, n_blk, n_uly = (lax.axis_size(a) for a in EVERY)
    qkv_width = (wq.shape[1] + wk.shape[1] + wv.shape[1]) // n_blk
    shapes = [
        (n_blk,) + hidden.shape,
        (n_dp, n_blk, n_uly, wq.shape[0], qkv_width),
        (n_dp, n_uly) + wo.shape,
        (n_dp, n_uly) + wd.shape,
        (n_dp, n_blk, n_uly) + gains.shape,
    ]
    return pl.pallas_call(
        front_kernel,
        out_shape=[jax.ShapeDtypeStruct(s, jnp.bfloat16) for s in shapes],
        in_specs=[HBM] * 7,
        out_specs=[HBM] * 5,
        scratch_shapes=semaphores(72),
        compiler_params=kernel_params(0),
    )(hidden, wq, wk, wv, wo, wd, gains)


def feed_forward_kernel(wg, wu, cotangent, all_wg, all_wu, all_cot, send, recv, here):
    links = Links(send, recv, here)
    links.greet(links.peers() + [links.x_way, links.y_way, links.core_way])
    swaps = [ColumnSwap(links, [(wg, all_wg, 0)]), ColumnSwap(links, [(wu, all_wu, 0)])]
    for swap in swaps:
        swap.start()
    keep = links.local(cotangent, all_cot.at[links.blk])
    planes = [PlaneGather(links, rows_of(w, True)) for w in (all_wg, all_wu)]
    swaps[0].arrived()
    planes[0].start()
    swaps[1].arrived()
    line = LineGather(links, cotangent, all_cot)
    line.send(0)
    planes[1].start()
    planes[0].hand_on()
    line.arrived()
    line.send(1)
    planes[1].hand_on()
    planes[0].last()
    for step in range(2, links.n_blk - 1):
        line.arrived()
        line.send(step)
    planes[1].last()
    line.arrived()
    for plane in planes:
        plane.arrived()
    keep.wait()
    links.finish()


def gather_feed_forward(wg, wu, cotangent):
    n_dp, n_blk, n_uly = (lax.axis_size(a) for a in EVERY)
    shapes = [
        (n_dp, n_blk, n_uly, wg.shape[0], wg.shape[1] // n_blk),
        (n_dp, n_blk, n_uly, wu.shape[0], wu.shape[1] // n_blk),
        (n_blk,) + cotangent.shape,
    ]
    return pl.pallas_call(
        feed_forward_kernel,
        out_shape=[jax.ShapeDtypeStruct(s, jnp.bfloat16) for s in shapes],
        in_specs=[HBM] * 3,
        out_specs=[HBM] * 3,
        scratch_shapes=semaphores(48),
        compiler_params=kernel_params(1),
    )(wg, wu, cotangent)


ROWS = 32


def each_block(count, body):
    def step(index, carry):
        body(pl.ds(pl.multiple_of(index * ROWS, ROWS), ROWS))
        return carry

    lax.fori_loop(0, count // ROWS, step, 0)


class LineScatter:
    def __init__(self, links, parts, rightward, leftward):
        self.links, self.parts = links, parts
        self.slots = {1: rightward, -1: leftward}
        self.tokens = parts.shape[1]
        self.number = links.used
        links.used += 2 * (links.n_blk - 1)

    def place(self, step, way):
        blk, last = self.links.blk, self.links.n_blk - 1
        target = last - step if way == 1 else step
        slot = self.slots[way].at[target - 1 if way == 1 else target]
        first = blk == (0 if way == 1 else last)
        beyond = target > blk if way == 1 else target < blk
        return target, slot, first, beyond

    def copy(self, step, way, source=None):
        links, (_, slot, _, _) = self.links, self.place(step, way)
        number = self.number + 2 * step + (way == 1)
        return pltpu.make_async_remote_copy(
            src_ref=slot if source is None else source,
            dst_ref=slot,
            send_sem=links.send.at[number],
            recv_sem=links.recv.at[number],
            device_id=(links.dp, links.blk + way, links.uly),
            device_id_type=MESH,
        )

    def move(self, step, way):
        parts = self.parts
        target, slot, first, beyond = self.place(step, way)

        @pl.when(jnp.logical_and(first, beyond))
        def _():
            self.copy(step, way, parts.at[target]).start()

        @pl.when(jnp.logical_and(jnp.logical_not(first), beyond))
        def _():
            self.copy(step, way).wait_recv()

            def body(rows):
                slot[rows, :] = slot[rows, :] + parts[target, rows, :]

            each_block(self.tokens, body)
            self.copy(step, way).start()

    def step(self, step):
        early = 2 * self.links.blk < self.links.n_blk

        @pl.when(early)
        def _():
            self.move(step, 1)
            self.move(step, -1)

        @pl.when(jnp.logical_not(early))
        def _():
            self.move(step, -1)
            self.move(step, 1)

    def finish(self, total):
        links, parts = self.links, self.parts
        blk, last = links.blk, links.n_blk - 1
        for step in range(last):
            for way in (1, -1):
                target, _, first, _ = self.place(step, way)
                here = jnp.logical_and(jnp.logical_not(first), target == blk)
                pl.when(here)(lambda step=step, way=way: self.copy(step, way).wait_recv())

        def start(rows):
            total[rows, :] = parts[blk, rows, :].astype(jnp.float32)

        each_block(self.tokens, start)
        for way, condition, index in ((1, blk > 0, blk - 1), (-1, blk < last, blk)):

            def add(way=way, index=index):
                def body(rows):
                    term = self.slots[way][index, rows, :]
                    total[rows, :] = total[rows, :] + term.astype(jnp.float32)

                each_block(self.tokens, body)

            pl.when(condition)(add)

    def sent(self):
        for step in range(self.links.n_blk - 1):
            for way in (1, -1):
                _, _, _, beyond = self.place(step, way)
                pl.when(beyond)(lambda step=step, way=way: self.copy(step, way).wait_send())


def line_scratch(n_blk, tokens, width):
    return [pltpu.VMEM((n_blk - 1, tokens, width), jnp.bfloat16)] * 2


class PlaneScatter:
    def __init__(self, links, parts, from_core, from_x, from_y, last_x, last_y):
        self.links, self.parts = links, parts
        self.from_core, self.from_x, self.from_y = from_core, from_x, from_y
        self.last_x, self.last_y = last_x, last_y
        self.core = lax.rem(links.uly, 2)
        self.row = lax.div(links.uly, 2)
        self.depth = parts.shape[3]
        self.core_copies = {}

    def chunk(self, dp, row, core, half=None):
        uly = row * 2 + core
        if half is None:
            return self.parts.at[dp, :, uly]
        depth = self.depth // 2
        return self.parts.at[dp, :, uly, pl.ds(half * depth, depth)]

    def add(self, target, source):
        blocks, depth, _ = target.shape
        rows = 32 if depth % 32 == 0 else 16

        def body(index, carry):
            block = lax.div(index, depth // rows)
            at = pl.ds(pl.multiple_of(lax.rem(index, depth // rows) * rows, rows), rows)
            target[block, at, :] = target[block, at, :] + source[block, at, :]
            return carry

        lax.fori_loop(0, blocks * (depth // rows), body, 0)

    def between_cores(self, which):
        links = self.links
        dp = links.dp if which == 1 else links.other_dp
        self.core_copies[which] = [
            links.to(
                self.chunk(dp, row, 1 - self.core), self.from_core.at[which, row], links.core_way
            )
            for row in range(2)
        ]

    def across_chips(self):
        links = self.links
        self.x_copies, self.y_copies = [], []
        for which, dp in ((0, links.other_dp), (1, links.dp)):
            for row in range(2):
                self.core_copies[which][row].arrived()
                self.add(self.chunk(dp, row, self.core), self.from_core.at[which, row])
            if which == 0:
                for row in range(2):
                    self.x_copies.append(
                        links.to(
                            self.chunk(dp, row, self.core, 0), self.from_x.at[row], links.x_way
                        )
                    )
        for group in range(links.n_dp):
            self.y_copies.append(
                links.to(
                    self.chunk(group, 1 - self.row, self.core, 1),
                    self.from_y.at[group],
                    links.y_way,
                )
            )

    def second_way(self):
        links = self.links
        for row in range(2):
            self.x_copies[row].arrived()
            self.add(self.chunk(links.dp, row, self.core, 0), self.from_x.at[row])
        self.y_last = links.to(
            self.chunk(links.dp, 1 - self.row, self.core, 0), self.last_y, links.y_way
        )
        for group in range(links.n_dp):
            self.y_copies[group].arrived()
            self.add(self.chunk(group, self.row, self.core, 1), self.from_y.at[group])
        self.x_last = links.to(
            self.chunk(links.other_dp, self.row, self.core, 1), self.last_x, links.x_way
        )

    def result(self, write):
        links = self.links
        for half, copy, source in ((0, self.y_last, self.last_y), (1, self.x_last, self.last_x)):
            copy.arrived()
            own = self.chunk(links.dp, self.row, self.core, half)
            blocks, depth, _ = source.shape
            rows = 32 if depth % 32 == 0 else 16

            def body(index, carry, own=own, source=source, half=half, depth=depth, rows=rows):
                block = lax.div(index, depth // rows)
                start = pl.multiple_of(lax.rem(index, depth // rows) * rows, rows)
                at = pl.ds(start, rows)
                value = own[block, at, :].astype(jnp.float32)
                value = value + source[block, at, :].astype(jnp.float32)
                write(block, pl.ds(pl.multiple_of(start + half * depth, rows), rows), value)
                return carry

            lax.fori_loop(0, blocks * (depth // rows), body, 0)


def plane_scratch(n_dp, blocks, n_uly, depth, width):
    shapes = [
        (n_dp, blocks, n_uly, depth, width),
        (n_dp, 2, blocks, depth, width),
        (2, blocks, depth // 2, width),
        (n_dp, blocks, depth // 2, width),
        (blocks, depth // 2, width),
        (blocks, depth // 2, width),
    ]
    return [pltpu.VMEM(shape, jnp.bfloat16) for shape in shapes]


def weight_grad(left, right, parts, dp, together):
    _, blocks, n_uly, depth, width = parts.shape
    steps = n_uly // together
    columns = 512

    def body(index, carry):
        block, step = lax.div(index, steps), lax.rem(index, steps)
        start = ((dp * blocks + block) * n_uly + step * together) * depth
        rows = left[:, pl.ds(pl.multiple_of(start, 128), together * depth)].T
        for column in range(0, width, columns):
            part = jnp.dot(
                rows, right[:, column : column + columns], preferred_element_type=jnp.float32
            )
            parts[dp, block, pl.ds(step * together, together), :, column : column + columns] = (
                part.astype(jnp.bfloat16).reshape(together, depth, columns)
            )
        return carry

    lax.fori_loop(0, blocks * steps, body, 0)


def middle_kernel(
    heads,
    wo,
    source,
    gain,
    middle,
    all_normed,
    parts,
    rightward,
    leftward,
    normed,
    send,
    recv,
    here,
):
    links = Links(send, recv, here)
    links.greet(links.peers())
    tokens = source.shape[0]
    for blk in (links.n_blk - 1, 0) + tuple(range(1, links.n_blk - 1)):
        parts[blk] = jnp.dot(heads[blk], wo[...], preferred_element_type=jnp.float32).astype(
            jnp.bfloat16
        )
    scatter = LineScatter(links, parts, rightward, leftward)
    for step in range(links.n_blk - 1):
        scatter.step(step)
    scatter.finish(middle)

    def body(rows):
        total = middle[rows, :] + source[rows, :].astype(jnp.float32)
        middle[rows, :] = total
        normed[rows, :] = (total * rms_scale(total) * gain[...]).astype(jnp.bfloat16)

    each_block(tokens, body)
    keep = links.local(normed, all_normed.at[links.blk])
    line = LineGather(links, normed, all_normed)
    for step in range(links.n_blk - 1):
        line.send(step)
        line.arrived()
    keep.wait()
    scatter.sent()
    links.finish()


def exchange_middle(heads, wo, source, gain):
    n_blk = lax.axis_size(BLK)
    tokens, width = source.shape
    return pl.pallas_call(
        middle_kernel,
        out_shape=[
            jax.ShapeDtypeStruct((tokens, width), jnp.float32),
            jax.ShapeDtypeStruct((n_blk, tokens, width), jnp.bfloat16),
        ],
        in_specs=[VMEM] * 4,
        out_specs=[VMEM, HBM],
        scratch_shapes=[pltpu.VMEM((n_blk, tokens, width), jnp.bfloat16)]
        + line_scratch(n_blk, tokens, width)
        + [pltpu.VMEM((tokens, width), jnp.bfloat16)]
        + semaphores(16),
        compiler_params=kernel_params(2),
    )(heads, wo, source, gain)


def back_rows(grad_normed, source, gain):
    scale = rms_scale(source)
    unit = source * scale
    scaled = grad_normed * gain
    back = scale * (scaled - unit * jnp.mean(scaled * unit, axis=-1, keepdims=True))
    return back, jnp.sum(grad_normed * unit, axis=0, keepdims=True)


def back_kernel(
    grad_parts,
    middle,
    cotangent,
    gain,
    all_normed,
    grad_gate_pre,
    grad_up_pre,
    activated,
    all_cot,
    grad_middle,
    gain_term,
    all_low,
    grad_gate,
    grad_up,
    grad_down,
    rightward,
    leftward,
    low,
    gate_1,
    gate_2,
    gate_3,
    gate_4,
    gate_5,
    gate_6,
    up_1,
    up_2,
    up_3,
    up_4,
    up_5,
    up_6,
    down_1,
    down_2,
    down_3,
    down_4,
    down_5,
    down_6,
    send,
    recv,
    here,
):
    links = Links(send, recv, here)
    links.greet(links.peers() + [links.x_way, links.y_way, links.core_way])
    scatter = LineScatter(links, grad_parts, rightward, leftward)
    gate = PlaneScatter(links, gate_1, gate_2, gate_3, gate_4, gate_5, gate_6)
    up = PlaneScatter(links, up_1, up_2, up_3, up_4, up_5, up_6)
    down = PlaneScatter(links, down_1, down_2, down_3, down_4, down_5, down_6)

    def compute(scatter, left, right, parts, together):
        for which, dp in ((0, links.other_dp), (1, links.dp)):
            weight_grad(left, right, parts, dp, together)
            scatter.between_cores(which)

    compute(gate, all_normed, grad_gate_pre, gate_1, 4)
    scatter.step(0)
    compute(up, all_normed, grad_up_pre, up_1, 4)
    gate.across_chips()
    scatter.step(1)
    compute(down, activated, all_cot, down_1, 2)
    up.across_chips()
    for step in range(2, links.n_blk - 1):
        scatter.step(step)
    down.across_chips()
    scatter.finish(grad_middle)
    gain_term[...] = jnp.zeros_like(gain_term)

    def body(rows):
        back, term = back_rows(grad_middle[rows, :], middle[rows, :], gain[...])
        grad = cotangent[rows, :].astype(jnp.float32) + back
        gain_term[...] += term
        grad_middle[rows, :] = grad
        low[rows, :] = grad.astype(jnp.bfloat16)

    each_block(middle.shape[0], body)
    keep = links.local(low, all_low.at[links.blk])
    line = LineGather(links, low, all_low)
    line.send(0)
    gate.second_way()
    line.arrived()
    for step in range(1, links.n_blk - 1):
        line.send(step)
        if step == 1:
            up.second_way()
        line.arrived()
    down.second_way()

    def into(target):
        def write(block, rows, values):
            target[block, rows, :] = values.astype(target.dtype)

        return write

    gate.result(into(grad_gate))
    up.result(into(grad_up))
    down.result(into(grad_down))
    keep.wait()
    scatter.sent()
    links.finish()


def exchange_back(
    grad_parts, middle, cotangent, gain, all_normed, grad_gate_pre, grad_up_pre, activated, all_cot
):
    n_dp, n_blk, n_uly = (lax.axis_size(a) for a in EVERY)
    _, tokens, width = grad_parts.shape
    ff = grad_gate_pre.shape[1]
    depth = width // (n_dp * n_blk * n_uly)
    down_depth = ff // (n_dp * n_uly)
    return pl.pallas_call(
        back_kernel,
        out_shape=[
            jax.ShapeDtypeStruct((tokens, width), jnp.float32),
            jax.ShapeDtypeStruct((1, width), jnp.float32),
            jax.ShapeDtypeStruct((n_blk, tokens, width), jnp.bfloat16),
            jax.ShapeDtypeStruct((n_blk, depth, ff), jnp.bfloat16),
            jax.ShapeDtypeStruct((n_blk, depth, ff), jnp.bfloat16),
            jax.ShapeDtypeStruct((1, down_depth, width), jnp.float32),
        ],
        in_specs=[VMEM] * 9,
        out_specs=[VMEM, VMEM, HBM, VMEM, VMEM, VMEM],
        scratch_shapes=line_scratch(n_blk, tokens, width)
        + [pltpu.VMEM((tokens, width), jnp.bfloat16)]
        + plane_scratch(n_dp, n_blk, n_uly, depth, ff) * 2
        + plane_scratch(n_dp, 1, n_uly, down_depth, width)
        + semaphores(48),
        compiler_params=kernel_params(3, 60),
    )(
        grad_parts,
        middle,
        cotangent,
        gain,
        all_normed,
        grad_gate_pre,
        grad_up_pre,
        activated,
        all_cot,
    )


def last_kernel(
    grad_parts,
    source,
    grad_middle,
    gain,
    normed,
    grad_qkv,
    heads,
    all_low,
    small,
    grad_hidden,
    grad_w_qkv,
    grad_wo,
    small_sum,
    rightward,
    leftward,
    qkv_1,
    qkv_2,
    qkv_3,
    qkv_4,
    qkv_5,
    qkv_6,
    wo_1,
    wo_2,
    wo_3,
    wo_4,
    wo_5,
    wo_6,
    summed,
    small_in,
    small_total,
    send,
    recv,
    here,
):
    links = Links(send, recv, here)
    links.greet(links.peers() + [links.x_way, links.y_way, links.core_way])
    scatter = LineScatter(links, grad_parts, rightward, leftward)
    qkv = PlaneScatter(links, qkv_1, qkv_2, qkv_3, qkv_4, qkv_5, qkv_6)
    out = PlaneScatter(links, wo_1, wo_2, wo_3, wo_4, wo_5, wo_6)

    small_copies = [links.to(small, small_in.at[links.blk], device) for device in links.peers()]
    small_in[links.blk] = small[...]

    for which, dp in ((0, links.other_dp), (1, links.dp)):
        weight_grad(normed, grad_qkv, qkv_1, dp, 4)
        qkv.between_cores(which)
    scatter.step(0)
    for which, dp in ((0, links.other_dp), (1, links.dp)):
        weight_grad(heads, all_low, wo_1, dp, 4)
        out.between_cores(which)
    qkv.across_chips()
    for copy in small_copies:
        copy.arrived()
    total = small_in[0]
    for blk in range(1, links.n_blk):
        total = total + small_in[blk]
    small_total[0] = total
    pending = links.to(small_total.at[0], small_in.at[links.n_blk], links.x_way)
    out.across_chips()
    scatter.step(1)
    pending.arrived()
    small_total[1] = small_total[0] + small_in[links.n_blk]
    pending = links.to(small_total.at[1], small_in.at[links.n_blk + 1], links.y_way)
    qkv.second_way()
    pending.arrived()
    small_total[2] = small_total[1] + small_in[links.n_blk + 1]
    pending = links.to(small_total.at[2], small_in.at[links.n_blk + 2], links.core_way)
    for step in range(2, links.n_blk - 1):
        scatter.step(step)
    out.second_way()
    pending.arrived()
    small_sum[...] = small_total[2] + small_in[links.n_blk + 2]

    def write(block, rows, values):
        summed[block, rows, :] = values.astype(jnp.bfloat16)

    qkv.result(write)
    swapped = []
    for step in range(1, links.n_blk):
        peer = links.peer(step)
        swapped.append(
            links.to(
                summed.at[peer], grad_w_qkv.at[links.blk], (links.dp, peer, links.uly)
            )
        )
    keep = links.local(summed.at[links.blk], grad_w_qkv.at[links.blk])
    scatter.finish(grad_hidden)

    def body(rows):
        back, _ = back_rows(
            grad_hidden[rows, :], source[rows, :].astype(jnp.float32), gain[...]
        )
        grad_hidden[rows, :] = grad_middle[rows, :] + back

    each_block(source.shape[0], body)

    def write_out(block, rows, values):
        grad_wo[block, rows, :] = values

    out.result(write_out)
    for copy in swapped:
        copy.arrived()
    keep.wait()
    scatter.sent()
    links.finish()


def exchange_last(grad_parts, source, grad_middle, gain, normed, grad_qkv, heads, all_low, small):
    n_dp, n_blk, n_uly = (lax.axis_size(a) for a in EVERY)
    _, tokens, width = grad_parts.shape
    columns = grad_qkv.shape[1]
    depth = width // (n_dp * n_blk * n_uly)
    out_depth = heads.shape[1] // (n_dp * n_uly)
    return pl.pallas_call(
        last_kernel,
        out_shape=[
            jax.ShapeDtypeStruct((tokens, width), jnp.float32),
            jax.ShapeDtypeStruct((n_blk, depth, columns), jnp.bfloat16),
            jax.ShapeDtypeStruct((1, out_depth, width), jnp.float32),
            jax.ShapeDtypeStruct(small.shape, jnp.float32),
        ],
        in_specs=[VMEM] * 9,
        out_specs=[VMEM, HBM, VMEM, VMEM],
        scratch_shapes=line_scratch(n_blk, tokens, width)
        + plane_scratch(n_dp, n_blk, n_uly, depth, columns)
        + plane_scratch(n_dp, 1, n_uly, out_depth, width)
        + [
            pltpu.VMEM((n_blk, depth, columns), jnp.bfloat16),
            pltpu.VMEM((n_blk + 3,) + small.shape, jnp.float32),
            pltpu.VMEM((3,) + small.shape, jnp.float32),
        ]
        + semaphores(48),
        compiler_params=kernel_params(4, 56),
    )(grad_parts, source, grad_middle, gain, normed, grad_qkv, heads, all_low, small)


def place_columns(blocks, n_dp):
    n_blk, rows, _ = blocks.shape
    split = blocks.reshape(n_blk, rows, n_dp, -1)
    return jnp.transpose(split, (1, 2, 0, 3)).reshape(rows, -1).astype(jnp.float32)


def product(left, right):
    return jnp.dot(left, right, preferred_element_type=jnp.float32)


def product_right(left, right):
    return lax.dot_general(
        left, right, (((1,), (1,)), ((), ())), preferred_element_type=jnp.float32
    )


def product_left(left, right):
    return lax.dot_general(
        left, right, (((0,), (0,)), ((), ())), preferred_element_type=jnp.float32
    )


def shards(
    hidden,
    span_order,
    attn_gain,
    w_query,
    key_weight,
    value_weight,
    w_out,
    q_gain,
    k_gain,
    mlp_gain,
    w_gate,
    w_up,
    w_down,
    cotangent,
):
    seqs, toks, width = hidden.shape
    n_dp, n_blk, n_uly = (lax.axis_size(a) for a in EVERY)
    blk_index = lax.axis_index(BLK)
    uly_index = lax.axis_index(ULY)
    local_q = QUERY_HEADS // n_blk
    local_kv = KEY_VALUE_HEADS // n_blk
    group = QUERY_HEADS // KEY_VALUE_HEADS
    half_len = toks * n_uly // 2
    score_scale = 1.0 / math.sqrt(HEAD_SIZE)
    rows = n_blk * seqs * toks
    f32, bf16 = jnp.float32, jnp.bfloat16
    own_hidden = hidden.reshape(seqs * toks, width)
    own_cotangent = cotangent.reshape(seqs * toks, width)

    def places(u):
        return (
            (jnp.arange(n_blk, dtype=jnp.int32)[:, None] * n_uly + u) * toks
            + jnp.arange(toks, dtype=jnp.int32)[None, :]
        )

    query_pos = positions_of(places(uly_index).reshape(-1), span_order, half_len)
    key_pos = jnp.concatenate(
        [positions_of(places(u).reshape(-1), span_order, half_len) for u in range(n_uly)]
    )
    angles = angles_of(query_pos, HEAD_SIZE).reshape(n_blk, 1, toks, HEAD_SIZE // 2)
    angles = jnp.broadcast_to(angles, (n_blk, seqs, toks, HEAD_SIZE // 2)).reshape(rows, -1)

    gain_rows = attn_gain.shape[0]
    own_gains = jnp.pad(jnp.stack([attn_gain, mlp_gain]), ((0, 14), (0, 128 - gain_rows)))
    all_hidden, w_qkv, wo, all_wd, all_gains = gather_front(
        own_hidden, w_query, key_weight, value_weight, w_out, w_down, own_gains
    )
    all_wg, all_wu, cot = gather_feed_forward(w_gate, w_up, own_cotangent)
    gains = all_gains[..., :2, :gain_rows].astype(f32)
    g_attn = gains[..., 0, :].reshape(1, width)
    g_mlp = gains[..., 1, :].reshape(1, width)
    w_qkv = w_qkv.reshape(width, -1)
    wo = wo.reshape(-1, width)
    wg, wu = all_wg.reshape(width, -1), all_wu.reshape(width, -1)
    wd = all_wd.reshape(-1, width)
    cot = cot.reshape(rows, width)

    source = all_hidden.reshape(rows, width).astype(f32)
    first_scale = rms_scale(source)
    normed = (source * first_scale * g_attn).astype(bf16)
    qkv = product(normed, w_qkv)
    q_end = local_q * HEAD_SIZE
    k_end = q_end + local_kv * HEAD_SIZE
    q_pre = qkv[:, :q_end].reshape(rows, local_q, HEAD_SIZE)
    k_pre = qkv[:, q_end:k_end].reshape(rows, local_kv, HEAD_SIZE)
    v_pre = qkv[:, k_end:].reshape(rows, local_kv, HEAD_SIZE)
    q_scale, k_scale = rms_scale(q_pre), rms_scale(k_pre)
    gain_q, gain_k = q_gain.astype(f32), k_gain.astype(f32)
    q_rot = rotate(q_pre * q_scale * gain_q, angles, 1.0).astype(bf16)
    k_rot = rotate(k_pre * k_scale * gain_k, angles, 1.0).astype(bf16)
    v_low = v_pre.astype(bf16)

    def by_head(x):
        heads = x.shape[1]
        x = x.reshape(n_blk, seqs, toks, heads, HEAD_SIZE)
        return jnp.transpose(x, (1, 3, 0, 2, 4)).reshape(seqs, heads, n_blk * toks, HEAD_SIZE)

    def from_head(x):
        heads = x.shape[1]
        x = x.reshape(seqs, heads, n_blk, toks, HEAD_SIZE)
        return jnp.transpose(x, (2, 0, 3, 1, 4)).reshape(rows, heads, HEAD_SIZE)

    q_len = n_blk * toks
    kv = jnp.stack([by_head(k_rot), by_head(v_low)])
    kv_all = lax.all_gather(kv, ULY, axis=3, tiled=True)
    keys, values = kv_all[0], kv_all[1]
    queries = by_head(q_rot).reshape(seqs, local_kv, group, q_len, HEAD_SIZE)
    allowed = query_pos[:, None] >= key_pos[None, :]
    scores = (
        jnp.einsum(EQ_SCORES, queries, keys, preferred_element_type=f32) * score_scale
    )
    scores = jnp.where(allowed, scores, -jnp.inf)
    top = jnp.max(scores, axis=-1, keepdims=True)
    weights = jnp.exp(scores - top)
    total = jnp.sum(weights, axis=-1, keepdims=True)
    lse = top + jnp.log(total)
    attended = (
        jnp.einsum(EQ_ATTEND, weights.astype(bf16), values, preferred_element_type=f32) / total
    )
    heads_flat = from_head(
        attended.astype(bf16).reshape(seqs, local_q, q_len, HEAD_SIZE)
    ).reshape(rows, local_q * HEAD_SIZE)

    middle, normed2 = exchange_middle(
        heads_flat.reshape(n_blk, seqs * toks, -1), wo, own_hidden, g_mlp
    )
    normed2 = normed2.reshape(rows, width)
    gate_pre = product(normed2, wg)
    up_pre = product(normed2, wu)
    sigmoid_gate = jax.nn.sigmoid(gate_pre)
    activated = (gate_pre * sigmoid_gate * up_pre).astype(bf16)
    out_parts = product(activated, wd).astype(bf16)
    grad_act = product_right(cot, wd)
    grad_gate_pre = (
        grad_act * up_pre * sigmoid_gate * (1.0 + gate_pre * (1.0 - sigmoid_gate))
    ).astype(bf16)
    grad_up_pre = (grad_act * gate_pre * sigmoid_gate).astype(bf16)
    grad_parts = (product_right(grad_gate_pre, wg) + product_right(grad_up_pre, wu)).astype(bf16)
    blocks = (n_blk, seqs * toks, width)
    out_sum = lax.psum_scatter(
        out_parts.reshape(blocks), BLK, scatter_dimension=0, tiled=True
    )
    output = (middle + out_sum[0].astype(f32)).astype(bf16)
    grad_middle, mlp_gain_term, middle_low, grad_gate, grad_up, grad_down = exchange_back(
        grad_parts.reshape(blocks),
        middle,
        own_cotangent,
        g_mlp,
        normed2,
        grad_gate_pre,
        grad_up_pre,
        activated,
        cot,
    )
    grad_gate = place_columns(lax.all_to_all(grad_gate, BLK, 0, 0), n_dp)
    grad_up = place_columns(lax.all_to_all(grad_up, BLK, 0, 0), n_dp)
    middle_low = middle_low.reshape(rows, width)
    grad_heads = by_head(
        product_right(middle_low, wo).astype(bf16).reshape(rows, local_q, HEAD_SIZE)
    ).reshape(seqs, local_kv, group, q_len, HEAD_SIZE)
    delta = jnp.sum(grad_heads.astype(f32) * attended, axis=-1, keepdims=True)
    probs = jnp.exp(scores - lse)
    grad_values = jnp.einsum(EQ_TO_KEYS, probs.astype(bf16), grad_heads, preferred_element_type=f32)
    grad_probs = jnp.einsum(EQ_SCORES, grad_heads, values, preferred_element_type=f32)
    grad_scores = (probs * (grad_probs - delta)).astype(bf16)
    grad_queries = score_scale * jnp.einsum(
        EQ_ATTEND, grad_scores, keys, preferred_element_type=f32
    )
    grad_keys = score_scale * jnp.einsum(
        EQ_TO_KEYS, grad_scores, queries, preferred_element_type=f32
    )
    grad_kv = lax.psum_scatter(
        jnp.stack([grad_keys, grad_values]).astype(bf16), ULY, scatter_dimension=3, tiled=True
    ).astype(f32)
    grad_q_normed = rotate(
        from_head(grad_queries.reshape(seqs, local_q, q_len, HEAD_SIZE)), angles, -1.0
    )
    grad_k_normed = rotate(from_head(grad_kv[0]), angles, -1.0)
    q_gain_term = jnp.sum(grad_q_normed * q_pre * q_scale, axis=(0, 1))
    k_gain_term = jnp.sum(grad_k_normed * k_pre * k_scale, axis=(0, 1))
    grad_q_pre = norm_back(grad_q_normed, q_pre, q_scale, gain_q).astype(bf16)
    grad_k_pre = norm_back(grad_k_normed, k_pre, k_scale, gain_k).astype(bf16)
    grad_v_pre = from_head(grad_kv[1]).astype(bf16)
    grad_qkv = jnp.concatenate(
        [g.reshape(rows, -1) for g in (grad_q_pre, grad_k_pre, grad_v_pre)], axis=-1
    )
    grad_normed_parts = product_right(grad_qkv, w_qkv)
    attn_gain_term = jnp.sum(grad_normed_parts * (source * first_scale), axis=0)
    small = jnp.concatenate([attn_gain_term, mlp_gain_term[0], q_gain_term, k_gain_term])
    small = jnp.pad(small, (0, -small.shape[0] % (8 * 128))).reshape(-1, 128)
    grad_hidden, grad_w_qkv, grad_out, small = exchange_last(
        grad_normed_parts.astype(bf16).reshape(blocks),
        own_hidden,
        grad_middle,
        g_attn,
        normed,
        grad_qkv,
        heads_flat,
        middle_low,
        small,
    )
    grad_query = place_columns(grad_w_qkv[..., :q_end], n_dp)
    grad_key = place_columns(grad_w_qkv[..., q_end:k_end], n_dp)
    grad_value = place_columns(grad_w_qkv[..., k_end:], n_dp)
    small = small.reshape(-1)
    gain_at = ((lax.axis_index(DP) * n_blk + blk_index) * n_uly + uly_index) * gain_rows
    grad_attn_gain = lax.dynamic_slice(small, (gain_at,), (gain_rows,))
    grad_mlp_gain = lax.dynamic_slice(small, (width + gain_at,), (gain_rows,))
    grad_q_gain = small[2 * width : 2 * width + HEAD_SIZE]
    grad_k_gain = small[2 * width + HEAD_SIZE : 2 * width + 2 * HEAD_SIZE]
    return (
        output.reshape(hidden.shape),
        grad_hidden.reshape(hidden.shape),
        grad_attn_gain,
        grad_query,
        grad_key,
        grad_value,
        grad_out[0],
        grad_q_gain,
        grad_k_gain,
        grad_mlp_gain,
        grad_gate,
        grad_up,
        grad_down[0],
    )


def solution(mesh):
    n_dp, n_blk, n_uly = (mesh.shape[a] for a in EVERY)
    aligned = (n_dp, n_uly) == (2, 4) and KEY_VALUE_HEADS % (n_dp * n_blk) == 0
    in_specs = (
        TOKENS,
        P(),
        P(EVERY),
        P(EVERY, None),
        P(EVERY, None),
        P(EVERY, None),
        P(EVERY, None),
        P(),
        P(),
        P(EVERY),
        P(EVERY, None),
        P(EVERY, None),
        P(EVERY, None),
        TOKENS,
    )
    out_specs = (
        TOKENS,
        TOKENS,
        P(EVERY),
        P(EVERY, None),
        P(EVERY, None),
        P(EVERY, None),
        P(EVERY, None),
        P(),
        P(),
        P(EVERY),
        P(EVERY, None),
        P(EVERY, None),
        P(EVERY, None),
    )
    return jax.shard_map(
        shards if aligned else shards_general,
        mesh=mesh, in_specs=in_specs, out_specs=out_specs, check_vma=False)
```

```python
import math

import jax
import jax.numpy as jnp
from jax import lax
from jax.experimental import pallas as pl
from jax.experimental.pallas import tpu as pltpu
from jax.sharding import PartitionSpec as P

QUERY_HEADS = 16
KEY_VALUE_HEADS = 8
HEAD_SIZE = 128


DP, BLK, ULY = "dp", "blk", "uly"
EVERY = (DP, BLK, ULY)
PLANE = (DP, ULY)
TOKENS = P(DP, (BLK, ULY), None)
EQ_KGQD_NKD_TO_KGQN = "kgqd,nkd->kgqn"
EQ_KGQN_KGQD_TO_NKD = "kgqn,kgqd->nkd"
EQ_KGQN_NKD_TO_KGQD = "kgqn,nkd->kgqd"
EQ_KGQN_QKGD_TO_NKD = "kgqn,qkgd->nkd"
EQ_QKGD_NKD_TO_KGQN = "qkgd,nkd->kgqn"
EQ_STD_DE_TO_STE = "std,de->ste"
EQ_STD_DF_TO_STF = "std,df->stf"
EQ_STD_ED_TO_STE = "std,ed->ste"
EQ_STD_FD_TO_STF = "std,fd->stf"
EQ_STD_STE_TO_DE = "std,ste->de"
EQ_STD_STF_TO_DF = "std,stf->df"
EQ_STE_DE_TO_STD = "ste,de->std"
EQ_STE_ED_TO_STD = "ste,ed->std"
EQ_STE_STD_TO_ED = "ste,std->ed"
EQ_STF_DF_TO_STD = "stf,df->std"
EQ_STF_FD_TO_STD = "stf,fd->std"
EQ_STF_STD_TO_FD = "stf,std->fd"

EPSILON = 1e-06
ROPE_BASE = 1000000.0


def rms_scale(source):
    return lax.rsqrt(jnp.mean(source * source, axis=-1, keepdims=True) + EPSILON)


def norm_back(grad_normed, source, norm_scale, gain):
    unit_rows = source * norm_scale
    scaled = grad_normed * gain
    return norm_scale * (scaled - unit_rows * jnp.mean(scaled * unit_rows, axis=-1, keepdims=True))


def angles_of(positions, head_dim):
    freq_steps = jnp.arange(head_dim // 2, dtype=jnp.float32)
    inverse = jnp.exp(freq_steps * (-2.0 * math.log(ROPE_BASE) / head_dim))
    return positions.astype(jnp.float32)[:, None] * inverse[None, :]


def rotate(source, angles, direction):
    half_dim = source.shape[-1] // 2
    cosine = jnp.cos(angles)[:, None, :]
    sine_part = direction * jnp.sin(angles)[:, None, :]
    first_half = source[..., :half_dim]
    second_half = source[..., half_dim:]
    return jnp.concatenate(
        [
            first_half * cosine - second_half * sine_part,
            second_half * cosine + first_half * sine_part,
        ],
        axis=-1,
    )


def positions_of(places, span_order, half_len):
    blocks_of = places // half_len
    block_ids = jnp.arange(span_order.shape[0], dtype=jnp.int32)
    chosen = jnp.sum(
        jnp.where(blocks_of[:, None] == block_ids[None, :], span_order[None, :], 0), axis=1
    )
    return chosen * half_len + places % half_len


def add_rows(buffer, new_rows):
    return buffer + new_rows


def shards_general(
    hidden,
    span_order,
    attn_gain,
    w_query,
    key_weight,
    value_weight,
    w_out,
    q_gain,
    k_gain,
    mlp_gain,
    w_gate,
    w_up,
    w_down,
    cotangent,
):
    sequence_count = hidden.shape[0]
    token_count = hidden.shape[1]
    ulysses_group_size = lax.axis_size(ULY)
    local_q = QUERY_HEADS // ulysses_group_size
    local_key_value = KEY_VALUE_HEADS // ulysses_group_size
    query_group_width = QUERY_HEADS // KEY_VALUE_HEADS
    block_len = token_count * ulysses_group_size
    half_len = block_len // 2
    score_scale = 1.0 / math.sqrt(HEAD_SIZE)
    blk_index = lax.axis_index(BLK)
    uly_index = lax.axis_index(ULY)
    first_place = (blk_index * ulysses_group_size + uly_index) * token_count
    local_angles = angles_of(
        positions_of(first_place + jnp.arange(token_count, dtype=jnp.int32), span_order, half_len),
        HEAD_SIZE,
    )
    query_pos = positions_of(
        blk_index * block_len + jnp.arange(block_len, dtype=jnp.int32), span_order, half_len
    )
    g_attn, wq_all, wk_all, wv_all, wo_all = (
        lax.all_gather(attn_gain, EVERY, axis=0, tiled=True),
        lax.all_gather(w_query, EVERY, axis=0, tiled=True),
        lax.all_gather(key_weight, EVERY, axis=0, tiled=True),
        lax.all_gather(value_weight, EVERY, axis=0, tiled=True),
        lax.all_gather(w_out, EVERY, axis=0, tiled=True),
    )
    source = hidden.astype(jnp.float32)
    first_scale = rms_scale(source)
    normalized_input = (source * first_scale * g_attn.astype(jnp.float32)).astype(jnp.bfloat16)
    q_pre = jnp.einsum(
        EQ_STD_DE_TO_STE, normalized_input, wq_all, preferred_element_type=jnp.float32
    ).reshape(sequence_count, token_count, QUERY_HEADS, HEAD_SIZE)
    key_before_norm = jnp.einsum(
        EQ_STD_DE_TO_STE, normalized_input, wk_all, preferred_element_type=jnp.float32
    ).reshape(sequence_count, token_count, KEY_VALUE_HEADS, HEAD_SIZE)
    value_before_norm = jnp.einsum(
        EQ_STD_DE_TO_STE, normalized_input, wv_all, preferred_element_type=jnp.float32
    ).reshape(sequence_count, token_count, KEY_VALUE_HEADS, HEAD_SIZE)
    q_scale = rms_scale(q_pre)
    k_scale = rms_scale(key_before_norm)
    gain_q = q_gain.astype(jnp.float32)
    gain_k = k_gain.astype(jnp.float32)
    q_rot = rotate(q_pre * q_scale * gain_q, local_angles, 1.0).astype(jnp.bfloat16)
    k_rot = rotate(key_before_norm * k_scale * gain_k, local_angles, 1.0).astype(jnp.bfloat16)
    v_low = value_before_norm.astype(jnp.bfloat16)
    q_heads, k_heads, v_heads = (
        lax.all_to_all(q_rot, ULY, split_axis=2, concat_axis=1, tiled=True),
        lax.all_to_all(k_rot, ULY, split_axis=2, concat_axis=1, tiled=True),
        lax.all_to_all(v_low, ULY, split_axis=2, concat_axis=1, tiled=True),
    )
    q_group = q_heads.reshape(
        sequence_count, block_len, local_key_value, query_group_width, HEAD_SIZE
    )
    stat_shape = (sequence_count, local_key_value, query_group_width, block_len)
    start_state = (
        jnp.full(stat_shape, -1e30, jnp.float32),
        jnp.zeros(stat_shape, jnp.float32),
        jnp.zeros(stat_shape + (HEAD_SIZE,), jnp.float32),
    )
    key_piece = lax.all_gather(k_heads, BLK, axis=1, tiled=True)
    value_piece = lax.all_gather(v_heads, BLK, axis=1, tiled=True)
    key_pos = positions_of(jnp.arange(key_piece.shape[1], dtype=jnp.int32), span_order, half_len)
    allowed = query_pos[:, None] >= key_pos[None, :]

    def attend_one_sequence(members):
        query_rows, key_rows, value_rows, top_seq, total_seq, accum_seq = members
        scores = (
            jnp.einsum(EQ_QKGD_NKD_TO_KGQN, query_rows, key_rows, preferred_element_type=jnp.float32)
            * score_scale
        )
        scores = jnp.where(allowed, scores, -jnp.inf)
        new_top = jnp.maximum(top_seq, jnp.max(scores, axis=-1))
        fading = jnp.exp(top_seq - new_top)
        weights = jnp.exp(scores - new_top[..., None])
        total_seq = total_seq * fading + jnp.sum(weights, axis=-1)
        accum_seq = accum_seq * fading[..., None] + jnp.einsum(
            EQ_KGQN_NKD_TO_KGQD,
            weights.astype(jnp.bfloat16),
            value_rows,
            preferred_element_type=jnp.float32,
        )
        return (new_top, total_seq, accum_seq)

    row_top, row_total, accum = lax.map(
        attend_one_sequence,
        (q_group, key_piece, value_piece, start_state[0], start_state[1], start_state[2]),
    )
    log_total = row_top + jnp.log(row_total)
    attention_output = jnp.transpose(accum / row_total[..., None], (0, 3, 1, 2, 4)).reshape(
        sequence_count, block_len, local_q, HEAD_SIZE
    )
    heads_seq = lax.all_to_all(
        attention_output.astype(jnp.bfloat16), ULY, split_axis=1, concat_axis=2, tiled=True
    )
    heads_flat = heads_seq.reshape(sequence_count, token_count, QUERY_HEADS * HEAD_SIZE)
    middle = source + jnp.einsum(
        EQ_STE_ED_TO_STD, heads_flat, wo_all, preferred_element_type=jnp.float32
    )
    g_mlp, wg_all, wu_all, wd_all = (
        lax.all_gather(mlp_gain, EVERY, axis=0, tiled=True),
        lax.all_gather(w_gate, EVERY, axis=0, tiled=True),
        lax.all_gather(w_up, EVERY, axis=0, tiled=True),
        lax.all_gather(w_down, EVERY, axis=0, tiled=True),
    )
    second_scale = rms_scale(middle)
    gain_mlp = g_mlp.astype(jnp.float32)
    normed2 = (middle * second_scale * gain_mlp).astype(jnp.bfloat16)
    gate_pre = jnp.einsum(EQ_STD_DF_TO_STF, normed2, wg_all, preferred_element_type=jnp.float32)
    up_pre = jnp.einsum(EQ_STD_DF_TO_STF, normed2, wu_all, preferred_element_type=jnp.float32)
    sigmoid_gate = jax.nn.sigmoid(gate_pre)
    activated = (gate_pre * sigmoid_gate * up_pre).astype(jnp.bfloat16)
    result = middle + jnp.einsum(
        EQ_STF_FD_TO_STD, activated, wd_all, preferred_element_type=jnp.float32
    )
    output = result.astype(jnp.bfloat16)
    g_mlp, wg_all, wu_all, wd_all = (
        lax.all_gather(mlp_gain, EVERY, axis=0, tiled=True),
        lax.all_gather(w_gate, EVERY, axis=0, tiled=True),
        lax.all_gather(w_up, EVERY, axis=0, tiled=True),
        lax.all_gather(w_down, EVERY, axis=0, tiled=True),
    )
    gain_mlp = g_mlp.astype(jnp.float32)
    grad_act = jnp.einsum(EQ_STD_FD_TO_STF, cotangent, wd_all, preferred_element_type=jnp.float32)
    grad_gate_pre = (
        grad_act * up_pre * sigmoid_gate * (1.0 + gate_pre * (1.0 - sigmoid_gate))
    ).astype(jnp.bfloat16)
    grad_up_pre = (grad_act * gate_pre * sigmoid_gate).astype(jnp.bfloat16)
    grad_gate = jnp.einsum(
        EQ_STD_STF_TO_DF, normed2, grad_gate_pre, preferred_element_type=jnp.float32
    )
    grad_up = jnp.einsum(EQ_STD_STF_TO_DF, normed2, grad_up_pre, preferred_element_type=jnp.float32)
    grad_normed2 = jnp.einsum(
        EQ_STF_DF_TO_STD, grad_gate_pre, wg_all, preferred_element_type=jnp.float32
    ) + jnp.einsum(EQ_STF_DF_TO_STD, grad_up_pre, wu_all, preferred_element_type=jnp.float32)
    mlp_gain_term = jnp.sum(grad_normed2 * middle * second_scale, axis=(0, 1))
    grad_middle = cotangent.astype(jnp.float32) + norm_back(
        grad_normed2, middle, second_scale, gain_mlp
    )
    grad_mlp_gain, grad_gate, grad_up = (
        lax.psum_scatter(mlp_gain_term, EVERY, scatter_dimension=0, tiled=True),
        lax.psum_scatter(grad_gate, EVERY, scatter_dimension=0, tiled=True),
        lax.psum_scatter(grad_up, EVERY, scatter_dimension=0, tiled=True),
    )
    g_attn, wq_all, wk_all, wv_all, wo_all = (
        lax.all_gather(attn_gain, EVERY, axis=0, tiled=True),
        lax.all_gather(w_query, EVERY, axis=0, tiled=True),
        lax.all_gather(key_weight, EVERY, axis=0, tiled=True),
        lax.all_gather(value_weight, EVERY, axis=0, tiled=True),
        lax.all_gather(w_out, EVERY, axis=0, tiled=True),
    )
    middle_low = grad_middle.astype(jnp.bfloat16)
    grad_out = jnp.einsum(EQ_STE_STD_TO_ED, heads_flat, middle_low, preferred_element_type=jnp.float32)
    grad_heads = (
        jnp.einsum(EQ_STD_ED_TO_STE, middle_low, wo_all, preferred_element_type=jnp.float32)
        .astype(jnp.bfloat16)
        .reshape(sequence_count, token_count, QUERY_HEADS, HEAD_SIZE)
    )
    grad_heads_local = lax.all_to_all(grad_heads, ULY, split_axis=2, concat_axis=1, tiled=True)
    grad_group = jnp.transpose(
        grad_heads_local.reshape(
            sequence_count, block_len, local_key_value, query_group_width, HEAD_SIZE
        ),
        (0, 2, 3, 1, 4),
    )
    delta = jnp.sum(grad_heads_local.astype(jnp.float32) * attention_output, axis=-1)
    delta = jnp.transpose(
        delta.reshape(sequence_count, block_len, local_key_value, query_group_width), (0, 2, 3, 1)
    )
    seq_length = block_len * lax.axis_size(BLK)
    zero_keys = jnp.zeros((sequence_count, seq_length, local_key_value, HEAD_SIZE), jnp.float32)
    back_state = (jnp.zeros(stat_shape + (HEAD_SIZE,), jnp.float32), zero_keys, zero_keys)
    key_piece = lax.all_gather(k_heads, BLK, axis=1, tiled=True)
    value_piece = lax.all_gather(v_heads, BLK, axis=1, tiled=True)
    key_pos = positions_of(jnp.arange(key_piece.shape[1], dtype=jnp.int32), span_order, half_len)
    back_allowed = query_pos[:, None] >= key_pos[None, :]

    def back_one_sequence(members):
        query_rows, grad_rows, lse_seq, delta_seq, key_rows, value_rows, dq_seq, dk_seq, dv_seq = (
            members
        )
        scores = (
            jnp.einsum(EQ_QKGD_NKD_TO_KGQN, query_rows, key_rows, preferred_element_type=jnp.float32)
            * score_scale
        )
        scores = jnp.where(back_allowed, scores, -jnp.inf)
        probs = jnp.exp(scores - lse_seq[..., None])
        grad_values = jnp.einsum(
            EQ_KGQN_KGQD_TO_NKD,
            probs.astype(jnp.bfloat16),
            grad_rows,
            preferred_element_type=jnp.float32,
        )
        grad_probs = jnp.einsum(
            EQ_KGQD_NKD_TO_KGQN, grad_rows, value_rows, preferred_element_type=jnp.float32
        )
        grad_scores = (probs * (grad_probs - delta_seq[..., None])).astype(jnp.bfloat16)
        dq_seq = dq_seq + score_scale * jnp.einsum(
            EQ_KGQN_NKD_TO_KGQD, grad_scores, key_rows, preferred_element_type=jnp.float32
        )
        grad_keys = score_scale * jnp.einsum(
            EQ_KGQN_QKGD_TO_NKD, grad_scores, query_rows, preferred_element_type=jnp.float32
        )
        return (dq_seq, add_rows(dk_seq, grad_keys), add_rows(dv_seq, grad_values))

    grad_q_group, grad_k_whole, grad_v_whole = lax.map(
        back_one_sequence,
        (
            q_group,
            grad_group,
            log_total,
            delta,
            key_piece,
            value_piece,
            back_state[0],
            back_state[1],
            back_state[2],
        ),
    )
    grad_k_block, grad_v_block = (
        lax.psum_scatter(
            grad_k_whole.astype(jnp.bfloat16), BLK, scatter_dimension=1, tiled=True
        ).astype(jnp.float32),
        lax.psum_scatter(
            grad_v_whole.astype(jnp.bfloat16), BLK, scatter_dimension=1, tiled=True
        ).astype(jnp.float32),
    )
    grad_q_block = jnp.transpose(grad_q_group, (0, 3, 1, 2, 4)).reshape(
        sequence_count, block_len, local_q, HEAD_SIZE
    )
    grad_q_seq, grad_k_seq, value_sequence_gradient = (
        lax.all_to_all(
            grad_q_block.astype(jnp.bfloat16), ULY, split_axis=1, concat_axis=2, tiled=True
        ).astype(grad_q_block.dtype),
        lax.all_to_all(
            grad_k_block.astype(jnp.bfloat16), ULY, split_axis=1, concat_axis=2, tiled=True
        ).astype(grad_k_block.dtype),
        lax.all_to_all(
            grad_v_block.astype(jnp.bfloat16), ULY, split_axis=1, concat_axis=2, tiled=True
        ).astype(grad_v_block.dtype),
    )
    grad_q_normed = rotate(grad_q_seq, local_angles, -1.0)
    grad_k_normed = rotate(grad_k_seq, local_angles, -1.0)
    q_gain_term = jnp.sum(grad_q_normed * q_pre * q_scale, axis=(0, 1, 2))
    k_gain_term = jnp.sum(grad_k_normed * key_before_norm * k_scale, axis=(0, 1, 2))
    grad_q_pre = (
        norm_back(grad_q_normed, q_pre, q_scale, gain_q)
        .astype(jnp.bfloat16)
        .reshape(sequence_count, token_count, QUERY_HEADS * HEAD_SIZE)
    )
    grad_k_pre = (
        norm_back(grad_k_normed, key_before_norm, k_scale, gain_k)
        .astype(jnp.bfloat16)
        .reshape(sequence_count, token_count, KEY_VALUE_HEADS * HEAD_SIZE)
    )
    value_pre_gradient = value_sequence_gradient.astype(jnp.bfloat16).reshape(
        sequence_count, token_count, KEY_VALUE_HEADS * HEAD_SIZE
    )
    grad_query = jnp.einsum(
        EQ_STD_STE_TO_DE, normalized_input, grad_q_pre, preferred_element_type=jnp.float32
    )
    grad_key = jnp.einsum(
        EQ_STD_STE_TO_DE, normalized_input, grad_k_pre, preferred_element_type=jnp.float32
    )
    grad_value = jnp.einsum(
        EQ_STD_STE_TO_DE, normalized_input, value_pre_gradient, preferred_element_type=jnp.float32
    )
    grad_normed = jnp.einsum(EQ_STE_DE_TO_STD, grad_q_pre, wq_all, preferred_element_type=jnp.float32)
    grad_normed = grad_normed + jnp.einsum(
        EQ_STE_DE_TO_STD, grad_k_pre, wk_all, preferred_element_type=jnp.float32
    )
    grad_normed = grad_normed + jnp.einsum(
        EQ_STE_DE_TO_STD, value_pre_gradient, wv_all, preferred_element_type=jnp.float32
    )
    attn_gain_term = jnp.sum(grad_normed * source * first_scale, axis=(0, 1))
    grad_hidden = grad_middle + norm_back(
        grad_normed, source, first_scale, g_attn.astype(jnp.float32)
    )
    grad_down = jnp.einsum(EQ_STF_STD_TO_FD, activated, cotangent, preferred_element_type=jnp.float32)
    grad_attn_gain, grad_query, grad_key, grad_value, grad_out, grad_down = (
        lax.psum_scatter(attn_gain_term, EVERY, scatter_dimension=0, tiled=True),
        lax.psum_scatter(grad_query, EVERY, scatter_dimension=0, tiled=True),
        lax.psum_scatter(grad_key, EVERY, scatter_dimension=0, tiled=True),
        lax.psum_scatter(grad_value, EVERY, scatter_dimension=0, tiled=True),
        lax.psum_scatter(grad_out, EVERY, scatter_dimension=0, tiled=True),
        lax.psum_scatter(grad_down, EVERY, scatter_dimension=0, tiled=True),
    )
    grad_q_gain, grad_k_gain = lax.psum((q_gain_term, k_gain_term), EVERY)
    return (
        output,
        grad_hidden,
        grad_attn_gain,
        grad_query,
        grad_key,
        grad_value,
        grad_out,
        grad_q_gain,
        grad_k_gain,
        grad_mlp_gain,
        grad_gate,
        grad_up,
        grad_down,
    )


MESH = pl.DeviceIdType.MESH
HBM = pl.BlockSpec(memory_space=pltpu.HBM)
VMEM = pl.BlockSpec(memory_space=pltpu.VMEM)
MIB = 1 << 20


def kernel_params(collective_id, vmem_mib=48):
    return pltpu.CompilerParams(
        collective_id=collective_id, has_side_effects=True, vmem_limit_bytes=vmem_mib * MIB
    )


def semaphores(count, local=16):
    return [
        pltpu.SemaphoreType.DMA((count,)),
        pltpu.SemaphoreType.DMA((count,)),
        pltpu.SemaphoreType.DMA((local,)),
    ]


class Copy:
    def __init__(self, descriptor, sends, receives):
        self.descriptor, self.sends, self.receives = descriptor, sends, receives

    def under(self, condition, action):
        if condition is None:
            action()
        else:
            pl.when(condition)(action)

    def start(self):
        self.under(self.sends, lambda: self.descriptor().start())
        return self

    def sent(self):
        self.under(self.sends, lambda: self.descriptor().wait_send())

    def arrived(self):
        self.under(self.receives, lambda: self.descriptor().wait_recv())


class Links:
    def __init__(self, send, recv, here):
        self.send, self.recv, self.here = send, recv, here
        self.used, self.used_here = 0, 0
        self.copies, self.local_copies = [], []
        self.n_dp, self.n_blk, self.n_uly = (lax.axis_size(a) for a in EVERY)
        self.dp, self.blk, self.uly = (lax.axis_index(a) for a in EVERY)
        self.other_dp = 1 - self.dp
        self.across = lax.rem(self.uly + 2, 4)
        self.twin = self.uly + 1 - 2 * lax.rem(self.uly, 2)
        self.x_way = (self.other_dp, self.blk, self.uly)
        self.y_way = (self.dp, self.blk, self.across)
        self.core_way = (self.dp, self.blk, self.twin)

    def peer(self, step):
        return lax.rem(self.blk + step, self.n_blk)

    def peers(self):
        return [(self.dp, self.peer(k), self.uly) for k in range(1, self.n_blk)]

    def greet(self, devices):
        barrier = pltpu.get_barrier_semaphore()
        for device in devices:
            pl.semaphore_signal(barrier, inc=1, device_id=device, device_id_type=MESH)
        pl.semaphore_wait(barrier, len(devices))

    def remote(self, source, target, device, sends=None, receives=None):
        slot = self.used
        self.used += 1

        def descriptor():
            return pltpu.make_async_remote_copy(
                src_ref=source(),
                dst_ref=target(),
                send_sem=self.send.at[slot],
                recv_sem=self.recv.at[slot],
                device_id=device,
                device_id_type=MESH,
            )

        copy = Copy(descriptor, sends, receives)
        self.copies.append(copy)
        return copy.start()

    def to(self, source, target, device):
        return self.remote(lambda: source, lambda: target, device)

    def local(self, source, target):
        copy = pltpu.make_async_copy(source, target, self.here.at[self.used_here])
        self.used_here += 1
        copy.start()
        self.local_copies.append(copy)
        return copy

    def finish(self):
        for copy in self.copies:
            copy.sent()


class LineGather:
    def __init__(self, links, own, whole):
        self.links, self.own, self.whole = links, own, whole
        self.waiting = []

    def send(self, step):
        links, whole = self.links, self.whole
        blk, last = links.blk, links.n_blk - 1

        def block(index):
            if step == 0:
                return lambda: self.own
            return lambda: whole.at[index]

        self.waiting = [
            links.remote(
                block(blk - step),
                lambda: whole.at[blk - step],
                (links.dp, blk + 1, links.uly),
                jnp.logical_and(blk >= step, blk < last),
                blk >= step + 1,
            ),
            links.remote(
                block(blk + step),
                lambda: whole.at[blk + step],
                (links.dp, blk - 1, links.uly),
                jnp.logical_and(blk + step <= last, blk > 0),
                blk + step + 1 <= last,
            ),
        ]

    def arrived(self):
        for copy in self.waiting:
            copy.arrived()


class PlaneGather:
    def __init__(self, links, at):
        self.links, self.at = links, at

    def start(self, own=None):
        links, at = self.links, self.at
        mine = at(links.dp, links.uly)
        own = mine if own is None else own
        self.from_x = links.to(own, mine, links.x_way)
        self.from_y = links.to(own, mine, links.y_way)
        self.from_core = [links.to(own, mine, links.core_way)]

    def hand_on(self):
        links, at = self.links, self.at
        self.from_x.arrived()
        half = at(links.other_dp, links.uly, 0)
        self.second_y = links.to(half, half, links.y_way)
        self.from_y.arrived()
        half = at(links.dp, links.across, 1)
        self.second_x = links.to(half, half, links.x_way)
        for chunk in (at(links.other_dp, links.uly), at(links.dp, links.across)):
            self.from_core.append(links.to(chunk, chunk, links.core_way))

    def last(self):
        links = self.links
        self.second_y.arrived()
        self.second_x.arrived()
        chunk = self.at(links.other_dp, links.across)
        self.from_core.append(links.to(chunk, chunk, links.core_way))

    def arrived(self):
        for copy in self.from_core:
            copy.arrived()


def rows_of(whole, blocked):
    def at(dp, uly, half=None):
        part = whole.at[dp, :, uly] if blocked else whole.at[dp, uly]
        if half is None:
            return part
        depth = whole.shape[-2] // 2
        rows = pl.ds(half * depth, depth)
        return part.at[:, rows] if blocked else part.at[rows]

    return at


class ColumnSwap:
    def __init__(self, links, pieces):
        self.links, self.pieces = links, pieces
        self.incoming, self.kept = [], []

    def parts(self, blk):
        links = self.links
        for weight, whole, offset in self.pieces:
            width = weight.shape[-1] // links.n_dp // links.n_blk
            for group in range(links.n_dp):
                start = (group * links.n_blk + blk) * width
                yield (
                    weight.at[:, pl.ds(pl.multiple_of(start, 128), width)],
                    whole.at[
                        links.dp, links.blk, links.uly, :, pl.ds(offset + group * width, width)
                    ],
                )

    def start(self):
        links = self.links
        for step in range(1, links.n_blk):
            device = (links.dp, links.peer(step), links.uly)
            for source, target in self.parts(links.peer(step)):
                self.incoming.append(links.to(source, target, device))
        for source, target in self.parts(links.blk):
            self.kept.append(links.local(source, target))

    def arrived(self):
        for copy in self.kept:
            copy.wait()
        for copy in self.incoming:
            copy.arrived()


def front_kernel(
    hidden,
    wq,
    wk,
    wv,
    wo,
    wd,
    gains,
    all_hidden,
    w_qkv,
    all_wo,
    all_wd,
    all_gains,
    send,
    recv,
    here,
):
    links = Links(send, recv, here)
    links.greet(links.peers() + [links.x_way, links.y_way, links.core_way])
    q_width, k_width = wq.shape[1] // links.n_blk, wk.shape[1] // links.n_blk
    swap = ColumnSwap(
        links, [(wq, w_qkv, 0), (wk, w_qkv, q_width), (wv, w_qkv, q_width + k_width)]
    )
    swap.start()
    gain_swap = []
    my_gains = all_gains.at[links.dp, links.blk, links.uly]
    for device in links.peers():
        gain_swap.append(links.to(gains, my_gains, device))
    keep = [
        links.local(gains, my_gains),
        links.local(hidden, all_hidden.at[links.blk]),
        links.local(wo, all_wo.at[links.dp, links.uly]),
        links.local(wd, all_wd.at[links.dp, links.uly]),
    ]
    line = LineGather(links, hidden, all_hidden)
    line.send(0)
    plane_wo = PlaneGather(links, rows_of(all_wo, False))
    plane_wo.start(wo)
    plane_qkv = PlaneGather(links, rows_of(w_qkv, True))
    plane_gain = PlaneGather(links, rows_of(all_gains, True))
    plane_wd = PlaneGather(links, rows_of(all_wd, False))
    swap.arrived()
    plane_qkv.start()
    keep[0].wait()
    for copy in gain_swap:
        copy.arrived()
    plane_gain.start()
    plane_wd.start(wd)
    for step in range(1, links.n_blk - 1):
        line.arrived()
        line.send(step)
        if step == 1:
            plane_wo.hand_on()
            plane_qkv.hand_on()
            plane_gain.hand_on()
    plane_wd.hand_on()
    plane_wo.last()
    plane_qkv.last()
    plane_gain.last()
    plane_wd.last()
    line.arrived()
    for plane in (plane_wo, plane_qkv, plane_gain, plane_wd):
        plane.arrived()
    for copy in keep[1:]:
        copy.wait()
    links.finish()


def gather_front(hidden, wq, wk, wv, wo, wd, gains):
    n_dp, n_blk, n_uly = (lax.axis_size(a) for a in EVERY)
    qkv_width = (wq.shape[1] + wk.shape[1] + wv.shape[1]) // n_blk
    shapes = [
        (n_blk,) + hidden.shape,
        (n_dp, n_blk, n_uly, wq.shape[0], qkv_width),
        (n_dp, n_uly) + wo.shape,
        (n_dp, n_uly) + wd.shape,
        (n_dp, n_blk, n_uly) + gains.shape,
    ]
    return pl.pallas_call(
        front_kernel,
        out_shape=[jax.ShapeDtypeStruct(s, jnp.bfloat16) for s in shapes],
        in_specs=[HBM] * 7,
        out_specs=[HBM] * 5,
        scratch_shapes=semaphores(72),
        compiler_params=kernel_params(0),
    )(hidden, wq, wk, wv, wo, wd, gains)


ROWS = 32


def each_block(count, body):
    def step(index, carry):
        body(pl.ds(pl.multiple_of(index * ROWS, ROWS), ROWS))
        return carry

    lax.fori_loop(0, count // ROWS, step, 0)


class LineScatter:
    def __init__(self, links, parts, rightward, leftward):
        self.links, self.parts = links, parts
        self.slots = {1: rightward, -1: leftward}
        self.tokens = parts.shape[1]
        self.number = links.used
        links.used += 2 * (links.n_blk - 1)

    def place(self, step, way):
        blk, last = self.links.blk, self.links.n_blk - 1
        target = last - step if way == 1 else step
        slot = self.slots[way].at[target - 1 if way == 1 else target]
        first = blk == (0 if way == 1 else last)
        beyond = target > blk if way == 1 else target < blk
        return target, slot, first, beyond

    def copy(self, step, way, source=None):
        links, (_, slot, _, _) = self.links, self.place(step, way)
        number = self.number + 2 * step + (way == 1)
        return pltpu.make_async_remote_copy(
            src_ref=slot if source is None else source,
            dst_ref=slot,
            send_sem=links.send.at[number],
            recv_sem=links.recv.at[number],
            device_id=(links.dp, links.blk + way, links.uly),
            device_id_type=MESH,
        )

    def start(self):
        for step in range(self.links.n_blk - 1):
            for way in (1, -1):
                target, _, first, beyond = self.place(step, way)

                @pl.when(jnp.logical_and(first, beyond))
                def _(step=step, way=way, target=target):
                    self.copy(step, way, self.parts.at[target]).start()

    def move(self, step, way):
        parts = self.parts
        target, slot, first, beyond = self.place(step, way)

        @pl.when(jnp.logical_and(jnp.logical_not(first), beyond))
        def _():
            self.copy(step, way).wait_recv()

            def body(rows):
                slot[rows, :] = slot[rows, :] + parts[target, rows, :]

            each_block(self.tokens, body)
            self.copy(step, way).start()

    def step(self, step):
        early = 2 * self.links.blk < self.links.n_blk

        @pl.when(early)
        def _():
            self.move(step, 1)
            self.move(step, -1)

        @pl.when(jnp.logical_not(early))
        def _():
            self.move(step, -1)
            self.move(step, 1)

    def finish(self, total):
        links, parts = self.links, self.parts
        blk, last = links.blk, links.n_blk - 1
        for step in range(last):
            for way in (1, -1):
                target, _, first, _ = self.place(step, way)
                here = jnp.logical_and(jnp.logical_not(first), target == blk)
                pl.when(here)(lambda step=step, way=way: self.copy(step, way).wait_recv())

        def start(rows):
            total[rows, :] = parts[blk, rows, :].astype(jnp.float32)

        each_block(self.tokens, start)
        for way, condition, index in ((1, blk > 0, blk - 1), (-1, blk < last, blk)):

            def add(way=way, index=index):
                def body(rows):
                    term = self.slots[way][index, rows, :]
                    total[rows, :] = total[rows, :] + term.astype(jnp.float32)

                each_block(self.tokens, body)

            pl.when(condition)(add)

    def sent(self):
        for step in range(self.links.n_blk - 1):
            for way in (1, -1):
                _, _, _, beyond = self.place(step, way)
                pl.when(beyond)(lambda step=step, way=way: self.copy(step, way).wait_send())


def line_scratch(n_blk, tokens, width):
    return [pltpu.VMEM((n_blk - 1, tokens, width), jnp.bfloat16)] * 2


class PlaneScatter:
    def __init__(self, links, parts, from_core, from_x, from_y, last_x, last_y):
        self.links, self.parts = links, parts
        self.from_core, self.from_x, self.from_y = from_core, from_x, from_y
        self.last_x, self.last_y = last_x, last_y
        self.core = lax.rem(links.uly, 2)
        self.row = lax.div(links.uly, 2)
        self.depth = parts.shape[3]
        self.core_copies = {}

    def chunk(self, dp, row, core, half=None):
        uly = row * 2 + core
        if half is None:
            return self.parts.at[dp, :, uly]
        depth = self.depth // 2
        return self.parts.at[dp, :, uly, pl.ds(half * depth, depth)]

    def add(self, target, source):
        blocks, depth, _ = target.shape
        rows = 32 if depth % 32 == 0 else 16

        def body(index, carry):
            block = lax.div(index, depth // rows)
            at = pl.ds(pl.multiple_of(lax.rem(index, depth // rows) * rows, rows), rows)
            target[block, at, :] = target[block, at, :] + source[block, at, :]
            return carry

        lax.fori_loop(0, blocks * (depth // rows), body, 0)

    def between_cores(self, which):
        links = self.links
        dp = links.dp if which == 1 else links.other_dp
        self.core_copies[which] = [
            links.to(
                self.chunk(dp, row, 1 - self.core), self.from_core.at[which, row], links.core_way
            )
            for row in range(2)
        ]

    def across_chips(self):
        links = self.links
        self.x_copies, self.y_copies = [], []
        for which, dp in ((0, links.other_dp), (1, links.dp)):
            for row in range(2):
                self.core_copies[which][row].arrived()
                self.add(self.chunk(dp, row, self.core), self.from_core.at[which, row])
            if which == 0:
                for row in range(2):
                    self.x_copies.append(
                        links.to(
                            self.chunk(dp, row, self.core, 0), self.from_x.at[row], links.x_way
                        )
                    )
        for group in range(links.n_dp):
            self.y_copies.append(
                links.to(
                    self.chunk(group, 1 - self.row, self.core, 1),
                    self.from_y.at[group],
                    links.y_way,
                )
            )

    def second_way(self):
        links = self.links
        for row in range(2):
            self.x_copies[row].arrived()
            self.add(self.chunk(links.dp, row, self.core, 0), self.from_x.at[row])
        self.y_last = links.to(
            self.chunk(links.dp, 1 - self.row, self.core, 0), self.last_y, links.y_way
        )
        for group in range(links.n_dp):
            self.y_copies[group].arrived()
            self.add(self.chunk(group, self.row, self.core, 1), self.from_y.at[group])
        self.x_last = links.to(
            self.chunk(links.other_dp, self.row, self.core, 1), self.last_x, links.x_way
        )

    def result(self, write):
        links = self.links
        for half, copy, source in ((0, self.y_last, self.last_y), (1, self.x_last, self.last_x)):
            copy.arrived()
            own = self.chunk(links.dp, self.row, self.core, half)
            blocks, depth, _ = source.shape
            rows = 32 if depth % 32 == 0 else 16

            def body(index, carry, own=own, source=source, half=half, depth=depth, rows=rows):
                block = lax.div(index, depth // rows)
                start = pl.multiple_of(lax.rem(index, depth // rows) * rows, rows)
                at = pl.ds(start, rows)
                value = own[block, at, :].astype(jnp.float32)
                value = value + source[block, at, :].astype(jnp.float32)
                write(block, pl.ds(pl.multiple_of(start + half * depth, rows), rows), value)
                return carry

            lax.fori_loop(0, blocks * (depth // rows), body, 0)


def plane_scratch(n_dp, blocks, n_uly, depth, width):
    shapes = [
        (n_dp, blocks, n_uly, depth, width),
        (n_dp, 2, blocks, depth, width),
        (2, blocks, depth // 2, width),
        (n_dp, blocks, depth // 2, width),
        (blocks, depth // 2, width),
        (blocks, depth // 2, width),
    ]
    return [pltpu.VMEM(shape, jnp.bfloat16) for shape in shapes]


def weight_grad(left, right, parts, dp, together):
    _, blocks, n_uly, depth, width = parts.shape
    steps = n_uly // together
    columns = 512

    def body(index, carry):
        block, step = lax.div(index, steps), lax.rem(index, steps)
        start = ((dp * blocks + block) * n_uly + step * together) * depth
        rows = left[:, pl.ds(pl.multiple_of(start, 128), together * depth)].T
        for column in range(0, width, columns):
            part = jnp.dot(
                rows, right[:, column : column + columns], preferred_element_type=jnp.float32
            )
            parts[dp, block, pl.ds(step * together, together), :, column : column + columns] = (
                part.astype(jnp.bfloat16).reshape(together, depth, columns)
            )
        return carry

    lax.fori_loop(0, blocks * steps, body, 0)


def turned(rows, cosine, sine):
    return rows * cosine + pltpu.roll(rows, HEAD_SIZE // 2, axis=1) * sine


def transposed_product(left, right):
    return lax.dot_general(
        left, right, (((0,), (0,)), ((), ())), preferred_element_type=jnp.float32
    )


def product_right(left, right):
    return lax.dot_general(
        left, right, (((1,), (1,)), ((), ())), preferred_element_type=jnp.float32
    )


SCORE_SCALE = 1.0 / math.sqrt(HEAD_SIZE)


def mask_scores(bias, query_pos, key_pos):
    size = bias.shape[0] // 4

    def body(index, carry):
        rows = pl.ds(pl.multiple_of(index * size, size), size)
        bias[rows, :] = jnp.where(query_pos[...] >= key_pos[rows, :], 0.0, -1e30)
        return carry

    lax.fori_loop(0, 4, body, 0)


class RowBlocks:
    def __init__(self, n_blk, seqs, toks):
        self.n_blk, self.seqs, self.toks = n_blk, seqs, toks

    def each(self, body):
        def step(index, carry):
            blk, seq = lax.div(index, self.seqs), lax.rem(index, self.seqs)
            body(
                seq,
                pl.ds(pl.multiple_of(index * self.toks, self.toks), self.toks),
                pl.multiple_of(blk * self.toks, self.toks),
            )
            return carry

        lax.fori_loop(0, self.n_blk * self.seqs, step, 0)


def attention_kernel(
    wg,
    wu,
    cotangent,
    hidden,
    w_qkv,
    gain,
    q_gain,
    k_gain,
    cosine,
    sine,
    query_pos,
    key_pos,
    all_wg,
    all_wu,
    all_cot,
    heads,
    normed,
    qkv,
    queries,
    key_values,
    lse,
    bias,
    send,
    recv,
    here,
):
    links = Links(send, recv, here)
    links.greet(links.peers() + [links.x_way, links.y_way, links.core_way])
    swaps = [ColumnSwap(links, [(wg, all_wg, 0)]), ColumnSwap(links, [(wu, all_wu, 0)])]
    for swap in swaps:
        swap.start()
    keep = links.local(cotangent, all_cot.at[links.blk])
    planes = [PlaneGather(links, rows_of(w, True)) for w in (all_wg, all_wu)]

    def norm(rows):
        source = hidden[rows, :].astype(jnp.float32)
        normed[rows, :] = (source * rms_scale(source) * gain[...]).astype(jnp.bfloat16)

    each_block(hidden.shape[0], norm)
    for column in range(0, qkv.shape[1], 256):
        qkv[:, column : column + 256] = jnp.dot(
            normed[...], w_qkv[:, column : column + 256], preferred_element_type=jnp.float32
        )
    seqs, kv_heads, q_rows, _ = queries.shape
    q_len = key_values.shape[4]
    group = q_rows // q_len
    blocks = RowBlocks(links.n_blk, seqs, q_len // links.n_blk)
    q_end = kv_heads * group * HEAD_SIZE
    k_end = q_end + kv_heads * HEAD_SIZE

    def place_keys(seq, rows, start):
        at = pl.ds(start, blocks.toks)
        for head in range(kv_heads):
            k_pre = qkv[rows, q_end + head * HEAD_SIZE : q_end + (head + 1) * HEAD_SIZE]
            k_row = turned(k_pre * rms_scale(k_pre) * k_gain[...], cosine[at, :], sine[at, :])
            v_row = qkv[rows, k_end + head * HEAD_SIZE : k_end + (head + 1) * HEAD_SIZE]
            key_values[links.uly, 0, seq, head, at, :] = k_row.astype(jnp.bfloat16)
            key_values[links.uly, 1, seq, head, at, :] = v_row.astype(jnp.bfloat16)

    blocks.each(place_keys)
    mine = key_values.at[links.uly]
    kv_core = links.to(mine, mine, links.core_way)
    kv_across = links.to(mine, mine, links.y_way)

    def place_queries(seq, rows, start):
        at = pl.ds(start, blocks.toks)
        for head in range(kv_heads * group):
            q_pre = qkv[rows, head * HEAD_SIZE : (head + 1) * HEAD_SIZE]
            q_row = turned(q_pre * rms_scale(q_pre) * q_gain[...], cosine[at, :], sine[at, :])
            to = pl.ds((head % group) * q_len + start, blocks.toks)
            queries[seq, head // group, to, :] = q_row.astype(jnp.bfloat16)

    blocks.each(place_queries)
    mask_scores(bias, query_pos, key_pos)
    swaps[0].arrived()
    planes[0].start()
    kv_across.arrived()
    theirs = key_values.at[links.across]
    kv_last = links.to(theirs, theirs, links.core_way)
    swaps[1].arrived()
    planes[1].start()
    line = LineGather(links, cotangent, all_cot)
    line.send(0)
    kv_core.arrived()
    kv_last.arrived()

    def attend(seq, head):
        def over_keys(piece, carry):
            total, mixed = carry
            rows = pl.ds(pl.multiple_of(piece * q_len, q_len), q_len)
            scores = product_right(key_values[piece, 0, seq, head], queries[seq, head])
            weights = jnp.exp(scores * SCORE_SCALE + bias[rows, :])
            total = total + jnp.sum(weights, axis=0, keepdims=True)
            mixed = mixed + transposed_product(
                key_values[piece, 1, seq, head], weights.astype(jnp.bfloat16)
            )
            return total, mixed

        total, mixed = lax.fori_loop(
            0,
            links.n_uly,
            over_keys,
            (
                jnp.zeros((1, q_rows), jnp.float32),
                jnp.zeros((HEAD_SIZE, q_rows), jnp.float32),
            ),
        )
        lse[seq * kv_heads + head] = jnp.log(total)
        attended = (mixed / total).T.astype(jnp.bfloat16)
        for member in range(group):
            column = (head * group + member) * HEAD_SIZE
            for blk in range(links.n_blk):
                row = (blk * seqs + seq) * blocks.toks
                start = member * q_len + blk * blocks.toks
                heads[row : row + blocks.toks, column : column + HEAD_SIZE] = attended[
                    start : start + blocks.toks, :
                ]

    def service_a():
        planes[0].hand_on()

    def service_b():
        line.arrived()
        line.send(1)
        planes[1].hand_on()

    def service_c():
        planes[0].last()
        for step in range(2, links.n_blk - 1):
            line.arrived()
            line.send(step)

    pairs = [(seq, head) for seq in range(seqs) for head in range(kv_heads)]
    services = [service_a, service_b, service_c]
    for number, (seq, head) in enumerate(pairs):
        attend(seq, head)
        if number < len(services):
            services[number]()
    for service in services[len(pairs) :]:
        service()
    planes[1].last()
    line.arrived()
    for plane in planes:
        plane.arrived()
    keep.wait()
    links.finish()


def attend_forward(
    wg, wu, cotangent, hidden, w_qkv, gain, q_gain, k_gain, cosine, sine, query_pos, key_pos, seqs
):
    n_dp, n_blk, n_uly = (lax.axis_size(a) for a in EVERY)
    rows = hidden.shape[0]
    kv_heads = KEY_VALUE_HEADS // n_blk
    q_len, q_rows = rows // seqs, query_pos.shape[1]
    low = [
        (n_dp, n_blk, n_uly, wg.shape[0], wg.shape[1] // n_blk),
        (n_dp, n_blk, n_uly, wu.shape[0], wu.shape[1] // n_blk),
        (n_blk,) + cotangent.shape,
        (rows, QUERY_HEADS // n_blk * HEAD_SIZE),
        hidden.shape,
    ]
    shapes = [jax.ShapeDtypeStruct(s, jnp.bfloat16) for s in low] + [
        jax.ShapeDtypeStruct((rows, w_qkv.shape[1]), jnp.float32),
        jax.ShapeDtypeStruct((seqs, kv_heads, q_rows, HEAD_SIZE), jnp.bfloat16),
        jax.ShapeDtypeStruct((n_uly, 2, seqs, kv_heads, q_len, HEAD_SIZE), jnp.bfloat16),
        jax.ShapeDtypeStruct((seqs * kv_heads, 1, q_rows), jnp.float32),
    ]
    return pl.pallas_call(
        attention_kernel,
        out_shape=shapes,
        in_specs=[HBM] * 3 + [VMEM] * 9,
        out_specs=[HBM] * 3 + [VMEM] * 6,
        scratch_shapes=[pltpu.VMEM((key_pos.shape[0], q_rows), jnp.float32)] + semaphores(48),
        compiler_params=kernel_params(1),
    )(
        wg,
        wu,
        cotangent,
        hidden,
        w_qkv,
        gain,
        q_gain,
        k_gain,
        cosine,
        sine,
        query_pos,
        key_pos,
    )


def attention_back_kernel(
    all_low,
    wo,
    queries,
    key_values,
    lse,
    qkv,
    q_gain,
    k_gain,
    cosine,
    sine,
    query_pos,
    key_pos,
    grad_gate,
    grad_up,
    grad_qkv,
    gain_terms,
    gate_rows,
    up_rows,
    bias,
    grad_heads,
    grad_rows,
    probs,
    grad_probs,
    grad_kv,
    from_core,
    from_across,
    send,
    recv,
    here,
):
    links = Links(send, recv, here)
    links.greet(links.peers() + [links.y_way, links.core_way])
    swapped, keep = [], []
    for source, target in ((grad_gate, gate_rows), (grad_up, up_rows)):
        for step in range(1, links.n_blk):
            peer = links.peer(step)
            swapped.append(
                links.to(source.at[peer], target.at[links.blk], (links.dp, peer, links.uly))
            )
        keep.append(links.local(source.at[links.blk], target.at[links.blk]))
    grad_heads[...] = product_right(all_low[...], wo[...])
    mask_scores(bias, query_pos, key_pos)
    seqs, kv_heads, q_rows, _ = queries.shape
    q_len = key_values.shape[4]
    group = q_rows // q_len
    blocks = RowBlocks(links.n_blk, seqs, q_len // links.n_blk)
    q_end = kv_heads * group * HEAD_SIZE
    k_end = q_end + kv_heads * HEAD_SIZE
    gain_terms[...] = jnp.zeros_like(gain_terms)

    def gather_rows(seq, rows, start):
        for head in range(kv_heads * group):
            to = pl.ds((head % group) * q_len + start, blocks.toks)
            grad_rows[seq, head // group, to, :] = grad_heads[
                rows, head * HEAD_SIZE : (head + 1) * HEAD_SIZE
            ].astype(jnp.bfloat16)

    blocks.each(gather_rows)

    def back_norm(upstream, pre, gain, at, which):
        upstream = turned(upstream, cosine[at, :], -sine[at, :])
        back, term = back_rows(upstream, pre, gain[...])
        gain_terms[which : which + 1, :] += term
        return back.astype(jnp.bfloat16)

    def back(seq, head):
        def first(piece, delta):
            rows = pl.ds(pl.multiple_of(piece * q_len, q_len), q_len)
            scores = product_right(key_values[piece, 0, seq, head], queries[seq, head])
            prob = jnp.exp(
                scores * SCORE_SCALE + bias[rows, :] - lse[seq * kv_heads + head]
            )
            grad_prob = product_right(key_values[piece, 1, seq, head], grad_rows[seq, head])
            probs[rows, :] = prob
            grad_probs[rows, :] = grad_prob
            return delta + jnp.sum(prob * grad_prob, axis=0, keepdims=True)

        delta = lax.fori_loop(0, links.n_uly, first, jnp.zeros((1, q_rows), jnp.float32))

        def second(piece, grad_query):
            rows = pl.ds(pl.multiple_of(piece * q_len, q_len), q_len)
            prob = probs[rows, :]
            grad_score = (prob * (grad_probs[rows, :] - delta)).astype(jnp.bfloat16)
            grad_kv[seq, piece, 0, head] = (
                SCORE_SCALE
                * jnp.dot(grad_score, queries[seq, head], preferred_element_type=jnp.float32)
            ).astype(jnp.bfloat16)
            grad_kv[seq, piece, 1, head] = jnp.dot(
                prob.astype(jnp.bfloat16),
                grad_rows[seq, head],
                preferred_element_type=jnp.float32,
            ).astype(jnp.bfloat16)
            return grad_query + transposed_product(key_values[piece, 0, seq, head], grad_score)

        grad_query = lax.fori_loop(
            0, links.n_uly, second, jnp.zeros((HEAD_SIZE, q_rows), jnp.float32)
        )
        grad_heads[:, :HEAD_SIZE] = (grad_query * SCORE_SCALE).T
        for member in range(group):
            column = (head * group + member) * HEAD_SIZE
            for blk in range(links.n_blk):
                row = (blk * seqs + seq) * blocks.toks
                at = pl.ds(blk * blocks.toks, blocks.toks)
                start = member * q_len + blk * blocks.toks
                grad_qkv[row : row + blocks.toks, column : column + HEAD_SIZE] = back_norm(
                    grad_heads[start : start + blocks.toks, :HEAD_SIZE],
                    qkv[row : row + blocks.toks, column : column + HEAD_SIZE],
                    q_gain,
                    at,
                    0,
                )

    core, line = lax.rem(links.uly, 2), lax.div(links.uly, 2)

    def add(target, source):
        for kind in range(2):
            for head in range(kv_heads):
                target[kind, head] = target[kind, head] + source[kind, head]

    def core_sums(seq):
        copies = [
            links.to(
                grad_kv.at[seq, row * 2 + 1 - core], from_core.at[seq, row], links.core_way
            )
            for row in range(2)
        ]
        return copies

    def across_sums(seq, copies):
        for row in range(2):
            copies[row].arrived()
            add(grad_kv.at[seq, row * 2 + core], from_core.at[seq, row])
        return links.to(
            grad_kv.at[seq, (1 - line) * 2 + core], from_across.at[seq], links.y_way
        )

    def own_keys(seq, copy):
        copy.arrived()
        for head in range(kv_heads):
            for blk in range(links.n_blk):
                row = (blk * seqs + seq) * blocks.toks
                at = pl.ds(blk * blocks.toks, blocks.toks)
                term = [
                    grad_kv[seq, links.uly, kind, head, at, :].astype(jnp.float32)
                    + from_across[seq, kind, head, at, :].astype(jnp.float32)
                    for kind in range(2)
                ]
                k_at = q_end + head * HEAD_SIZE
                v_at = k_end + head * HEAD_SIZE
                grad_qkv[row : row + blocks.toks, k_at : k_at + HEAD_SIZE] = back_norm(
                    term[0],
                    qkv[row : row + blocks.toks, k_at : k_at + HEAD_SIZE],
                    k_gain,
                    at,
                    1,
                )
                grad_qkv[row : row + blocks.toks, v_at : v_at + HEAD_SIZE] = term[1].astype(
                    jnp.bfloat16
                )

    stage, last = None, []
    for seq in range(seqs):
        for head in range(kv_heads):
            back(seq, head)
            if stage is not None:
                last.append((seq - 1, across_sums(seq - 1, stage)))
                stage = None
        stage = core_sums(seq)
    last.append((seqs - 1, across_sums(seqs - 1, stage)))
    for seq, copy in last:
        own_keys(seq, copy)
    for copy in keep:
        copy.wait()
    for copy in swapped:
        copy.arrived()
    links.finish()


def attend_back(
    all_low,
    wo,
    queries,
    key_values,
    lse,
    qkv,
    q_gain,
    k_gain,
    cosine,
    sine,
    query_pos,
    key_pos,
    grad_gate,
    grad_up,
):
    seqs, kv_heads, q_rows, _ = queries.shape
    n_uly, _, _, _, q_len, _ = key_values.shape
    rows = all_low.shape[0]
    keys = key_pos.shape[0]
    f32, low = jnp.float32, jnp.bfloat16
    scratch = [
        ((keys, q_rows), f32),
        ((rows, wo.shape[0]), f32),
        (queries.shape, low),
        ((keys, q_rows), f32),
        ((keys, q_rows), f32),
        ((seqs, n_uly, 2, kv_heads, q_len, HEAD_SIZE), low),
        ((seqs, 2, 2, kv_heads, q_len, HEAD_SIZE), low),
        ((seqs, 2, kv_heads, q_len, HEAD_SIZE), low),
    ]
    return pl.pallas_call(
        attention_back_kernel,
        out_shape=[
            jax.ShapeDtypeStruct(qkv.shape, low),
            jax.ShapeDtypeStruct((8, HEAD_SIZE), f32),
            jax.ShapeDtypeStruct(grad_gate.shape, low),
            jax.ShapeDtypeStruct(grad_up.shape, low),
        ],
        in_specs=[VMEM] * 12 + [HBM] * 2,
        out_specs=[VMEM] * 2 + [HBM] * 2,
        scratch_shapes=[pltpu.VMEM(shape, kind) for shape, kind in scratch] + semaphores(24),
        compiler_params=kernel_params(5),
    )(
        all_low,
        wo,
        queries,
        key_values,
        lse,
        qkv,
        q_gain,
        k_gain,
        cosine,
        sine,
        query_pos,
        key_pos,
        grad_gate,
        grad_up,
    )


def middle_kernel(
    heads,
    wo,
    source,
    gain,
    middle,
    all_normed,
    parts,
    rightward,
    leftward,
    normed,
    send,
    recv,
    here,
):
    links = Links(send, recv, here)
    links.greet(links.peers())
    tokens = source.shape[0]
    for blk in (links.n_blk - 1, 0) + tuple(range(1, links.n_blk - 1)):
        parts[blk] = jnp.dot(heads[blk], wo[...], preferred_element_type=jnp.float32).astype(
            jnp.bfloat16
        )
    scatter = LineScatter(links, parts, rightward, leftward)
    scatter.start()
    for step in range(links.n_blk - 1):
        scatter.step(step)
    scatter.finish(middle)

    def body(rows):
        total = middle[rows, :] + source[rows, :].astype(jnp.float32)
        middle[rows, :] = total
        normed[rows, :] = (total * rms_scale(total) * gain[...]).astype(jnp.bfloat16)

    each_block(tokens, body)
    keep = links.local(normed, all_normed.at[links.blk])
    line = LineGather(links, normed, all_normed)
    for step in range(links.n_blk - 1):
        line.send(step)
        line.arrived()
    keep.wait()
    scatter.sent()
    links.finish()


def exchange_middle(heads, wo, source, gain):
    n_blk = lax.axis_size(BLK)
    tokens, width = source.shape
    return pl.pallas_call(
        middle_kernel,
        out_shape=[
            jax.ShapeDtypeStruct((tokens, width), jnp.float32),
            jax.ShapeDtypeStruct((n_blk, tokens, width), jnp.bfloat16),
        ],
        in_specs=[VMEM] * 4,
        out_specs=[VMEM, HBM],
        scratch_shapes=[pltpu.VMEM((n_blk, tokens, width), jnp.bfloat16)]
        + line_scratch(n_blk, tokens, width)
        + [pltpu.VMEM((tokens, width), jnp.bfloat16)]
        + semaphores(16),
        compiler_params=kernel_params(2),
    )(heads, wo, source, gain)


def back_rows(grad_normed, source, gain):
    scale = rms_scale(source)
    unit = source * scale
    scaled = grad_normed * gain
    back = scale * (scaled - unit * jnp.mean(scaled * unit, axis=-1, keepdims=True))
    return back, jnp.sum(grad_normed * unit, axis=0, keepdims=True)


def back_kernel(
    grad_parts,
    out_parts,
    middle,
    cotangent,
    gain,
    all_normed,
    grad_gate_pre,
    grad_up_pre,
    activated,
    all_cot,
    output,
    grad_middle,
    gain_term,
    all_low,
    grad_gate,
    grad_up,
    grad_down,
    rightward,
    leftward,
    out_right,
    out_left,
    out_total,
    low,
    gate_1,
    gate_2,
    gate_3,
    gate_4,
    gate_5,
    gate_6,
    up_1,
    up_2,
    up_3,
    up_4,
    up_5,
    up_6,
    down_1,
    down_2,
    down_3,
    down_4,
    down_5,
    down_6,
    send,
    recv,
    here,
):
    links = Links(send, recv, here)
    links.greet(links.peers() + [links.x_way, links.y_way, links.core_way])
    scatter = LineScatter(links, grad_parts, rightward, leftward)
    scatter.start()
    out_scatter = LineScatter(links, out_parts, out_right, out_left)
    gate = PlaneScatter(links, gate_1, gate_2, gate_3, gate_4, gate_5, gate_6)
    up = PlaneScatter(links, up_1, up_2, up_3, up_4, up_5, up_6)
    down = PlaneScatter(links, down_1, down_2, down_3, down_4, down_5, down_6)

    def compute(scatter, left, right, parts, together):
        for which, dp in ((0, links.other_dp), (1, links.dp)):
            weight_grad(left, right, parts, dp, together)
            scatter.between_cores(which)

    compute(gate, all_normed, grad_gate_pre, gate_1, 4)
    scatter.step(0)
    compute(up, all_normed, grad_up_pre, up_1, 4)
    gate.across_chips()
    scatter.step(1)
    compute(down, activated, all_cot, down_1, 2)
    up.across_chips()
    for step in range(2, links.n_blk - 1):
        scatter.step(step)
    down.across_chips()
    scatter.finish(grad_middle)
    gain_term[...] = jnp.zeros_like(gain_term)

    def body(rows):
        back, term = back_rows(grad_middle[rows, :], middle[rows, :], gain[...])
        grad = cotangent[rows, :].astype(jnp.float32) + back
        gain_term[...] += term
        grad_middle[rows, :] = grad
        low[rows, :] = grad.astype(jnp.bfloat16)

    each_block(middle.shape[0], body)
    keep = links.local(low, all_low.at[links.blk])
    line = LineGather(links, low, all_low)
    line.send(0)
    out_scatter.start()
    gate.second_way()
    line.arrived()
    for step in range(1, links.n_blk - 1):
        line.send(step)
        out_scatter.step(step - 1)
        if step == 1:
            up.second_way()
        line.arrived()
    down.second_way()
    out_scatter.step(links.n_blk - 2)

    def into(target):
        def write(block, rows, values):
            target[block, rows, :] = values.astype(target.dtype)

        return write

    gate.result(into(grad_gate))
    up.result(into(grad_up))
    out_scatter.finish(out_total)

    def add_output(rows):
        output[rows, :] = (middle[rows, :] + out_total[rows, :]).astype(jnp.bfloat16)

    each_block(middle.shape[0], add_output)
    down.result(into(grad_down))
    keep.wait()
    scatter.sent()
    out_scatter.sent()
    links.finish()


def exchange_back(
    grad_parts,
    out_parts,
    middle,
    cotangent,
    gain,
    all_normed,
    grad_gate_pre,
    grad_up_pre,
    activated,
    all_cot,
):
    n_dp, n_blk, n_uly = (lax.axis_size(a) for a in EVERY)
    _, tokens, width = grad_parts.shape
    ff = grad_gate_pre.shape[1]
    depth = width // (n_dp * n_blk * n_uly)
    down_depth = ff // (n_dp * n_uly)
    return pl.pallas_call(
        back_kernel,
        out_shape=[
            jax.ShapeDtypeStruct((tokens, width), jnp.bfloat16),
            jax.ShapeDtypeStruct((tokens, width), jnp.float32),
            jax.ShapeDtypeStruct((1, width), jnp.float32),
            jax.ShapeDtypeStruct((n_blk, tokens, width), jnp.bfloat16),
            jax.ShapeDtypeStruct((n_blk, depth, ff), jnp.bfloat16),
            jax.ShapeDtypeStruct((n_blk, depth, ff), jnp.bfloat16),
            jax.ShapeDtypeStruct((1, down_depth, width), jnp.float32),
        ],
        in_specs=[VMEM] * 10,
        out_specs=[VMEM, VMEM, VMEM, HBM, VMEM, VMEM, VMEM],
        scratch_shapes=line_scratch(n_blk, tokens, width) * 2
        + [pltpu.VMEM((tokens, width), jnp.float32), pltpu.VMEM((tokens, width), jnp.bfloat16)]
        + plane_scratch(n_dp, n_blk, n_uly, depth, ff) * 2
        + plane_scratch(n_dp, 1, n_uly, down_depth, width)
        + semaphores(56),
        compiler_params=kernel_params(3, 63),
    )(
        grad_parts,
        out_parts,
        middle,
        cotangent,
        gain,
        all_normed,
        grad_gate_pre,
        grad_up_pre,
        activated,
        all_cot,
    )


def last_kernel(
    w_qkv,
    hidden,
    grad_middle,
    gain,
    normed,
    grad_qkv,
    heads,
    all_low,
    mlp_term,
    head_terms,
    grad_hidden,
    grad_w_qkv,
    grad_wo,
    small_sum,
    grad_parts,
    rightward,
    leftward,
    qkv_1,
    qkv_2,
    qkv_3,
    qkv_4,
    qkv_5,
    qkv_6,
    wo_1,
    wo_2,
    wo_3,
    wo_4,
    wo_5,
    wo_6,
    summed,
    small,
    attn_term,
    small_in,
    small_total,
    send,
    recv,
    here,
):
    links = Links(send, recv, here)
    links.greet(links.peers() + [links.x_way, links.y_way, links.core_way])
    scatter = LineScatter(links, grad_parts, rightward, leftward)
    qkv = PlaneScatter(links, qkv_1, qkv_2, qkv_3, qkv_4, qkv_5, qkv_6)
    out = PlaneScatter(links, wo_1, wo_2, wo_3, wo_4, wo_5, wo_6)

    attn_term[...] = jnp.zeros_like(attn_term)
    tokens = grad_parts.shape[1]
    for blk in (links.n_blk - 1, 0) + tuple(range(1, links.n_blk - 1)):
        grad_hidden[...] = product_right(
            grad_qkv[blk * tokens : (blk + 1) * tokens, :], w_qkv[...]
        )

        def collect(rows, blk=blk):
            part = grad_hidden[rows, :]
            source = hidden[blk, rows, :].astype(jnp.float32)
            grad_parts[blk, rows, :] = part.astype(jnp.bfloat16)
            attn_term[...] += jnp.sum(part * (source * rms_scale(source)), axis=0, keepdims=True)

        each_block(tokens, collect)
    scatter.start()
    small[...] = jnp.zeros_like(small)
    span = gain.shape[1] // 128
    for index in range(span):
        columns = slice(index * 128, (index + 1) * 128)
        small[index : index + 1, :] = attn_term[:, columns]
        small[span + index : span + index + 1, :] = mlp_term[:, columns]
    small[2 * span : 2 * span + 8, :] = head_terms[...]
    small_in[links.blk] = small[...]
    small_copies = [links.to(small, small_in.at[links.blk], device) for device in links.peers()]

    for which, dp in ((0, links.other_dp), (1, links.dp)):
        weight_grad(normed, grad_qkv, qkv_1, dp, 4)
        qkv.between_cores(which)
    scatter.step(0)
    for which, dp in ((0, links.other_dp), (1, links.dp)):
        weight_grad(heads, all_low, wo_1, dp, 4)
        out.between_cores(which)
    qkv.across_chips()
    for copy in small_copies:
        copy.arrived()
    total = small_in[0]
    for blk in range(1, links.n_blk):
        total = total + small_in[blk]
    small_total[0] = total
    pending = links.to(small_total.at[0], small_in.at[links.n_blk], links.x_way)
    out.across_chips()
    scatter.step(1)
    pending.arrived()
    small_total[1] = small_total[0] + small_in[links.n_blk]
    pending = links.to(small_total.at[1], small_in.at[links.n_blk + 1], links.y_way)
    qkv.second_way()
    pending.arrived()
    small_total[2] = small_total[1] + small_in[links.n_blk + 1]
    pending = links.to(small_total.at[2], small_in.at[links.n_blk + 2], links.core_way)
    for step in range(2, links.n_blk - 1):
        scatter.step(step)
    out.second_way()
    pending.arrived()
    small_sum[...] = small_total[2] + small_in[links.n_blk + 2]

    def write(block, rows, values):
        summed[block, rows, :] = values.astype(jnp.bfloat16)

    qkv.result(write)
    swapped = []
    for step in range(1, links.n_blk):
        peer = links.peer(step)
        swapped.append(
            links.to(
                summed.at[peer], grad_w_qkv.at[links.blk], (links.dp, peer, links.uly)
            )
        )
    keep = links.local(summed.at[links.blk], grad_w_qkv.at[links.blk])
    scatter.finish(grad_hidden)

    def body(rows):
        back, _ = back_rows(
            grad_hidden[rows, :], hidden[links.blk, rows, :].astype(jnp.float32), gain[...]
        )
        grad_hidden[rows, :] = grad_middle[rows, :] + back

    each_block(tokens, body)

    def write_out(block, rows, values):
        grad_wo[block, rows, :] = values

    out.result(write_out)
    for copy in swapped:
        copy.arrived()
    keep.wait()
    scatter.sent()
    links.finish()


def exchange_last(
    w_qkv,
    hidden,
    grad_middle,
    gain,
    normed,
    grad_qkv,
    heads,
    all_low,
    mlp_term,
    head_terms,
):
    n_dp, n_blk, n_uly = (lax.axis_size(a) for a in EVERY)
    _, tokens, width = hidden.shape
    columns = grad_qkv.shape[1]
    depth = width // (n_dp * n_blk * n_uly)
    out_depth = heads.shape[1] // (n_dp * n_uly)
    small = (2 * width // 128 + 8, 128)
    return pl.pallas_call(
        last_kernel,
        out_shape=[
            jax.ShapeDtypeStruct((tokens, width), jnp.float32),
            jax.ShapeDtypeStruct((n_blk, depth, columns), jnp.bfloat16),
            jax.ShapeDtypeStruct((1, out_depth, width), jnp.float32),
            jax.ShapeDtypeStruct(small, jnp.float32),
        ],
        in_specs=[VMEM] * 10,
        out_specs=[VMEM, HBM, VMEM, VMEM],
        scratch_shapes=[pltpu.VMEM((n_blk, tokens, width), jnp.bfloat16)]
        + line_scratch(n_blk, tokens, width)
        + plane_scratch(n_dp, n_blk, n_uly, depth, columns)
        + plane_scratch(n_dp, 1, n_uly, out_depth, width)
        + [
            pltpu.VMEM((n_blk, depth, columns), jnp.bfloat16),
            pltpu.VMEM(small, jnp.float32),
            pltpu.VMEM((1, width), jnp.float32),
            pltpu.VMEM((n_blk + 3,) + small, jnp.float32),
            pltpu.VMEM((3,) + small, jnp.float32),
        ]
        + semaphores(48),
        compiler_params=kernel_params(4, 56),
    )(
        w_qkv,
        hidden,
        grad_middle,
        gain,
        normed,
        grad_qkv,
        heads,
        all_low,
        mlp_term,
        head_terms,
    )


def place_columns(blocks, n_dp):
    n_blk, rows, _ = blocks.shape
    split = blocks.reshape(n_blk, rows, n_dp, -1)
    return jnp.transpose(split, (1, 2, 0, 3)).reshape(rows, -1).astype(jnp.float32)


def product(left, right):
    return jnp.dot(left, right, preferred_element_type=jnp.float32)


def shards(
    hidden,
    span_order,
    attn_gain,
    w_query,
    key_weight,
    value_weight,
    w_out,
    q_gain,
    k_gain,
    mlp_gain,
    w_gate,
    w_up,
    w_down,
    cotangent,
):
    seqs, toks, width = hidden.shape
    n_dp, n_blk, n_uly = (lax.axis_size(a) for a in EVERY)
    blk_index = lax.axis_index(BLK)
    uly_index = lax.axis_index(ULY)
    group = QUERY_HEADS // KEY_VALUE_HEADS
    half_len = toks * n_uly // 2
    rows = n_blk * seqs * toks
    f32, bf16 = jnp.float32, jnp.bfloat16
    own_hidden = hidden.reshape(seqs * toks, width)
    own_cotangent = cotangent.reshape(seqs * toks, width)

    def positions(u):
        places = (
            jnp.arange(n_blk, dtype=jnp.int32)[:, None] * n_uly + u
        ) * toks + jnp.arange(toks, dtype=jnp.int32)[None, :]
        return positions_of(places.reshape(-1), span_order, half_len)

    own_pos = positions(uly_index)
    query_pos = jnp.tile(own_pos, group)[None, :]
    key_pos = jnp.concatenate([positions(u) for u in range(n_uly)])[:, None]
    angles = angles_of(own_pos, HEAD_SIZE)
    cosine, sine = jnp.cos(angles), jnp.sin(angles)
    cosine = jnp.concatenate([cosine, cosine], axis=1)
    sine = jnp.concatenate([-sine, sine], axis=1)
    gain_q, gain_k = q_gain.astype(f32)[None, :], k_gain.astype(f32)[None, :]

    gain_rows = attn_gain.shape[0]
    own_gains = jnp.pad(jnp.stack([attn_gain, mlp_gain]), ((0, 14), (0, 128 - gain_rows)))
    all_hidden, w_qkv, wo, all_wd, all_gains = gather_front(
        own_hidden, w_query, key_weight, value_weight, w_out, w_down, own_gains
    )
    gains = all_gains[..., :2, :gain_rows].astype(f32)
    g_attn = gains[..., 0, :].reshape(1, width)
    g_mlp = gains[..., 1, :].reshape(1, width)
    w_qkv = w_qkv.reshape(width, -1)
    wo = wo.reshape(-1, width)
    (
        all_wg,
        all_wu,
        cot,
        heads_flat,
        normed,
        qkv,
        queries,
        key_values,
        lse,
    ) = attend_forward(
        w_gate,
        w_up,
        own_cotangent,
        all_hidden.reshape(rows, width),
        w_qkv,
        g_attn,
        gain_q,
        gain_k,
        cosine,
        sine,
        query_pos,
        key_pos,
        seqs,
    )
    wg, wu = all_wg.reshape(width, -1), all_wu.reshape(width, -1)
    wd = all_wd.reshape(-1, width)
    cot = cot.reshape(rows, width)
    middle, normed2 = exchange_middle(
        heads_flat.reshape(n_blk, seqs * toks, -1), wo, own_hidden, g_mlp
    )
    normed2 = normed2.reshape(rows, width)
    gate_pre = product(normed2, wg)
    up_pre = product(normed2, wu)
    sigmoid_gate = jax.nn.sigmoid(gate_pre)
    activated = (gate_pre * sigmoid_gate * up_pre).astype(bf16)
    out_parts = product(activated, wd).astype(bf16)
    grad_act = product_right(cot, wd)
    grad_gate_pre = (
        grad_act * up_pre * sigmoid_gate * (1.0 + gate_pre * (1.0 - sigmoid_gate))
    ).astype(bf16)
    grad_up_pre = (grad_act * gate_pre * sigmoid_gate).astype(bf16)
    grad_parts = (product_right(grad_gate_pre, wg) + product_right(grad_up_pre, wu)).astype(bf16)
    blocks = (n_blk, seqs * toks, width)
    output, grad_middle, mlp_gain_term, middle_low, grad_gate, grad_up, grad_down = exchange_back(
        grad_parts.reshape(blocks),
        out_parts.reshape(blocks),
        middle,
        own_cotangent,
        g_mlp,
        normed2,
        grad_gate_pre,
        grad_up_pre,
        activated,
        cot,
    )
    middle_low = middle_low.reshape(rows, width)
    grad_qkv, head_terms, grad_gate, grad_up = attend_back(
        middle_low,
        wo,
        queries,
        key_values,
        lse,
        qkv,
        gain_q,
        gain_k,
        cosine,
        sine,
        query_pos,
        key_pos,
        grad_gate,
        grad_up,
    )
    grad_gate, grad_up = place_columns(grad_gate, n_dp), place_columns(grad_up, n_dp)
    grad_hidden, grad_w_qkv, grad_out, small = exchange_last(
        w_qkv,
        all_hidden,
        grad_middle,
        g_attn,
        normed,
        grad_qkv,
        heads_flat,
        middle_low,
        mlp_gain_term,
        head_terms,
    )
    q_end = QUERY_HEADS // n_blk * HEAD_SIZE
    k_end = q_end + KEY_VALUE_HEADS // n_blk * HEAD_SIZE
    grad_query = place_columns(grad_w_qkv[..., :q_end], n_dp)
    grad_key = place_columns(grad_w_qkv[..., q_end:k_end], n_dp)
    grad_value = place_columns(grad_w_qkv[..., k_end:], n_dp)
    small = small.reshape(-1)
    gain_at = ((lax.axis_index(DP) * n_blk + blk_index) * n_uly + uly_index) * gain_rows
    grad_attn_gain = lax.dynamic_slice(small, (gain_at,), (gain_rows,))
    grad_mlp_gain = lax.dynamic_slice(small, (width + gain_at,), (gain_rows,))
    grad_q_gain = small[2 * width : 2 * width + HEAD_SIZE]
    grad_k_gain = small[2 * width + HEAD_SIZE : 2 * width + 2 * HEAD_SIZE]
    return (
        output.reshape(hidden.shape),
        grad_hidden.reshape(hidden.shape),
        grad_attn_gain,
        grad_query,
        grad_key,
        grad_value,
        grad_out[0],
        grad_q_gain,
        grad_k_gain,
        grad_mlp_gain,
        grad_gate,
        grad_up,
        grad_down[0],
    )


def solution(mesh):
    n_dp, n_blk, n_uly = (mesh.shape[a] for a in EVERY)
    aligned = (n_dp, n_uly) == (2, 4) and KEY_VALUE_HEADS % (n_dp * n_blk) == 0
    in_specs = (
        TOKENS,
        P(),
        P(EVERY),
        P(EVERY, None),
        P(EVERY, None),
        P(EVERY, None),
        P(EVERY, None),
        P(),
        P(),
        P(EVERY),
        P(EVERY, None),
        P(EVERY, None),
        P(EVERY, None),
        TOKENS,
    )
    out_specs = (
        TOKENS,
        TOKENS,
        P(EVERY),
        P(EVERY, None),
        P(EVERY, None),
        P(EVERY, None),
        P(EVERY, None),
        P(),
        P(),
        P(EVERY),
        P(EVERY, None),
        P(EVERY, None),
        P(EVERY, None),
    )
    return jax.shard_map(
        shards if aligned else shards_general,
        mesh=mesh, in_specs=in_specs, out_specs=out_specs, check_vma=False)
```

```python
import math

import jax
import jax.numpy as jnp
from jax import lax
from jax.experimental import pallas as pl
from jax.experimental.pallas import tpu as pltpu
from jax.sharding import PartitionSpec as P

QUERY_HEADS = 16
KEY_VALUE_HEADS = 8
HEAD_SIZE = 128


DP, BLK, ULY = "dp", "blk", "uly"
EVERY = (DP, BLK, ULY)
PLANE = (DP, ULY)
TOKENS = P(DP, (BLK, ULY), None)
EQ_KGQD_NKD_TO_KGQN = "kgqd,nkd->kgqn"
EQ_KGQN_KGQD_TO_NKD = "kgqn,kgqd->nkd"
EQ_KGQN_NKD_TO_KGQD = "kgqn,nkd->kgqd"
EQ_KGQN_QKGD_TO_NKD = "kgqn,qkgd->nkd"
EQ_QKGD_NKD_TO_KGQN = "qkgd,nkd->kgqn"
EQ_STD_DE_TO_STE = "std,de->ste"
EQ_STD_DF_TO_STF = "std,df->stf"
EQ_STD_ED_TO_STE = "std,ed->ste"
EQ_STD_FD_TO_STF = "std,fd->stf"
EQ_STD_STE_TO_DE = "std,ste->de"
EQ_STD_STF_TO_DF = "std,stf->df"
EQ_STE_DE_TO_STD = "ste,de->std"
EQ_STE_ED_TO_STD = "ste,ed->std"
EQ_STE_STD_TO_ED = "ste,std->ed"
EQ_STF_DF_TO_STD = "stf,df->std"
EQ_STF_FD_TO_STD = "stf,fd->std"
EQ_STF_STD_TO_FD = "stf,std->fd"

EPSILON = 1e-06
ROPE_BASE = 1000000.0


def rms_scale(source):
    return lax.rsqrt(jnp.mean(source * source, axis=-1, keepdims=True) + EPSILON)


def norm_back(grad_normed, source, norm_scale, gain):
    unit_rows = source * norm_scale
    scaled = grad_normed * gain
    return norm_scale * (scaled - unit_rows * jnp.mean(scaled * unit_rows, axis=-1, keepdims=True))


def angles_of(positions, head_dim):
    freq_steps = jnp.arange(head_dim // 2, dtype=jnp.float32)
    inverse = jnp.exp(freq_steps * (-2.0 * math.log(ROPE_BASE) / head_dim))
    return positions.astype(jnp.float32)[:, None] * inverse[None, :]


def rotate(source, angles, direction):
    half_dim = source.shape[-1] // 2
    cosine = jnp.cos(angles)[:, None, :]
    sine_part = direction * jnp.sin(angles)[:, None, :]
    first_half = source[..., :half_dim]
    second_half = source[..., half_dim:]
    return jnp.concatenate(
        [
            first_half * cosine - second_half * sine_part,
            second_half * cosine + first_half * sine_part,
        ],
        axis=-1,
    )


def positions_of(places, span_order, half_len):
    blocks_of = places // half_len
    block_ids = jnp.arange(span_order.shape[0], dtype=jnp.int32)
    chosen = jnp.sum(
        jnp.where(blocks_of[:, None] == block_ids[None, :], span_order[None, :], 0), axis=1
    )
    return chosen * half_len + places % half_len


def add_rows(buffer, new_rows):
    return buffer + new_rows


def shards_general(
    hidden,
    span_order,
    attn_gain,
    w_query,
    key_weight,
    value_weight,
    w_out,
    q_gain,
    k_gain,
    mlp_gain,
    w_gate,
    w_up,
    w_down,
    cotangent,
):
    sequence_count = hidden.shape[0]
    token_count = hidden.shape[1]
    ulysses_group_size = lax.axis_size(ULY)
    local_q = QUERY_HEADS // ulysses_group_size
    local_key_value = KEY_VALUE_HEADS // ulysses_group_size
    query_group_width = QUERY_HEADS // KEY_VALUE_HEADS
    block_len = token_count * ulysses_group_size
    half_len = block_len // 2
    score_scale = 1.0 / math.sqrt(HEAD_SIZE)
    blk_index = lax.axis_index(BLK)
    uly_index = lax.axis_index(ULY)
    first_place = (blk_index * ulysses_group_size + uly_index) * token_count
    local_angles = angles_of(
        positions_of(first_place + jnp.arange(token_count, dtype=jnp.int32), span_order, half_len),
        HEAD_SIZE,
    )
    query_pos = positions_of(
        blk_index * block_len + jnp.arange(block_len, dtype=jnp.int32), span_order, half_len
    )
    g_attn, wq_all, wk_all, wv_all, wo_all = (
        lax.all_gather(attn_gain, EVERY, axis=0, tiled=True),
        lax.all_gather(w_query, EVERY, axis=0, tiled=True),
        lax.all_gather(key_weight, EVERY, axis=0, tiled=True),
        lax.all_gather(value_weight, EVERY, axis=0, tiled=True),
        lax.all_gather(w_out, EVERY, axis=0, tiled=True),
    )
    source = hidden.astype(jnp.float32)
    first_scale = rms_scale(source)
    normalized_input = (source * first_scale * g_attn.astype(jnp.float32)).astype(jnp.bfloat16)
    q_pre = jnp.einsum(
        EQ_STD_DE_TO_STE, normalized_input, wq_all, preferred_element_type=jnp.float32
    ).reshape(sequence_count, token_count, QUERY_HEADS, HEAD_SIZE)
    key_before_norm = jnp.einsum(
        EQ_STD_DE_TO_STE, normalized_input, wk_all, preferred_element_type=jnp.float32
    ).reshape(sequence_count, token_count, KEY_VALUE_HEADS, HEAD_SIZE)
    value_before_norm = jnp.einsum(
        EQ_STD_DE_TO_STE, normalized_input, wv_all, preferred_element_type=jnp.float32
    ).reshape(sequence_count, token_count, KEY_VALUE_HEADS, HEAD_SIZE)
    q_scale = rms_scale(q_pre)
    k_scale = rms_scale(key_before_norm)
    gain_q = q_gain.astype(jnp.float32)
    gain_k = k_gain.astype(jnp.float32)
    q_rot = rotate(q_pre * q_scale * gain_q, local_angles, 1.0).astype(jnp.bfloat16)
    k_rot = rotate(key_before_norm * k_scale * gain_k, local_angles, 1.0).astype(jnp.bfloat16)
    v_low = value_before_norm.astype(jnp.bfloat16)
    q_heads, k_heads, v_heads = (
        lax.all_to_all(q_rot, ULY, split_axis=2, concat_axis=1, tiled=True),
        lax.all_to_all(k_rot, ULY, split_axis=2, concat_axis=1, tiled=True),
        lax.all_to_all(v_low, ULY, split_axis=2, concat_axis=1, tiled=True),
    )
    q_group = q_heads.reshape(
        sequence_count, block_len, local_key_value, query_group_width, HEAD_SIZE
    )
    stat_shape = (sequence_count, local_key_value, query_group_width, block_len)
    start_state = (
        jnp.full(stat_shape, -1e30, jnp.float32),
        jnp.zeros(stat_shape, jnp.float32),
        jnp.zeros(stat_shape + (HEAD_SIZE,), jnp.float32),
    )
    key_piece = lax.all_gather(k_heads, BLK, axis=1, tiled=True)
    value_piece = lax.all_gather(v_heads, BLK, axis=1, tiled=True)
    key_pos = positions_of(jnp.arange(key_piece.shape[1], dtype=jnp.int32), span_order, half_len)
    allowed = query_pos[:, None] >= key_pos[None, :]

    def attend_one_sequence(members):
        query_rows, key_rows, value_rows, top_seq, total_seq, accum_seq = members
        scores = (
            jnp.einsum(EQ_QKGD_NKD_TO_KGQN, query_rows, key_rows, preferred_element_type=jnp.float32)
            * score_scale
        )
        scores = jnp.where(allowed, scores, -jnp.inf)
        new_top = jnp.maximum(top_seq, jnp.max(scores, axis=-1))
        fading = jnp.exp(top_seq - new_top)
        weights = jnp.exp(scores - new_top[..., None])
        total_seq = total_seq * fading + jnp.sum(weights, axis=-1)
        accum_seq = accum_seq * fading[..., None] + jnp.einsum(
            EQ_KGQN_NKD_TO_KGQD,
            weights.astype(jnp.bfloat16),
            value_rows,
            preferred_element_type=jnp.float32,
        )
        return (new_top, total_seq, accum_seq)

    row_top, row_total, accum = lax.map(
        attend_one_sequence,
        (q_group, key_piece, value_piece, start_state[0], start_state[1], start_state[2]),
    )
    log_total = row_top + jnp.log(row_total)
    attention_output = jnp.transpose(accum / row_total[..., None], (0, 3, 1, 2, 4)).reshape(
        sequence_count, block_len, local_q, HEAD_SIZE
    )
    heads_seq = lax.all_to_all(
        attention_output.astype(jnp.bfloat16), ULY, split_axis=1, concat_axis=2, tiled=True
    )
    heads_flat = heads_seq.reshape(sequence_count, token_count, QUERY_HEADS * HEAD_SIZE)
    middle = source + jnp.einsum(
        EQ_STE_ED_TO_STD, heads_flat, wo_all, preferred_element_type=jnp.float32
    )
    g_mlp, wg_all, wu_all, wd_all = (
        lax.all_gather(mlp_gain, EVERY, axis=0, tiled=True),
        lax.all_gather(w_gate, EVERY, axis=0, tiled=True),
        lax.all_gather(w_up, EVERY, axis=0, tiled=True),
        lax.all_gather(w_down, EVERY, axis=0, tiled=True),
    )
    second_scale = rms_scale(middle)
    gain_mlp = g_mlp.astype(jnp.float32)
    normed2 = (middle * second_scale * gain_mlp).astype(jnp.bfloat16)
    gate_pre = jnp.einsum(EQ_STD_DF_TO_STF, normed2, wg_all, preferred_element_type=jnp.float32)
    up_pre = jnp.einsum(EQ_STD_DF_TO_STF, normed2, wu_all, preferred_element_type=jnp.float32)
    sigmoid_gate = jax.nn.sigmoid(gate_pre)
    activated = (gate_pre * sigmoid_gate * up_pre).astype(jnp.bfloat16)
    result = middle + jnp.einsum(
        EQ_STF_FD_TO_STD, activated, wd_all, preferred_element_type=jnp.float32
    )
    output = result.astype(jnp.bfloat16)
    g_mlp, wg_all, wu_all, wd_all = (
        lax.all_gather(mlp_gain, EVERY, axis=0, tiled=True),
        lax.all_gather(w_gate, EVERY, axis=0, tiled=True),
        lax.all_gather(w_up, EVERY, axis=0, tiled=True),
        lax.all_gather(w_down, EVERY, axis=0, tiled=True),
    )
    gain_mlp = g_mlp.astype(jnp.float32)
    grad_act = jnp.einsum(EQ_STD_FD_TO_STF, cotangent, wd_all, preferred_element_type=jnp.float32)
    grad_gate_pre = (
        grad_act * up_pre * sigmoid_gate * (1.0 + gate_pre * (1.0 - sigmoid_gate))
    ).astype(jnp.bfloat16)
    grad_up_pre = (grad_act * gate_pre * sigmoid_gate).astype(jnp.bfloat16)
    grad_gate = jnp.einsum(
        EQ_STD_STF_TO_DF, normed2, grad_gate_pre, preferred_element_type=jnp.float32
    )
    grad_up = jnp.einsum(EQ_STD_STF_TO_DF, normed2, grad_up_pre, preferred_element_type=jnp.float32)
    grad_normed2 = jnp.einsum(
        EQ_STF_DF_TO_STD, grad_gate_pre, wg_all, preferred_element_type=jnp.float32
    ) + jnp.einsum(EQ_STF_DF_TO_STD, grad_up_pre, wu_all, preferred_element_type=jnp.float32)
    mlp_gain_term = jnp.sum(grad_normed2 * middle * second_scale, axis=(0, 1))
    grad_middle = cotangent.astype(jnp.float32) + norm_back(
        grad_normed2, middle, second_scale, gain_mlp
    )
    grad_mlp_gain, grad_gate, grad_up = (
        lax.psum_scatter(mlp_gain_term, EVERY, scatter_dimension=0, tiled=True),
        lax.psum_scatter(grad_gate, EVERY, scatter_dimension=0, tiled=True),
        lax.psum_scatter(grad_up, EVERY, scatter_dimension=0, tiled=True),
    )
    g_attn, wq_all, wk_all, wv_all, wo_all = (
        lax.all_gather(attn_gain, EVERY, axis=0, tiled=True),
        lax.all_gather(w_query, EVERY, axis=0, tiled=True),
        lax.all_gather(key_weight, EVERY, axis=0, tiled=True),
        lax.all_gather(value_weight, EVERY, axis=0, tiled=True),
        lax.all_gather(w_out, EVERY, axis=0, tiled=True),
    )
    middle_low = grad_middle.astype(jnp.bfloat16)
    grad_out = jnp.einsum(EQ_STE_STD_TO_ED, heads_flat, middle_low, preferred_element_type=jnp.float32)
    grad_heads = (
        jnp.einsum(EQ_STD_ED_TO_STE, middle_low, wo_all, preferred_element_type=jnp.float32)
        .astype(jnp.bfloat16)
        .reshape(sequence_count, token_count, QUERY_HEADS, HEAD_SIZE)
    )
    grad_heads_local = lax.all_to_all(grad_heads, ULY, split_axis=2, concat_axis=1, tiled=True)
    grad_group = jnp.transpose(
        grad_heads_local.reshape(
            sequence_count, block_len, local_key_value, query_group_width, HEAD_SIZE
        ),
        (0, 2, 3, 1, 4),
    )
    delta = jnp.sum(grad_heads_local.astype(jnp.float32) * attention_output, axis=-1)
    delta = jnp.transpose(
        delta.reshape(sequence_count, block_len, local_key_value, query_group_width), (0, 2, 3, 1)
    )
    seq_length = block_len * lax.axis_size(BLK)
    zero_keys = jnp.zeros((sequence_count, seq_length, local_key_value, HEAD_SIZE), jnp.float32)
    back_state = (jnp.zeros(stat_shape + (HEAD_SIZE,), jnp.float32), zero_keys, zero_keys)
    key_piece = lax.all_gather(k_heads, BLK, axis=1, tiled=True)
    value_piece = lax.all_gather(v_heads, BLK, axis=1, tiled=True)
    key_pos = positions_of(jnp.arange(key_piece.shape[1], dtype=jnp.int32), span_order, half_len)
    back_allowed = query_pos[:, None] >= key_pos[None, :]

    def back_one_sequence(members):
        query_rows, grad_rows, lse_seq, delta_seq, key_rows, value_rows, dq_seq, dk_seq, dv_seq = (
            members
        )
        scores = (
            jnp.einsum(EQ_QKGD_NKD_TO_KGQN, query_rows, key_rows, preferred_element_type=jnp.float32)
            * score_scale
        )
        scores = jnp.where(back_allowed, scores, -jnp.inf)
        probs = jnp.exp(scores - lse_seq[..., None])
        grad_values = jnp.einsum(
            EQ_KGQN_KGQD_TO_NKD,
            probs.astype(jnp.bfloat16),
            grad_rows,
            preferred_element_type=jnp.float32,
        )
        grad_probs = jnp.einsum(
            EQ_KGQD_NKD_TO_KGQN, grad_rows, value_rows, preferred_element_type=jnp.float32
        )
        grad_scores = (probs * (grad_probs - delta_seq[..., None])).astype(jnp.bfloat16)
        dq_seq = dq_seq + score_scale * jnp.einsum(
            EQ_KGQN_NKD_TO_KGQD, grad_scores, key_rows, preferred_element_type=jnp.float32
        )
        grad_keys = score_scale * jnp.einsum(
            EQ_KGQN_QKGD_TO_NKD, grad_scores, query_rows, preferred_element_type=jnp.float32
        )
        return (dq_seq, add_rows(dk_seq, grad_keys), add_rows(dv_seq, grad_values))

    grad_q_group, grad_k_whole, grad_v_whole = lax.map(
        back_one_sequence,
        (
            q_group,
            grad_group,
            log_total,
            delta,
            key_piece,
            value_piece,
            back_state[0],
            back_state[1],
            back_state[2],
        ),
    )
    grad_k_block, grad_v_block = (
        lax.psum_scatter(
            grad_k_whole.astype(jnp.bfloat16), BLK, scatter_dimension=1, tiled=True
        ).astype(jnp.float32),
        lax.psum_scatter(
            grad_v_whole.astype(jnp.bfloat16), BLK, scatter_dimension=1, tiled=True
        ).astype(jnp.float32),
    )
    grad_q_block = jnp.transpose(grad_q_group, (0, 3, 1, 2, 4)).reshape(
        sequence_count, block_len, local_q, HEAD_SIZE
    )
    grad_q_seq, grad_k_seq, value_sequence_gradient = (
        lax.all_to_all(
            grad_q_block.astype(jnp.bfloat16), ULY, split_axis=1, concat_axis=2, tiled=True
        ).astype(grad_q_block.dtype),
        lax.all_to_all(
            grad_k_block.astype(jnp.bfloat16), ULY, split_axis=1, concat_axis=2, tiled=True
        ).astype(grad_k_block.dtype),
        lax.all_to_all(
            grad_v_block.astype(jnp.bfloat16), ULY, split_axis=1, concat_axis=2, tiled=True
        ).astype(grad_v_block.dtype),
    )
    grad_q_normed = rotate(grad_q_seq, local_angles, -1.0)
    grad_k_normed = rotate(grad_k_seq, local_angles, -1.0)
    q_gain_term = jnp.sum(grad_q_normed * q_pre * q_scale, axis=(0, 1, 2))
    k_gain_term = jnp.sum(grad_k_normed * key_before_norm * k_scale, axis=(0, 1, 2))
    grad_q_pre = (
        norm_back(grad_q_normed, q_pre, q_scale, gain_q)
        .astype(jnp.bfloat16)
        .reshape(sequence_count, token_count, QUERY_HEADS * HEAD_SIZE)
    )
    grad_k_pre = (
        norm_back(grad_k_normed, key_before_norm, k_scale, gain_k)
        .astype(jnp.bfloat16)
        .reshape(sequence_count, token_count, KEY_VALUE_HEADS * HEAD_SIZE)
    )
    value_pre_gradient = value_sequence_gradient.astype(jnp.bfloat16).reshape(
        sequence_count, token_count, KEY_VALUE_HEADS * HEAD_SIZE
    )
    grad_query = jnp.einsum(
        EQ_STD_STE_TO_DE, normalized_input, grad_q_pre, preferred_element_type=jnp.float32
    )
    grad_key = jnp.einsum(
        EQ_STD_STE_TO_DE, normalized_input, grad_k_pre, preferred_element_type=jnp.float32
    )
    grad_value = jnp.einsum(
        EQ_STD_STE_TO_DE, normalized_input, value_pre_gradient, preferred_element_type=jnp.float32
    )
    grad_normed = jnp.einsum(EQ_STE_DE_TO_STD, grad_q_pre, wq_all, preferred_element_type=jnp.float32)
    grad_normed = grad_normed + jnp.einsum(
        EQ_STE_DE_TO_STD, grad_k_pre, wk_all, preferred_element_type=jnp.float32
    )
    grad_normed = grad_normed + jnp.einsum(
        EQ_STE_DE_TO_STD, value_pre_gradient, wv_all, preferred_element_type=jnp.float32
    )
    attn_gain_term = jnp.sum(grad_normed * source * first_scale, axis=(0, 1))
    grad_hidden = grad_middle + norm_back(
        grad_normed, source, first_scale, g_attn.astype(jnp.float32)
    )
    grad_down = jnp.einsum(EQ_STF_STD_TO_FD, activated, cotangent, preferred_element_type=jnp.float32)
    grad_attn_gain, grad_query, grad_key, grad_value, grad_out, grad_down = (
        lax.psum_scatter(attn_gain_term, EVERY, scatter_dimension=0, tiled=True),
        lax.psum_scatter(grad_query, EVERY, scatter_dimension=0, tiled=True),
        lax.psum_scatter(grad_key, EVERY, scatter_dimension=0, tiled=True),
        lax.psum_scatter(grad_value, EVERY, scatter_dimension=0, tiled=True),
        lax.psum_scatter(grad_out, EVERY, scatter_dimension=0, tiled=True),
        lax.psum_scatter(grad_down, EVERY, scatter_dimension=0, tiled=True),
    )
    grad_q_gain, grad_k_gain = lax.psum((q_gain_term, k_gain_term), EVERY)
    return (
        output,
        grad_hidden,
        grad_attn_gain,
        grad_query,
        grad_key,
        grad_value,
        grad_out,
        grad_q_gain,
        grad_k_gain,
        grad_mlp_gain,
        grad_gate,
        grad_up,
        grad_down,
    )


MESH = pl.DeviceIdType.MESH
HBM = pl.BlockSpec(memory_space=pltpu.HBM)
VMEM = pl.BlockSpec(memory_space=pltpu.VMEM)
MIB = 1 << 20


def kernel_params(collective_id, vmem_mib=48):
    return pltpu.CompilerParams(
        collective_id=collective_id, has_side_effects=True, vmem_limit_bytes=vmem_mib * MIB
    )


def semaphores(count, local=16):
    return [
        pltpu.SemaphoreType.DMA((count,)),
        pltpu.SemaphoreType.DMA((count,)),
        pltpu.SemaphoreType.DMA((local,)),
    ]


class Copy:
    def __init__(self, descriptor, sends, receives):
        self.descriptor, self.sends, self.receives = descriptor, sends, receives

    def under(self, condition, action):
        if condition is None:
            action()
        else:
            pl.when(condition)(action)

    def start(self):
        self.under(self.sends, lambda: self.descriptor().start())
        return self

    def sent(self):
        self.under(self.sends, lambda: self.descriptor().wait_send())

    def arrived(self):
        self.under(self.receives, lambda: self.descriptor().wait_recv())


class Links:
    def __init__(self, send, recv, here):
        self.send, self.recv, self.here = send, recv, here
        self.used, self.used_here = 0, 0
        self.copies, self.local_copies = [], []
        self.n_dp, self.n_blk, self.n_uly = (lax.axis_size(a) for a in EVERY)
        self.dp, self.blk, self.uly = (lax.axis_index(a) for a in EVERY)
        self.other_dp = 1 - self.dp
        self.across = lax.rem(self.uly + 2, 4)
        self.twin = self.uly + 1 - 2 * lax.rem(self.uly, 2)
        self.x_way = (self.other_dp, self.blk, self.uly)
        self.y_way = (self.dp, self.blk, self.across)
        self.core_way = (self.dp, self.blk, self.twin)

    def peer(self, step):
        return lax.rem(self.blk + step, self.n_blk)

    def peers(self):
        return [(self.dp, self.peer(k), self.uly) for k in range(1, self.n_blk)]

    def greet(self, devices):
        barrier = pltpu.get_barrier_semaphore()
        for device in devices:
            pl.semaphore_signal(barrier, inc=1, device_id=device, device_id_type=MESH)
        pl.semaphore_wait(barrier, len(devices))

    def remote(self, source, target, device, sends=None, receives=None):
        slot = self.used
        self.used += 1

        def descriptor():
            return pltpu.make_async_remote_copy(
                src_ref=source(),
                dst_ref=target(),
                send_sem=self.send.at[slot],
                recv_sem=self.recv.at[slot],
                device_id=device,
                device_id_type=MESH,
            )

        copy = Copy(descriptor, sends, receives)
        self.copies.append(copy)
        return copy.start()

    def to(self, source, target, device):
        return self.remote(lambda: source, lambda: target, device)

    def local(self, source, target):
        copy = pltpu.make_async_copy(source, target, self.here.at[self.used_here])
        self.used_here += 1
        copy.start()
        self.local_copies.append(copy)
        return copy

    def finish(self):
        for copy in self.copies:
            copy.sent()


class LineGather:
    def __init__(self, links, own, whole):
        self.links, self.own, self.whole = links, own, whole
        self.waiting = []

    def send(self, step):
        links, whole = self.links, self.whole
        blk, last = links.blk, links.n_blk - 1

        def block(index):
            if step == 0:
                return lambda: self.own
            return lambda: whole.at[index]

        self.waiting = [
            links.remote(
                block(blk - step),
                lambda: whole.at[blk - step],
                (links.dp, blk + 1, links.uly),
                jnp.logical_and(blk >= step, blk < last),
                blk >= step + 1,
            ),
            links.remote(
                block(blk + step),
                lambda: whole.at[blk + step],
                (links.dp, blk - 1, links.uly),
                jnp.logical_and(blk + step <= last, blk > 0),
                blk + step + 1 <= last,
            ),
        ]

    def arrived(self):
        for copy in self.waiting:
            copy.arrived()


class PlaneGather:
    def __init__(self, links, at):
        self.links, self.at = links, at

    def start(self, own=None):
        links, at = self.links, self.at
        mine = at(links.dp, links.uly)
        own = mine if own is None else own
        self.from_x = links.to(own, mine, links.x_way)
        self.from_y = links.to(own, mine, links.y_way)
        self.from_core = [links.to(own, mine, links.core_way)]

    def hand_on(self):
        links, at = self.links, self.at
        self.from_x.arrived()
        half = at(links.other_dp, links.uly, 0)
        self.second_y = links.to(half, half, links.y_way)
        self.from_y.arrived()
        half = at(links.dp, links.across, 1)
        self.second_x = links.to(half, half, links.x_way)
        for chunk in (at(links.other_dp, links.uly), at(links.dp, links.across)):
            self.from_core.append(links.to(chunk, chunk, links.core_way))

    def last(self):
        links = self.links
        self.second_y.arrived()
        self.second_x.arrived()
        chunk = self.at(links.other_dp, links.across)
        self.from_core.append(links.to(chunk, chunk, links.core_way))

    def arrived(self):
        for copy in self.from_core:
            copy.arrived()


def rows_of(whole, blocked):
    def at(dp, uly, half=None):
        part = whole.at[dp, :, uly] if blocked else whole.at[dp, uly]
        if half is None:
            return part
        depth = whole.shape[-2] // 2
        rows = pl.ds(half * depth, depth)
        return part.at[:, rows] if blocked else part.at[rows]

    return at


class ColumnSwap:
    def __init__(self, links, pieces):
        self.links, self.pieces = links, pieces
        self.incoming, self.kept = [], []

    def parts(self, blk):
        links = self.links
        for weight, whole, offset in self.pieces:
            width = weight.shape[-1] // links.n_dp // links.n_blk
            for group in range(links.n_dp):
                start = (group * links.n_blk + blk) * width
                yield (
                    weight.at[:, pl.ds(pl.multiple_of(start, 128), width)],
                    whole.at[links.blk, :, pl.ds(offset + group * width, width)],
                )

    def start(self):
        links = self.links
        for step in range(1, links.n_blk):
            device = (links.dp, links.peer(step), links.uly)
            for source, target in self.parts(links.peer(step)):
                self.incoming.append(links.to(source, target, device))
        for source, target in self.parts(links.blk):
            self.kept.append(links.local(source, target))

    def arrived(self):
        for copy in self.kept:
            copy.wait()
        for copy in self.incoming:
            copy.arrived()


def front_kernel(
    hidden,
    wq,
    wk,
    wv,
    wo,
    wd,
    gains,
    all_hidden,
    w_qkv,
    all_wo,
    all_wd,
    all_gains,
    send,
    recv,
    here,
):
    links = Links(send, recv, here)
    links.greet(links.peers() + [links.x_way, links.y_way, links.core_way])
    q_width, k_width = wq.shape[1] // links.n_blk, wk.shape[1] // links.n_blk
    chunk = w_qkv.at[links.dp, :, links.uly]
    swap = ColumnSwap(
        links, [(wq, chunk, 0), (wk, chunk, q_width), (wv, chunk, q_width + k_width)]
    )
    plane_wo = PlaneGather(links, rows_of(all_wo, False))
    plane_wd = PlaneGather(links, rows_of(all_wd, False))
    plane_qkv = PlaneGather(links, rows_of(w_qkv, True))
    plane_gain = PlaneGather(links, rows_of(all_gains, True))
    swap.start()
    my_gains = all_gains.at[links.dp, links.blk, links.uly]
    gain_swap = [links.to(gains, my_gains, device) for device in links.peers()]
    plane_wo.start(wo)
    plane_wd.start(wd)
    keep = [
        links.local(gains, my_gains),
        links.local(hidden, all_hidden.at[links.blk]),
        links.local(wo, all_wo.at[links.dp, links.uly]),
        links.local(wd, all_wd.at[links.dp, links.uly]),
    ]
    swap.arrived()
    line = LineGather(links, hidden, all_hidden)
    line.send(0)
    plane_qkv.start()
    keep[0].wait()
    for copy in gain_swap:
        copy.arrived()
    plane_gain.start()
    plane_wo.hand_on()
    plane_wd.hand_on()
    line.arrived()
    line.send(1)
    plane_qkv.hand_on()
    plane_gain.hand_on()
    plane_wo.last()
    for step in range(2, links.n_blk - 1):
        line.arrived()
        line.send(step)
    plane_wd.last()
    plane_qkv.last()
    plane_gain.last()
    line.arrived()
    for plane in (plane_wo, plane_qkv, plane_gain, plane_wd):
        plane.arrived()
    for copy in keep[1:]:
        copy.wait()
    links.finish()


def gather_front(hidden, wq, wk, wv, wo, wd, gains):
    n_dp, n_blk, n_uly = (lax.axis_size(a) for a in EVERY)
    qkv_width = (wq.shape[1] + wk.shape[1] + wv.shape[1]) // n_blk
    shapes = [
        (n_blk,) + hidden.shape,
        (n_dp, n_blk, n_uly, wq.shape[0], qkv_width),
        (n_dp, n_uly) + wo.shape,
        (n_dp, n_uly) + wd.shape,
        (n_dp, n_blk, n_uly) + gains.shape,
    ]
    return pl.pallas_call(
        front_kernel,
        out_shape=[jax.ShapeDtypeStruct(s, jnp.bfloat16) for s in shapes],
        in_specs=[HBM] * 7,
        out_specs=[HBM] * 5,
        scratch_shapes=semaphores(72),
        compiler_params=kernel_params(0, 62),
    )(hidden, wq, wk, wv, wo, wd, gains)


ROWS = 32


def each_block(count, body):
    def step(index, carry):
        body(pl.ds(pl.multiple_of(index * ROWS, ROWS), ROWS))
        return carry

    lax.fori_loop(0, count // ROWS, step, 0)


class LineScatter:
    def __init__(self, links, parts, rightward, leftward):
        self.links, self.parts = links, parts
        self.slots = {1: rightward, -1: leftward}
        self.tokens = parts.shape[1]
        self.number = links.used
        links.used += 2 * (links.n_blk - 1)

    def place(self, step, way):
        blk, last = self.links.blk, self.links.n_blk - 1
        target = last - step if way == 1 else step
        slot = self.slots[way].at[target - 1 if way == 1 else target]
        first = blk == (0 if way == 1 else last)
        beyond = target > blk if way == 1 else target < blk
        return target, slot, first, beyond

    def copy(self, step, way, source=None):
        links, (_, slot, _, _) = self.links, self.place(step, way)
        number = self.number + 2 * step + (way == 1)
        return pltpu.make_async_remote_copy(
            src_ref=slot if source is None else source,
            dst_ref=slot,
            send_sem=links.send.at[number],
            recv_sem=links.recv.at[number],
            device_id=(links.dp, links.blk + way, links.uly),
            device_id_type=MESH,
        )

    def start(self):
        for step in range(self.links.n_blk - 1):
            for way in (1, -1):
                target, _, first, beyond = self.place(step, way)

                @pl.when(jnp.logical_and(first, beyond))
                def _(step=step, way=way, target=target):
                    self.copy(step, way, self.parts.at[target]).start()

    def move(self, step, way):
        parts = self.parts
        target, slot, first, beyond = self.place(step, way)

        @pl.when(jnp.logical_and(jnp.logical_not(first), beyond))
        def _():
            self.copy(step, way).wait_recv()

            def body(rows):
                slot[rows, :] = slot[rows, :] + parts[target, rows, :]

            each_block(self.tokens, body)
            self.copy(step, way).start()

    def step(self, step):
        early = 2 * self.links.blk < self.links.n_blk

        @pl.when(early)
        def _():
            self.move(step, 1)
            self.move(step, -1)

        @pl.when(jnp.logical_not(early))
        def _():
            self.move(step, -1)
            self.move(step, 1)

    def finish(self, total):
        links, parts = self.links, self.parts
        blk, last = links.blk, links.n_blk - 1
        for step in range(last):
            for way in (1, -1):
                target, _, first, _ = self.place(step, way)
                here = jnp.logical_and(jnp.logical_not(first), target == blk)
                pl.when(here)(lambda step=step, way=way: self.copy(step, way).wait_recv())

        def start(rows):
            total[rows, :] = parts[blk, rows, :].astype(jnp.float32)

        each_block(self.tokens, start)
        for way, condition, index in ((1, blk > 0, blk - 1), (-1, blk < last, blk)):

            def add(way=way, index=index):
                def body(rows):
                    term = self.slots[way][index, rows, :]
                    total[rows, :] = total[rows, :] + term.astype(jnp.float32)

                each_block(self.tokens, body)

            pl.when(condition)(add)

    def sent(self):
        for step in range(self.links.n_blk - 1):
            for way in (1, -1):
                _, _, _, beyond = self.place(step, way)
                pl.when(beyond)(lambda step=step, way=way: self.copy(step, way).wait_send())


def line_scratch(n_blk, tokens, width):
    return [pltpu.VMEM((n_blk - 1, tokens, width), jnp.bfloat16)] * 2


class PlaneScatter:
    def __init__(self, links, parts, from_core, from_x, from_y, last_x, last_y):
        self.links, self.parts = links, parts
        self.from_core, self.from_x, self.from_y = from_core, from_x, from_y
        self.last_x, self.last_y = last_x, last_y
        self.core = lax.rem(links.uly, 2)
        self.row = lax.div(links.uly, 2)
        self.depth = parts.shape[3]
        self.core_copies = {}

    def chunk(self, dp, row, core, half=None):
        uly = row * 2 + core
        if half is None:
            return self.parts.at[dp, :, uly]
        depth = self.depth // 2
        return self.parts.at[dp, :, uly, pl.ds(half * depth, depth)]

    def add(self, target, source):
        blocks, depth, _ = target.shape
        rows = 32 if depth % 32 == 0 else 16

        def body(index, carry):
            block = lax.div(index, depth // rows)
            at = pl.ds(pl.multiple_of(lax.rem(index, depth // rows) * rows, rows), rows)
            target[block, at, :] = target[block, at, :] + source[block, at, :]
            return carry

        lax.fori_loop(0, blocks * (depth // rows), body, 0)

    def between_cores(self, which):
        links = self.links
        dp = links.dp if which == 1 else links.other_dp
        self.core_copies[which] = [
            links.to(
                self.chunk(dp, row, 1 - self.core), self.from_core.at[which, row], links.core_way
            )
            for row in range(2)
        ]

    def across_chips(self):
        links = self.links
        self.x_copies, self.y_copies = [], []
        for which, dp in ((0, links.other_dp), (1, links.dp)):
            for row in range(2):
                self.core_copies[which][row].arrived()
                self.add(self.chunk(dp, row, self.core), self.from_core.at[which, row])
            if which == 0:
                for row in range(2):
                    self.x_copies.append(
                        links.to(
                            self.chunk(dp, row, self.core, 0), self.from_x.at[row], links.x_way
                        )
                    )
        for group in range(links.n_dp):
            self.y_copies.append(
                links.to(
                    self.chunk(group, 1 - self.row, self.core, 1),
                    self.from_y.at[group],
                    links.y_way,
                )
            )

    def second_way(self):
        links = self.links
        for row in range(2):
            self.x_copies[row].arrived()
            self.add(self.chunk(links.dp, row, self.core, 0), self.from_x.at[row])
        self.y_last = links.to(
            self.chunk(links.dp, 1 - self.row, self.core, 0), self.last_y, links.y_way
        )
        for group in range(links.n_dp):
            self.y_copies[group].arrived()
            self.add(self.chunk(group, self.row, self.core, 1), self.from_y.at[group])
        self.x_last = links.to(
            self.chunk(links.other_dp, self.row, self.core, 1), self.last_x, links.x_way
        )

    def result(self, write):
        links = self.links
        for half, copy, source in ((0, self.y_last, self.last_y), (1, self.x_last, self.last_x)):
            copy.arrived()
            own = self.chunk(links.dp, self.row, self.core, half)
            blocks, depth, _ = source.shape
            rows = 32 if depth % 32 == 0 else 16

            def body(index, carry, own=own, source=source, half=half, depth=depth, rows=rows):
                block = lax.div(index, depth // rows)
                start = pl.multiple_of(lax.rem(index, depth // rows) * rows, rows)
                at = pl.ds(start, rows)
                value = own[block, at, :].astype(jnp.float32)
                value = value + source[block, at, :].astype(jnp.float32)
                write(block, pl.ds(pl.multiple_of(start + half * depth, rows), rows), value)
                return carry

            lax.fori_loop(0, blocks * (depth // rows), body, 0)


def plane_scratch(n_dp, blocks, n_uly, depth, width):
    shapes = [
        (n_dp, blocks, n_uly, depth, width),
        (n_dp, 2, blocks, depth, width),
        (2, blocks, depth // 2, width),
        (n_dp, blocks, depth // 2, width),
        (blocks, depth // 2, width),
        (blocks, depth // 2, width),
    ]
    return [pltpu.VMEM(shape, jnp.bfloat16) for shape in shapes]


def weight_grad(left, right, parts, dp, together):
    _, blocks, n_uly, depth, width = parts.shape
    steps = n_uly // together
    columns = 512

    def body(index, carry):
        block, step = lax.div(index, steps), lax.rem(index, steps)
        start = ((dp * blocks + block) * n_uly + step * together) * depth
        rows = left[:, pl.ds(pl.multiple_of(start, 128), together * depth)].T
        for column in range(0, width, columns):
            part = jnp.dot(
                rows, right[:, column : column + columns], preferred_element_type=jnp.float32
            )
            parts[dp, block, pl.ds(step * together, together), :, column : column + columns] = (
                part.astype(jnp.bfloat16).reshape(together, depth, columns)
            )
        return carry

    lax.fori_loop(0, blocks * steps, body, 0)


def turned(rows, cosine, sine):
    return rows * cosine + pltpu.roll(rows, HEAD_SIZE // 2, axis=1) * sine


def transposed_product(left, right):
    return lax.dot_general(
        left, right, (((0,), (0,)), ((), ())), preferred_element_type=jnp.float32
    )


def product_right(left, right):
    return lax.dot_general(
        left, right, (((1,), (1,)), ((), ())), preferred_element_type=jnp.float32
    )


SCORE_SCALE = 1.0 / math.sqrt(HEAD_SIZE)


def mask_scores(bias, query_pos, key_pos):
    size = bias.shape[0] // 4

    def body(index, carry):
        rows = pl.ds(pl.multiple_of(index * size, size), size)
        bias[rows, :] = jnp.where(query_pos[...] >= key_pos[rows, :], 0.0, -1e30)
        return carry

    lax.fori_loop(0, 4, body, 0)


class RowBlocks:
    def __init__(self, n_blk, seqs, toks):
        self.n_blk, self.seqs, self.toks = n_blk, seqs, toks

    def each(self, body):
        def step(index, carry):
            blk, seq = lax.div(index, self.seqs), lax.rem(index, self.seqs)
            body(
                seq,
                pl.ds(pl.multiple_of(index * self.toks, self.toks), self.toks),
                pl.multiple_of(blk * self.toks, self.toks),
            )
            return carry

        lax.fori_loop(0, self.n_blk * self.seqs, step, 0)


def attention_kernel(
    wg,
    wu,
    hidden,
    w_qkv,
    gain,
    q_gain,
    k_gain,
    cosine,
    sine,
    query_pos,
    key_pos,
    rows_wg,
    rows_wu,
    heads,
    normed,
    qkv,
    queries,
    key_values,
    lse,
    bias,
    send,
    recv,
    here,
):
    links = Links(send, recv, here)
    links.greet(links.peers() + [links.y_way, links.core_way])
    swap = ColumnSwap(links, [(wg, rows_wg, 0), (wu, rows_wu, 0)])
    swap.start()

    def norm(rows):
        source = hidden[rows, :].astype(jnp.float32)
        normed[rows, :] = (source * rms_scale(source) * gain[...]).astype(jnp.bfloat16)

    each_block(hidden.shape[0], norm)
    for column in range(0, qkv.shape[1], 256):
        qkv[:, column : column + 256] = jnp.dot(
            normed[...], w_qkv[:, column : column + 256], preferred_element_type=jnp.float32
        )
    seqs, kv_heads, q_rows, _ = queries.shape
    q_len = key_values.shape[4]
    group = q_rows // q_len
    blocks = RowBlocks(links.n_blk, seqs, q_len // links.n_blk)
    q_end = kv_heads * group * HEAD_SIZE
    k_end = q_end + kv_heads * HEAD_SIZE

    def place_keys(seq, rows, start):
        at = pl.ds(start, blocks.toks)
        for head in range(kv_heads):
            k_pre = qkv[rows, q_end + head * HEAD_SIZE : q_end + (head + 1) * HEAD_SIZE]
            k_row = turned(k_pre * rms_scale(k_pre) * k_gain[...], cosine[at, :], sine[at, :])
            v_row = qkv[rows, k_end + head * HEAD_SIZE : k_end + (head + 1) * HEAD_SIZE]
            key_values[links.uly, 0, seq, head, at, :] = k_row.astype(jnp.bfloat16)
            key_values[links.uly, 1, seq, head, at, :] = v_row.astype(jnp.bfloat16)

    blocks.each(place_keys)
    mine = key_values.at[links.uly]
    kv_core = links.to(mine, mine, links.core_way)
    kv_across = links.to(mine, mine, links.y_way)

    def place_queries(seq, rows, start):
        at = pl.ds(start, blocks.toks)
        for head in range(kv_heads * group):
            q_pre = qkv[rows, head * HEAD_SIZE : (head + 1) * HEAD_SIZE]
            q_row = turned(q_pre * rms_scale(q_pre) * q_gain[...], cosine[at, :], sine[at, :])
            to = pl.ds((head % group) * q_len + start, blocks.toks)
            queries[seq, head // group, to, :] = q_row.astype(jnp.bfloat16)

    blocks.each(place_queries)
    mask_scores(bias, query_pos, key_pos)
    kv_across.arrived()
    theirs = key_values.at[links.across]
    kv_last = links.to(theirs, theirs, links.core_way)
    kv_core.arrived()
    kv_last.arrived()

    def attend(seq, head):
        def over_keys(piece, carry):
            total, mixed = carry
            rows = pl.ds(pl.multiple_of(piece * q_len, q_len), q_len)
            scores = product_right(key_values[piece, 0, seq, head], queries[seq, head])
            weights = jnp.exp(scores * SCORE_SCALE + bias[rows, :])
            total = total + jnp.sum(weights, axis=0, keepdims=True)
            mixed = mixed + transposed_product(
                key_values[piece, 1, seq, head], weights.astype(jnp.bfloat16)
            )
            return total, mixed

        total, mixed = lax.fori_loop(
            0,
            links.n_uly,
            over_keys,
            (
                jnp.zeros((1, q_rows), jnp.float32),
                jnp.zeros((HEAD_SIZE, q_rows), jnp.float32),
            ),
        )
        lse[seq * kv_heads + head] = jnp.log(total)
        attended = (mixed / total).T.astype(jnp.bfloat16)
        for member in range(group):
            column = (head * group + member) * HEAD_SIZE
            for blk in range(links.n_blk):
                row = (blk * seqs + seq) * blocks.toks
                start = member * q_len + blk * blocks.toks
                heads[row : row + blocks.toks, column : column + HEAD_SIZE] = attended[
                    start : start + blocks.toks, :
                ]

    for seq in range(seqs):
        for head in range(kv_heads):
            attend(seq, head)
    swap.arrived()
    links.finish()


def attend_forward(
    wg, wu, hidden, w_qkv, gain, q_gain, k_gain, cosine, sine, query_pos, key_pos, seqs
):
    _, n_blk, n_uly = (lax.axis_size(a) for a in EVERY)
    rows = hidden.shape[0]
    kv_heads = KEY_VALUE_HEADS // n_blk
    q_len, q_rows = rows // seqs, query_pos.shape[1]
    low = [
        (n_blk, wg.shape[0], wg.shape[1] // n_blk),
        (n_blk, wu.shape[0], wu.shape[1] // n_blk),
        (rows, QUERY_HEADS // n_blk * HEAD_SIZE),
        hidden.shape,
    ]
    shapes = [jax.ShapeDtypeStruct(s, jnp.bfloat16) for s in low] + [
        jax.ShapeDtypeStruct((rows, w_qkv.shape[1]), jnp.float32),
        jax.ShapeDtypeStruct((seqs, kv_heads, q_rows, HEAD_SIZE), jnp.bfloat16),
        jax.ShapeDtypeStruct((n_uly, 2, seqs, kv_heads, q_len, HEAD_SIZE), jnp.bfloat16),
        jax.ShapeDtypeStruct((seqs * kv_heads, 1, q_rows), jnp.float32),
    ]
    return pl.pallas_call(
        attention_kernel,
        out_shape=shapes,
        in_specs=[HBM] * 2 + [VMEM] * 9,
        out_specs=[HBM] * 2 + [VMEM] * 6,
        scratch_shapes=[pltpu.VMEM((key_pos.shape[0], q_rows), jnp.float32)] + semaphores(32),
        compiler_params=kernel_params(1, 60),
    )(
        wg,
        wu,
        hidden,
        w_qkv,
        gain,
        q_gain,
        k_gain,
        cosine,
        sine,
        query_pos,
        key_pos,
    )


def attention_back_kernel(
    all_low,
    wo,
    queries,
    key_values,
    lse,
    qkv,
    q_gain,
    k_gain,
    cosine,
    sine,
    query_pos,
    key_pos,
    grad_gate,
    grad_up,
    grad_qkv,
    gain_terms,
    gate_rows,
    up_rows,
    bias,
    grad_heads,
    grad_rows,
    probs,
    grad_probs,
    grad_kv,
    from_core,
    from_across,
    send,
    recv,
    here,
):
    links = Links(send, recv, here)
    links.greet(links.peers() + [links.y_way, links.core_way])
    swapped, keep = [], []
    for source, target in ((grad_gate, gate_rows), (grad_up, up_rows)):
        for step in range(1, links.n_blk):
            peer = links.peer(step)
            swapped.append(
                links.to(source.at[peer], target.at[links.blk], (links.dp, peer, links.uly))
            )
        keep.append(links.local(source.at[links.blk], target.at[links.blk]))
    grad_heads[...] = product_right(all_low[...], wo[...])
    mask_scores(bias, query_pos, key_pos)
    seqs, kv_heads, q_rows, _ = queries.shape
    q_len = key_values.shape[4]
    group = q_rows // q_len
    blocks = RowBlocks(links.n_blk, seqs, q_len // links.n_blk)
    q_end = kv_heads * group * HEAD_SIZE
    k_end = q_end + kv_heads * HEAD_SIZE
    gain_terms[...] = jnp.zeros_like(gain_terms)

    def gather_rows(seq, rows, start):
        for head in range(kv_heads * group):
            to = pl.ds((head % group) * q_len + start, blocks.toks)
            grad_rows[seq, head // group, to, :] = grad_heads[
                rows, head * HEAD_SIZE : (head + 1) * HEAD_SIZE
            ].astype(jnp.bfloat16)

    blocks.each(gather_rows)

    def back_norm(upstream, pre, gain, at, which):
        upstream = turned(upstream, cosine[at, :], -sine[at, :])
        back, term = back_rows(upstream, pre, gain[...])
        gain_terms[which : which + 1, :] += term
        return back.astype(jnp.bfloat16)

    def back(seq, head):
        def first(piece, delta):
            rows = pl.ds(pl.multiple_of(piece * q_len, q_len), q_len)
            scores = product_right(key_values[piece, 0, seq, head], queries[seq, head])
            prob = jnp.exp(
                scores * SCORE_SCALE + bias[rows, :] - lse[seq * kv_heads + head]
            )
            grad_prob = product_right(key_values[piece, 1, seq, head], grad_rows[seq, head])
            probs[rows, :] = prob
            grad_probs[rows, :] = grad_prob
            return delta + jnp.sum(prob * grad_prob, axis=0, keepdims=True)

        delta = lax.fori_loop(0, links.n_uly, first, jnp.zeros((1, q_rows), jnp.float32))

        def second(piece, grad_query):
            rows = pl.ds(pl.multiple_of(piece * q_len, q_len), q_len)
            prob = probs[rows, :]
            grad_score = (prob * (grad_probs[rows, :] - delta)).astype(jnp.bfloat16)
            grad_kv[seq, piece, 0, head] = (
                SCORE_SCALE
                * jnp.dot(grad_score, queries[seq, head], preferred_element_type=jnp.float32)
            ).astype(jnp.bfloat16)
            grad_kv[seq, piece, 1, head] = jnp.dot(
                prob.astype(jnp.bfloat16),
                grad_rows[seq, head],
                preferred_element_type=jnp.float32,
            ).astype(jnp.bfloat16)
            return grad_query + transposed_product(key_values[piece, 0, seq, head], grad_score)

        grad_query = lax.fori_loop(
            0, links.n_uly, second, jnp.zeros((HEAD_SIZE, q_rows), jnp.float32)
        )
        grad_heads[:, :HEAD_SIZE] = (grad_query * SCORE_SCALE).T
        for member in range(group):
            column = (head * group + member) * HEAD_SIZE
            for blk in range(links.n_blk):
                row = (blk * seqs + seq) * blocks.toks
                at = pl.ds(blk * blocks.toks, blocks.toks)
                start = member * q_len + blk * blocks.toks
                grad_qkv[row : row + blocks.toks, column : column + HEAD_SIZE] = back_norm(
                    grad_heads[start : start + blocks.toks, :HEAD_SIZE],
                    qkv[row : row + blocks.toks, column : column + HEAD_SIZE],
                    q_gain,
                    at,
                    0,
                )

    core, line = lax.rem(links.uly, 2), lax.div(links.uly, 2)

    def add(target, source):
        for kind in range(2):
            for head in range(kv_heads):
                target[kind, head] = target[kind, head] + source[kind, head]

    def core_sums(seq):
        copies = [
            links.to(
                grad_kv.at[seq, row * 2 + 1 - core], from_core.at[seq, row], links.core_way
            )
            for row in range(2)
        ]
        return copies

    def across_sums(seq, copies):
        for row in range(2):
            copies[row].arrived()
            add(grad_kv.at[seq, row * 2 + core], from_core.at[seq, row])
        return links.to(
            grad_kv.at[seq, (1 - line) * 2 + core], from_across.at[seq], links.y_way
        )

    def own_keys(seq, copy):
        copy.arrived()
        for head in range(kv_heads):
            for blk in range(links.n_blk):
                row = (blk * seqs + seq) * blocks.toks
                at = pl.ds(blk * blocks.toks, blocks.toks)
                term = [
                    grad_kv[seq, links.uly, kind, head, at, :].astype(jnp.float32)
                    + from_across[seq, kind, head, at, :].astype(jnp.float32)
                    for kind in range(2)
                ]
                k_at = q_end + head * HEAD_SIZE
                v_at = k_end + head * HEAD_SIZE
                grad_qkv[row : row + blocks.toks, k_at : k_at + HEAD_SIZE] = back_norm(
                    term[0],
                    qkv[row : row + blocks.toks, k_at : k_at + HEAD_SIZE],
                    k_gain,
                    at,
                    1,
                )
                grad_qkv[row : row + blocks.toks, v_at : v_at + HEAD_SIZE] = term[1].astype(
                    jnp.bfloat16
                )

    stage, last = None, []
    for seq in range(seqs):
        for head in range(kv_heads):
            back(seq, head)
            if stage is not None:
                last.append((seq - 1, across_sums(seq - 1, stage)))
                stage = None
        stage = core_sums(seq)
    last.append((seqs - 1, across_sums(seqs - 1, stage)))
    for seq, copy in last:
        own_keys(seq, copy)
    for copy in keep:
        copy.wait()
    for copy in swapped:
        copy.arrived()
    links.finish()


def attend_back(
    all_low,
    wo,
    queries,
    key_values,
    lse,
    qkv,
    q_gain,
    k_gain,
    cosine,
    sine,
    query_pos,
    key_pos,
    grad_gate,
    grad_up,
):
    seqs, kv_heads, q_rows, _ = queries.shape
    n_uly, _, _, _, q_len, _ = key_values.shape
    rows = all_low.shape[0]
    keys = key_pos.shape[0]
    f32, low = jnp.float32, jnp.bfloat16
    scratch = [
        ((keys, q_rows), f32),
        ((rows, wo.shape[0]), f32),
        (queries.shape, low),
        ((keys, q_rows), f32),
        ((keys, q_rows), f32),
        ((seqs, n_uly, 2, kv_heads, q_len, HEAD_SIZE), low),
        ((seqs, 2, 2, kv_heads, q_len, HEAD_SIZE), low),
        ((seqs, 2, kv_heads, q_len, HEAD_SIZE), low),
    ]
    return pl.pallas_call(
        attention_back_kernel,
        out_shape=[
            jax.ShapeDtypeStruct(qkv.shape, low),
            jax.ShapeDtypeStruct((8, HEAD_SIZE), f32),
            jax.ShapeDtypeStruct(grad_gate.shape, low),
            jax.ShapeDtypeStruct(grad_up.shape, low),
        ],
        in_specs=[VMEM] * 12 + [HBM] * 2,
        out_specs=[VMEM] * 2 + [HBM] * 2,
        scratch_shapes=[pltpu.VMEM(shape, kind) for shape, kind in scratch] + semaphores(24),
        compiler_params=kernel_params(5),
    )(
        all_low,
        wo,
        queries,
        key_values,
        lse,
        qkv,
        q_gain,
        k_gain,
        cosine,
        sine,
        query_pos,
        key_pos,
        grad_gate,
        grad_up,
    )


def middle_kernel(
    heads,
    wo,
    source,
    gain,
    rows_wg,
    rows_wu,
    cotangent,
    middle,
    all_normed,
    all_wg,
    all_wu,
    all_cot,
    parts,
    rightward,
    leftward,
    normed,
    send,
    recv,
    here,
):
    links = Links(send, recv, here)
    links.greet(links.peers() + [links.x_way, links.y_way, links.core_way])
    planes, keep = [], []
    for chunk, whole in ((rows_wg, all_wg), (rows_wu, all_wu)):
        at = rows_of(whole, True)
        plane = PlaneGather(links, at)
        plane.start(chunk)
        planes.append(plane)
        keep.append(links.local(chunk, at(links.dp, links.uly)))
    keep.append(links.local(cotangent, all_cot.at[links.blk]))
    tokens = source.shape[0]
    for blk in (links.n_blk - 1, 0) + tuple(range(1, links.n_blk - 1)):
        parts[blk] = jnp.dot(heads[blk], wo[...], preferred_element_type=jnp.float32).astype(
            jnp.bfloat16
        )
    scatter = LineScatter(links, parts, rightward, leftward)
    scatter.start()
    cot_line = LineGather(links, cotangent, all_cot)
    for step in range(links.n_blk - 1):
        cot_line.send(step)
        scatter.step(step)
        cot_line.arrived()
        if step < len(planes):
            planes[step].hand_on()
    scatter.finish(middle)

    def body(rows):
        total = middle[rows, :] + source[rows, :].astype(jnp.float32)
        middle[rows, :] = total
        normed[rows, :] = (total * rms_scale(total) * gain[...]).astype(jnp.bfloat16)

    each_block(tokens, body)
    keep.append(links.local(normed, all_normed.at[links.blk]))
    line = LineGather(links, normed, all_normed)
    for step in range(links.n_blk - 1):
        line.send(step)
        if step < len(planes):
            planes[step].last()
        line.arrived()
    for plane in planes:
        plane.arrived()
    for copy in keep:
        copy.wait()
    scatter.sent()
    links.finish()


def exchange_middle(heads, wo, source, gain, rows_wg, rows_wu, cotangent):
    n_dp, n_blk, n_uly = (lax.axis_size(a) for a in EVERY)
    tokens, width = source.shape
    low = [(n_blk, tokens, width)]
    low += [(n_dp, n_blk, n_uly) + chunk.shape[1:] for chunk in (rows_wg, rows_wu)]
    low.append((n_blk, tokens, width))
    return pl.pallas_call(
        middle_kernel,
        out_shape=[jax.ShapeDtypeStruct((tokens, width), jnp.float32)]
        + [jax.ShapeDtypeStruct(shape, jnp.bfloat16) for shape in low],
        in_specs=[VMEM] * 4 + [HBM] * 3,
        out_specs=[VMEM] + [HBM] * 4,
        scratch_shapes=[pltpu.VMEM((n_blk, tokens, width), jnp.bfloat16)]
        + line_scratch(n_blk, tokens, width)
        + [pltpu.VMEM((tokens, width), jnp.bfloat16)]
        + semaphores(48),
        compiler_params=kernel_params(2, 60),
    )(heads, wo, source, gain, rows_wg, rows_wu, cotangent)


def back_rows(grad_normed, source, gain):
    scale = rms_scale(source)
    unit = source * scale
    scaled = grad_normed * gain
    back = scale * (scaled - unit * jnp.mean(scaled * unit, axis=-1, keepdims=True))
    return back, jnp.sum(grad_normed * unit, axis=0, keepdims=True)


def back_kernel(
    grad_parts,
    out_parts,
    middle,
    cotangent,
    gain,
    all_normed,
    grad_gate_pre,
    grad_up_pre,
    activated,
    all_cot,
    output,
    grad_middle,
    gain_term,
    all_low,
    grad_gate,
    grad_up,
    grad_down,
    rightward,
    leftward,
    out_right,
    out_left,
    out_total,
    low,
    gate_1,
    gate_2,
    gate_3,
    gate_4,
    gate_5,
    gate_6,
    up_1,
    up_2,
    up_3,
    up_4,
    up_5,
    up_6,
    down_1,
    down_2,
    down_3,
    down_4,
    down_5,
    down_6,
    send,
    recv,
    here,
):
    links = Links(send, recv, here)
    links.greet(links.peers() + [links.x_way, links.y_way, links.core_way])
    scatter = LineScatter(links, grad_parts, rightward, leftward)
    scatter.start()
    out_scatter = LineScatter(links, out_parts, out_right, out_left)
    gate = PlaneScatter(links, gate_1, gate_2, gate_3, gate_4, gate_5, gate_6)
    up = PlaneScatter(links, up_1, up_2, up_3, up_4, up_5, up_6)
    down = PlaneScatter(links, down_1, down_2, down_3, down_4, down_5, down_6)

    def compute(scatter, left, right, parts, together):
        for which, dp in ((0, links.other_dp), (1, links.dp)):
            weight_grad(left, right, parts, dp, together)
            scatter.between_cores(which)

    compute(gate, all_normed, grad_gate_pre, gate_1, 4)
    scatter.step(0)
    compute(up, all_normed, grad_up_pre, up_1, 4)
    gate.across_chips()
    scatter.step(1)
    compute(down, activated, all_cot, down_1, 2)
    up.across_chips()
    for step in range(2, links.n_blk - 1):
        scatter.step(step)
    down.across_chips()
    scatter.finish(grad_middle)
    gain_term[...] = jnp.zeros_like(gain_term)

    def body(rows):
        back, term = back_rows(grad_middle[rows, :], middle[rows, :], gain[...])
        grad = cotangent[rows, :].astype(jnp.float32) + back
        gain_term[...] += term
        grad_middle[rows, :] = grad
        low[rows, :] = grad.astype(jnp.bfloat16)

    each_block(middle.shape[0], body)
    keep = links.local(low, all_low.at[links.blk])
    line = LineGather(links, low, all_low)
    line.send(0)
    out_scatter.start()
    gate.second_way()
    line.arrived()
    for step in range(1, links.n_blk - 1):
        line.send(step)
        out_scatter.step(step - 1)
        if step == 1:
            up.second_way()
        line.arrived()
    down.second_way()
    out_scatter.step(links.n_blk - 2)

    def into(target):
        def write(block, rows, values):
            target[block, rows, :] = values.astype(target.dtype)

        return write

    gate.result(into(grad_gate))
    up.result(into(grad_up))
    out_scatter.finish(out_total)

    def add_output(rows):
        output[rows, :] = (middle[rows, :] + out_total[rows, :]).astype(jnp.bfloat16)

    each_block(middle.shape[0], add_output)
    down.result(into(grad_down))
    keep.wait()
    scatter.sent()
    out_scatter.sent()
    links.finish()


def exchange_back(
    grad_parts,
    out_parts,
    middle,
    cotangent,
    gain,
    all_normed,
    grad_gate_pre,
    grad_up_pre,
    activated,
    all_cot,
):
    n_dp, n_blk, n_uly = (lax.axis_size(a) for a in EVERY)
    _, tokens, width = grad_parts.shape
    ff = grad_gate_pre.shape[1]
    depth = width // (n_dp * n_blk * n_uly)
    down_depth = ff // (n_dp * n_uly)
    return pl.pallas_call(
        back_kernel,
        out_shape=[
            jax.ShapeDtypeStruct((tokens, width), jnp.bfloat16),
            jax.ShapeDtypeStruct((tokens, width), jnp.float32),
            jax.ShapeDtypeStruct((1, width), jnp.float32),
            jax.ShapeDtypeStruct((n_blk, tokens, width), jnp.bfloat16),
            jax.ShapeDtypeStruct((n_blk, depth, ff), jnp.bfloat16),
            jax.ShapeDtypeStruct((n_blk, depth, ff), jnp.bfloat16),
            jax.ShapeDtypeStruct((1, down_depth, width), jnp.float32),
        ],
        in_specs=[VMEM] * 10,
        out_specs=[VMEM, VMEM, VMEM, HBM, VMEM, VMEM, VMEM],
        scratch_shapes=line_scratch(n_blk, tokens, width) * 2
        + [pltpu.VMEM((tokens, width), jnp.float32), pltpu.VMEM((tokens, width), jnp.bfloat16)]
        + plane_scratch(n_dp, n_blk, n_uly, depth, ff) * 2
        + plane_scratch(n_dp, 1, n_uly, down_depth, width)
        + semaphores(56),
        compiler_params=kernel_params(3, 63),
    )(
        grad_parts,
        out_parts,
        middle,
        cotangent,
        gain,
        all_normed,
        grad_gate_pre,
        grad_up_pre,
        activated,
        all_cot,
    )


def last_kernel(
    w_qkv,
    hidden,
    grad_middle,
    gain,
    normed,
    grad_qkv,
    heads,
    all_low,
    mlp_term,
    head_terms,
    grad_hidden,
    grad_w_qkv,
    grad_wo,
    small_sum,
    grad_parts,
    rightward,
    leftward,
    qkv_1,
    qkv_2,
    qkv_3,
    qkv_4,
    qkv_5,
    qkv_6,
    wo_1,
    wo_2,
    wo_3,
    wo_4,
    wo_5,
    wo_6,
    summed,
    small,
    attn_term,
    small_in,
    small_total,
    send,
    recv,
    here,
):
    links = Links(send, recv, here)
    links.greet(links.peers() + [links.x_way, links.y_way, links.core_way])
    scatter = LineScatter(links, grad_parts, rightward, leftward)
    qkv = PlaneScatter(links, qkv_1, qkv_2, qkv_3, qkv_4, qkv_5, qkv_6)
    out = PlaneScatter(links, wo_1, wo_2, wo_3, wo_4, wo_5, wo_6)

    for which, dp in ((0, links.other_dp), (1, links.dp)):
        weight_grad(normed, grad_qkv, qkv_1, dp, 4)
        qkv.between_cores(which)
    attn_term[...] = jnp.zeros_like(attn_term)
    tokens = grad_parts.shape[1]
    for blk in (links.n_blk - 1, 0) + tuple(range(1, links.n_blk - 1)):
        grad_hidden[...] = product_right(
            grad_qkv[blk * tokens : (blk + 1) * tokens, :], w_qkv[...]
        )

        def collect(rows, blk=blk):
            part = grad_hidden[rows, :]
            source = hidden[blk, rows, :].astype(jnp.float32)
            grad_parts[blk, rows, :] = part.astype(jnp.bfloat16)
            attn_term[...] += jnp.sum(part * (source * rms_scale(source)), axis=0, keepdims=True)

        each_block(tokens, collect)
    scatter.start()
    qkv.across_chips()
    small[...] = jnp.zeros_like(small)
    span = gain.shape[1] // 128
    for index in range(span):
        columns = slice(index * 128, (index + 1) * 128)
        small[index : index + 1, :] = attn_term[:, columns]
        small[span + index : span + index + 1, :] = mlp_term[:, columns]
    small[2 * span : 2 * span + 8, :] = head_terms[...]
    small_in[links.blk] = small[...]
    small_copies = [links.to(small, small_in.at[links.blk], device) for device in links.peers()]
    for which, dp in ((0, links.other_dp), (1, links.dp)):
        weight_grad(heads, all_low, wo_1, dp, 4)
        out.between_cores(which)
    scatter.step(0)
    out.across_chips()
    for copy in small_copies:
        copy.arrived()
    total = small_in[0]
    for blk in range(1, links.n_blk):
        total = total + small_in[blk]
    small_total[0] = total
    pending = links.to(small_total.at[0], small_in.at[links.n_blk], links.x_way)
    qkv.second_way()
    pending.arrived()
    small_total[1] = small_total[0] + small_in[links.n_blk]
    pending = links.to(small_total.at[1], small_in.at[links.n_blk + 1], links.y_way)
    scatter.step(1)
    out.second_way()
    pending.arrived()
    small_total[2] = small_total[1] + small_in[links.n_blk + 1]
    pending = links.to(small_total.at[2], small_in.at[links.n_blk + 2], links.core_way)

    def write(block, rows, values):
        summed[block, rows, :] = values.astype(jnp.bfloat16)

    qkv.result(write)
    swapped = []
    for step in range(1, links.n_blk):
        peer = links.peer(step)
        swapped.append(
            links.to(summed.at[peer], grad_w_qkv.at[links.blk], (links.dp, peer, links.uly))
        )
    keep = links.local(summed.at[links.blk], grad_w_qkv.at[links.blk])
    for step in range(2, links.n_blk - 1):
        scatter.step(step)
    pending.arrived()
    small_sum[...] = small_total[2] + small_in[links.n_blk + 2]
    scatter.finish(grad_hidden)

    def body(rows):
        back, _ = back_rows(
            grad_hidden[rows, :], hidden[links.blk, rows, :].astype(jnp.float32), gain[...]
        )
        grad_hidden[rows, :] = grad_middle[rows, :] + back

    each_block(tokens, body)

    def write_out(block, rows, values):
        grad_wo[block, rows, :] = values

    out.result(write_out)
    for copy in swapped:
        copy.arrived()
    keep.wait()
    scatter.sent()
    links.finish()


def exchange_last(
    w_qkv,
    hidden,
    grad_middle,
    gain,
    normed,
    grad_qkv,
    heads,
    all_low,
    mlp_term,
    head_terms,
):
    n_dp, n_blk, n_uly = (lax.axis_size(a) for a in EVERY)
    _, tokens, width = hidden.shape
    columns = grad_qkv.shape[1]
    depth = width // (n_dp * n_blk * n_uly)
    out_depth = heads.shape[1] // (n_dp * n_uly)
    small = (2 * width // 128 + 8, 128)
    return pl.pallas_call(
        last_kernel,
        out_shape=[
            jax.ShapeDtypeStruct((tokens, width), jnp.float32),
            jax.ShapeDtypeStruct((n_blk, depth, columns), jnp.bfloat16),
            jax.ShapeDtypeStruct((1, out_depth, width), jnp.float32),
            jax.ShapeDtypeStruct(small, jnp.float32),
        ],
        in_specs=[VMEM] * 10,
        out_specs=[VMEM, HBM, VMEM, VMEM],
        scratch_shapes=[pltpu.VMEM((n_blk, tokens, width), jnp.bfloat16)]
        + line_scratch(n_blk, tokens, width)
        + plane_scratch(n_dp, n_blk, n_uly, depth, columns)
        + plane_scratch(n_dp, 1, n_uly, out_depth, width)
        + [
            pltpu.VMEM((n_blk, depth, columns), jnp.bfloat16),
            pltpu.VMEM(small, jnp.float32),
            pltpu.VMEM((1, width), jnp.float32),
            pltpu.VMEM((n_blk + 3,) + small, jnp.float32),
            pltpu.VMEM((3,) + small, jnp.float32),
        ]
        + semaphores(48),
        compiler_params=kernel_params(4, 56),
    )(
        w_qkv,
        hidden,
        grad_middle,
        gain,
        normed,
        grad_qkv,
        heads,
        all_low,
        mlp_term,
        head_terms,
    )


def finish_kernel(
    gate,
    up,
    qkv,
    wo,
    wd,
    hidden,
    out,
    f_gate,
    f_up,
    f_q,
    f_k,
    f_v,
    f_wo,
    f_wd,
    f_hidden,
    f_out,
):
    n_blk, depth, _ = gate.shape

    def place(source, offset, target):
        width = target.shape[1] // (n_blk * 2)
        for blk in range(n_blk):
            for group in range(2):
                to = (group * n_blk + blk) * width
                at = offset + group * width
                target[:, to : to + width] = source[blk, :, at : at + width].astype(jnp.float32)

    place(gate, 0, f_gate)
    place(up, 0, f_up)
    q_width = f_q.shape[1] // n_blk
    k_width = f_k.shape[1] // n_blk
    place(qkv, 0, f_q)
    place(qkv, q_width, f_k)
    place(qkv, q_width + k_width, f_v)
    f_wo[...] = wo[0]
    f_wd[...] = wd[0]
    f_hidden[...] = hidden[...]
    f_out[...] = out[...]


def finish(gate, up, qkv, wo, wd, hidden, out, shapes):
    return pl.pallas_call(
        finish_kernel,
        out_shape=[jax.ShapeDtypeStruct(shape, jnp.float32) for shape in shapes]
        + [
            jax.ShapeDtypeStruct(wo.shape[1:], jnp.float32),
            jax.ShapeDtypeStruct(wd.shape[1:], jnp.float32),
            jax.ShapeDtypeStruct(hidden.shape, jnp.float32),
            jax.ShapeDtypeStruct(out.shape, jnp.bfloat16),
        ],
        in_specs=[VMEM] * 7,
        out_specs=[VMEM] * 9,
        compiler_params=pltpu.CompilerParams(vmem_limit_bytes=40 * MIB),
    )(gate, up, qkv, wo, wd, hidden, out)


def product(left, right):
    return jnp.dot(left, right, preferred_element_type=jnp.float32)


def shards(
    hidden,
    span_order,
    attn_gain,
    w_query,
    key_weight,
    value_weight,
    w_out,
    q_gain,
    k_gain,
    mlp_gain,
    w_gate,
    w_up,
    w_down,
    cotangent,
):
    seqs, toks, width = hidden.shape
    n_dp, n_blk, n_uly = (lax.axis_size(a) for a in EVERY)
    blk_index = lax.axis_index(BLK)
    uly_index = lax.axis_index(ULY)
    group = QUERY_HEADS // KEY_VALUE_HEADS
    half_len = toks * n_uly // 2
    rows = n_blk * seqs * toks
    f32, bf16 = jnp.float32, jnp.bfloat16
    own_hidden = hidden.reshape(seqs * toks, width)
    own_cotangent = cotangent.reshape(seqs * toks, width)

    def positions(u):
        places = (
            jnp.arange(n_blk, dtype=jnp.int32)[:, None] * n_uly + u
        ) * toks + jnp.arange(toks, dtype=jnp.int32)[None, :]
        return positions_of(places.reshape(-1), span_order, half_len)

    own_pos = positions(uly_index)
    query_pos = jnp.tile(own_pos, group)[None, :]
    key_pos = jnp.concatenate([positions(u) for u in range(n_uly)])[:, None]
    angles = angles_of(own_pos, HEAD_SIZE)
    cosine, sine = jnp.cos(angles), jnp.sin(angles)
    cosine = jnp.concatenate([cosine, cosine], axis=1)
    sine = jnp.concatenate([-sine, sine], axis=1)
    gain_q, gain_k = q_gain.astype(f32)[None, :], k_gain.astype(f32)[None, :]

    gain_rows = attn_gain.shape[0]
    own_gains = jnp.pad(jnp.stack([attn_gain, mlp_gain]), ((0, 14), (0, 128 - gain_rows)))
    all_hidden, w_qkv, wo, all_wd, all_gains = gather_front(
        own_hidden, w_query, key_weight, value_weight, w_out, w_down, own_gains
    )
    gains = all_gains[..., :2, :gain_rows].astype(f32)
    g_attn = gains[..., 0, :].reshape(1, width)
    g_mlp = gains[..., 1, :].reshape(1, width)
    w_qkv = w_qkv.reshape(width, -1)
    wo = wo.reshape(-1, width)
    (
        rows_wg,
        rows_wu,
        heads_flat,
        normed,
        qkv,
        queries,
        key_values,
        lse,
    ) = attend_forward(
        w_gate,
        w_up,
        all_hidden.reshape(rows, width),
        w_qkv,
        g_attn,
        gain_q,
        gain_k,
        cosine,
        sine,
        query_pos,
        key_pos,
        seqs,
    )
    middle, normed2, all_wg, all_wu, cot = exchange_middle(
        heads_flat.reshape(n_blk, seqs * toks, -1),
        wo,
        own_hidden,
        g_mlp,
        rows_wg,
        rows_wu,
        own_cotangent,
    )
    wg, wu = all_wg.reshape(width, -1), all_wu.reshape(width, -1)
    wd = all_wd.reshape(-1, width)
    cot = cot.reshape(rows, width)
    normed2 = normed2.reshape(rows, width)
    gate_pre = product(normed2, wg)
    up_pre = product(normed2, wu)
    sigmoid_gate = jax.nn.sigmoid(gate_pre)
    activated = (gate_pre * sigmoid_gate * up_pre).astype(bf16)
    out_parts = product(activated, wd).astype(bf16)
    grad_act = product_right(cot, wd)
    grad_gate_pre = (
        grad_act * up_pre * sigmoid_gate * (1.0 + gate_pre * (1.0 - sigmoid_gate))
    ).astype(bf16)
    grad_up_pre = (grad_act * gate_pre * sigmoid_gate).astype(bf16)
    grad_parts = (product_right(grad_gate_pre, wg) + product_right(grad_up_pre, wu)).astype(bf16)
    blocks = (n_blk, seqs * toks, width)
    output, grad_middle, mlp_gain_term, middle_low, grad_gate, grad_up, grad_down = exchange_back(
        grad_parts.reshape(blocks),
        out_parts.reshape(blocks),
        middle,
        own_cotangent,
        g_mlp,
        normed2,
        grad_gate_pre,
        grad_up_pre,
        activated,
        cot,
    )
    middle_low = middle_low.reshape(rows, width)
    grad_qkv, head_terms, grad_gate, grad_up = attend_back(
        middle_low,
        wo,
        queries,
        key_values,
        lse,
        qkv,
        gain_q,
        gain_k,
        cosine,
        sine,
        query_pos,
        key_pos,
        grad_gate,
        grad_up,
    )
    grad_hidden, grad_w_qkv, grad_out, small = exchange_last(
        w_qkv,
        all_hidden,
        grad_middle,
        g_attn,
        normed,
        grad_qkv,
        heads_flat,
        middle_low,
        mlp_gain_term,
        head_terms,
    )
    (
        grad_gate,
        grad_up,
        grad_query,
        grad_key,
        grad_value,
        grad_out,
        grad_down,
        grad_hidden,
        output,
    ) = finish(
        grad_gate,
        grad_up,
        grad_w_qkv,
        grad_out,
        grad_down,
        grad_hidden,
        output,
        [w.shape for w in (w_gate, w_up, w_query, key_weight, value_weight)],
    )
    small = small.reshape(-1)
    gain_at = ((lax.axis_index(DP) * n_blk + blk_index) * n_uly + uly_index) * gain_rows
    grad_attn_gain = lax.dynamic_slice(small, (gain_at,), (gain_rows,))
    grad_mlp_gain = lax.dynamic_slice(small, (width + gain_at,), (gain_rows,))
    grad_q_gain = small[2 * width : 2 * width + HEAD_SIZE]
    grad_k_gain = small[2 * width + HEAD_SIZE : 2 * width + 2 * HEAD_SIZE]
    return (
        output.reshape(hidden.shape),
        grad_hidden.reshape(hidden.shape),
        grad_attn_gain,
        grad_query,
        grad_key,
        grad_value,
        grad_out,
        grad_q_gain,
        grad_k_gain,
        grad_mlp_gain,
        grad_gate,
        grad_up,
        grad_down,
    )


def solution(mesh):
    n_dp, n_blk, n_uly = (mesh.shape[a] for a in EVERY)
    aligned = (n_dp, n_uly) == (2, 4) and KEY_VALUE_HEADS % (n_dp * n_blk) == 0
    in_specs = (
        TOKENS,
        P(),
        P(EVERY),
        P(EVERY, None),
        P(EVERY, None),
        P(EVERY, None),
        P(EVERY, None),
        P(),
        P(),
        P(EVERY),
        P(EVERY, None),
        P(EVERY, None),
        P(EVERY, None),
        TOKENS,
    )
    out_specs = (
        TOKENS,
        TOKENS,
        P(EVERY),
        P(EVERY, None),
        P(EVERY, None),
        P(EVERY, None),
        P(EVERY, None),
        P(),
        P(),
        P(EVERY),
        P(EVERY, None),
        P(EVERY, None),
        P(EVERY, None),
    )
    return jax.shard_map(
        shards if aligned else shards_general,
        mesh=mesh, in_specs=in_specs, out_specs=out_specs, check_vma=False)
```

```python
import math

import jax
import jax.numpy as jnp
from jax import lax
from jax.experimental import pallas as pl
from jax.experimental.pallas import tpu as pltpu
from jax.sharding import PartitionSpec as P

QUERY_HEADS = 16
KEY_VALUE_HEADS = 8
HEAD_SIZE = 128


DP, BLK, ULY = "dp", "blk", "uly"
EVERY = (DP, BLK, ULY)
PLANE = (DP, ULY)
TOKENS = P(DP, (BLK, ULY), None)
EQ_KGQD_NKD_TO_KGQN = "kgqd,nkd->kgqn"
EQ_KGQN_KGQD_TO_NKD = "kgqn,kgqd->nkd"
EQ_KGQN_NKD_TO_KGQD = "kgqn,nkd->kgqd"
EQ_KGQN_QKGD_TO_NKD = "kgqn,qkgd->nkd"
EQ_QKGD_NKD_TO_KGQN = "qkgd,nkd->kgqn"
EQ_STD_DE_TO_STE = "std,de->ste"
EQ_STD_DF_TO_STF = "std,df->stf"
EQ_STD_ED_TO_STE = "std,ed->ste"
EQ_STD_FD_TO_STF = "std,fd->stf"
EQ_STD_STE_TO_DE = "std,ste->de"
EQ_STD_STF_TO_DF = "std,stf->df"
EQ_STE_DE_TO_STD = "ste,de->std"
EQ_STE_ED_TO_STD = "ste,ed->std"
EQ_STE_STD_TO_ED = "ste,std->ed"
EQ_STF_DF_TO_STD = "stf,df->std"
EQ_STF_FD_TO_STD = "stf,fd->std"
EQ_STF_STD_TO_FD = "stf,std->fd"

EPSILON = 1e-06
ROPE_BASE = 1000000.0


def rms_scale(source):
    return lax.rsqrt(jnp.mean(source * source, axis=-1, keepdims=True) + EPSILON)


def norm_back(grad_normed, source, norm_scale, gain):
    unit_rows = source * norm_scale
    scaled = grad_normed * gain
    return norm_scale * (scaled - unit_rows * jnp.mean(scaled * unit_rows, axis=-1, keepdims=True))


def angles_of(positions, head_dim):
    freq_steps = jnp.arange(head_dim // 2, dtype=jnp.float32)
    inverse = jnp.exp(freq_steps * (-2.0 * math.log(ROPE_BASE) / head_dim))
    return positions.astype(jnp.float32)[:, None] * inverse[None, :]


def rotate(source, angles, direction):
    half_dim = source.shape[-1] // 2
    cosine = jnp.cos(angles)[:, None, :]
    sine_part = direction * jnp.sin(angles)[:, None, :]
    first_half = source[..., :half_dim]
    second_half = source[..., half_dim:]
    return jnp.concatenate(
        [
            first_half * cosine - second_half * sine_part,
            second_half * cosine + first_half * sine_part,
        ],
        axis=-1,
    )


def positions_of(places, span_order, half_len):
    blocks_of = places // half_len
    block_ids = jnp.arange(span_order.shape[0], dtype=jnp.int32)
    chosen = jnp.sum(
        jnp.where(blocks_of[:, None] == block_ids[None, :], span_order[None, :], 0), axis=1
    )
    return chosen * half_len + places % half_len


def add_rows(buffer, new_rows):
    return buffer + new_rows


def shards_general(
    hidden,
    span_order,
    attn_gain,
    w_query,
    key_weight,
    value_weight,
    w_out,
    q_gain,
    k_gain,
    mlp_gain,
    w_gate,
    w_up,
    w_down,
    cotangent,
):
    sequence_count = hidden.shape[0]
    token_count = hidden.shape[1]
    ulysses_group_size = lax.axis_size(ULY)
    local_q = QUERY_HEADS // ulysses_group_size
    local_key_value = KEY_VALUE_HEADS // ulysses_group_size
    query_group_width = QUERY_HEADS // KEY_VALUE_HEADS
    block_len = token_count * ulysses_group_size
    half_len = block_len // 2
    score_scale = 1.0 / math.sqrt(HEAD_SIZE)
    blk_index = lax.axis_index(BLK)
    uly_index = lax.axis_index(ULY)
    first_place = (blk_index * ulysses_group_size + uly_index) * token_count
    local_angles = angles_of(
        positions_of(first_place + jnp.arange(token_count, dtype=jnp.int32), span_order, half_len),
        HEAD_SIZE,
    )
    query_pos = positions_of(
        blk_index * block_len + jnp.arange(block_len, dtype=jnp.int32), span_order, half_len
    )
    g_attn, wq_all, wk_all, wv_all, wo_all = (
        lax.all_gather(attn_gain, EVERY, axis=0, tiled=True),
        lax.all_gather(w_query, EVERY, axis=0, tiled=True),
        lax.all_gather(key_weight, EVERY, axis=0, tiled=True),
        lax.all_gather(value_weight, EVERY, axis=0, tiled=True),
        lax.all_gather(w_out, EVERY, axis=0, tiled=True),
    )
    source = hidden.astype(jnp.float32)
    first_scale = rms_scale(source)
    normalized_input = (source * first_scale * g_attn.astype(jnp.float32)).astype(jnp.bfloat16)
    q_pre = jnp.einsum(
        EQ_STD_DE_TO_STE, normalized_input, wq_all, preferred_element_type=jnp.float32
    ).reshape(sequence_count, token_count, QUERY_HEADS, HEAD_SIZE)
    key_before_norm = jnp.einsum(
        EQ_STD_DE_TO_STE, normalized_input, wk_all, preferred_element_type=jnp.float32
    ).reshape(sequence_count, token_count, KEY_VALUE_HEADS, HEAD_SIZE)
    value_before_norm = jnp.einsum(
        EQ_STD_DE_TO_STE, normalized_input, wv_all, preferred_element_type=jnp.float32
    ).reshape(sequence_count, token_count, KEY_VALUE_HEADS, HEAD_SIZE)
    q_scale = rms_scale(q_pre)
    k_scale = rms_scale(key_before_norm)
    gain_q = q_gain.astype(jnp.float32)
    gain_k = k_gain.astype(jnp.float32)
    q_rot = rotate(q_pre * q_scale * gain_q, local_angles, 1.0).astype(jnp.bfloat16)
    k_rot = rotate(key_before_norm * k_scale * gain_k, local_angles, 1.0).astype(jnp.bfloat16)
    v_low = value_before_norm.astype(jnp.bfloat16)
    q_heads, k_heads, v_heads = (
        lax.all_to_all(q_rot, ULY, split_axis=2, concat_axis=1, tiled=True),
        lax.all_to_all(k_rot, ULY, split_axis=2, concat_axis=1, tiled=True),
        lax.all_to_all(v_low, ULY, split_axis=2, concat_axis=1, tiled=True),
    )
    q_group = q_heads.reshape(
        sequence_count, block_len, local_key_value, query_group_width, HEAD_SIZE
    )
    stat_shape = (sequence_count, local_key_value, query_group_width, block_len)
    start_state = (
        jnp.full(stat_shape, -1e30, jnp.float32),
        jnp.zeros(stat_shape, jnp.float32),
        jnp.zeros(stat_shape + (HEAD_SIZE,), jnp.float32),
    )
    key_piece = lax.all_gather(k_heads, BLK, axis=1, tiled=True)
    value_piece = lax.all_gather(v_heads, BLK, axis=1, tiled=True)
    key_pos = positions_of(jnp.arange(key_piece.shape[1], dtype=jnp.int32), span_order, half_len)
    allowed = query_pos[:, None] >= key_pos[None, :]

    def attend_one_sequence(members):
        query_rows, key_rows, value_rows, top_seq, total_seq, accum_seq = members
        scores = (
            jnp.einsum(EQ_QKGD_NKD_TO_KGQN, query_rows, key_rows, preferred_element_type=jnp.float32)
            * score_scale
        )
        scores = jnp.where(allowed, scores, -jnp.inf)
        new_top = jnp.maximum(top_seq, jnp.max(scores, axis=-1))
        fading = jnp.exp(top_seq - new_top)
        weights = jnp.exp(scores - new_top[..., None])
        total_seq = total_seq * fading + jnp.sum(weights, axis=-1)
        accum_seq = accum_seq * fading[..., None] + jnp.einsum(
            EQ_KGQN_NKD_TO_KGQD,
            weights.astype(jnp.bfloat16),
            value_rows,
            preferred_element_type=jnp.float32,
        )
        return (new_top, total_seq, accum_seq)

    row_top, row_total, accum = lax.map(
        attend_one_sequence,
        (q_group, key_piece, value_piece, start_state[0], start_state[1], start_state[2]),
    )
    log_total = row_top + jnp.log(row_total)
    attention_output = jnp.transpose(accum / row_total[..., None], (0, 3, 1, 2, 4)).reshape(
        sequence_count, block_len, local_q, HEAD_SIZE
    )
    heads_seq = lax.all_to_all(
        attention_output.astype(jnp.bfloat16), ULY, split_axis=1, concat_axis=2, tiled=True
    )
    heads_flat = heads_seq.reshape(sequence_count, token_count, QUERY_HEADS * HEAD_SIZE)
    middle = source + jnp.einsum(
        EQ_STE_ED_TO_STD, heads_flat, wo_all, preferred_element_type=jnp.float32
    )
    g_mlp, wg_all, wu_all, wd_all = (
        lax.all_gather(mlp_gain, EVERY, axis=0, tiled=True),
        lax.all_gather(w_gate, EVERY, axis=0, tiled=True),
        lax.all_gather(w_up, EVERY, axis=0, tiled=True),
        lax.all_gather(w_down, EVERY, axis=0, tiled=True),
    )
    second_scale = rms_scale(middle)
    gain_mlp = g_mlp.astype(jnp.float32)
    normed2 = (middle * second_scale * gain_mlp).astype(jnp.bfloat16)
    gate_pre = jnp.einsum(EQ_STD_DF_TO_STF, normed2, wg_all, preferred_element_type=jnp.float32)
    up_pre = jnp.einsum(EQ_STD_DF_TO_STF, normed2, wu_all, preferred_element_type=jnp.float32)
    sigmoid_gate = jax.nn.sigmoid(gate_pre)
    activated = (gate_pre * sigmoid_gate * up_pre).astype(jnp.bfloat16)
    result = middle + jnp.einsum(
        EQ_STF_FD_TO_STD, activated, wd_all, preferred_element_type=jnp.float32
    )
    output = result.astype(jnp.bfloat16)
    g_mlp, wg_all, wu_all, wd_all = (
        lax.all_gather(mlp_gain, EVERY, axis=0, tiled=True),
        lax.all_gather(w_gate, EVERY, axis=0, tiled=True),
        lax.all_gather(w_up, EVERY, axis=0, tiled=True),
        lax.all_gather(w_down, EVERY, axis=0, tiled=True),
    )
    gain_mlp = g_mlp.astype(jnp.float32)
    grad_act = jnp.einsum(EQ_STD_FD_TO_STF, cotangent, wd_all, preferred_element_type=jnp.float32)
    grad_gate_pre = (
        grad_act * up_pre * sigmoid_gate * (1.0 + gate_pre * (1.0 - sigmoid_gate))
    ).astype(jnp.bfloat16)
    grad_up_pre = (grad_act * gate_pre * sigmoid_gate).astype(jnp.bfloat16)
    grad_gate = jnp.einsum(
        EQ_STD_STF_TO_DF, normed2, grad_gate_pre, preferred_element_type=jnp.float32
    )
    grad_up = jnp.einsum(EQ_STD_STF_TO_DF, normed2, grad_up_pre, preferred_element_type=jnp.float32)
    grad_normed2 = jnp.einsum(
        EQ_STF_DF_TO_STD, grad_gate_pre, wg_all, preferred_element_type=jnp.float32
    ) + jnp.einsum(EQ_STF_DF_TO_STD, grad_up_pre, wu_all, preferred_element_type=jnp.float32)
    mlp_gain_term = jnp.sum(grad_normed2 * middle * second_scale, axis=(0, 1))
    grad_middle = cotangent.astype(jnp.float32) + norm_back(
        grad_normed2, middle, second_scale, gain_mlp
    )
    grad_mlp_gain, grad_gate, grad_up = (
        lax.psum_scatter(mlp_gain_term, EVERY, scatter_dimension=0, tiled=True),
        lax.psum_scatter(grad_gate, EVERY, scatter_dimension=0, tiled=True),
        lax.psum_scatter(grad_up, EVERY, scatter_dimension=0, tiled=True),
    )
    g_attn, wq_all, wk_all, wv_all, wo_all = (
        lax.all_gather(attn_gain, EVERY, axis=0, tiled=True),
        lax.all_gather(w_query, EVERY, axis=0, tiled=True),
        lax.all_gather(key_weight, EVERY, axis=0, tiled=True),
        lax.all_gather(value_weight, EVERY, axis=0, tiled=True),
        lax.all_gather(w_out, EVERY, axis=0, tiled=True),
    )
    middle_low = grad_middle.astype(jnp.bfloat16)
    grad_out = jnp.einsum(EQ_STE_STD_TO_ED, heads_flat, middle_low, preferred_element_type=jnp.float32)
    grad_heads = (
        jnp.einsum(EQ_STD_ED_TO_STE, middle_low, wo_all, preferred_element_type=jnp.float32)
        .astype(jnp.bfloat16)
        .reshape(sequence_count, token_count, QUERY_HEADS, HEAD_SIZE)
    )
    grad_heads_local = lax.all_to_all(grad_heads, ULY, split_axis=2, concat_axis=1, tiled=True)
    grad_group = jnp.transpose(
        grad_heads_local.reshape(
            sequence_count, block_len, local_key_value, query_group_width, HEAD_SIZE
        ),
        (0, 2, 3, 1, 4),
    )
    delta = jnp.sum(grad_heads_local.astype(jnp.float32) * attention_output, axis=-1)
    delta = jnp.transpose(
        delta.reshape(sequence_count, block_len, local_key_value, query_group_width), (0, 2, 3, 1)
    )
    seq_length = block_len * lax.axis_size(BLK)
    zero_keys = jnp.zeros((sequence_count, seq_length, local_key_value, HEAD_SIZE), jnp.float32)
    back_state = (jnp.zeros(stat_shape + (HEAD_SIZE,), jnp.float32), zero_keys, zero_keys)
    key_piece = lax.all_gather(k_heads, BLK, axis=1, tiled=True)
    value_piece = lax.all_gather(v_heads, BLK, axis=1, tiled=True)
    key_pos = positions_of(jnp.arange(key_piece.shape[1], dtype=jnp.int32), span_order, half_len)
    back_allowed = query_pos[:, None] >= key_pos[None, :]

    def back_one_sequence(members):
        query_rows, grad_rows, lse_seq, delta_seq, key_rows, value_rows, dq_seq, dk_seq, dv_seq = (
            members
        )
        scores = (
            jnp.einsum(EQ_QKGD_NKD_TO_KGQN, query_rows, key_rows, preferred_element_type=jnp.float32)
            * score_scale
        )
        scores = jnp.where(back_allowed, scores, -jnp.inf)
        probs = jnp.exp(scores - lse_seq[..., None])
        grad_values = jnp.einsum(
            EQ_KGQN_KGQD_TO_NKD,
            probs.astype(jnp.bfloat16),
            grad_rows,
            preferred_element_type=jnp.float32,
        )
        grad_probs = jnp.einsum(
            EQ_KGQD_NKD_TO_KGQN, grad_rows, value_rows, preferred_element_type=jnp.float32
        )
        grad_scores = (probs * (grad_probs - delta_seq[..., None])).astype(jnp.bfloat16)
        dq_seq = dq_seq + score_scale * jnp.einsum(
            EQ_KGQN_NKD_TO_KGQD, grad_scores, key_rows, preferred_element_type=jnp.float32
        )
        grad_keys = score_scale * jnp.einsum(
            EQ_KGQN_QKGD_TO_NKD, grad_scores, query_rows, preferred_element_type=jnp.float32
        )
        return (dq_seq, add_rows(dk_seq, grad_keys), add_rows(dv_seq, grad_values))

    grad_q_group, grad_k_whole, grad_v_whole = lax.map(
        back_one_sequence,
        (
            q_group,
            grad_group,
            log_total,
            delta,
            key_piece,
            value_piece,
            back_state[0],
            back_state[1],
            back_state[2],
        ),
    )
    grad_k_block, grad_v_block = (
        lax.psum_scatter(
            grad_k_whole.astype(jnp.bfloat16), BLK, scatter_dimension=1, tiled=True
        ).astype(jnp.float32),
        lax.psum_scatter(
            grad_v_whole.astype(jnp.bfloat16), BLK, scatter_dimension=1, tiled=True
        ).astype(jnp.float32),
    )
    grad_q_block = jnp.transpose(grad_q_group, (0, 3, 1, 2, 4)).reshape(
        sequence_count, block_len, local_q, HEAD_SIZE
    )
    grad_q_seq, grad_k_seq, value_sequence_gradient = (
        lax.all_to_all(
            grad_q_block.astype(jnp.bfloat16), ULY, split_axis=1, concat_axis=2, tiled=True
        ).astype(grad_q_block.dtype),
        lax.all_to_all(
            grad_k_block.astype(jnp.bfloat16), ULY, split_axis=1, concat_axis=2, tiled=True
        ).astype(grad_k_block.dtype),
        lax.all_to_all(
            grad_v_block.astype(jnp.bfloat16), ULY, split_axis=1, concat_axis=2, tiled=True
        ).astype(grad_v_block.dtype),
    )
    grad_q_normed = rotate(grad_q_seq, local_angles, -1.0)
    grad_k_normed = rotate(grad_k_seq, local_angles, -1.0)
    q_gain_term = jnp.sum(grad_q_normed * q_pre * q_scale, axis=(0, 1, 2))
    k_gain_term = jnp.sum(grad_k_normed * key_before_norm * k_scale, axis=(0, 1, 2))
    grad_q_pre = (
        norm_back(grad_q_normed, q_pre, q_scale, gain_q)
        .astype(jnp.bfloat16)
        .reshape(sequence_count, token_count, QUERY_HEADS * HEAD_SIZE)
    )
    grad_k_pre = (
        norm_back(grad_k_normed, key_before_norm, k_scale, gain_k)
        .astype(jnp.bfloat16)
        .reshape(sequence_count, token_count, KEY_VALUE_HEADS * HEAD_SIZE)
    )
    value_pre_gradient = value_sequence_gradient.astype(jnp.bfloat16).reshape(
        sequence_count, token_count, KEY_VALUE_HEADS * HEAD_SIZE
    )
    grad_query = jnp.einsum(
        EQ_STD_STE_TO_DE, normalized_input, grad_q_pre, preferred_element_type=jnp.float32
    )
    grad_key = jnp.einsum(
        EQ_STD_STE_TO_DE, normalized_input, grad_k_pre, preferred_element_type=jnp.float32
    )
    grad_value = jnp.einsum(
        EQ_STD_STE_TO_DE, normalized_input, value_pre_gradient, preferred_element_type=jnp.float32
    )
    grad_normed = jnp.einsum(EQ_STE_DE_TO_STD, grad_q_pre, wq_all, preferred_element_type=jnp.float32)
    grad_normed = grad_normed + jnp.einsum(
        EQ_STE_DE_TO_STD, grad_k_pre, wk_all, preferred_element_type=jnp.float32
    )
    grad_normed = grad_normed + jnp.einsum(
        EQ_STE_DE_TO_STD, value_pre_gradient, wv_all, preferred_element_type=jnp.float32
    )
    attn_gain_term = jnp.sum(grad_normed * source * first_scale, axis=(0, 1))
    grad_hidden = grad_middle + norm_back(
        grad_normed, source, first_scale, g_attn.astype(jnp.float32)
    )
    grad_down = jnp.einsum(EQ_STF_STD_TO_FD, activated, cotangent, preferred_element_type=jnp.float32)
    grad_attn_gain, grad_query, grad_key, grad_value, grad_out, grad_down = (
        lax.psum_scatter(attn_gain_term, EVERY, scatter_dimension=0, tiled=True),
        lax.psum_scatter(grad_query, EVERY, scatter_dimension=0, tiled=True),
        lax.psum_scatter(grad_key, EVERY, scatter_dimension=0, tiled=True),
        lax.psum_scatter(grad_value, EVERY, scatter_dimension=0, tiled=True),
        lax.psum_scatter(grad_out, EVERY, scatter_dimension=0, tiled=True),
        lax.psum_scatter(grad_down, EVERY, scatter_dimension=0, tiled=True),
    )
    grad_q_gain, grad_k_gain = lax.psum((q_gain_term, k_gain_term), EVERY)
    return (
        output,
        grad_hidden,
        grad_attn_gain,
        grad_query,
        grad_key,
        grad_value,
        grad_out,
        grad_q_gain,
        grad_k_gain,
        grad_mlp_gain,
        grad_gate,
        grad_up,
        grad_down,
    )


MESH = pl.DeviceIdType.MESH
HBM = pl.BlockSpec(memory_space=pltpu.HBM)
VMEM = pl.BlockSpec(memory_space=pltpu.VMEM)
MIB = 1 << 20


def kernel_params(collective_id, vmem_mib=48):
    return pltpu.CompilerParams(
        collective_id=collective_id, has_side_effects=True, vmem_limit_bytes=vmem_mib * MIB
    )


def semaphores(count, local=16):
    return [
        pltpu.SemaphoreType.DMA((count,)),
        pltpu.SemaphoreType.DMA((count,)),
        pltpu.SemaphoreType.DMA((local,)),
    ]


class Copy:
    def __init__(self, descriptor, sends, receives):
        self.descriptor, self.sends, self.receives = descriptor, sends, receives

    def under(self, condition, action):
        if condition is None:
            action()
        else:
            pl.when(condition)(action)

    def start(self):
        self.under(self.sends, lambda: self.descriptor().start())
        return self

    def sent(self):
        self.under(self.sends, lambda: self.descriptor().wait_send())

    def arrived(self):
        self.under(self.receives, lambda: self.descriptor().wait_recv())


class Links:
    def __init__(self, send, recv, here):
        self.send, self.recv, self.here = send, recv, here
        self.used, self.used_here = 0, 0
        self.copies, self.local_copies = [], []
        self.n_dp, self.n_blk, self.n_uly = (lax.axis_size(a) for a in EVERY)
        self.dp, self.blk, self.uly = (lax.axis_index(a) for a in EVERY)
        self.other_dp = 1 - self.dp
        self.across = lax.rem(self.uly + 2, 4)
        self.twin = self.uly + 1 - 2 * lax.rem(self.uly, 2)
        self.x_way = (self.other_dp, self.blk, self.uly)
        self.y_way = (self.dp, self.blk, self.across)
        self.core_way = (self.dp, self.blk, self.twin)

    def peer(self, step):
        return lax.rem(self.blk + step, self.n_blk)

    def peers(self):
        return [(self.dp, self.peer(k), self.uly) for k in range(1, self.n_blk)]

    def greet(self, devices):
        barrier = pltpu.get_barrier_semaphore()
        for device in devices:
            pl.semaphore_signal(barrier, inc=1, device_id=device, device_id_type=MESH)
        pl.semaphore_wait(barrier, len(devices))

    def remote(self, source, target, device, sends=None, receives=None):
        slot = self.used
        self.used += 1

        def descriptor():
            return pltpu.make_async_remote_copy(
                src_ref=source(),
                dst_ref=target(),
                send_sem=self.send.at[slot],
                recv_sem=self.recv.at[slot],
                device_id=device,
                device_id_type=MESH,
            )

        copy = Copy(descriptor, sends, receives)
        self.copies.append(copy)
        return copy.start()

    def to(self, source, target, device):
        return self.remote(lambda: source, lambda: target, device)

    def local(self, source, target):
        copy = pltpu.make_async_copy(source, target, self.here.at[self.used_here])
        self.used_here += 1
        copy.start()
        self.local_copies.append(copy)
        return copy

    def finish(self):
        for copy in self.copies:
            copy.sent()


class LineGather:
    def __init__(self, links, own, whole):
        self.links, self.own, self.whole = links, own, whole
        self.waiting = []

    def send(self, step):
        links, whole = self.links, self.whole
        blk, last = links.blk, links.n_blk - 1

        def block(index):
            if step == 0:
                return lambda: self.own
            return lambda: whole.at[index]

        self.waiting = [
            links.remote(
                block(blk - step),
                lambda: whole.at[blk - step],
                (links.dp, blk + 1, links.uly),
                jnp.logical_and(blk >= step, blk < last),
                blk >= step + 1,
            ),
            links.remote(
                block(blk + step),
                lambda: whole.at[blk + step],
                (links.dp, blk - 1, links.uly),
                jnp.logical_and(blk + step <= last, blk > 0),
                blk + step + 1 <= last,
            ),
        ]

    def arrived(self):
        for copy in self.waiting:
            copy.arrived()


class PlaneGather:
    def __init__(self, links, at):
        self.links, self.at = links, at

    def start(self, own=None):
        links, at = self.links, self.at
        mine = at(links.dp, links.uly)
        own = mine if own is None else own
        self.from_x = links.to(own, mine, links.x_way)
        self.from_y = links.to(own, mine, links.y_way)
        self.from_core = [links.to(own, mine, links.core_way)]

    def hand_on(self):
        links, at = self.links, self.at
        self.from_x.arrived()
        half = at(links.other_dp, links.uly, 0)
        self.second_y = links.to(half, half, links.y_way)
        self.from_y.arrived()
        half = at(links.dp, links.across, 1)
        self.second_x = links.to(half, half, links.x_way)
        for chunk in (at(links.other_dp, links.uly), at(links.dp, links.across)):
            self.from_core.append(links.to(chunk, chunk, links.core_way))

    def last(self):
        links = self.links
        self.second_y.arrived()
        self.second_x.arrived()
        chunk = self.at(links.other_dp, links.across)
        self.from_core.append(links.to(chunk, chunk, links.core_way))

    def arrived(self):
        for copy in self.from_core:
            copy.arrived()


def rows_of(whole, blocked):
    def at(dp, uly, half=None):
        part = whole.at[dp, :, uly] if blocked else whole.at[dp, uly]
        if half is None:
            return part
        depth = whole.shape[-2] // 2
        rows = pl.ds(half * depth, depth)
        return part.at[:, rows] if blocked else part.at[rows]

    return at


class ColumnSwap:
    def __init__(self, links, pieces):
        self.links, self.pieces = links, pieces
        self.incoming, self.kept = [], []

    def parts(self, blk):
        links = self.links
        for weight, whole, offset in self.pieces:
            width = weight.shape[-1] // links.n_dp // links.n_blk
            for group in range(links.n_dp):
                start = (group * links.n_blk + blk) * width
                yield (
                    weight.at[:, pl.ds(pl.multiple_of(start, 128), width)],
                    whole.at[links.blk, :, pl.ds(offset + group * width, width)],
                )

    def start(self):
        links = self.links
        for step in range(1, links.n_blk):
            device = (links.dp, links.peer(step), links.uly)
            for source, target in self.parts(links.peer(step)):
                self.incoming.append(links.to(source, target, device))
        for source, target in self.parts(links.blk):
            self.kept.append(links.local(source, target))

    def arrived(self):
        for copy in self.kept:
            copy.wait()
        for copy in self.incoming:
            copy.arrived()


def front_kernel(
    hidden,
    wq,
    wk,
    wv,
    wo,
    wd,
    gains,
    cotangent,
    all_hidden,
    w_qkv,
    all_wo,
    all_wd,
    all_gains,
    all_cot,
    send,
    recv,
    here,
):
    links = Links(send, recv, here)
    links.greet(links.peers() + [links.x_way, links.y_way, links.core_way])
    q_width, k_width = wq.shape[1] // links.n_blk, wk.shape[1] // links.n_blk
    chunk = w_qkv.at[links.dp, :, links.uly]
    swap = ColumnSwap(
        links, [(wq, chunk, 0), (wk, chunk, q_width), (wv, chunk, q_width + k_width)]
    )
    plane_wo = PlaneGather(links, rows_of(all_wo, False))
    plane_wd = PlaneGather(links, rows_of(all_wd, False))
    plane_qkv = PlaneGather(links, rows_of(w_qkv, True))
    plane_gain = PlaneGather(links, rows_of(all_gains, True))
    swap.start()
    my_gains = all_gains.at[links.dp, links.blk, links.uly]
    gain_swap = [links.to(gains, my_gains, device) for device in links.peers()]
    plane_wo.start(wo)
    plane_wd.start(wd)
    keep = [
        links.local(gains, my_gains),
        links.local(hidden, all_hidden.at[links.blk]),
        links.local(cotangent, all_cot.at[links.blk]),
        links.local(wo, all_wo.at[links.dp, links.uly]),
        links.local(wd, all_wd.at[links.dp, links.uly]),
    ]
    swap.arrived()
    line = LineGather(links, hidden, all_hidden)
    line.send(0)
    plane_qkv.start()
    keep[0].wait()
    for copy in gain_swap:
        copy.arrived()
    plane_gain.start()
    plane_wo.hand_on()
    line.arrived()
    line.send(1)
    plane_wd.hand_on()
    plane_qkv.hand_on()
    plane_gain.hand_on()
    plane_wo.last()
    for step in range(2, links.n_blk - 1):
        line.arrived()
        line.send(step)
    cot_line = LineGather(links, cotangent, all_cot)
    cot_line.send(0)
    plane_wd.last()
    plane_qkv.last()
    plane_gain.last()
    line.arrived()
    cot_line.arrived()
    for plane in (plane_wo, plane_qkv, plane_gain, plane_wd):
        plane.arrived()
    for copy in keep[1:]:
        copy.wait()
    links.finish()


def gather_front(hidden, wq, wk, wv, wo, wd, gains, cotangent):
    n_dp, n_blk, n_uly = (lax.axis_size(a) for a in EVERY)
    qkv_width = (wq.shape[1] + wk.shape[1] + wv.shape[1]) // n_blk
    shapes = [
        (n_blk,) + hidden.shape,
        (n_dp, n_blk, n_uly, wq.shape[0], qkv_width),
        (n_dp, n_uly) + wo.shape,
        (n_dp, n_uly) + wd.shape,
        (n_dp, n_blk, n_uly) + gains.shape,
        (n_blk,) + cotangent.shape,
    ]
    return pl.pallas_call(
        front_kernel,
        out_shape=[jax.ShapeDtypeStruct(s, jnp.bfloat16) for s in shapes],
        in_specs=[HBM] * 8,
        out_specs=[HBM] * 6,
        scratch_shapes=semaphores(72),
        compiler_params=kernel_params(0, 62),
    )(hidden, wq, wk, wv, wo, wd, gains, cotangent)


ROWS = 32


def each_block(count, body):
    def step(index, carry):
        body(pl.ds(pl.multiple_of(index * ROWS, ROWS), ROWS))
        return carry

    lax.fori_loop(0, count // ROWS, step, 0)


class LineScatter:
    def __init__(self, links, parts, rightward, leftward):
        self.links, self.parts = links, parts
        self.slots = {1: rightward, -1: leftward}
        self.tokens = parts.shape[1]
        self.number = links.used
        self.last = links.n_blk - 1
        links.used += 2 * self.last

    def target(self, step, way):
        return self.last - step if way == 1 else step

    def slot(self, step, way):
        target = self.target(step, way)
        return self.slots[way].at[target - 1 if way == 1 else target]

    def place(self, way):
        return self.links.blk if way == 1 else self.last - self.links.blk

    def copy(self, step, way, source=None):
        links, slot = self.links, self.slot(step, way)
        number = self.number + 2 * step + (1 if way == 1 else 0)
        return pltpu.make_async_remote_copy(
            src_ref=slot if source is None else source,
            dst_ref=slot,
            send_sem=links.send.at[number],
            recv_sem=links.recv.at[number],
            device_id=(links.dp, links.blk + way, links.uly),
            device_id_type=MESH,
        )

    def start(self):
        for step in range(self.last):
            for way in (1, -1):

                @pl.when(self.place(way) == 0)
                def _(step=step, way=way):
                    self.copy(step, way, self.parts.at[self.target(step, way)]).start()

    def tick(self, tick):
        for way in (1, -1):

            @pl.when(jnp.logical_and(self.place(way) >= 1, self.place(way) <= tick))
            def _(way=way):
                step = tick - self.place(way)
                self.copy(step, way).wait_recv()
                slot, target = self.slot(step, way), self.target(step, way)

                def body(rows):
                    slot[rows, :] = slot[rows, :] + self.parts[target, rows, :]

                each_block(self.tokens, body)
                self.copy(step, way).start()

    def finish(self, total):
        blk, last = self.links.blk, self.last

        def start(rows):
            total[rows, :] = self.parts[blk, rows, :].astype(jnp.float32)

        each_block(self.tokens, start)
        for way in (1, -1):

            @pl.when(self.place(way) >= 1)
            def _(way=way):
                step = last - self.place(way)
                self.copy(step, way).wait_recv()
                slot = self.slot(step, way)

                def body(rows):
                    total[rows, :] = total[rows, :] + slot[rows, :].astype(jnp.float32)

                each_block(self.tokens, body)

    def sent(self):
        for step in range(self.last):
            for way in (1, -1):
                beyond = self.place(way) + step < self.last
                pl.when(beyond)(lambda step=step, way=way: self.copy(step, way).wait_send())


def line_scratch(n_blk, tokens, width):
    return [pltpu.VMEM((n_blk - 1, tokens, width), jnp.bfloat16)] * 2


class PlaneScatter:
    def __init__(self, links, parts, from_core, from_x, from_y, last_x, last_y):
        self.links, self.parts = links, parts
        self.from_core, self.from_x, self.from_y = from_core, from_x, from_y
        self.last_x, self.last_y = last_x, last_y
        self.core = lax.rem(links.uly, 2)
        self.row = lax.div(links.uly, 2)
        self.depth = parts.shape[3]
        self.core_copies = {}

    def chunk(self, dp, row, core, half=None):
        uly = row * 2 + core
        if half is None:
            return self.parts.at[dp, :, uly]
        depth = self.depth // 2
        return self.parts.at[dp, :, uly, pl.ds(half * depth, depth)]

    def add(self, target, source):
        blocks, depth, _ = target.shape
        rows = 32 if depth % 32 == 0 else 16

        def body(index, carry):
            block = lax.div(index, depth // rows)
            at = pl.ds(pl.multiple_of(lax.rem(index, depth // rows) * rows, rows), rows)
            target[block, at, :] = target[block, at, :] + source[block, at, :]
            return carry

        lax.fori_loop(0, blocks * (depth // rows), body, 0)

    def between_cores(self, which):
        links = self.links
        dp = links.dp if which == 1 else links.other_dp
        self.core_copies[which] = [
            links.to(
                self.chunk(dp, row, 1 - self.core), self.from_core.at[which, row], links.core_way
            )
            for row in range(2)
        ]

    def across_chips(self):
        links = self.links
        self.x_copies, self.y_copies = [], []
        for which, dp in ((0, links.other_dp), (1, links.dp)):
            for row in range(2):
                self.core_copies[which][row].arrived()
                self.add(self.chunk(dp, row, self.core), self.from_core.at[which, row])
            if which == 0:
                for row in range(2):
                    self.x_copies.append(
                        links.to(
                            self.chunk(dp, row, self.core, 0), self.from_x.at[row], links.x_way
                        )
                    )
        for group in range(links.n_dp):
            self.y_copies.append(
                links.to(
                    self.chunk(group, 1 - self.row, self.core, 1),
                    self.from_y.at[group],
                    links.y_way,
                )
            )

    def second_way(self):
        links = self.links
        for row in range(2):
            self.x_copies[row].arrived()
            self.add(self.chunk(links.dp, row, self.core, 0), self.from_x.at[row])
        self.y_last = links.to(
            self.chunk(links.dp, 1 - self.row, self.core, 0), self.last_y, links.y_way
        )
        for group in range(links.n_dp):
            self.y_copies[group].arrived()
            self.add(self.chunk(group, self.row, self.core, 1), self.from_y.at[group])
        self.x_last = links.to(
            self.chunk(links.other_dp, self.row, self.core, 1), self.last_x, links.x_way
        )

    def result(self, write):
        links = self.links
        for half, copy, source in ((0, self.y_last, self.last_y), (1, self.x_last, self.last_x)):
            copy.arrived()
            own = self.chunk(links.dp, self.row, self.core, half)
            blocks, depth, _ = source.shape
            rows = 32 if depth % 32 == 0 else 16

            def body(index, carry, own=own, source=source, half=half, depth=depth, rows=rows):
                block = lax.div(index, depth // rows)
                start = pl.multiple_of(lax.rem(index, depth // rows) * rows, rows)
                at = pl.ds(start, rows)
                value = own[block, at, :].astype(jnp.float32)
                value = value + source[block, at, :].astype(jnp.float32)
                write(block, pl.ds(pl.multiple_of(start + half * depth, rows), rows), value)
                return carry

            lax.fori_loop(0, blocks * (depth // rows), body, 0)


def plane_scratch(n_dp, blocks, n_uly, depth, width):
    shapes = [
        (n_dp, blocks, n_uly, depth, width),
        (n_dp, 2, blocks, depth, width),
        (2, blocks, depth // 2, width),
        (n_dp, blocks, depth // 2, width),
        (blocks, depth // 2, width),
        (blocks, depth // 2, width),
    ]
    return [pltpu.VMEM(shape, jnp.bfloat16) for shape in shapes]


def weight_grad(left, right, parts, dp, together):
    _, blocks, n_uly, depth, width = parts.shape
    steps = n_uly // together
    columns = 512

    def body(index, carry):
        block, step = lax.div(index, steps), lax.rem(index, steps)
        start = ((dp * blocks + block) * n_uly + step * together) * depth
        rows = left[:, pl.ds(pl.multiple_of(start, 128), together * depth)].T
        for column in range(0, width, columns):
            part = jnp.dot(
                rows, right[:, column : column + columns], preferred_element_type=jnp.float32
            )
            parts[dp, block, pl.ds(step * together, together), :, column : column + columns] = (
                part.astype(jnp.bfloat16).reshape(together, depth, columns)
            )
        return carry

    lax.fori_loop(0, blocks * steps, body, 0)


def turned(rows, cosine, sine):
    return rows * cosine + pltpu.roll(rows, HEAD_SIZE // 2, axis=1) * sine


def transposed_product(left, right):
    return lax.dot_general(
        left, right, (((0,), (0,)), ((), ())), preferred_element_type=jnp.float32
    )


def product_right(left, right):
    return lax.dot_general(
        left, right, (((1,), (1,)), ((), ())), preferred_element_type=jnp.float32
    )


SCORE_SCALE = 1.0 / math.sqrt(HEAD_SIZE)


def mask_scores(bias, query_pos, key_pos):
    size = bias.shape[0] // 4

    def body(index, carry):
        rows = pl.ds(pl.multiple_of(index * size, size), size)
        bias[rows, :] = jnp.where(query_pos[...] >= key_pos[rows, :], 0.0, -1e30)
        return carry

    lax.fori_loop(0, 4, body, 0)


class RowBlocks:
    def __init__(self, n_blk, seqs, toks):
        self.n_blk, self.seqs, self.toks = n_blk, seqs, toks

    def each(self, body):
        def step(index, carry):
            blk, seq = lax.div(index, self.seqs), lax.rem(index, self.seqs)
            body(
                seq,
                pl.ds(pl.multiple_of(index * self.toks, self.toks), self.toks),
                pl.multiple_of(blk * self.toks, self.toks),
            )
            return carry

        lax.fori_loop(0, self.n_blk * self.seqs, step, 0)


def attention_kernel(
    wg,
    wu,
    _,
    hidden,
    w_qkv,
    gain,
    q_gain,
    k_gain,
    cosine,
    sine,
    query_pos,
    key_pos,
    rows_wg,
    rows_wu,
    all_cot,
    heads,
    normed,
    qkv,
    queries,
    key_values,
    lse,
    bias,
    send,
    recv,
    here,
):
    links = Links(send, recv, here)
    links.greet(links.peers() + [links.y_way, links.core_way])
    swap = ColumnSwap(links, [(wg, rows_wg, 0), (wu, rows_wu, 0)])
    swap.start()
    line = LineGather(links, None, all_cot)
    line.send(1)

    def norm(rows):
        source = hidden[rows, :].astype(jnp.float32)
        normed[rows, :] = (source * rms_scale(source) * gain[...]).astype(jnp.bfloat16)

    each_block(hidden.shape[0], norm)
    for column in range(0, qkv.shape[1], 256):
        qkv[:, column : column + 256] = jnp.dot(
            normed[...], w_qkv[:, column : column + 256], preferred_element_type=jnp.float32
        )
    seqs, kv_heads, q_rows, _ = queries.shape
    q_len = key_values.shape[4]
    group = q_rows // q_len
    blocks = RowBlocks(links.n_blk, seqs, q_len // links.n_blk)
    q_end = kv_heads * group * HEAD_SIZE
    k_end = q_end + kv_heads * HEAD_SIZE

    def place_keys(seq, rows, start):
        at = pl.ds(start, blocks.toks)
        for head in range(kv_heads):
            k_pre = qkv[rows, q_end + head * HEAD_SIZE : q_end + (head + 1) * HEAD_SIZE]
            k_row = turned(k_pre * rms_scale(k_pre) * k_gain[...], cosine[at, :], sine[at, :])
            v_row = qkv[rows, k_end + head * HEAD_SIZE : k_end + (head + 1) * HEAD_SIZE]
            key_values[links.uly, 0, seq, head, at, :] = k_row.astype(jnp.bfloat16)
            key_values[links.uly, 1, seq, head, at, :] = v_row.astype(jnp.bfloat16)

    blocks.each(place_keys)
    mine = key_values.at[links.uly]
    kv_core = links.to(mine, mine, links.core_way)
    kv_across = links.to(mine, mine, links.y_way)

    def place_queries(seq, rows, start):
        at = pl.ds(start, blocks.toks)
        for head in range(kv_heads * group):
            q_pre = qkv[rows, head * HEAD_SIZE : (head + 1) * HEAD_SIZE]
            q_row = turned(q_pre * rms_scale(q_pre) * q_gain[...], cosine[at, :], sine[at, :])
            to = pl.ds((head % group) * q_len + start, blocks.toks)
            queries[seq, head // group, to, :] = q_row.astype(jnp.bfloat16)

    blocks.each(place_queries)
    mask_scores(bias, query_pos, key_pos)
    kv_across.arrived()
    theirs = key_values.at[links.across]
    kv_last = links.to(theirs, theirs, links.core_way)
    kv_core.arrived()
    kv_last.arrived()

    def attend(seq, head):
        def over_keys(piece, carry):
            total, mixed = carry
            rows = pl.ds(pl.multiple_of(piece * q_len, q_len), q_len)
            scores = product_right(key_values[piece, 0, seq, head], queries[seq, head])
            weights = jnp.exp(scores * SCORE_SCALE + bias[rows, :])
            total = total + jnp.sum(weights, axis=0, keepdims=True)
            mixed = mixed + transposed_product(
                key_values[piece, 1, seq, head], weights.astype(jnp.bfloat16)
            )
            return total, mixed

        total, mixed = lax.fori_loop(
            0,
            links.n_uly,
            over_keys,
            (
                jnp.zeros((1, q_rows), jnp.float32),
                jnp.zeros((HEAD_SIZE, q_rows), jnp.float32),
            ),
        )
        lse[seq * kv_heads + head] = jnp.log(total)
        attended = (mixed / total).T.astype(jnp.bfloat16)
        for member in range(group):
            column = (head * group + member) * HEAD_SIZE
            for blk in range(links.n_blk):
                row = (blk * seqs + seq) * blocks.toks
                start = member * q_len + blk * blocks.toks
                heads[row : row + blocks.toks, column : column + HEAD_SIZE] = attended[
                    start : start + blocks.toks, :
                ]

    for seq in range(seqs):
        for head in range(kv_heads):
            attend(seq, head)
    swap.arrived()
    line.arrived()
    links.finish()


def attend_forward(
    wg, wu, all_cot, hidden, w_qkv, gain, q_gain, k_gain, cosine, sine, query_pos, key_pos, seqs
):
    _, n_blk, n_uly = (lax.axis_size(a) for a in EVERY)
    rows = hidden.shape[0]
    kv_heads = KEY_VALUE_HEADS // n_blk
    q_len, q_rows = rows // seqs, query_pos.shape[1]
    low = [
        (n_blk, wg.shape[0], wg.shape[1] // n_blk),
        (n_blk, wu.shape[0], wu.shape[1] // n_blk),
        all_cot.shape,
        (rows, QUERY_HEADS // n_blk * HEAD_SIZE),
        hidden.shape,
    ]
    shapes = [jax.ShapeDtypeStruct(s, jnp.bfloat16) for s in low] + [
        jax.ShapeDtypeStruct((rows, w_qkv.shape[1]), jnp.float32),
        jax.ShapeDtypeStruct((seqs, kv_heads, q_rows, HEAD_SIZE), jnp.bfloat16),
        jax.ShapeDtypeStruct((n_uly, 2, seqs, kv_heads, q_len, HEAD_SIZE), jnp.bfloat16),
        jax.ShapeDtypeStruct((seqs * kv_heads, 1, q_rows), jnp.float32),
    ]
    return pl.pallas_call(
        attention_kernel,
        out_shape=shapes,
        in_specs=[HBM] * 3 + [VMEM] * 9,
        out_specs=[HBM] * 3 + [VMEM] * 6,
        input_output_aliases={2: 2},
        scratch_shapes=[pltpu.VMEM((key_pos.shape[0], q_rows), jnp.float32)] + semaphores(32),
        compiler_params=kernel_params(1, 60),
    )(
        wg,
        wu,
        all_cot,
        hidden,
        w_qkv,
        gain,
        q_gain,
        k_gain,
        cosine,
        sine,
        query_pos,
        key_pos,
    )


def attention_back_kernel(
    all_low,
    wo,
    queries,
    key_values,
    lse,
    qkv,
    q_gain,
    k_gain,
    cosine,
    sine,
    query_pos,
    key_pos,
    grad_gate,
    grad_up,
    grad_qkv,
    gain_terms,
    gate_rows,
    up_rows,
    bias,
    grad_heads,
    grad_rows,
    probs,
    grad_probs,
    grad_kv,
    from_core,
    from_across,
    send,
    recv,
    here,
):
    links = Links(send, recv, here)
    links.greet(links.peers() + [links.y_way, links.core_way])
    swapped, keep = [], []
    for source, target in ((grad_gate, gate_rows), (grad_up, up_rows)):
        for step in range(1, links.n_blk):
            peer = links.peer(step)
            swapped.append(
                links.to(source.at[peer], target.at[links.blk], (links.dp, peer, links.uly))
            )
        keep.append(links.local(source.at[links.blk], target.at[links.blk]))
    grad_heads[...] = product_right(all_low[...], wo[...])
    mask_scores(bias, query_pos, key_pos)
    seqs, kv_heads, q_rows, _ = queries.shape
    q_len = key_values.shape[4]
    group = q_rows // q_len
    blocks = RowBlocks(links.n_blk, seqs, q_len // links.n_blk)
    q_end = kv_heads * group * HEAD_SIZE
    k_end = q_end + kv_heads * HEAD_SIZE
    gain_terms[...] = jnp.zeros_like(gain_terms)

    def gather_rows(seq, rows, start):
        for head in range(kv_heads * group):
            to = pl.ds((head % group) * q_len + start, blocks.toks)
            grad_rows[seq, head // group, to, :] = grad_heads[
                rows, head * HEAD_SIZE : (head + 1) * HEAD_SIZE
            ].astype(jnp.bfloat16)

    blocks.each(gather_rows)

    def back_norm(upstream, pre, gain, at, which):
        upstream = turned(upstream, cosine[at, :], -sine[at, :])
        back, term = back_rows(upstream, pre, gain[...])
        gain_terms[which : which + 1, :] += term
        return back.astype(jnp.bfloat16)

    def back(seq, head):
        def first(piece, delta):
            rows = pl.ds(pl.multiple_of(piece * q_len, q_len), q_len)
            scores = product_right(key_values[piece, 0, seq, head], queries[seq, head])
            prob = jnp.exp(
                scores * SCORE_SCALE + bias[rows, :] - lse[seq * kv_heads + head]
            )
            grad_prob = product_right(key_values[piece, 1, seq, head], grad_rows[seq, head])
            probs[rows, :] = prob
            grad_probs[rows, :] = grad_prob
            return delta + jnp.sum(prob * grad_prob, axis=0, keepdims=True)

        delta = lax.fori_loop(0, links.n_uly, first, jnp.zeros((1, q_rows), jnp.float32))

        def second(piece, grad_query):
            rows = pl.ds(pl.multiple_of(piece * q_len, q_len), q_len)
            prob = probs[rows, :]
            grad_score = (prob * (grad_probs[rows, :] - delta)).astype(jnp.bfloat16)
            grad_kv[seq, piece, 0, head] = (
                SCORE_SCALE
                * jnp.dot(grad_score, queries[seq, head], preferred_element_type=jnp.float32)
            ).astype(jnp.bfloat16)
            grad_kv[seq, piece, 1, head] = jnp.dot(
                prob.astype(jnp.bfloat16),
                grad_rows[seq, head],
                preferred_element_type=jnp.float32,
            ).astype(jnp.bfloat16)
            return grad_query + transposed_product(key_values[piece, 0, seq, head], grad_score)

        grad_query = lax.fori_loop(
            0, links.n_uly, second, jnp.zeros((HEAD_SIZE, q_rows), jnp.float32)
        )
        grad_heads[:, :HEAD_SIZE] = (grad_query * SCORE_SCALE).T
        for member in range(group):
            column = (head * group + member) * HEAD_SIZE
            for blk in range(links.n_blk):
                row = (blk * seqs + seq) * blocks.toks
                at = pl.ds(blk * blocks.toks, blocks.toks)
                start = member * q_len + blk * blocks.toks
                grad_qkv[row : row + blocks.toks, column : column + HEAD_SIZE] = back_norm(
                    grad_heads[start : start + blocks.toks, :HEAD_SIZE],
                    qkv[row : row + blocks.toks, column : column + HEAD_SIZE],
                    q_gain,
                    at,
                    0,
                )

    core, line = lax.rem(links.uly, 2), lax.div(links.uly, 2)

    def add(target, source):
        for kind in range(2):
            for head in range(kv_heads):
                target[kind, head] = target[kind, head] + source[kind, head]

    def core_sums(seq):
        copies = [
            links.to(
                grad_kv.at[seq, row * 2 + 1 - core], from_core.at[seq, row], links.core_way
            )
            for row in range(2)
        ]
        return copies

    def across_sums(seq, copies):
        for row in range(2):
            copies[row].arrived()
            add(grad_kv.at[seq, row * 2 + core], from_core.at[seq, row])
        return links.to(
            grad_kv.at[seq, (1 - line) * 2 + core], from_across.at[seq], links.y_way
        )

    def own_keys(seq, copy):
        copy.arrived()
        for head in range(kv_heads):
            for blk in range(links.n_blk):
                row = (blk * seqs + seq) * blocks.toks
                at = pl.ds(blk * blocks.toks, blocks.toks)
                term = [
                    grad_kv[seq, links.uly, kind, head, at, :].astype(jnp.float32)
                    + from_across[seq, kind, head, at, :].astype(jnp.float32)
                    for kind in range(2)
                ]
                k_at = q_end + head * HEAD_SIZE
                v_at = k_end + head * HEAD_SIZE
                grad_qkv[row : row + blocks.toks, k_at : k_at + HEAD_SIZE] = back_norm(
                    term[0],
                    qkv[row : row + blocks.toks, k_at : k_at + HEAD_SIZE],
                    k_gain,
                    at,
                    1,
                )
                grad_qkv[row : row + blocks.toks, v_at : v_at + HEAD_SIZE] = term[1].astype(
                    jnp.bfloat16
                )

    stage, last = None, []
    for seq in range(seqs):
        for head in range(kv_heads):
            back(seq, head)
            if stage is not None:
                last.append((seq - 1, across_sums(seq - 1, stage)))
                stage = None
        stage = core_sums(seq)
    last.append((seqs - 1, across_sums(seqs - 1, stage)))
    for seq, copy in last:
        own_keys(seq, copy)
    for copy in keep:
        copy.wait()
    for copy in swapped:
        copy.arrived()
    links.finish()


def attend_back(
    all_low,
    wo,
    queries,
    key_values,
    lse,
    qkv,
    q_gain,
    k_gain,
    cosine,
    sine,
    query_pos,
    key_pos,
    grad_gate,
    grad_up,
):
    seqs, kv_heads, q_rows, _ = queries.shape
    n_uly, _, _, _, q_len, _ = key_values.shape
    rows = all_low.shape[0]
    keys = key_pos.shape[0]
    f32, low = jnp.float32, jnp.bfloat16
    scratch = [
        ((keys, q_rows), f32),
        ((rows, wo.shape[0]), f32),
        (queries.shape, low),
        ((keys, q_rows), f32),
        ((keys, q_rows), f32),
        ((seqs, n_uly, 2, kv_heads, q_len, HEAD_SIZE), low),
        ((seqs, 2, 2, kv_heads, q_len, HEAD_SIZE), low),
        ((seqs, 2, kv_heads, q_len, HEAD_SIZE), low),
    ]
    return pl.pallas_call(
        attention_back_kernel,
        out_shape=[
            jax.ShapeDtypeStruct(qkv.shape, low),
            jax.ShapeDtypeStruct((8, HEAD_SIZE), f32),
            jax.ShapeDtypeStruct(grad_gate.shape, low),
            jax.ShapeDtypeStruct(grad_up.shape, low),
        ],
        in_specs=[VMEM] * 12 + [HBM] * 2,
        out_specs=[VMEM] * 2 + [HBM] * 2,
        scratch_shapes=[pltpu.VMEM(shape, kind) for shape, kind in scratch] + semaphores(24),
        compiler_params=kernel_params(5),
    )(
        all_low,
        wo,
        queries,
        key_values,
        lse,
        qkv,
        q_gain,
        k_gain,
        cosine,
        sine,
        query_pos,
        key_pos,
        grad_gate,
        grad_up,
    )


def middle_kernel(
    heads,
    wo,
    source,
    gain,
    rows_wg,
    rows_wu,
    _,
    middle,
    all_normed,
    all_wg,
    all_wu,
    all_cot,
    parts,
    rightward,
    leftward,
    normed,
    send,
    recv,
    here,
):
    links = Links(send, recv, here)
    links.greet(links.peers() + [links.x_way, links.y_way, links.core_way])
    planes, keep = [], []
    for chunk, whole in ((rows_wg, all_wg), (rows_wu, all_wu)):
        at = rows_of(whole, True)
        plane = PlaneGather(links, at)
        plane.start(chunk)
        planes.append(plane)
        keep.append(links.local(chunk, at(links.dp, links.uly)))
    tokens = source.shape[0]
    for blk in (links.n_blk - 1, 0) + tuple(range(1, links.n_blk - 1)):
        parts[blk] = jnp.dot(heads[blk], wo[...], preferred_element_type=jnp.float32).astype(
            jnp.bfloat16
        )
    scatter = LineScatter(links, parts, rightward, leftward)
    scatter.start()
    cot_line = LineGather(links, None, all_cot)
    for step in range(2, links.n_blk - 1):
        cot_line.send(step)
    for tick in range(1, links.n_blk - 1):
        scatter.tick(tick)
        if tick == 1:
            planes[0].hand_on()
    scatter.finish(middle)
    cot_line.arrived()

    def body(rows):
        total = middle[rows, :] + source[rows, :].astype(jnp.float32)
        middle[rows, :] = total
        normed[rows, :] = (total * rms_scale(total) * gain[...]).astype(jnp.bfloat16)

    each_block(tokens, body)
    keep.append(links.local(normed, all_normed.at[links.blk]))
    line = LineGather(links, normed, all_normed)
    for step in range(links.n_blk - 1):
        line.send(step)
        if step == 0:
            planes[1].hand_on()
        if step == 1:
            planes[0].last()
        line.arrived()
    planes[1].last()
    for plane in planes:
        plane.arrived()
    for copy in keep:
        copy.wait()
    scatter.sent()
    links.finish()


def exchange_middle(heads, wo, source, gain, rows_wg, rows_wu, all_cot):
    n_dp, n_blk, n_uly = (lax.axis_size(a) for a in EVERY)
    tokens, width = source.shape
    low = [(n_blk, tokens, width)]
    low += [(n_dp, n_blk, n_uly) + chunk.shape[1:] for chunk in (rows_wg, rows_wu)]
    low.append(all_cot.shape)
    return pl.pallas_call(
        middle_kernel,
        out_shape=[jax.ShapeDtypeStruct((tokens, width), jnp.float32)]
        + [jax.ShapeDtypeStruct(shape, jnp.bfloat16) for shape in low],
        in_specs=[VMEM] * 4 + [HBM] * 3,
        out_specs=[VMEM] + [HBM] * 4,
        input_output_aliases={6: 4},
        scratch_shapes=[pltpu.VMEM((n_blk, tokens, width), jnp.bfloat16)]
        + line_scratch(n_blk, tokens, width)
        + [pltpu.VMEM((tokens, width), jnp.bfloat16)]
        + semaphores(48),
        compiler_params=kernel_params(2, 60),
    )(heads, wo, source, gain, rows_wg, rows_wu, all_cot)


def back_rows(grad_normed, source, gain):
    scale = rms_scale(source)
    unit = source * scale
    scaled = grad_normed * gain
    back = scale * (scaled - unit * jnp.mean(scaled * unit, axis=-1, keepdims=True))
    return back, jnp.sum(grad_normed * unit, axis=0, keepdims=True)


def back_kernel(
    grad_parts,
    out_parts,
    middle,
    cotangent,
    gain,
    all_normed,
    grad_gate_pre,
    grad_up_pre,
    activated,
    all_cot,
    output,
    grad_middle,
    gain_term,
    all_low,
    grad_gate,
    grad_up,
    grad_down,
    rightward,
    leftward,
    out_right,
    out_left,
    out_total,
    low,
    gate_1,
    gate_2,
    gate_3,
    gate_4,
    gate_5,
    gate_6,
    up_1,
    up_2,
    up_3,
    up_4,
    up_5,
    up_6,
    down_1,
    down_2,
    down_3,
    down_4,
    down_5,
    down_6,
    send,
    recv,
    here,
):
    links = Links(send, recv, here)
    links.greet(links.peers() + [links.x_way, links.y_way, links.core_way])
    scatter = LineScatter(links, grad_parts, rightward, leftward)
    scatter.start()
    out_scatter = LineScatter(links, out_parts, out_right, out_left)
    gate = PlaneScatter(links, gate_1, gate_2, gate_3, gate_4, gate_5, gate_6)
    up = PlaneScatter(links, up_1, up_2, up_3, up_4, up_5, up_6)
    down = PlaneScatter(links, down_1, down_2, down_3, down_4, down_5, down_6)

    def compute(scatter, left, right, parts, together):
        for which, dp in ((0, links.other_dp), (1, links.dp)):
            weight_grad(left, right, parts, dp, together)
            scatter.between_cores(which)

    compute(gate, all_normed, grad_gate_pre, gate_1, 4)
    scatter.tick(1)
    gate.across_chips()
    compute(up, all_normed, grad_up_pre, up_1, 4)
    for tick in range(2, links.n_blk - 1):
        scatter.tick(tick)
    up.across_chips()
    compute(down, activated, all_cot, down_1, 2)
    scatter.finish(grad_middle)
    gain_term[...] = jnp.zeros_like(gain_term)

    def body(rows):
        back, term = back_rows(grad_middle[rows, :], middle[rows, :], gain[...])
        grad = cotangent[rows, :].astype(jnp.float32) + back
        gain_term[...] += term
        grad_middle[rows, :] = grad
        low[rows, :] = grad.astype(jnp.bfloat16)

    each_block(middle.shape[0], body)
    keep = links.local(low, all_low.at[links.blk])
    line = LineGather(links, low, all_low)
    line.send(0)
    out_scatter.start()
    down.across_chips()
    gate.second_way()
    line.arrived()
    line.send(1)
    up.second_way()
    line.arrived()
    out_scatter.tick(1)
    for step in range(2, links.n_blk - 1):
        line.send(step)
        out_scatter.tick(step)
        if step == 2:
            down.second_way()
        line.arrived()

    def into(target):
        def write(block, rows, values):
            target[block, rows, :] = values.astype(target.dtype)

        return write

    gate.result(into(grad_gate))
    up.result(into(grad_up))
    out_scatter.finish(out_total)

    def add_output(rows):
        output[rows, :] = (middle[rows, :] + out_total[rows, :]).astype(jnp.bfloat16)

    each_block(middle.shape[0], add_output)
    down.result(into(grad_down))
    keep.wait()
    scatter.sent()
    out_scatter.sent()
    links.finish()


def exchange_back(
    grad_parts,
    out_parts,
    middle,
    cotangent,
    gain,
    all_normed,
    grad_gate_pre,
    grad_up_pre,
    activated,
    all_cot,
):
    n_dp, n_blk, n_uly = (lax.axis_size(a) for a in EVERY)
    _, tokens, width = grad_parts.shape
    ff = grad_gate_pre.shape[1]
    depth = width // (n_dp * n_blk * n_uly)
    down_depth = ff // (n_dp * n_uly)
    return pl.pallas_call(
        back_kernel,
        out_shape=[
            jax.ShapeDtypeStruct((tokens, width), jnp.bfloat16),
            jax.ShapeDtypeStruct((tokens, width), jnp.float32),
            jax.ShapeDtypeStruct((1, width), jnp.float32),
            jax.ShapeDtypeStruct((n_blk, tokens, width), jnp.bfloat16),
            jax.ShapeDtypeStruct((n_blk, depth, ff), jnp.bfloat16),
            jax.ShapeDtypeStruct((n_blk, depth, ff), jnp.bfloat16),
            jax.ShapeDtypeStruct((1, down_depth, width), jnp.float32),
        ],
        in_specs=[VMEM] * 10,
        out_specs=[VMEM, VMEM, VMEM, HBM, VMEM, VMEM, VMEM],
        scratch_shapes=line_scratch(n_blk, tokens, width) * 2
        + [pltpu.VMEM((tokens, width), jnp.float32), pltpu.VMEM((tokens, width), jnp.bfloat16)]
        + plane_scratch(n_dp, n_blk, n_uly, depth, ff) * 2
        + plane_scratch(n_dp, 1, n_uly, down_depth, width)
        + semaphores(56),
        compiler_params=kernel_params(3, 63),
    )(
        grad_parts,
        out_parts,
        middle,
        cotangent,
        gain,
        all_normed,
        grad_gate_pre,
        grad_up_pre,
        activated,
        all_cot,
    )


def last_kernel(
    w_qkv,
    hidden,
    grad_middle,
    gain,
    normed,
    grad_qkv,
    heads,
    all_low,
    mlp_term,
    head_terms,
    grad_hidden,
    grad_w_qkv,
    grad_wo,
    small_sum,
    grad_parts,
    rightward,
    leftward,
    qkv_1,
    qkv_2,
    qkv_3,
    qkv_4,
    qkv_5,
    qkv_6,
    wo_1,
    wo_2,
    wo_3,
    wo_4,
    wo_5,
    wo_6,
    summed,
    small,
    attn_term,
    small_in,
    small_total,
    send,
    recv,
    here,
):
    links = Links(send, recv, here)
    links.greet(links.peers() + [links.x_way, links.y_way, links.core_way])
    scatter = LineScatter(links, grad_parts, rightward, leftward)
    qkv = PlaneScatter(links, qkv_1, qkv_2, qkv_3, qkv_4, qkv_5, qkv_6)
    out = PlaneScatter(links, wo_1, wo_2, wo_3, wo_4, wo_5, wo_6)

    for which, dp in ((0, links.other_dp), (1, links.dp)):
        weight_grad(normed, grad_qkv, qkv_1, dp, 4)
        qkv.between_cores(which)
    attn_term[...] = jnp.zeros_like(attn_term)
    tokens = grad_parts.shape[1]
    for column in range(0, w_qkv.shape[0], 512):
        grad_parts[:, :, column : column + 512] = (
            product_right(grad_qkv[...], w_qkv[column : column + 512, :])
            .astype(jnp.bfloat16)
            .reshape(links.n_blk, tokens, 512)
        )
    scatter.start()
    qkv.across_chips()

    def collect(rows):
        for blk in range(links.n_blk):
            source = hidden[blk, rows, :].astype(jnp.float32)
            part = grad_parts[blk, rows, :].astype(jnp.float32)
            attn_term[...] += jnp.sum(part * (source * rms_scale(source)), axis=0, keepdims=True)

    each_block(tokens, collect)
    small[...] = jnp.zeros_like(small)
    span = gain.shape[1] // 128
    for index in range(span):
        columns = slice(index * 128, (index + 1) * 128)
        small[index : index + 1, :] = attn_term[:, columns]
        small[span + index : span + index + 1, :] = mlp_term[:, columns]
    small[2 * span : 2 * span + 8, :] = head_terms[...]
    small_in[links.blk] = small[...]
    small_copies = [links.to(small, small_in.at[links.blk], device) for device in links.peers()]
    for which, dp in ((0, links.other_dp), (1, links.dp)):
        weight_grad(heads, all_low, wo_1, dp, 4)
        out.between_cores(which)
    scatter.tick(1)
    out.across_chips()
    for copy in small_copies:
        copy.arrived()
    total = small_in[0]
    for blk in range(1, links.n_blk):
        total = total + small_in[blk]
    small_total[0] = total
    pending = links.to(small_total.at[0], small_in.at[links.n_blk], links.x_way)
    qkv.second_way()
    pending.arrived()
    small_total[1] = small_total[0] + small_in[links.n_blk]
    pending = links.to(small_total.at[1], small_in.at[links.n_blk + 1], links.y_way)
    for tick in range(2, links.n_blk - 1):
        scatter.tick(tick)
    out.second_way()
    pending.arrived()
    small_total[2] = small_total[1] + small_in[links.n_blk + 1]
    pending = links.to(small_total.at[2], small_in.at[links.n_blk + 2], links.core_way)

    def write(block, rows, values):
        summed[block, rows, :] = values.astype(jnp.bfloat16)

    qkv.result(write)
    swapped = []
    for step in range(1, links.n_blk):
        peer = links.peer(step)
        swapped.append(
            links.to(summed.at[peer], grad_w_qkv.at[links.blk], (links.dp, peer, links.uly))
        )
    keep = links.local(summed.at[links.blk], grad_w_qkv.at[links.blk])
    pending.arrived()
    small_sum[...] = small_total[2] + small_in[links.n_blk + 2]
    scatter.finish(grad_hidden)

    def body(rows):
        back, _ = back_rows(
            grad_hidden[rows, :], hidden[links.blk, rows, :].astype(jnp.float32), gain[...]
        )
        grad_hidden[rows, :] = grad_middle[rows, :] + back

    each_block(tokens, body)

    def write_out(block, rows, values):
        grad_wo[block, rows, :] = values

    out.result(write_out)
    for copy in swapped:
        copy.arrived()
    keep.wait()
    scatter.sent()
    links.finish()


def exchange_last(
    w_qkv,
    hidden,
    grad_middle,
    gain,
    normed,
    grad_qkv,
    heads,
    all_low,
    mlp_term,
    head_terms,
):
    n_dp, n_blk, n_uly = (lax.axis_size(a) for a in EVERY)
    _, tokens, width = hidden.shape
    columns = grad_qkv.shape[1]
    depth = width // (n_dp * n_blk * n_uly)
    out_depth = heads.shape[1] // (n_dp * n_uly)
    small = (2 * width // 128 + 8, 128)
    return pl.pallas_call(
        last_kernel,
        out_shape=[
            jax.ShapeDtypeStruct((tokens, width), jnp.float32),
            jax.ShapeDtypeStruct((n_blk, depth, columns), jnp.bfloat16),
            jax.ShapeDtypeStruct((1, out_depth, width), jnp.float32),
            jax.ShapeDtypeStruct(small, jnp.float32),
        ],
        in_specs=[VMEM] * 10,
        out_specs=[VMEM, HBM, VMEM, VMEM],
        scratch_shapes=[pltpu.VMEM((n_blk, tokens, width), jnp.bfloat16)]
        + line_scratch(n_blk, tokens, width)
        + plane_scratch(n_dp, n_blk, n_uly, depth, columns)
        + plane_scratch(n_dp, 1, n_uly, out_depth, width)
        + [
            pltpu.VMEM((n_blk, depth, columns), jnp.bfloat16),
            pltpu.VMEM(small, jnp.float32),
            pltpu.VMEM((1, width), jnp.float32),
            pltpu.VMEM((n_blk + 3,) + small, jnp.float32),
            pltpu.VMEM((3,) + small, jnp.float32),
        ]
        + semaphores(48),
        compiler_params=kernel_params(4, 56),
    )(
        w_qkv,
        hidden,
        grad_middle,
        gain,
        normed,
        grad_qkv,
        heads,
        all_low,
        mlp_term,
        head_terms,
    )


def finish_kernel(
    gate,
    up,
    qkv,
    wo,
    wd,
    hidden,
    out,
    f_gate,
    f_up,
    f_q,
    f_k,
    f_v,
    f_wo,
    f_wd,
    f_hidden,
    f_out,
):
    n_blk, depth, _ = gate.shape

    def place(source, offset, target):
        width = target.shape[1] // (n_blk * 2)
        for blk in range(n_blk):
            for group in range(2):
                to = (group * n_blk + blk) * width
                at = offset + group * width
                target[:, to : to + width] = source[blk, :, at : at + width].astype(jnp.float32)

    place(gate, 0, f_gate)
    place(up, 0, f_up)
    q_width = f_q.shape[1] // n_blk
    k_width = f_k.shape[1] // n_blk
    place(qkv, 0, f_q)
    place(qkv, q_width, f_k)
    place(qkv, q_width + k_width, f_v)
    f_wo[...] = wo[0]
    f_wd[...] = wd[0]
    f_hidden[...] = hidden[...]
    f_out[...] = out[...]


def finish(gate, up, qkv, wo, wd, hidden, out, shapes):
    return pl.pallas_call(
        finish_kernel,
        out_shape=[jax.ShapeDtypeStruct(shape, jnp.float32) for shape in shapes]
        + [
            jax.ShapeDtypeStruct(wo.shape[1:], jnp.float32),
            jax.ShapeDtypeStruct(wd.shape[1:], jnp.float32),
            jax.ShapeDtypeStruct(hidden.shape, jnp.float32),
            jax.ShapeDtypeStruct(out.shape, jnp.bfloat16),
        ],
        in_specs=[VMEM] * 7,
        out_specs=[VMEM] * 9,
        compiler_params=pltpu.CompilerParams(vmem_limit_bytes=40 * MIB),
    )(gate, up, qkv, wo, wd, hidden, out)


def product(left, right):
    return jnp.dot(left, right, preferred_element_type=jnp.float32)


def shards(
    hidden,
    span_order,
    attn_gain,
    w_query,
    key_weight,
    value_weight,
    w_out,
    q_gain,
    k_gain,
    mlp_gain,
    w_gate,
    w_up,
    w_down,
    cotangent,
):
    seqs, toks, width = hidden.shape
    n_dp, n_blk, n_uly = (lax.axis_size(a) for a in EVERY)
    blk_index = lax.axis_index(BLK)
    uly_index = lax.axis_index(ULY)
    group = QUERY_HEADS // KEY_VALUE_HEADS
    half_len = toks * n_uly // 2
    rows = n_blk * seqs * toks
    f32, bf16 = jnp.float32, jnp.bfloat16
    own_hidden = hidden.reshape(seqs * toks, width)
    own_cotangent = cotangent.reshape(seqs * toks, width)

    def positions(u):
        places = (
            jnp.arange(n_blk, dtype=jnp.int32)[:, None] * n_uly + u
        ) * toks + jnp.arange(toks, dtype=jnp.int32)[None, :]
        return positions_of(places.reshape(-1), span_order, half_len)

    own_pos = positions(uly_index)
    query_pos = jnp.tile(own_pos, group)[None, :]
    key_pos = jnp.concatenate([positions(u) for u in range(n_uly)])[:, None]
    angles = angles_of(own_pos, HEAD_SIZE)
    cosine, sine = jnp.cos(angles), jnp.sin(angles)
    cosine = jnp.concatenate([cosine, cosine], axis=1)
    sine = jnp.concatenate([-sine, sine], axis=1)
    gain_q, gain_k = q_gain.astype(f32)[None, :], k_gain.astype(f32)[None, :]

    gain_rows = attn_gain.shape[0]
    own_gains = jnp.pad(jnp.stack([attn_gain, mlp_gain]), ((0, 14), (0, 128 - gain_rows)))
    all_hidden, w_qkv, wo, all_wd, all_gains, cot = gather_front(
        own_hidden,
        w_query,
        key_weight,
        value_weight,
        w_out,
        w_down,
        own_gains,
        own_cotangent,
    )
    gains = all_gains[..., :2, :gain_rows].astype(f32)
    g_attn = gains[..., 0, :].reshape(1, width)
    g_mlp = gains[..., 1, :].reshape(1, width)
    w_qkv = w_qkv.reshape(width, -1)
    wo = wo.reshape(-1, width)
    (
        rows_wg,
        rows_wu,
        cot,
        heads_flat,
        normed,
        qkv,
        queries,
        key_values,
        lse,
    ) = attend_forward(
        w_gate,
        w_up,
        cot,
        all_hidden.reshape(rows, width),
        w_qkv,
        g_attn,
        gain_q,
        gain_k,
        cosine,
        sine,
        query_pos,
        key_pos,
        seqs,
    )
    middle, normed2, all_wg, all_wu, cot = exchange_middle(
        heads_flat.reshape(n_blk, seqs * toks, -1),
        wo,
        own_hidden,
        g_mlp,
        rows_wg,
        rows_wu,
        cot,
    )
    wg, wu = all_wg.reshape(width, -1), all_wu.reshape(width, -1)
    wd = all_wd.reshape(-1, width)
    cot = cot.reshape(rows, width)
    normed2 = normed2.reshape(rows, width)
    gate_pre = product(normed2, wg)
    up_pre = product(normed2, wu)
    sigmoid_gate = jax.nn.sigmoid(gate_pre)
    activated = (gate_pre * sigmoid_gate * up_pre).astype(bf16)
    out_parts = product(activated, wd).astype(bf16)
    grad_act = product_right(cot, wd)
    grad_gate_pre = (
        grad_act * up_pre * sigmoid_gate * (1.0 + gate_pre * (1.0 - sigmoid_gate))
    ).astype(bf16)
    grad_up_pre = (grad_act * gate_pre * sigmoid_gate).astype(bf16)
    grad_parts = (product_right(grad_gate_pre, wg) + product_right(grad_up_pre, wu)).astype(bf16)
    blocks = (n_blk, seqs * toks, width)
    output, grad_middle, mlp_gain_term, middle_low, grad_gate, grad_up, grad_down = exchange_back(
        grad_parts.reshape(blocks),
        out_parts.reshape(blocks),
        middle,
        own_cotangent,
        g_mlp,
        normed2,
        grad_gate_pre,
        grad_up_pre,
        activated,
        cot,
    )
    middle_low = middle_low.reshape(rows, width)
    grad_qkv, head_terms, grad_gate, grad_up = attend_back(
        middle_low,
        wo,
        queries,
        key_values,
        lse,
        qkv,
        gain_q,
        gain_k,
        cosine,
        sine,
        query_pos,
        key_pos,
        grad_gate,
        grad_up,
    )
    grad_hidden, grad_w_qkv, grad_out, small = exchange_last(
        w_qkv,
        all_hidden,
        grad_middle,
        g_attn,
        normed,
        grad_qkv,
        heads_flat,
        middle_low,
        mlp_gain_term,
        head_terms,
    )
    (
        grad_gate,
        grad_up,
        grad_query,
        grad_key,
        grad_value,
        grad_out,
        grad_down,
        grad_hidden,
        output,
    ) = finish(
        grad_gate,
        grad_up,
        grad_w_qkv,
        grad_out,
        grad_down,
        grad_hidden,
        output,
        [w.shape for w in (w_gate, w_up, w_query, key_weight, value_weight)],
    )
    small = small.reshape(-1)
    gain_at = ((lax.axis_index(DP) * n_blk + blk_index) * n_uly + uly_index) * gain_rows
    grad_attn_gain = lax.dynamic_slice(small, (gain_at,), (gain_rows,))
    grad_mlp_gain = lax.dynamic_slice(small, (width + gain_at,), (gain_rows,))
    grad_q_gain = small[2 * width : 2 * width + HEAD_SIZE]
    grad_k_gain = small[2 * width + HEAD_SIZE : 2 * width + 2 * HEAD_SIZE]
    return (
        output.reshape(hidden.shape),
        grad_hidden.reshape(hidden.shape),
        grad_attn_gain,
        grad_query,
        grad_key,
        grad_value,
        grad_out,
        grad_q_gain,
        grad_k_gain,
        grad_mlp_gain,
        grad_gate,
        grad_up,
        grad_down,
    )


def solution(mesh):
    n_dp, n_blk, n_uly = (mesh.shape[a] for a in EVERY)
    aligned = (n_dp, n_uly) == (2, 4) and KEY_VALUE_HEADS % (n_dp * n_blk) == 0
    in_specs = (
        TOKENS,
        P(),
        P(EVERY),
        P(EVERY, None),
        P(EVERY, None),
        P(EVERY, None),
        P(EVERY, None),
        P(),
        P(),
        P(EVERY),
        P(EVERY, None),
        P(EVERY, None),
        P(EVERY, None),
        TOKENS,
    )
    out_specs = (
        TOKENS,
        TOKENS,
        P(EVERY),
        P(EVERY, None),
        P(EVERY, None),
        P(EVERY, None),
        P(EVERY, None),
        P(),
        P(),
        P(EVERY),
        P(EVERY, None),
        P(EVERY, None),
        P(EVERY, None),
    )
    return jax.shard_map(
        shards if aligned else shards_general,
        mesh=mesh, in_specs=in_specs, out_specs=out_specs, check_vma=False)
```

```python
import math

import jax
import jax.numpy as jnp
from jax import lax
from jax.experimental import pallas as pl
from jax.experimental.pallas import tpu as pltpu
from jax.sharding import PartitionSpec as P

QUERY_HEADS = 16
KEY_VALUE_HEADS = 8
HEAD_SIZE = 128


DP, BLK, ULY = "dp", "blk", "uly"
EVERY = (DP, BLK, ULY)
PLANE = (DP, ULY)
TOKENS = P(DP, (BLK, ULY), None)
EQ_KGQD_NKD_TO_KGQN = "kgqd,nkd->kgqn"
EQ_KGQN_KGQD_TO_NKD = "kgqn,kgqd->nkd"
EQ_KGQN_NKD_TO_KGQD = "kgqn,nkd->kgqd"
EQ_KGQN_QKGD_TO_NKD = "kgqn,qkgd->nkd"
EQ_QKGD_NKD_TO_KGQN = "qkgd,nkd->kgqn"
EQ_STD_DE_TO_STE = "std,de->ste"
EQ_STD_DF_TO_STF = "std,df->stf"
EQ_STD_ED_TO_STE = "std,ed->ste"
EQ_STD_FD_TO_STF = "std,fd->stf"
EQ_STD_STE_TO_DE = "std,ste->de"
EQ_STD_STF_TO_DF = "std,stf->df"
EQ_STE_DE_TO_STD = "ste,de->std"
EQ_STE_ED_TO_STD = "ste,ed->std"
EQ_STE_STD_TO_ED = "ste,std->ed"
EQ_STF_DF_TO_STD = "stf,df->std"
EQ_STF_FD_TO_STD = "stf,fd->std"
EQ_STF_STD_TO_FD = "stf,std->fd"

EPSILON = 1e-06
ROPE_BASE = 1000000.0


def rms_scale(source):
    return lax.rsqrt(jnp.mean(source * source, axis=-1, keepdims=True) + EPSILON)


def norm_back(grad_normed, source, norm_scale, gain):
    unit_rows = source * norm_scale
    scaled = grad_normed * gain
    return norm_scale * (scaled - unit_rows * jnp.mean(scaled * unit_rows, axis=-1, keepdims=True))


def angles_of(positions, head_dim):
    freq_steps = jnp.arange(head_dim // 2, dtype=jnp.float32)
    inverse = jnp.exp(freq_steps * (-2.0 * math.log(ROPE_BASE) / head_dim))
    return positions.astype(jnp.float32)[:, None] * inverse[None, :]


def rotate(source, angles, direction):
    half_dim = source.shape[-1] // 2
    cosine = jnp.cos(angles)[:, None, :]
    sine_part = direction * jnp.sin(angles)[:, None, :]
    first_half = source[..., :half_dim]
    second_half = source[..., half_dim:]
    return jnp.concatenate(
        [
            first_half * cosine - second_half * sine_part,
            second_half * cosine + first_half * sine_part,
        ],
        axis=-1,
    )


def positions_of(places, span_order, half_len):
    blocks_of = places // half_len
    block_ids = jnp.arange(span_order.shape[0], dtype=jnp.int32)
    chosen = jnp.sum(
        jnp.where(blocks_of[:, None] == block_ids[None, :], span_order[None, :], 0), axis=1
    )
    return chosen * half_len + places % half_len


def add_rows(buffer, new_rows):
    return buffer + new_rows


def shards_general(
    hidden,
    span_order,
    attn_gain,
    w_query,
    key_weight,
    value_weight,
    w_out,
    q_gain,
    k_gain,
    mlp_gain,
    w_gate,
    w_up,
    w_down,
    cotangent,
):
    sequence_count = hidden.shape[0]
    token_count = hidden.shape[1]
    ulysses_group_size = lax.axis_size(ULY)
    local_q = QUERY_HEADS // ulysses_group_size
    local_key_value = KEY_VALUE_HEADS // ulysses_group_size
    query_group_width = QUERY_HEADS // KEY_VALUE_HEADS
    block_len = token_count * ulysses_group_size
    half_len = block_len // 2
    score_scale = 1.0 / math.sqrt(HEAD_SIZE)
    blk_index = lax.axis_index(BLK)
    uly_index = lax.axis_index(ULY)
    first_place = (blk_index * ulysses_group_size + uly_index) * token_count
    local_angles = angles_of(
        positions_of(first_place + jnp.arange(token_count, dtype=jnp.int32), span_order, half_len),
        HEAD_SIZE,
    )
    query_pos = positions_of(
        blk_index * block_len + jnp.arange(block_len, dtype=jnp.int32), span_order, half_len
    )
    g_attn, wq_all, wk_all, wv_all, wo_all = (
        lax.all_gather(attn_gain, EVERY, axis=0, tiled=True),
        lax.all_gather(w_query, EVERY, axis=0, tiled=True),
        lax.all_gather(key_weight, EVERY, axis=0, tiled=True),
        lax.all_gather(value_weight, EVERY, axis=0, tiled=True),
        lax.all_gather(w_out, EVERY, axis=0, tiled=True),
    )
    source = hidden.astype(jnp.float32)
    first_scale = rms_scale(source)
    normalized_input = (source * first_scale * g_attn.astype(jnp.float32)).astype(jnp.bfloat16)
    q_pre = jnp.einsum(
        EQ_STD_DE_TO_STE, normalized_input, wq_all, preferred_element_type=jnp.float32
    ).reshape(sequence_count, token_count, QUERY_HEADS, HEAD_SIZE)
    key_before_norm = jnp.einsum(
        EQ_STD_DE_TO_STE, normalized_input, wk_all, preferred_element_type=jnp.float32
    ).reshape(sequence_count, token_count, KEY_VALUE_HEADS, HEAD_SIZE)
    value_before_norm = jnp.einsum(
        EQ_STD_DE_TO_STE, normalized_input, wv_all, preferred_element_type=jnp.float32
    ).reshape(sequence_count, token_count, KEY_VALUE_HEADS, HEAD_SIZE)
    q_scale = rms_scale(q_pre)
    k_scale = rms_scale(key_before_norm)
    gain_q = q_gain.astype(jnp.float32)
    gain_k = k_gain.astype(jnp.float32)
    q_rot = rotate(q_pre * q_scale * gain_q, local_angles, 1.0).astype(jnp.bfloat16)
    k_rot = rotate(key_before_norm * k_scale * gain_k, local_angles, 1.0).astype(jnp.bfloat16)
    v_low = value_before_norm.astype(jnp.bfloat16)
    q_heads, k_heads, v_heads = (
        lax.all_to_all(q_rot, ULY, split_axis=2, concat_axis=1, tiled=True),
        lax.all_to_all(k_rot, ULY, split_axis=2, concat_axis=1, tiled=True),
        lax.all_to_all(v_low, ULY, split_axis=2, concat_axis=1, tiled=True),
    )
    q_group = q_heads.reshape(
        sequence_count, block_len, local_key_value, query_group_width, HEAD_SIZE
    )
    stat_shape = (sequence_count, local_key_value, query_group_width, block_len)
    start_state = (
        jnp.full(stat_shape, -1e30, jnp.float32),
        jnp.zeros(stat_shape, jnp.float32),
        jnp.zeros(stat_shape + (HEAD_SIZE,), jnp.float32),
    )
    key_piece = lax.all_gather(k_heads, BLK, axis=1, tiled=True)
    value_piece = lax.all_gather(v_heads, BLK, axis=1, tiled=True)
    key_pos = positions_of(jnp.arange(key_piece.shape[1], dtype=jnp.int32), span_order, half_len)
    allowed = query_pos[:, None] >= key_pos[None, :]

    def attend_one_sequence(members):
        query_rows, key_rows, value_rows, top_seq, total_seq, accum_seq = members
        scores = (
            jnp.einsum(EQ_QKGD_NKD_TO_KGQN, query_rows, key_rows, preferred_element_type=jnp.float32)
            * score_scale
        )
        scores = jnp.where(allowed, scores, -jnp.inf)
        new_top = jnp.maximum(top_seq, jnp.max(scores, axis=-1))
        fading = jnp.exp(top_seq - new_top)
        weights = jnp.exp(scores - new_top[..., None])
        total_seq = total_seq * fading + jnp.sum(weights, axis=-1)
        accum_seq = accum_seq * fading[..., None] + jnp.einsum(
            EQ_KGQN_NKD_TO_KGQD,
            weights.astype(jnp.bfloat16),
            value_rows,
            preferred_element_type=jnp.float32,
        )
        return (new_top, total_seq, accum_seq)

    row_top, row_total, accum = lax.map(
        attend_one_sequence,
        (q_group, key_piece, value_piece, start_state[0], start_state[1], start_state[2]),
    )
    log_total = row_top + jnp.log(row_total)
    attention_output = jnp.transpose(accum / row_total[..., None], (0, 3, 1, 2, 4)).reshape(
        sequence_count, block_len, local_q, HEAD_SIZE
    )
    heads_seq = lax.all_to_all(
        attention_output.astype(jnp.bfloat16), ULY, split_axis=1, concat_axis=2, tiled=True
    )
    heads_flat = heads_seq.reshape(sequence_count, token_count, QUERY_HEADS * HEAD_SIZE)
    middle = source + jnp.einsum(
        EQ_STE_ED_TO_STD, heads_flat, wo_all, preferred_element_type=jnp.float32
    )
    g_mlp, wg_all, wu_all, wd_all = (
        lax.all_gather(mlp_gain, EVERY, axis=0, tiled=True),
        lax.all_gather(w_gate, EVERY, axis=0, tiled=True),
        lax.all_gather(w_up, EVERY, axis=0, tiled=True),
        lax.all_gather(w_down, EVERY, axis=0, tiled=True),
    )
    second_scale = rms_scale(middle)
    gain_mlp = g_mlp.astype(jnp.float32)
    normed2 = (middle * second_scale * gain_mlp).astype(jnp.bfloat16)
    gate_pre = jnp.einsum(EQ_STD_DF_TO_STF, normed2, wg_all, preferred_element_type=jnp.float32)
    up_pre = jnp.einsum(EQ_STD_DF_TO_STF, normed2, wu_all, preferred_element_type=jnp.float32)
    sigmoid_gate = jax.nn.sigmoid(gate_pre)
    activated = (gate_pre * sigmoid_gate * up_pre).astype(jnp.bfloat16)
    result = middle + jnp.einsum(
        EQ_STF_FD_TO_STD, activated, wd_all, preferred_element_type=jnp.float32
    )
    output = result.astype(jnp.bfloat16)
    g_mlp, wg_all, wu_all, wd_all = (
        lax.all_gather(mlp_gain, EVERY, axis=0, tiled=True),
        lax.all_gather(w_gate, EVERY, axis=0, tiled=True),
        lax.all_gather(w_up, EVERY, axis=0, tiled=True),
        lax.all_gather(w_down, EVERY, axis=0, tiled=True),
    )
    gain_mlp = g_mlp.astype(jnp.float32)
    grad_act = jnp.einsum(EQ_STD_FD_TO_STF, cotangent, wd_all, preferred_element_type=jnp.float32)
    grad_gate_pre = (
        grad_act * up_pre * sigmoid_gate * (1.0 + gate_pre * (1.0 - sigmoid_gate))
    ).astype(jnp.bfloat16)
    grad_up_pre = (grad_act * gate_pre * sigmoid_gate).astype(jnp.bfloat16)
    grad_gate = jnp.einsum(
        EQ_STD_STF_TO_DF, normed2, grad_gate_pre, preferred_element_type=jnp.float32
    )
    grad_up = jnp.einsum(EQ_STD_STF_TO_DF, normed2, grad_up_pre, preferred_element_type=jnp.float32)
    grad_normed2 = jnp.einsum(
        EQ_STF_DF_TO_STD, grad_gate_pre, wg_all, preferred_element_type=jnp.float32
    ) + jnp.einsum(EQ_STF_DF_TO_STD, grad_up_pre, wu_all, preferred_element_type=jnp.float32)
    mlp_gain_term = jnp.sum(grad_normed2 * middle * second_scale, axis=(0, 1))
    grad_middle = cotangent.astype(jnp.float32) + norm_back(
        grad_normed2, middle, second_scale, gain_mlp
    )
    grad_mlp_gain, grad_gate, grad_up = (
        lax.psum_scatter(mlp_gain_term, EVERY, scatter_dimension=0, tiled=True),
        lax.psum_scatter(grad_gate, EVERY, scatter_dimension=0, tiled=True),
        lax.psum_scatter(grad_up, EVERY, scatter_dimension=0, tiled=True),
    )
    g_attn, wq_all, wk_all, wv_all, wo_all = (
        lax.all_gather(attn_gain, EVERY, axis=0, tiled=True),
        lax.all_gather(w_query, EVERY, axis=0, tiled=True),
        lax.all_gather(key_weight, EVERY, axis=0, tiled=True),
        lax.all_gather(value_weight, EVERY, axis=0, tiled=True),
        lax.all_gather(w_out, EVERY, axis=0, tiled=True),
    )
    middle_low = grad_middle.astype(jnp.bfloat16)
    grad_out = jnp.einsum(EQ_STE_STD_TO_ED, heads_flat, middle_low, preferred_element_type=jnp.float32)
    grad_heads = (
        jnp.einsum(EQ_STD_ED_TO_STE, middle_low, wo_all, preferred_element_type=jnp.float32)
        .astype(jnp.bfloat16)
        .reshape(sequence_count, token_count, QUERY_HEADS, HEAD_SIZE)
    )
    grad_heads_local = lax.all_to_all(grad_heads, ULY, split_axis=2, concat_axis=1, tiled=True)
    grad_group = jnp.transpose(
        grad_heads_local.reshape(
            sequence_count, block_len, local_key_value, query_group_width, HEAD_SIZE
        ),
        (0, 2, 3, 1, 4),
    )
    delta = jnp.sum(grad_heads_local.astype(jnp.float32) * attention_output, axis=-1)
    delta = jnp.transpose(
        delta.reshape(sequence_count, block_len, local_key_value, query_group_width), (0, 2, 3, 1)
    )
    seq_length = block_len * lax.axis_size(BLK)
    zero_keys = jnp.zeros((sequence_count, seq_length, local_key_value, HEAD_SIZE), jnp.float32)
    back_state = (jnp.zeros(stat_shape + (HEAD_SIZE,), jnp.float32), zero_keys, zero_keys)
    key_piece = lax.all_gather(k_heads, BLK, axis=1, tiled=True)
    value_piece = lax.all_gather(v_heads, BLK, axis=1, tiled=True)
    key_pos = positions_of(jnp.arange(key_piece.shape[1], dtype=jnp.int32), span_order, half_len)
    back_allowed = query_pos[:, None] >= key_pos[None, :]

    def back_one_sequence(members):
        query_rows, grad_rows, lse_seq, delta_seq, key_rows, value_rows, dq_seq, dk_seq, dv_seq = (
            members
        )
        scores = (
            jnp.einsum(EQ_QKGD_NKD_TO_KGQN, query_rows, key_rows, preferred_element_type=jnp.float32)
            * score_scale
        )
        scores = jnp.where(back_allowed, scores, -jnp.inf)
        probs = jnp.exp(scores - lse_seq[..., None])
        grad_values = jnp.einsum(
            EQ_KGQN_KGQD_TO_NKD,
            probs.astype(jnp.bfloat16),
            grad_rows,
            preferred_element_type=jnp.float32,
        )
        grad_probs = jnp.einsum(
            EQ_KGQD_NKD_TO_KGQN, grad_rows, value_rows, preferred_element_type=jnp.float32
        )
        grad_scores = (probs * (grad_probs - delta_seq[..., None])).astype(jnp.bfloat16)
        dq_seq = dq_seq + score_scale * jnp.einsum(
            EQ_KGQN_NKD_TO_KGQD, grad_scores, key_rows, preferred_element_type=jnp.float32
        )
        grad_keys = score_scale * jnp.einsum(
            EQ_KGQN_QKGD_TO_NKD, grad_scores, query_rows, preferred_element_type=jnp.float32
        )
        return (dq_seq, add_rows(dk_seq, grad_keys), add_rows(dv_seq, grad_values))

    grad_q_group, grad_k_whole, grad_v_whole = lax.map(
        back_one_sequence,
        (
            q_group,
            grad_group,
            log_total,
            delta,
            key_piece,
            value_piece,
            back_state[0],
            back_state[1],
            back_state[2],
        ),
    )
    grad_k_block, grad_v_block = (
        lax.psum_scatter(
            grad_k_whole.astype(jnp.bfloat16), BLK, scatter_dimension=1, tiled=True
        ).astype(jnp.float32),
        lax.psum_scatter(
            grad_v_whole.astype(jnp.bfloat16), BLK, scatter_dimension=1, tiled=True
        ).astype(jnp.float32),
    )
    grad_q_block = jnp.transpose(grad_q_group, (0, 3, 1, 2, 4)).reshape(
        sequence_count, block_len, local_q, HEAD_SIZE
    )
    grad_q_seq, grad_k_seq, value_sequence_gradient = (
        lax.all_to_all(
            grad_q_block.astype(jnp.bfloat16), ULY, split_axis=1, concat_axis=2, tiled=True
        ).astype(grad_q_block.dtype),
        lax.all_to_all(
            grad_k_block.astype(jnp.bfloat16), ULY, split_axis=1, concat_axis=2, tiled=True
        ).astype(grad_k_block.dtype),
        lax.all_to_all(
            grad_v_block.astype(jnp.bfloat16), ULY, split_axis=1, concat_axis=2, tiled=True
        ).astype(grad_v_block.dtype),
    )
    grad_q_normed = rotate(grad_q_seq, local_angles, -1.0)
    grad_k_normed = rotate(grad_k_seq, local_angles, -1.0)
    q_gain_term = jnp.sum(grad_q_normed * q_pre * q_scale, axis=(0, 1, 2))
    k_gain_term = jnp.sum(grad_k_normed * key_before_norm * k_scale, axis=(0, 1, 2))
    grad_q_pre = (
        norm_back(grad_q_normed, q_pre, q_scale, gain_q)
        .astype(jnp.bfloat16)
        .reshape(sequence_count, token_count, QUERY_HEADS * HEAD_SIZE)
    )
    grad_k_pre = (
        norm_back(grad_k_normed, key_before_norm, k_scale, gain_k)
        .astype(jnp.bfloat16)
        .reshape(sequence_count, token_count, KEY_VALUE_HEADS * HEAD_SIZE)
    )
    value_pre_gradient = value_sequence_gradient.astype(jnp.bfloat16).reshape(
        sequence_count, token_count, KEY_VALUE_HEADS * HEAD_SIZE
    )
    grad_query = jnp.einsum(
        EQ_STD_STE_TO_DE, normalized_input, grad_q_pre, preferred_element_type=jnp.float32
    )
    grad_key = jnp.einsum(
        EQ_STD_STE_TO_DE, normalized_input, grad_k_pre, preferred_element_type=jnp.float32
    )
    grad_value = jnp.einsum(
        EQ_STD_STE_TO_DE, normalized_input, value_pre_gradient, preferred_element_type=jnp.float32
    )
    grad_normed = jnp.einsum(EQ_STE_DE_TO_STD, grad_q_pre, wq_all, preferred_element_type=jnp.float32)
    grad_normed = grad_normed + jnp.einsum(
        EQ_STE_DE_TO_STD, grad_k_pre, wk_all, preferred_element_type=jnp.float32
    )
    grad_normed = grad_normed + jnp.einsum(
        EQ_STE_DE_TO_STD, value_pre_gradient, wv_all, preferred_element_type=jnp.float32
    )
    attn_gain_term = jnp.sum(grad_normed * source * first_scale, axis=(0, 1))
    grad_hidden = grad_middle + norm_back(
        grad_normed, source, first_scale, g_attn.astype(jnp.float32)
    )
    grad_down = jnp.einsum(EQ_STF_STD_TO_FD, activated, cotangent, preferred_element_type=jnp.float32)
    grad_attn_gain, grad_query, grad_key, grad_value, grad_out, grad_down = (
        lax.psum_scatter(attn_gain_term, EVERY, scatter_dimension=0, tiled=True),
        lax.psum_scatter(grad_query, EVERY, scatter_dimension=0, tiled=True),
        lax.psum_scatter(grad_key, EVERY, scatter_dimension=0, tiled=True),
        lax.psum_scatter(grad_value, EVERY, scatter_dimension=0, tiled=True),
        lax.psum_scatter(grad_out, EVERY, scatter_dimension=0, tiled=True),
        lax.psum_scatter(grad_down, EVERY, scatter_dimension=0, tiled=True),
    )
    grad_q_gain, grad_k_gain = lax.psum((q_gain_term, k_gain_term), EVERY)
    return (
        output,
        grad_hidden,
        grad_attn_gain,
        grad_query,
        grad_key,
        grad_value,
        grad_out,
        grad_q_gain,
        grad_k_gain,
        grad_mlp_gain,
        grad_gate,
        grad_up,
        grad_down,
    )


MESH = pl.DeviceIdType.MESH
HBM = pl.BlockSpec(memory_space=pltpu.HBM)
VMEM = pl.BlockSpec(memory_space=pltpu.VMEM)
MIB = 1 << 20


def kernel_params(collective_id, vmem_mib=62):
    return pltpu.CompilerParams(
        collective_id=collective_id, has_side_effects=True, vmem_limit_bytes=vmem_mib * MIB
    )


def semaphores(count, local=16):
    return [
        pltpu.SemaphoreType.DMA((count,)),
        pltpu.SemaphoreType.DMA((count,)),
        pltpu.SemaphoreType.DMA((local,)),
    ]


class Copy:
    def __init__(self, descriptor, sends, receives):
        self.descriptor, self.sends, self.receives = descriptor, sends, receives

    def under(self, condition, action):
        if condition is None:
            action()
        else:
            pl.when(condition)(action)

    def start(self):
        self.under(self.sends, lambda: self.descriptor().start())
        return self

    def sent(self):
        self.under(self.sends, lambda: self.descriptor().wait_send())

    def arrived(self):
        self.under(self.receives, lambda: self.descriptor().wait_recv())


class Links:
    def __init__(self, send, recv, here):
        self.send, self.recv, self.here = send, recv, here
        self.used, self.used_here = 0, 0
        self.copies, self.local_copies = [], []
        self.n_dp, self.n_blk, self.n_uly = (lax.axis_size(a) for a in EVERY)
        self.dp, self.blk, self.uly = (lax.axis_index(a) for a in EVERY)
        self.other_dp = 1 - self.dp
        self.across = lax.rem(self.uly + 2, 4)
        self.twin = self.uly + 1 - 2 * lax.rem(self.uly, 2)
        self.x_way = (self.other_dp, self.blk, self.uly)
        self.y_way = (self.dp, self.blk, self.across)
        self.core_way = (self.dp, self.blk, self.twin)

    def peer(self, step):
        return lax.rem(self.blk + step, self.n_blk)

    def peers(self):
        return [(self.dp, self.peer(k), self.uly) for k in range(1, self.n_blk)]

    def greet(self, devices):
        barrier = pltpu.get_barrier_semaphore()
        for device in devices:
            pl.semaphore_signal(barrier, inc=1, device_id=device, device_id_type=MESH)
        pl.semaphore_wait(barrier, len(devices))

    def remote(self, source, target, device, sends=None, receives=None):
        slot = self.used
        self.used += 1

        def descriptor():
            return pltpu.make_async_remote_copy(
                src_ref=source(),
                dst_ref=target(),
                send_sem=self.send.at[slot],
                recv_sem=self.recv.at[slot],
                device_id=device,
                device_id_type=MESH,
            )

        copy = Copy(descriptor, sends, receives)
        self.copies.append(copy)
        return copy.start()

    def to(self, source, target, device):
        return self.remote(lambda: source, lambda: target, device)

    def local(self, source, target):
        copy = pltpu.make_async_copy(source, target, self.here.at[self.used_here])
        self.used_here += 1
        copy.start()
        self.local_copies.append(copy)
        return copy

    def finish(self):
        for copy in self.copies:
            copy.sent()


class LineGather:
    def __init__(self, links, own, whole):
        self.links, self.own, self.whole = links, own, whole
        self.waiting = []

    def send(self, step):
        links, whole = self.links, self.whole
        blk, last = links.blk, links.n_blk - 1

        def block(index):
            if step == 0:
                return lambda: self.own
            return lambda: whole.at[index]

        self.waiting = [
            links.remote(
                block(blk - step),
                lambda: whole.at[blk - step],
                (links.dp, blk + 1, links.uly),
                jnp.logical_and(blk >= step, blk < last),
                blk >= step + 1,
            ),
            links.remote(
                block(blk + step),
                lambda: whole.at[blk + step],
                (links.dp, blk - 1, links.uly),
                jnp.logical_and(blk + step <= last, blk > 0),
                blk + step + 1 <= last,
            ),
        ]

    def arrived(self):
        for copy in self.waiting:
            copy.arrived()


def halves(tokens):
    return [pl.ds(0, tokens // 2), pl.ds(tokens // 2, tokens // 2)]


class HalvedLine:
    def __init__(self, links, own, whole):
        self.lines = [
            LineGather(links, None if own is None else own.at[rows], whole.at[:, rows])
            for rows in halves(whole.shape[1])
        ]

    def send(self, step):
        for line in self.lines:
            line.send(step)

    def advance(self, step):
        for line in self.lines:
            line.arrived()
            line.send(step)

    def arrived(self):
        for line in self.lines:
            line.arrived()


class PlaneGather:
    def __init__(self, links, at):
        self.links, self.at = links, at

    def start(self, own=None):
        links, at = self.links, self.at
        mine = at(links.dp, links.uly)
        own = mine if own is None else own
        self.from_x = links.to(own, mine, links.x_way)
        self.from_y = links.to(own, mine, links.y_way)
        self.from_core = [links.to(own, mine, links.core_way)]

    def hand_on(self):
        links, at = self.links, self.at
        self.from_x.arrived()
        half = at(links.other_dp, links.uly, 0)
        self.second_y = links.to(half, half, links.y_way)
        self.from_y.arrived()
        half = at(links.dp, links.across, 1)
        self.second_x = links.to(half, half, links.x_way)
        for chunk in (at(links.other_dp, links.uly), at(links.dp, links.across)):
            self.from_core.append(links.to(chunk, chunk, links.core_way))

    def last(self):
        links = self.links
        self.second_y.arrived()
        self.second_x.arrived()
        chunk = self.at(links.other_dp, links.across)
        self.from_core.append(links.to(chunk, chunk, links.core_way))

    def arrived(self):
        for copy in self.from_core:
            copy.arrived()


def rows_of(whole, blocked):
    def at(dp, uly, half=None):
        part = whole.at[dp, :, uly] if blocked else whole.at[dp, uly]
        if half is None:
            return part
        depth = whole.shape[-2] // 2
        rows = pl.ds(half * depth, depth)
        return part.at[:, rows] if blocked else part.at[rows]

    return at


class ColumnSwap:
    def __init__(self, links, pieces):
        self.links, self.pieces = links, pieces
        self.incoming, self.kept = [], []

    def parts(self, blk):
        links = self.links
        for weight, whole, offset in self.pieces:
            width = weight.shape[-1] // links.n_dp // links.n_blk
            for group in range(links.n_dp):
                start = (group * links.n_blk + blk) * width
                yield (
                    weight.at[:, pl.ds(pl.multiple_of(start, 128), width)],
                    whole.at[links.blk, :, pl.ds(offset + group * width, width)],
                )

    def start(self):
        links = self.links
        for step in range(1, links.n_blk):
            device = (links.dp, links.peer(step), links.uly)
            for source, target in self.parts(links.peer(step)):
                self.incoming.append(links.to(source, target, device))
        for source, target in self.parts(links.blk):
            self.kept.append(links.local(source, target))

    def arrived(self):
        for copy in self.kept:
            copy.wait()
        for copy in self.incoming:
            copy.arrived()


def front_kernel(
    hidden,
    wq,
    wk,
    wv,
    wo,
    wd,
    gains,
    cotangent,
    all_hidden,
    w_qkv,
    all_wo,
    all_wd,
    all_gains,
    all_cot,
    send,
    recv,
    here,
):
    links = Links(send, recv, here)
    links.greet(links.peers() + [links.x_way, links.y_way, links.core_way])
    q_width, k_width = wq.shape[1] // links.n_blk, wk.shape[1] // links.n_blk
    chunk = w_qkv.at[links.dp, :, links.uly]
    swap = ColumnSwap(
        links, [(wq, chunk, 0), (wk, chunk, q_width), (wv, chunk, q_width + k_width)]
    )
    plane_wo = PlaneGather(links, rows_of(all_wo, False))
    plane_wd = PlaneGather(links, rows_of(all_wd, False))
    plane_qkv = PlaneGather(links, rows_of(w_qkv, True))
    plane_gain = PlaneGather(links, rows_of(all_gains, True))
    swap.start()
    my_gains = all_gains.at[links.dp, links.blk, links.uly]
    gain_swap = [links.to(gains, my_gains, device) for device in links.peers()]
    plane_wo.start(wo)
    plane_wd.start(wd)
    keep = [
        links.local(gains, my_gains),
        links.local(hidden, all_hidden.at[links.blk]),
        links.local(cotangent, all_cot.at[links.blk]),
        links.local(wo, all_wo.at[links.dp, links.uly]),
        links.local(wd, all_wd.at[links.dp, links.uly]),
    ]
    swap.arrived()
    line = HalvedLine(links, hidden, all_hidden)
    line.send(0)
    plane_qkv.start()
    keep[0].wait()
    for copy in gain_swap:
        copy.arrived()
    plane_gain.start()
    plane_wo.hand_on()
    line.advance(1)
    plane_wd.hand_on()
    plane_qkv.hand_on()
    plane_gain.hand_on()
    plane_wo.last()
    for step in range(2, links.n_blk - 1):
        line.advance(step)
    cot_line = HalvedLine(links, cotangent, all_cot)
    cot_line.send(0)
    plane_wd.last()
    plane_qkv.last()
    plane_gain.last()
    line.arrived()
    cot_line.arrived()
    for plane in (plane_wo, plane_qkv, plane_gain, plane_wd):
        plane.arrived()
    for copy in keep[1:]:
        copy.wait()
    links.finish()


def gather_front(hidden, wq, wk, wv, wo, wd, gains, cotangent):
    n_dp, n_blk, n_uly = (lax.axis_size(a) for a in EVERY)
    qkv_width = (wq.shape[1] + wk.shape[1] + wv.shape[1]) // n_blk
    shapes = [
        (n_blk,) + hidden.shape,
        (n_dp, n_blk, n_uly, wq.shape[0], qkv_width),
        (n_dp, n_uly) + wo.shape,
        (n_dp, n_uly) + wd.shape,
        (n_dp, n_blk, n_uly) + gains.shape,
        (n_blk,) + cotangent.shape,
    ]
    return pl.pallas_call(
        front_kernel,
        out_shape=[jax.ShapeDtypeStruct(s, jnp.bfloat16) for s in shapes],
        in_specs=[HBM] * 8,
        out_specs=[HBM] * 6,
        scratch_shapes=semaphores(72),
        compiler_params=kernel_params(0),
    )(hidden, wq, wk, wv, wo, wd, gains, cotangent)


ROWS = 32


def each_block(count, body):
    def step(index, carry):
        body(pl.ds(pl.multiple_of(index * ROWS, ROWS), ROWS))
        return carry

    lax.fori_loop(0, count // ROWS, step, 0)


class LineScatter:
    def __init__(self, links, parts, rightward, leftward):
        self.links, self.parts = links, parts
        self.slots = {1: rightward, -1: leftward}
        self.tokens = parts.shape[1]
        self.number = links.used
        self.last = links.n_blk - 1
        links.used += 2 * self.last

    def target(self, step, way):
        return self.last - step if way == 1 else step

    def slot(self, step, way):
        target = self.target(step, way)
        return self.slots[way].at[target - 1 if way == 1 else target]

    def place(self, way):
        return self.links.blk if way == 1 else self.last - self.links.blk

    def copy(self, step, way, source=None):
        links, slot = self.links, self.slot(step, way)
        number = self.number + 2 * step + (1 if way == 1 else 0)
        return pltpu.make_async_remote_copy(
            src_ref=slot if source is None else source,
            dst_ref=slot,
            send_sem=links.send.at[number],
            recv_sem=links.recv.at[number],
            device_id=(links.dp, links.blk + way, links.uly),
            device_id_type=MESH,
        )

    def start(self):
        for step in range(self.last):
            for way in (1, -1):

                @pl.when(self.place(way) == 0)
                def _(step=step, way=way):
                    self.copy(step, way, self.parts.at[self.target(step, way)]).start()

    def tick(self, tick):
        for way in (1, -1):

            @pl.when(jnp.logical_and(self.place(way) >= 1, self.place(way) <= tick))
            def _(way=way):
                step = tick - self.place(way)
                self.copy(step, way).wait_recv()
                slot, target = self.slot(step, way), self.target(step, way)

                def body(rows):
                    slot[rows, :] = slot[rows, :] + self.parts[target, rows, :]

                each_block(self.tokens, body)
                self.copy(step, way).start()

    def finish(self, total):
        blk, last = self.links.blk, self.last

        def start(rows):
            total[rows, :] = self.parts[blk, rows, :].astype(jnp.float32)

        each_block(self.tokens, start)
        for way in (1, -1):

            @pl.when(self.place(way) >= 1)
            def _(way=way):
                step = last - self.place(way)
                self.copy(step, way).wait_recv()
                slot = self.slot(step, way)

                def body(rows):
                    total[rows, :] = total[rows, :] + slot[rows, :].astype(jnp.float32)

                each_block(self.tokens, body)

    def sent(self):
        for step in range(self.last):
            for way in (1, -1):
                beyond = self.place(way) + step < self.last
                pl.when(beyond)(lambda step=step, way=way: self.copy(step, way).wait_send())


def halved_sums(links, parts, rightward, leftward):
    return [
        LineScatter(links, parts.at[:, rows], rightward.at[:, rows], leftward.at[:, rows])
        for rows in halves(parts.shape[1])
    ]


def line_scratch(n_blk, tokens, width):
    return [pltpu.VMEM((n_blk - 1, tokens, width), jnp.bfloat16)] * 2


class PlaneScatter:
    def __init__(self, links, parts, from_core, from_x, from_y, last_x, last_y):
        self.links, self.parts = links, parts
        self.own_core_only = from_core is None
        self.from_core, self.from_x, self.from_y = from_core, from_x, from_y
        self.last_x, self.last_y = last_x, last_y
        self.core = lax.rem(links.uly, 2)
        self.row = lax.div(links.uly, 2)
        self.depth = parts.shape[3]
        self.core_copies = {}

    def chunk(self, dp, row, core, half=None):
        if self.own_core_only:
            part = self.parts.at[dp, row]
        else:
            part = self.parts.at[dp, :, row * 2 + core]
        if half is None:
            return part
        depth = self.depth // 2
        return part.at[:, pl.ds(half * depth, depth)]

    def add(self, target, source):
        blocks, depth, _ = target.shape
        rows = 32 if depth % 32 == 0 else 16

        def body(index, carry):
            block = lax.div(index, depth // rows)
            at = pl.ds(pl.multiple_of(lax.rem(index, depth // rows) * rows, rows), rows)
            target[block, at, :] = target[block, at, :] + source[block, at, :]
            return carry

        lax.fori_loop(0, blocks * (depth // rows), body, 0)

    def between_cores(self, which):
        links = self.links
        dp = links.dp if which == 1 else links.other_dp
        self.core_copies[which] = [
            links.to(
                self.chunk(dp, row, 1 - self.core), self.from_core.at[which, row], links.core_way
            )
            for row in range(2)
        ]

    def core_sums(self, which):
        links = self.links
        dp = links.dp if which == 1 else links.other_dp
        for row in range(2):
            self.core_copies[which][row].arrived()
            self.add(self.chunk(dp, row, self.core), self.from_core.at[which, row])

    def across_chips(self):
        links = self.links
        if not self.own_core_only:
            self.core_sums(0)
        self.x_copies = [
            links.to(
                self.chunk(links.other_dp, row, self.core, 0), self.from_x.at[row], links.x_way
            )
            for row in range(2)
        ]
        if not self.own_core_only:
            self.core_sums(1)
        self.y_copies = [
            links.to(
                self.chunk(group, 1 - self.row, self.core, 1),
                self.from_y.at[group],
                links.y_way,
            )
            for group in range(links.n_dp)
        ]

    def second_way(self):
        links = self.links
        for row in range(2):
            self.x_copies[row].arrived()
            self.add(self.chunk(links.dp, row, self.core, 0), self.from_x.at[row])
        self.y_last = links.to(
            self.chunk(links.dp, 1 - self.row, self.core, 0), self.last_y, links.y_way
        )
        for group in range(links.n_dp):
            self.y_copies[group].arrived()
            self.add(self.chunk(group, self.row, self.core, 1), self.from_y.at[group])
        self.x_last = links.to(
            self.chunk(links.other_dp, self.row, self.core, 1), self.last_x, links.x_way
        )

    def result(self, write):
        links = self.links
        for half, copy, source in ((0, self.y_last, self.last_y), (1, self.x_last, self.last_x)):
            copy.arrived()
            own = self.chunk(links.dp, self.row, self.core, half)
            blocks, depth, _ = source.shape
            rows = 32 if depth % 32 == 0 else 16

            def body(index, carry, own=own, source=source, half=half, depth=depth, rows=rows):
                block = lax.div(index, depth // rows)
                start = pl.multiple_of(lax.rem(index, depth // rows) * rows, rows)
                at = pl.ds(start, rows)
                value = own[block, at, :].astype(jnp.float32)
                value = value + source[block, at, :].astype(jnp.float32)
                write(block, pl.ds(pl.multiple_of(start + half * depth, rows), rows), value)
                return carry

            lax.fori_loop(0, blocks * (depth // rows), body, 0)


def plane_shapes(n_dp, blocks, n_uly, depth, width):
    return [
        (n_dp, blocks, n_uly, depth, width),
        (n_dp, 2, blocks, depth, width),
        (2, blocks, depth // 2, width),
        (n_dp, blocks, depth // 2, width),
        (blocks, depth // 2, width),
        (blocks, depth // 2, width),
    ]


def plane_scratch(*sizes):
    return [pltpu.VMEM(shape, jnp.bfloat16) for shape in plane_shapes(*sizes)]


def weight_grad(left, right, parts, dp):
    _, blocks, n_uly, depth, width = parts.shape
    columns, count = 512, blocks * n_uly * depth
    rows = left[:, pl.ds(pl.multiple_of(dp * count, 128), count)].T

    def body(index, carry):
        at = pl.ds(pl.multiple_of(index * columns, columns), columns)
        part = jnp.dot(rows, right[:, at], preferred_element_type=jnp.float32)
        parts[dp, :, :, :, at] = part.astype(jnp.bfloat16).reshape(blocks, n_uly, depth, columns)
        return carry

    lax.fori_loop(0, width // columns, body, 0)


def turned(rows, cosine, sine):
    return rows * cosine + pltpu.roll(rows, HEAD_SIZE // 2, axis=1) * sine


def transposed_product(left, right):
    return lax.dot_general(
        left, right, (((0,), (0,)), ((), ())), preferred_element_type=jnp.float32
    )


def product_right(left, right):
    return lax.dot_general(
        left, right, (((1,), (1,)), ((), ())), preferred_element_type=jnp.float32
    )


SCORE_SCALE = 1.0 / math.sqrt(HEAD_SIZE)


def mask_scores(bias, query_pos, key_pos):
    size = bias.shape[0] // 4

    def body(index, carry):
        rows = pl.ds(pl.multiple_of(index * size, size), size)
        bias[rows, :] = jnp.where(query_pos[...] >= key_pos[rows, :], 0.0, -1e30)
        return carry

    lax.fori_loop(0, 4, body, 0)


class RowBlocks:
    def __init__(self, n_blk, seqs, toks):
        self.n_blk, self.seqs, self.toks = n_blk, seqs, toks

    def each(self, body):
        def step(index, carry):
            blk, seq = lax.div(index, self.seqs), lax.rem(index, self.seqs)
            body(
                seq,
                pl.ds(pl.multiple_of(index * self.toks, self.toks), self.toks),
                pl.multiple_of(blk * self.toks, self.toks),
            )
            return carry

        lax.fori_loop(0, self.n_blk * self.seqs, step, 0)


def attention_kernel(
    wg,
    wu,
    _,
    hidden,
    w_qkv,
    gain,
    q_gain,
    k_gain,
    cosine,
    sine,
    query_pos,
    key_pos,
    rows_wg,
    rows_wu,
    all_cot,
    heads,
    normed,
    qkv,
    queries,
    key_values,
    lse,
    bias,
    send,
    recv,
    here,
):
    links = Links(send, recv, here)
    links.greet(links.peers() + [links.y_way, links.core_way])
    swap = ColumnSwap(links, [(wg, rows_wg, 0), (wu, rows_wu, 0)])
    swap.start()
    line = HalvedLine(links, None, all_cot)
    line.send(1)

    def norm(rows):
        source = hidden[rows, :].astype(jnp.float32)
        normed[rows, :] = (source * rms_scale(source) * gain[...]).astype(jnp.bfloat16)

    each_block(hidden.shape[0], norm)
    for column in range(0, qkv.shape[1], 256):
        qkv[:, column : column + 256] = jnp.dot(
            normed[...], w_qkv[:, column : column + 256], preferred_element_type=jnp.float32
        )
    seqs, kv_heads, q_rows, _ = queries.shape
    q_len = key_values.shape[4]
    group = q_rows // q_len
    blocks = RowBlocks(links.n_blk, seqs, q_len // links.n_blk)
    q_end = kv_heads * group * HEAD_SIZE
    k_end = q_end + kv_heads * HEAD_SIZE

    def place_keys(seq, rows, start):
        at = pl.ds(start, blocks.toks)
        for head in range(kv_heads):
            k_pre = qkv[rows, q_end + head * HEAD_SIZE : q_end + (head + 1) * HEAD_SIZE]
            k_row = turned(k_pre * rms_scale(k_pre) * k_gain[...], cosine[at, :], sine[at, :])
            v_row = qkv[rows, k_end + head * HEAD_SIZE : k_end + (head + 1) * HEAD_SIZE]
            key_values[links.uly, 0, seq, head, at, :] = k_row.astype(jnp.bfloat16)
            key_values[links.uly, 1, seq, head, at, :] = v_row.astype(jnp.bfloat16)

    blocks.each(place_keys)
    mine = key_values.at[links.uly]
    kv_core = links.to(mine, mine, links.core_way)
    kv_across = links.to(mine, mine, links.y_way)

    def place_queries(seq, rows, start):
        at = pl.ds(start, blocks.toks)
        for head in range(kv_heads * group):
            q_pre = qkv[rows, head * HEAD_SIZE : (head + 1) * HEAD_SIZE]
            q_row = turned(q_pre * rms_scale(q_pre) * q_gain[...], cosine[at, :], sine[at, :])
            to = pl.ds((head % group) * q_len + start, blocks.toks)
            queries[seq, head // group, to, :] = q_row.astype(jnp.bfloat16)

    blocks.each(place_queries)
    mask_scores(bias, query_pos, key_pos)
    kv_across.arrived()
    theirs = key_values.at[links.across]
    kv_last = links.to(theirs, theirs, links.core_way)
    kv_core.arrived()
    kv_last.arrived()

    def attend(seq, head):
        def over_keys(piece, carry):
            total, mixed = carry
            rows = pl.ds(pl.multiple_of(piece * q_len, q_len), q_len)
            scores = product_right(key_values[piece, 0, seq, head], queries[seq, head])
            weights = jnp.exp(scores * SCORE_SCALE + bias[rows, :])
            total = total + jnp.sum(weights, axis=0, keepdims=True)
            mixed = mixed + transposed_product(
                key_values[piece, 1, seq, head], weights.astype(jnp.bfloat16)
            )
            return total, mixed

        total, mixed = lax.fori_loop(
            0,
            links.n_uly,
            over_keys,
            (
                jnp.zeros((1, q_rows), jnp.float32),
                jnp.zeros((HEAD_SIZE, q_rows), jnp.float32),
            ),
        )
        lse[seq * kv_heads + head] = jnp.log(total)
        attended = (mixed / total).T.astype(jnp.bfloat16)
        for member in range(group):
            column = (head * group + member) * HEAD_SIZE
            for blk in range(links.n_blk):
                row = (blk * seqs + seq) * blocks.toks
                start = member * q_len + blk * blocks.toks
                heads[row : row + blocks.toks, column : column + HEAD_SIZE] = attended[
                    start : start + blocks.toks, :
                ]

    for seq in range(seqs):
        for head in range(kv_heads):
            attend(seq, head)
    swap.arrived()
    line.arrived()
    links.finish()


def attend_forward(
    wg, wu, all_cot, hidden, w_qkv, gain, q_gain, k_gain, cosine, sine, query_pos, key_pos, seqs
):
    _, n_blk, n_uly = (lax.axis_size(a) for a in EVERY)
    rows = hidden.shape[0]
    kv_heads = KEY_VALUE_HEADS // n_blk
    q_len, q_rows = rows // seqs, query_pos.shape[1]
    low = [
        (n_blk, wg.shape[0], wg.shape[1] // n_blk),
        (n_blk, wu.shape[0], wu.shape[1] // n_blk),
        all_cot.shape,
        (rows, QUERY_HEADS // n_blk * HEAD_SIZE),
        hidden.shape,
    ]
    shapes = [jax.ShapeDtypeStruct(s, jnp.bfloat16) for s in low] + [
        jax.ShapeDtypeStruct((rows, w_qkv.shape[1]), jnp.float32),
        jax.ShapeDtypeStruct((seqs, kv_heads, q_rows, HEAD_SIZE), jnp.bfloat16),
        jax.ShapeDtypeStruct((n_uly, 2, seqs, kv_heads, q_len, HEAD_SIZE), jnp.bfloat16),
        jax.ShapeDtypeStruct((seqs * kv_heads, 1, q_rows), jnp.float32),
    ]
    return pl.pallas_call(
        attention_kernel,
        out_shape=shapes,
        in_specs=[HBM] * 3 + [VMEM] * 9,
        out_specs=[HBM] * 3 + [VMEM] * 6,
        input_output_aliases={2: 2},
        scratch_shapes=[pltpu.VMEM((key_pos.shape[0], q_rows), jnp.float32)] + semaphores(32),
        compiler_params=kernel_params(1),
    )(
        wg,
        wu,
        all_cot,
        hidden,
        w_qkv,
        gain,
        q_gain,
        k_gain,
        cosine,
        sine,
        query_pos,
        key_pos,
    )


def attention_back_kernel(
    all_low,
    wo,
    queries,
    key_values,
    lse,
    qkv,
    q_gain,
    k_gain,
    cosine,
    sine,
    query_pos,
    key_pos,
    grad_gate,
    grad_up,
    part_down,
    grad_qkv,
    gain_terms,
    grad_down,
    gate_rows,
    up_rows,
    bias,
    grad_heads,
    grad_rows,
    probs,
    grad_probs,
    grad_kv,
    from_core,
    from_across,
    down_1,
    down_3,
    down_4,
    down_5,
    down_6,
    send,
    recv,
    here,
):
    links = Links(send, recv, here)
    links.greet(links.peers() + [links.x_way, links.y_way, links.core_way])
    down = PlaneScatter(links, down_1, None, down_3, down_4, down_5, down_6)
    links.local(part_down, down_1).wait()
    down.across_chips()
    swapped, keep = [], []
    for source, target in ((grad_gate, gate_rows), (grad_up, up_rows)):
        for step in range(1, links.n_blk):
            peer = links.peer(step)
            swapped.append(
                links.to(source.at[peer], target.at[links.blk], (links.dp, peer, links.uly))
            )
        keep.append(links.local(source.at[links.blk], target.at[links.blk]))
    grad_heads[...] = product_right(all_low[...], wo[...])
    mask_scores(bias, query_pos, key_pos)
    seqs, kv_heads, q_rows, _ = queries.shape
    q_len = key_values.shape[4]
    group = q_rows // q_len
    blocks = RowBlocks(links.n_blk, seqs, q_len // links.n_blk)
    q_end = kv_heads * group * HEAD_SIZE
    k_end = q_end + kv_heads * HEAD_SIZE
    gain_terms[...] = jnp.zeros_like(gain_terms)

    def gather_rows(seq, rows, start):
        for head in range(kv_heads * group):
            to = pl.ds((head % group) * q_len + start, blocks.toks)
            grad_rows[seq, head // group, to, :] = grad_heads[
                rows, head * HEAD_SIZE : (head + 1) * HEAD_SIZE
            ].astype(jnp.bfloat16)

    blocks.each(gather_rows)

    def back_norm(upstream, pre, gain, at, which):
        upstream = turned(upstream, cosine[at, :], -sine[at, :])
        back, term = back_rows(upstream, pre, gain[...])
        gain_terms[which : which + 1, :] += term
        return back.astype(jnp.bfloat16)

    def back(seq, head):
        def first(piece, delta):
            rows = pl.ds(pl.multiple_of(piece * q_len, q_len), q_len)
            scores = product_right(key_values[piece, 0, seq, head], queries[seq, head])
            prob = jnp.exp(
                scores * SCORE_SCALE + bias[rows, :] - lse[seq * kv_heads + head]
            )
            grad_prob = product_right(key_values[piece, 1, seq, head], grad_rows[seq, head])
            probs[rows, :] = prob
            grad_probs[rows, :] = grad_prob
            return delta + jnp.sum(prob * grad_prob, axis=0, keepdims=True)

        delta = lax.fori_loop(0, links.n_uly, first, jnp.zeros((1, q_rows), jnp.float32))

        def second(piece, grad_query):
            rows = pl.ds(pl.multiple_of(piece * q_len, q_len), q_len)
            prob = probs[rows, :]
            grad_score = (prob * (grad_probs[rows, :] - delta)).astype(jnp.bfloat16)
            grad_kv[seq, piece, 0, head] = (
                SCORE_SCALE
                * jnp.dot(grad_score, queries[seq, head], preferred_element_type=jnp.float32)
            ).astype(jnp.bfloat16)
            grad_kv[seq, piece, 1, head] = jnp.dot(
                prob.astype(jnp.bfloat16),
                grad_rows[seq, head],
                preferred_element_type=jnp.float32,
            ).astype(jnp.bfloat16)
            return grad_query + transposed_product(key_values[piece, 0, seq, head], grad_score)

        grad_query = lax.fori_loop(
            0, links.n_uly, second, jnp.zeros((HEAD_SIZE, q_rows), jnp.float32)
        )
        grad_heads[:, :HEAD_SIZE] = (grad_query * SCORE_SCALE).T
        for member in range(group):
            column = (head * group + member) * HEAD_SIZE
            for blk in range(links.n_blk):
                row = (blk * seqs + seq) * blocks.toks
                at = pl.ds(blk * blocks.toks, blocks.toks)
                start = member * q_len + blk * blocks.toks
                grad_qkv[row : row + blocks.toks, column : column + HEAD_SIZE] = back_norm(
                    grad_heads[start : start + blocks.toks, :HEAD_SIZE],
                    qkv[row : row + blocks.toks, column : column + HEAD_SIZE],
                    q_gain,
                    at,
                    0,
                )

    core, line = lax.rem(links.uly, 2), lax.div(links.uly, 2)

    def add(target, source):
        for kind in range(2):
            for head in range(kv_heads):
                target[kind, head] = target[kind, head] + source[kind, head]

    def core_sums(seq):
        copies = [
            links.to(
                grad_kv.at[seq, row * 2 + 1 - core], from_core.at[seq, row], links.core_way
            )
            for row in range(2)
        ]
        return copies

    def across_sums(seq, copies):
        for row in range(2):
            copies[row].arrived()
            add(grad_kv.at[seq, row * 2 + core], from_core.at[seq, row])
        return links.to(
            grad_kv.at[seq, (1 - line) * 2 + core], from_across.at[seq], links.y_way
        )

    def own_keys(seq, copy):
        copy.arrived()
        for head in range(kv_heads):
            for blk in range(links.n_blk):
                row = (blk * seqs + seq) * blocks.toks
                at = pl.ds(blk * blocks.toks, blocks.toks)
                term = [
                    grad_kv[seq, links.uly, kind, head, at, :].astype(jnp.float32)
                    + from_across[seq, kind, head, at, :].astype(jnp.float32)
                    for kind in range(2)
                ]
                k_at = q_end + head * HEAD_SIZE
                v_at = k_end + head * HEAD_SIZE
                grad_qkv[row : row + blocks.toks, k_at : k_at + HEAD_SIZE] = back_norm(
                    term[0],
                    qkv[row : row + blocks.toks, k_at : k_at + HEAD_SIZE],
                    k_gain,
                    at,
                    1,
                )
                grad_qkv[row : row + blocks.toks, v_at : v_at + HEAD_SIZE] = term[1].astype(
                    jnp.bfloat16
                )

    stage, last = None, []
    for seq in range(seqs):
        for head in range(kv_heads):
            back(seq, head)
            if seq == 0 and head == kv_heads - 1:
                down.second_way()
            if stage is not None:
                last.append((seq - 1, across_sums(seq - 1, stage)))
                stage = None
        stage = core_sums(seq)
    last.append((seqs - 1, across_sums(seqs - 1, stage)))
    for seq, copy in last:
        own_keys(seq, copy)

    def write(block, rows, values):
        grad_down[block, rows, :] = values

    down.result(write)
    for copy in keep:
        copy.wait()
    for copy in swapped:
        copy.arrived()
    links.finish()


def attend_back(
    all_low,
    wo,
    queries,
    key_values,
    lse,
    qkv,
    q_gain,
    k_gain,
    cosine,
    sine,
    query_pos,
    key_pos,
    grad_gate,
    grad_up,
    part_down,
):
    seqs, kv_heads, q_rows, _ = queries.shape
    n_uly, _, _, _, q_len, _ = key_values.shape
    rows = all_low.shape[0]
    keys = key_pos.shape[0]
    f32, low = jnp.float32, jnp.bfloat16
    scratch = [
        ((keys, q_rows), f32),
        ((rows, wo.shape[0]), f32),
        (queries.shape, low),
        ((keys, q_rows), f32),
        ((keys, q_rows), f32),
        ((seqs, n_uly, 2, kv_heads, q_len, HEAD_SIZE), low),
        ((seqs, 2, 2, kv_heads, q_len, HEAD_SIZE), low),
        ((seqs, 2, kv_heads, q_len, HEAD_SIZE), low),
        (part_down.shape, low),
    ]
    n_dp, _, _, depth, width = part_down.shape
    scratch += [(shape, low) for shape in plane_shapes(n_dp, 1, n_uly, depth, width)[2:]]
    return pl.pallas_call(
        attention_back_kernel,
        out_shape=[
            jax.ShapeDtypeStruct(qkv.shape, low),
            jax.ShapeDtypeStruct((8, HEAD_SIZE), f32),
            jax.ShapeDtypeStruct((1, depth, width), f32),
            jax.ShapeDtypeStruct(grad_gate.shape, low),
            jax.ShapeDtypeStruct(grad_up.shape, low),
        ],
        in_specs=[VMEM] * 12 + [HBM] * 3,
        out_specs=[VMEM] * 3 + [HBM] * 2,
        scratch_shapes=[pltpu.VMEM(shape, kind) for shape, kind in scratch] + semaphores(40),
        compiler_params=kernel_params(5),
    )(
        all_low,
        wo,
        queries,
        key_values,
        lse,
        qkv,
        q_gain,
        k_gain,
        cosine,
        sine,
        query_pos,
        key_pos,
        grad_gate,
        grad_up,
        part_down,
    )


def middle_kernel(
    heads,
    wo,
    source,
    gain,
    rows_wg,
    rows_wu,
    _,
    middle,
    all_normed,
    all_wg,
    all_wu,
    all_cot,
    parts,
    rightward,
    leftward,
    normed,
    send,
    recv,
    here,
):
    links = Links(send, recv, here)
    links.greet(links.peers() + [links.x_way, links.y_way, links.core_way])
    planes, keep = [], []
    for chunk, whole in ((rows_wg, all_wg), (rows_wu, all_wu)):
        at = rows_of(whole, True)
        plane = PlaneGather(links, at)
        plane.start(chunk)
        planes.append(plane)
        keep.append(links.local(chunk, at(links.dp, links.uly)))
    tokens = source.shape[0]
    for blk in (links.n_blk - 1, 0) + tuple(range(1, links.n_blk - 1)):
        parts[blk] = jnp.dot(heads[blk], wo[...], preferred_element_type=jnp.float32).astype(
            jnp.bfloat16
        )
    sums = halved_sums(links, parts, rightward, leftward)
    for half in sums:
        half.start()
    cot_line = LineGather(links, None, all_cot)
    for step in range(2, links.n_blk - 1):
        cot_line.send(step)
    lines = []

    def settle(half, rows_of_half):
        half.finish(middle.at[rows_of_half])

        def body(rows):
            at = pl.ds(pl.multiple_of(rows_of_half.start + rows.start, ROWS), ROWS)
            total = middle[at, :] + source[at, :].astype(jnp.float32)
            middle[at, :] = total
            normed[at, :] = (total * rms_scale(total) * gain[...]).astype(jnp.bfloat16)

        each_block(tokens // 2, body)
        line = LineGather(links, normed.at[rows_of_half], all_normed.at[:, rows_of_half])
        line.send(0)
        lines.append(line)

    spans = halves(tokens)
    for tick in range(1, links.n_blk - 1):
        sums[0].tick(tick)
    settle(sums[0], spans[0])
    planes[0].hand_on()
    for tick in range(1, links.n_blk - 1):
        sums[1].tick(tick)
    settle(sums[1], spans[1])
    cot_line.arrived()
    keep.append(links.local(normed, all_normed.at[links.blk]))
    for step in range(1, links.n_blk - 1):
        for line in lines:
            line.arrived()
            line.send(step)
        if step == 1:
            planes[1].hand_on()
        if step == 2:
            planes[0].last()
    planes[1].last()
    for line in lines:
        line.arrived()
    for plane in planes:
        plane.arrived()
    for copy in keep:
        copy.wait()
    for half in sums:
        half.sent()
    links.finish()


def exchange_middle(heads, wo, source, gain, rows_wg, rows_wu, all_cot):
    n_dp, n_blk, n_uly = (lax.axis_size(a) for a in EVERY)
    tokens, width = source.shape
    low = [(n_blk, tokens, width)]
    low += [(n_dp, n_blk, n_uly) + chunk.shape[1:] for chunk in (rows_wg, rows_wu)]
    low.append(all_cot.shape)
    return pl.pallas_call(
        middle_kernel,
        out_shape=[jax.ShapeDtypeStruct((tokens, width), jnp.float32)]
        + [jax.ShapeDtypeStruct(shape, jnp.bfloat16) for shape in low],
        in_specs=[VMEM] * 4 + [HBM] * 3,
        out_specs=[VMEM] + [HBM] * 4,
        input_output_aliases={6: 4},
        scratch_shapes=[pltpu.VMEM((n_blk, tokens, width), jnp.bfloat16)]
        + line_scratch(n_blk, tokens, width)
        + [pltpu.VMEM((tokens, width), jnp.bfloat16)]
        + semaphores(64),
        compiler_params=kernel_params(2),
    )(heads, wo, source, gain, rows_wg, rows_wu, all_cot)


def back_rows(grad_normed, source, gain):
    scale = rms_scale(source)
    unit = source * scale
    scaled = grad_normed * gain
    back = scale * (scaled - unit * jnp.mean(scaled * unit, axis=-1, keepdims=True))
    return back, jnp.sum(grad_normed * unit, axis=0, keepdims=True)


def back_kernel(
    grad_parts,
    out_parts,
    middle,
    cotangent,
    gain,
    all_normed,
    grad_gate_pre,
    grad_up_pre,
    activated,
    all_cot,
    output,
    grad_middle,
    gain_term,
    all_low,
    grad_gate,
    grad_up,
    part_down,
    rightward,
    leftward,
    out_right,
    out_left,
    out_total,
    low,
    gate_1,
    gate_2,
    gate_3,
    gate_4,
    gate_5,
    gate_6,
    up_1,
    up_2,
    up_3,
    up_4,
    up_5,
    up_6,
    down_1,
    down_2,
    send,
    recv,
    here,
):
    links = Links(send, recv, here)
    links.greet(links.peers() + [links.x_way, links.y_way, links.core_way])
    sums = halved_sums(links, grad_parts, rightward, leftward)
    for half in sums:
        half.start()
    out_sums = halved_sums(links, out_parts, out_right, out_left)
    gate = PlaneScatter(links, gate_1, gate_2, gate_3, gate_4, gate_5, gate_6)
    up = PlaneScatter(links, up_1, up_2, up_3, up_4, up_5, up_6)
    down = PlaneScatter(links, down_1, down_2, None, None, None, None)
    gain_term[...] = jnp.zeros_like(gain_term)
    tokens = middle.shape[0]
    spans, lines, keep = halves(tokens), [], []

    def compute(plane, which, left, right):
        dp = links.dp if which == 1 else links.other_dp
        weight_grad(left, right, plane.parts, dp)
        plane.between_cores(which)

    def settle(half, rows_of_half):
        half.finish(grad_middle.at[rows_of_half])

        def body(rows):
            at = pl.ds(pl.multiple_of(rows_of_half.start + rows.start, ROWS), ROWS)
            back, term = back_rows(grad_middle[at, :], middle[at, :], gain[...])
            grad = cotangent[at, :].astype(jnp.float32) + back
            gain_term[...] += term
            grad_middle[at, :] = grad
            low[at, :] = grad.astype(jnp.bfloat16)

        each_block(tokens // 2, body)
        line = LineGather(links, low.at[rows_of_half], all_low.at[:, rows_of_half])
        line.send(0)
        lines.append(line)

    ticks = range(1, links.n_blk - 1)
    compute(gate, 0, all_normed, grad_gate_pre)
    compute(gate, 1, all_normed, grad_gate_pre)
    for tick in ticks:
        sums[0].tick(tick)
        if tick == 1:
            gate.across_chips()
    compute(up, 0, all_normed, grad_up_pre)
    settle(sums[0], spans[0])
    compute(up, 1, all_normed, grad_up_pre)
    for tick in ticks:
        sums[1].tick(tick)
        if tick == 1:
            up.across_chips()
            compute(down, 0, activated, all_cot)
    compute(down, 1, activated, all_cot)
    settle(sums[1], spans[1])
    for half in out_sums:
        half.start()
    keep.append(links.local(low, all_low.at[links.blk]))
    gate.second_way()
    for step in range(1, links.n_blk - 1):
        for line in lines:
            line.arrived()
            line.send(step)
        if step == 1:
            for which in (0, 1):
                down.core_sums(which)
            for dp in range(links.n_dp):
                for row in range(2):
                    keep.append(
                        links.local(down.chunk(dp, row, down.core), part_down.at[dp, row])
                    )
            up.second_way()
        for half in out_sums:
            half.tick(step)
    for line in lines:
        line.arrived()

    def into(target):
        def write(block, rows, values):
            target[block, rows, :] = values.astype(target.dtype)

        return write

    gate.result(into(grad_gate))
    for half, rows_of_half in zip(out_sums, spans):
        half.finish(out_total.at[rows_of_half])

    def add_output(rows):
        output[rows, :] = (middle[rows, :] + out_total[rows, :]).astype(jnp.bfloat16)

    each_block(tokens, add_output)
    up.result(into(grad_up))
    for copy in keep:
        copy.wait()
    for half in sums + out_sums:
        half.sent()
    links.finish()


def exchange_back(
    grad_parts,
    out_parts,
    middle,
    cotangent,
    gain,
    all_normed,
    grad_gate_pre,
    grad_up_pre,
    activated,
    all_cot,
):
    n_dp, n_blk, n_uly = (lax.axis_size(a) for a in EVERY)
    _, tokens, width = grad_parts.shape
    ff = grad_gate_pre.shape[1]
    depth = width // (n_dp * n_blk * n_uly)
    down_depth = ff // (n_dp * n_uly)
    return pl.pallas_call(
        back_kernel,
        out_shape=[
            jax.ShapeDtypeStruct((tokens, width), jnp.bfloat16),
            jax.ShapeDtypeStruct((tokens, width), jnp.float32),
            jax.ShapeDtypeStruct((1, width), jnp.float32),
            jax.ShapeDtypeStruct((n_blk, tokens, width), jnp.bfloat16),
            jax.ShapeDtypeStruct((n_blk, depth, ff), jnp.bfloat16),
            jax.ShapeDtypeStruct((n_blk, depth, ff), jnp.bfloat16),
            jax.ShapeDtypeStruct((n_dp, 2, 1, down_depth, width), jnp.bfloat16),
        ],
        in_specs=[VMEM] * 10,
        out_specs=[VMEM, VMEM, VMEM, HBM, VMEM, VMEM, HBM],
        scratch_shapes=line_scratch(n_blk, tokens, width) * 2
        + [pltpu.VMEM((tokens, width), jnp.float32), pltpu.VMEM((tokens, width), jnp.bfloat16)]
        + plane_scratch(n_dp, n_blk, n_uly, depth, ff) * 2
        + plane_scratch(n_dp, 1, n_uly, down_depth, width)[:2]
        + semaphores(72),
        compiler_params=kernel_params(3),
    )(
        grad_parts,
        out_parts,
        middle,
        cotangent,
        gain,
        all_normed,
        grad_gate_pre,
        grad_up_pre,
        activated,
        all_cot,
    )


def last_kernel(
    w_qkv,
    hidden,
    grad_middle,
    gain,
    normed,
    grad_qkv,
    heads,
    all_low,
    mlp_term,
    head_terms,
    grad_hidden,
    grad_w_qkv,
    grad_wo,
    small_sum,
    grad_parts,
    rightward,
    leftward,
    qkv_1,
    qkv_2,
    qkv_3,
    qkv_4,
    qkv_5,
    qkv_6,
    wo_1,
    wo_2,
    wo_3,
    wo_4,
    wo_5,
    wo_6,
    summed,
    small,
    attn_term,
    small_in,
    small_total,
    send,
    recv,
    here,
):
    links = Links(send, recv, here)
    links.greet(links.peers() + [links.x_way, links.y_way, links.core_way])
    sums = halved_sums(links, grad_parts, rightward, leftward)
    qkv = PlaneScatter(links, qkv_1, qkv_2, qkv_3, qkv_4, qkv_5, qkv_6)
    out = PlaneScatter(links, wo_1, wo_2, wo_3, wo_4, wo_5, wo_6)

    attn_term[...] = jnp.zeros_like(attn_term)
    tokens = grad_parts.shape[1]
    for column in range(0, w_qkv.shape[0], 512):
        grad_parts[:, :, column : column + 512] = (
            product_right(grad_qkv[...], w_qkv[column : column + 512, :])
            .astype(jnp.bfloat16)
            .reshape(links.n_blk, tokens, 512)
        )
    for half in sums:
        half.start()
    for which, dp in ((0, links.other_dp), (1, links.dp)):
        weight_grad(normed, grad_qkv, qkv_1, dp)
        qkv.between_cores(which)

    def collect(rows):
        for blk in range(links.n_blk):
            source = hidden[blk, rows, :].astype(jnp.float32)
            part = grad_parts[blk, rows, :].astype(jnp.float32)
            attn_term[...] += jnp.sum(part * (source * rms_scale(source)), axis=0, keepdims=True)

    sums[0].tick(1)
    each_block(tokens, collect)
    qkv.across_chips()
    for tick in range(2, links.n_blk - 1):
        sums[0].tick(tick)
    small[...] = jnp.zeros_like(small)
    span = gain.shape[1] // 128
    for index in range(span):
        columns = slice(index * 128, (index + 1) * 128)
        small[index : index + 1, :] = attn_term[:, columns]
        small[span + index : span + index + 1, :] = mlp_term[:, columns]
    small[2 * span : 2 * span + 8, :] = head_terms[...]
    small_in[links.blk] = small[...]
    small_copies = [links.to(small, small_in.at[links.blk], device) for device in links.peers()]
    for which, dp in ((0, links.other_dp), (1, links.dp)):
        weight_grad(heads, all_low, wo_1, dp)
        out.between_cores(which)
    sums[1].tick(1)
    out.across_chips()
    for copy in small_copies:
        copy.arrived()
    total = small_in[0]
    for blk in range(1, links.n_blk):
        total = total + small_in[blk]
    small_total[0] = total
    pending = links.to(small_total.at[0], small_in.at[links.n_blk], links.x_way)
    qkv.second_way()
    pending.arrived()
    small_total[1] = small_total[0] + small_in[links.n_blk]
    pending = links.to(small_total.at[1], small_in.at[links.n_blk + 1], links.y_way)
    for tick in range(2, links.n_blk - 1):
        sums[1].tick(tick)
    out.second_way()
    pending.arrived()
    small_total[2] = small_total[1] + small_in[links.n_blk + 1]
    pending = links.to(small_total.at[2], small_in.at[links.n_blk + 2], links.core_way)

    def write(block, rows, values):
        summed[block, rows, :] = values.astype(jnp.bfloat16)

    qkv.result(write)
    swapped = []
    for step in range(1, links.n_blk):
        peer = links.peer(step)
        swapped.append(
            links.to(summed.at[peer], grad_w_qkv.at[links.blk], (links.dp, peer, links.uly))
        )
    keep = links.local(summed.at[links.blk], grad_w_qkv.at[links.blk])
    pending.arrived()
    small_sum[...] = small_total[2] + small_in[links.n_blk + 2]
    for half, rows_of_half in zip(sums, halves(tokens)):
        half.finish(grad_hidden.at[rows_of_half])

    def body(rows):
        back, _ = back_rows(
            grad_hidden[rows, :], hidden[links.blk, rows, :].astype(jnp.float32), gain[...]
        )
        grad_hidden[rows, :] = grad_middle[rows, :] + back

    each_block(tokens, body)

    def write_out(block, rows, values):
        grad_wo[block, rows, :] = values

    out.result(write_out)
    for copy in swapped:
        copy.arrived()
    keep.wait()
    for half in sums:
        half.sent()
    links.finish()


def exchange_last(
    w_qkv,
    hidden,
    grad_middle,
    gain,
    normed,
    grad_qkv,
    heads,
    all_low,
    mlp_term,
    head_terms,
):
    n_dp, n_blk, n_uly = (lax.axis_size(a) for a in EVERY)
    _, tokens, width = hidden.shape
    columns = grad_qkv.shape[1]
    depth = width // (n_dp * n_blk * n_uly)
    out_depth = heads.shape[1] // (n_dp * n_uly)
    small = (2 * width // 128 + 8, 128)
    return pl.pallas_call(
        last_kernel,
        out_shape=[
            jax.ShapeDtypeStruct((tokens, width), jnp.float32),
            jax.ShapeDtypeStruct((n_blk, depth, columns), jnp.bfloat16),
            jax.ShapeDtypeStruct((1, out_depth, width), jnp.float32),
            jax.ShapeDtypeStruct(small, jnp.float32),
        ],
        in_specs=[VMEM] * 10,
        out_specs=[VMEM, HBM, VMEM, VMEM],
        scratch_shapes=[pltpu.VMEM((n_blk, tokens, width), jnp.bfloat16)]
        + line_scratch(n_blk, tokens, width)
        + plane_scratch(n_dp, n_blk, n_uly, depth, columns)
        + plane_scratch(n_dp, 1, n_uly, out_depth, width)
        + [
            pltpu.VMEM((n_blk, depth, columns), jnp.bfloat16),
            pltpu.VMEM(small, jnp.float32),
            pltpu.VMEM((1, width), jnp.float32),
            pltpu.VMEM((n_blk + 3,) + small, jnp.float32),
            pltpu.VMEM((3,) + small, jnp.float32),
        ]
        + semaphores(64),
        compiler_params=kernel_params(4),
    )(
        w_qkv,
        hidden,
        grad_middle,
        gain,
        normed,
        grad_qkv,
        heads,
        all_low,
        mlp_term,
        head_terms,
    )


def finish_kernel(
    gate,
    up,
    qkv,
    wo,
    wd,
    hidden,
    out,
    small,
    f_gate,
    f_up,
    f_q,
    f_k,
    f_v,
    f_wo,
    f_wd,
    f_hidden,
    f_out,
    f_attn,
    f_mlp,
):
    n_blk, depth, _ = gate.shape

    def place(source, offset, target):
        width = target.shape[1] // (n_blk * 2)
        for blk in range(n_blk):
            for group in range(2):
                to = (group * n_blk + blk) * width
                at = offset + group * width
                target[:, to : to + width] = source[blk, :, at : at + width].astype(jnp.float32)

    place(gate, 0, f_gate)
    place(up, 0, f_up)
    q_width = f_q.shape[1] // n_blk
    k_width = f_k.shape[1] // n_blk
    place(qkv, 0, f_q)
    place(qkv, q_width, f_k)
    place(qkv, q_width + k_width, f_v)
    f_wo[...] = wo[0]
    f_wd[...] = wd[0]
    f_hidden[...] = hidden[...]
    f_out[...] = out[...]
    size = f_attn.shape[1]
    device = (lax.axis_index(DP) * n_blk + lax.axis_index(BLK)) * lax.axis_size(ULY)
    device = device + lax.axis_index(ULY)
    per_row = 128 // size
    span = (2 * n_blk * lax.axis_size(ULY)) // per_row
    for first, target in ((0, f_attn), (span, f_mlp)):
        row = small[pl.ds(first + lax.div(device, per_row), 1), :]
        value = row[:, :size]
        for place_in_row in range(1, per_row):
            here = lax.rem(device, per_row) == place_in_row
            value = jnp.where(
                here, row[:, place_in_row * size : (place_in_row + 1) * size], value
            )
        target[...] = value


def finish(gate, up, qkv, wo, wd, hidden, out, small, gain_rows, shapes):
    return pl.pallas_call(
        finish_kernel,
        out_shape=[jax.ShapeDtypeStruct(shape, jnp.float32) for shape in shapes]
        + [
            jax.ShapeDtypeStruct(wo.shape[1:], jnp.float32),
            jax.ShapeDtypeStruct(wd.shape[1:], jnp.float32),
            jax.ShapeDtypeStruct(hidden.shape, jnp.float32),
            jax.ShapeDtypeStruct(out.shape, jnp.bfloat16),
            jax.ShapeDtypeStruct((1, gain_rows), jnp.float32),
            jax.ShapeDtypeStruct((1, gain_rows), jnp.float32),
        ],
        in_specs=[VMEM] * 8,
        out_specs=[VMEM] * 11,
        compiler_params=pltpu.CompilerParams(vmem_limit_bytes=62 * MIB),
    )(gate, up, qkv, wo, wd, hidden, out, small)


def product(left, right):
    return jnp.dot(left, right, preferred_element_type=jnp.float32)


def shards(
    hidden,
    span_order,
    attn_gain,
    w_query,
    key_weight,
    value_weight,
    w_out,
    q_gain,
    k_gain,
    mlp_gain,
    w_gate,
    w_up,
    w_down,
    cotangent,
):
    seqs, toks, width = hidden.shape
    n_dp, n_blk, n_uly = (lax.axis_size(a) for a in EVERY)
    blk_index = lax.axis_index(BLK)
    uly_index = lax.axis_index(ULY)
    group = QUERY_HEADS // KEY_VALUE_HEADS
    half_len = toks * n_uly // 2
    rows = n_blk * seqs * toks
    f32, bf16 = jnp.float32, jnp.bfloat16
    own_hidden = hidden.reshape(seqs * toks, width)
    own_cotangent = cotangent.reshape(seqs * toks, width)

    def positions(u):
        places = (
            jnp.arange(n_blk, dtype=jnp.int32)[:, None] * n_uly + u
        ) * toks + jnp.arange(toks, dtype=jnp.int32)[None, :]
        return positions_of(places.reshape(-1), span_order, half_len)

    own_pos = positions(uly_index)
    query_pos = jnp.tile(own_pos, group)[None, :]
    key_pos = jnp.concatenate([positions(u) for u in range(n_uly)])[:, None]
    angles = angles_of(own_pos, HEAD_SIZE)
    cosine, sine = jnp.cos(angles), jnp.sin(angles)
    cosine = jnp.concatenate([cosine, cosine], axis=1)
    sine = jnp.concatenate([-sine, sine], axis=1)
    gain_q, gain_k = q_gain.astype(f32)[None, :], k_gain.astype(f32)[None, :]

    gain_rows = attn_gain.shape[0]
    own_gains = jnp.pad(jnp.stack([attn_gain, mlp_gain]), ((0, 14), (0, 128 - gain_rows)))
    all_hidden, w_qkv, wo, all_wd, all_gains, cot = gather_front(
        own_hidden,
        w_query,
        key_weight,
        value_weight,
        w_out,
        w_down,
        own_gains,
        own_cotangent,
    )
    gains = all_gains[..., :2, :gain_rows].astype(f32)
    g_attn = gains[..., 0, :].reshape(1, width)
    g_mlp = gains[..., 1, :].reshape(1, width)
    w_qkv = w_qkv.reshape(width, -1)
    wo = wo.reshape(-1, width)
    (
        rows_wg,
        rows_wu,
        cot,
        heads_flat,
        normed,
        qkv,
        queries,
        key_values,
        lse,
    ) = attend_forward(
        w_gate,
        w_up,
        cot,
        all_hidden.reshape(rows, width),
        w_qkv,
        g_attn,
        gain_q,
        gain_k,
        cosine,
        sine,
        query_pos,
        key_pos,
        seqs,
    )
    middle, normed2, all_wg, all_wu, cot = exchange_middle(
        heads_flat.reshape(n_blk, seqs * toks, -1),
        wo,
        own_hidden,
        g_mlp,
        rows_wg,
        rows_wu,
        cot,
    )
    wg, wu = all_wg.reshape(width, -1), all_wu.reshape(width, -1)
    wd = all_wd.reshape(-1, width)
    cot = cot.reshape(rows, width)
    normed2 = normed2.reshape(rows, width)
    gate_pre = product(normed2, wg)
    up_pre = product(normed2, wu)
    sigmoid_gate = jax.nn.sigmoid(gate_pre)
    activated = (gate_pre * sigmoid_gate * up_pre).astype(bf16)
    out_parts = product(activated, wd).astype(bf16)
    grad_act = product_right(cot, wd)
    grad_gate_pre = (
        grad_act * up_pre * sigmoid_gate * (1.0 + gate_pre * (1.0 - sigmoid_gate))
    ).astype(bf16)
    grad_up_pre = (grad_act * gate_pre * sigmoid_gate).astype(bf16)
    grad_parts = (product_right(grad_gate_pre, wg) + product_right(grad_up_pre, wu)).astype(bf16)
    blocks = (n_blk, seqs * toks, width)
    output, grad_middle, mlp_gain_term, middle_low, grad_gate, grad_up, part_down = exchange_back(
        grad_parts.reshape(blocks),
        out_parts.reshape(blocks),
        middle,
        own_cotangent,
        g_mlp,
        normed2,
        grad_gate_pre,
        grad_up_pre,
        activated,
        cot,
    )
    middle_low = middle_low.reshape(rows, width)
    grad_qkv, head_terms, grad_down, grad_gate, grad_up = attend_back(
        middle_low,
        wo,
        queries,
        key_values,
        lse,
        qkv,
        gain_q,
        gain_k,
        cosine,
        sine,
        query_pos,
        key_pos,
        grad_gate,
        grad_up,
        part_down,
    )
    grad_hidden, grad_w_qkv, grad_out, small = exchange_last(
        w_qkv,
        all_hidden,
        grad_middle,
        g_attn,
        normed,
        grad_qkv,
        heads_flat,
        middle_low,
        mlp_gain_term,
        head_terms,
    )
    (
        grad_gate,
        grad_up,
        grad_query,
        grad_key,
        grad_value,
        grad_out,
        grad_down,
        grad_hidden,
        output,
        grad_attn_gain,
        grad_mlp_gain,
    ) = finish(
        grad_gate,
        grad_up,
        grad_w_qkv,
        grad_out,
        grad_down,
        grad_hidden,
        output,
        small,
        gain_rows,
        [w.shape for w in (w_gate, w_up, w_query, key_weight, value_weight)],
    )
    small = small.reshape(-1)
    grad_q_gain = small[2 * width : 2 * width + HEAD_SIZE]
    grad_k_gain = small[2 * width + HEAD_SIZE : 2 * width + 2 * HEAD_SIZE]
    return (
        output.reshape(hidden.shape),
        grad_hidden.reshape(hidden.shape),
        grad_attn_gain.reshape(gain_rows),
        grad_query,
        grad_key,
        grad_value,
        grad_out,
        grad_q_gain,
        grad_k_gain,
        grad_mlp_gain.reshape(gain_rows),
        grad_gate,
        grad_up,
        grad_down,
    )


def solution(mesh):
    n_dp, n_blk, n_uly = (mesh.shape[a] for a in EVERY)
    aligned = (n_dp, n_uly) == (2, 4) and KEY_VALUE_HEADS % (n_dp * n_blk) == 0
    in_specs = (
        TOKENS,
        P(),
        P(EVERY),
        P(EVERY, None),
        P(EVERY, None),
        P(EVERY, None),
        P(EVERY, None),
        P(),
        P(),
        P(EVERY),
        P(EVERY, None),
        P(EVERY, None),
        P(EVERY, None),
        TOKENS,
    )
    out_specs = (
        TOKENS,
        TOKENS,
        P(EVERY),
        P(EVERY, None),
        P(EVERY, None),
        P(EVERY, None),
        P(EVERY, None),
        P(),
        P(),
        P(EVERY),
        P(EVERY, None),
        P(EVERY, None),
        P(EVERY, None),
    )
    return jax.shard_map(
        shards if aligned else shards_general,
        mesh=mesh, in_specs=in_specs, out_specs=out_specs, check_vma=False)
```

```python
import functools
import math

import jax
import jax.numpy as jnp
from jax import lax
from jax.experimental import pallas as pl
from jax.experimental.pallas import tpu as pltpu
from jax.sharding import PartitionSpec as P

QUERY_HEADS = 16
KEY_VALUE_HEADS = 8
HEAD_SIZE = 128


DP, BLK, ULY = "dp", "blk", "uly"
EVERY = (DP, BLK, ULY)
PLANE = (DP, ULY)
TOKENS = P(DP, (BLK, ULY), None)
EQ_KGQD_NKD_TO_KGQN = "kgqd,nkd->kgqn"
EQ_KGQN_KGQD_TO_NKD = "kgqn,kgqd->nkd"
EQ_KGQN_NKD_TO_KGQD = "kgqn,nkd->kgqd"
EQ_KGQN_QKGD_TO_NKD = "kgqn,qkgd->nkd"
EQ_QKGD_NKD_TO_KGQN = "qkgd,nkd->kgqn"
EQ_STD_DE_TO_STE = "std,de->ste"
EQ_STD_DF_TO_STF = "std,df->stf"
EQ_STD_ED_TO_STE = "std,ed->ste"
EQ_STD_FD_TO_STF = "std,fd->stf"
EQ_STD_STE_TO_DE = "std,ste->de"
EQ_STD_STF_TO_DF = "std,stf->df"
EQ_STE_DE_TO_STD = "ste,de->std"
EQ_STE_ED_TO_STD = "ste,ed->std"
EQ_STE_STD_TO_ED = "ste,std->ed"
EQ_STF_DF_TO_STD = "stf,df->std"
EQ_STF_FD_TO_STD = "stf,fd->std"
EQ_STF_STD_TO_FD = "stf,std->fd"

EPSILON = 1e-06
ROPE_BASE = 1000000.0


def rms_scale(source):
    return lax.rsqrt(jnp.mean(source * source, axis=-1, keepdims=True) + EPSILON)


def norm_back(grad_normed, source, norm_scale, gain):
    unit_rows = source * norm_scale
    scaled = grad_normed * gain
    return norm_scale * (scaled - unit_rows * jnp.mean(scaled * unit_rows, axis=-1, keepdims=True))


def angles_of(positions, head_dim):
    freq_steps = jnp.arange(head_dim // 2, dtype=jnp.float32)
    inverse = jnp.exp(freq_steps * (-2.0 * math.log(ROPE_BASE) / head_dim))
    return positions.astype(jnp.float32)[:, None] * inverse[None, :]


def rotate(source, angles, direction):
    half_dim = source.shape[-1] // 2
    cosine = jnp.cos(angles)[:, None, :]
    sine_part = direction * jnp.sin(angles)[:, None, :]
    first_half = source[..., :half_dim]
    second_half = source[..., half_dim:]
    return jnp.concatenate(
        [
            first_half * cosine - second_half * sine_part,
            second_half * cosine + first_half * sine_part,
        ],
        axis=-1,
    )


def positions_of(places, span_order, half_len):
    blocks_of = places // half_len
    block_ids = jnp.arange(span_order.shape[0], dtype=jnp.int32)
    chosen = jnp.sum(
        jnp.where(blocks_of[:, None] == block_ids[None, :], span_order[None, :], 0), axis=1
    )
    return chosen * half_len + places % half_len


def add_rows(buffer, new_rows):
    return buffer + new_rows


def shards_general(
    hidden,
    span_order,
    attn_gain,
    w_query,
    key_weight,
    value_weight,
    w_out,
    q_gain,
    k_gain,
    mlp_gain,
    w_gate,
    w_up,
    w_down,
    cotangent,
):
    sequence_count = hidden.shape[0]
    token_count = hidden.shape[1]
    ulysses_group_size = lax.axis_size(ULY)
    local_q = QUERY_HEADS // ulysses_group_size
    local_key_value = KEY_VALUE_HEADS // ulysses_group_size
    query_group_width = QUERY_HEADS // KEY_VALUE_HEADS
    block_len = token_count * ulysses_group_size
    half_len = block_len // 2
    score_scale = 1.0 / math.sqrt(HEAD_SIZE)
    blk_index = lax.axis_index(BLK)
    uly_index = lax.axis_index(ULY)
    first_place = (blk_index * ulysses_group_size + uly_index) * token_count
    local_angles = angles_of(
        positions_of(first_place + jnp.arange(token_count, dtype=jnp.int32), span_order, half_len),
        HEAD_SIZE,
    )
    query_pos = positions_of(
        blk_index * block_len + jnp.arange(block_len, dtype=jnp.int32), span_order, half_len
    )
    g_attn, wq_all, wk_all, wv_all, wo_all = (
        lax.all_gather(attn_gain, EVERY, axis=0, tiled=True),
        lax.all_gather(w_query, EVERY, axis=0, tiled=True),
        lax.all_gather(key_weight, EVERY, axis=0, tiled=True),
        lax.all_gather(value_weight, EVERY, axis=0, tiled=True),
        lax.all_gather(w_out, EVERY, axis=0, tiled=True),
    )
    source = hidden.astype(jnp.float32)
    first_scale = rms_scale(source)
    normalized_input = (source * first_scale * g_attn.astype(jnp.float32)).astype(jnp.bfloat16)
    q_pre = jnp.einsum(
        EQ_STD_DE_TO_STE, normalized_input, wq_all, preferred_element_type=jnp.float32
    ).reshape(sequence_count, token_count, QUERY_HEADS, HEAD_SIZE)
    key_before_norm = jnp.einsum(
        EQ_STD_DE_TO_STE, normalized_input, wk_all, preferred_element_type=jnp.float32
    ).reshape(sequence_count, token_count, KEY_VALUE_HEADS, HEAD_SIZE)
    value_before_norm = jnp.einsum(
        EQ_STD_DE_TO_STE, normalized_input, wv_all, preferred_element_type=jnp.float32
    ).reshape(sequence_count, token_count, KEY_VALUE_HEADS, HEAD_SIZE)
    q_scale = rms_scale(q_pre)
    k_scale = rms_scale(key_before_norm)
    gain_q = q_gain.astype(jnp.float32)
    gain_k = k_gain.astype(jnp.float32)
    q_rot = rotate(q_pre * q_scale * gain_q, local_angles, 1.0).astype(jnp.bfloat16)
    k_rot = rotate(key_before_norm * k_scale * gain_k, local_angles, 1.0).astype(jnp.bfloat16)
    v_low = value_before_norm.astype(jnp.bfloat16)
    q_heads, k_heads, v_heads = (
        lax.all_to_all(q_rot, ULY, split_axis=2, concat_axis=1, tiled=True),
        lax.all_to_all(k_rot, ULY, split_axis=2, concat_axis=1, tiled=True),
        lax.all_to_all(v_low, ULY, split_axis=2, concat_axis=1, tiled=True),
    )
    q_group = q_heads.reshape(
        sequence_count, block_len, local_key_value, query_group_width, HEAD_SIZE
    )
    stat_shape = (sequence_count, local_key_value, query_group_width, block_len)
    start_state = (
        jnp.full(stat_shape, -1e30, jnp.float32),
        jnp.zeros(stat_shape, jnp.float32),
        jnp.zeros(stat_shape + (HEAD_SIZE,), jnp.float32),
    )
    key_piece = lax.all_gather(k_heads, BLK, axis=1, tiled=True)
    value_piece = lax.all_gather(v_heads, BLK, axis=1, tiled=True)
    key_pos = positions_of(jnp.arange(key_piece.shape[1], dtype=jnp.int32), span_order, half_len)
    allowed = query_pos[:, None] >= key_pos[None, :]

    def attend_one_sequence(members):
        query_rows, key_rows, value_rows, top_seq, total_seq, accum_seq = members
        scores = (
            jnp.einsum(EQ_QKGD_NKD_TO_KGQN, query_rows, key_rows, preferred_element_type=jnp.float32)
            * score_scale
        )
        scores = jnp.where(allowed, scores, -jnp.inf)
        new_top = jnp.maximum(top_seq, jnp.max(scores, axis=-1))
        fading = jnp.exp(top_seq - new_top)
        weights = jnp.exp(scores - new_top[..., None])
        total_seq = total_seq * fading + jnp.sum(weights, axis=-1)
        accum_seq = accum_seq * fading[..., None] + jnp.einsum(
            EQ_KGQN_NKD_TO_KGQD,
            weights.astype(jnp.bfloat16),
            value_rows,
            preferred_element_type=jnp.float32,
        )
        return (new_top, total_seq, accum_seq)

    row_top, row_total, accum = lax.map(
        attend_one_sequence,
        (q_group, key_piece, value_piece, start_state[0], start_state[1], start_state[2]),
    )
    log_total = row_top + jnp.log(row_total)
    attention_output = jnp.transpose(accum / row_total[..., None], (0, 3, 1, 2, 4)).reshape(
        sequence_count, block_len, local_q, HEAD_SIZE
    )
    heads_seq = lax.all_to_all(
        attention_output.astype(jnp.bfloat16), ULY, split_axis=1, concat_axis=2, tiled=True
    )
    heads_flat = heads_seq.reshape(sequence_count, token_count, QUERY_HEADS * HEAD_SIZE)
    middle = source + jnp.einsum(
        EQ_STE_ED_TO_STD, heads_flat, wo_all, preferred_element_type=jnp.float32
    )
    g_mlp, wg_all, wu_all, wd_all = (
        lax.all_gather(mlp_gain, EVERY, axis=0, tiled=True),
        lax.all_gather(w_gate, EVERY, axis=0, tiled=True),
        lax.all_gather(w_up, EVERY, axis=0, tiled=True),
        lax.all_gather(w_down, EVERY, axis=0, tiled=True),
    )
    second_scale = rms_scale(middle)
    gain_mlp = g_mlp.astype(jnp.float32)
    normed2 = (middle * second_scale * gain_mlp).astype(jnp.bfloat16)
    gate_pre = jnp.einsum(EQ_STD_DF_TO_STF, normed2, wg_all, preferred_element_type=jnp.float32)
    up_pre = jnp.einsum(EQ_STD_DF_TO_STF, normed2, wu_all, preferred_element_type=jnp.float32)
    sigmoid_gate = jax.nn.sigmoid(gate_pre)
    activated = (gate_pre * sigmoid_gate * up_pre).astype(jnp.bfloat16)
    result = middle + jnp.einsum(
        EQ_STF_FD_TO_STD, activated, wd_all, preferred_element_type=jnp.float32
    )
    output = result.astype(jnp.bfloat16)
    g_mlp, wg_all, wu_all, wd_all = (
        lax.all_gather(mlp_gain, EVERY, axis=0, tiled=True),
        lax.all_gather(w_gate, EVERY, axis=0, tiled=True),
        lax.all_gather(w_up, EVERY, axis=0, tiled=True),
        lax.all_gather(w_down, EVERY, axis=0, tiled=True),
    )
    gain_mlp = g_mlp.astype(jnp.float32)
    grad_act = jnp.einsum(EQ_STD_FD_TO_STF, cotangent, wd_all, preferred_element_type=jnp.float32)
    grad_gate_pre = (
        grad_act * up_pre * sigmoid_gate * (1.0 + gate_pre * (1.0 - sigmoid_gate))
    ).astype(jnp.bfloat16)
    grad_up_pre = (grad_act * gate_pre * sigmoid_gate).astype(jnp.bfloat16)
    grad_gate = jnp.einsum(
        EQ_STD_STF_TO_DF, normed2, grad_gate_pre, preferred_element_type=jnp.float32
    )
    grad_up = jnp.einsum(EQ_STD_STF_TO_DF, normed2, grad_up_pre, preferred_element_type=jnp.float32)
    grad_normed2 = jnp.einsum(
        EQ_STF_DF_TO_STD, grad_gate_pre, wg_all, preferred_element_type=jnp.float32
    ) + jnp.einsum(EQ_STF_DF_TO_STD, grad_up_pre, wu_all, preferred_element_type=jnp.float32)
    mlp_gain_term = jnp.sum(grad_normed2 * middle * second_scale, axis=(0, 1))
    grad_middle = cotangent.astype(jnp.float32) + norm_back(
        grad_normed2, middle, second_scale, gain_mlp
    )
    grad_mlp_gain, grad_gate, grad_up = (
        lax.psum_scatter(mlp_gain_term, EVERY, scatter_dimension=0, tiled=True),
        lax.psum_scatter(grad_gate, EVERY, scatter_dimension=0, tiled=True),
        lax.psum_scatter(grad_up, EVERY, scatter_dimension=0, tiled=True),
    )
    g_attn, wq_all, wk_all, wv_all, wo_all = (
        lax.all_gather(attn_gain, EVERY, axis=0, tiled=True),
        lax.all_gather(w_query, EVERY, axis=0, tiled=True),
        lax.all_gather(key_weight, EVERY, axis=0, tiled=True),
        lax.all_gather(value_weight, EVERY, axis=0, tiled=True),
        lax.all_gather(w_out, EVERY, axis=0, tiled=True),
    )
    middle_low = grad_middle.astype(jnp.bfloat16)
    grad_out = jnp.einsum(EQ_STE_STD_TO_ED, heads_flat, middle_low, preferred_element_type=jnp.float32)
    grad_heads = (
        jnp.einsum(EQ_STD_ED_TO_STE, middle_low, wo_all, preferred_element_type=jnp.float32)
        .astype(jnp.bfloat16)
        .reshape(sequence_count, token_count, QUERY_HEADS, HEAD_SIZE)
    )
    grad_heads_local = lax.all_to_all(grad_heads, ULY, split_axis=2, concat_axis=1, tiled=True)
    grad_group = jnp.transpose(
        grad_heads_local.reshape(
            sequence_count, block_len, local_key_value, query_group_width, HEAD_SIZE
        ),
        (0, 2, 3, 1, 4),
    )
    delta = jnp.sum(grad_heads_local.astype(jnp.float32) * attention_output, axis=-1)
    delta = jnp.transpose(
        delta.reshape(sequence_count, block_len, local_key_value, query_group_width), (0, 2, 3, 1)
    )
    seq_length = block_len * lax.axis_size(BLK)
    zero_keys = jnp.zeros((sequence_count, seq_length, local_key_value, HEAD_SIZE), jnp.float32)
    back_state = (jnp.zeros(stat_shape + (HEAD_SIZE,), jnp.float32), zero_keys, zero_keys)
    key_piece = lax.all_gather(k_heads, BLK, axis=1, tiled=True)
    value_piece = lax.all_gather(v_heads, BLK, axis=1, tiled=True)
    key_pos = positions_of(jnp.arange(key_piece.shape[1], dtype=jnp.int32), span_order, half_len)
    back_allowed = query_pos[:, None] >= key_pos[None, :]

    def back_one_sequence(members):
        query_rows, grad_rows, lse_seq, delta_seq, key_rows, value_rows, dq_seq, dk_seq, dv_seq = (
            members
        )
        scores = (
            jnp.einsum(EQ_QKGD_NKD_TO_KGQN, query_rows, key_rows, preferred_element_type=jnp.float32)
            * score_scale
        )
        scores = jnp.where(back_allowed, scores, -jnp.inf)
        probs = jnp.exp(scores - lse_seq[..., None])
        grad_values = jnp.einsum(
            EQ_KGQN_KGQD_TO_NKD,
            probs.astype(jnp.bfloat16),
            grad_rows,
            preferred_element_type=jnp.float32,
        )
        grad_probs = jnp.einsum(
            EQ_KGQD_NKD_TO_KGQN, grad_rows, value_rows, preferred_element_type=jnp.float32
        )
        grad_scores = (probs * (grad_probs - delta_seq[..., None])).astype(jnp.bfloat16)
        dq_seq = dq_seq + score_scale * jnp.einsum(
            EQ_KGQN_NKD_TO_KGQD, grad_scores, key_rows, preferred_element_type=jnp.float32
        )
        grad_keys = score_scale * jnp.einsum(
            EQ_KGQN_QKGD_TO_NKD, grad_scores, query_rows, preferred_element_type=jnp.float32
        )
        return (dq_seq, add_rows(dk_seq, grad_keys), add_rows(dv_seq, grad_values))

    grad_q_group, grad_k_whole, grad_v_whole = lax.map(
        back_one_sequence,
        (
            q_group,
            grad_group,
            log_total,
            delta,
            key_piece,
            value_piece,
            back_state[0],
            back_state[1],
            back_state[2],
        ),
    )
    grad_k_block, grad_v_block = (
        lax.psum_scatter(
            grad_k_whole.astype(jnp.bfloat16), BLK, scatter_dimension=1, tiled=True
        ).astype(jnp.float32),
        lax.psum_scatter(
            grad_v_whole.astype(jnp.bfloat16), BLK, scatter_dimension=1, tiled=True
        ).astype(jnp.float32),
    )
    grad_q_block = jnp.transpose(grad_q_group, (0, 3, 1, 2, 4)).reshape(
        sequence_count, block_len, local_q, HEAD_SIZE
    )
    grad_q_seq, grad_k_seq, value_sequence_gradient = (
        lax.all_to_all(
            grad_q_block.astype(jnp.bfloat16), ULY, split_axis=1, concat_axis=2, tiled=True
        ).astype(grad_q_block.dtype),
        lax.all_to_all(
            grad_k_block.astype(jnp.bfloat16), ULY, split_axis=1, concat_axis=2, tiled=True
        ).astype(grad_k_block.dtype),
        lax.all_to_all(
            grad_v_block.astype(jnp.bfloat16), ULY, split_axis=1, concat_axis=2, tiled=True
        ).astype(grad_v_block.dtype),
    )
    grad_q_normed = rotate(grad_q_seq, local_angles, -1.0)
    grad_k_normed = rotate(grad_k_seq, local_angles, -1.0)
    q_gain_term = jnp.sum(grad_q_normed * q_pre * q_scale, axis=(0, 1, 2))
    k_gain_term = jnp.sum(grad_k_normed * key_before_norm * k_scale, axis=(0, 1, 2))
    grad_q_pre = (
        norm_back(grad_q_normed, q_pre, q_scale, gain_q)
        .astype(jnp.bfloat16)
        .reshape(sequence_count, token_count, QUERY_HEADS * HEAD_SIZE)
    )
    grad_k_pre = (
        norm_back(grad_k_normed, key_before_norm, k_scale, gain_k)
        .astype(jnp.bfloat16)
        .reshape(sequence_count, token_count, KEY_VALUE_HEADS * HEAD_SIZE)
    )
    value_pre_gradient = value_sequence_gradient.astype(jnp.bfloat16).reshape(
        sequence_count, token_count, KEY_VALUE_HEADS * HEAD_SIZE
    )
    grad_query = jnp.einsum(
        EQ_STD_STE_TO_DE, normalized_input, grad_q_pre, preferred_element_type=jnp.float32
    )
    grad_key = jnp.einsum(
        EQ_STD_STE_TO_DE, normalized_input, grad_k_pre, preferred_element_type=jnp.float32
    )
    grad_value = jnp.einsum(
        EQ_STD_STE_TO_DE, normalized_input, value_pre_gradient, preferred_element_type=jnp.float32
    )
    grad_normed = jnp.einsum(EQ_STE_DE_TO_STD, grad_q_pre, wq_all, preferred_element_type=jnp.float32)
    grad_normed = grad_normed + jnp.einsum(
        EQ_STE_DE_TO_STD, grad_k_pre, wk_all, preferred_element_type=jnp.float32
    )
    grad_normed = grad_normed + jnp.einsum(
        EQ_STE_DE_TO_STD, value_pre_gradient, wv_all, preferred_element_type=jnp.float32
    )
    attn_gain_term = jnp.sum(grad_normed * source * first_scale, axis=(0, 1))
    grad_hidden = grad_middle + norm_back(
        grad_normed, source, first_scale, g_attn.astype(jnp.float32)
    )
    grad_down = jnp.einsum(EQ_STF_STD_TO_FD, activated, cotangent, preferred_element_type=jnp.float32)
    grad_attn_gain, grad_query, grad_key, grad_value, grad_out, grad_down = (
        lax.psum_scatter(attn_gain_term, EVERY, scatter_dimension=0, tiled=True),
        lax.psum_scatter(grad_query, EVERY, scatter_dimension=0, tiled=True),
        lax.psum_scatter(grad_key, EVERY, scatter_dimension=0, tiled=True),
        lax.psum_scatter(grad_value, EVERY, scatter_dimension=0, tiled=True),
        lax.psum_scatter(grad_out, EVERY, scatter_dimension=0, tiled=True),
        lax.psum_scatter(grad_down, EVERY, scatter_dimension=0, tiled=True),
    )
    grad_q_gain, grad_k_gain = lax.psum((q_gain_term, k_gain_term), EVERY)
    return (
        output,
        grad_hidden,
        grad_attn_gain,
        grad_query,
        grad_key,
        grad_value,
        grad_out,
        grad_q_gain,
        grad_k_gain,
        grad_mlp_gain,
        grad_gate,
        grad_up,
        grad_down,
    )


MESH = pl.DeviceIdType.MESH
HBM = pl.BlockSpec(memory_space=pltpu.HBM)
VMEM = pl.BlockSpec(memory_space=pltpu.VMEM)
MIB = 1 << 20


def kernel_params(collective_id, vmem_mib=62):
    return pltpu.CompilerParams(
        collective_id=collective_id, has_side_effects=True, vmem_limit_bytes=vmem_mib * MIB
    )


def semaphores(count, local=16):
    return [
        pltpu.SemaphoreType.DMA((count,)),
        pltpu.SemaphoreType.DMA((count,)),
        pltpu.SemaphoreType.DMA((local,)),
    ]


class Copy:
    def __init__(self, descriptor, sends, receives):
        self.descriptor, self.sends, self.receives = descriptor, sends, receives

    def under(self, condition, action):
        if condition is None:
            action()
        else:
            pl.when(condition)(action)

    def start(self):
        self.under(self.sends, lambda: self.descriptor().start())
        return self

    def sent(self):
        self.under(self.sends, lambda: self.descriptor().wait_send())

    def arrived(self):
        self.under(self.receives, lambda: self.descriptor().wait_recv())


class Links:
    def __init__(self, send, recv, here):
        self.send, self.recv, self.here = send, recv, here
        self.used, self.used_here = 0, 0
        self.copies, self.local_copies = [], []
        self.n_dp, self.n_blk, self.n_uly = (lax.axis_size(a) for a in EVERY)
        self.dp, self.blk, self.uly = (lax.axis_index(a) for a in EVERY)
        self.other_dp = 1 - self.dp
        self.across = lax.rem(self.uly + 2, 4)
        self.twin = self.uly + 1 - 2 * lax.rem(self.uly, 2)
        self.x_way = (self.other_dp, self.blk, self.uly)
        self.y_way = (self.dp, self.blk, self.across)
        self.core_way = (self.dp, self.blk, self.twin)

    def peer(self, step):
        return lax.rem(self.blk + step, self.n_blk)

    def peers(self):
        return [(self.dp, self.peer(k), self.uly) for k in range(1, self.n_blk)]

    def greet(self, devices):
        barrier = pltpu.get_barrier_semaphore()
        for device in devices:
            pl.semaphore_signal(barrier, inc=1, device_id=device, device_id_type=MESH)
        pl.semaphore_wait(barrier, len(devices))

    def remote(self, source, target, device, sends=None, receives=None):
        slot = self.used
        self.used += 1

        def descriptor():
            return pltpu.make_async_remote_copy(
                src_ref=source(),
                dst_ref=target(),
                send_sem=self.send.at[slot],
                recv_sem=self.recv.at[slot],
                device_id=device,
                device_id_type=MESH,
            )

        copy = Copy(descriptor, sends, receives)
        self.copies.append(copy)
        return copy.start()

    def to(self, source, target, device):
        return self.remote(lambda: source, lambda: target, device)

    def local(self, source, target):
        copy = pltpu.make_async_copy(source, target, self.here.at[self.used_here])
        self.used_here += 1
        copy.start()
        self.local_copies.append(copy)
        return copy

    def finish(self):
        for copy in self.copies:
            copy.sent()


class LineGather:
    def __init__(self, links, own, whole):
        self.links, self.own, self.whole = links, own, whole
        self.waiting = []

    def send(self, step):
        links, whole = self.links, self.whole
        blk, last = links.blk, links.n_blk - 1

        def block(index):
            if step == 0:
                return lambda: self.own
            return lambda: whole.at[index]

        self.waiting = [
            links.remote(
                block(blk - step),
                lambda: whole.at[blk - step],
                (links.dp, blk + 1, links.uly),
                jnp.logical_and(blk >= step, blk < last),
                blk >= step + 1,
            ),
            links.remote(
                block(blk + step),
                lambda: whole.at[blk + step],
                (links.dp, blk - 1, links.uly),
                jnp.logical_and(blk + step <= last, blk > 0),
                blk + step + 1 <= last,
            ),
        ]

    def arrived(self):
        for copy in self.waiting:
            copy.arrived()


def halves(tokens):
    return [pl.ds(0, tokens // 2), pl.ds(tokens // 2, tokens // 2)]


class HalvedLine:
    def __init__(self, links, own, whole):
        self.lines = [
            LineGather(links, None if own is None else own.at[rows], whole.at[:, rows])
            for rows in halves(whole.shape[1])
        ]

    def send(self, step):
        for line in self.lines:
            line.send(step)

    def advance(self, step):
        for line in self.lines:
            line.arrived()
            line.send(step)

    def arrived(self):
        for line in self.lines:
            line.arrived()


class PlaneGather:
    def __init__(self, links, at):
        self.links, self.at = links, at

    def start_x(self, own):
        links = self.links
        mine = self.at(links.dp, links.uly)
        self.from_x = links.to(own, mine, links.x_way)
        self.from_core = [links.to(own, mine, links.core_way)]

    def start_y(self, own):
        links = self.links
        self.from_y = links.to(own, self.at(links.dp, links.uly), links.y_way)

    def start(self, own=None):
        own = self.at(self.links.dp, self.links.uly) if own is None else own
        self.start_x(own)
        self.start_y(own)

    def hand_on(self):
        links, at = self.links, self.at
        self.from_x.arrived()
        half = at(links.other_dp, links.uly, 0)
        self.second_y = links.to(half, half, links.y_way)
        self.from_y.arrived()
        half = at(links.dp, links.across, 1)
        self.second_x = links.to(half, half, links.x_way)
        for chunk in (at(links.other_dp, links.uly), at(links.dp, links.across)):
            self.from_core.append(links.to(chunk, chunk, links.core_way))

    def last(self):
        links = self.links
        self.second_y.arrived()
        self.second_x.arrived()
        chunk = self.at(links.other_dp, links.across)
        self.from_core.append(links.to(chunk, chunk, links.core_way))

    def arrived(self):
        for copy in self.from_core:
            copy.arrived()


def rows_of(whole, blocked):
    def at(dp, uly, half=None):
        part = whole.at[dp, :, uly] if blocked else whole.at[dp, uly]
        if half is None:
            return part
        depth = whole.shape[-2] // 2
        rows = pl.ds(half * depth, depth)
        return part.at[:, rows] if blocked else part.at[rows]

    return at


class ColumnSwap:
    def __init__(self, links, pieces):
        self.links, self.pieces = links, pieces
        self.incoming, self.kept = [], []

    def parts(self, blk):
        links = self.links
        for weight, whole, offset in self.pieces:
            width = weight.shape[-1] // links.n_dp // links.n_blk
            for group in range(links.n_dp):
                start = (group * links.n_blk + blk) * width
                yield (
                    weight.at[:, pl.ds(pl.multiple_of(start, 128), width)],
                    whole.at[links.blk, :, pl.ds(offset + group * width, width)],
                )

    def start(self):
        links = self.links
        for step in range(1, links.n_blk):
            device = (links.dp, links.peer(step), links.uly)
            for source, target in self.parts(links.peer(step)):
                self.incoming.append(links.to(source, target, device))
        for source, target in self.parts(links.blk):
            self.kept.append(links.local(source, target))

    def arrived(self):
        for copy in self.kept:
            copy.wait()
        for copy in self.incoming:
            copy.arrived()


def write_positions(links, span_order, toks, cosine, sine, query_pos, key_pos):
    half_len = toks * links.n_uly // 2

    def first(blk, uly):
        chunk = span_order[2 * blk + lax.div(uly, links.n_uly // 2)]
        return chunk * half_len + lax.rem(uly, links.n_uly // 2) * toks

    lane = lax.broadcasted_iota(jnp.int32, (toks, HEAD_SIZE), 1)
    row = lax.broadcasted_iota(jnp.int32, (toks, HEAD_SIZE), 0)
    upper = lane >= HEAD_SIZE // 2
    step = jnp.where(upper, lane - HEAD_SIZE // 2, lane).astype(jnp.float32)
    inverse = jnp.exp(step * (-2.0 * math.log(ROPE_BASE) / HEAD_SIZE))
    for blk in range(links.n_blk):
        angles = (first(blk, links.uly) + row).astype(jnp.float32) * inverse
        at = slice(blk * toks, (blk + 1) * toks)
        cosine[at, :] = jnp.cos(angles)
        turn = jnp.sin(angles)
        sine[at, :] = jnp.where(upper, turn, -turn)
    lane = lax.broadcasted_iota(jnp.int32, query_pos.shape, 1)
    place = jnp.zeros(query_pos.shape, jnp.int32)
    for start in range(0, query_pos.shape[1], toks):
        blk = start // toks % links.n_blk
        here = jnp.logical_and(lane >= start, lane < start + toks)
        place = jnp.where(here, first(blk, links.uly) + lane - start, place)
    query_pos[...] = place
    row = lax.broadcasted_iota(jnp.int32, (toks, 1), 0)
    for uly in range(links.n_uly):
        for blk in range(links.n_blk):
            start = (uly * links.n_blk + blk) * toks
            key_pos[start : start + toks, :] = row + first(blk, jnp.int32(uly))


def write_gains(links, all_gains, size, targets):
    per_row = 128 // size
    for which, target in enumerate(targets):
        for place in range(target.shape[1] // 128):
            pieces = []
            for part in range(per_row):
                device = place * per_row + part
                plane, uly = device // links.n_uly, device % links.n_uly
                gains = all_gains[plane // links.n_blk, plane % links.n_blk, uly]
                pieces.append(gains.astype(jnp.float32)[which : which + 1, :size])
            target[:, place * 128 : (place + 1) * 128] = jnp.concatenate(pieces, axis=1)


def front_kernel(
    toks,
    gain_rows,
    span_order,
    hidden,
    wq,
    wk,
    wv,
    wo,
    gains,
    all_hidden,
    w_qkv,
    all_wo,
    attn_gain,
    mlp_gain,
    cosine,
    sine,
    query_pos,
    key_pos,
    all_gains,
    send,
    recv,
    here,
):
    links = Links(send, recv, here)
    links.greet(links.peers() + [links.x_way, links.y_way, links.core_way])
    q_width, k_width = wq.shape[1] // links.n_blk, wk.shape[1] // links.n_blk
    chunk = w_qkv.at[links.dp, :, links.uly]
    swap = ColumnSwap(
        links, [(wq, chunk, 0), (wk, chunk, q_width), (wv, chunk, q_width + k_width)]
    )
    plane_wo = PlaneGather(links, rows_of(all_wo, False))
    plane_qkv = PlaneGather(links, rows_of(w_qkv, True))
    plane_gain = PlaneGather(links, rows_of(all_gains, True))
    swap.start()
    my_gains = all_gains.at[links.dp, links.blk, links.uly]
    gain_swap = [links.to(gains, my_gains, device) for device in links.peers()]
    plane_wo.start(wo)
    line = HalvedLine(links, hidden, all_hidden)
    line.send(0)
    keep = [
        links.local(gains, my_gains),
        links.local(hidden, all_hidden.at[links.blk]),
        links.local(wo, all_wo.at[links.dp, links.uly]),
    ]
    write_positions(links, span_order, toks, cosine, sine, query_pos, key_pos)
    swap.arrived()
    plane_qkv.start()
    keep[0].wait()
    for copy in gain_swap:
        copy.arrived()
    plane_gain.start()
    plane_wo.hand_on()
    line.advance(1)
    plane_qkv.hand_on()
    plane_gain.hand_on()
    plane_wo.last()
    for step in range(2, links.n_blk - 1):
        line.advance(step)
    plane_qkv.last()
    plane_gain.last()
    plane_gain.arrived()
    write_gains(links, all_gains, gain_rows, (attn_gain, mlp_gain))
    line.arrived()
    for plane in (plane_wo, plane_qkv):
        plane.arrived()
    for copy in keep[1:]:
        copy.wait()
    links.finish()


SMEM = pl.BlockSpec(memory_space=pltpu.SMEM)


def gather_front(span_order, hidden, wq, wk, wv, wo, gains, toks, gain_rows):
    n_dp, n_blk, n_uly = (lax.axis_size(a) for a in EVERY)
    width = hidden.shape[1]
    group = QUERY_HEADS // KEY_VALUE_HEADS
    low = [
        (n_blk,) + hidden.shape,
        (n_dp, n_blk, n_uly, wq.shape[0], (wq.shape[1] + wk.shape[1] + wv.shape[1]) // n_blk),
        (n_dp, n_uly) + wo.shape,
    ]
    f32, i32 = jnp.float32, jnp.int32
    small = [
        ((1, width), f32),
        ((1, width), f32),
        ((n_blk * toks, HEAD_SIZE), f32),
        ((n_blk * toks, HEAD_SIZE), f32),
        ((1, group * n_blk * toks), i32),
        ((n_uly * n_blk * toks, 1), i32),
    ]
    return pl.pallas_call(
        functools.partial(front_kernel, toks, gain_rows),
        out_shape=[jax.ShapeDtypeStruct(shape, jnp.bfloat16) for shape in low]
        + [jax.ShapeDtypeStruct(shape, kind) for shape, kind in small],
        in_specs=[SMEM] + [HBM] * 6,
        out_specs=[HBM] * 3 + [VMEM] * 6,
        scratch_shapes=[pltpu.VMEM((n_dp, n_blk, n_uly) + gains.shape, jnp.bfloat16)]
        + semaphores(72),
        compiler_params=kernel_params(0),
    )(span_order, hidden, wq, wk, wv, wo, gains)


ROWS = 32


def each_block(count, body):
    def step(index, carry):
        body(pl.ds(pl.multiple_of(index * ROWS, ROWS), ROWS))
        return carry

    lax.fori_loop(0, count // ROWS, step, 0)


class LineScatter:
    def __init__(self, links, parts, rightward, leftward):
        self.links, self.parts = links, parts
        self.slots = {1: rightward, -1: leftward}
        self.tokens = parts.shape[1]
        self.number = links.used
        self.last = links.n_blk - 1
        links.used += 2 * self.last

    def target(self, step, way):
        return self.last - step if way == 1 else step

    def slot(self, step, way):
        target = self.target(step, way)
        return self.slots[way].at[target - 1 if way == 1 else target]

    def place(self, way):
        return self.links.blk if way == 1 else self.last - self.links.blk

    def copy(self, step, way, source=None):
        links, slot = self.links, self.slot(step, way)
        number = self.number + 2 * step + (1 if way == 1 else 0)
        return pltpu.make_async_remote_copy(
            src_ref=slot if source is None else source,
            dst_ref=slot,
            send_sem=links.send.at[number],
            recv_sem=links.recv.at[number],
            device_id=(links.dp, links.blk + way, links.uly),
            device_id_type=MESH,
        )

    def start(self):
        for step in range(self.last):
            for way in (1, -1):

                @pl.when(self.place(way) == 0)
                def _(step=step, way=way):
                    self.copy(step, way, self.parts.at[self.target(step, way)]).start()

    def tick(self, tick):
        for way in (1, -1):

            @pl.when(jnp.logical_and(self.place(way) >= 1, self.place(way) <= tick))
            def _(way=way):
                step = tick - self.place(way)
                self.copy(step, way).wait_recv()
                slot, target = self.slot(step, way), self.target(step, way)

                def body(rows):
                    slot[rows, :] = slot[rows, :] + self.parts[target, rows, :]

                each_block(self.tokens, body)
                self.copy(step, way).start()

    def finish(self, total):
        blk, last = self.links.blk, self.last

        def start(rows):
            total[rows, :] = self.parts[blk, rows, :].astype(jnp.float32)

        each_block(self.tokens, start)
        for way in (1, -1):

            @pl.when(self.place(way) >= 1)
            def _(way=way):
                step = last - self.place(way)
                self.copy(step, way).wait_recv()
                slot = self.slot(step, way)

                def body(rows):
                    total[rows, :] = total[rows, :] + slot[rows, :].astype(jnp.float32)

                each_block(self.tokens, body)

    def sent(self):
        for step in range(self.last):
            for way in (1, -1):
                beyond = self.place(way) + step < self.last
                pl.when(beyond)(lambda step=step, way=way: self.copy(step, way).wait_send())


def halved_sums(links, parts, rightward, leftward):
    return [
        LineScatter(links, parts.at[:, rows], rightward.at[:, rows], leftward.at[:, rows])
        for rows in halves(parts.shape[1])
    ]


class OutputHalf:
    def __init__(self, links, which, parts, middle, rightward, leftward, total):
        rows = halves(middle.shape[0])[which]
        self.middle, self.total = middle.at[rows], total
        self.sum = LineScatter(links, parts.at[:, rows], rightward, leftward)

    def write(self, output):
        self.sum.finish(self.total)

        def body(rows):
            output[rows, :] = (self.middle[rows, :] + self.total[rows, :]).astype(jnp.bfloat16)

        each_block(self.middle.shape[0], body)


def output_scratch(n_blk, tokens, width):
    return line_scratch(n_blk, tokens // 2, width) + [
        pltpu.VMEM((tokens // 2, width), jnp.float32)
    ]


def line_scratch(n_blk, tokens, width):
    return [pltpu.VMEM((n_blk - 1, tokens, width), jnp.bfloat16)] * 2


class PlaneScatter:
    def __init__(self, links, parts, from_core, from_x, from_y, last_x, last_y):
        self.links, self.parts = links, parts
        self.own_core_only = from_core is None
        self.from_core, self.from_x, self.from_y = from_core, from_x, from_y
        self.last_x, self.last_y = last_x, last_y
        self.core = lax.rem(links.uly, 2)
        self.row = lax.div(links.uly, 2)
        self.depth = parts.shape[3]
        self.core_copies = {}

    def chunk(self, dp, row, core, half=None):
        if self.own_core_only:
            part = self.parts.at[dp, row]
        else:
            part = self.parts.at[dp, :, row * 2 + core]
        if half is None:
            return part
        depth = self.depth // 2
        return part.at[:, pl.ds(half * depth, depth)]

    def add(self, target, source):
        blocks, depth, _ = target.shape
        rows = 32 if depth % 32 == 0 else 16

        def body(index, carry):
            block = lax.div(index, depth // rows)
            at = pl.ds(pl.multiple_of(lax.rem(index, depth // rows) * rows, rows), rows)
            target[block, at, :] = target[block, at, :] + source[block, at, :]
            return carry

        lax.fori_loop(0, blocks * (depth // rows), body, 0)

    def between_cores(self, which):
        links = self.links
        dp = links.dp if which == 1 else links.other_dp
        self.core_copies[which] = [
            links.to(
                self.chunk(dp, row, 1 - self.core), self.from_core.at[which, row], links.core_way
            )
            for row in range(2)
        ]

    def core_sums(self, which):
        links = self.links
        dp = links.dp if which == 1 else links.other_dp
        for row in range(2):
            self.core_copies[which][row].arrived()
            self.add(self.chunk(dp, row, self.core), self.from_core.at[which, row])

    def across_chips(self):
        links = self.links
        if not self.own_core_only:
            self.core_sums(0)
        self.x_copies = [
            links.to(
                self.chunk(links.other_dp, row, self.core, 0), self.from_x.at[row], links.x_way
            )
            for row in range(2)
        ]
        if not self.own_core_only:
            self.core_sums(1)
        self.y_copies = [
            links.to(
                self.chunk(group, 1 - self.row, self.core, 1),
                self.from_y.at[group],
                links.y_way,
            )
            for group in range(links.n_dp)
        ]

    def second_way(self):
        links = self.links
        for row in range(2):
            self.x_copies[row].arrived()
            self.add(self.chunk(links.dp, row, self.core, 0), self.from_x.at[row])
        self.y_last = links.to(
            self.chunk(links.dp, 1 - self.row, self.core, 0), self.last_y, links.y_way
        )
        for group in range(links.n_dp):
            self.y_copies[group].arrived()
            self.add(self.chunk(group, self.row, self.core, 1), self.from_y.at[group])
        self.x_last = links.to(
            self.chunk(links.other_dp, self.row, self.core, 1), self.last_x, links.x_way
        )

    def result(self, write):
        links = self.links
        for half, copy, source in ((0, self.y_last, self.last_y), (1, self.x_last, self.last_x)):
            copy.arrived()
            own = self.chunk(links.dp, self.row, self.core, half)
            blocks, depth, _ = source.shape
            rows = 32 if depth % 32 == 0 else 16

            def body(index, carry, own=own, source=source, half=half, depth=depth, rows=rows):
                block = lax.div(index, depth // rows)
                start = pl.multiple_of(lax.rem(index, depth // rows) * rows, rows)
                at = pl.ds(start, rows)
                value = own[block, at, :].astype(jnp.float32)
                value = value + source[block, at, :].astype(jnp.float32)
                write(block, pl.ds(pl.multiple_of(start + half * depth, rows), rows), value)
                return carry

            lax.fori_loop(0, blocks * (depth // rows), body, 0)


def plane_shapes(n_dp, blocks, n_uly, depth, width):
    return [
        (n_dp, blocks, n_uly, depth, width),
        (n_dp, 2, blocks, depth, width),
        (2, blocks, depth // 2, width),
        (n_dp, blocks, depth // 2, width),
        (blocks, depth // 2, width),
        (blocks, depth // 2, width),
    ]


def plane_scratch(*sizes):
    return [pltpu.VMEM(shape, jnp.bfloat16) for shape in plane_shapes(*sizes)]


def weight_grad(left, right, parts, dp):
    _, blocks, n_uly, depth, width = parts.shape
    columns, count = 512, blocks * n_uly * depth
    rows = left[:, pl.ds(pl.multiple_of(dp * count, 128), count)].T

    def body(index, carry):
        at = pl.ds(pl.multiple_of(index * columns, columns), columns)
        part = jnp.dot(rows, right[:, at], preferred_element_type=jnp.float32)
        parts[dp, :, :, :, at] = part.astype(jnp.bfloat16).reshape(blocks, n_uly, depth, columns)
        return carry

    lax.fori_loop(0, width // columns, body, 0)


def turned(rows, cosine, sine):
    return rows * cosine + pltpu.roll(rows, HEAD_SIZE // 2, axis=1) * sine


def transposed_product(left, right):
    return lax.dot_general(
        left, right, (((0,), (0,)), ((), ())), preferred_element_type=jnp.float32
    )


def product_right(left, right):
    return lax.dot_general(
        left, right, (((1,), (1,)), ((), ())), preferred_element_type=jnp.float32
    )


SCORE_SCALE = 1.0 / math.sqrt(HEAD_SIZE)


def mask_scores(bias, query_pos, key_pos):
    size = bias.shape[0] // 4

    def body(index, carry):
        rows = pl.ds(pl.multiple_of(index * size, size), size)
        bias[rows, :] = jnp.where(query_pos[...] >= key_pos[rows, :], 0.0, -1e30)
        return carry

    lax.fori_loop(0, 4, body, 0)


class RowBlocks:
    def __init__(self, n_blk, seqs, toks):
        self.n_blk, self.seqs, self.toks = n_blk, seqs, toks

    def each(self, body):
        def step(index, carry):
            blk, seq = lax.div(index, self.seqs), lax.rem(index, self.seqs)
            body(
                seq,
                pl.ds(pl.multiple_of(index * self.toks, self.toks), self.toks),
                pl.multiple_of(blk * self.toks, self.toks),
            )
            return carry

        lax.fori_loop(0, self.n_blk * self.seqs, step, 0)


def attention_kernel(
    wg,
    wu,
    wd,
    cotangent,
    hidden,
    w_qkv,
    gain,
    q_gain,
    k_gain,
    cosine,
    sine,
    query_pos,
    key_pos,
    rows_wg,
    rows_wu,
    all_wd,
    all_cot,
    heads,
    normed,
    qkv,
    queries,
    key_values,
    lse,
    bias,
    send,
    recv,
    here,
):
    links = Links(send, recv, here)
    links.greet(links.peers() + [links.x_way, links.y_way, links.core_way])
    swap = ColumnSwap(links, [(wg, rows_wg, 0), (wu, rows_wu, 0)])
    swap.start()
    plane = PlaneGather(links, rows_of(all_wd, False))
    plane.start_x(wd)
    line = HalvedLine(links, cotangent, all_cot)
    line.send(0)
    keep = [
        links.local(cotangent, all_cot.at[links.blk]),
        links.local(wd, all_wd.at[links.dp, links.uly]),
    ]

    def norm(rows):
        source = hidden[rows, :].astype(jnp.float32)
        normed[rows, :] = (source * rms_scale(source) * gain[...]).astype(jnp.bfloat16)

    each_block(hidden.shape[0], norm)
    for column in range(0, qkv.shape[1], 256):
        qkv[:, column : column + 256] = jnp.dot(
            normed[...], w_qkv[:, column : column + 256], preferred_element_type=jnp.float32
        )
    seqs, kv_heads, q_rows, _ = queries.shape
    q_len = key_values.shape[4]
    group = q_rows // q_len
    blocks = RowBlocks(links.n_blk, seqs, q_len // links.n_blk)
    q_end = kv_heads * group * HEAD_SIZE
    k_end = q_end + kv_heads * HEAD_SIZE

    def place_keys(seq, rows, start):
        at = pl.ds(start, blocks.toks)
        for head in range(kv_heads):
            k_pre = qkv[rows, q_end + head * HEAD_SIZE : q_end + (head + 1) * HEAD_SIZE]
            k_row = turned(k_pre * rms_scale(k_pre) * k_gain[...], cosine[at, :], sine[at, :])
            v_row = qkv[rows, k_end + head * HEAD_SIZE : k_end + (head + 1) * HEAD_SIZE]
            key_values[links.uly, 0, seq, head, at, :] = k_row.astype(jnp.bfloat16)
            key_values[links.uly, 1, seq, head, at, :] = v_row.astype(jnp.bfloat16)

    blocks.each(place_keys)
    mine = key_values.at[links.uly]
    kv_core = links.to(mine, mine, links.core_way)
    kv_across = links.to(mine, mine, links.y_way)
    plane.start_y(wd)

    def place_queries(seq, rows, start):
        at = pl.ds(start, blocks.toks)
        for head in range(kv_heads * group):
            q_pre = qkv[rows, head * HEAD_SIZE : (head + 1) * HEAD_SIZE]
            q_row = turned(q_pre * rms_scale(q_pre) * q_gain[...], cosine[at, :], sine[at, :])
            to = pl.ds((head % group) * q_len + start, blocks.toks)
            queries[seq, head // group, to, :] = q_row.astype(jnp.bfloat16)

    blocks.each(place_queries)
    mask_scores(bias, query_pos, key_pos)
    kv_across.arrived()
    theirs = key_values.at[links.across]
    kv_last = links.to(theirs, theirs, links.core_way)
    kv_core.arrived()
    kv_last.arrived()

    def attend(seq, head):
        def over_keys(piece, carry):
            total, mixed = carry
            rows = pl.ds(pl.multiple_of(piece * q_len, q_len), q_len)
            scores = product_right(key_values[piece, 0, seq, head], queries[seq, head])
            weights = jnp.exp(scores * SCORE_SCALE + bias[rows, :])
            total = total + jnp.sum(weights, axis=0, keepdims=True)
            mixed = mixed + transposed_product(
                key_values[piece, 1, seq, head], weights.astype(jnp.bfloat16)
            )
            return total, mixed

        total, mixed = lax.fori_loop(
            0,
            links.n_uly,
            over_keys,
            (
                jnp.zeros((1, q_rows), jnp.float32),
                jnp.zeros((HEAD_SIZE, q_rows), jnp.float32),
            ),
        )
        lse[seq * kv_heads + head] = jnp.log(total)
        attended = (mixed / total).T.astype(jnp.bfloat16)
        for member in range(group):
            column = (head * group + member) * HEAD_SIZE
            for blk in range(links.n_blk):
                row = (blk * seqs + seq) * blocks.toks
                start = member * q_len + blk * blocks.toks
                heads[row : row + blocks.toks, column : column + HEAD_SIZE] = attended[
                    start : start + blocks.toks, :
                ]

    pairs = [(seq, head) for seq in range(seqs) for head in range(kv_heads)]
    for number, (seq, head) in enumerate(pairs):
        attend(seq, head)
        if number == len(pairs) // 2:
            plane.hand_on()
    plane.last()
    swap.arrived()
    line.arrived()
    for copy in keep:
        copy.wait()
    plane.arrived()
    links.finish()


def attend_forward(
    wg, wu, wd, cotangent, hidden, w_qkv, gain, q_gain, k_gain, cosine, sine, query_pos, key_pos, seqs
):
    n_dp, n_blk, n_uly = (lax.axis_size(a) for a in EVERY)
    rows = hidden.shape[0]
    kv_heads = KEY_VALUE_HEADS // n_blk
    q_len, q_rows = rows // seqs, query_pos.shape[1]
    low = [
        (n_blk, wg.shape[0], wg.shape[1] // n_blk),
        (n_blk, wu.shape[0], wu.shape[1] // n_blk),
        (n_dp, n_uly) + wd.shape,
        (n_blk,) + cotangent.shape,
        (rows, QUERY_HEADS // n_blk * HEAD_SIZE),
        hidden.shape,
    ]
    shapes = [jax.ShapeDtypeStruct(s, jnp.bfloat16) for s in low] + [
        jax.ShapeDtypeStruct((rows, w_qkv.shape[1]), jnp.float32),
        jax.ShapeDtypeStruct((seqs, kv_heads, q_rows, HEAD_SIZE), jnp.bfloat16),
        jax.ShapeDtypeStruct((n_uly, 2, seqs, kv_heads, q_len, HEAD_SIZE), jnp.bfloat16),
        jax.ShapeDtypeStruct((seqs * kv_heads, 1, q_rows), jnp.float32),
    ]
    return pl.pallas_call(
        attention_kernel,
        out_shape=shapes,
        in_specs=[HBM] * 4 + [VMEM] * 9,
        out_specs=[HBM] * 4 + [VMEM] * 6,
        scratch_shapes=[pltpu.VMEM((key_pos.shape[0], q_rows), jnp.float32)] + semaphores(32),
        compiler_params=kernel_params(1),
    )(
        wg,
        wu,
        wd,
        cotangent,
        hidden,
        w_qkv,
        gain,
        q_gain,
        k_gain,
        cosine,
        sine,
        query_pos,
        key_pos,
    )


def attention_back_kernel(
    all_low,
    wo,
    queries,
    key_values,
    lse,
    qkv,
    q_gain,
    k_gain,
    cosine,
    sine,
    query_pos,
    key_pos,
    out_parts,
    middle,
    grad_gate,
    grad_up,
    part_down,
    grad_qkv,
    gain_terms,
    grad_down,
    output,
    gate_rows,
    up_rows,
    bias,
    grad_heads,
    grad_rows,
    probs,
    grad_probs,
    grad_kv,
    from_core,
    from_across,
    down_1,
    down_3,
    down_4,
    down_5,
    down_6,
    out_right,
    out_left,
    out_total,
    send,
    recv,
    here,
):
    links = Links(send, recv, here)
    links.greet(links.peers() + [links.x_way, links.y_way, links.core_way])
    out = OutputHalf(links, 0, out_parts, middle, out_right, out_left, out_total)
    out.sum.start()
    down = PlaneScatter(links, down_1, None, down_3, down_4, down_5, down_6)
    links.local(part_down, down_1).wait()
    down.across_chips()
    swapped, keep = [], []
    for source, target in ((grad_gate, gate_rows), (grad_up, up_rows)):
        for step in range(1, links.n_blk):
            peer = links.peer(step)
            swapped.append(
                links.to(source.at[peer], target.at[links.blk], (links.dp, peer, links.uly))
            )
        keep.append(links.local(source.at[links.blk], target.at[links.blk]))
    grad_heads[...] = product_right(all_low[...], wo[...])
    mask_scores(bias, query_pos, key_pos)
    seqs, kv_heads, q_rows, _ = queries.shape
    q_len = key_values.shape[4]
    group = q_rows // q_len
    blocks = RowBlocks(links.n_blk, seqs, q_len // links.n_blk)
    q_end = kv_heads * group * HEAD_SIZE
    k_end = q_end + kv_heads * HEAD_SIZE
    gain_terms[...] = jnp.zeros_like(gain_terms)

    def gather_rows(seq, rows, start):
        for head in range(kv_heads * group):
            to = pl.ds((head % group) * q_len + start, blocks.toks)
            grad_rows[seq, head // group, to, :] = grad_heads[
                rows, head * HEAD_SIZE : (head + 1) * HEAD_SIZE
            ].astype(jnp.bfloat16)

    blocks.each(gather_rows)

    def back_norm(upstream, pre, gain, at, which):
        upstream = turned(upstream, cosine[at, :], -sine[at, :])
        back, term = back_rows(upstream, pre, gain[...])
        gain_terms[which : which + 1, :] += term
        return back.astype(jnp.bfloat16)

    def back(seq, head):
        def first(piece, delta):
            rows = pl.ds(pl.multiple_of(piece * q_len, q_len), q_len)
            scores = product_right(key_values[piece, 0, seq, head], queries[seq, head])
            prob = jnp.exp(
                scores * SCORE_SCALE + bias[rows, :] - lse[seq * kv_heads + head]
            )
            grad_prob = product_right(key_values[piece, 1, seq, head], grad_rows[seq, head])
            probs[rows, :] = prob
            grad_probs[rows, :] = grad_prob
            return delta + jnp.sum(prob * grad_prob, axis=0, keepdims=True)

        delta = lax.fori_loop(0, links.n_uly, first, jnp.zeros((1, q_rows), jnp.float32))

        def second(piece, grad_query):
            rows = pl.ds(pl.multiple_of(piece * q_len, q_len), q_len)
            prob = probs[rows, :]
            grad_score = (prob * (grad_probs[rows, :] - delta)).astype(jnp.bfloat16)
            grad_kv[seq, piece, 0, head] = (
                SCORE_SCALE
                * jnp.dot(grad_score, queries[seq, head], preferred_element_type=jnp.float32)
            ).astype(jnp.bfloat16)
            grad_kv[seq, piece, 1, head] = jnp.dot(
                prob.astype(jnp.bfloat16),
                grad_rows[seq, head],
                preferred_element_type=jnp.float32,
            ).astype(jnp.bfloat16)
            return grad_query + transposed_product(key_values[piece, 0, seq, head], grad_score)

        grad_query = lax.fori_loop(
            0, links.n_uly, second, jnp.zeros((HEAD_SIZE, q_rows), jnp.float32)
        )
        grad_heads[:, :HEAD_SIZE] = (grad_query * SCORE_SCALE).T
        for member in range(group):
            column = (head * group + member) * HEAD_SIZE
            for blk in range(links.n_blk):
                row = (blk * seqs + seq) * blocks.toks
                at = pl.ds(blk * blocks.toks, blocks.toks)
                start = member * q_len + blk * blocks.toks
                grad_qkv[row : row + blocks.toks, column : column + HEAD_SIZE] = back_norm(
                    grad_heads[start : start + blocks.toks, :HEAD_SIZE],
                    qkv[row : row + blocks.toks, column : column + HEAD_SIZE],
                    q_gain,
                    at,
                    0,
                )

    core, line = lax.rem(links.uly, 2), lax.div(links.uly, 2)

    def add(target, source):
        for kind in range(2):
            for head in range(kv_heads):
                target[kind, head] = target[kind, head] + source[kind, head]

    def core_sums(seq):
        copies = [
            links.to(
                grad_kv.at[seq, row * 2 + 1 - core], from_core.at[seq, row], links.core_way
            )
            for row in range(2)
        ]
        return copies

    def across_sums(seq, copies):
        for row in range(2):
            copies[row].arrived()
            add(grad_kv.at[seq, row * 2 + core], from_core.at[seq, row])
        return links.to(
            grad_kv.at[seq, (1 - line) * 2 + core], from_across.at[seq], links.y_way
        )

    def own_keys(seq, copy):
        copy.arrived()
        for head in range(kv_heads):
            for blk in range(links.n_blk):
                row = (blk * seqs + seq) * blocks.toks
                at = pl.ds(blk * blocks.toks, blocks.toks)
                term = [
                    grad_kv[seq, links.uly, kind, head, at, :].astype(jnp.float32)
                    + from_across[seq, kind, head, at, :].astype(jnp.float32)
                    for kind in range(2)
                ]
                k_at = q_end + head * HEAD_SIZE
                v_at = k_end + head * HEAD_SIZE
                grad_qkv[row : row + blocks.toks, k_at : k_at + HEAD_SIZE] = back_norm(
                    term[0],
                    qkv[row : row + blocks.toks, k_at : k_at + HEAD_SIZE],
                    k_gain,
                    at,
                    1,
                )
                grad_qkv[row : row + blocks.toks, v_at : v_at + HEAD_SIZE] = term[1].astype(
                    jnp.bfloat16
                )

    stage, last = None, []
    for seq in range(seqs):
        for head in range(kv_heads):
            back(seq, head)
            if seq == 0 and head == kv_heads - 1:
                out.sum.tick(1)
                down.second_way()
            if seq == 1 and head == 0:
                for tick in range(2, links.n_blk - 1):
                    out.sum.tick(tick)
            if stage is not None:
                last.append((seq - 1, across_sums(seq - 1, stage)))
                stage = None
        stage = core_sums(seq)
    last.append((seqs - 1, across_sums(seqs - 1, stage)))
    for seq, copy in last:
        own_keys(seq, copy)

    def write(block, rows, values):
        grad_down[block, rows, :] = values

    down.result(write)
    out.write(output)
    out.sum.sent()
    for copy in keep:
        copy.wait()
    for copy in swapped:
        copy.arrived()
    links.finish()


def attend_back(
    all_low,
    wo,
    queries,
    key_values,
    lse,
    qkv,
    q_gain,
    k_gain,
    cosine,
    sine,
    query_pos,
    key_pos,
    out_parts,
    middle,
    grad_gate,
    grad_up,
    part_down,
):
    seqs, kv_heads, q_rows, _ = queries.shape
    n_uly, _, _, _, q_len, _ = key_values.shape
    rows = all_low.shape[0]
    keys = key_pos.shape[0]
    f32, low = jnp.float32, jnp.bfloat16
    scratch = [
        ((keys, q_rows), f32),
        ((rows, wo.shape[0]), f32),
        (queries.shape, low),
        ((keys, q_rows), f32),
        ((keys, q_rows), f32),
        ((seqs, n_uly, 2, kv_heads, q_len, HEAD_SIZE), low),
        ((seqs, 2, 2, kv_heads, q_len, HEAD_SIZE), low),
        ((seqs, 2, kv_heads, q_len, HEAD_SIZE), low),
        (part_down.shape, low),
    ]
    n_dp, _, _, depth, width = part_down.shape
    n_blk, tokens, _ = out_parts.shape
    scratch += [(shape, low) for shape in plane_shapes(n_dp, 1, n_uly, depth, width)[2:]]
    return pl.pallas_call(
        attention_back_kernel,
        out_shape=[
            jax.ShapeDtypeStruct(qkv.shape, low),
            jax.ShapeDtypeStruct((8, HEAD_SIZE), f32),
            jax.ShapeDtypeStruct((1, depth, width), f32),
            jax.ShapeDtypeStruct((tokens // 2, width), low),
            jax.ShapeDtypeStruct(grad_gate.shape, low),
            jax.ShapeDtypeStruct(grad_up.shape, low),
        ],
        in_specs=[VMEM] * 14 + [HBM] * 3,
        out_specs=[VMEM] * 4 + [HBM] * 2,
        scratch_shapes=[pltpu.VMEM(shape, kind) for shape, kind in scratch]
        + output_scratch(n_blk, tokens, width)
        + semaphores(40),
        compiler_params=kernel_params(5),
    )(
        all_low,
        wo,
        queries,
        key_values,
        lse,
        qkv,
        q_gain,
        k_gain,
        cosine,
        sine,
        query_pos,
        key_pos,
        out_parts,
        middle,
        grad_gate,
        grad_up,
        part_down,
    )


def middle_kernel(
    heads,
    wo,
    source,
    gain,
    rows_wg,
    rows_wu,
    _,
    middle,
    all_normed,
    all_wg,
    all_wu,
    all_cot,
    parts,
    rightward,
    leftward,
    normed,
    send,
    recv,
    here,
):
    links = Links(send, recv, here)
    links.greet(links.peers() + [links.x_way, links.y_way, links.core_way])
    planes, keep = [], []
    for chunk, whole in ((rows_wg, all_wg), (rows_wu, all_wu)):
        at = rows_of(whole, True)
        plane = PlaneGather(links, at)
        plane.start(chunk)
        planes.append(plane)
        keep.append(links.local(chunk, at(links.dp, links.uly)))
    tokens = source.shape[0]
    for blk in (links.n_blk - 1, 0) + tuple(range(1, links.n_blk - 1)):
        parts[blk] = jnp.dot(heads[blk], wo[...], preferred_element_type=jnp.float32).astype(
            jnp.bfloat16
        )
    sums = halved_sums(links, parts, rightward, leftward)
    for half in sums:
        half.start()
    cot_lines = HalvedLine(links, None, all_cot).lines
    cot_lines[0].send(1)
    lines = []

    def settle(half, rows_of_half):
        half.finish(middle.at[rows_of_half])

        def body(rows):
            at = pl.ds(pl.multiple_of(rows_of_half.start + rows.start, ROWS), ROWS)
            total = middle[at, :] + source[at, :].astype(jnp.float32)
            middle[at, :] = total
            normed[at, :] = (total * rms_scale(total) * gain[...]).astype(jnp.bfloat16)

        each_block(tokens // 2, body)
        line = LineGather(links, normed.at[rows_of_half], all_normed.at[:, rows_of_half])
        line.send(0)
        lines.append(line)

    spans = halves(tokens)
    for tick in range(1, links.n_blk - 1):
        sums[0].tick(tick)
        if tick == 1:
            cot_lines[1].send(1)
    settle(sums[0], spans[0])
    planes[0].hand_on()
    for tick in range(1, links.n_blk - 1):
        sums[1].tick(tick)
        for line in cot_lines:
            line.arrived()
            if tick + 1 < links.n_blk - 1:
                line.send(tick + 1)
    settle(sums[1], spans[1])
    keep.append(links.local(normed, all_normed.at[links.blk]))
    for step in range(1, links.n_blk - 1):
        for line in lines:
            line.arrived()
            line.send(step)
        if step == 1:
            planes[1].hand_on()
        if step == 2:
            planes[0].last()
    planes[1].last()
    for line in lines:
        line.arrived()
    for plane in planes:
        plane.arrived()
    for copy in keep:
        copy.wait()
    for half in sums:
        half.sent()
    links.finish()


def exchange_middle(heads, wo, source, gain, rows_wg, rows_wu, all_cot):
    n_dp, n_blk, n_uly = (lax.axis_size(a) for a in EVERY)
    tokens, width = source.shape
    low = [(n_blk, tokens, width)]
    low += [(n_dp, n_blk, n_uly) + chunk.shape[1:] for chunk in (rows_wg, rows_wu)]
    low.append(all_cot.shape)
    return pl.pallas_call(
        middle_kernel,
        out_shape=[jax.ShapeDtypeStruct((tokens, width), jnp.float32)]
        + [jax.ShapeDtypeStruct(shape, jnp.bfloat16) for shape in low],
        in_specs=[VMEM] * 4 + [HBM] * 3,
        out_specs=[VMEM] + [HBM] * 4,
        input_output_aliases={6: 4},
        scratch_shapes=[pltpu.VMEM((n_blk, tokens, width), jnp.bfloat16)]
        + line_scratch(n_blk, tokens, width)
        + [pltpu.VMEM((tokens, width), jnp.bfloat16)]
        + semaphores(64),
        compiler_params=kernel_params(2),
    )(heads, wo, source, gain, rows_wg, rows_wu, all_cot)


def back_rows(grad_normed, source, gain):
    scale = rms_scale(source)
    unit = source * scale
    scaled = grad_normed * gain
    back = scale * (scaled - unit * jnp.mean(scaled * unit, axis=-1, keepdims=True))
    return back, jnp.sum(grad_normed * unit, axis=0, keepdims=True)


def back_kernel(
    grad_parts,
    middle,
    cotangent,
    gain,
    all_normed,
    grad_gate_pre,
    grad_up_pre,
    activated,
    all_cot,
    grad_middle,
    gain_term,
    all_low,
    grad_gate,
    grad_up,
    part_down,
    rightward,
    leftward,
    low,
    gate_1,
    gate_2,
    gate_3,
    gate_4,
    gate_5,
    gate_6,
    up_1,
    up_2,
    up_3,
    up_4,
    up_5,
    up_6,
    down_1,
    down_2,
    send,
    recv,
    here,
):
    links = Links(send, recv, here)
    links.greet(links.peers() + [links.x_way, links.y_way, links.core_way])
    sums = halved_sums(links, grad_parts, rightward, leftward)
    for half in sums:
        half.start()
    gate = PlaneScatter(links, gate_1, gate_2, gate_3, gate_4, gate_5, gate_6)
    up = PlaneScatter(links, up_1, up_2, up_3, up_4, up_5, up_6)
    down = PlaneScatter(links, down_1, down_2, None, None, None, None)
    gain_term[...] = jnp.zeros_like(gain_term)
    tokens = middle.shape[0]
    spans, lines, keep = halves(tokens), [], []

    def compute(plane, which, left, right):
        dp = links.dp if which == 1 else links.other_dp
        weight_grad(left, right, plane.parts, dp)
        plane.between_cores(which)

    def settle(half, rows_of_half):
        half.finish(grad_middle.at[rows_of_half])

        def body(rows):
            at = pl.ds(pl.multiple_of(rows_of_half.start + rows.start, ROWS), ROWS)
            back, term = back_rows(grad_middle[at, :], middle[at, :], gain[...])
            grad = cotangent[at, :].astype(jnp.float32) + back
            gain_term[...] += term
            grad_middle[at, :] = grad
            low[at, :] = grad.astype(jnp.bfloat16)

        each_block(tokens // 2, body)
        line = LineGather(links, low.at[rows_of_half], all_low.at[:, rows_of_half])
        line.send(0)
        lines.append(line)

    ticks = range(1, links.n_blk - 1)
    compute(gate, 0, all_normed, grad_gate_pre)
    compute(gate, 1, all_normed, grad_gate_pre)
    for tick in ticks:
        sums[0].tick(tick)
        if tick == 1:
            gate.across_chips()
    compute(up, 0, all_normed, grad_up_pre)
    settle(sums[0], spans[0])
    compute(up, 1, all_normed, grad_up_pre)
    for tick in ticks:
        sums[1].tick(tick)
        if tick == 1:
            up.across_chips()
            compute(down, 0, activated, all_cot)
    compute(down, 1, activated, all_cot)
    settle(sums[1], spans[1])
    keep.append(links.local(low, all_low.at[links.blk]))
    gate.second_way()
    for step in range(1, links.n_blk - 1):
        for line in lines:
            line.arrived()
            line.send(step)
        if step == 1:
            for which in (0, 1):
                down.core_sums(which)
            for dp in range(links.n_dp):
                for row in range(2):
                    keep.append(
                        links.local(down.chunk(dp, row, down.core), part_down.at[dp, row])
                    )
            up.second_way()
    for line in lines:
        line.arrived()

    def into(target):
        def write(block, rows, values):
            target[block, rows, :] = values.astype(target.dtype)

        return write

    gate.result(into(grad_gate))
    up.result(into(grad_up))
    for copy in keep:
        copy.wait()
    for half in sums:
        half.sent()
    links.finish()


def exchange_back(
    grad_parts,
    middle,
    cotangent,
    gain,
    all_normed,
    grad_gate_pre,
    grad_up_pre,
    activated,
    all_cot,
):
    n_dp, n_blk, n_uly = (lax.axis_size(a) for a in EVERY)
    _, tokens, width = grad_parts.shape
    ff = grad_gate_pre.shape[1]
    depth = width // (n_dp * n_blk * n_uly)
    down_depth = ff // (n_dp * n_uly)
    return pl.pallas_call(
        back_kernel,
        out_shape=[
            jax.ShapeDtypeStruct((tokens, width), jnp.float32),
            jax.ShapeDtypeStruct((1, width), jnp.float32),
            jax.ShapeDtypeStruct((n_blk, tokens, width), jnp.bfloat16),
            jax.ShapeDtypeStruct((n_blk, depth, ff), jnp.bfloat16),
            jax.ShapeDtypeStruct((n_blk, depth, ff), jnp.bfloat16),
            jax.ShapeDtypeStruct((n_dp, 2, 1, down_depth, width), jnp.bfloat16),
        ],
        in_specs=[VMEM] * 9,
        out_specs=[VMEM, VMEM, HBM, VMEM, VMEM, HBM],
        scratch_shapes=line_scratch(n_blk, tokens, width)
        + [pltpu.VMEM((tokens, width), jnp.bfloat16)]
        + plane_scratch(n_dp, n_blk, n_uly, depth, ff) * 2
        + plane_scratch(n_dp, 1, n_uly, down_depth, width)[:2]
        + semaphores(72),
        compiler_params=kernel_params(3),
    )(
        grad_parts,
        middle,
        cotangent,
        gain,
        all_normed,
        grad_gate_pre,
        grad_up_pre,
        activated,
        all_cot,
    )


def last_kernel(
    w_qkv,
    hidden,
    grad_middle,
    gain,
    normed,
    grad_qkv,
    heads,
    all_low,
    mlp_term,
    head_terms,
    out_parts,
    middle,
    grad_hidden,
    grad_w_qkv,
    grad_wo,
    small_sum,
    output,
    grad_parts,
    rightward,
    leftward,
    qkv_1,
    qkv_2,
    qkv_3,
    qkv_4,
    qkv_5,
    qkv_6,
    wo_1,
    wo_2,
    wo_3,
    wo_4,
    wo_5,
    wo_6,
    summed,
    small,
    attn_term,
    small_in,
    small_total,
    out_right,
    out_left,
    out_total,
    send,
    recv,
    here,
):
    links = Links(send, recv, here)
    links.greet(links.peers() + [links.x_way, links.y_way, links.core_way])
    sums = halved_sums(links, grad_parts, rightward, leftward)
    qkv = PlaneScatter(links, qkv_1, qkv_2, qkv_3, qkv_4, qkv_5, qkv_6)
    out = PlaneScatter(links, wo_1, wo_2, wo_3, wo_4, wo_5, wo_6)

    output_half = OutputHalf(links, 1, out_parts, middle, out_right, out_left, out_total)
    for which, dp in ((0, links.other_dp), (1, links.dp)):
        weight_grad(normed, grad_qkv, qkv_1, dp)
        qkv.between_cores(which)
    attn_term[...] = jnp.zeros_like(attn_term)
    tokens = grad_parts.shape[1]
    for column in range(0, w_qkv.shape[0], 512):
        grad_parts[:, :, column : column + 512] = (
            product_right(grad_qkv[...], w_qkv[column : column + 512, :])
            .astype(jnp.bfloat16)
            .reshape(links.n_blk, tokens, 512)
        )
    for half in sums:
        half.start()
    output_half.sum.start()
    qkv.across_chips()

    def collect(rows):
        for blk in range(links.n_blk):
            source = hidden[blk, rows, :].astype(jnp.float32)
            part = grad_parts[blk, rows, :].astype(jnp.float32)
            attn_term[...] += jnp.sum(part * (source * rms_scale(source)), axis=0, keepdims=True)

    each_block(tokens, collect)
    sums[0].tick(1)
    for tick in range(2, links.n_blk - 1):
        sums[0].tick(tick)
    small[...] = jnp.zeros_like(small)
    span = gain.shape[1] // 128
    for index in range(span):
        columns = slice(index * 128, (index + 1) * 128)
        small[index : index + 1, :] = attn_term[:, columns]
        small[span + index : span + index + 1, :] = mlp_term[:, columns]
    small[2 * span : 2 * span + 8, :] = head_terms[...]
    small_in[links.blk] = small[...]
    small_copies = [links.to(small, small_in.at[links.blk], device) for device in links.peers()]
    for which, dp in ((0, links.other_dp), (1, links.dp)):
        weight_grad(heads, all_low, wo_1, dp)
        out.between_cores(which)
    sums[1].tick(1)
    out.across_chips()
    for copy in small_copies:
        copy.arrived()
    total = small_in[0]
    for blk in range(1, links.n_blk):
        total = total + small_in[blk]
    small_total[0] = total
    pending = links.to(small_total.at[0], small_in.at[links.n_blk], links.x_way)
    qkv.second_way()
    pending.arrived()
    small_total[1] = small_total[0] + small_in[links.n_blk]
    pending = links.to(small_total.at[1], small_in.at[links.n_blk + 1], links.y_way)
    for tick in range(2, links.n_blk - 1):
        sums[1].tick(tick)
    output_half.sum.tick(1)
    out.second_way()
    pending.arrived()
    small_total[2] = small_total[1] + small_in[links.n_blk + 1]
    pending = links.to(small_total.at[2], small_in.at[links.n_blk + 2], links.core_way)

    def write(block, rows, values):
        summed[block, rows, :] = values.astype(jnp.bfloat16)

    qkv.result(write)
    swapped = []
    for step in range(1, links.n_blk):
        peer = links.peer(step)
        swapped.append(
            links.to(summed.at[peer], grad_w_qkv.at[links.blk], (links.dp, peer, links.uly))
        )
    keep = links.local(summed.at[links.blk], grad_w_qkv.at[links.blk])
    for tick in range(2, links.n_blk - 1):
        output_half.sum.tick(tick)
    pending.arrived()
    small_sum[...] = small_total[2] + small_in[links.n_blk + 2]
    for half, rows_of_half in zip(sums, halves(tokens)):
        half.finish(grad_hidden.at[rows_of_half])

    def body(rows):
        back, _ = back_rows(
            grad_hidden[rows, :], hidden[links.blk, rows, :].astype(jnp.float32), gain[...]
        )
        grad_hidden[rows, :] = grad_middle[rows, :] + back

    each_block(tokens, body)

    def write_out(block, rows, values):
        grad_wo[block, rows, :] = values

    out.result(write_out)
    output_half.write(output)
    output_half.sum.sent()
    for copy in swapped:
        copy.arrived()
    keep.wait()
    for half in sums:
        half.sent()
    links.finish()


def exchange_last(
    w_qkv,
    hidden,
    grad_middle,
    gain,
    normed,
    grad_qkv,
    heads,
    all_low,
    mlp_term,
    head_terms,
    out_parts,
    middle,
):
    n_dp, n_blk, n_uly = (lax.axis_size(a) for a in EVERY)
    _, tokens, width = hidden.shape
    columns = grad_qkv.shape[1]
    depth = width // (n_dp * n_blk * n_uly)
    out_depth = heads.shape[1] // (n_dp * n_uly)
    small = (2 * width // 128 + 8, 128)
    return pl.pallas_call(
        last_kernel,
        out_shape=[
            jax.ShapeDtypeStruct((tokens, width), jnp.float32),
            jax.ShapeDtypeStruct((n_blk, depth, columns), jnp.bfloat16),
            jax.ShapeDtypeStruct((1, out_depth, width), jnp.float32),
            jax.ShapeDtypeStruct(small, jnp.float32),
            jax.ShapeDtypeStruct((tokens // 2, width), jnp.bfloat16),
        ],
        in_specs=[VMEM] * 12,
        out_specs=[VMEM, HBM, VMEM, VMEM, VMEM],
        scratch_shapes=[pltpu.VMEM((n_blk, tokens, width), jnp.bfloat16)]
        + line_scratch(n_blk, tokens, width)
        + plane_scratch(n_dp, n_blk, n_uly, depth, columns)
        + plane_scratch(n_dp, 1, n_uly, out_depth, width)
        + [
            pltpu.VMEM((n_blk, depth, columns), jnp.bfloat16),
            pltpu.VMEM(small, jnp.float32),
            pltpu.VMEM((1, width), jnp.float32),
            pltpu.VMEM((n_blk + 3,) + small, jnp.float32),
            pltpu.VMEM((3,) + small, jnp.float32),
        ]
        + output_scratch(n_blk, tokens, width)
        + semaphores(64),
        compiler_params=kernel_params(4),
    )(
        w_qkv,
        hidden,
        grad_middle,
        gain,
        normed,
        grad_qkv,
        heads,
        all_low,
        mlp_term,
        head_terms,
        out_parts,
        middle,
    )


def finish_kernel(
    gate,
    up,
    qkv,
    wo,
    wd,
    hidden,
    out_0,
    out_1,
    small,
    f_gate,
    f_up,
    f_q,
    f_k,
    f_v,
    f_wo,
    f_wd,
    f_hidden,
    f_out,
    f_attn,
    f_mlp,
):
    n_blk, depth, _ = gate.shape

    def place(source, offset, target):
        width = target.shape[1] // (n_blk * 2)
        for blk in range(n_blk):
            for group in range(2):
                to = (group * n_blk + blk) * width
                at = offset + group * width
                target[:, to : to + width] = source[blk, :, at : at + width].astype(jnp.float32)

    place(gate, 0, f_gate)
    place(up, 0, f_up)
    q_width = f_q.shape[1] // n_blk
    k_width = f_k.shape[1] // n_blk
    place(qkv, 0, f_q)
    place(qkv, q_width, f_k)
    place(qkv, q_width + k_width, f_v)
    f_wo[...] = wo[0]
    f_wd[...] = wd[0]
    f_hidden[...] = hidden[...]
    half = out_0.shape[0]
    f_out[:half, :] = out_0[...]
    f_out[half:, :] = out_1[...]
    size = f_attn.shape[1]
    device = (lax.axis_index(DP) * n_blk + lax.axis_index(BLK)) * lax.axis_size(ULY)
    device = device + lax.axis_index(ULY)
    per_row = 128 // size
    span = (2 * n_blk * lax.axis_size(ULY)) // per_row
    for first, target in ((0, f_attn), (span, f_mlp)):
        row = small[pl.ds(first + lax.div(device, per_row), 1), :]
        value = row[:, :size]
        for place_in_row in range(1, per_row):
            here = lax.rem(device, per_row) == place_in_row
            value = jnp.where(
                here, row[:, place_in_row * size : (place_in_row + 1) * size], value
            )
        target[...] = value


def finish(gate, up, qkv, wo, wd, hidden, out_0, out_1, small, gain_rows, shapes):
    return pl.pallas_call(
        finish_kernel,
        out_shape=[jax.ShapeDtypeStruct(shape, jnp.float32) for shape in shapes]
        + [
            jax.ShapeDtypeStruct(wo.shape[1:], jnp.float32),
            jax.ShapeDtypeStruct(wd.shape[1:], jnp.float32),
            jax.ShapeDtypeStruct(hidden.shape, jnp.float32),
            jax.ShapeDtypeStruct(hidden.shape, jnp.bfloat16),
            jax.ShapeDtypeStruct((1, gain_rows), jnp.float32),
            jax.ShapeDtypeStruct((1, gain_rows), jnp.float32),
        ],
        in_specs=[VMEM] * 9,
        out_specs=[VMEM] * 11,
        compiler_params=pltpu.CompilerParams(vmem_limit_bytes=62 * MIB),
    )(gate, up, qkv, wo, wd, hidden, out_0, out_1, small)


def product(left, right):
    return jnp.dot(left, right, preferred_element_type=jnp.float32)


def shards(
    hidden,
    span_order,
    attn_gain,
    w_query,
    key_weight,
    value_weight,
    w_out,
    q_gain,
    k_gain,
    mlp_gain,
    w_gate,
    w_up,
    w_down,
    cotangent,
):
    seqs, toks, width = hidden.shape
    n_dp, n_blk, n_uly = (lax.axis_size(a) for a in EVERY)
    rows = n_blk * seqs * toks
    f32, bf16 = jnp.float32, jnp.bfloat16
    own_hidden = hidden.reshape(seqs * toks, width)
    own_cotangent = cotangent.reshape(seqs * toks, width)

    gain_q, gain_k = q_gain.astype(f32)[None, :], k_gain.astype(f32)[None, :]

    gain_rows = attn_gain.shape[0]
    own_gains = jnp.pad(jnp.stack([attn_gain, mlp_gain]), ((0, 30), (0, 128 - gain_rows)))
    (
        all_hidden,
        w_qkv,
        wo,
        g_attn,
        g_mlp,
        cosine,
        sine,
        query_pos,
        key_pos,
    ) = gather_front(
        span_order,
        own_hidden,
        w_query,
        key_weight,
        value_weight,
        w_out,
        own_gains,
        toks,
        gain_rows,
    )
    w_qkv = w_qkv.reshape(width, -1)
    wo = wo.reshape(-1, width)
    (
        rows_wg,
        rows_wu,
        all_wd,
        cot,
        heads_flat,
        normed,
        qkv,
        queries,
        key_values,
        lse,
    ) = attend_forward(
        w_gate,
        w_up,
        w_down,
        own_cotangent,
        all_hidden.reshape(rows, width),
        w_qkv,
        g_attn,
        gain_q,
        gain_k,
        cosine,
        sine,
        query_pos,
        key_pos,
        seqs,
    )
    middle, normed2, all_wg, all_wu, cot = exchange_middle(
        heads_flat.reshape(n_blk, seqs * toks, -1),
        wo,
        own_hidden,
        g_mlp,
        rows_wg,
        rows_wu,
        cot,
    )
    wg, wu = all_wg.reshape(width, -1), all_wu.reshape(width, -1)
    wd = all_wd.reshape(-1, width)
    cot = cot.reshape(rows, width)
    normed2 = normed2.reshape(rows, width)
    gate_pre = product(normed2, wg)
    up_pre = product(normed2, wu)
    sigmoid_gate = jax.nn.sigmoid(gate_pre)
    activated = (gate_pre * sigmoid_gate * up_pre).astype(bf16)
    out_parts = product(activated, wd).astype(bf16)
    grad_act = product_right(cot, wd)
    grad_gate_pre = (
        grad_act * up_pre * sigmoid_gate * (1.0 + gate_pre * (1.0 - sigmoid_gate))
    ).astype(bf16)
    grad_up_pre = (grad_act * gate_pre * sigmoid_gate).astype(bf16)
    grad_parts = (product_right(grad_gate_pre, wg) + product_right(grad_up_pre, wu)).astype(bf16)
    blocks = (n_blk, seqs * toks, width)
    grad_middle, mlp_gain_term, middle_low, grad_gate, grad_up, part_down = exchange_back(
        grad_parts.reshape(blocks),
        middle,
        own_cotangent,
        g_mlp,
        normed2,
        grad_gate_pre,
        grad_up_pre,
        activated,
        cot,
    )
    middle_low = middle_low.reshape(rows, width)
    out_parts = out_parts.reshape(blocks)
    grad_qkv, head_terms, grad_down, output_0, grad_gate, grad_up = attend_back(
        middle_low,
        wo,
        queries,
        key_values,
        lse,
        qkv,
        gain_q,
        gain_k,
        cosine,
        sine,
        query_pos,
        key_pos,
        out_parts,
        middle,
        grad_gate,
        grad_up,
        part_down,
    )
    grad_hidden, grad_w_qkv, grad_out, small, output_1 = exchange_last(
        w_qkv,
        all_hidden,
        grad_middle,
        g_attn,
        normed,
        grad_qkv,
        heads_flat,
        middle_low,
        mlp_gain_term,
        head_terms,
        out_parts,
        middle,
    )
    (
        grad_gate,
        grad_up,
        grad_query,
        grad_key,
        grad_value,
        grad_out,
        grad_down,
        grad_hidden,
        output,
        grad_attn_gain,
        grad_mlp_gain,
    ) = finish(
        grad_gate,
        grad_up,
        grad_w_qkv,
        grad_out,
        grad_down,
        grad_hidden,
        output_0,
        output_1,
        small,
        gain_rows,
        [w.shape for w in (w_gate, w_up, w_query, key_weight, value_weight)],
    )
    small = small.reshape(-1)
    grad_q_gain = small[2 * width : 2 * width + HEAD_SIZE]
    grad_k_gain = small[2 * width + HEAD_SIZE : 2 * width + 2 * HEAD_SIZE]
    return (
        output.reshape(hidden.shape),
        grad_hidden.reshape(hidden.shape),
        grad_attn_gain.reshape(gain_rows),
        grad_query,
        grad_key,
        grad_value,
        grad_out,
        grad_q_gain,
        grad_k_gain,
        grad_mlp_gain.reshape(gain_rows),
        grad_gate,
        grad_up,
        grad_down,
    )


def solution(mesh):
    n_dp, n_blk, n_uly = (mesh.shape[a] for a in EVERY)
    aligned = (n_dp, n_uly) == (2, 4) and KEY_VALUE_HEADS % (n_dp * n_blk) == 0
    in_specs = (
        TOKENS,
        P(),
        P(EVERY),
        P(EVERY, None),
        P(EVERY, None),
        P(EVERY, None),
        P(EVERY, None),
        P(),
        P(),
        P(EVERY),
        P(EVERY, None),
        P(EVERY, None),
        P(EVERY, None),
        TOKENS,
    )
    out_specs = (
        TOKENS,
        TOKENS,
        P(EVERY),
        P(EVERY, None),
        P(EVERY, None),
        P(EVERY, None),
        P(EVERY, None),
        P(),
        P(),
        P(EVERY),
        P(EVERY, None),
        P(EVERY, None),
        P(EVERY, None),
    )
    return jax.shard_map(
        shards if aligned else shards_general,
        mesh=mesh, in_specs=in_specs, out_specs=out_specs, check_vma=False)
```

```python
import functools
import math

import jax
import jax.numpy as jnp
from jax import lax
from jax.experimental import pallas as pl
from jax.experimental.pallas import tpu as pltpu
from jax.sharding import PartitionSpec as P

QUERY_HEADS = 16
KEY_VALUE_HEADS = 8
HEAD_SIZE = 128


DP, BLK, ULY = "dp", "blk", "uly"
EVERY = (DP, BLK, ULY)
PLANE = (DP, ULY)
TOKENS = P(DP, (BLK, ULY), None)
EQ_KGQD_NKD_TO_KGQN = "kgqd,nkd->kgqn"
EQ_KGQN_KGQD_TO_NKD = "kgqn,kgqd->nkd"
EQ_KGQN_NKD_TO_KGQD = "kgqn,nkd->kgqd"
EQ_KGQN_QKGD_TO_NKD = "kgqn,qkgd->nkd"
EQ_QKGD_NKD_TO_KGQN = "qkgd,nkd->kgqn"
EQ_STD_DE_TO_STE = "std,de->ste"
EQ_STD_DF_TO_STF = "std,df->stf"
EQ_STD_ED_TO_STE = "std,ed->ste"
EQ_STD_FD_TO_STF = "std,fd->stf"
EQ_STD_STE_TO_DE = "std,ste->de"
EQ_STD_STF_TO_DF = "std,stf->df"
EQ_STE_DE_TO_STD = "ste,de->std"
EQ_STE_ED_TO_STD = "ste,ed->std"
EQ_STE_STD_TO_ED = "ste,std->ed"
EQ_STF_DF_TO_STD = "stf,df->std"
EQ_STF_FD_TO_STD = "stf,fd->std"
EQ_STF_STD_TO_FD = "stf,std->fd"

EPSILON = 1e-06
ROPE_BASE = 1000000.0


def rms_scale(source):
    return lax.rsqrt(jnp.mean(source * source, axis=-1, keepdims=True) + EPSILON)


def norm_back(grad_normed, source, norm_scale, gain):
    unit_rows = source * norm_scale
    scaled = grad_normed * gain
    return norm_scale * (scaled - unit_rows * jnp.mean(scaled * unit_rows, axis=-1, keepdims=True))


def angles_of(positions, head_dim):
    freq_steps = jnp.arange(head_dim // 2, dtype=jnp.float32)
    inverse = jnp.exp(freq_steps * (-2.0 * math.log(ROPE_BASE) / head_dim))
    return positions.astype(jnp.float32)[:, None] * inverse[None, :]


def rotate(source, angles, direction):
    half_dim = source.shape[-1] // 2
    cosine = jnp.cos(angles)[:, None, :]
    sine_part = direction * jnp.sin(angles)[:, None, :]
    first_half = source[..., :half_dim]
    second_half = source[..., half_dim:]
    return jnp.concatenate(
        [
            first_half * cosine - second_half * sine_part,
            second_half * cosine + first_half * sine_part,
        ],
        axis=-1,
    )


def positions_of(places, span_order, half_len):
    blocks_of = places // half_len
    block_ids = jnp.arange(span_order.shape[0], dtype=jnp.int32)
    chosen = jnp.sum(
        jnp.where(blocks_of[:, None] == block_ids[None, :], span_order[None, :], 0), axis=1
    )
    return chosen * half_len + places % half_len


def add_rows(buffer, new_rows):
    return buffer + new_rows


def shards_general(
    hidden,
    span_order,
    attn_gain,
    w_query,
    key_weight,
    value_weight,
    w_out,
    q_gain,
    k_gain,
    mlp_gain,
    w_gate,
    w_up,
    w_down,
    cotangent,
):
    sequence_count = hidden.shape[0]
    token_count = hidden.shape[1]
    ulysses_group_size = lax.axis_size(ULY)
    local_q = QUERY_HEADS // ulysses_group_size
    local_key_value = KEY_VALUE_HEADS // ulysses_group_size
    query_group_width = QUERY_HEADS // KEY_VALUE_HEADS
    block_len = token_count * ulysses_group_size
    half_len = block_len // 2
    score_scale = 1.0 / math.sqrt(HEAD_SIZE)
    blk_index = lax.axis_index(BLK)
    uly_index = lax.axis_index(ULY)
    first_place = (blk_index * ulysses_group_size + uly_index) * token_count
    local_angles = angles_of(
        positions_of(first_place + jnp.arange(token_count, dtype=jnp.int32), span_order, half_len),
        HEAD_SIZE,
    )
    query_pos = positions_of(
        blk_index * block_len + jnp.arange(block_len, dtype=jnp.int32), span_order, half_len
    )
    g_attn, wq_all, wk_all, wv_all, wo_all = (
        lax.all_gather(attn_gain, EVERY, axis=0, tiled=True),
        lax.all_gather(w_query, EVERY, axis=0, tiled=True),
        lax.all_gather(key_weight, EVERY, axis=0, tiled=True),
        lax.all_gather(value_weight, EVERY, axis=0, tiled=True),
        lax.all_gather(w_out, EVERY, axis=0, tiled=True),
    )
    source = hidden.astype(jnp.float32)
    first_scale = rms_scale(source)
    normalized_input = (source * first_scale * g_attn.astype(jnp.float32)).astype(jnp.bfloat16)
    q_pre = jnp.einsum(
        EQ_STD_DE_TO_STE, normalized_input, wq_all, preferred_element_type=jnp.float32
    ).reshape(sequence_count, token_count, QUERY_HEADS, HEAD_SIZE)
    key_before_norm = jnp.einsum(
        EQ_STD_DE_TO_STE, normalized_input, wk_all, preferred_element_type=jnp.float32
    ).reshape(sequence_count, token_count, KEY_VALUE_HEADS, HEAD_SIZE)
    value_before_norm = jnp.einsum(
        EQ_STD_DE_TO_STE, normalized_input, wv_all, preferred_element_type=jnp.float32
    ).reshape(sequence_count, token_count, KEY_VALUE_HEADS, HEAD_SIZE)
    q_scale = rms_scale(q_pre)
    k_scale = rms_scale(key_before_norm)
    gain_q = q_gain.astype(jnp.float32)
    gain_k = k_gain.astype(jnp.float32)
    q_rot = rotate(q_pre * q_scale * gain_q, local_angles, 1.0).astype(jnp.bfloat16)
    k_rot = rotate(key_before_norm * k_scale * gain_k, local_angles, 1.0).astype(jnp.bfloat16)
    v_low = value_before_norm.astype(jnp.bfloat16)
    q_heads, k_heads, v_heads = (
        lax.all_to_all(q_rot, ULY, split_axis=2, concat_axis=1, tiled=True),
        lax.all_to_all(k_rot, ULY, split_axis=2, concat_axis=1, tiled=True),
        lax.all_to_all(v_low, ULY, split_axis=2, concat_axis=1, tiled=True),
    )
    q_group = q_heads.reshape(
        sequence_count, block_len, local_key_value, query_group_width, HEAD_SIZE
    )
    stat_shape = (sequence_count, local_key_value, query_group_width, block_len)
    start_state = (
        jnp.full(stat_shape, -1e30, jnp.float32),
        jnp.zeros(stat_shape, jnp.float32),
        jnp.zeros(stat_shape + (HEAD_SIZE,), jnp.float32),
    )
    key_piece = lax.all_gather(k_heads, BLK, axis=1, tiled=True)
    value_piece = lax.all_gather(v_heads, BLK, axis=1, tiled=True)
    key_pos = positions_of(jnp.arange(key_piece.shape[1], dtype=jnp.int32), span_order, half_len)
    allowed = query_pos[:, None] >= key_pos[None, :]

    def attend_one_sequence(members):
        query_rows, key_rows, value_rows, top_seq, total_seq, accum_seq = members
        scores = (
            jnp.einsum(EQ_QKGD_NKD_TO_KGQN, query_rows, key_rows, preferred_element_type=jnp.float32)
            * score_scale
        )
        scores = jnp.where(allowed, scores, -jnp.inf)
        new_top = jnp.maximum(top_seq, jnp.max(scores, axis=-1))
        fading = jnp.exp(top_seq - new_top)
        weights = jnp.exp(scores - new_top[..., None])
        total_seq = total_seq * fading + jnp.sum(weights, axis=-1)
        accum_seq = accum_seq * fading[..., None] + jnp.einsum(
            EQ_KGQN_NKD_TO_KGQD,
            weights.astype(jnp.bfloat16),
            value_rows,
            preferred_element_type=jnp.float32,
        )
        return (new_top, total_seq, accum_seq)

    row_top, row_total, accum = lax.map(
        attend_one_sequence,
        (q_group, key_piece, value_piece, start_state[0], start_state[1], start_state[2]),
    )
    log_total = row_top + jnp.log(row_total)
    attention_output = jnp.transpose(accum / row_total[..., None], (0, 3, 1, 2, 4)).reshape(
        sequence_count, block_len, local_q, HEAD_SIZE
    )
    heads_seq = lax.all_to_all(
        attention_output.astype(jnp.bfloat16), ULY, split_axis=1, concat_axis=2, tiled=True
    )
    heads_flat = heads_seq.reshape(sequence_count, token_count, QUERY_HEADS * HEAD_SIZE)
    middle = source + jnp.einsum(
        EQ_STE_ED_TO_STD, heads_flat, wo_all, preferred_element_type=jnp.float32
    )
    g_mlp, wg_all, wu_all, wd_all = (
        lax.all_gather(mlp_gain, EVERY, axis=0, tiled=True),
        lax.all_gather(w_gate, EVERY, axis=0, tiled=True),
        lax.all_gather(w_up, EVERY, axis=0, tiled=True),
        lax.all_gather(w_down, EVERY, axis=0, tiled=True),
    )
    second_scale = rms_scale(middle)
    gain_mlp = g_mlp.astype(jnp.float32)
    normed2 = (middle * second_scale * gain_mlp).astype(jnp.bfloat16)
    gate_pre = jnp.einsum(EQ_STD_DF_TO_STF, normed2, wg_all, preferred_element_type=jnp.float32)
    up_pre = jnp.einsum(EQ_STD_DF_TO_STF, normed2, wu_all, preferred_element_type=jnp.float32)
    sigmoid_gate = jax.nn.sigmoid(gate_pre)
    activated = (gate_pre * sigmoid_gate * up_pre).astype(jnp.bfloat16)
    result = middle + jnp.einsum(
        EQ_STF_FD_TO_STD, activated, wd_all, preferred_element_type=jnp.float32
    )
    output = result.astype(jnp.bfloat16)
    g_mlp, wg_all, wu_all, wd_all = (
        lax.all_gather(mlp_gain, EVERY, axis=0, tiled=True),
        lax.all_gather(w_gate, EVERY, axis=0, tiled=True),
        lax.all_gather(w_up, EVERY, axis=0, tiled=True),
        lax.all_gather(w_down, EVERY, axis=0, tiled=True),
    )
    gain_mlp = g_mlp.astype(jnp.float32)
    grad_act = jnp.einsum(EQ_STD_FD_TO_STF, cotangent, wd_all, preferred_element_type=jnp.float32)
    grad_gate_pre = (
        grad_act * up_pre * sigmoid_gate * (1.0 + gate_pre * (1.0 - sigmoid_gate))
    ).astype(jnp.bfloat16)
    grad_up_pre = (grad_act * gate_pre * sigmoid_gate).astype(jnp.bfloat16)
    grad_gate = jnp.einsum(
        EQ_STD_STF_TO_DF, normed2, grad_gate_pre, preferred_element_type=jnp.float32
    )
    grad_up = jnp.einsum(EQ_STD_STF_TO_DF, normed2, grad_up_pre, preferred_element_type=jnp.float32)
    grad_normed2 = jnp.einsum(
        EQ_STF_DF_TO_STD, grad_gate_pre, wg_all, preferred_element_type=jnp.float32
    ) + jnp.einsum(EQ_STF_DF_TO_STD, grad_up_pre, wu_all, preferred_element_type=jnp.float32)
    mlp_gain_term = jnp.sum(grad_normed2 * middle * second_scale, axis=(0, 1))
    grad_middle = cotangent.astype(jnp.float32) + norm_back(
        grad_normed2, middle, second_scale, gain_mlp
    )
    grad_mlp_gain, grad_gate, grad_up = (
        lax.psum_scatter(mlp_gain_term, EVERY, scatter_dimension=0, tiled=True),
        lax.psum_scatter(grad_gate, EVERY, scatter_dimension=0, tiled=True),
        lax.psum_scatter(grad_up, EVERY, scatter_dimension=0, tiled=True),
    )
    g_attn, wq_all, wk_all, wv_all, wo_all = (
        lax.all_gather(attn_gain, EVERY, axis=0, tiled=True),
        lax.all_gather(w_query, EVERY, axis=0, tiled=True),
        lax.all_gather(key_weight, EVERY, axis=0, tiled=True),
        lax.all_gather(value_weight, EVERY, axis=0, tiled=True),
        lax.all_gather(w_out, EVERY, axis=0, tiled=True),
    )
    middle_low = grad_middle.astype(jnp.bfloat16)
    grad_out = jnp.einsum(EQ_STE_STD_TO_ED, heads_flat, middle_low, preferred_element_type=jnp.float32)
    grad_heads = (
        jnp.einsum(EQ_STD_ED_TO_STE, middle_low, wo_all, preferred_element_type=jnp.float32)
        .astype(jnp.bfloat16)
        .reshape(sequence_count, token_count, QUERY_HEADS, HEAD_SIZE)
    )
    grad_heads_local = lax.all_to_all(grad_heads, ULY, split_axis=2, concat_axis=1, tiled=True)
    grad_group = jnp.transpose(
        grad_heads_local.reshape(
            sequence_count, block_len, local_key_value, query_group_width, HEAD_SIZE
        ),
        (0, 2, 3, 1, 4),
    )
    delta = jnp.sum(grad_heads_local.astype(jnp.float32) * attention_output, axis=-1)
    delta = jnp.transpose(
        delta.reshape(sequence_count, block_len, local_key_value, query_group_width), (0, 2, 3, 1)
    )
    seq_length = block_len * lax.axis_size(BLK)
    zero_keys = jnp.zeros((sequence_count, seq_length, local_key_value, HEAD_SIZE), jnp.float32)
    back_state = (jnp.zeros(stat_shape + (HEAD_SIZE,), jnp.float32), zero_keys, zero_keys)
    key_piece = lax.all_gather(k_heads, BLK, axis=1, tiled=True)
    value_piece = lax.all_gather(v_heads, BLK, axis=1, tiled=True)
    key_pos = positions_of(jnp.arange(key_piece.shape[1], dtype=jnp.int32), span_order, half_len)
    back_allowed = query_pos[:, None] >= key_pos[None, :]

    def back_one_sequence(members):
        query_rows, grad_rows, lse_seq, delta_seq, key_rows, value_rows, dq_seq, dk_seq, dv_seq = (
            members
        )
        scores = (
            jnp.einsum(EQ_QKGD_NKD_TO_KGQN, query_rows, key_rows, preferred_element_type=jnp.float32)
            * score_scale
        )
        scores = jnp.where(back_allowed, scores, -jnp.inf)
        probs = jnp.exp(scores - lse_seq[..., None])
        grad_values = jnp.einsum(
            EQ_KGQN_KGQD_TO_NKD,
            probs.astype(jnp.bfloat16),
            grad_rows,
            preferred_element_type=jnp.float32,
        )
        grad_probs = jnp.einsum(
            EQ_KGQD_NKD_TO_KGQN, grad_rows, value_rows, preferred_element_type=jnp.float32
        )
        grad_scores = (probs * (grad_probs - delta_seq[..., None])).astype(jnp.bfloat16)
        dq_seq = dq_seq + score_scale * jnp.einsum(
            EQ_KGQN_NKD_TO_KGQD, grad_scores, key_rows, preferred_element_type=jnp.float32
        )
        grad_keys = score_scale * jnp.einsum(
            EQ_KGQN_QKGD_TO_NKD, grad_scores, query_rows, preferred_element_type=jnp.float32
        )
        return (dq_seq, add_rows(dk_seq, grad_keys), add_rows(dv_seq, grad_values))

    grad_q_group, grad_k_whole, grad_v_whole = lax.map(
        back_one_sequence,
        (
            q_group,
            grad_group,
            log_total,
            delta,
            key_piece,
            value_piece,
            back_state[0],
            back_state[1],
            back_state[2],
        ),
    )
    grad_k_block, grad_v_block = (
        lax.psum_scatter(
            grad_k_whole.astype(jnp.bfloat16), BLK, scatter_dimension=1, tiled=True
        ).astype(jnp.float32),
        lax.psum_scatter(
            grad_v_whole.astype(jnp.bfloat16), BLK, scatter_dimension=1, tiled=True
        ).astype(jnp.float32),
    )
    grad_q_block = jnp.transpose(grad_q_group, (0, 3, 1, 2, 4)).reshape(
        sequence_count, block_len, local_q, HEAD_SIZE
    )
    grad_q_seq, grad_k_seq, value_sequence_gradient = (
        lax.all_to_all(
            grad_q_block.astype(jnp.bfloat16), ULY, split_axis=1, concat_axis=2, tiled=True
        ).astype(grad_q_block.dtype),
        lax.all_to_all(
            grad_k_block.astype(jnp.bfloat16), ULY, split_axis=1, concat_axis=2, tiled=True
        ).astype(grad_k_block.dtype),
        lax.all_to_all(
            grad_v_block.astype(jnp.bfloat16), ULY, split_axis=1, concat_axis=2, tiled=True
        ).astype(grad_v_block.dtype),
    )
    grad_q_normed = rotate(grad_q_seq, local_angles, -1.0)
    grad_k_normed = rotate(grad_k_seq, local_angles, -1.0)
    q_gain_term = jnp.sum(grad_q_normed * q_pre * q_scale, axis=(0, 1, 2))
    k_gain_term = jnp.sum(grad_k_normed * key_before_norm * k_scale, axis=(0, 1, 2))
    grad_q_pre = (
        norm_back(grad_q_normed, q_pre, q_scale, gain_q)
        .astype(jnp.bfloat16)
        .reshape(sequence_count, token_count, QUERY_HEADS * HEAD_SIZE)
    )
    grad_k_pre = (
        norm_back(grad_k_normed, key_before_norm, k_scale, gain_k)
        .astype(jnp.bfloat16)
        .reshape(sequence_count, token_count, KEY_VALUE_HEADS * HEAD_SIZE)
    )
    value_pre_gradient = value_sequence_gradient.astype(jnp.bfloat16).reshape(
        sequence_count, token_count, KEY_VALUE_HEADS * HEAD_SIZE
    )
    grad_query = jnp.einsum(
        EQ_STD_STE_TO_DE, normalized_input, grad_q_pre, preferred_element_type=jnp.float32
    )
    grad_key = jnp.einsum(
        EQ_STD_STE_TO_DE, normalized_input, grad_k_pre, preferred_element_type=jnp.float32
    )
    grad_value = jnp.einsum(
        EQ_STD_STE_TO_DE, normalized_input, value_pre_gradient, preferred_element_type=jnp.float32
    )
    grad_normed = jnp.einsum(EQ_STE_DE_TO_STD, grad_q_pre, wq_all, preferred_element_type=jnp.float32)
    grad_normed = grad_normed + jnp.einsum(
        EQ_STE_DE_TO_STD, grad_k_pre, wk_all, preferred_element_type=jnp.float32
    )
    grad_normed = grad_normed + jnp.einsum(
        EQ_STE_DE_TO_STD, value_pre_gradient, wv_all, preferred_element_type=jnp.float32
    )
    attn_gain_term = jnp.sum(grad_normed * source * first_scale, axis=(0, 1))
    grad_hidden = grad_middle + norm_back(
        grad_normed, source, first_scale, g_attn.astype(jnp.float32)
    )
    grad_down = jnp.einsum(EQ_STF_STD_TO_FD, activated, cotangent, preferred_element_type=jnp.float32)
    grad_attn_gain, grad_query, grad_key, grad_value, grad_out, grad_down = (
        lax.psum_scatter(attn_gain_term, EVERY, scatter_dimension=0, tiled=True),
        lax.psum_scatter(grad_query, EVERY, scatter_dimension=0, tiled=True),
        lax.psum_scatter(grad_key, EVERY, scatter_dimension=0, tiled=True),
        lax.psum_scatter(grad_value, EVERY, scatter_dimension=0, tiled=True),
        lax.psum_scatter(grad_out, EVERY, scatter_dimension=0, tiled=True),
        lax.psum_scatter(grad_down, EVERY, scatter_dimension=0, tiled=True),
    )
    grad_q_gain, grad_k_gain = lax.psum((q_gain_term, k_gain_term), EVERY)
    return (
        output,
        grad_hidden,
        grad_attn_gain,
        grad_query,
        grad_key,
        grad_value,
        grad_out,
        grad_q_gain,
        grad_k_gain,
        grad_mlp_gain,
        grad_gate,
        grad_up,
        grad_down,
    )


MESH = pl.DeviceIdType.MESH
HBM = pl.BlockSpec(memory_space=pltpu.HBM)
VMEM = pl.BlockSpec(memory_space=pltpu.VMEM)
MIB = 1 << 20


def kernel_params(collective_id, vmem_mib=62):
    return pltpu.CompilerParams(
        collective_id=collective_id, has_side_effects=True, vmem_limit_bytes=vmem_mib * MIB
    )


def semaphores(count, local=16):
    return [
        pltpu.SemaphoreType.DMA((count,)),
        pltpu.SemaphoreType.DMA((count,)),
        pltpu.SemaphoreType.DMA((local,)),
    ]


class Copy:
    def __init__(self, descriptor, sends, receives):
        self.descriptor, self.sends, self.receives = descriptor, sends, receives

    def under(self, condition, action):
        if condition is None:
            action()
        else:
            pl.when(condition)(action)

    def start(self):
        self.under(self.sends, lambda: self.descriptor().start())
        return self

    def sent(self):
        self.under(self.sends, lambda: self.descriptor().wait_send())

    def arrived(self):
        self.under(self.receives, lambda: self.descriptor().wait_recv())


class Links:
    def __init__(self, send, recv, here):
        self.send, self.recv, self.here = send, recv, here
        self.used, self.used_here = 0, 0
        self.copies, self.local_copies = [], []
        self.n_dp, self.n_blk, self.n_uly = (lax.axis_size(a) for a in EVERY)
        self.dp, self.blk, self.uly = (lax.axis_index(a) for a in EVERY)
        self.other_dp = 1 - self.dp
        self.across = lax.rem(self.uly + 2, 4)
        self.twin = self.uly + 1 - 2 * lax.rem(self.uly, 2)
        self.x_way = (self.other_dp, self.blk, self.uly)
        self.y_way = (self.dp, self.blk, self.across)
        self.core_way = (self.dp, self.blk, self.twin)

    def peer(self, step):
        return lax.rem(self.blk + step, self.n_blk)

    def peers(self):
        return [(self.dp, self.peer(k), self.uly) for k in range(1, self.n_blk)]

    def greet(self, devices):
        barrier = pltpu.get_barrier_semaphore()
        for device in devices:
            pl.semaphore_signal(barrier, inc=1, device_id=device, device_id_type=MESH)
        pl.semaphore_wait(barrier, len(devices))

    def remote(self, source, target, device, sends=None, receives=None):
        slot = self.used
        self.used += 1

        def descriptor():
            return pltpu.make_async_remote_copy(
                src_ref=source(),
                dst_ref=target(),
                send_sem=self.send.at[slot],
                recv_sem=self.recv.at[slot],
                device_id=device,
                device_id_type=MESH,
            )

        copy = Copy(descriptor, sends, receives)
        self.copies.append(copy)
        return copy.start()

    def to(self, source, target, device):
        return self.remote(lambda: source, lambda: target, device)

    def local(self, source, target):
        copy = pltpu.make_async_copy(source, target, self.here.at[self.used_here])
        self.used_here += 1
        copy.start()
        self.local_copies.append(copy)
        return copy

    def finish(self):
        for copy in self.copies:
            copy.sent()


class LineGather:
    def __init__(self, links, own, whole):
        self.links, self.own, self.whole = links, own, whole
        self.waiting = []

    def send(self, step):
        links, whole = self.links, self.whole
        blk, last = links.blk, links.n_blk - 1

        def block(index):
            if step == 0:
                return lambda: self.own
            return lambda: whole.at[index]

        self.waiting = [
            links.remote(
                block(blk - step),
                lambda: whole.at[blk - step],
                (links.dp, blk + 1, links.uly),
                jnp.logical_and(blk >= step, blk < last),
                blk >= step + 1,
            ),
            links.remote(
                block(blk + step),
                lambda: whole.at[blk + step],
                (links.dp, blk - 1, links.uly),
                jnp.logical_and(blk + step <= last, blk > 0),
                blk + step + 1 <= last,
            ),
        ]

    def arrived(self):
        for copy in self.waiting:
            copy.arrived()


def halves(tokens):
    return [pl.ds(0, tokens // 2), pl.ds(tokens // 2, tokens // 2)]


class HalvedLine:
    def __init__(self, links, own, whole):
        self.lines = [
            LineGather(links, None if own is None else own.at[rows], whole.at[:, rows])
            for rows in halves(whole.shape[1])
        ]

    def send(self, step):
        for line in self.lines:
            line.send(step)

    def advance(self, step):
        for line in self.lines:
            line.arrived()
            line.send(step)

    def arrived(self):
        for line in self.lines:
            line.arrived()


class PlaneGather:
    def __init__(self, links, at):
        self.links, self.at = links, at

    def start_x(self, own):
        links = self.links
        mine = self.at(links.dp, links.uly)
        self.from_x = links.to(own, mine, links.x_way)
        self.from_core = [links.to(own, mine, links.core_way)]

    def start_y(self, own):
        links = self.links
        self.from_y = links.to(own, self.at(links.dp, links.uly), links.y_way)

    def start(self, own=None):
        own = self.at(self.links.dp, self.links.uly) if own is None else own
        self.start_x(own)
        self.start_y(own)

    def hand_on(self):
        links, at = self.links, self.at
        self.from_x.arrived()
        half = at(links.other_dp, links.uly, 0)
        self.second_y = links.to(half, half, links.y_way)
        self.from_y.arrived()
        half = at(links.dp, links.across, 1)
        self.second_x = links.to(half, half, links.x_way)
        for chunk in (at(links.other_dp, links.uly), at(links.dp, links.across)):
            self.from_core.append(links.to(chunk, chunk, links.core_way))

    def last(self):
        links = self.links
        self.second_y.arrived()
        self.second_x.arrived()
        chunk = self.at(links.other_dp, links.across)
        self.from_core.append(links.to(chunk, chunk, links.core_way))

    def arrived(self):
        for copy in self.from_core:
            copy.arrived()


def rows_of(whole, blocked):
    def at(dp, uly, half=None):
        part = whole.at[dp, :, uly] if blocked else whole.at[dp, uly]
        if half is None:
            return part
        depth = whole.shape[-2] // 2
        rows = pl.ds(half * depth, depth)
        return part.at[:, rows] if blocked else part.at[rows]

    return at


class ColumnSwap:
    def __init__(self, links, pieces):
        self.links, self.pieces = links, pieces
        self.incoming, self.kept = [], []

    def parts(self, blk):
        links = self.links
        for weight, whole, offset in self.pieces:
            width = weight.shape[-1] // links.n_dp // links.n_blk
            for group in range(links.n_dp):
                start = (group * links.n_blk + blk) * width
                yield (
                    weight.at[:, pl.ds(pl.multiple_of(start, 128), width)],
                    whole.at[links.blk, :, pl.ds(offset + group * width, width)],
                )

    def start(self):
        links = self.links
        for step in range(1, links.n_blk):
            device = (links.dp, links.peer(step), links.uly)
            for source, target in self.parts(links.peer(step)):
                self.incoming.append(links.to(source, target, device))
        for source, target in self.parts(links.blk):
            self.kept.append(links.local(source, target))

    def arrived(self):
        for copy in self.kept:
            copy.wait()
        for copy in self.incoming:
            copy.arrived()


def write_positions(links, span_order, toks, cosine, sine, query_pos, key_pos):
    half_len = toks * links.n_uly // 2

    def first(blk, uly):
        chunk = span_order[2 * blk + lax.div(uly, links.n_uly // 2)]
        return chunk * half_len + lax.rem(uly, links.n_uly // 2) * toks

    lane = lax.broadcasted_iota(jnp.int32, (toks, HEAD_SIZE), 1)
    row = lax.broadcasted_iota(jnp.int32, (toks, HEAD_SIZE), 0)
    upper = lane >= HEAD_SIZE // 2
    step = jnp.where(upper, lane - HEAD_SIZE // 2, lane).astype(jnp.float32)
    inverse = jnp.exp(step * (-2.0 * math.log(ROPE_BASE) / HEAD_SIZE))
    for blk in range(links.n_blk):
        angles = (first(blk, links.uly) + row).astype(jnp.float32) * inverse
        at = slice(blk * toks, (blk + 1) * toks)
        cosine[at, :] = jnp.cos(angles)
        turn = jnp.sin(angles)
        sine[at, :] = jnp.where(upper, turn, -turn)
    lane = lax.broadcasted_iota(jnp.int32, query_pos.shape, 1)
    place = jnp.zeros(query_pos.shape, jnp.int32)
    for start in range(0, query_pos.shape[1], toks):
        blk = start // toks % links.n_blk
        here = jnp.logical_and(lane >= start, lane < start + toks)
        place = jnp.where(here, first(blk, links.uly) + lane - start, place)
    query_pos[...] = place
    row = lax.broadcasted_iota(jnp.int32, (toks, 1), 0)
    for uly in range(links.n_uly):
        for blk in range(links.n_blk):
            start = (uly * links.n_blk + blk) * toks
            key_pos[start : start + toks, :] = row + first(blk, jnp.int32(uly))


def write_gains(links, all_gains, size, targets):
    per_row = 128 // size
    for which, target in enumerate(targets):
        for place in range(target.shape[1] // 128):
            pieces = []
            for part in range(per_row):
                device = place * per_row + part
                plane, uly = device // links.n_uly, device % links.n_uly
                gains = all_gains[plane // links.n_blk, plane % links.n_blk, uly]
                pieces.append(gains.astype(jnp.float32)[which : which + 1, :size])
            target[:, place * 128 : (place + 1) * 128] = jnp.concatenate(pieces, axis=1)


def front_kernel(
    toks,
    gain_rows,
    span_order,
    hidden,
    wq,
    wk,
    wv,
    wo,
    gains,
    all_hidden,
    w_qkv,
    all_wo,
    attn_gain,
    mlp_gain,
    cosine,
    sine,
    query_pos,
    key_pos,
    all_gains,
    send,
    recv,
    here,
):
    links = Links(send, recv, here)
    links.greet(links.peers() + [links.x_way, links.y_way, links.core_way])
    q_width, k_width = wq.shape[1] // links.n_blk, wk.shape[1] // links.n_blk
    chunk = w_qkv.at[links.dp, :, links.uly]
    swap = ColumnSwap(
        links, [(wq, chunk, 0), (wk, chunk, q_width), (wv, chunk, q_width + k_width)]
    )
    plane_wo = PlaneGather(links, rows_of(all_wo, False))
    plane_qkv = PlaneGather(links, rows_of(w_qkv, True))
    plane_gain = PlaneGather(links, rows_of(all_gains, True))
    swap.start()
    my_gains = all_gains.at[links.dp, links.blk, links.uly]
    gain_swap = [links.to(gains, my_gains, device) for device in links.peers()]
    plane_wo.start(wo)
    line = HalvedLine(links, hidden, all_hidden)
    line.send(0)
    keep = [
        links.local(gains, my_gains),
        links.local(hidden, all_hidden.at[links.blk]),
        links.local(wo, all_wo.at[links.dp, links.uly]),
    ]
    write_positions(links, span_order, toks, cosine, sine, query_pos, key_pos)
    swap.arrived()
    plane_qkv.start()
    keep[0].wait()
    for copy in gain_swap:
        copy.arrived()
    plane_gain.start()
    plane_wo.hand_on()
    line.advance(1)
    plane_qkv.hand_on()
    plane_gain.hand_on()
    plane_wo.last()
    for step in range(2, links.n_blk - 1):
        line.advance(step)
    plane_qkv.last()
    plane_gain.last()
    plane_gain.arrived()
    write_gains(links, all_gains, gain_rows, (attn_gain, mlp_gain))
    line.arrived()
    for plane in (plane_wo, plane_qkv):
        plane.arrived()
    for copy in keep[1:]:
        copy.wait()
    links.finish()


SMEM = pl.BlockSpec(memory_space=pltpu.SMEM)


def gather_front(span_order, hidden, wq, wk, wv, wo, gains, toks, gain_rows):
    n_dp, n_blk, n_uly = (lax.axis_size(a) for a in EVERY)
    width = hidden.shape[1]
    group = QUERY_HEADS // KEY_VALUE_HEADS
    low = [
        (n_blk,) + hidden.shape,
        (n_dp, n_blk, n_uly, wq.shape[0], (wq.shape[1] + wk.shape[1] + wv.shape[1]) // n_blk),
        (n_dp, n_uly) + wo.shape,
    ]
    f32, i32 = jnp.float32, jnp.int32
    small = [
        ((1, width), f32),
        ((1, width), f32),
        ((n_blk * toks, HEAD_SIZE), f32),
        ((n_blk * toks, HEAD_SIZE), f32),
        ((1, group * n_blk * toks), i32),
        ((n_uly * n_blk * toks, 1), i32),
    ]
    return pl.pallas_call(
        functools.partial(front_kernel, toks, gain_rows),
        out_shape=[jax.ShapeDtypeStruct(shape, jnp.bfloat16) for shape in low]
        + [jax.ShapeDtypeStruct(shape, kind) for shape, kind in small],
        in_specs=[SMEM] + [HBM] * 6,
        out_specs=[HBM] * 3 + [VMEM] * 6,
        scratch_shapes=[pltpu.VMEM((n_dp, n_blk, n_uly) + gains.shape, jnp.bfloat16)]
        + semaphores(72),
        compiler_params=kernel_params(0),
    )(span_order, hidden, wq, wk, wv, wo, gains)


ROWS = 32


def each_block(count, body):
    def step(index, carry):
        body(pl.ds(pl.multiple_of(index * ROWS, ROWS), ROWS))
        return carry

    lax.fori_loop(0, count // ROWS, step, 0)


class LineScatter:
    def __init__(self, links, parts, rightward, leftward):
        self.links, self.parts = links, parts
        self.slots = {1: rightward, -1: leftward}
        self.tokens = parts.shape[1]
        self.number = links.used
        self.last = links.n_blk - 1
        links.used += 2 * self.last

    def target(self, step, way):
        return self.last - step if way == 1 else step

    def slot(self, step, way):
        target = self.target(step, way)
        return self.slots[way].at[target - 1 if way == 1 else target]

    def place(self, way):
        return self.links.blk if way == 1 else self.last - self.links.blk

    def copy(self, step, way, source=None):
        links, slot = self.links, self.slot(step, way)
        number = self.number + 2 * step + (1 if way == 1 else 0)
        return pltpu.make_async_remote_copy(
            src_ref=slot if source is None else source,
            dst_ref=slot,
            send_sem=links.send.at[number],
            recv_sem=links.recv.at[number],
            device_id=(links.dp, links.blk + way, links.uly),
            device_id_type=MESH,
        )

    def start(self):
        for step in range(self.last):
            for way in (1, -1):

                @pl.when(self.place(way) == 0)
                def _(step=step, way=way):
                    self.copy(step, way, self.parts.at[self.target(step, way)]).start()

    def tick(self, tick):
        for way in (1, -1):

            @pl.when(jnp.logical_and(self.place(way) >= 1, self.place(way) <= tick))
            def _(way=way):
                step = tick - self.place(way)
                self.copy(step, way).wait_recv()
                slot, target = self.slot(step, way), self.target(step, way)

                def body(rows):
                    slot[rows, :] = slot[rows, :] + self.parts[target, rows, :]

                each_block(self.tokens, body)
                self.copy(step, way).start()

    def finish(self, total):
        blk, last = self.links.blk, self.last

        def start(rows):
            total[rows, :] = self.parts[blk, rows, :].astype(jnp.float32)

        each_block(self.tokens, start)
        for way in (1, -1):

            @pl.when(self.place(way) >= 1)
            def _(way=way):
                step = last - self.place(way)
                self.copy(step, way).wait_recv()
                slot = self.slot(step, way)

                def body(rows):
                    total[rows, :] = total[rows, :] + slot[rows, :].astype(jnp.float32)

                each_block(self.tokens, body)

    def sent(self):
        for step in range(self.last):
            for way in (1, -1):
                beyond = self.place(way) + step < self.last
                pl.when(beyond)(lambda step=step, way=way: self.copy(step, way).wait_send())


def halved_sums(links, parts, rightward, leftward):
    return [
        LineScatter(links, parts.at[:, rows], rightward.at[:, rows], leftward.at[:, rows])
        for rows in halves(parts.shape[1])
    ]


class OutputHalf:
    def __init__(self, links, which, parts, middle, rightward, leftward, total):
        rows = halves(middle.shape[0])[which]
        self.middle, self.total = middle.at[rows], total
        self.sum = LineScatter(links, parts.at[:, rows], rightward, leftward)

    def write(self, output):
        self.sum.finish(self.total)

        def body(rows):
            output[rows, :] = (self.middle[rows, :] + self.total[rows, :]).astype(jnp.bfloat16)

        each_block(self.middle.shape[0], body)


def output_scratch(n_blk, tokens, width):
    return line_scratch(n_blk, tokens // 2, width) + [
        pltpu.VMEM((tokens // 2, width), jnp.float32)
    ]


def line_scratch(n_blk, tokens, width):
    return [pltpu.VMEM((n_blk - 1, tokens, width), jnp.bfloat16)] * 2


class PlaneScatter:
    def __init__(self, links, parts, from_core, from_x, from_y, last_x, last_y):
        self.links, self.parts = links, parts
        self.own_core_only = from_core is None
        self.from_core, self.from_x, self.from_y = from_core, from_x, from_y
        self.last_x, self.last_y = last_x, last_y
        self.core = lax.rem(links.uly, 2)
        self.row = lax.div(links.uly, 2)
        self.depth = parts.shape[3]
        self.core_copies = {}

    def chunk(self, dp, row, core, half=None):
        if self.own_core_only:
            part = self.parts.at[dp, row]
        else:
            part = self.parts.at[dp, :, row * 2 + core]
        if half is None:
            return part
        depth = self.depth // 2
        return part.at[:, pl.ds(half * depth, depth)]

    def add(self, target, source):
        blocks, depth, _ = target.shape
        rows = 32 if depth % 32 == 0 else 16

        def body(index, carry):
            block = lax.div(index, depth // rows)
            at = pl.ds(pl.multiple_of(lax.rem(index, depth // rows) * rows, rows), rows)
            target[block, at, :] = target[block, at, :] + source[block, at, :]
            return carry

        lax.fori_loop(0, blocks * (depth // rows), body, 0)

    def between_cores(self, which):
        links = self.links
        dp = links.dp if which == 1 else links.other_dp
        self.core_copies[which] = [
            links.to(
                self.chunk(dp, row, 1 - self.core), self.from_core.at[which, row], links.core_way
            )
            for row in range(2)
        ]

    def core_sums(self, which):
        links = self.links
        dp = links.dp if which == 1 else links.other_dp
        for row in range(2):
            self.core_copies[which][row].arrived()
            self.add(self.chunk(dp, row, self.core), self.from_core.at[which, row])

    def across_chips(self):
        links = self.links
        if not self.own_core_only:
            self.core_sums(0)
        self.x_copies = [
            links.to(
                self.chunk(links.other_dp, row, self.core, 0), self.from_x.at[row], links.x_way
            )
            for row in range(2)
        ]
        if not self.own_core_only:
            self.core_sums(1)
        self.y_copies = [
            links.to(
                self.chunk(group, 1 - self.row, self.core, 1),
                self.from_y.at[group],
                links.y_way,
            )
            for group in range(links.n_dp)
        ]

    def second_way(self):
        links = self.links
        for row in range(2):
            self.x_copies[row].arrived()
            self.add(self.chunk(links.dp, row, self.core, 0), self.from_x.at[row])
        self.y_last = links.to(
            self.chunk(links.dp, 1 - self.row, self.core, 0), self.last_y, links.y_way
        )
        for group in range(links.n_dp):
            self.y_copies[group].arrived()
            self.add(self.chunk(group, self.row, self.core, 1), self.from_y.at[group])
        self.x_last = links.to(
            self.chunk(links.other_dp, self.row, self.core, 1), self.last_x, links.x_way
        )

    def result(self, write):
        links = self.links
        for half, copy, source in ((0, self.y_last, self.last_y), (1, self.x_last, self.last_x)):
            copy.arrived()
            own = self.chunk(links.dp, self.row, self.core, half)
            blocks, depth, _ = source.shape
            rows = 32 if depth % 32 == 0 else 16

            def body(index, carry, own=own, source=source, half=half, depth=depth, rows=rows):
                block = lax.div(index, depth // rows)
                start = pl.multiple_of(lax.rem(index, depth // rows) * rows, rows)
                at = pl.ds(start, rows)
                value = own[block, at, :].astype(jnp.float32)
                value = value + source[block, at, :].astype(jnp.float32)
                write(block, pl.ds(pl.multiple_of(start + half * depth, rows), rows), value)
                return carry

            lax.fori_loop(0, blocks * (depth // rows), body, 0)


def plane_shapes(n_dp, blocks, n_uly, depth, width):
    return [
        (n_dp, blocks, n_uly, depth, width),
        (n_dp, 2, blocks, depth, width),
        (2, blocks, depth // 2, width),
        (n_dp, blocks, depth // 2, width),
        (blocks, depth // 2, width),
        (blocks, depth // 2, width),
    ]


def plane_scratch(*sizes):
    return [pltpu.VMEM(shape, jnp.bfloat16) for shape in plane_shapes(*sizes)]


def weight_grad(rows, right, parts, dp):
    _, blocks, n_uly, depth, width = parts.shape
    columns = 512

    def body(index, carry):
        at = pl.ds(pl.multiple_of(index * columns, columns), columns)
        part = jnp.dot(rows[...], right[:, at], preferred_element_type=jnp.float32)
        parts[dp, :, :, :, at] = part.astype(jnp.bfloat16).reshape(blocks, n_uly, depth, columns)
        return carry

    lax.fori_loop(0, width // columns, body, 0)


def rows_turned(left, parts, dp):
    count = parts.shape[1] * parts.shape[2] * parts.shape[3]
    return left[:, pl.ds(pl.multiple_of(dp * count, 128), count)].T


def turned(rows, cosine, sine):
    return rows * cosine + pltpu.roll(rows, HEAD_SIZE // 2, axis=1) * sine


def transposed_product(left, right):
    return lax.dot_general(
        left, right, (((0,), (0,)), ((), ())), preferred_element_type=jnp.float32
    )


def product_right(left, right):
    return lax.dot_general(
        left, right, (((1,), (1,)), ((), ())), preferred_element_type=jnp.float32
    )


SCORE_SCALE = 1.0 / math.sqrt(HEAD_SIZE)


def mask_scores(bias, query_pos, key_pos):
    size = bias.shape[0] // 4

    def body(index, carry):
        rows = pl.ds(pl.multiple_of(index * size, size), size)
        bias[rows, :] = jnp.where(query_pos[...] >= key_pos[rows, :], 0.0, -1e30)
        return carry

    lax.fori_loop(0, 4, body, 0)


class RowBlocks:
    def __init__(self, n_blk, seqs, toks):
        self.n_blk, self.seqs, self.toks = n_blk, seqs, toks

    def each(self, body):
        def step(index, carry):
            blk, seq = lax.div(index, self.seqs), lax.rem(index, self.seqs)
            body(
                seq,
                pl.ds(pl.multiple_of(index * self.toks, self.toks), self.toks),
                pl.multiple_of(blk * self.toks, self.toks),
            )
            return carry

        lax.fori_loop(0, self.n_blk * self.seqs, step, 0)


def attention_kernel(
    wg,
    wu,
    wd,
    cotangent,
    hidden,
    w_qkv,
    gain,
    q_gain,
    k_gain,
    cosine,
    sine,
    query_pos,
    key_pos,
    rows_wg,
    rows_wu,
    all_wd,
    all_cot,
    heads,
    normed,
    qkv,
    queries,
    key_values,
    lse,
    bias,
    send,
    recv,
    here,
):
    links = Links(send, recv, here)
    links.greet(links.peers() + [links.x_way, links.y_way, links.core_way])
    swap = ColumnSwap(links, [(wg, rows_wg, 0), (wu, rows_wu, 0)])
    swap.start()
    plane = PlaneGather(links, rows_of(all_wd, False))
    plane.start(wd)
    line = HalvedLine(links, cotangent, all_cot)
    line.send(0)
    keep = [
        links.local(cotangent, all_cot.at[links.blk]),
        links.local(wd, all_wd.at[links.dp, links.uly]),
    ]

    def norm(rows):
        source = hidden[rows, :].astype(jnp.float32)
        normed[rows, :] = (source * rms_scale(source) * gain[...]).astype(jnp.bfloat16)

    each_block(hidden.shape[0], norm)
    for column in range(0, qkv.shape[1], 256):
        qkv[:, column : column + 256] = jnp.dot(
            normed[...], w_qkv[:, column : column + 256], preferred_element_type=jnp.float32
        )
    seqs, kv_heads, q_rows, _ = queries.shape
    q_len = key_values.shape[4]
    group = q_rows // q_len
    blocks = RowBlocks(links.n_blk, seqs, q_len // links.n_blk)
    q_end = kv_heads * group * HEAD_SIZE
    k_end = q_end + kv_heads * HEAD_SIZE

    def place_keys(seq, rows, start):
        at = pl.ds(start, blocks.toks)
        for head in range(kv_heads):
            k_pre = qkv[rows, q_end + head * HEAD_SIZE : q_end + (head + 1) * HEAD_SIZE]
            k_row = turned(k_pre * rms_scale(k_pre) * k_gain[...], cosine[at, :], sine[at, :])
            v_row = qkv[rows, k_end + head * HEAD_SIZE : k_end + (head + 1) * HEAD_SIZE]
            key_values[links.uly, 0, seq, head, at, :] = k_row.astype(jnp.bfloat16)
            key_values[links.uly, 1, seq, head, at, :] = v_row.astype(jnp.bfloat16)

    blocks.each(place_keys)
    mine = key_values.at[links.uly]
    kv_core = links.to(mine, mine, links.core_way)
    kv_across = links.to(mine, mine, links.y_way)

    def place_queries(seq, rows, start):
        at = pl.ds(start, blocks.toks)
        for head in range(kv_heads * group):
            q_pre = qkv[rows, head * HEAD_SIZE : (head + 1) * HEAD_SIZE]
            q_row = turned(q_pre * rms_scale(q_pre) * q_gain[...], cosine[at, :], sine[at, :])
            to = pl.ds((head % group) * q_len + start, blocks.toks)
            queries[seq, head // group, to, :] = q_row.astype(jnp.bfloat16)

    blocks.each(place_queries)
    mask_scores(bias, query_pos, key_pos)
    kv_across.arrived()
    theirs = key_values.at[links.across]
    kv_last = links.to(theirs, theirs, links.core_way)
    plane.hand_on()
    kv_core.arrived()
    kv_last.arrived()

    def attend(seq, head):
        def over_keys(piece, carry):
            total, mixed = carry
            rows = pl.ds(pl.multiple_of(piece * q_len, q_len), q_len)
            scores = product_right(key_values[piece, 0, seq, head], queries[seq, head])
            weights = jnp.exp(scores * SCORE_SCALE + bias[rows, :])
            total = total + jnp.sum(weights, axis=0, keepdims=True)
            mixed = mixed + transposed_product(
                key_values[piece, 1, seq, head], weights.astype(jnp.bfloat16)
            )
            return total, mixed

        total, mixed = lax.fori_loop(
            0,
            links.n_uly,
            over_keys,
            (
                jnp.zeros((1, q_rows), jnp.float32),
                jnp.zeros((HEAD_SIZE, q_rows), jnp.float32),
            ),
        )
        lse[seq * kv_heads + head] = jnp.log(total)
        attended = (mixed / total).T.astype(jnp.bfloat16)
        for member in range(group):
            column = (head * group + member) * HEAD_SIZE
            for blk in range(links.n_blk):
                row = (blk * seqs + seq) * blocks.toks
                start = member * q_len + blk * blocks.toks
                heads[row : row + blocks.toks, column : column + HEAD_SIZE] = attended[
                    start : start + blocks.toks, :
                ]

    pairs = [(seq, head) for seq in range(seqs) for head in range(kv_heads)]
    for number, (seq, head) in enumerate(pairs):
        attend(seq, head)
        if number == len(pairs) // 2:
            plane.last()
    swap.arrived()
    line.arrived()
    for copy in keep:
        copy.wait()
    plane.arrived()
    links.finish()


def attend_forward(
    wg, wu, wd, cotangent, hidden, w_qkv, gain, q_gain, k_gain, cosine, sine, query_pos, key_pos, seqs
):
    n_dp, n_blk, n_uly = (lax.axis_size(a) for a in EVERY)
    rows = hidden.shape[0]
    kv_heads = KEY_VALUE_HEADS // n_blk
    q_len, q_rows = rows // seqs, query_pos.shape[1]
    low = [
        (n_blk, wg.shape[0], wg.shape[1] // n_blk),
        (n_blk, wu.shape[0], wu.shape[1] // n_blk),
        (n_dp, n_uly) + wd.shape,
        (n_blk,) + cotangent.shape,
        (rows, QUERY_HEADS // n_blk * HEAD_SIZE),
        hidden.shape,
    ]
    shapes = [jax.ShapeDtypeStruct(s, jnp.bfloat16) for s in low] + [
        jax.ShapeDtypeStruct((rows, w_qkv.shape[1]), jnp.float32),
        jax.ShapeDtypeStruct((seqs, kv_heads, q_rows, HEAD_SIZE), jnp.bfloat16),
        jax.ShapeDtypeStruct((n_uly, 2, seqs, kv_heads, q_len, HEAD_SIZE), jnp.bfloat16),
        jax.ShapeDtypeStruct((seqs * kv_heads, 1, q_rows), jnp.float32),
    ]
    return pl.pallas_call(
        attention_kernel,
        out_shape=shapes,
        in_specs=[HBM] * 4 + [VMEM] * 9,
        out_specs=[HBM] * 4 + [VMEM] * 6,
        scratch_shapes=[pltpu.VMEM((key_pos.shape[0], q_rows), jnp.float32)] + semaphores(32),
        compiler_params=kernel_params(1),
    )(
        wg,
        wu,
        wd,
        cotangent,
        hidden,
        w_qkv,
        gain,
        q_gain,
        k_gain,
        cosine,
        sine,
        query_pos,
        key_pos,
    )


def attention_back_kernel(
    all_low,
    wo,
    queries,
    key_values,
    lse,
    qkv,
    q_gain,
    k_gain,
    cosine,
    sine,
    query_pos,
    key_pos,
    out_parts,
    middle,
    grad_gate,
    grad_up,
    part_down,
    grad_qkv,
    gain_terms,
    grad_down,
    output,
    gate_rows,
    up_rows,
    bias,
    grad_heads,
    grad_rows,
    probs,
    grad_probs,
    grad_kv,
    from_core,
    from_across,
    down_1,
    down_3,
    down_4,
    down_5,
    down_6,
    out_right,
    out_left,
    out_total,
    send,
    recv,
    here,
):
    links = Links(send, recv, here)
    links.greet(links.peers() + [links.x_way, links.y_way, links.core_way])
    out = OutputHalf(links, 0, out_parts, middle, out_right, out_left, out_total)
    out.sum.start()
    down = PlaneScatter(links, down_1, None, down_3, down_4, down_5, down_6)
    links.local(part_down, down_1).wait()
    down.across_chips()
    grad_heads[...] = product_right(all_low[...], wo[...])
    mask_scores(bias, query_pos, key_pos)
    seqs, kv_heads, q_rows, _ = queries.shape
    q_len = key_values.shape[4]
    group = q_rows // q_len
    blocks = RowBlocks(links.n_blk, seqs, q_len // links.n_blk)
    q_end = kv_heads * group * HEAD_SIZE
    k_end = q_end + kv_heads * HEAD_SIZE
    gain_terms[...] = jnp.zeros_like(gain_terms)

    def gather_rows(seq, rows, start):
        for head in range(kv_heads * group):
            to = pl.ds((head % group) * q_len + start, blocks.toks)
            grad_rows[seq, head // group, to, :] = grad_heads[
                rows, head * HEAD_SIZE : (head + 1) * HEAD_SIZE
            ].astype(jnp.bfloat16)

    blocks.each(gather_rows)
    out.sum.tick(1)

    def back_norm(upstream, pre, gain, at, which):
        upstream = turned(upstream, cosine[at, :], -sine[at, :])
        gain_terms[which : which + 1, :] += jnp.sum(
            upstream * pre * rms_scale(pre), axis=0, keepdims=True
        )
        return back_rows(upstream, pre, gain[...]).astype(jnp.bfloat16)

    def back(seq, head):
        def first(piece, delta):
            rows = pl.ds(pl.multiple_of(piece * q_len, q_len), q_len)
            scores = product_right(key_values[piece, 0, seq, head], queries[seq, head])
            prob = jnp.exp(
                scores * SCORE_SCALE + bias[rows, :] - lse[seq * kv_heads + head]
            )
            grad_prob = product_right(key_values[piece, 1, seq, head], grad_rows[seq, head])
            probs[rows, :] = prob
            grad_probs[rows, :] = grad_prob
            return delta + jnp.sum(prob * grad_prob, axis=0, keepdims=True)

        delta = lax.fori_loop(0, links.n_uly, first, jnp.zeros((1, q_rows), jnp.float32))

        def second(piece, grad_query):
            rows = pl.ds(pl.multiple_of(piece * q_len, q_len), q_len)
            prob = probs[rows, :]
            grad_score = (prob * (grad_probs[rows, :] - delta)).astype(jnp.bfloat16)
            grad_kv[seq, piece, 0, head] = (
                SCORE_SCALE
                * jnp.dot(grad_score, queries[seq, head], preferred_element_type=jnp.float32)
            ).astype(jnp.bfloat16)
            grad_kv[seq, piece, 1, head] = jnp.dot(
                prob.astype(jnp.bfloat16),
                grad_rows[seq, head],
                preferred_element_type=jnp.float32,
            ).astype(jnp.bfloat16)
            return grad_query + transposed_product(key_values[piece, 0, seq, head], grad_score)

        grad_query = lax.fori_loop(
            0, links.n_uly, second, jnp.zeros((HEAD_SIZE, q_rows), jnp.float32)
        )
        grad_heads[:, :HEAD_SIZE] = (grad_query * SCORE_SCALE).T
        for member in range(group):
            column = (head * group + member) * HEAD_SIZE
            for blk in range(links.n_blk):
                row = (blk * seqs + seq) * blocks.toks
                at = pl.ds(blk * blocks.toks, blocks.toks)
                start = member * q_len + blk * blocks.toks
                grad_qkv[row : row + blocks.toks, column : column + HEAD_SIZE] = back_norm(
                    grad_heads[start : start + blocks.toks, :HEAD_SIZE],
                    qkv[row : row + blocks.toks, column : column + HEAD_SIZE],
                    q_gain,
                    at,
                    0,
                )

    swapped, keep = [], []

    def swap_columns():
        for source, target in ((grad_gate, gate_rows), (grad_up, up_rows)):
            for step in range(1, links.n_blk):
                peer = links.peer(step)
                swapped.append(
                    links.to(source.at[peer], target.at[links.blk], (links.dp, peer, links.uly))
                )
            keep.append(links.local(source.at[links.blk], target.at[links.blk]))

    core, line = lax.rem(links.uly, 2), lax.div(links.uly, 2)

    def add(target, source):
        for kind in range(2):
            for head in range(kv_heads):
                target[kind, head] = target[kind, head] + source[kind, head]

    def core_sums(seq):
        copies = [
            links.to(
                grad_kv.at[seq, row * 2 + 1 - core], from_core.at[seq, row], links.core_way
            )
            for row in range(2)
        ]
        return copies

    def across_sums(seq, copies):
        for row in range(2):
            copies[row].arrived()
            add(grad_kv.at[seq, row * 2 + core], from_core.at[seq, row])
        return links.to(
            grad_kv.at[seq, (1 - line) * 2 + core], from_across.at[seq], links.y_way
        )

    def own_keys(seq, copy):
        copy.arrived()
        for head in range(kv_heads):
            for blk in range(links.n_blk):
                row = (blk * seqs + seq) * blocks.toks
                at = pl.ds(blk * blocks.toks, blocks.toks)
                term = [
                    grad_kv[seq, links.uly, kind, head, at, :].astype(jnp.float32)
                    + from_across[seq, kind, head, at, :].astype(jnp.float32)
                    for kind in range(2)
                ]
                k_at = q_end + head * HEAD_SIZE
                v_at = k_end + head * HEAD_SIZE
                grad_qkv[row : row + blocks.toks, k_at : k_at + HEAD_SIZE] = back_norm(
                    term[0],
                    qkv[row : row + blocks.toks, k_at : k_at + HEAD_SIZE],
                    k_gain,
                    at,
                    1,
                )
                grad_qkv[row : row + blocks.toks, v_at : v_at + HEAD_SIZE] = term[1].astype(
                    jnp.bfloat16
                )

    stage, last = None, []
    for seq in range(seqs):
        for head in range(kv_heads):
            back(seq, head)
            if seq == 0 and head == 0:
                for tick in range(2, links.n_blk - 1):
                    out.sum.tick(tick)
                swap_columns()
            if seq == 0 and head == kv_heads - 1:
                down.second_way()
            if stage is not None:
                last.append((seq - 1, across_sums(seq - 1, stage)))
                stage = None
        stage = core_sums(seq)
    last.append((seqs - 1, across_sums(seqs - 1, stage)))
    for seq, copy in last:
        own_keys(seq, copy)

    def write(block, rows, values):
        grad_down[block, rows, :] = values

    down.result(write)
    out.write(output)
    out.sum.sent()
    for copy in keep:
        copy.wait()
    for copy in swapped:
        copy.arrived()
    links.finish()


def attend_back(
    all_low,
    wo,
    queries,
    key_values,
    lse,
    qkv,
    q_gain,
    k_gain,
    cosine,
    sine,
    query_pos,
    key_pos,
    out_parts,
    middle,
    grad_gate,
    grad_up,
    part_down,
):
    seqs, kv_heads, q_rows, _ = queries.shape
    n_uly, _, _, _, q_len, _ = key_values.shape
    rows = all_low.shape[0]
    keys = key_pos.shape[0]
    f32, low = jnp.float32, jnp.bfloat16
    scratch = [
        ((keys, q_rows), f32),
        ((rows, wo.shape[0]), f32),
        (queries.shape, low),
        ((keys, q_rows), f32),
        ((keys, q_rows), f32),
        ((seqs, n_uly, 2, kv_heads, q_len, HEAD_SIZE), low),
        ((seqs, 2, 2, kv_heads, q_len, HEAD_SIZE), low),
        ((seqs, 2, kv_heads, q_len, HEAD_SIZE), low),
        (part_down.shape, low),
    ]
    n_dp, _, _, depth, width = part_down.shape
    n_blk, tokens, _ = out_parts.shape
    scratch += [(shape, low) for shape in plane_shapes(n_dp, 1, n_uly, depth, width)[2:]]
    return pl.pallas_call(
        attention_back_kernel,
        out_shape=[
            jax.ShapeDtypeStruct(qkv.shape, low),
            jax.ShapeDtypeStruct((8, HEAD_SIZE), f32),
            jax.ShapeDtypeStruct((1, depth, width), f32),
            jax.ShapeDtypeStruct((tokens // 2, width), low),
            jax.ShapeDtypeStruct(grad_gate.shape, low),
            jax.ShapeDtypeStruct(grad_up.shape, low),
        ],
        in_specs=[VMEM] * 14 + [HBM] * 3,
        out_specs=[VMEM] * 4 + [HBM] * 2,
        scratch_shapes=[pltpu.VMEM(shape, kind) for shape, kind in scratch]
        + output_scratch(n_blk, tokens, width)
        + semaphores(40),
        compiler_params=kernel_params(5),
    )(
        all_low,
        wo,
        queries,
        key_values,
        lse,
        qkv,
        q_gain,
        k_gain,
        cosine,
        sine,
        query_pos,
        key_pos,
        out_parts,
        middle,
        grad_gate,
        grad_up,
        part_down,
    )


def middle_kernel(
    heads,
    wo,
    source,
    gain,
    rows_wg,
    rows_wu,
    _,
    middle,
    all_normed,
    all_wg,
    all_wu,
    all_cot,
    parts,
    rightward,
    leftward,
    normed,
    send,
    recv,
    here,
):
    links = Links(send, recv, here)
    links.greet(links.peers() + [links.x_way, links.y_way, links.core_way])
    planes, keep = [], []
    for chunk, whole in ((rows_wg, all_wg), (rows_wu, all_wu)):
        at = rows_of(whole, True)
        plane = PlaneGather(links, at)
        plane.start(chunk)
        planes.append(plane)
        keep.append(links.local(chunk, at(links.dp, links.uly)))
    tokens = source.shape[0]
    for blk in (links.n_blk - 1, 0) + tuple(range(1, links.n_blk - 1)):
        parts[blk] = jnp.dot(heads[blk], wo[...], preferred_element_type=jnp.float32).astype(
            jnp.bfloat16
        )
    sums = halved_sums(links, parts, rightward, leftward)
    for half in sums:
        half.start()
    cot_lines = HalvedLine(links, None, all_cot).lines
    cot_lines[0].send(1)
    lines = []

    def settle(half, rows_of_half):
        half.finish(middle.at[rows_of_half])

        def body(rows):
            at = pl.ds(pl.multiple_of(rows_of_half.start + rows.start, ROWS), ROWS)
            total = middle[at, :] + source[at, :].astype(jnp.float32)
            middle[at, :] = total
            normed[at, :] = (total * rms_scale(total) * gain[...]).astype(jnp.bfloat16)

        each_block(tokens // 2, body)
        line = LineGather(links, normed.at[rows_of_half], all_normed.at[:, rows_of_half])
        line.send(0)
        lines.append(line)

    spans = halves(tokens)
    for tick in range(1, links.n_blk - 1):
        sums[0].tick(tick)
        if tick == 1:
            cot_lines[1].send(1)
    settle(sums[0], spans[0])
    planes[0].hand_on()
    for tick in range(1, links.n_blk - 1):
        sums[1].tick(tick)
        for line in cot_lines:
            line.arrived()
            if tick + 1 < links.n_blk - 1:
                line.send(tick + 1)
    settle(sums[1], spans[1])
    keep.append(links.local(normed, all_normed.at[links.blk]))
    for step in range(1, links.n_blk - 1):
        for line in lines:
            line.arrived()
            line.send(step)
        if step == 1:
            planes[1].hand_on()
        if step == 2:
            planes[0].last()
    planes[1].last()
    for line in lines:
        line.arrived()
    for plane in planes:
        plane.arrived()
    for copy in keep:
        copy.wait()
    for half in sums:
        half.sent()
    links.finish()


def exchange_middle(heads, wo, source, gain, rows_wg, rows_wu, all_cot):
    n_dp, n_blk, n_uly = (lax.axis_size(a) for a in EVERY)
    tokens, width = source.shape
    low = [(n_blk, tokens, width)]
    low += [(n_dp, n_blk, n_uly) + chunk.shape[1:] for chunk in (rows_wg, rows_wu)]
    low.append(all_cot.shape)
    return pl.pallas_call(
        middle_kernel,
        out_shape=[jax.ShapeDtypeStruct((tokens, width), jnp.float32)]
        + [jax.ShapeDtypeStruct(shape, jnp.bfloat16) for shape in low],
        in_specs=[VMEM] * 4 + [HBM] * 3,
        out_specs=[VMEM] + [HBM] * 4,
        input_output_aliases={6: 4},
        scratch_shapes=[pltpu.VMEM((n_blk, tokens, width), jnp.bfloat16)]
        + line_scratch(n_blk, tokens, width)
        + [pltpu.VMEM((tokens, width), jnp.bfloat16)]
        + semaphores(64),
        compiler_params=kernel_params(2),
    )(heads, wo, source, gain, rows_wg, rows_wu, all_cot)


def back_rows(grad_normed, source, gain):
    unit = source * rms_scale(source)
    scaled = grad_normed * gain
    return rms_scale(source) * (
        scaled - unit * jnp.mean(scaled * unit, axis=-1, keepdims=True)
    )


def back_kernel(
    grad_parts,
    middle,
    cotangent,
    gain,
    all_normed,
    grad_gate_pre,
    grad_up_pre,
    activated,
    all_cot,
    grad_middle,
    all_low,
    grad_gate,
    grad_up,
    part_down,
    rightward,
    leftward,
    low,
    turned_low,
    gate_1,
    gate_2,
    gate_3,
    gate_4,
    gate_5,
    gate_6,
    up_1,
    up_2,
    up_3,
    up_4,
    up_5,
    up_6,
    down_1,
    down_2,
    send,
    recv,
    here,
):
    links = Links(send, recv, here)
    links.greet(links.peers() + [links.x_way, links.y_way, links.core_way])
    sums = halved_sums(links, grad_parts, rightward, leftward)
    for half in sums:
        half.start()
    gate = PlaneScatter(links, gate_1, gate_2, gate_3, gate_4, gate_5, gate_6)
    up = PlaneScatter(links, up_1, up_2, up_3, up_4, up_5, up_6)
    down = PlaneScatter(links, down_1, down_2, None, None, None, None)
    tokens = middle.shape[0]
    spans, lines, keep = halves(tokens), [], []

    def compute(plane, which, rows, right):
        dp = links.dp if which == 1 else links.other_dp
        weight_grad(rows, right, plane.parts, dp)
        plane.between_cores(which)

    def turn(which):
        dp = links.dp if which == 1 else links.other_dp
        turned_low[which] = rows_turned(all_normed, gate_1, dp)

    def compute_down(which):
        dp = links.dp if which == 1 else links.other_dp
        compute(down, which, rows_turned(activated, down_1, dp), all_cot)

    def settle(half, rows_of_half):
        half.finish(grad_middle.at[rows_of_half])

        def body(rows):
            at = pl.ds(pl.multiple_of(rows_of_half.start + rows.start, ROWS), ROWS)
            back = back_rows(grad_middle[at, :], middle[at, :], gain[...])
            grad = cotangent[at, :].astype(jnp.float32) + back
            grad_middle[at, :] = grad
            low[at, :] = grad.astype(jnp.bfloat16)

        each_block(tokens // 2, body)
        line = LineGather(links, low.at[rows_of_half], all_low.at[:, rows_of_half])
        line.send(0)
        lines.append(line)

    later = range(2, links.n_blk - 1)
    turn(0)
    compute(gate, 0, turned_low.at[0], grad_gate_pre)
    sums[0].tick(1)
    turn(1)
    compute(gate, 1, turned_low.at[1], grad_gate_pre)
    for tick in later:
        sums[0].tick(tick)
    gate.across_chips()
    settle(sums[0], spans[0])
    compute(up, 0, turned_low.at[0], grad_up_pre)
    sums[1].tick(1)
    compute(up, 1, turned_low.at[1], grad_up_pre)
    for tick in later:
        sums[1].tick(tick)
    up.across_chips()
    settle(sums[1], spans[1])
    keep.append(links.local(low, all_low.at[links.blk]))
    compute_down(0)
    for step in range(1, links.n_blk - 1):
        for line in lines:
            line.arrived()
            line.send(step)
        if step == 1:
            gate.second_way()
            compute_down(1)
    up.second_way()
    for which in (0, 1):
        down.core_sums(which)
    for dp in range(links.n_dp):
        for row in range(2):
            keep.append(links.local(down.chunk(dp, row, down.core), part_down.at[dp, row]))
    for line in lines:
        line.arrived()

    def into(target):
        def write(block, rows, values):
            target[block, rows, :] = values.astype(target.dtype)

        return write

    gate.result(into(grad_gate))
    up.result(into(grad_up))
    for copy in keep:
        copy.wait()
    for half in sums:
        half.sent()
    links.finish()


def exchange_back(
    grad_parts,
    middle,
    cotangent,
    gain,
    all_normed,
    grad_gate_pre,
    grad_up_pre,
    activated,
    all_cot,
):
    n_dp, n_blk, n_uly = (lax.axis_size(a) for a in EVERY)
    _, tokens, width = grad_parts.shape
    ff = grad_gate_pre.shape[1]
    depth = width // (n_dp * n_blk * n_uly)
    down_depth = ff // (n_dp * n_uly)
    return pl.pallas_call(
        back_kernel,
        out_shape=[
            jax.ShapeDtypeStruct((tokens, width), jnp.float32),
            jax.ShapeDtypeStruct((n_blk, tokens, width), jnp.bfloat16),
            jax.ShapeDtypeStruct((n_blk, depth, ff), jnp.bfloat16),
            jax.ShapeDtypeStruct((n_blk, depth, ff), jnp.bfloat16),
            jax.ShapeDtypeStruct((n_dp, 2, 1, down_depth, width), jnp.bfloat16),
        ],
        in_specs=[VMEM] * 9,
        out_specs=[VMEM, HBM, VMEM, VMEM, HBM],
        scratch_shapes=line_scratch(n_blk, tokens, width)
        + [
            pltpu.VMEM((tokens, width), jnp.bfloat16),
            pltpu.VMEM((n_dp, width // n_dp, n_blk * tokens), jnp.bfloat16),
        ]
        + plane_scratch(n_dp, n_blk, n_uly, depth, ff) * 2
        + plane_scratch(n_dp, 1, n_uly, down_depth, width)[:2]
        + semaphores(72),
        compiler_params=kernel_params(3),
    )(
        grad_parts,
        middle,
        cotangent,
        gain,
        all_normed,
        grad_gate_pre,
        grad_up_pre,
        activated,
        all_cot,
    )


def last_kernel(
    w_qkv,
    hidden,
    grad_middle,
    gain,
    normed,
    grad_qkv,
    heads,
    all_low,
    head_terms,
    out_parts,
    middle,
    grad_hidden,
    grad_w_qkv,
    grad_wo,
    small_sum,
    output,
    grad_parts,
    rightward,
    leftward,
    qkv_1,
    qkv_2,
    qkv_3,
    qkv_4,
    qkv_5,
    qkv_6,
    wo_1,
    wo_2,
    wo_3,
    wo_4,
    wo_5,
    wo_6,
    summed,
    small_in,
    small_total,
    out_right,
    out_left,
    out_total,
    send,
    recv,
    here,
):
    links = Links(send, recv, here)
    links.greet(links.peers() + [links.x_way, links.y_way, links.core_way])
    sums = halved_sums(links, grad_parts, rightward, leftward)
    qkv = PlaneScatter(links, qkv_1, qkv_2, qkv_3, qkv_4, qkv_5, qkv_6)
    out = PlaneScatter(links, wo_1, wo_2, wo_3, wo_4, wo_5, wo_6)

    output_half = OutputHalf(links, 1, out_parts, middle, out_right, out_left, out_total)
    small_in[links.blk] = head_terms[...]
    small_copies = [
        links.to(head_terms, small_in.at[links.blk], device) for device in links.peers()
    ]

    def compute(plane, which, left, right):
        dp = links.dp if which == 1 else links.other_dp
        weight_grad(rows_turned(left, plane.parts, dp), right, plane.parts, dp)
        plane.between_cores(which)

    compute(qkv, 0, normed, grad_qkv)
    for copy in small_copies:
        copy.arrived()
    total = small_in[0]
    for blk in range(1, links.n_blk):
        total = total + small_in[blk]
    small_total[0] = total
    pending = links.to(small_total.at[0], small_in.at[links.n_blk], links.x_way)
    compute(qkv, 1, normed, grad_qkv)
    pending.arrived()
    small_total[1] = small_total[0] + small_in[links.n_blk]
    pending = links.to(small_total.at[1], small_in.at[links.n_blk + 1], links.y_way)
    tokens = grad_parts.shape[1]
    for column in range(0, w_qkv.shape[0], 512):
        grad_parts[:, :, column : column + 512] = (
            product_right(grad_qkv[...], w_qkv[column : column + 512, :])
            .astype(jnp.bfloat16)
            .reshape(links.n_blk, tokens, 512)
        )
    for half in sums:
        half.start()
    output_half.sum.start()
    pending.arrived()
    small_total[2] = small_total[1] + small_in[links.n_blk + 1]
    pending = links.to(small_total.at[2], small_in.at[links.n_blk + 2], links.core_way)
    qkv.across_chips()
    sums[0].tick(1)
    compute(out, 0, heads, all_low)
    for tick in range(2, links.n_blk - 1):
        sums[0].tick(tick)
    compute(out, 1, heads, all_low)
    pending.arrived()
    small_sum[...] = small_total[2] + small_in[links.n_blk + 2]
    sums[1].tick(1)
    out.across_chips()
    qkv.second_way()
    for tick in range(2, links.n_blk - 1):
        sums[1].tick(tick)
    output_half.sum.tick(1)
    out.second_way()

    def write(block, rows, values):
        summed[block, rows, :] = values.astype(jnp.bfloat16)

    qkv.result(write)
    swapped = []
    for step in range(1, links.n_blk):
        peer = links.peer(step)
        swapped.append(
            links.to(summed.at[peer], grad_w_qkv.at[links.blk], (links.dp, peer, links.uly))
        )
    keep = links.local(summed.at[links.blk], grad_w_qkv.at[links.blk])
    for tick in range(2, links.n_blk - 1):
        output_half.sum.tick(tick)
    for half, rows_of_half in zip(sums, halves(tokens)):
        half.finish(grad_hidden.at[rows_of_half])

    def body(rows):
        back = back_rows(grad_hidden[rows, :], hidden[rows, :].astype(jnp.float32), gain[...])
        grad_hidden[rows, :] = grad_middle[rows, :] + back

    each_block(tokens, body)

    def write_out(block, rows, values):
        grad_wo[block, rows, :] = values

    out.result(write_out)
    output_half.write(output)
    output_half.sum.sent()
    for copy in swapped:
        copy.arrived()
    keep.wait()
    for half in sums:
        half.sent()
    links.finish()


def exchange_last(
    w_qkv,
    hidden,
    grad_middle,
    gain,
    normed,
    grad_qkv,
    heads,
    all_low,
    head_terms,
    out_parts,
    middle,
):
    n_dp, _, n_uly = (lax.axis_size(a) for a in EVERY)
    n_blk, tokens, width = out_parts.shape
    columns = grad_qkv.shape[1]
    depth = width // (n_dp * n_blk * n_uly)
    out_depth = heads.shape[1] // (n_dp * n_uly)
    small = head_terms.shape
    return pl.pallas_call(
        last_kernel,
        out_shape=[
            jax.ShapeDtypeStruct((tokens, width), jnp.float32),
            jax.ShapeDtypeStruct((n_blk, depth, columns), jnp.bfloat16),
            jax.ShapeDtypeStruct((1, out_depth, width), jnp.float32),
            jax.ShapeDtypeStruct(small, jnp.float32),
            jax.ShapeDtypeStruct((tokens // 2, width), jnp.bfloat16),
        ],
        in_specs=[VMEM] * 11,
        out_specs=[VMEM, HBM, VMEM, VMEM, VMEM],
        scratch_shapes=[pltpu.VMEM((n_blk, tokens, width), jnp.bfloat16)]
        + line_scratch(n_blk, tokens, width)
        + plane_scratch(n_dp, n_blk, n_uly, depth, columns)
        + plane_scratch(n_dp, 1, n_uly, out_depth, width)
        + [
            pltpu.VMEM((n_blk, depth, columns), jnp.bfloat16),
            pltpu.VMEM((n_blk + 3,) + small, jnp.float32),
            pltpu.VMEM((3,) + small, jnp.float32),
        ]
        + output_scratch(n_blk, tokens, width)
        + semaphores(64),
        compiler_params=kernel_params(4),
    )(
        w_qkv,
        hidden,
        grad_middle,
        gain,
        normed,
        grad_qkv,
        heads,
        all_low,
        head_terms,
        out_parts,
        middle,
    )


def finish_kernel(
    gate,
    up,
    qkv,
    wo,
    wd,
    hidden,
    out_0,
    out_1,
    w_gate,
    w_up,
    w_query,
    key_weight,
    value_weight,
    attn_gain,
    mlp_gain,
    f_gate,
    f_up,
    f_q,
    f_k,
    f_v,
    f_wo,
    f_wd,
    f_hidden,
    f_out,
    f_attn,
    f_mlp,
):
    n_blk, depth, _ = gate.shape

    def place(source, offset, target):
        width = target.shape[1] // (n_blk * 2)
        for blk in range(n_blk):
            for group in range(2):
                to = (group * n_blk + blk) * width
                at = offset + group * width
                target[:, to : to + width] = source[blk, :, at : at + width].astype(jnp.float32)

    def gain_back(pairs, gain):
        total = jnp.zeros((depth, 128), jnp.float32)
        for weight, grad in pairs:
            for column in range(0, weight.shape[1], 128):
                at = slice(column, column + 128)
                total = total + weight[:, at].astype(jnp.float32) * grad[:, at]
        column = jnp.sum(total, axis=1, keepdims=True)
        square = (depth, depth)
        same = lax.broadcasted_iota(jnp.int32, square, 0) == lax.broadcasted_iota(
            jnp.int32, square, 1
        )
        return jnp.sum(jnp.where(same, column, 0.0), axis=0, keepdims=True) / gain[...]

    place(gate, 0, f_gate)
    place(up, 0, f_up)
    q_width = f_q.shape[1] // n_blk
    k_width = f_k.shape[1] // n_blk
    place(qkv, 0, f_q)
    place(qkv, q_width, f_k)
    place(qkv, q_width + k_width, f_v)
    f_wo[...] = wo[0]
    f_wd[...] = wd[0]
    f_hidden[...] = hidden[...]
    half = out_0.shape[0]
    f_out[:half, :] = out_0[...]
    f_out[half:, :] = out_1[...]
    f_attn[...] = gain_back(((w_query, f_q), (key_weight, f_k), (value_weight, f_v)), attn_gain)
    f_mlp[...] = gain_back(((w_gate, f_gate), (w_up, f_up)), mlp_gain)


def finish(gate, up, qkv, wo, wd, hidden, out_0, out_1, weights, gains):
    return pl.pallas_call(
        finish_kernel,
        out_shape=[jax.ShapeDtypeStruct(w.shape, jnp.float32) for w in weights]
        + [
            jax.ShapeDtypeStruct(wo.shape[1:], jnp.float32),
            jax.ShapeDtypeStruct(wd.shape[1:], jnp.float32),
            jax.ShapeDtypeStruct(hidden.shape, jnp.float32),
            jax.ShapeDtypeStruct(hidden.shape, jnp.bfloat16),
        ]
        + [jax.ShapeDtypeStruct(gain.shape, jnp.float32) for gain in gains],
        in_specs=[VMEM] * 15,
        out_specs=[VMEM] * 11,
        compiler_params=pltpu.CompilerParams(vmem_limit_bytes=62 * MIB),
    )(gate, up, qkv, wo, wd, hidden, out_0, out_1, *weights, *gains)


def product(left, right):
    return jnp.dot(left, right, preferred_element_type=jnp.float32)


def shards(
    hidden,
    span_order,
    attn_gain,
    w_query,
    key_weight,
    value_weight,
    w_out,
    q_gain,
    k_gain,
    mlp_gain,
    w_gate,
    w_up,
    w_down,
    cotangent,
):
    seqs, toks, width = hidden.shape
    n_dp, n_blk, n_uly = (lax.axis_size(a) for a in EVERY)
    rows = n_blk * seqs * toks
    f32, bf16 = jnp.float32, jnp.bfloat16
    own_hidden = hidden.reshape(seqs * toks, width)
    own_cotangent = cotangent.reshape(seqs * toks, width)

    gain_q, gain_k = q_gain.astype(f32)[None, :], k_gain.astype(f32)[None, :]

    gain_rows = attn_gain.shape[0]
    own_gains = jnp.pad(jnp.stack([attn_gain, mlp_gain]), ((0, 30), (0, 128 - gain_rows)))
    (
        all_hidden,
        w_qkv,
        wo,
        g_attn,
        g_mlp,
        cosine,
        sine,
        query_pos,
        key_pos,
    ) = gather_front(
        span_order,
        own_hidden,
        w_query,
        key_weight,
        value_weight,
        w_out,
        own_gains,
        toks,
        gain_rows,
    )
    w_qkv = w_qkv.reshape(width, -1)
    wo = wo.reshape(-1, width)
    (
        rows_wg,
        rows_wu,
        all_wd,
        cot,
        heads_flat,
        normed,
        qkv,
        queries,
        key_values,
        lse,
    ) = attend_forward(
        w_gate,
        w_up,
        w_down,
        own_cotangent,
        all_hidden.reshape(rows, width),
        w_qkv,
        g_attn,
        gain_q,
        gain_k,
        cosine,
        sine,
        query_pos,
        key_pos,
        seqs,
    )
    middle, normed2, all_wg, all_wu, cot = exchange_middle(
        heads_flat.reshape(n_blk, seqs * toks, -1),
        wo,
        own_hidden,
        g_mlp,
        rows_wg,
        rows_wu,
        cot,
    )
    wg, wu = all_wg.reshape(width, -1), all_wu.reshape(width, -1)
    wd = all_wd.reshape(-1, width)
    cot = cot.reshape(rows, width)
    normed2 = normed2.reshape(rows, width)
    gate_pre = product(normed2, wg)
    up_pre = product(normed2, wu)
    sigmoid_gate = jax.nn.sigmoid(gate_pre)
    activated = (gate_pre * sigmoid_gate * up_pre).astype(bf16)
    out_parts = product(activated, wd).astype(bf16)
    grad_act = product_right(cot, wd)
    grad_gate_pre = (
        grad_act * up_pre * sigmoid_gate * (1.0 + gate_pre * (1.0 - sigmoid_gate))
    ).astype(bf16)
    grad_up_pre = (grad_act * gate_pre * sigmoid_gate).astype(bf16)
    grad_parts = (product_right(grad_gate_pre, wg) + product_right(grad_up_pre, wu)).astype(bf16)
    blocks = (n_blk, seqs * toks, width)
    grad_middle, middle_low, grad_gate, grad_up, part_down = exchange_back(
        grad_parts.reshape(blocks),
        middle,
        own_cotangent,
        g_mlp,
        normed2,
        grad_gate_pre,
        grad_up_pre,
        activated,
        cot,
    )
    middle_low = middle_low.reshape(rows, width)
    out_parts = out_parts.reshape(blocks)
    grad_qkv, head_terms, grad_down, output_0, grad_gate, grad_up = attend_back(
        middle_low,
        wo,
        queries,
        key_values,
        lse,
        qkv,
        gain_q,
        gain_k,
        cosine,
        sine,
        query_pos,
        key_pos,
        out_parts,
        middle,
        grad_gate,
        grad_up,
        part_down,
    )
    grad_hidden, grad_w_qkv, grad_out, small, output_1 = exchange_last(
        w_qkv,
        own_hidden,
        grad_middle,
        g_attn,
        normed,
        grad_qkv,
        heads_flat,
        middle_low,
        head_terms,
        out_parts,
        middle,
    )
    (
        grad_gate,
        grad_up,
        grad_query,
        grad_key,
        grad_value,
        grad_out,
        grad_down,
        grad_hidden,
        output,
        grad_attn_gain,
        grad_mlp_gain,
    ) = finish(
        grad_gate,
        grad_up,
        grad_w_qkv,
        grad_out,
        grad_down,
        grad_hidden,
        output_0,
        output_1,
        (w_gate, w_up, w_query, key_weight, value_weight),
        [g.astype(f32)[None, :] for g in (attn_gain, mlp_gain)],
    )
    grad_q_gain, grad_k_gain = small[0], small[1]
    return (
        output.reshape(hidden.shape),
        grad_hidden.reshape(hidden.shape),
        grad_attn_gain.reshape(gain_rows),
        grad_query,
        grad_key,
        grad_value,
        grad_out,
        grad_q_gain,
        grad_k_gain,
        grad_mlp_gain.reshape(gain_rows),
        grad_gate,
        grad_up,
        grad_down,
    )


def solution(mesh):
    n_dp, n_blk, n_uly = (mesh.shape[a] for a in EVERY)
    aligned = (n_dp, n_uly) == (2, 4) and KEY_VALUE_HEADS % (n_dp * n_blk) == 0
    in_specs = (
        TOKENS,
        P(),
        P(EVERY),
        P(EVERY, None),
        P(EVERY, None),
        P(EVERY, None),
        P(EVERY, None),
        P(),
        P(),
        P(EVERY),
        P(EVERY, None),
        P(EVERY, None),
        P(EVERY, None),
        TOKENS,
    )
    out_specs = (
        TOKENS,
        TOKENS,
        P(EVERY),
        P(EVERY, None),
        P(EVERY, None),
        P(EVERY, None),
        P(EVERY, None),
        P(),
        P(),
        P(EVERY),
        P(EVERY, None),
        P(EVERY, None),
        P(EVERY, None),
    )
    return jax.shard_map(
        shards if aligned else shards_general,
        mesh=mesh, in_specs=in_specs, out_specs=out_specs, check_vma=False)
```

```python
import functools
import math

import jax
import jax.numpy as jnp
from jax import lax
from jax.experimental import pallas as pl
from jax.experimental.pallas import tpu as pltpu
from jax.sharding import PartitionSpec as P

QUERY_HEADS = 16
KEY_VALUE_HEADS = 8
HEAD_SIZE = 128


DP, BLK, ULY = "dp", "blk", "uly"
EVERY = (DP, BLK, ULY)
PLANE = (DP, ULY)
TOKENS = P(DP, (BLK, ULY), None)
EQ_KGQD_NKD_TO_KGQN = "kgqd,nkd->kgqn"
EQ_KGQN_KGQD_TO_NKD = "kgqn,kgqd->nkd"
EQ_KGQN_NKD_TO_KGQD = "kgqn,nkd->kgqd"
EQ_KGQN_QKGD_TO_NKD = "kgqn,qkgd->nkd"
EQ_QKGD_NKD_TO_KGQN = "qkgd,nkd->kgqn"
EQ_STD_DE_TO_STE = "std,de->ste"
EQ_STD_DF_TO_STF = "std,df->stf"
EQ_STD_ED_TO_STE = "std,ed->ste"
EQ_STD_FD_TO_STF = "std,fd->stf"
EQ_STD_STE_TO_DE = "std,ste->de"
EQ_STD_STF_TO_DF = "std,stf->df"
EQ_STE_DE_TO_STD = "ste,de->std"
EQ_STE_ED_TO_STD = "ste,ed->std"
EQ_STE_STD_TO_ED = "ste,std->ed"
EQ_STF_DF_TO_STD = "stf,df->std"
EQ_STF_FD_TO_STD = "stf,fd->std"
EQ_STF_STD_TO_FD = "stf,std->fd"

EPSILON = 1e-06
ROPE_BASE = 1000000.0


def rms_scale(source):
    return lax.rsqrt(jnp.mean(source * source, axis=-1, keepdims=True) + EPSILON)


def norm_back(grad_normed, source, norm_scale, gain):
    unit_rows = source * norm_scale
    scaled = grad_normed * gain
    return norm_scale * (scaled - unit_rows * jnp.mean(scaled * unit_rows, axis=-1, keepdims=True))


def angles_of(positions, head_dim):
    freq_steps = jnp.arange(head_dim // 2, dtype=jnp.float32)
    inverse = jnp.exp(freq_steps * (-2.0 * math.log(ROPE_BASE) / head_dim))
    return positions.astype(jnp.float32)[:, None] * inverse[None, :]


def rotate(source, angles, direction):
    half_dim = source.shape[-1] // 2
    cosine = jnp.cos(angles)[:, None, :]
    sine_part = direction * jnp.sin(angles)[:, None, :]
    first_half = source[..., :half_dim]
    second_half = source[..., half_dim:]
    return jnp.concatenate(
        [
            first_half * cosine - second_half * sine_part,
            second_half * cosine + first_half * sine_part,
        ],
        axis=-1,
    )


def positions_of(places, span_order, half_len):
    blocks_of = places // half_len
    block_ids = jnp.arange(span_order.shape[0], dtype=jnp.int32)
    chosen = jnp.sum(
        jnp.where(blocks_of[:, None] == block_ids[None, :], span_order[None, :], 0), axis=1
    )
    return chosen * half_len + places % half_len


def add_rows(buffer, new_rows):
    return buffer + new_rows


def shards_general(
    hidden,
    span_order,
    attn_gain,
    w_query,
    key_weight,
    value_weight,
    w_out,
    q_gain,
    k_gain,
    mlp_gain,
    w_gate,
    w_up,
    w_down,
    cotangent,
):
    sequence_count = hidden.shape[0]
    token_count = hidden.shape[1]
    ulysses_group_size = lax.axis_size(ULY)
    local_q = QUERY_HEADS // ulysses_group_size
    local_key_value = KEY_VALUE_HEADS // ulysses_group_size
    query_group_width = QUERY_HEADS // KEY_VALUE_HEADS
    block_len = token_count * ulysses_group_size
    half_len = block_len // 2
    score_scale = 1.0 / math.sqrt(HEAD_SIZE)
    blk_index = lax.axis_index(BLK)
    uly_index = lax.axis_index(ULY)
    first_place = (blk_index * ulysses_group_size + uly_index) * token_count
    local_angles = angles_of(
        positions_of(first_place + jnp.arange(token_count, dtype=jnp.int32), span_order, half_len),
        HEAD_SIZE,
    )
    query_pos = positions_of(
        blk_index * block_len + jnp.arange(block_len, dtype=jnp.int32), span_order, half_len
    )
    g_attn, wq_all, wk_all, wv_all, wo_all = (
        lax.all_gather(attn_gain, EVERY, axis=0, tiled=True),
        lax.all_gather(w_query, EVERY, axis=0, tiled=True),
        lax.all_gather(key_weight, EVERY, axis=0, tiled=True),
        lax.all_gather(value_weight, EVERY, axis=0, tiled=True),
        lax.all_gather(w_out, EVERY, axis=0, tiled=True),
    )
    source = hidden.astype(jnp.float32)
    first_scale = rms_scale(source)
    normalized_input = (source * first_scale * g_attn.astype(jnp.float32)).astype(jnp.bfloat16)
    q_pre = jnp.einsum(
        EQ_STD_DE_TO_STE, normalized_input, wq_all, preferred_element_type=jnp.float32
    ).reshape(sequence_count, token_count, QUERY_HEADS, HEAD_SIZE)
    key_before_norm = jnp.einsum(
        EQ_STD_DE_TO_STE, normalized_input, wk_all, preferred_element_type=jnp.float32
    ).reshape(sequence_count, token_count, KEY_VALUE_HEADS, HEAD_SIZE)
    value_before_norm = jnp.einsum(
        EQ_STD_DE_TO_STE, normalized_input, wv_all, preferred_element_type=jnp.float32
    ).reshape(sequence_count, token_count, KEY_VALUE_HEADS, HEAD_SIZE)
    q_scale = rms_scale(q_pre)
    k_scale = rms_scale(key_before_norm)
    gain_q = q_gain.astype(jnp.float32)
    gain_k = k_gain.astype(jnp.float32)
    q_rot = rotate(q_pre * q_scale * gain_q, local_angles, 1.0).astype(jnp.bfloat16)
    k_rot = rotate(key_before_norm * k_scale * gain_k, local_angles, 1.0).astype(jnp.bfloat16)
    v_low = value_before_norm.astype(jnp.bfloat16)
    q_heads, k_heads, v_heads = (
        lax.all_to_all(q_rot, ULY, split_axis=2, concat_axis=1, tiled=True),
        lax.all_to_all(k_rot, ULY, split_axis=2, concat_axis=1, tiled=True),
        lax.all_to_all(v_low, ULY, split_axis=2, concat_axis=1, tiled=True),
    )
    q_group = q_heads.reshape(
        sequence_count, block_len, local_key_value, query_group_width, HEAD_SIZE
    )
    stat_shape = (sequence_count, local_key_value, query_group_width, block_len)
    start_state = (
        jnp.full(stat_shape, -1e30, jnp.float32),
        jnp.zeros(stat_shape, jnp.float32),
        jnp.zeros(stat_shape + (HEAD_SIZE,), jnp.float32),
    )
    key_piece = lax.all_gather(k_heads, BLK, axis=1, tiled=True)
    value_piece = lax.all_gather(v_heads, BLK, axis=1, tiled=True)
    key_pos = positions_of(jnp.arange(key_piece.shape[1], dtype=jnp.int32), span_order, half_len)
    allowed = query_pos[:, None] >= key_pos[None, :]

    def attend_one_sequence(members):
        query_rows, key_rows, value_rows, top_seq, total_seq, accum_seq = members
        scores = (
            jnp.einsum(EQ_QKGD_NKD_TO_KGQN, query_rows, key_rows, preferred_element_type=jnp.float32)
            * score_scale
        )
        scores = jnp.where(allowed, scores, -jnp.inf)
        new_top = jnp.maximum(top_seq, jnp.max(scores, axis=-1))
        fading = jnp.exp(top_seq - new_top)
        weights = jnp.exp(scores - new_top[..., None])
        total_seq = total_seq * fading + jnp.sum(weights, axis=-1)
        accum_seq = accum_seq * fading[..., None] + jnp.einsum(
            EQ_KGQN_NKD_TO_KGQD,
            weights.astype(jnp.bfloat16),
            value_rows,
            preferred_element_type=jnp.float32,
        )
        return (new_top, total_seq, accum_seq)

    row_top, row_total, accum = lax.map(
        attend_one_sequence,
        (q_group, key_piece, value_piece, start_state[0], start_state[1], start_state[2]),
    )
    log_total = row_top + jnp.log(row_total)
    attention_output = jnp.transpose(accum / row_total[..., None], (0, 3, 1, 2, 4)).reshape(
        sequence_count, block_len, local_q, HEAD_SIZE
    )
    heads_seq = lax.all_to_all(
        attention_output.astype(jnp.bfloat16), ULY, split_axis=1, concat_axis=2, tiled=True
    )
    heads_flat = heads_seq.reshape(sequence_count, token_count, QUERY_HEADS * HEAD_SIZE)
    middle = source + jnp.einsum(
        EQ_STE_ED_TO_STD, heads_flat, wo_all, preferred_element_type=jnp.float32
    )
    g_mlp, wg_all, wu_all, wd_all = (
        lax.all_gather(mlp_gain, EVERY, axis=0, tiled=True),
        lax.all_gather(w_gate, EVERY, axis=0, tiled=True),
        lax.all_gather(w_up, EVERY, axis=0, tiled=True),
        lax.all_gather(w_down, EVERY, axis=0, tiled=True),
    )
    second_scale = rms_scale(middle)
    gain_mlp = g_mlp.astype(jnp.float32)
    normed2 = (middle * second_scale * gain_mlp).astype(jnp.bfloat16)
    gate_pre = jnp.einsum(EQ_STD_DF_TO_STF, normed2, wg_all, preferred_element_type=jnp.float32)
    up_pre = jnp.einsum(EQ_STD_DF_TO_STF, normed2, wu_all, preferred_element_type=jnp.float32)
    sigmoid_gate = jax.nn.sigmoid(gate_pre)
    activated = (gate_pre * sigmoid_gate * up_pre).astype(jnp.bfloat16)
    result = middle + jnp.einsum(
        EQ_STF_FD_TO_STD, activated, wd_all, preferred_element_type=jnp.float32
    )
    output = result.astype(jnp.bfloat16)
    g_mlp, wg_all, wu_all, wd_all = (
        lax.all_gather(mlp_gain, EVERY, axis=0, tiled=True),
        lax.all_gather(w_gate, EVERY, axis=0, tiled=True),
        lax.all_gather(w_up, EVERY, axis=0, tiled=True),
        lax.all_gather(w_down, EVERY, axis=0, tiled=True),
    )
    gain_mlp = g_mlp.astype(jnp.float32)
    grad_act = jnp.einsum(EQ_STD_FD_TO_STF, cotangent, wd_all, preferred_element_type=jnp.float32)
    grad_gate_pre = (
        grad_act * up_pre * sigmoid_gate * (1.0 + gate_pre * (1.0 - sigmoid_gate))
    ).astype(jnp.bfloat16)
    grad_up_pre = (grad_act * gate_pre * sigmoid_gate).astype(jnp.bfloat16)
    grad_gate = jnp.einsum(
        EQ_STD_STF_TO_DF, normed2, grad_gate_pre, preferred_element_type=jnp.float32
    )
    grad_up = jnp.einsum(EQ_STD_STF_TO_DF, normed2, grad_up_pre, preferred_element_type=jnp.float32)
    grad_normed2 = jnp.einsum(
        EQ_STF_DF_TO_STD, grad_gate_pre, wg_all, preferred_element_type=jnp.float32
    ) + jnp.einsum(EQ_STF_DF_TO_STD, grad_up_pre, wu_all, preferred_element_type=jnp.float32)
    mlp_gain_term = jnp.sum(grad_normed2 * middle * second_scale, axis=(0, 1))
    grad_middle = cotangent.astype(jnp.float32) + norm_back(
        grad_normed2, middle, second_scale, gain_mlp
    )
    grad_mlp_gain, grad_gate, grad_up = (
        lax.psum_scatter(mlp_gain_term, EVERY, scatter_dimension=0, tiled=True),
        lax.psum_scatter(grad_gate, EVERY, scatter_dimension=0, tiled=True),
        lax.psum_scatter(grad_up, EVERY, scatter_dimension=0, tiled=True),
    )
    g_attn, wq_all, wk_all, wv_all, wo_all = (
        lax.all_gather(attn_gain, EVERY, axis=0, tiled=True),
        lax.all_gather(w_query, EVERY, axis=0, tiled=True),
        lax.all_gather(key_weight, EVERY, axis=0, tiled=True),
        lax.all_gather(value_weight, EVERY, axis=0, tiled=True),
        lax.all_gather(w_out, EVERY, axis=0, tiled=True),
    )
    middle_low = grad_middle.astype(jnp.bfloat16)
    grad_out = jnp.einsum(EQ_STE_STD_TO_ED, heads_flat, middle_low, preferred_element_type=jnp.float32)
    grad_heads = (
        jnp.einsum(EQ_STD_ED_TO_STE, middle_low, wo_all, preferred_element_type=jnp.float32)
        .astype(jnp.bfloat16)
        .reshape(sequence_count, token_count, QUERY_HEADS, HEAD_SIZE)
    )
    grad_heads_local = lax.all_to_all(grad_heads, ULY, split_axis=2, concat_axis=1, tiled=True)
    grad_group = jnp.transpose(
        grad_heads_local.reshape(
            sequence_count, block_len, local_key_value, query_group_width, HEAD_SIZE
        ),
        (0, 2, 3, 1, 4),
    )
    delta = jnp.sum(grad_heads_local.astype(jnp.float32) * attention_output, axis=-1)
    delta = jnp.transpose(
        delta.reshape(sequence_count, block_len, local_key_value, query_group_width), (0, 2, 3, 1)
    )
    seq_length = block_len * lax.axis_size(BLK)
    zero_keys = jnp.zeros((sequence_count, seq_length, local_key_value, HEAD_SIZE), jnp.float32)
    back_state = (jnp.zeros(stat_shape + (HEAD_SIZE,), jnp.float32), zero_keys, zero_keys)
    key_piece = lax.all_gather(k_heads, BLK, axis=1, tiled=True)
    value_piece = lax.all_gather(v_heads, BLK, axis=1, tiled=True)
    key_pos = positions_of(jnp.arange(key_piece.shape[1], dtype=jnp.int32), span_order, half_len)
    back_allowed = query_pos[:, None] >= key_pos[None, :]

    def back_one_sequence(members):
        query_rows, grad_rows, lse_seq, delta_seq, key_rows, value_rows, dq_seq, dk_seq, dv_seq = (
            members
        )
        scores = (
            jnp.einsum(EQ_QKGD_NKD_TO_KGQN, query_rows, key_rows, preferred_element_type=jnp.float32)
            * score_scale
        )
        scores = jnp.where(back_allowed, scores, -jnp.inf)
        probs = jnp.exp(scores - lse_seq[..., None])
        grad_values = jnp.einsum(
            EQ_KGQN_KGQD_TO_NKD,
            probs.astype(jnp.bfloat16),
            grad_rows,
            preferred_element_type=jnp.float32,
        )
        grad_probs = jnp.einsum(
            EQ_KGQD_NKD_TO_KGQN, grad_rows, value_rows, preferred_element_type=jnp.float32
        )
        grad_scores = (probs * (grad_probs - delta_seq[..., None])).astype(jnp.bfloat16)
        dq_seq = dq_seq + score_scale * jnp.einsum(
            EQ_KGQN_NKD_TO_KGQD, grad_scores, key_rows, preferred_element_type=jnp.float32
        )
        grad_keys = score_scale * jnp.einsum(
            EQ_KGQN_QKGD_TO_NKD, grad_scores, query_rows, preferred_element_type=jnp.float32
        )
        return (dq_seq, add_rows(dk_seq, grad_keys), add_rows(dv_seq, grad_values))

    grad_q_group, grad_k_whole, grad_v_whole = lax.map(
        back_one_sequence,
        (
            q_group,
            grad_group,
            log_total,
            delta,
            key_piece,
            value_piece,
            back_state[0],
            back_state[1],
            back_state[2],
        ),
    )
    grad_k_block, grad_v_block = (
        lax.psum_scatter(
            grad_k_whole.astype(jnp.bfloat16), BLK, scatter_dimension=1, tiled=True
        ).astype(jnp.float32),
        lax.psum_scatter(
            grad_v_whole.astype(jnp.bfloat16), BLK, scatter_dimension=1, tiled=True
        ).astype(jnp.float32),
    )
    grad_q_block = jnp.transpose(grad_q_group, (0, 3, 1, 2, 4)).reshape(
        sequence_count, block_len, local_q, HEAD_SIZE
    )
    grad_q_seq, grad_k_seq, value_sequence_gradient = (
        lax.all_to_all(
            grad_q_block.astype(jnp.bfloat16), ULY, split_axis=1, concat_axis=2, tiled=True
        ).astype(grad_q_block.dtype),
        lax.all_to_all(
            grad_k_block.astype(jnp.bfloat16), ULY, split_axis=1, concat_axis=2, tiled=True
        ).astype(grad_k_block.dtype),
        lax.all_to_all(
            grad_v_block.astype(jnp.bfloat16), ULY, split_axis=1, concat_axis=2, tiled=True
        ).astype(grad_v_block.dtype),
    )
    grad_q_normed = rotate(grad_q_seq, local_angles, -1.0)
    grad_k_normed = rotate(grad_k_seq, local_angles, -1.0)
    q_gain_term = jnp.sum(grad_q_normed * q_pre * q_scale, axis=(0, 1, 2))
    k_gain_term = jnp.sum(grad_k_normed * key_before_norm * k_scale, axis=(0, 1, 2))
    grad_q_pre = (
        norm_back(grad_q_normed, q_pre, q_scale, gain_q)
        .astype(jnp.bfloat16)
        .reshape(sequence_count, token_count, QUERY_HEADS * HEAD_SIZE)
    )
    grad_k_pre = (
        norm_back(grad_k_normed, key_before_norm, k_scale, gain_k)
        .astype(jnp.bfloat16)
        .reshape(sequence_count, token_count, KEY_VALUE_HEADS * HEAD_SIZE)
    )
    value_pre_gradient = value_sequence_gradient.astype(jnp.bfloat16).reshape(
        sequence_count, token_count, KEY_VALUE_HEADS * HEAD_SIZE
    )
    grad_query = jnp.einsum(
        EQ_STD_STE_TO_DE, normalized_input, grad_q_pre, preferred_element_type=jnp.float32
    )
    grad_key = jnp.einsum(
        EQ_STD_STE_TO_DE, normalized_input, grad_k_pre, preferred_element_type=jnp.float32
    )
    grad_value = jnp.einsum(
        EQ_STD_STE_TO_DE, normalized_input, value_pre_gradient, preferred_element_type=jnp.float32
    )
    grad_normed = jnp.einsum(EQ_STE_DE_TO_STD, grad_q_pre, wq_all, preferred_element_type=jnp.float32)
    grad_normed = grad_normed + jnp.einsum(
        EQ_STE_DE_TO_STD, grad_k_pre, wk_all, preferred_element_type=jnp.float32
    )
    grad_normed = grad_normed + jnp.einsum(
        EQ_STE_DE_TO_STD, value_pre_gradient, wv_all, preferred_element_type=jnp.float32
    )
    attn_gain_term = jnp.sum(grad_normed * source * first_scale, axis=(0, 1))
    grad_hidden = grad_middle + norm_back(
        grad_normed, source, first_scale, g_attn.astype(jnp.float32)
    )
    grad_down = jnp.einsum(EQ_STF_STD_TO_FD, activated, cotangent, preferred_element_type=jnp.float32)
    grad_attn_gain, grad_query, grad_key, grad_value, grad_out, grad_down = (
        lax.psum_scatter(attn_gain_term, EVERY, scatter_dimension=0, tiled=True),
        lax.psum_scatter(grad_query, EVERY, scatter_dimension=0, tiled=True),
        lax.psum_scatter(grad_key, EVERY, scatter_dimension=0, tiled=True),
        lax.psum_scatter(grad_value, EVERY, scatter_dimension=0, tiled=True),
        lax.psum_scatter(grad_out, EVERY, scatter_dimension=0, tiled=True),
        lax.psum_scatter(grad_down, EVERY, scatter_dimension=0, tiled=True),
    )
    grad_q_gain, grad_k_gain = lax.psum((q_gain_term, k_gain_term), EVERY)
    return (
        output,
        grad_hidden,
        grad_attn_gain,
        grad_query,
        grad_key,
        grad_value,
        grad_out,
        grad_q_gain,
        grad_k_gain,
        grad_mlp_gain,
        grad_gate,
        grad_up,
        grad_down,
    )


MESH = pl.DeviceIdType.MESH
HBM = pl.BlockSpec(memory_space=pltpu.HBM)
VMEM = pl.BlockSpec(memory_space=pltpu.VMEM)
MIB = 1 << 20


def kernel_params(collective_id, vmem_mib=62):
    return pltpu.CompilerParams(
        collective_id=collective_id, has_side_effects=True, vmem_limit_bytes=vmem_mib * MIB
    )


def semaphores(count, local=16):
    return [
        pltpu.SemaphoreType.DMA((count,)),
        pltpu.SemaphoreType.DMA((count,)),
        pltpu.SemaphoreType.DMA((local,)),
    ]


class Copy:
    def __init__(self, descriptor, sends, receives):
        self.descriptor, self.sends, self.receives = descriptor, sends, receives

    def under(self, condition, action):
        if condition is None:
            action()
        else:
            pl.when(condition)(action)

    def start(self):
        self.under(self.sends, lambda: self.descriptor().start())
        return self

    def sent(self):
        self.under(self.sends, lambda: self.descriptor().wait_send())

    def arrived(self):
        self.under(self.receives, lambda: self.descriptor().wait_recv())


class Links:
    def __init__(self, send, recv, here):
        self.send, self.recv, self.here = send, recv, here
        self.used, self.used_here = 0, 0
        self.copies, self.local_copies = [], []
        self.n_dp, self.n_blk, self.n_uly = (lax.axis_size(a) for a in EVERY)
        self.dp, self.blk, self.uly = (lax.axis_index(a) for a in EVERY)
        self.other_dp = 1 - self.dp
        self.across = lax.rem(self.uly + 2, 4)
        self.twin = self.uly + 1 - 2 * lax.rem(self.uly, 2)
        self.x_way = (self.other_dp, self.blk, self.uly)
        self.y_way = (self.dp, self.blk, self.across)
        self.core_way = (self.dp, self.blk, self.twin)

    def peer(self, step):
        return lax.rem(self.blk + step, self.n_blk)

    def peers(self):
        return [(self.dp, self.peer(k), self.uly) for k in range(1, self.n_blk)]

    def greet(self, devices):
        barrier = pltpu.get_barrier_semaphore()
        for device in devices:
            pl.semaphore_signal(barrier, inc=1, device_id=device, device_id_type=MESH)
        pl.semaphore_wait(barrier, len(devices))

    def remote(self, source, target, device, sends=None, receives=None):
        slot = self.used
        self.used += 1

        def descriptor():
            return pltpu.make_async_remote_copy(
                src_ref=source(),
                dst_ref=target(),
                send_sem=self.send.at[slot],
                recv_sem=self.recv.at[slot],
                device_id=device,
                device_id_type=MESH,
            )

        copy = Copy(descriptor, sends, receives)
        self.copies.append(copy)
        return copy.start()

    def to(self, source, target, device):
        return self.remote(lambda: source, lambda: target, device)

    def local(self, source, target):
        copy = pltpu.make_async_copy(source, target, self.here.at[self.used_here])
        self.used_here += 1
        copy.start()
        self.local_copies.append(copy)
        return copy

    def finish(self):
        for copy in self.copies:
            copy.sent()


class LineGather:
    def __init__(self, links, own, whole):
        self.links, self.own, self.whole = links, own, whole
        self.waiting = []

    def send(self, step):
        links, whole = self.links, self.whole
        blk, last = links.blk, links.n_blk - 1

        def block(index):
            if step == 0:
                return lambda: self.own
            return lambda: whole.at[index]

        self.waiting = [
            links.remote(
                block(blk - step),
                lambda: whole.at[blk - step],
                (links.dp, blk + 1, links.uly),
                jnp.logical_and(blk >= step, blk < last),
                blk >= step + 1,
            ),
            links.remote(
                block(blk + step),
                lambda: whole.at[blk + step],
                (links.dp, blk - 1, links.uly),
                jnp.logical_and(blk + step <= last, blk > 0),
                blk + step + 1 <= last,
            ),
        ]

    def arrived(self):
        for copy in self.waiting:
            copy.arrived()


def halves(tokens):
    return [pl.ds(0, tokens // 2), pl.ds(tokens // 2, tokens // 2)]


class HalvedLine:
    def __init__(self, links, own, whole):
        self.lines = [
            LineGather(links, None if own is None else own.at[rows], whole.at[:, rows])
            for rows in halves(whole.shape[1])
        ]

    def send(self, step):
        for line in self.lines:
            line.send(step)

    def advance(self, step):
        for line in self.lines:
            line.arrived()
            line.send(step)

    def arrived(self):
        for line in self.lines:
            line.arrived()


class PlaneGather:
    def __init__(self, links, at):
        self.links, self.at = links, at

    def start_x(self, own):
        links = self.links
        mine = self.at(links.dp, links.uly)
        self.from_x = links.to(own, mine, links.x_way)
        self.from_core = [links.to(own, mine, links.core_way)]

    def start_y(self, own):
        links = self.links
        self.from_y = links.to(own, self.at(links.dp, links.uly), links.y_way)

    def start(self, own=None):
        own = self.at(self.links.dp, self.links.uly) if own is None else own
        self.start_x(own)
        self.start_y(own)

    def hand_on(self):
        links, at = self.links, self.at
        self.from_x.arrived()
        half = at(links.other_dp, links.uly, 0)
        self.second_y = links.to(half, half, links.y_way)
        self.from_y.arrived()
        half = at(links.dp, links.across, 1)
        self.second_x = links.to(half, half, links.x_way)
        for chunk in (at(links.other_dp, links.uly), at(links.dp, links.across)):
            self.from_core.append(links.to(chunk, chunk, links.core_way))

    def last(self):
        links = self.links
        self.second_y.arrived()
        self.second_x.arrived()
        chunk = self.at(links.other_dp, links.across)
        self.from_core.append(links.to(chunk, chunk, links.core_way))

    def arrived(self):
        for copy in self.from_core:
            copy.arrived()


def rows_of(whole, blocked):
    def at(dp, uly, half=None):
        part = whole.at[dp, :, uly] if blocked else whole.at[dp, uly]
        if half is None:
            return part
        depth = whole.shape[-2] // 2
        rows = pl.ds(half * depth, depth)
        return part.at[:, rows] if blocked else part.at[rows]

    return at


class ColumnSwap:
    def __init__(self, links, pieces):
        self.links, self.pieces = links, pieces
        self.incoming, self.kept = [], []

    def parts(self, blk):
        links = self.links
        for weight, whole, offset in self.pieces:
            width = weight.shape[-1] // links.n_dp // links.n_blk
            for group in range(links.n_dp):
                start = (group * links.n_blk + blk) * width
                yield (
                    weight.at[:, pl.ds(pl.multiple_of(start, 128), width)],
                    whole.at[links.blk, :, pl.ds(offset + group * width, width)],
                )

    def start(self):
        links = self.links
        for step in range(1, links.n_blk):
            device = (links.dp, links.peer(step), links.uly)
            for source, target in self.parts(links.peer(step)):
                self.incoming.append(links.to(source, target, device))
        for source, target in self.parts(links.blk):
            self.kept.append(links.local(source, target))

    def arrived(self):
        for copy in self.kept:
            copy.wait()
        for copy in self.incoming:
            copy.arrived()


def write_positions(links, span_order, toks, cosine, sine, query_pos, key_pos):
    half_len = toks * links.n_uly // 2

    def first(blk, uly):
        chunk = span_order[2 * blk + lax.div(uly, links.n_uly // 2)]
        return chunk * half_len + lax.rem(uly, links.n_uly // 2) * toks

    lane = lax.broadcasted_iota(jnp.int32, (toks, HEAD_SIZE), 1)
    row = lax.broadcasted_iota(jnp.int32, (toks, HEAD_SIZE), 0)
    upper = lane >= HEAD_SIZE // 2
    step = jnp.where(upper, lane - HEAD_SIZE // 2, lane).astype(jnp.float32)
    inverse = jnp.exp(step * (-2.0 * math.log(ROPE_BASE) / HEAD_SIZE))
    for blk in range(links.n_blk):
        angles = (first(blk, links.uly) + row).astype(jnp.float32) * inverse
        at = slice(blk * toks, (blk + 1) * toks)
        cosine[at, :] = jnp.cos(angles)
        turn = jnp.sin(angles)
        sine[at, :] = jnp.where(upper, turn, -turn)
    lane = lax.broadcasted_iota(jnp.int32, query_pos.shape, 1)
    place = jnp.zeros(query_pos.shape, jnp.int32)
    for start in range(0, query_pos.shape[1], toks):
        blk = start // toks % links.n_blk
        here = jnp.logical_and(lane >= start, lane < start + toks)
        place = jnp.where(here, first(blk, links.uly) + lane - start, place)
    query_pos[...] = place
    row = lax.broadcasted_iota(jnp.int32, (toks, 1), 0)
    for uly in range(links.n_uly):
        for blk in range(links.n_blk):
            start = (uly * links.n_blk + blk) * toks
            key_pos[start : start + toks, :] = row + first(blk, jnp.int32(uly))


def write_gains(links, all_gains, size, targets):
    per_row = 128 // size
    for which, target in enumerate(targets):
        for place in range(target.shape[1] // 128):
            pieces = []
            for part in range(per_row):
                device = place * per_row + part
                plane, uly = device // links.n_uly, device % links.n_uly
                gains = all_gains[plane // links.n_blk, plane % links.n_blk, uly]
                pieces.append(gains.astype(jnp.float32)[which : which + 1, :size])
            target[:, place * 128 : (place + 1) * 128] = jnp.concatenate(pieces, axis=1)


def front_kernel(
    toks,
    gain_rows,
    span_order,
    hidden,
    wq,
    wk,
    wv,
    wo,
    gains,
    all_hidden,
    w_qkv,
    all_wo,
    attn_gain,
    mlp_gain,
    cosine,
    sine,
    query_pos,
    key_pos,
    all_gains,
    send,
    recv,
    here,
):
    links = Links(send, recv, here)
    links.greet(links.peers() + [links.x_way, links.y_way, links.core_way])
    q_width, k_width = wq.shape[1] // links.n_blk, wk.shape[1] // links.n_blk
    chunk = w_qkv.at[links.dp, :, links.uly]
    swap = ColumnSwap(
        links, [(wq, chunk, 0), (wk, chunk, q_width), (wv, chunk, q_width + k_width)]
    )
    plane_wo = PlaneGather(links, rows_of(all_wo, False))
    plane_qkv = PlaneGather(links, rows_of(w_qkv, True))
    plane_gain = PlaneGather(links, rows_of(all_gains, True))
    swap.start()
    my_gains = all_gains.at[links.dp, links.blk, links.uly]
    gain_swap = [links.to(gains, my_gains, device) for device in links.peers()]
    plane_wo.start(wo)
    line = HalvedLine(links, hidden, all_hidden)
    line.send(0)
    keep = [
        links.local(gains, my_gains),
        links.local(hidden, all_hidden.at[links.blk]),
        links.local(wo, all_wo.at[links.dp, links.uly]),
    ]
    write_positions(links, span_order, toks, cosine, sine, query_pos, key_pos)
    swap.arrived()
    plane_qkv.start()
    keep[0].wait()
    for copy in gain_swap:
        copy.arrived()
    plane_gain.start()
    plane_wo.hand_on()
    line.advance(1)
    plane_qkv.hand_on()
    plane_gain.hand_on()
    plane_wo.last()
    for step in range(2, links.n_blk - 1):
        line.advance(step)
    plane_qkv.last()
    plane_gain.last()
    plane_gain.arrived()
    write_gains(links, all_gains, gain_rows, (attn_gain, mlp_gain))
    line.arrived()
    for plane in (plane_wo, plane_qkv):
        plane.arrived()
    for copy in keep[1:]:
        copy.wait()
    links.finish()


SMEM = pl.BlockSpec(memory_space=pltpu.SMEM)


def gather_front(span_order, hidden, wq, wk, wv, wo, gains, toks, gain_rows):
    n_dp, n_blk, n_uly = (lax.axis_size(a) for a in EVERY)
    width = hidden.shape[1]
    group = QUERY_HEADS // KEY_VALUE_HEADS
    low = [
        (n_blk,) + hidden.shape,
        (n_dp, n_blk, n_uly, wq.shape[0], (wq.shape[1] + wk.shape[1] + wv.shape[1]) // n_blk),
        (n_dp, n_uly) + wo.shape,
    ]
    f32, i32 = jnp.float32, jnp.int32
    small = [
        ((1, width), f32),
        ((1, width), f32),
        ((n_blk * toks, HEAD_SIZE), f32),
        ((n_blk * toks, HEAD_SIZE), f32),
        ((1, group * n_blk * toks), i32),
        ((n_uly * n_blk * toks, 1), i32),
    ]
    return pl.pallas_call(
        functools.partial(front_kernel, toks, gain_rows),
        out_shape=[jax.ShapeDtypeStruct(shape, jnp.bfloat16) for shape in low]
        + [jax.ShapeDtypeStruct(shape, kind) for shape, kind in small],
        in_specs=[SMEM] + [HBM] * 6,
        out_specs=[HBM] * 3 + [VMEM] * 6,
        scratch_shapes=[pltpu.VMEM((n_dp, n_blk, n_uly) + gains.shape, jnp.bfloat16)]
        + semaphores(72),
        compiler_params=kernel_params(0),
    )(span_order, hidden, wq, wk, wv, wo, gains)


ROWS = 32


def each_block(count, body):
    def step(index, carry):
        body(pl.ds(pl.multiple_of(index * ROWS, ROWS), ROWS))
        return carry

    lax.fori_loop(0, count // ROWS, step, 0)


class LineScatter:
    def __init__(self, links, parts, rightward, leftward):
        self.links, self.parts = links, parts
        self.slots = {1: rightward, -1: leftward}
        self.tokens = parts.shape[1]
        self.number = links.used
        self.last = links.n_blk - 1
        links.used += 2 * self.last

    def target(self, step, way):
        return self.last - step if way == 1 else step

    def slot(self, step, way):
        target = self.target(step, way)
        return self.slots[way].at[target - 1 if way == 1 else target]

    def place(self, way):
        return self.links.blk if way == 1 else self.last - self.links.blk

    def copy(self, step, way, source=None):
        links, slot = self.links, self.slot(step, way)
        number = self.number + 2 * step + (1 if way == 1 else 0)
        return pltpu.make_async_remote_copy(
            src_ref=slot if source is None else source,
            dst_ref=slot,
            send_sem=links.send.at[number],
            recv_sem=links.recv.at[number],
            device_id=(links.dp, links.blk + way, links.uly),
            device_id_type=MESH,
        )

    def start(self):
        for step in range(self.last):
            for way in (1, -1):

                @pl.when(self.place(way) == 0)
                def _(step=step, way=way):
                    self.copy(step, way, self.parts.at[self.target(step, way)]).start()

    def tick(self, tick):
        for way in (1, -1):

            @pl.when(jnp.logical_and(self.place(way) >= 1, self.place(way) <= tick))
            def _(way=way):
                step = tick - self.place(way)
                self.copy(step, way).wait_recv()
                slot, target = self.slot(step, way), self.target(step, way)

                def body(rows):
                    slot[rows, :] = slot[rows, :] + self.parts[target, rows, :]

                each_block(self.tokens, body)
                self.copy(step, way).start()

    def finish(self, total):
        blk, last = self.links.blk, self.last

        def start(rows):
            total[rows, :] = self.parts[blk, rows, :].astype(jnp.float32)

        each_block(self.tokens, start)
        for way in (1, -1):

            @pl.when(self.place(way) >= 1)
            def _(way=way):
                step = last - self.place(way)
                self.copy(step, way).wait_recv()
                slot = self.slot(step, way)

                def body(rows):
                    total[rows, :] = total[rows, :] + slot[rows, :].astype(jnp.float32)

                each_block(self.tokens, body)

    def sent(self):
        for step in range(self.last):
            for way in (1, -1):
                beyond = self.place(way) + step < self.last
                pl.when(beyond)(lambda step=step, way=way: self.copy(step, way).wait_send())


def halved_sums(links, parts, rightward, leftward):
    return [
        LineScatter(links, parts.at[:, rows], rightward.at[:, rows], leftward.at[:, rows])
        for rows in halves(parts.shape[1])
    ]


class OutputHalf:
    def __init__(self, links, which, parts, middle, rightward, leftward, total):
        rows = halves(middle.shape[0])[which]
        self.middle, self.total = middle.at[rows], total
        self.sum = LineScatter(links, parts.at[:, rows], rightward, leftward)

    def write(self, output):
        self.sum.finish(self.total)

        def body(rows):
            output[rows, :] = (self.middle[rows, :] + self.total[rows, :]).astype(jnp.bfloat16)

        each_block(self.middle.shape[0], body)


def output_scratch(n_blk, tokens, width):
    return line_scratch(n_blk, tokens // 2, width) + [
        pltpu.VMEM((tokens // 2, width), jnp.float32)
    ]


def line_scratch(n_blk, tokens, width):
    return [pltpu.VMEM((n_blk - 1, tokens, width), jnp.bfloat16)] * 2


class PlaneScatter:
    def __init__(self, links, parts, from_core, from_x, from_y, last_x, last_y):
        self.links, self.parts = links, parts
        self.own_core_only = from_core is None
        self.from_core, self.from_x, self.from_y = from_core, from_x, from_y
        self.last_x, self.last_y = last_x, last_y
        self.core = lax.rem(links.uly, 2)
        self.row = lax.div(links.uly, 2)
        self.depth = parts.shape[3]
        self.core_copies = {}

    def chunk(self, dp, row, core, half=None):
        if self.own_core_only:
            part = self.parts.at[dp, row]
        else:
            part = self.parts.at[dp, :, row * 2 + core]
        if half is None:
            return part
        depth = self.depth // 2
        return part.at[:, pl.ds(half * depth, depth)]

    def add(self, target, source):
        blocks, depth, _ = target.shape
        rows = 32 if depth % 32 == 0 else 16

        def body(index, carry):
            block = lax.div(index, depth // rows)
            at = pl.ds(pl.multiple_of(lax.rem(index, depth // rows) * rows, rows), rows)
            target[block, at, :] = target[block, at, :] + source[block, at, :]
            return carry

        lax.fori_loop(0, blocks * (depth // rows), body, 0)

    def between_cores(self, which):
        links = self.links
        dp = links.dp if which == 1 else links.other_dp
        self.core_copies[which] = [
            links.to(
                self.chunk(dp, row, 1 - self.core), self.from_core.at[which, row], links.core_way
            )
            for row in range(2)
        ]

    def core_sums(self, which):
        links = self.links
        dp = links.dp if which == 1 else links.other_dp
        for row in range(2):
            self.core_copies[which][row].arrived()
            self.add(self.chunk(dp, row, self.core), self.from_core.at[which, row])

    def across_chips(self):
        links = self.links
        if not self.own_core_only:
            self.core_sums(0)
        self.x_copies = [
            links.to(
                self.chunk(links.other_dp, row, self.core, 0), self.from_x.at[row], links.x_way
            )
            for row in range(2)
        ]
        if not self.own_core_only:
            self.core_sums(1)
        self.y_copies = [
            links.to(
                self.chunk(group, 1 - self.row, self.core, 1),
                self.from_y.at[group],
                links.y_way,
            )
            for group in range(links.n_dp)
        ]

    def second_way(self):
        links = self.links
        for row in range(2):
            self.x_copies[row].arrived()
            self.add(self.chunk(links.dp, row, self.core, 0), self.from_x.at[row])
        self.y_last = links.to(
            self.chunk(links.dp, 1 - self.row, self.core, 0), self.last_y, links.y_way
        )
        for group in range(links.n_dp):
            self.y_copies[group].arrived()
            self.add(self.chunk(group, self.row, self.core, 1), self.from_y.at[group])
        self.x_last = links.to(
            self.chunk(links.other_dp, self.row, self.core, 1), self.last_x, links.x_way
        )

    def result(self, write):
        links = self.links
        for half, copy, source in ((0, self.y_last, self.last_y), (1, self.x_last, self.last_x)):
            copy.arrived()
            own = self.chunk(links.dp, self.row, self.core, half)
            blocks, depth, _ = source.shape
            rows = 32 if depth % 32 == 0 else 16

            def body(index, carry, own=own, source=source, half=half, depth=depth, rows=rows):
                block = lax.div(index, depth // rows)
                start = pl.multiple_of(lax.rem(index, depth // rows) * rows, rows)
                at = pl.ds(start, rows)
                value = own[block, at, :].astype(jnp.float32)
                value = value + source[block, at, :].astype(jnp.float32)
                write(block, pl.ds(pl.multiple_of(start + half * depth, rows), rows), value)
                return carry

            lax.fori_loop(0, blocks * (depth // rows), body, 0)


def plane_shapes(n_dp, blocks, n_uly, depth, width):
    return [
        (n_dp, blocks, n_uly, depth, width),
        (n_dp, 2, blocks, depth, width),
        (2, blocks, depth // 2, width),
        (n_dp, blocks, depth // 2, width),
        (blocks, depth // 2, width),
        (blocks, depth // 2, width),
    ]


def plane_scratch(*sizes):
    return [pltpu.VMEM(shape, jnp.bfloat16) for shape in plane_shapes(*sizes)]


def weight_grad(rows, right, parts, dp):
    _, blocks, n_uly, depth, width = parts.shape
    columns = 512

    def body(index, carry):
        at = pl.ds(pl.multiple_of(index * columns, columns), columns)
        part = jnp.dot(rows[...], right[:, at], preferred_element_type=jnp.float32)
        parts[dp, :, :, :, at] = part.astype(jnp.bfloat16).reshape(blocks, n_uly, depth, columns)
        return carry

    lax.fori_loop(0, width // columns, body, 0)


def rows_turned(left, parts, dp):
    count = parts.shape[1] * parts.shape[2] * parts.shape[3]
    return left[:, pl.ds(pl.multiple_of(dp * count, 128), count)].T


def turned(rows, cosine, sine):
    return rows * cosine + pltpu.roll(rows, HEAD_SIZE // 2, axis=1) * sine


def transposed_product(left, right):
    return lax.dot_general(
        left, right, (((0,), (0,)), ((), ())), preferred_element_type=jnp.float32
    )


def product_right(left, right):
    return lax.dot_general(
        left, right, (((1,), (1,)), ((), ())), preferred_element_type=jnp.float32
    )


SCORE_SCALE = 1.0 / math.sqrt(HEAD_SIZE)


def mask_scores(bias, query_pos, key_pos):
    size = bias.shape[0] // 4

    def body(index, carry):
        rows = pl.ds(pl.multiple_of(index * size, size), size)
        bias[rows, :] = jnp.where(query_pos[...] >= key_pos[rows, :], 0.0, -1e30)
        return carry

    lax.fori_loop(0, 4, body, 0)


class RowBlocks:
    def __init__(self, n_blk, seqs, toks):
        self.n_blk, self.seqs, self.toks = n_blk, seqs, toks

    def each(self, body):
        def step(index, carry):
            blk, seq = lax.div(index, self.seqs), lax.rem(index, self.seqs)
            body(
                seq,
                pl.ds(pl.multiple_of(index * self.toks, self.toks), self.toks),
                pl.multiple_of(blk * self.toks, self.toks),
            )
            return carry

        lax.fori_loop(0, self.n_blk * self.seqs, step, 0)


def attention_kernel(
    wg,
    wu,
    cotangent,
    hidden,
    w_qkv,
    gain,
    q_gain,
    k_gain,
    cosine,
    sine,
    query_pos,
    key_pos,
    rows_wg,
    rows_wu,
    all_cot,
    heads,
    normed,
    qkv,
    queries,
    key_values,
    lse,
    bias,
    send,
    recv,
    here,
):
    links = Links(send, recv, here)
    links.greet(links.peers() + [links.y_way, links.core_way])
    swap = ColumnSwap(links, [(wg, rows_wg, 0), (wu, rows_wu, 0)])
    swap.start()
    line = HalvedLine(links, cotangent, all_cot)
    line.send(0)
    keep = links.local(cotangent, all_cot.at[links.blk])

    def norm(rows):
        source = hidden[rows, :].astype(jnp.float32)
        normed[rows, :] = (source * rms_scale(source) * gain[...]).astype(jnp.bfloat16)

    each_block(hidden.shape[0], norm)
    for column in range(0, qkv.shape[1], 256):
        qkv[:, column : column + 256] = jnp.dot(
            normed[...], w_qkv[:, column : column + 256], preferred_element_type=jnp.float32
        )
    seqs, kv_heads, q_rows, _ = queries.shape
    q_len = key_values.shape[4]
    group = q_rows // q_len
    blocks = RowBlocks(links.n_blk, seqs, q_len // links.n_blk)
    q_end = kv_heads * group * HEAD_SIZE
    k_end = q_end + kv_heads * HEAD_SIZE

    def place_keys(seq, rows, start):
        at = pl.ds(start, blocks.toks)
        for head in range(kv_heads):
            k_pre = qkv[rows, q_end + head * HEAD_SIZE : q_end + (head + 1) * HEAD_SIZE]
            k_row = turned(k_pre * rms_scale(k_pre) * k_gain[...].astype(jnp.float32), cosine[at, :], sine[at, :])
            v_row = qkv[rows, k_end + head * HEAD_SIZE : k_end + (head + 1) * HEAD_SIZE]
            key_values[links.uly, 0, seq, head, at, :] = k_row.astype(jnp.bfloat16)
            key_values[links.uly, 1, seq, head, at, :] = v_row.astype(jnp.bfloat16)

    blocks.each(place_keys)
    mine = key_values.at[links.uly]
    kv_core = links.to(mine, mine, links.core_way)
    kv_across = links.to(mine, mine, links.y_way)

    def place_queries(seq, rows, start):
        at = pl.ds(start, blocks.toks)
        for head in range(kv_heads * group):
            q_pre = qkv[rows, head * HEAD_SIZE : (head + 1) * HEAD_SIZE]
            q_row = turned(q_pre * rms_scale(q_pre) * q_gain[...].astype(jnp.float32), cosine[at, :], sine[at, :])
            to = pl.ds((head % group) * q_len + start, blocks.toks)
            queries[seq, head // group, to, :] = q_row.astype(jnp.bfloat16)

    blocks.each(place_queries)
    mask_scores(bias, query_pos, key_pos)
    kv_across.arrived()
    theirs = key_values.at[links.across]
    kv_last = links.to(theirs, theirs, links.core_way)
    kv_core.arrived()
    kv_last.arrived()

    def attend(seq, head):
        def over_keys(piece, carry):
            total, mixed = carry
            rows = pl.ds(pl.multiple_of(piece * q_len, q_len), q_len)
            scores = product_right(key_values[piece, 0, seq, head], queries[seq, head])
            weights = jnp.exp(scores * SCORE_SCALE + bias[rows, :])
            total = total + jnp.sum(weights, axis=0, keepdims=True)
            mixed = mixed + transposed_product(
                key_values[piece, 1, seq, head], weights.astype(jnp.bfloat16)
            )
            return total, mixed

        total, mixed = lax.fori_loop(
            0,
            links.n_uly,
            over_keys,
            (
                jnp.zeros((1, q_rows), jnp.float32),
                jnp.zeros((HEAD_SIZE, q_rows), jnp.float32),
            ),
        )
        lse[seq * kv_heads + head] = jnp.log(total)
        attended = (mixed / total).T.astype(jnp.bfloat16)
        for member in range(group):
            column = (head * group + member) * HEAD_SIZE
            for blk in range(links.n_blk):
                row = (blk * seqs + seq) * blocks.toks
                start = member * q_len + blk * blocks.toks
                heads[row : row + blocks.toks, column : column + HEAD_SIZE] = attended[
                    start : start + blocks.toks, :
                ]

    for seq in range(seqs):
        for head in range(kv_heads):
            attend(seq, head)
    swap.arrived()
    line.arrived()
    keep.wait()
    links.finish()


def attend_forward(
    wg, wu, cotangent, hidden, w_qkv, gain, q_gain, k_gain, cosine, sine, query_pos, key_pos, seqs
):
    _, n_blk, n_uly = (lax.axis_size(a) for a in EVERY)
    rows = hidden.shape[0]
    kv_heads = KEY_VALUE_HEADS // n_blk
    q_len, q_rows = rows // seqs, query_pos.shape[1]
    low = [
        (n_blk, wg.shape[0], wg.shape[1] // n_blk),
        (n_blk, wu.shape[0], wu.shape[1] // n_blk),
        (n_blk,) + cotangent.shape,
        (rows, QUERY_HEADS // n_blk * HEAD_SIZE),
        hidden.shape,
    ]
    shapes = [jax.ShapeDtypeStruct(s, jnp.bfloat16) for s in low] + [
        jax.ShapeDtypeStruct((rows, w_qkv.shape[1]), jnp.float32),
        jax.ShapeDtypeStruct((seqs, kv_heads, q_rows, HEAD_SIZE), jnp.bfloat16),
        jax.ShapeDtypeStruct((n_uly, 2, seqs, kv_heads, q_len, HEAD_SIZE), jnp.bfloat16),
        jax.ShapeDtypeStruct((seqs * kv_heads, 1, q_rows), jnp.float32),
    ]
    return pl.pallas_call(
        attention_kernel,
        out_shape=shapes,
        in_specs=[HBM] * 3 + [VMEM] * 9,
        out_specs=[HBM] * 3 + [VMEM] * 6,
        scratch_shapes=[pltpu.VMEM((key_pos.shape[0], q_rows), jnp.float32)] + semaphores(32),
        compiler_params=kernel_params(1),
    )(
        wg,
        wu,
        cotangent,
        hidden,
        w_qkv,
        gain,
        q_gain,
        k_gain,
        cosine,
        sine,
        query_pos,
        key_pos,
    )


def attention_back_kernel(
    all_low,
    wo,
    queries,
    key_values,
    lse,
    qkv,
    q_gain,
    k_gain,
    cosine,
    sine,
    query_pos,
    key_pos,
    grad_gate,
    grad_up,
    part_down,
    grad_qkv,
    gain_terms,
    grad_down,
    gate_rows,
    up_rows,
    bias,
    grad_heads,
    grad_rows,
    probs,
    grad_probs,
    grad_kv,
    from_core,
    from_across,
    down_1,
    down_3,
    down_4,
    down_5,
    down_6,
    send,
    recv,
    here,
):
    links = Links(send, recv, here)
    links.greet(links.peers() + [links.x_way, links.y_way, links.core_way])
    down = PlaneScatter(links, down_1, None, down_3, down_4, down_5, down_6)
    links.local(part_down, down_1).wait()
    down.across_chips()
    swapped, keep = [], []
    for source, target in ((grad_gate, gate_rows), (grad_up, up_rows)):
        for step in range(1, links.n_blk):
            peer = links.peer(step)
            swapped.append(
                links.to(source.at[peer], target.at[links.blk], (links.dp, peer, links.uly))
            )
        keep.append(links.local(source.at[links.blk], target.at[links.blk]))
    grad_heads[...] = product_right(all_low[...], wo[...])
    mask_scores(bias, query_pos, key_pos)
    seqs, kv_heads, q_rows, _ = queries.shape
    q_len = key_values.shape[4]
    group = q_rows // q_len
    blocks = RowBlocks(links.n_blk, seqs, q_len // links.n_blk)
    q_end = kv_heads * group * HEAD_SIZE
    k_end = q_end + kv_heads * HEAD_SIZE
    gain_terms[...] = jnp.zeros_like(gain_terms)

    def gather_rows(seq, rows, start):
        for head in range(kv_heads * group):
            to = pl.ds((head % group) * q_len + start, blocks.toks)
            grad_rows[seq, head // group, to, :] = grad_heads[
                rows, head * HEAD_SIZE : (head + 1) * HEAD_SIZE
            ].astype(jnp.bfloat16)

    blocks.each(gather_rows)

    def back_norm(upstream, pre, gain, at, which):
        upstream = turned(upstream, cosine[at, :], -sine[at, :])
        gain_terms[which : which + 1, :] += jnp.sum(
            upstream * pre * rms_scale(pre), axis=0, keepdims=True
        )
        return back_rows(upstream, pre, gain[...].astype(jnp.float32)).astype(jnp.bfloat16)

    def back(seq, head):
        def first(piece, delta):
            rows = pl.ds(pl.multiple_of(piece * q_len, q_len), q_len)
            scores = product_right(key_values[piece, 0, seq, head], queries[seq, head])
            prob = jnp.exp(
                scores * SCORE_SCALE + bias[rows, :] - lse[seq * kv_heads + head]
            )
            grad_prob = product_right(key_values[piece, 1, seq, head], grad_rows[seq, head])
            probs[rows, :] = prob
            grad_probs[rows, :] = grad_prob
            return delta + jnp.sum(prob * grad_prob, axis=0, keepdims=True)

        delta = lax.fori_loop(0, links.n_uly, first, jnp.zeros((1, q_rows), jnp.float32))

        def second(piece, grad_query):
            rows = pl.ds(pl.multiple_of(piece * q_len, q_len), q_len)
            prob = probs[rows, :]
            grad_score = (prob * (grad_probs[rows, :] - delta)).astype(jnp.bfloat16)
            grad_kv[seq, piece, 0, head] = (
                SCORE_SCALE
                * jnp.dot(grad_score, queries[seq, head], preferred_element_type=jnp.float32)
            ).astype(jnp.bfloat16)
            grad_kv[seq, piece, 1, head] = jnp.dot(
                prob.astype(jnp.bfloat16),
                grad_rows[seq, head],
                preferred_element_type=jnp.float32,
            ).astype(jnp.bfloat16)
            return grad_query + transposed_product(key_values[piece, 0, seq, head], grad_score)

        grad_query = lax.fori_loop(
            0, links.n_uly, second, jnp.zeros((HEAD_SIZE, q_rows), jnp.float32)
        )
        grad_heads[:, :HEAD_SIZE] = (grad_query * SCORE_SCALE).T
        for member in range(group):
            column = (head * group + member) * HEAD_SIZE
            for blk in range(links.n_blk):
                row = (blk * seqs + seq) * blocks.toks
                at = pl.ds(blk * blocks.toks, blocks.toks)
                start = member * q_len + blk * blocks.toks
                grad_qkv[row : row + blocks.toks, column : column + HEAD_SIZE] = back_norm(
                    grad_heads[start : start + blocks.toks, :HEAD_SIZE],
                    qkv[row : row + blocks.toks, column : column + HEAD_SIZE],
                    q_gain,
                    at,
                    0,
                )

    core, line = lax.rem(links.uly, 2), lax.div(links.uly, 2)

    def add(target, source):
        for kind in range(2):
            for head in range(kv_heads):
                target[kind, head] = target[kind, head] + source[kind, head]

    def core_sums(seq):
        copies = [
            links.to(
                grad_kv.at[seq, row * 2 + 1 - core], from_core.at[seq, row], links.core_way
            )
            for row in range(2)
        ]
        return copies

    def across_sums(seq, copies):
        for row in range(2):
            copies[row].arrived()
            add(grad_kv.at[seq, row * 2 + core], from_core.at[seq, row])
        return links.to(
            grad_kv.at[seq, (1 - line) * 2 + core], from_across.at[seq], links.y_way
        )

    def own_keys(seq, copy):
        copy.arrived()
        for head in range(kv_heads):
            for blk in range(links.n_blk):
                row = (blk * seqs + seq) * blocks.toks
                at = pl.ds(blk * blocks.toks, blocks.toks)
                term = [
                    grad_kv[seq, links.uly, kind, head, at, :].astype(jnp.float32)
                    + from_across[seq, kind, head, at, :].astype(jnp.float32)
                    for kind in range(2)
                ]
                k_at = q_end + head * HEAD_SIZE
                v_at = k_end + head * HEAD_SIZE
                grad_qkv[row : row + blocks.toks, k_at : k_at + HEAD_SIZE] = back_norm(
                    term[0],
                    qkv[row : row + blocks.toks, k_at : k_at + HEAD_SIZE],
                    k_gain,
                    at,
                    1,
                )
                grad_qkv[row : row + blocks.toks, v_at : v_at + HEAD_SIZE] = term[1].astype(
                    jnp.bfloat16
                )

    stage, last = None, []
    for seq in range(seqs):
        for head in range(kv_heads):
            back(seq, head)
            if seq == 0 and head == kv_heads - 1:
                down.second_way()
            if stage is not None:
                last.append((seq - 1, across_sums(seq - 1, stage)))
                stage = None
        stage = core_sums(seq)
    last.append((seqs - 1, across_sums(seqs - 1, stage)))
    for seq, copy in last:
        own_keys(seq, copy)

    def write(block, rows, values):
        grad_down[block, rows, :] = values

    down.result(write)
    for copy in keep:
        copy.wait()
    for copy in swapped:
        copy.arrived()
    links.finish()


def attend_back(
    all_low,
    wo,
    queries,
    key_values,
    lse,
    qkv,
    q_gain,
    k_gain,
    cosine,
    sine,
    query_pos,
    key_pos,
    grad_gate,
    grad_up,
    part_down,
):
    seqs, kv_heads, q_rows, _ = queries.shape
    n_uly, _, _, _, q_len, _ = key_values.shape
    rows = all_low.shape[0]
    keys = key_pos.shape[0]
    f32, low = jnp.float32, jnp.bfloat16
    scratch = [
        ((keys, q_rows), f32),
        ((rows, wo.shape[0]), f32),
        (queries.shape, low),
        ((keys, q_rows), f32),
        ((keys, q_rows), f32),
        ((seqs, n_uly, 2, kv_heads, q_len, HEAD_SIZE), low),
        ((seqs, 2, 2, kv_heads, q_len, HEAD_SIZE), low),
        ((seqs, 2, kv_heads, q_len, HEAD_SIZE), low),
        (part_down.shape, low),
    ]
    n_dp, _, _, depth, width = part_down.shape
    scratch += [(shape, low) for shape in plane_shapes(n_dp, 1, n_uly, depth, width)[2:]]
    return pl.pallas_call(
        attention_back_kernel,
        out_shape=[
            jax.ShapeDtypeStruct(qkv.shape, low),
            jax.ShapeDtypeStruct((8, HEAD_SIZE), f32),
            jax.ShapeDtypeStruct((1, depth, width), f32),
            jax.ShapeDtypeStruct(grad_gate.shape, low),
            jax.ShapeDtypeStruct(grad_up.shape, low),
        ],
        in_specs=[VMEM] * 12 + [HBM] * 3,
        out_specs=[VMEM] * 3 + [HBM] * 2,
        scratch_shapes=[pltpu.VMEM(shape, kind) for shape, kind in scratch]
        + semaphores(40),
        compiler_params=kernel_params(5),
    )(
        all_low,
        wo,
        queries,
        key_values,
        lse,
        qkv,
        q_gain,
        k_gain,
        cosine,
        sine,
        query_pos,
        key_pos,
        grad_gate,
        grad_up,
        part_down,
    )


def middle_kernel(
    heads,
    wo,
    source,
    gain,
    rows_wg,
    rows_wu,
    _,
    middle,
    all_normed,
    all_wg,
    all_wu,
    all_cot,
    parts,
    rightward,
    leftward,
    normed,
    send,
    recv,
    here,
):
    links = Links(send, recv, here)
    links.greet(links.peers() + [links.x_way, links.y_way, links.core_way])
    tokens = source.shape[0]
    for blk in (links.n_blk - 1, 0) + tuple(range(1, links.n_blk - 1)):
        parts[blk] = jnp.dot(heads[blk], wo[...], preferred_element_type=jnp.float32).astype(
            jnp.bfloat16
        )
    sums = halved_sums(links, parts, rightward, leftward)
    for half in sums:
        half.start()
    planes, keep = [], []
    for chunk, whole in ((rows_wg, all_wg), (rows_wu, all_wu)):
        at = rows_of(whole, True)
        plane = PlaneGather(links, at)
        plane.start(chunk)
        planes.append(plane)
        keep.append(links.local(chunk, at(links.dp, links.uly)))
    cot_lines = HalvedLine(links, None, all_cot).lines
    cot_lines[0].send(1)
    lines = []

    def settle(half, rows_of_half):
        half.finish(middle.at[rows_of_half])

        def body(rows):
            at = pl.ds(pl.multiple_of(rows_of_half.start + rows.start, ROWS), ROWS)
            total = middle[at, :] + source[at, :].astype(jnp.float32)
            middle[at, :] = total
            normed[at, :] = (total * rms_scale(total) * gain[...]).astype(jnp.bfloat16)

        each_block(tokens // 2, body)
        line = LineGather(links, normed.at[rows_of_half], all_normed.at[:, rows_of_half])
        line.send(0)
        lines.append(line)

    spans = halves(tokens)
    for tick in range(1, links.n_blk - 1):
        sums[0].tick(tick)
        if tick == 1:
            cot_lines[1].send(1)
    settle(sums[0], spans[0])
    planes[0].hand_on()
    for tick in range(1, links.n_blk - 1):
        sums[1].tick(tick)
        for line in cot_lines:
            line.arrived()
            if tick + 1 < links.n_blk - 1:
                line.send(tick + 1)
    settle(sums[1], spans[1])
    keep.append(links.local(normed, all_normed.at[links.blk]))
    for step in range(1, links.n_blk - 1):
        for line in lines:
            line.arrived()
            line.send(step)
        if step == 1:
            planes[1].hand_on()
        if step == 2:
            planes[0].last()
    planes[1].last()
    for line in lines:
        line.arrived()
    for plane in planes:
        plane.arrived()
    for copy in keep:
        copy.wait()
    for half in sums:
        half.sent()
    links.finish()


def exchange_middle(heads, wo, source, gain, rows_wg, rows_wu, all_cot):
    n_dp, n_blk, n_uly = (lax.axis_size(a) for a in EVERY)
    tokens, width = source.shape
    low = [(n_blk, tokens, width)]
    low += [(n_dp, n_blk, n_uly) + chunk.shape[1:] for chunk in (rows_wg, rows_wu)]
    low.append(all_cot.shape)
    return pl.pallas_call(
        middle_kernel,
        out_shape=[jax.ShapeDtypeStruct((tokens, width), jnp.float32)]
        + [jax.ShapeDtypeStruct(shape, jnp.bfloat16) for shape in low],
        in_specs=[VMEM] * 4 + [HBM] * 3,
        out_specs=[VMEM] + [HBM] * 4,
        input_output_aliases={6: 4},
        scratch_shapes=[pltpu.VMEM((n_blk, tokens, width), jnp.bfloat16)]
        + line_scratch(n_blk, tokens, width)
        + [pltpu.VMEM((tokens, width), jnp.bfloat16)]
        + semaphores(64),
        compiler_params=kernel_params(2),
    )(heads, wo, source, gain, rows_wg, rows_wu, all_cot)


def back_rows(grad_normed, source, gain):
    unit = source * rms_scale(source)
    scaled = grad_normed * gain
    return rms_scale(source) * (
        scaled - unit * jnp.mean(scaled * unit, axis=-1, keepdims=True)
    )


def back_kernel(
    grad_parts,
    out_parts,
    middle,
    cotangent,
    gain,
    all_normed,
    grad_gate_pre,
    grad_up_pre,
    activated,
    all_cot,
    output,
    grad_middle,
    all_low,
    grad_gate,
    grad_up,
    part_down,
    rightward,
    leftward,
    out_right,
    out_left,
    out_total,
    low,
    turned_low,
    gate_1,
    gate_2,
    gate_3,
    gate_4,
    gate_5,
    gate_6,
    up_1,
    up_2,
    up_3,
    up_4,
    up_5,
    up_6,
    down_1,
    down_2,
    send,
    recv,
    here,
):
    links = Links(send, recv, here)
    links.greet(links.peers() + [links.x_way, links.y_way, links.core_way])
    sums = halved_sums(links, grad_parts, rightward, leftward)
    for half in sums:
        half.start()
    out = OutputHalf(links, 0, out_parts, middle, out_right, out_left, out_total)
    gate = PlaneScatter(links, gate_1, gate_2, gate_3, gate_4, gate_5, gate_6)
    up = PlaneScatter(links, up_1, up_2, up_3, up_4, up_5, up_6)
    down = PlaneScatter(links, down_1, down_2, None, None, None, None)
    tokens = middle.shape[0]
    spans, lines, keep = halves(tokens), [], []

    def compute(plane, which, rows, right):
        dp = links.dp if which == 1 else links.other_dp
        weight_grad(rows, right, plane.parts, dp)
        plane.between_cores(which)

    def turn(which):
        dp = links.dp if which == 1 else links.other_dp
        turned_low[which] = rows_turned(all_normed, gate_1, dp)

    def compute_down(which):
        dp = links.dp if which == 1 else links.other_dp
        compute(down, which, rows_turned(activated, down_1, dp), all_cot)

    def settle(half, rows_of_half):
        half.finish(grad_middle.at[rows_of_half])

        def body(rows):
            at = pl.ds(pl.multiple_of(rows_of_half.start + rows.start, ROWS), ROWS)
            back = back_rows(grad_middle[at, :], middle[at, :], gain[...])
            grad = cotangent[at, :].astype(jnp.float32) + back
            grad_middle[at, :] = grad
            low[at, :] = grad.astype(jnp.bfloat16)

        each_block(tokens // 2, body)
        line = LineGather(links, low.at[rows_of_half], all_low.at[:, rows_of_half])
        line.send(0)
        lines.append(line)

    later = range(2, links.n_blk - 1)
    turn(0)
    compute(gate, 0, turned_low.at[0], grad_gate_pre)
    sums[0].tick(1)
    turn(1)
    compute(gate, 1, turned_low.at[1], grad_gate_pre)
    for tick in later:
        sums[0].tick(tick)
    gate.across_chips()
    settle(sums[0], spans[0])
    compute(up, 0, turned_low.at[0], grad_up_pre)
    sums[1].tick(1)
    compute(up, 1, turned_low.at[1], grad_up_pre)
    for tick in later:
        sums[1].tick(tick)
    up.across_chips()
    settle(sums[1], spans[1])
    out.sum.start()
    keep.append(links.local(low, all_low.at[links.blk]))
    compute_down(0)
    for step in range(1, links.n_blk - 1):
        for line in lines:
            line.arrived()
            line.send(step)
        if step == 1:
            gate.second_way()
            compute_down(1)
    out.sum.tick(1)
    up.second_way()
    for which in (0, 1):
        down.core_sums(which)
    for dp in range(links.n_dp):
        for row in range(2):
            keep.append(links.local(down.chunk(dp, row, down.core), part_down.at[dp, row]))
    for tick in later:
        out.sum.tick(tick)
    for line in lines:
        line.arrived()

    def into(target):
        def write(block, rows, values):
            target[block, rows, :] = values.astype(target.dtype)

        return write

    gate.result(into(grad_gate))
    up.result(into(grad_up))
    out.write(output)
    out.sum.sent()
    for copy in keep:
        copy.wait()
    for half in sums:
        half.sent()
    links.finish()


def exchange_back(
    grad_parts,
    out_parts,
    middle,
    cotangent,
    gain,
    all_normed,
    grad_gate_pre,
    grad_up_pre,
    activated,
    all_cot,
):
    n_dp, n_blk, n_uly = (lax.axis_size(a) for a in EVERY)
    _, tokens, width = grad_parts.shape
    ff = grad_gate_pre.shape[1]
    depth = width // (n_dp * n_blk * n_uly)
    down_depth = ff // (n_dp * n_uly)
    return pl.pallas_call(
        back_kernel,
        out_shape=[
            jax.ShapeDtypeStruct((tokens // 2, width), jnp.bfloat16),
            jax.ShapeDtypeStruct((tokens, width), jnp.float32),
            jax.ShapeDtypeStruct((n_blk, tokens, width), jnp.bfloat16),
            jax.ShapeDtypeStruct((n_blk, depth, ff), jnp.bfloat16),
            jax.ShapeDtypeStruct((n_blk, depth, ff), jnp.bfloat16),
            jax.ShapeDtypeStruct((n_dp, 2, 1, down_depth, width), jnp.bfloat16),
        ],
        in_specs=[VMEM] * 10,
        out_specs=[VMEM, VMEM, HBM, VMEM, VMEM, HBM],
        scratch_shapes=line_scratch(n_blk, tokens, width)
        + output_scratch(n_blk, tokens, width)
        + [
            pltpu.VMEM((tokens, width), jnp.bfloat16),
            pltpu.VMEM((n_dp, width // n_dp, n_blk * tokens), jnp.bfloat16),
        ]
        + plane_scratch(n_dp, n_blk, n_uly, depth, ff) * 2
        + plane_scratch(n_dp, 1, n_uly, down_depth, width)[:2]
        + semaphores(72),
        compiler_params=kernel_params(3),
    )(
        grad_parts,
        out_parts,
        middle,
        cotangent,
        gain,
        all_normed,
        grad_gate_pre,
        grad_up_pre,
        activated,
        all_cot,
    )


def last_kernel(
    w_qkv,
    hidden,
    grad_middle,
    gain,
    normed,
    grad_qkv,
    heads,
    all_low,
    head_terms,
    out_parts,
    middle,
    grad_hidden,
    grad_w_qkv,
    grad_wo,
    small_sum,
    output,
    grad_parts,
    rightward,
    leftward,
    qkv_1,
    qkv_2,
    qkv_3,
    qkv_4,
    qkv_5,
    qkv_6,
    wo_1,
    wo_2,
    wo_3,
    wo_4,
    wo_5,
    wo_6,
    summed,
    small_in,
    small_total,
    out_right,
    out_left,
    out_total,
    send,
    recv,
    here,
):
    links = Links(send, recv, here)
    links.greet(links.peers() + [links.x_way, links.y_way, links.core_way])
    sums = halved_sums(links, grad_parts, rightward, leftward)
    qkv = PlaneScatter(links, qkv_1, qkv_2, qkv_3, qkv_4, qkv_5, qkv_6)
    out = PlaneScatter(links, wo_1, wo_2, wo_3, wo_4, wo_5, wo_6)

    output_half = OutputHalf(links, 1, out_parts, middle, out_right, out_left, out_total)
    small_in[links.blk] = head_terms[...]
    small_copies = [
        links.to(head_terms, small_in.at[links.blk], device) for device in links.peers()
    ]

    def compute(plane, which, left, right):
        dp = links.dp if which == 1 else links.other_dp
        weight_grad(rows_turned(left, plane.parts, dp), right, plane.parts, dp)
        plane.between_cores(which)

    output_half.sum.start()
    compute(qkv, 0, normed, grad_qkv)
    for copy in small_copies:
        copy.arrived()
    total = small_in[0]
    for blk in range(1, links.n_blk):
        total = total + small_in[blk]
    small_total[0] = total
    pending = links.to(small_total.at[0], small_in.at[links.n_blk], links.x_way)
    compute(qkv, 1, normed, grad_qkv)
    output_half.sum.tick(1)
    pending.arrived()
    small_total[1] = small_total[0] + small_in[links.n_blk]
    pending = links.to(small_total.at[1], small_in.at[links.n_blk + 1], links.y_way)
    tokens = grad_parts.shape[1]
    for column in range(0, w_qkv.shape[0], 512):
        grad_parts[:, :, column : column + 512] = (
            product_right(grad_qkv[...], w_qkv[column : column + 512, :])
            .astype(jnp.bfloat16)
            .reshape(links.n_blk, tokens, 512)
        )
    for half in sums:
        half.start()
    pending.arrived()
    small_total[2] = small_total[1] + small_in[links.n_blk + 1]
    pending = links.to(small_total.at[2], small_in.at[links.n_blk + 2], links.core_way)
    qkv.across_chips()
    for tick in range(2, links.n_blk - 1):
        output_half.sum.tick(tick)
    pending.arrived()
    small_sum[...] = small_total[2] + small_in[links.n_blk + 2]
    sums[0].tick(1)
    compute(out, 0, heads, all_low)
    for tick in range(2, links.n_blk - 1):
        sums[0].tick(tick)
    compute(out, 1, heads, all_low)
    qkv.second_way()
    out.across_chips()
    output_half.write(output)

    def write(block, rows, values):
        summed[block, rows, :] = values.astype(jnp.bfloat16)

    qkv.result(write)
    swapped = []
    for step in range(1, links.n_blk):
        peer = links.peer(step)
        swapped.append(
            links.to(summed.at[peer], grad_w_qkv.at[links.blk], (links.dp, peer, links.uly))
        )
    keep = links.local(summed.at[links.blk], grad_w_qkv.at[links.blk])
    sums[1].tick(1)
    out.second_way()
    for tick in range(2, links.n_blk - 1):
        sums[1].tick(tick)
    for half, rows_of_half in zip(sums, halves(tokens)):
        half.finish(grad_hidden.at[rows_of_half])

    def body(rows):
        back = back_rows(grad_hidden[rows, :], hidden[rows, :].astype(jnp.float32), gain[...])
        grad_hidden[rows, :] = grad_middle[rows, :] + back

    each_block(tokens, body)

    def write_out(block, rows, values):
        grad_wo[block, rows, :] = values

    out.result(write_out)
    output_half.sum.sent()
    for copy in swapped:
        copy.arrived()
    keep.wait()
    for half in sums:
        half.sent()
    links.finish()


def exchange_last(
    w_qkv,
    hidden,
    grad_middle,
    gain,
    normed,
    grad_qkv,
    heads,
    all_low,
    head_terms,
    out_parts,
    middle,
):
    n_dp, _, n_uly = (lax.axis_size(a) for a in EVERY)
    n_blk, tokens, width = out_parts.shape
    columns = grad_qkv.shape[1]
    depth = width // (n_dp * n_blk * n_uly)
    out_depth = heads.shape[1] // (n_dp * n_uly)
    small = head_terms.shape
    return pl.pallas_call(
        last_kernel,
        out_shape=[
            jax.ShapeDtypeStruct((tokens, width), jnp.float32),
            jax.ShapeDtypeStruct((n_blk, depth, columns), jnp.bfloat16),
            jax.ShapeDtypeStruct((1, out_depth, width), jnp.float32),
            jax.ShapeDtypeStruct(small, jnp.float32),
            jax.ShapeDtypeStruct((tokens // 2, width), jnp.bfloat16),
        ],
        in_specs=[VMEM] * 11,
        out_specs=[VMEM, HBM, VMEM, VMEM, VMEM],
        scratch_shapes=[pltpu.VMEM((n_blk, tokens, width), jnp.bfloat16)]
        + line_scratch(n_blk, tokens, width)
        + plane_scratch(n_dp, n_blk, n_uly, depth, columns)
        + plane_scratch(n_dp, 1, n_uly, out_depth, width)
        + [
            pltpu.VMEM((n_blk, depth, columns), jnp.bfloat16),
            pltpu.VMEM((n_blk + 3,) + small, jnp.float32),
            pltpu.VMEM((3,) + small, jnp.float32),
        ]
        + output_scratch(n_blk, tokens, width)
        + semaphores(64),
        compiler_params=kernel_params(4),
    )(
        w_qkv,
        hidden,
        grad_middle,
        gain,
        normed,
        grad_qkv,
        heads,
        all_low,
        head_terms,
        out_parts,
        middle,
    )


def finish_kernel(
    gate,
    up,
    qkv,
    wo,
    wd,
    hidden,
    out_0,
    out_1,
    w_gate,
    w_up,
    w_query,
    key_weight,
    value_weight,
    attn_gain,
    mlp_gain,
    small,
    f_gate,
    f_up,
    f_q,
    f_k,
    f_v,
    f_wo,
    f_wd,
    f_hidden,
    f_out,
    f_attn,
    f_mlp,
    f_q_gain,
    f_k_gain,
):
    n_blk, depth, _ = gate.shape

    def place(source, offset, target):
        width = target.shape[1] // (n_blk * 2)
        for blk in range(n_blk):
            for group in range(2):
                to = (group * n_blk + blk) * width
                at = offset + group * width
                target[:, to : to + width] = source[blk, :, at : at + width].astype(jnp.float32)

    def gain_back(pairs, gain):
        total = jnp.zeros((depth, 128), jnp.float32)
        for weight, grad in pairs:
            for column in range(0, weight.shape[1], 128):
                at = slice(column, column + 128)
                total = total + weight[:, at].astype(jnp.float32) * grad[:, at]
        column = jnp.sum(total, axis=1, keepdims=True)
        square = (depth, depth)
        same = lax.broadcasted_iota(jnp.int32, square, 0) == lax.broadcasted_iota(
            jnp.int32, square, 1
        )
        return jnp.sum(jnp.where(same, column, 0.0), axis=0, keepdims=True) / gain[
            ...
        ].astype(jnp.float32)

    place(gate, 0, f_gate)
    place(up, 0, f_up)
    q_width = f_q.shape[1] // n_blk
    k_width = f_k.shape[1] // n_blk
    place(qkv, 0, f_q)
    place(qkv, q_width, f_k)
    place(qkv, q_width + k_width, f_v)
    f_q_gain[...] = small[0:1, :]
    f_k_gain[...] = small[1:2, :]
    f_wo[...] = wo[0]
    f_wd[...] = wd[0]
    f_hidden[...] = hidden[...]
    half = out_0.shape[0]
    f_out[:half, :] = out_0[...]
    f_out[half:, :] = out_1[...]
    f_attn[...] = gain_back(((w_query, f_q), (key_weight, f_k), (value_weight, f_v)), attn_gain)
    f_mlp[...] = gain_back(((w_gate, f_gate), (w_up, f_up)), mlp_gain)


def finish(gate, up, qkv, wo, wd, hidden, out_0, out_1, weights, gains, small):
    return pl.pallas_call(
        finish_kernel,
        out_shape=[jax.ShapeDtypeStruct(w.shape, jnp.float32) for w in weights]
        + [
            jax.ShapeDtypeStruct(wo.shape[1:], jnp.float32),
            jax.ShapeDtypeStruct(wd.shape[1:], jnp.float32),
            jax.ShapeDtypeStruct(hidden.shape, jnp.float32),
            jax.ShapeDtypeStruct(hidden.shape, jnp.bfloat16),
        ]
        + [jax.ShapeDtypeStruct(gain.shape, jnp.float32) for gain in gains]
        + [jax.ShapeDtypeStruct((1, small.shape[1]), jnp.float32)] * 2,
        in_specs=[VMEM] * 16,
        out_specs=[VMEM] * 13,
        compiler_params=pltpu.CompilerParams(vmem_limit_bytes=62 * MIB),
    )(gate, up, qkv, wo, wd, hidden, out_0, out_1, *weights, *gains, small)


def product(left, right):
    return jnp.dot(left, right, preferred_element_type=jnp.float32)


def shards(
    hidden,
    span_order,
    attn_gain,
    w_query,
    key_weight,
    value_weight,
    w_out,
    q_gain,
    k_gain,
    mlp_gain,
    w_gate,
    w_up,
    w_down,
    cotangent,
):
    seqs, toks, width = hidden.shape
    n_dp, n_blk, n_uly = (lax.axis_size(a) for a in EVERY)
    rows = n_blk * seqs * toks
    bf16 = jnp.bfloat16
    own_hidden = hidden.reshape(seqs * toks, width)
    own_cotangent = cotangent.reshape(seqs * toks, width)

    gain_q, gain_k = q_gain[None, :], k_gain[None, :]
    all_wd = lax.all_gather(w_down, PLANE, axis=0, tiled=True)

    gain_rows = attn_gain.shape[0]
    own_gains = jnp.pad(jnp.stack([attn_gain, mlp_gain]), ((0, 30), (0, 128 - gain_rows)))
    (
        all_hidden,
        w_qkv,
        wo,
        g_attn,
        g_mlp,
        cosine,
        sine,
        query_pos,
        key_pos,
    ) = gather_front(
        span_order,
        own_hidden,
        w_query,
        key_weight,
        value_weight,
        w_out,
        own_gains,
        toks,
        gain_rows,
    )
    w_qkv = w_qkv.reshape(width, -1)
    wo = wo.reshape(-1, width)
    (
        rows_wg,
        rows_wu,
        cot,
        heads_flat,
        normed,
        qkv,
        queries,
        key_values,
        lse,
    ) = attend_forward(
        w_gate,
        w_up,
        own_cotangent,
        all_hidden.reshape(rows, width),
        w_qkv,
        g_attn,
        gain_q,
        gain_k,
        cosine,
        sine,
        query_pos,
        key_pos,
        seqs,
    )
    middle, normed2, all_wg, all_wu, cot = exchange_middle(
        heads_flat.reshape(n_blk, seqs * toks, -1),
        wo,
        own_hidden,
        g_mlp,
        rows_wg,
        rows_wu,
        cot,
    )
    wg, wu = all_wg.reshape(width, -1), all_wu.reshape(width, -1)
    wd = all_wd.reshape(-1, width)
    cot = cot.reshape(rows, width)
    normed2 = normed2.reshape(rows, width)
    gate_pre = product(normed2, wg)
    up_pre = product(normed2, wu)
    sigmoid_gate = jax.nn.sigmoid(gate_pre)
    activated = (gate_pre * sigmoid_gate * up_pre).astype(bf16)
    out_parts = product(activated, wd).astype(bf16)
    grad_act = product_right(cot, wd)
    grad_gate_pre = (
        grad_act * up_pre * sigmoid_gate * (1.0 + gate_pre * (1.0 - sigmoid_gate))
    ).astype(bf16)
    grad_up_pre = (grad_act * gate_pre * sigmoid_gate).astype(bf16)
    grad_parts = (product_right(grad_gate_pre, wg) + product_right(grad_up_pre, wu)).astype(bf16)
    blocks = (n_blk, seqs * toks, width)
    out_parts = out_parts.reshape(blocks)
    output_0, grad_middle, middle_low, grad_gate, grad_up, part_down = exchange_back(
        grad_parts.reshape(blocks),
        out_parts,
        middle,
        own_cotangent,
        g_mlp,
        normed2,
        grad_gate_pre,
        grad_up_pre,
        activated,
        cot,
    )
    middle_low = middle_low.reshape(rows, width)
    grad_qkv, head_terms, grad_down, grad_gate, grad_up = attend_back(
        middle_low,
        wo,
        queries,
        key_values,
        lse,
        qkv,
        gain_q,
        gain_k,
        cosine,
        sine,
        query_pos,
        key_pos,
        grad_gate,
        grad_up,
        part_down,
    )
    grad_hidden, grad_w_qkv, grad_out, small, output_1 = exchange_last(
        w_qkv,
        own_hidden,
        grad_middle,
        g_attn,
        normed,
        grad_qkv,
        heads_flat,
        middle_low,
        head_terms,
        out_parts,
        middle,
    )
    (
        grad_gate,
        grad_up,
        grad_query,
        grad_key,
        grad_value,
        grad_out,
        grad_down,
        grad_hidden,
        output,
        grad_attn_gain,
        grad_mlp_gain,
        grad_q_gain,
        grad_k_gain,
    ) = finish(
        grad_gate,
        grad_up,
        grad_w_qkv,
        grad_out,
        grad_down,
        grad_hidden,
        output_0,
        output_1,
        (w_gate, w_up, w_query, key_weight, value_weight),
        [g[None, :] for g in (attn_gain, mlp_gain)],
        small,
    )
    return (
        output.reshape(hidden.shape),
        grad_hidden.reshape(hidden.shape),
        grad_attn_gain.reshape(gain_rows),
        grad_query,
        grad_key,
        grad_value,
        grad_out,
        grad_q_gain[0],
        grad_k_gain[0],
        grad_mlp_gain.reshape(gain_rows),
        grad_gate,
        grad_up,
        grad_down,
    )


def solution(mesh):
    n_dp, n_blk, n_uly = (mesh.shape[a] for a in EVERY)
    aligned = (n_dp, n_uly) == (2, 4) and KEY_VALUE_HEADS % (n_dp * n_blk) == 0
    in_specs = (
        TOKENS,
        P(),
        P(EVERY),
        P(EVERY, None),
        P(EVERY, None),
        P(EVERY, None),
        P(EVERY, None),
        P(),
        P(),
        P(EVERY),
        P(EVERY, None),
        P(EVERY, None),
        P(EVERY, None),
        TOKENS,
    )
    out_specs = (
        TOKENS,
        TOKENS,
        P(EVERY),
        P(EVERY, None),
        P(EVERY, None),
        P(EVERY, None),
        P(EVERY, None),
        P(),
        P(),
        P(EVERY),
        P(EVERY, None),
        P(EVERY, None),
        P(EVERY, None),
    )
    return jax.shard_map(
        shards if aligned else shards_general,
        mesh=mesh, in_specs=in_specs, out_specs=out_specs, check_vma=False)
```

```python
import functools
import math

import jax
import jax.numpy as jnp
from jax import lax
from jax.experimental import pallas as pl
from jax.experimental.pallas import tpu as pltpu
from jax.sharding import PartitionSpec as P

QUERY_HEADS = 16
KEY_VALUE_HEADS = 8
HEAD_SIZE = 128


DP, BLK, ULY = "dp", "blk", "uly"
EVERY = (DP, BLK, ULY)
PLANE = (DP, ULY)
TOKENS = P(DP, (BLK, ULY), None)
EQ_KGQD_NKD_TO_KGQN = "kgqd,nkd->kgqn"
EQ_KGQN_KGQD_TO_NKD = "kgqn,kgqd->nkd"
EQ_KGQN_NKD_TO_KGQD = "kgqn,nkd->kgqd"
EQ_KGQN_QKGD_TO_NKD = "kgqn,qkgd->nkd"
EQ_QKGD_NKD_TO_KGQN = "qkgd,nkd->kgqn"
EQ_STD_DE_TO_STE = "std,de->ste"
EQ_STD_DF_TO_STF = "std,df->stf"
EQ_STD_ED_TO_STE = "std,ed->ste"
EQ_STD_FD_TO_STF = "std,fd->stf"
EQ_STD_STE_TO_DE = "std,ste->de"
EQ_STD_STF_TO_DF = "std,stf->df"
EQ_STE_DE_TO_STD = "ste,de->std"
EQ_STE_ED_TO_STD = "ste,ed->std"
EQ_STE_STD_TO_ED = "ste,std->ed"
EQ_STF_DF_TO_STD = "stf,df->std"
EQ_STF_FD_TO_STD = "stf,fd->std"
EQ_STF_STD_TO_FD = "stf,std->fd"

EPSILON = 1e-06
ROPE_BASE = 1000000.0


def rms_scale(source):
    return lax.rsqrt(jnp.mean(source * source, axis=-1, keepdims=True) + EPSILON)


def norm_back(grad_normed, source, norm_scale, gain):
    unit_rows = source * norm_scale
    scaled = grad_normed * gain
    return norm_scale * (scaled - unit_rows * jnp.mean(scaled * unit_rows, axis=-1, keepdims=True))


def angles_of(positions, head_dim):
    freq_steps = jnp.arange(head_dim // 2, dtype=jnp.float32)
    inverse = jnp.exp(freq_steps * (-2.0 * math.log(ROPE_BASE) / head_dim))
    return positions.astype(jnp.float32)[:, None] * inverse[None, :]


def rotate(source, angles, direction):
    half_dim = source.shape[-1] // 2
    cosine = jnp.cos(angles)[:, None, :]
    sine_part = direction * jnp.sin(angles)[:, None, :]
    first_half = source[..., :half_dim]
    second_half = source[..., half_dim:]
    return jnp.concatenate(
        [
            first_half * cosine - second_half * sine_part,
            second_half * cosine + first_half * sine_part,
        ],
        axis=-1,
    )


def positions_of(places, span_order, half_len):
    blocks_of = places // half_len
    block_ids = jnp.arange(span_order.shape[0], dtype=jnp.int32)
    chosen = jnp.sum(
        jnp.where(blocks_of[:, None] == block_ids[None, :], span_order[None, :], 0), axis=1
    )
    return chosen * half_len + places % half_len


def add_rows(buffer, new_rows):
    return buffer + new_rows


def shards_general(
    hidden,
    span_order,
    attn_gain,
    w_query,
    key_weight,
    value_weight,
    w_out,
    q_gain,
    k_gain,
    mlp_gain,
    w_gate,
    w_up,
    w_down,
    cotangent,
):
    sequence_count = hidden.shape[0]
    token_count = hidden.shape[1]
    ulysses_group_size = lax.axis_size(ULY)
    local_q = QUERY_HEADS // ulysses_group_size
    local_key_value = KEY_VALUE_HEADS // ulysses_group_size
    query_group_width = QUERY_HEADS // KEY_VALUE_HEADS
    block_len = token_count * ulysses_group_size
    half_len = block_len // 2
    score_scale = 1.0 / math.sqrt(HEAD_SIZE)
    blk_index = lax.axis_index(BLK)
    uly_index = lax.axis_index(ULY)
    first_place = (blk_index * ulysses_group_size + uly_index) * token_count
    local_angles = angles_of(
        positions_of(first_place + jnp.arange(token_count, dtype=jnp.int32), span_order, half_len),
        HEAD_SIZE,
    )
    query_pos = positions_of(
        blk_index * block_len + jnp.arange(block_len, dtype=jnp.int32), span_order, half_len
    )
    g_attn, wq_all, wk_all, wv_all, wo_all = (
        lax.all_gather(attn_gain, EVERY, axis=0, tiled=True),
        lax.all_gather(w_query, EVERY, axis=0, tiled=True),
        lax.all_gather(key_weight, EVERY, axis=0, tiled=True),
        lax.all_gather(value_weight, EVERY, axis=0, tiled=True),
        lax.all_gather(w_out, EVERY, axis=0, tiled=True),
    )
    source = hidden.astype(jnp.float32)
    first_scale = rms_scale(source)
    normalized_input = (source * first_scale * g_attn.astype(jnp.float32)).astype(jnp.bfloat16)
    q_pre = jnp.einsum(
        EQ_STD_DE_TO_STE, normalized_input, wq_all, preferred_element_type=jnp.float32
    ).reshape(sequence_count, token_count, QUERY_HEADS, HEAD_SIZE)
    key_before_norm = jnp.einsum(
        EQ_STD_DE_TO_STE, normalized_input, wk_all, preferred_element_type=jnp.float32
    ).reshape(sequence_count, token_count, KEY_VALUE_HEADS, HEAD_SIZE)
    value_before_norm = jnp.einsum(
        EQ_STD_DE_TO_STE, normalized_input, wv_all, preferred_element_type=jnp.float32
    ).reshape(sequence_count, token_count, KEY_VALUE_HEADS, HEAD_SIZE)
    q_scale = rms_scale(q_pre)
    k_scale = rms_scale(key_before_norm)
    gain_q = q_gain.astype(jnp.float32)
    gain_k = k_gain.astype(jnp.float32)
    q_rot = rotate(q_pre * q_scale * gain_q, local_angles, 1.0).astype(jnp.bfloat16)
    k_rot = rotate(key_before_norm * k_scale * gain_k, local_angles, 1.0).astype(jnp.bfloat16)
    v_low = value_before_norm.astype(jnp.bfloat16)
    q_heads, k_heads, v_heads = (
        lax.all_to_all(q_rot, ULY, split_axis=2, concat_axis=1, tiled=True),
        lax.all_to_all(k_rot, ULY, split_axis=2, concat_axis=1, tiled=True),
        lax.all_to_all(v_low, ULY, split_axis=2, concat_axis=1, tiled=True),
    )
    q_group = q_heads.reshape(
        sequence_count, block_len, local_key_value, query_group_width, HEAD_SIZE
    )
    stat_shape = (sequence_count, local_key_value, query_group_width, block_len)
    start_state = (
        jnp.full(stat_shape, -1e30, jnp.float32),
        jnp.zeros(stat_shape, jnp.float32),
        jnp.zeros(stat_shape + (HEAD_SIZE,), jnp.float32),
    )
    key_piece = lax.all_gather(k_heads, BLK, axis=1, tiled=True)
    value_piece = lax.all_gather(v_heads, BLK, axis=1, tiled=True)
    key_pos = positions_of(jnp.arange(key_piece.shape[1], dtype=jnp.int32), span_order, half_len)
    allowed = query_pos[:, None] >= key_pos[None, :]

    def attend_one_sequence(members):
        query_rows, key_rows, value_rows, top_seq, total_seq, accum_seq = members
        scores = (
            jnp.einsum(EQ_QKGD_NKD_TO_KGQN, query_rows, key_rows, preferred_element_type=jnp.float32)
            * score_scale
        )
        scores = jnp.where(allowed, scores, -jnp.inf)
        new_top = jnp.maximum(top_seq, jnp.max(scores, axis=-1))
        fading = jnp.exp(top_seq - new_top)
        weights = jnp.exp(scores - new_top[..., None])
        total_seq = total_seq * fading + jnp.sum(weights, axis=-1)
        accum_seq = accum_seq * fading[..., None] + jnp.einsum(
            EQ_KGQN_NKD_TO_KGQD,
            weights.astype(jnp.bfloat16),
            value_rows,
            preferred_element_type=jnp.float32,
        )
        return (new_top, total_seq, accum_seq)

    row_top, row_total, accum = lax.map(
        attend_one_sequence,
        (q_group, key_piece, value_piece, start_state[0], start_state[1], start_state[2]),
    )
    log_total = row_top + jnp.log(row_total)
    attention_output = jnp.transpose(accum / row_total[..., None], (0, 3, 1, 2, 4)).reshape(
        sequence_count, block_len, local_q, HEAD_SIZE
    )
    heads_seq = lax.all_to_all(
        attention_output.astype(jnp.bfloat16), ULY, split_axis=1, concat_axis=2, tiled=True
    )
    heads_flat = heads_seq.reshape(sequence_count, token_count, QUERY_HEADS * HEAD_SIZE)
    middle = source + jnp.einsum(
        EQ_STE_ED_TO_STD, heads_flat, wo_all, preferred_element_type=jnp.float32
    )
    g_mlp, wg_all, wu_all, wd_all = (
        lax.all_gather(mlp_gain, EVERY, axis=0, tiled=True),
        lax.all_gather(w_gate, EVERY, axis=0, tiled=True),
        lax.all_gather(w_up, EVERY, axis=0, tiled=True),
        lax.all_gather(w_down, EVERY, axis=0, tiled=True),
    )
    second_scale = rms_scale(middle)
    gain_mlp = g_mlp.astype(jnp.float32)
    normed2 = (middle * second_scale * gain_mlp).astype(jnp.bfloat16)
    gate_pre = jnp.einsum(EQ_STD_DF_TO_STF, normed2, wg_all, preferred_element_type=jnp.float32)
    up_pre = jnp.einsum(EQ_STD_DF_TO_STF, normed2, wu_all, preferred_element_type=jnp.float32)
    sigmoid_gate = jax.nn.sigmoid(gate_pre)
    activated = (gate_pre * sigmoid_gate * up_pre).astype(jnp.bfloat16)
    result = middle + jnp.einsum(
        EQ_STF_FD_TO_STD, activated, wd_all, preferred_element_type=jnp.float32
    )
    output = result.astype(jnp.bfloat16)
    g_mlp, wg_all, wu_all, wd_all = (
        lax.all_gather(mlp_gain, EVERY, axis=0, tiled=True),
        lax.all_gather(w_gate, EVERY, axis=0, tiled=True),
        lax.all_gather(w_up, EVERY, axis=0, tiled=True),
        lax.all_gather(w_down, EVERY, axis=0, tiled=True),
    )
    gain_mlp = g_mlp.astype(jnp.float32)
    grad_act = jnp.einsum(EQ_STD_FD_TO_STF, cotangent, wd_all, preferred_element_type=jnp.float32)
    grad_gate_pre = (
        grad_act * up_pre * sigmoid_gate * (1.0 + gate_pre * (1.0 - sigmoid_gate))
    ).astype(jnp.bfloat16)
    grad_up_pre = (grad_act * gate_pre * sigmoid_gate).astype(jnp.bfloat16)
    grad_gate = jnp.einsum(
        EQ_STD_STF_TO_DF, normed2, grad_gate_pre, preferred_element_type=jnp.float32
    )
    grad_up = jnp.einsum(EQ_STD_STF_TO_DF, normed2, grad_up_pre, preferred_element_type=jnp.float32)
    grad_normed2 = jnp.einsum(
        EQ_STF_DF_TO_STD, grad_gate_pre, wg_all, preferred_element_type=jnp.float32
    ) + jnp.einsum(EQ_STF_DF_TO_STD, grad_up_pre, wu_all, preferred_element_type=jnp.float32)
    mlp_gain_term = jnp.sum(grad_normed2 * middle * second_scale, axis=(0, 1))
    grad_middle = cotangent.astype(jnp.float32) + norm_back(
        grad_normed2, middle, second_scale, gain_mlp
    )
    grad_mlp_gain, grad_gate, grad_up = (
        lax.psum_scatter(mlp_gain_term, EVERY, scatter_dimension=0, tiled=True),
        lax.psum_scatter(grad_gate, EVERY, scatter_dimension=0, tiled=True),
        lax.psum_scatter(grad_up, EVERY, scatter_dimension=0, tiled=True),
    )
    g_attn, wq_all, wk_all, wv_all, wo_all = (
        lax.all_gather(attn_gain, EVERY, axis=0, tiled=True),
        lax.all_gather(w_query, EVERY, axis=0, tiled=True),
        lax.all_gather(key_weight, EVERY, axis=0, tiled=True),
        lax.all_gather(value_weight, EVERY, axis=0, tiled=True),
        lax.all_gather(w_out, EVERY, axis=0, tiled=True),
    )
    middle_low = grad_middle.astype(jnp.bfloat16)
    grad_out = jnp.einsum(EQ_STE_STD_TO_ED, heads_flat, middle_low, preferred_element_type=jnp.float32)
    grad_heads = (
        jnp.einsum(EQ_STD_ED_TO_STE, middle_low, wo_all, preferred_element_type=jnp.float32)
        .astype(jnp.bfloat16)
        .reshape(sequence_count, token_count, QUERY_HEADS, HEAD_SIZE)
    )
    grad_heads_local = lax.all_to_all(grad_heads, ULY, split_axis=2, concat_axis=1, tiled=True)
    grad_group = jnp.transpose(
        grad_heads_local.reshape(
            sequence_count, block_len, local_key_value, query_group_width, HEAD_SIZE
        ),
        (0, 2, 3, 1, 4),
    )
    delta = jnp.sum(grad_heads_local.astype(jnp.float32) * attention_output, axis=-1)
    delta = jnp.transpose(
        delta.reshape(sequence_count, block_len, local_key_value, query_group_width), (0, 2, 3, 1)
    )
    seq_length = block_len * lax.axis_size(BLK)
    zero_keys = jnp.zeros((sequence_count, seq_length, local_key_value, HEAD_SIZE), jnp.float32)
    back_state = (jnp.zeros(stat_shape + (HEAD_SIZE,), jnp.float32), zero_keys, zero_keys)
    key_piece = lax.all_gather(k_heads, BLK, axis=1, tiled=True)
    value_piece = lax.all_gather(v_heads, BLK, axis=1, tiled=True)
    key_pos = positions_of(jnp.arange(key_piece.shape[1], dtype=jnp.int32), span_order, half_len)
    back_allowed = query_pos[:, None] >= key_pos[None, :]

    def back_one_sequence(members):
        query_rows, grad_rows, lse_seq, delta_seq, key_rows, value_rows, dq_seq, dk_seq, dv_seq = (
            members
        )
        scores = (
            jnp.einsum(EQ_QKGD_NKD_TO_KGQN, query_rows, key_rows, preferred_element_type=jnp.float32)
            * score_scale
        )
        scores = jnp.where(back_allowed, scores, -jnp.inf)
        probs = jnp.exp(scores - lse_seq[..., None])
        grad_values = jnp.einsum(
            EQ_KGQN_KGQD_TO_NKD,
            probs.astype(jnp.bfloat16),
            grad_rows,
            preferred_element_type=jnp.float32,
        )
        grad_probs = jnp.einsum(
            EQ_KGQD_NKD_TO_KGQN, grad_rows, value_rows, preferred_element_type=jnp.float32
        )
        grad_scores = (probs * (grad_probs - delta_seq[..., None])).astype(jnp.bfloat16)
        dq_seq = dq_seq + score_scale * jnp.einsum(
            EQ_KGQN_NKD_TO_KGQD, grad_scores, key_rows, preferred_element_type=jnp.float32
        )
        grad_keys = score_scale * jnp.einsum(
            EQ_KGQN_QKGD_TO_NKD, grad_scores, query_rows, preferred_element_type=jnp.float32
        )
        return (dq_seq, add_rows(dk_seq, grad_keys), add_rows(dv_seq, grad_values))

    grad_q_group, grad_k_whole, grad_v_whole = lax.map(
        back_one_sequence,
        (
            q_group,
            grad_group,
            log_total,
            delta,
            key_piece,
            value_piece,
            back_state[0],
            back_state[1],
            back_state[2],
        ),
    )
    grad_k_block, grad_v_block = (
        lax.psum_scatter(
            grad_k_whole.astype(jnp.bfloat16), BLK, scatter_dimension=1, tiled=True
        ).astype(jnp.float32),
        lax.psum_scatter(
            grad_v_whole.astype(jnp.bfloat16), BLK, scatter_dimension=1, tiled=True
        ).astype(jnp.float32),
    )
    grad_q_block = jnp.transpose(grad_q_group, (0, 3, 1, 2, 4)).reshape(
        sequence_count, block_len, local_q, HEAD_SIZE
    )
    grad_q_seq, grad_k_seq, value_sequence_gradient = (
        lax.all_to_all(
            grad_q_block.astype(jnp.bfloat16), ULY, split_axis=1, concat_axis=2, tiled=True
        ).astype(grad_q_block.dtype),
        lax.all_to_all(
            grad_k_block.astype(jnp.bfloat16), ULY, split_axis=1, concat_axis=2, tiled=True
        ).astype(grad_k_block.dtype),
        lax.all_to_all(
            grad_v_block.astype(jnp.bfloat16), ULY, split_axis=1, concat_axis=2, tiled=True
        ).astype(grad_v_block.dtype),
    )
    grad_q_normed = rotate(grad_q_seq, local_angles, -1.0)
    grad_k_normed = rotate(grad_k_seq, local_angles, -1.0)
    q_gain_term = jnp.sum(grad_q_normed * q_pre * q_scale, axis=(0, 1, 2))
    k_gain_term = jnp.sum(grad_k_normed * key_before_norm * k_scale, axis=(0, 1, 2))
    grad_q_pre = (
        norm_back(grad_q_normed, q_pre, q_scale, gain_q)
        .astype(jnp.bfloat16)
        .reshape(sequence_count, token_count, QUERY_HEADS * HEAD_SIZE)
    )
    grad_k_pre = (
        norm_back(grad_k_normed, key_before_norm, k_scale, gain_k)
        .astype(jnp.bfloat16)
        .reshape(sequence_count, token_count, KEY_VALUE_HEADS * HEAD_SIZE)
    )
    value_pre_gradient = value_sequence_gradient.astype(jnp.bfloat16).reshape(
        sequence_count, token_count, KEY_VALUE_HEADS * HEAD_SIZE
    )
    grad_query = jnp.einsum(
        EQ_STD_STE_TO_DE, normalized_input, grad_q_pre, preferred_element_type=jnp.float32
    )
    grad_key = jnp.einsum(
        EQ_STD_STE_TO_DE, normalized_input, grad_k_pre, preferred_element_type=jnp.float32
    )
    grad_value = jnp.einsum(
        EQ_STD_STE_TO_DE, normalized_input, value_pre_gradient, preferred_element_type=jnp.float32
    )
    grad_normed = jnp.einsum(EQ_STE_DE_TO_STD, grad_q_pre, wq_all, preferred_element_type=jnp.float32)
    grad_normed = grad_normed + jnp.einsum(
        EQ_STE_DE_TO_STD, grad_k_pre, wk_all, preferred_element_type=jnp.float32
    )
    grad_normed = grad_normed + jnp.einsum(
        EQ_STE_DE_TO_STD, value_pre_gradient, wv_all, preferred_element_type=jnp.float32
    )
    attn_gain_term = jnp.sum(grad_normed * source * first_scale, axis=(0, 1))
    grad_hidden = grad_middle + norm_back(
        grad_normed, source, first_scale, g_attn.astype(jnp.float32)
    )
    grad_down = jnp.einsum(EQ_STF_STD_TO_FD, activated, cotangent, preferred_element_type=jnp.float32)
    grad_attn_gain, grad_query, grad_key, grad_value, grad_out, grad_down = (
        lax.psum_scatter(attn_gain_term, EVERY, scatter_dimension=0, tiled=True),
        lax.psum_scatter(grad_query, EVERY, scatter_dimension=0, tiled=True),
        lax.psum_scatter(grad_key, EVERY, scatter_dimension=0, tiled=True),
        lax.psum_scatter(grad_value, EVERY, scatter_dimension=0, tiled=True),
        lax.psum_scatter(grad_out, EVERY, scatter_dimension=0, tiled=True),
        lax.psum_scatter(grad_down, EVERY, scatter_dimension=0, tiled=True),
    )
    grad_q_gain, grad_k_gain = lax.psum((q_gain_term, k_gain_term), EVERY)
    return (
        output,
        grad_hidden,
        grad_attn_gain,
        grad_query,
        grad_key,
        grad_value,
        grad_out,
        grad_q_gain,
        grad_k_gain,
        grad_mlp_gain,
        grad_gate,
        grad_up,
        grad_down,
    )


MESH = pl.DeviceIdType.MESH
HBM = pl.BlockSpec(memory_space=pltpu.HBM)
VMEM = pl.BlockSpec(memory_space=pltpu.VMEM)
MIB = 1 << 20


def kernel_params(collective_id, vmem_mib=62):
    return pltpu.CompilerParams(
        collective_id=collective_id, has_side_effects=True, vmem_limit_bytes=vmem_mib * MIB
    )


def semaphores(count, local=16):
    return [
        pltpu.SemaphoreType.DMA((count,)),
        pltpu.SemaphoreType.DMA((count,)),
        pltpu.SemaphoreType.DMA((local,)),
    ]


class Copy:
    def __init__(self, descriptor, sends, receives):
        self.descriptor, self.sends, self.receives = descriptor, sends, receives

    def under(self, condition, action):
        if condition is None:
            action()
        else:
            pl.when(condition)(action)

    def start(self):
        self.under(self.sends, lambda: self.descriptor().start())
        return self

    def sent(self):
        self.under(self.sends, lambda: self.descriptor().wait_send())

    def arrived(self):
        self.under(self.receives, lambda: self.descriptor().wait_recv())


class Links:
    def __init__(self, send, recv, here):
        self.send, self.recv, self.here = send, recv, here
        self.used, self.used_here = 0, 0
        self.copies, self.local_copies = [], []
        self.n_dp, self.n_blk, self.n_uly = (lax.axis_size(a) for a in EVERY)
        self.dp, self.blk, self.uly = (lax.axis_index(a) for a in EVERY)
        self.other_dp = 1 - self.dp
        self.across = lax.rem(self.uly + 2, 4)
        self.twin = self.uly + 1 - 2 * lax.rem(self.uly, 2)
        self.x_way = (self.other_dp, self.blk, self.uly)
        self.y_way = (self.dp, self.blk, self.across)
        self.core_way = (self.dp, self.blk, self.twin)

    def peer(self, step):
        return lax.rem(self.blk + step, self.n_blk)

    def peers(self):
        return [(self.dp, self.peer(k), self.uly) for k in range(1, self.n_blk)]

    def greet(self, devices):
        barrier = pltpu.get_barrier_semaphore()
        for device in devices:
            pl.semaphore_signal(barrier, inc=1, device_id=device, device_id_type=MESH)
        pl.semaphore_wait(barrier, len(devices))

    def remote(self, source, target, device, sends=None, receives=None):
        slot = self.used
        self.used += 1

        def descriptor():
            return pltpu.make_async_remote_copy(
                src_ref=source(),
                dst_ref=target(),
                send_sem=self.send.at[slot],
                recv_sem=self.recv.at[slot],
                device_id=device,
                device_id_type=MESH,
            )

        copy = Copy(descriptor, sends, receives)
        self.copies.append(copy)
        return copy.start()

    def to(self, source, target, device):
        return self.remote(lambda: source, lambda: target, device)

    def local(self, source, target):
        copy = pltpu.make_async_copy(source, target, self.here.at[self.used_here])
        self.used_here += 1
        copy.start()
        self.local_copies.append(copy)
        return copy

    def finish(self):
        for copy in self.copies:
            copy.sent()


class LineGather:
    def __init__(self, links, own, whole):
        self.links, self.own, self.whole = links, own, whole
        self.waiting = []

    def send(self, step):
        links, whole = self.links, self.whole
        blk, last = links.blk, links.n_blk - 1

        def block(index):
            if step == 0:
                return lambda: self.own
            return lambda: whole.at[index]

        self.waiting = [
            links.remote(
                block(blk - step),
                lambda: whole.at[blk - step],
                (links.dp, blk + 1, links.uly),
                jnp.logical_and(blk >= step, blk < last),
                blk >= step + 1,
            ),
            links.remote(
                block(blk + step),
                lambda: whole.at[blk + step],
                (links.dp, blk - 1, links.uly),
                jnp.logical_and(blk + step <= last, blk > 0),
                blk + step + 1 <= last,
            ),
        ]

    def arrived(self):
        for copy in self.waiting:
            copy.arrived()


def halves(tokens):
    return [pl.ds(0, tokens // 2), pl.ds(tokens // 2, tokens // 2)]


class HalvedLine:
    def __init__(self, links, own, whole):
        self.lines = [
            LineGather(links, None if own is None else own.at[rows], whole.at[:, rows])
            for rows in halves(whole.shape[1])
        ]

    def send(self, step):
        for line in self.lines:
            line.send(step)

    def advance(self, step):
        for line in self.lines:
            line.arrived()
            line.send(step)

    def arrived(self):
        for line in self.lines:
            line.arrived()


class PlaneGather:
    def __init__(self, links, at):
        self.links, self.at = links, at

    def start_x(self, own):
        links = self.links
        mine = self.at(links.dp, links.uly)
        self.from_x = links.to(own, mine, links.x_way)
        self.from_core = [links.to(own, mine, links.core_way)]

    def start_y(self, own):
        links = self.links
        self.from_y = links.to(own, self.at(links.dp, links.uly), links.y_way)

    def start(self, own=None):
        own = self.at(self.links.dp, self.links.uly) if own is None else own
        self.start_x(own)
        self.start_y(own)

    def hand_on(self):
        links, at = self.links, self.at
        self.from_x.arrived()
        half = at(links.other_dp, links.uly, 0)
        self.second_y = links.to(half, half, links.y_way)
        self.from_y.arrived()
        half = at(links.dp, links.across, 1)
        self.second_x = links.to(half, half, links.x_way)
        for chunk in (at(links.other_dp, links.uly), at(links.dp, links.across)):
            self.from_core.append(links.to(chunk, chunk, links.core_way))

    def last(self):
        links = self.links
        self.second_y.arrived()
        self.second_x.arrived()
        chunk = self.at(links.other_dp, links.across)
        self.from_core.append(links.to(chunk, chunk, links.core_way))

    def arrived(self):
        for copy in self.from_core:
            copy.arrived()


def rows_of(whole, blocked):
    def at(dp, uly, half=None):
        part = whole.at[dp, :, uly] if blocked else whole.at[dp, uly]
        if half is None:
            return part
        depth = whole.shape[-2] // 2
        rows = pl.ds(half * depth, depth)
        return part.at[:, rows] if blocked else part.at[rows]

    return at


class ColumnSwap:
    def __init__(self, links, pieces):
        self.links, self.pieces = links, pieces
        self.incoming, self.kept = [], []

    def parts(self, blk):
        links = self.links
        for weight, whole, offset in self.pieces:
            width = weight.shape[-1] // links.n_dp // links.n_blk
            for group in range(links.n_dp):
                start = (group * links.n_blk + blk) * width
                yield (
                    weight.at[:, pl.ds(pl.multiple_of(start, 128), width)],
                    whole.at[links.blk, :, pl.ds(offset + group * width, width)],
                )

    def start(self):
        links = self.links
        for step in range(1, links.n_blk):
            device = (links.dp, links.peer(step), links.uly)
            for source, target in self.parts(links.peer(step)):
                self.incoming.append(links.to(source, target, device))
        for source, target in self.parts(links.blk):
            self.kept.append(links.local(source, target))

    def arrived(self):
        for copy in self.kept:
            copy.wait()
        for copy in self.incoming:
            copy.arrived()


def write_positions(links, span_order, toks, cosine, sine, query_pos, key_pos):
    half_len = toks * links.n_uly // 2

    def first(blk, uly):
        chunk = span_order[2 * blk + lax.div(uly, links.n_uly // 2)]
        return chunk * half_len + lax.rem(uly, links.n_uly // 2) * toks

    lane = lax.broadcasted_iota(jnp.int32, (toks, HEAD_SIZE), 1)
    row = lax.broadcasted_iota(jnp.int32, (toks, HEAD_SIZE), 0)
    upper = lane >= HEAD_SIZE // 2
    step = jnp.where(upper, lane - HEAD_SIZE // 2, lane).astype(jnp.float32)
    inverse = jnp.exp(step * (-2.0 * math.log(ROPE_BASE) / HEAD_SIZE))
    for blk in range(links.n_blk):
        angles = (first(blk, links.uly) + row).astype(jnp.float32) * inverse
        at = slice(blk * toks, (blk + 1) * toks)
        cosine[at, :] = jnp.cos(angles)
        turn = jnp.sin(angles)
        sine[at, :] = jnp.where(upper, turn, -turn)
    lane = lax.broadcasted_iota(jnp.int32, query_pos.shape, 1)
    place = jnp.zeros(query_pos.shape, jnp.int32)
    for start in range(0, query_pos.shape[1], toks):
        blk = start // toks % links.n_blk
        here = jnp.logical_and(lane >= start, lane < start + toks)
        place = jnp.where(here, first(blk, links.uly) + lane - start, place)
    query_pos[...] = place
    row = lax.broadcasted_iota(jnp.int32, (toks, 1), 0)
    for uly in range(links.n_uly):
        for blk in range(links.n_blk):
            start = (uly * links.n_blk + blk) * toks
            key_pos[start : start + toks, :] = row + first(blk, jnp.int32(uly))


def write_gains(links, all_gains, size, targets):
    per_row = 128 // size
    for which, target in enumerate(targets):
        for place in range(target.shape[1] // 128):
            pieces = []
            for part in range(per_row):
                device = place * per_row + part
                plane, uly = device // links.n_uly, device % links.n_uly
                gains = all_gains[plane // links.n_blk, plane % links.n_blk, uly]
                pieces.append(gains.astype(jnp.float32)[which : which + 1, :size])
            target[:, place * 128 : (place + 1) * 128] = jnp.concatenate(pieces, axis=1)


ROWS = 32


def each_block(count, body):
    def step(index, carry):
        body(pl.ds(pl.multiple_of(index * ROWS, ROWS), ROWS))
        return carry

    lax.fori_loop(0, count // ROWS, step, 0)


class LineScatter:
    def __init__(self, links, parts, rightward, leftward):
        self.links, self.parts = links, parts
        self.slots = {1: rightward, -1: leftward}
        self.tokens = parts.shape[1]
        self.number = links.used
        self.last = links.n_blk - 1
        links.used += 2 * self.last

    def target(self, step, way):
        return self.last - step if way == 1 else step

    def slot(self, step, way):
        target = self.target(step, way)
        return self.slots[way].at[target - 1 if way == 1 else target]

    def place(self, way):
        return self.links.blk if way == 1 else self.last - self.links.blk

    def copy(self, step, way, source=None):
        links, slot = self.links, self.slot(step, way)
        number = self.number + 2 * step + (1 if way == 1 else 0)
        return pltpu.make_async_remote_copy(
            src_ref=slot if source is None else source,
            dst_ref=slot,
            send_sem=links.send.at[number],
            recv_sem=links.recv.at[number],
            device_id=(links.dp, links.blk + way, links.uly),
            device_id_type=MESH,
        )

    def start(self):
        for step in range(self.last):
            for way in (1, -1):

                @pl.when(self.place(way) == 0)
                def _(step=step, way=way):
                    self.copy(step, way, self.parts.at[self.target(step, way)]).start()

    def tick(self, tick):
        for way in (1, -1):

            @pl.when(jnp.logical_and(self.place(way) >= 1, self.place(way) <= tick))
            def _(way=way):
                step = tick - self.place(way)
                self.copy(step, way).wait_recv()
                slot, target = self.slot(step, way), self.target(step, way)

                def body(rows):
                    slot[rows, :] = slot[rows, :] + self.parts[target, rows, :]

                each_block(self.tokens, body)
                self.copy(step, way).start()

    def finish(self, total):
        blk, last = self.links.blk, self.last

        def start(rows):
            total[rows, :] = self.parts[blk, rows, :].astype(jnp.float32)

        each_block(self.tokens, start)
        for way in (1, -1):

            @pl.when(self.place(way) >= 1)
            def _(way=way):
                step = last - self.place(way)
                self.copy(step, way).wait_recv()
                slot = self.slot(step, way)

                def body(rows):
                    total[rows, :] = total[rows, :] + slot[rows, :].astype(jnp.float32)

                each_block(self.tokens, body)

    def sent(self):
        for step in range(self.last):
            for way in (1, -1):
                beyond = self.place(way) + step < self.last
                pl.when(beyond)(lambda step=step, way=way: self.copy(step, way).wait_send())


def halved_sums(links, parts, rightward, leftward):
    return [
        LineScatter(links, parts.at[:, rows], rightward.at[:, rows], leftward.at[:, rows])
        for rows in halves(parts.shape[1])
    ]


class OutputHalf:
    def __init__(self, links, which, parts, middle, rightward, leftward, total):
        rows = halves(middle.shape[0])[which]
        self.middle, self.total = middle.at[rows], total
        self.sum = LineScatter(links, parts.at[:, rows], rightward, leftward)

    def write(self, output):
        self.sum.finish(self.total)

        def body(rows):
            output[rows, :] = (self.middle[rows, :] + self.total[rows, :]).astype(jnp.bfloat16)

        each_block(self.middle.shape[0], body)


def output_scratch(n_blk, tokens, width):
    return line_scratch(n_blk, tokens // 2, width) + [
        pltpu.VMEM((tokens // 2, width), jnp.float32)
    ]


def line_scratch(n_blk, tokens, width):
    return [pltpu.VMEM((n_blk - 1, tokens, width), jnp.bfloat16)] * 2


class PlaneScatter:
    def __init__(self, links, parts, from_core, from_x, from_y, last_x, last_y):
        self.links, self.parts = links, parts
        self.own_core_only = from_core is None
        self.from_core, self.from_x, self.from_y = from_core, from_x, from_y
        self.last_x, self.last_y = last_x, last_y
        self.core = lax.rem(links.uly, 2)
        self.row = lax.div(links.uly, 2)
        self.depth = parts.shape[3]
        self.core_copies = {}

    def chunk(self, dp, row, core, half=None):
        if self.own_core_only:
            part = self.parts.at[dp, row]
        else:
            part = self.parts.at[dp, :, row * 2 + core]
        if half is None:
            return part
        depth = self.depth // 2
        return part.at[:, pl.ds(half * depth, depth)]

    def add(self, target, source):
        blocks, depth, _ = target.shape
        rows = 32 if depth % 32 == 0 else 16

        def body(index, carry):
            block = lax.div(index, depth // rows)
            at = pl.ds(pl.multiple_of(lax.rem(index, depth // rows) * rows, rows), rows)
            target[block, at, :] = target[block, at, :] + source[block, at, :]
            return carry

        lax.fori_loop(0, blocks * (depth // rows), body, 0)

    def between_cores(self, which):
        links = self.links
        dp = links.dp if which == 1 else links.other_dp
        self.core_copies[which] = [
            links.to(
                self.chunk(dp, row, 1 - self.core), self.from_core.at[which, row], links.core_way
            )
            for row in range(2)
        ]

    def core_sums(self, which):
        links = self.links
        dp = links.dp if which == 1 else links.other_dp
        for row in range(2):
            self.core_copies[which][row].arrived()
            self.add(self.chunk(dp, row, self.core), self.from_core.at[which, row])

    def across_chips(self):
        links = self.links
        if not self.own_core_only:
            self.core_sums(0)
        self.x_copies = [
            links.to(
                self.chunk(links.other_dp, row, self.core, 0), self.from_x.at[row], links.x_way
            )
            for row in range(2)
        ]
        if not self.own_core_only:
            self.core_sums(1)
        self.y_copies = [
            links.to(
                self.chunk(group, 1 - self.row, self.core, 1),
                self.from_y.at[group],
                links.y_way,
            )
            for group in range(links.n_dp)
        ]

    def second_way(self):
        links = self.links
        for row in range(2):
            self.x_copies[row].arrived()
            self.add(self.chunk(links.dp, row, self.core, 0), self.from_x.at[row])
        self.y_last = links.to(
            self.chunk(links.dp, 1 - self.row, self.core, 0), self.last_y, links.y_way
        )
        for group in range(links.n_dp):
            self.y_copies[group].arrived()
            self.add(self.chunk(group, self.row, self.core, 1), self.from_y.at[group])
        self.x_last = links.to(
            self.chunk(links.other_dp, self.row, self.core, 1), self.last_x, links.x_way
        )

    def result(self, write):
        links = self.links
        for half, copy, source in ((0, self.y_last, self.last_y), (1, self.x_last, self.last_x)):
            copy.arrived()
            own = self.chunk(links.dp, self.row, self.core, half)
            blocks, depth, _ = source.shape
            rows = 32 if depth % 32 == 0 else 16

            def body(index, carry, own=own, source=source, half=half, depth=depth, rows=rows):
                block = lax.div(index, depth // rows)
                start = pl.multiple_of(lax.rem(index, depth // rows) * rows, rows)
                at = pl.ds(start, rows)
                value = own[block, at, :].astype(jnp.float32)
                value = value + source[block, at, :].astype(jnp.float32)
                write(block, pl.ds(pl.multiple_of(start + half * depth, rows), rows), value)
                return carry

            lax.fori_loop(0, blocks * (depth // rows), body, 0)


def plane_shapes(n_dp, blocks, n_uly, depth, width):
    return [
        (n_dp, blocks, n_uly, depth, width),
        (n_dp, 2, blocks, depth, width),
        (2, blocks, depth // 2, width),
        (n_dp, blocks, depth // 2, width),
        (blocks, depth // 2, width),
        (blocks, depth // 2, width),
    ]


def plane_scratch(*sizes):
    return [pltpu.VMEM(shape, jnp.bfloat16) for shape in plane_shapes(*sizes)]


def weight_grad(rows, right, parts, dp):
    _, blocks, n_uly, depth, width = parts.shape
    columns = 512

    def body(index, carry):
        at = pl.ds(pl.multiple_of(index * columns, columns), columns)
        part = jnp.dot(rows[...], right[:, at], preferred_element_type=jnp.float32)
        parts[dp, :, :, :, at] = part.astype(jnp.bfloat16).reshape(blocks, n_uly, depth, columns)
        return carry

    lax.fori_loop(0, width // columns, body, 0)


def rows_turned(left, parts, dp):
    count = parts.shape[1] * parts.shape[2] * parts.shape[3]
    return left[:, pl.ds(pl.multiple_of(dp * count, 128), count)].T


def turned(rows, cosine, sine):
    return rows * cosine + pltpu.roll(rows, HEAD_SIZE // 2, axis=1) * sine


def transposed_product(left, right):
    return lax.dot_general(
        left, right, (((0,), (0,)), ((), ())), preferred_element_type=jnp.float32
    )


def product_right(left, right):
    return lax.dot_general(
        left, right, (((1,), (1,)), ((), ())), preferred_element_type=jnp.float32
    )


SCORE_SCALE = 1.0 / math.sqrt(HEAD_SIZE)


def mask_scores(bias, query_pos, key_pos):
    size = bias.shape[0] // 4

    def body(index, carry):
        rows = pl.ds(pl.multiple_of(index * size, size), size)
        bias[rows, :] = jnp.where(query_pos[...] >= key_pos[rows, :], 0.0, -1e30)
        return carry

    lax.fori_loop(0, 4, body, 0)


class RowBlocks:
    def __init__(self, n_blk, seqs, toks):
        self.n_blk, self.seqs, self.toks = n_blk, seqs, toks

    def each(self, body):
        def step(index, carry):
            blk, seq = lax.div(index, self.seqs), lax.rem(index, self.seqs)
            body(
                seq,
                pl.ds(pl.multiple_of(index * self.toks, self.toks), self.toks),
                pl.multiple_of(blk * self.toks, self.toks),
            )
            return carry

        lax.fori_loop(0, self.n_blk * self.seqs, step, 0)


def attention_back_kernel(
    all_low,
    wo,
    queries,
    key_values,
    lse,
    qkv,
    q_gain,
    k_gain,
    cosine,
    sine,
    query_pos,
    key_pos,
    grad_gate,
    grad_up,
    part_down,
    grad_qkv,
    gain_terms,
    grad_down,
    gate_rows,
    up_rows,
    bias,
    grad_heads,
    grad_rows,
    probs,
    grad_probs,
    grad_kv,
    from_core,
    from_across,
    down_1,
    down_3,
    down_4,
    down_5,
    down_6,
    send,
    recv,
    here,
):
    links = Links(send, recv, here)
    links.greet(links.peers() + [links.x_way, links.y_way, links.core_way])
    down = PlaneScatter(links, down_1, None, down_3, down_4, down_5, down_6)
    links.local(part_down, down_1).wait()
    down.across_chips()
    swapped, keep = [], []
    for source, target in ((grad_gate, gate_rows), (grad_up, up_rows)):
        for step in range(1, links.n_blk):
            peer = links.peer(step)
            swapped.append(
                links.to(source.at[peer], target.at[links.blk], (links.dp, peer, links.uly))
            )
        keep.append(links.local(source.at[links.blk], target.at[links.blk]))
    grad_heads[...] = product_right(all_low[...], wo[...])
    mask_scores(bias, query_pos, key_pos)
    seqs, kv_heads, q_rows, _ = queries.shape
    q_len = key_values.shape[4]
    group = q_rows // q_len
    blocks = RowBlocks(links.n_blk, seqs, q_len // links.n_blk)
    q_end = kv_heads * group * HEAD_SIZE
    k_end = q_end + kv_heads * HEAD_SIZE
    gain_terms[...] = jnp.zeros_like(gain_terms)

    def gather_rows(seq, rows, start):
        for head in range(kv_heads * group):
            to = pl.ds((head % group) * q_len + start, blocks.toks)
            grad_rows[seq, head // group, to, :] = grad_heads[
                rows, head * HEAD_SIZE : (head + 1) * HEAD_SIZE
            ].astype(jnp.bfloat16)

    blocks.each(gather_rows)

    def back_norm(upstream, pre, gain, at, which):
        upstream = turned(upstream, cosine[at, :], -sine[at, :])
        gain_terms[which : which + 1, :] += jnp.sum(
            upstream * pre * rms_scale(pre), axis=0, keepdims=True
        )
        return back_rows(upstream, pre, gain[...].astype(jnp.float32)).astype(jnp.bfloat16)

    def back(seq, head):
        def first(piece, delta):
            rows = pl.ds(pl.multiple_of(piece * q_len, q_len), q_len)
            scores = product_right(key_values[piece, 0, seq, head], queries[seq, head])
            prob = jnp.exp(
                scores * SCORE_SCALE + bias[rows, :] - lse[seq * kv_heads + head]
            )
            grad_prob = product_right(key_values[piece, 1, seq, head], grad_rows[seq, head])
            probs[rows, :] = prob
            grad_probs[rows, :] = grad_prob
            return delta + jnp.sum(prob * grad_prob, axis=0, keepdims=True)

        delta = lax.fori_loop(0, links.n_uly, first, jnp.zeros((1, q_rows), jnp.float32))

        def second(piece, grad_query):
            rows = pl.ds(pl.multiple_of(piece * q_len, q_len), q_len)
            prob = probs[rows, :]
            grad_score = (prob * (grad_probs[rows, :] - delta)).astype(jnp.bfloat16)
            grad_kv[seq, piece, 0, head] = (
                SCORE_SCALE
                * jnp.dot(grad_score, queries[seq, head], preferred_element_type=jnp.float32)
            ).astype(jnp.bfloat16)
            grad_kv[seq, piece, 1, head] = jnp.dot(
                prob.astype(jnp.bfloat16),
                grad_rows[seq, head],
                preferred_element_type=jnp.float32,
            ).astype(jnp.bfloat16)
            return grad_query + transposed_product(key_values[piece, 0, seq, head], grad_score)

        grad_query = lax.fori_loop(
            0, links.n_uly, second, jnp.zeros((HEAD_SIZE, q_rows), jnp.float32)
        )
        grad_heads[:, :HEAD_SIZE] = (grad_query * SCORE_SCALE).T
        for member in range(group):
            column = (head * group + member) * HEAD_SIZE
            for blk in range(links.n_blk):
                row = (blk * seqs + seq) * blocks.toks
                at = pl.ds(blk * blocks.toks, blocks.toks)
                start = member * q_len + blk * blocks.toks
                grad_qkv[row : row + blocks.toks, column : column + HEAD_SIZE] = back_norm(
                    grad_heads[start : start + blocks.toks, :HEAD_SIZE],
                    qkv[row : row + blocks.toks, column : column + HEAD_SIZE],
                    q_gain,
                    at,
                    0,
                )

    core, line = lax.rem(links.uly, 2), lax.div(links.uly, 2)

    def add(target, source):
        for kind in range(2):
            for head in range(kv_heads):
                target[kind, head] = target[kind, head] + source[kind, head]

    def core_sums(seq):
        copies = [
            links.to(
                grad_kv.at[seq, row * 2 + 1 - core], from_core.at[seq, row], links.core_way
            )
            for row in range(2)
        ]
        return copies

    def across_sums(seq, copies):
        for row in range(2):
            copies[row].arrived()
            add(grad_kv.at[seq, row * 2 + core], from_core.at[seq, row])
        return links.to(
            grad_kv.at[seq, (1 - line) * 2 + core], from_across.at[seq], links.y_way
        )

    def own_keys(seq, copy):
        copy.arrived()
        for head in range(kv_heads):
            for blk in range(links.n_blk):
                row = (blk * seqs + seq) * blocks.toks
                at = pl.ds(blk * blocks.toks, blocks.toks)
                term = [
                    grad_kv[seq, links.uly, kind, head, at, :].astype(jnp.float32)
                    + from_across[seq, kind, head, at, :].astype(jnp.float32)
                    for kind in range(2)
                ]
                k_at = q_end + head * HEAD_SIZE
                v_at = k_end + head * HEAD_SIZE
                grad_qkv[row : row + blocks.toks, k_at : k_at + HEAD_SIZE] = back_norm(
                    term[0],
                    qkv[row : row + blocks.toks, k_at : k_at + HEAD_SIZE],
                    k_gain,
                    at,
                    1,
                )
                grad_qkv[row : row + blocks.toks, v_at : v_at + HEAD_SIZE] = term[1].astype(
                    jnp.bfloat16
                )

    stage, last = None, []
    for seq in range(seqs):
        for head in range(kv_heads):
            back(seq, head)
            if seq == 0 and head == kv_heads - 1:
                down.second_way()
            if stage is not None:
                last.append((seq - 1, across_sums(seq - 1, stage)))
                stage = None
        stage = core_sums(seq)
    last.append((seqs - 1, across_sums(seqs - 1, stage)))
    for seq, copy in last:
        own_keys(seq, copy)

    def write(block, rows, values):
        grad_down[block, rows, :] = values

    down.result(write)
    for copy in keep:
        copy.wait()
    for copy in swapped:
        copy.arrived()
    links.finish()


def attend_back(
    all_low,
    wo,
    queries,
    key_values,
    lse,
    qkv,
    q_gain,
    k_gain,
    cosine,
    sine,
    query_pos,
    key_pos,
    grad_gate,
    grad_up,
    part_down,
):
    seqs, kv_heads, q_rows, _ = queries.shape
    n_uly, _, _, _, q_len, _ = key_values.shape
    rows = all_low.shape[0]
    keys = key_pos.shape[0]
    f32, low = jnp.float32, jnp.bfloat16
    scratch = [
        ((keys, q_rows), f32),
        ((rows, wo.shape[0]), f32),
        (queries.shape, low),
        ((keys, q_rows), f32),
        ((keys, q_rows), f32),
        ((seqs, n_uly, 2, kv_heads, q_len, HEAD_SIZE), low),
        ((seqs, 2, 2, kv_heads, q_len, HEAD_SIZE), low),
        ((seqs, 2, kv_heads, q_len, HEAD_SIZE), low),
        (part_down.shape, low),
    ]
    n_dp, _, _, depth, width = part_down.shape
    scratch += [(shape, low) for shape in plane_shapes(n_dp, 1, n_uly, depth, width)[2:]]
    return pl.pallas_call(
        attention_back_kernel,
        out_shape=[
            jax.ShapeDtypeStruct(qkv.shape, low),
            jax.ShapeDtypeStruct((8, HEAD_SIZE), f32),
            jax.ShapeDtypeStruct((1, depth, width), f32),
            jax.ShapeDtypeStruct(grad_gate.shape, low),
            jax.ShapeDtypeStruct(grad_up.shape, low),
        ],
        in_specs=[VMEM] * 12 + [HBM] * 3,
        out_specs=[VMEM] * 3 + [HBM] * 2,
        scratch_shapes=[pltpu.VMEM(shape, kind) for shape, kind in scratch]
        + semaphores(40),
        compiler_params=kernel_params(5),
    )(
        all_low,
        wo,
        queries,
        key_values,
        lse,
        qkv,
        q_gain,
        k_gain,
        cosine,
        sine,
        query_pos,
        key_pos,
        grad_gate,
        grad_up,
        part_down,
    )


def forward_kernel(
    toks,
    gain_rows,
    span_order,
    hidden,
    wq,
    wk,
    wv,
    wo,
    wg,
    wu,
    wd,
    cotangent,
    gains,
    q_gain,
    k_gain,
    all_qkv,
    all_wo,
    all_wg,
    all_wu,
    all_wd,
    all_cot,
    attn_gain,
    mlp_gain,
    cosine,
    sine,
    query_pos,
    key_pos,
    heads,
    normed,
    qkv,
    queries,
    key_values,
    lse,
    middle,
    all_normed,
    all_gains,
    all_hidden,
    near_qkv,
    near_wo,
    bias,
    parts,
    rightward,
    leftward,
    own_normed,
    send,
    recv,
    here,
):
    links = Links(send, recv, here)
    links.greet(links.peers() + [links.x_way, links.y_way, links.core_way])
    tokens, width = hidden.shape
    spans = halves(tokens)
    q_width, k_width = wq.shape[1] // links.n_blk, wk.shape[1] // links.n_blk
    chunk = all_qkv.at[links.dp, :, links.uly]
    swap = ColumnSwap(
        links, [(wq, chunk, 0), (wk, chunk, q_width), (wv, chunk, q_width + k_width)]
    )
    plane_wo = PlaneGather(links, rows_of(all_wo, False))
    plane_wd = PlaneGather(links, rows_of(all_wd, False))
    plane_qkv = PlaneGather(links, rows_of(all_qkv, True))
    plane_gain = PlaneGather(links, rows_of(all_gains, True))
    swap.start()
    my_gains = all_gains.at[links.dp, links.blk, links.uly]
    gain_swap = [links.to(gains, my_gains, device) for device in links.peers()]
    plane_wo.start(wo)
    line = HalvedLine(links, hidden, all_hidden)
    line.send(0)
    keep = [
        links.local(gains, my_gains),
        links.local(hidden, all_hidden.at[links.blk]),
        links.local(wo, all_wo.at[links.dp, links.uly]),
        links.local(wd, all_wd.at[links.dp, links.uly]),
        links.local(cotangent, all_cot.at[links.blk]),
    ]
    write_positions(links, span_order, toks, cosine, sine, query_pos, key_pos)
    swap.arrived()
    plane_qkv.start()
    keep[0].wait()
    for copy in gain_swap:
        copy.arrived()
    plane_gain.start()
    plane_wd.start(wd)
    mask_scores(bias, query_pos, key_pos)
    plane_wo.hand_on()
    line.advance(1)
    plane_qkv.hand_on()
    plane_gain.hand_on()
    plane_wo.last()
    for step in range(2, links.n_blk - 1):
        line.advance(step)
    pairs = [(wg, all_wg), (wu, all_wu)]
    planes = [PlaneGather(links, rows_of(whole, True)) for _, whole in pairs]
    swaps = [
        ColumnSwap(links, [(weight, whole.at[links.dp, :, links.uly], 0)])
        for weight, whole in pairs
    ]
    for swap in swaps:
        swap.start()
    cot_line = HalvedLine(links, cotangent, all_cot)
    cot_line.send(0)
    plane_qkv.last()
    plane_gain.last()
    plane_gain.arrived()
    write_gains(links, all_gains, gain_rows, (attn_gain, mlp_gain))
    plane_wd.hand_on()
    for copy in keep[1:]:
        copy.wait()
    plane_wo.arrived()
    plane_qkv.arrived()
    near = [links.local(all_qkv, near_qkv), links.local(all_wo, near_wo)]
    for half, rows_of_half in zip(line.lines, spans):
        half.arrived()

        def norm(rows, rows_of_half=rows_of_half):
            at = pl.ds(pl.multiple_of(rows_of_half.start + rows.start, ROWS), ROWS)
            for blk in range(links.n_blk):
                source = all_hidden[blk, at, :].astype(jnp.float32)
                to = pl.ds(pl.multiple_of(blk * tokens + at.start, ROWS), ROWS)
                normed[to, :] = (source * rms_scale(source) * attn_gain[...]).astype(
                    jnp.bfloat16
                )

        each_block(tokens // 2, norm)
    for copy in near:
        copy.wait()
    for column in range(0, qkv.shape[1], 256):
        weight = near_qkv[:, :, :, :, column : column + 256].reshape(width, 256)
        qkv[:, column : column + 256] = jnp.dot(
            normed[...], weight, preferred_element_type=jnp.float32
        )
    seqs, kv_heads, q_rows, _ = queries.shape
    q_len = key_values.shape[4]
    group = q_rows // q_len
    blocks = RowBlocks(links.n_blk, seqs, q_len // links.n_blk)
    q_end = kv_heads * group * HEAD_SIZE
    k_end = q_end + kv_heads * HEAD_SIZE

    def rotated(rows, column, gain, at):
        pre = qkv[rows, column : column + HEAD_SIZE]
        gain = gain[...].astype(jnp.float32)
        return turned(pre * rms_scale(pre) * gain, cosine[at, :], sine[at, :]).astype(
            jnp.bfloat16
        )

    def place_keys(seq, rows, start):
        at = pl.ds(start, blocks.toks)
        for head in range(kv_heads):
            column = head * HEAD_SIZE
            key_values[links.uly, 0, seq, head, at, :] = rotated(
                rows, q_end + column, k_gain, at
            )
            key_values[links.uly, 1, seq, head, at, :] = qkv[
                rows, k_end + column : k_end + column + HEAD_SIZE
            ].astype(jnp.bfloat16)

    blocks.each(place_keys)
    mine = key_values.at[links.uly]
    kv_core = links.to(mine, mine, links.core_way)
    kv_across = links.to(mine, mine, links.y_way)

    def place_queries(seq, rows, start):
        at = pl.ds(start, blocks.toks)
        for head in range(kv_heads * group):
            to = pl.ds((head % group) * q_len + start, blocks.toks)
            queries[seq, head // group, to, :] = rotated(rows, head * HEAD_SIZE, q_gain, at)

    blocks.each(place_queries)
    plane_wd.last()
    swaps[0].arrived()
    planes[0].start()
    kv_across.arrived()
    theirs = key_values.at[links.across]
    kv_last = links.to(theirs, theirs, links.core_way)
    kv_core.arrived()
    kv_last.arrived()

    def attend(seq, head):
        def over_keys(piece, carry):
            total, mixed = carry
            rows = pl.ds(pl.multiple_of(piece * q_len, q_len), q_len)
            scores = product_right(key_values[piece, 0, seq, head], queries[seq, head])
            weights = jnp.exp(scores * SCORE_SCALE + bias[rows, :])
            total = total + jnp.sum(weights, axis=0, keepdims=True)
            mixed = mixed + transposed_product(
                key_values[piece, 1, seq, head], weights.astype(jnp.bfloat16)
            )
            return total, mixed

        total, mixed = lax.fori_loop(
            0,
            links.n_uly,
            over_keys,
            (
                jnp.zeros((1, q_rows), jnp.float32),
                jnp.zeros((HEAD_SIZE, q_rows), jnp.float32),
            ),
        )
        lse[seq * kv_heads + head] = jnp.log(total)
        attended = (mixed / total).T.astype(jnp.bfloat16)
        for member in range(group):
            column = (head * group + member) * HEAD_SIZE
            for blk in range(links.n_blk):
                row = (blk * seqs + seq) * blocks.toks
                start = member * q_len + blk * blocks.toks
                heads[row : row + blocks.toks, column : column + HEAD_SIZE] = attended[
                    start : start + blocks.toks, :
                ]

    for seq in range(seqs):
        for head in range(kv_heads):
            attend(seq, head)
            if seq == 0 and head == kv_heads - 1:
                swaps[1].arrived()
                planes[1].start()
    out_weight = near_wo[...].reshape(heads.shape[1], width)
    for blk in (links.n_blk - 1, 0) + tuple(range(1, links.n_blk - 1)):
        parts[blk] = jnp.dot(
            heads[blk * tokens : (blk + 1) * tokens, :],
            out_weight,
            preferred_element_type=jnp.float32,
        ).astype(jnp.bfloat16)
    sums = halved_sums(links, parts, rightward, leftward)
    for half in sums:
        half.start()
    planes[0].hand_on()
    cot_line.lines[0].arrived()
    cot_line.lines[0].send(1)
    lines = []

    def settle(half, rows_of_half):
        half.finish(middle.at[rows_of_half])

        def body(rows):
            at = pl.ds(pl.multiple_of(rows_of_half.start + rows.start, ROWS), ROWS)
            total = middle[at, :] + all_hidden[links.blk, at, :].astype(jnp.float32)
            middle[at, :] = total
            own_normed[at, :] = (total * rms_scale(total) * mlp_gain[...]).astype(jnp.bfloat16)

        each_block(tokens // 2, body)
        next_line = LineGather(links, own_normed.at[rows_of_half], all_normed.at[:, rows_of_half])
        next_line.send(0)
        lines.append(next_line)

    for tick in range(1, links.n_blk - 1):
        sums[0].tick(tick)
        if tick == 1:
            cot_line.lines[1].arrived()
            cot_line.lines[1].send(1)
    settle(sums[0], spans[0])
    for tick in range(1, links.n_blk - 1):
        sums[1].tick(tick)
        for half in cot_line.lines:
            half.arrived()
            if tick + 1 < links.n_blk - 1:
                half.send(tick + 1)
    settle(sums[1], spans[1])
    last_local = links.local(own_normed, all_normed.at[links.blk])
    planes[0].last()
    planes[1].hand_on()
    for step in range(1, links.n_blk - 1):
        for half in lines:
            half.arrived()
            half.send(step)
    planes[1].last()
    for half in lines:
        half.arrived()
    for plane in [plane_wd] + planes:
        plane.arrived()
    last_local.wait()
    for half in sums:
        half.sent()
    links.finish()


SMEM = pl.BlockSpec(memory_space=pltpu.SMEM)


def forward(
    span_order,
    hidden,
    wq,
    wk,
    wv,
    wo,
    wg,
    wu,
    wd,
    cotangent,
    gains,
    q_gain,
    k_gain,
    seqs,
    gain_rows,
):
    n_dp, n_blk, n_uly = (lax.axis_size(a) for a in EVERY)
    tokens, width = hidden.shape
    toks = tokens // seqs
    rows, q_len = n_blk * tokens, n_blk * toks
    group = QUERY_HEADS // KEY_VALUE_HEADS
    kv_heads = KEY_VALUE_HEADS // n_blk
    q_rows, keys = group * q_len, n_uly * q_len
    columns = (wq.shape[1] + wk.shape[1] + wv.shape[1]) // n_blk
    f32, low, i32 = jnp.float32, jnp.bfloat16, jnp.int32
    ff = wg.shape[1] // n_blk
    far = [
        (n_dp, n_blk, n_uly, wq.shape[0], columns),
        (n_dp, n_uly) + wo.shape,
        (n_dp, n_blk, n_uly, wg.shape[0], ff),
        (n_dp, n_blk, n_uly, wu.shape[0], ff),
        (n_dp, n_uly) + wd.shape,
        (n_blk, tokens, width),
    ]
    near = [
        ((1, width), f32),
        ((1, width), f32),
        ((q_len, HEAD_SIZE), f32),
        ((q_len, HEAD_SIZE), f32),
        ((1, q_rows), i32),
        ((keys, 1), i32),
        ((rows, kv_heads * group * HEAD_SIZE), low),
        ((rows, width), low),
        ((rows, columns), f32),
        ((seqs, kv_heads, q_rows, HEAD_SIZE), low),
        ((n_uly, 2, seqs, kv_heads, q_len, HEAD_SIZE), low),
        ((seqs * kv_heads, 1, q_rows), f32),
        ((tokens, width), f32),
        ((n_blk, tokens, width), low),
    ]
    scratch = [
        ((n_dp, n_blk, n_uly) + gains.shape, low),
        ((n_blk, tokens, width), low),
        (far[0], low),
        (far[1], low),
        ((keys, q_rows), f32),
        ((n_blk, tokens, width), low),
        ((n_blk - 1, tokens, width), low),
        ((n_blk - 1, tokens, width), low),
        ((tokens, width), low),
    ]
    return pl.pallas_call(
        functools.partial(forward_kernel, toks, gain_rows),
        out_shape=[jax.ShapeDtypeStruct(shape, low) for shape in far]
        + [jax.ShapeDtypeStruct(shape, kind) for shape, kind in near],
        in_specs=[SMEM] + [HBM] * 10 + [VMEM] * 2,
        out_specs=[HBM] * len(far) + [VMEM] * len(near),
        scratch_shapes=[pltpu.VMEM(shape, kind) for shape, kind in scratch]
        + semaphores(160, 32),
        compiler_params=kernel_params(0),
    )(span_order, hidden, wq, wk, wv, wo, wg, wu, wd, cotangent, gains, q_gain, k_gain)


def back_rows(grad_normed, source, gain):
    unit = source * rms_scale(source)
    scaled = grad_normed * gain
    return rms_scale(source) * (
        scaled - unit * jnp.mean(scaled * unit, axis=-1, keepdims=True)
    )


def back_kernel(
    grad_parts,
    out_parts,
    middle,
    cotangent,
    gain,
    all_normed,
    grad_gate_pre,
    grad_up_pre,
    activated,
    all_cot,
    output,
    grad_middle,
    all_low,
    grad_gate,
    grad_up,
    part_down,
    rightward,
    leftward,
    out_right,
    out_left,
    out_total,
    low,
    turned_low,
    gate_1,
    gate_2,
    gate_3,
    gate_4,
    gate_5,
    gate_6,
    up_1,
    up_2,
    up_3,
    up_4,
    up_5,
    up_6,
    down_1,
    down_2,
    send,
    recv,
    here,
):
    links = Links(send, recv, here)
    links.greet(links.peers() + [links.x_way, links.y_way, links.core_way])
    sums = halved_sums(links, grad_parts, rightward, leftward)
    for half in sums:
        half.start()
    out = OutputHalf(links, 0, out_parts, middle, out_right, out_left, out_total)
    gate = PlaneScatter(links, gate_1, gate_2, gate_3, gate_4, gate_5, gate_6)
    up = PlaneScatter(links, up_1, up_2, up_3, up_4, up_5, up_6)
    down = PlaneScatter(links, down_1, down_2, None, None, None, None)
    tokens = middle.shape[0]
    spans, lines, keep = halves(tokens), [], []

    def compute(plane, which, rows, right):
        dp = links.dp if which == 1 else links.other_dp
        weight_grad(rows, right, plane.parts, dp)
        plane.between_cores(which)

    def turn(which):
        dp = links.dp if which == 1 else links.other_dp
        turned_low[which] = rows_turned(all_normed, gate_1, dp)

    def compute_down(which):
        dp = links.dp if which == 1 else links.other_dp
        compute(down, which, rows_turned(activated, down_1, dp), all_cot)

    def settle(half, rows_of_half):
        half.finish(grad_middle.at[rows_of_half])

        def body(rows):
            at = pl.ds(pl.multiple_of(rows_of_half.start + rows.start, ROWS), ROWS)
            back = back_rows(grad_middle[at, :], middle[at, :], gain[...])
            grad = cotangent[at, :].astype(jnp.float32) + back
            grad_middle[at, :] = grad
            low[at, :] = grad.astype(jnp.bfloat16)

        each_block(tokens // 2, body)
        line = LineGather(links, low.at[rows_of_half], all_low.at[:, rows_of_half])
        line.send(0)
        lines.append(line)

    later = range(2, links.n_blk - 1)
    turn(0)
    compute(gate, 0, turned_low.at[0], grad_gate_pre)
    sums[0].tick(1)
    turn(1)
    compute(gate, 1, turned_low.at[1], grad_gate_pre)
    for tick in later:
        sums[0].tick(tick)
    gate.across_chips()
    settle(sums[0], spans[0])
    compute(up, 0, turned_low.at[0], grad_up_pre)
    sums[1].tick(1)
    compute(up, 1, turned_low.at[1], grad_up_pre)
    for tick in later:
        sums[1].tick(tick)
    up.across_chips()
    settle(sums[1], spans[1])
    out.sum.start()
    keep.append(links.local(low, all_low.at[links.blk]))
    compute_down(0)
    for step in range(1, links.n_blk - 1):
        for line in lines:
            line.arrived()
            line.send(step)
        if step == 1:
            gate.second_way()
            compute_down(1)
    out.sum.tick(1)
    up.second_way()
    for which in (0, 1):
        down.core_sums(which)
    for dp in range(links.n_dp):
        for row in range(2):
            keep.append(links.local(down.chunk(dp, row, down.core), part_down.at[dp, row]))
    for tick in later:
        out.sum.tick(tick)
    for line in lines:
        line.arrived()

    def into(target):
        def write(block, rows, values):
            target[block, rows, :] = values.astype(target.dtype)

        return write

    gate.result(into(grad_gate))
    up.result(into(grad_up))
    out.write(output)
    out.sum.sent()
    for copy in keep:
        copy.wait()
    for half in sums:
        half.sent()
    links.finish()


def exchange_back(
    grad_parts,
    out_parts,
    middle,
    cotangent,
    gain,
    all_normed,
    grad_gate_pre,
    grad_up_pre,
    activated,
    all_cot,
):
    n_dp, n_blk, n_uly = (lax.axis_size(a) for a in EVERY)
    _, tokens, width = grad_parts.shape
    ff = grad_gate_pre.shape[1]
    depth = width // (n_dp * n_blk * n_uly)
    down_depth = ff // (n_dp * n_uly)
    return pl.pallas_call(
        back_kernel,
        out_shape=[
            jax.ShapeDtypeStruct((tokens // 2, width), jnp.bfloat16),
            jax.ShapeDtypeStruct((tokens, width), jnp.float32),
            jax.ShapeDtypeStruct((n_blk, tokens, width), jnp.bfloat16),
            jax.ShapeDtypeStruct((n_blk, depth, ff), jnp.bfloat16),
            jax.ShapeDtypeStruct((n_blk, depth, ff), jnp.bfloat16),
            jax.ShapeDtypeStruct((n_dp, 2, 1, down_depth, width), jnp.bfloat16),
        ],
        in_specs=[VMEM] * 10,
        out_specs=[VMEM, VMEM, HBM, VMEM, VMEM, HBM],
        scratch_shapes=line_scratch(n_blk, tokens, width)
        + output_scratch(n_blk, tokens, width)
        + [
            pltpu.VMEM((tokens, width), jnp.bfloat16),
            pltpu.VMEM((n_dp, width // n_dp, n_blk * tokens), jnp.bfloat16),
        ]
        + plane_scratch(n_dp, n_blk, n_uly, depth, ff) * 2
        + plane_scratch(n_dp, 1, n_uly, down_depth, width)[:2]
        + semaphores(72),
        compiler_params=kernel_params(3),
    )(
        grad_parts,
        out_parts,
        middle,
        cotangent,
        gain,
        all_normed,
        grad_gate_pre,
        grad_up_pre,
        activated,
        all_cot,
    )


def last_kernel(
    w_qkv,
    hidden,
    grad_middle,
    gain,
    normed,
    grad_qkv,
    heads,
    all_low,
    head_terms,
    out_parts,
    middle,
    grad_hidden,
    grad_w_qkv,
    grad_wo,
    small_sum,
    output,
    grad_parts,
    rightward,
    leftward,
    qkv_1,
    qkv_2,
    qkv_3,
    qkv_4,
    qkv_5,
    qkv_6,
    wo_1,
    wo_2,
    wo_3,
    wo_4,
    wo_5,
    wo_6,
    summed,
    small_in,
    small_total,
    out_right,
    out_left,
    out_total,
    send,
    recv,
    here,
):
    links = Links(send, recv, here)
    links.greet(links.peers() + [links.x_way, links.y_way, links.core_way])
    sums = halved_sums(links, grad_parts, rightward, leftward)
    qkv = PlaneScatter(links, qkv_1, qkv_2, qkv_3, qkv_4, qkv_5, qkv_6)
    out = PlaneScatter(links, wo_1, wo_2, wo_3, wo_4, wo_5, wo_6)

    output_half = OutputHalf(links, 1, out_parts, middle, out_right, out_left, out_total)
    small_in[links.blk] = head_terms[...]
    small_copies = [
        links.to(head_terms, small_in.at[links.blk], device) for device in links.peers()
    ]

    def compute(plane, which, left, right):
        dp = links.dp if which == 1 else links.other_dp
        weight_grad(rows_turned(left, plane.parts, dp), right, plane.parts, dp)
        plane.between_cores(which)

    output_half.sum.start()
    compute(qkv, 0, normed, grad_qkv)
    for copy in small_copies:
        copy.arrived()
    total = small_in[0]
    for blk in range(1, links.n_blk):
        total = total + small_in[blk]
    small_total[0] = total
    pending = links.to(small_total.at[0], small_in.at[links.n_blk], links.x_way)
    compute(qkv, 1, normed, grad_qkv)
    output_half.sum.tick(1)
    pending.arrived()
    small_total[1] = small_total[0] + small_in[links.n_blk]
    pending = links.to(small_total.at[1], small_in.at[links.n_blk + 1], links.y_way)
    tokens = grad_parts.shape[1]
    for column in range(0, w_qkv.shape[0], 512):
        grad_parts[:, :, column : column + 512] = (
            product_right(grad_qkv[...], w_qkv[column : column + 512, :])
            .astype(jnp.bfloat16)
            .reshape(links.n_blk, tokens, 512)
        )
    for half in sums:
        half.start()
    pending.arrived()
    small_total[2] = small_total[1] + small_in[links.n_blk + 1]
    pending = links.to(small_total.at[2], small_in.at[links.n_blk + 2], links.core_way)
    qkv.across_chips()
    for tick in range(2, links.n_blk - 1):
        output_half.sum.tick(tick)
    pending.arrived()
    small_sum[...] = small_total[2] + small_in[links.n_blk + 2]
    sums[0].tick(1)
    compute(out, 0, heads, all_low)
    for tick in range(2, links.n_blk - 1):
        sums[0].tick(tick)
    compute(out, 1, heads, all_low)
    qkv.second_way()
    out.across_chips()
    output_half.write(output)

    def write(block, rows, values):
        summed[block, rows, :] = values.astype(jnp.bfloat16)

    qkv.result(write)
    swapped = []
    for step in range(1, links.n_blk):
        peer = links.peer(step)
        swapped.append(
            links.to(summed.at[peer], grad_w_qkv.at[links.blk], (links.dp, peer, links.uly))
        )
    keep = links.local(summed.at[links.blk], grad_w_qkv.at[links.blk])
    sums[1].tick(1)
    out.second_way()
    for tick in range(2, links.n_blk - 1):
        sums[1].tick(tick)
    for half, rows_of_half in zip(sums, halves(tokens)):
        half.finish(grad_hidden.at[rows_of_half])

    def body(rows):
        back = back_rows(grad_hidden[rows, :], hidden[rows, :].astype(jnp.float32), gain[...])
        grad_hidden[rows, :] = grad_middle[rows, :] + back

    each_block(tokens, body)

    def write_out(block, rows, values):
        grad_wo[block, rows, :] = values

    out.result(write_out)
    output_half.sum.sent()
    for copy in swapped:
        copy.arrived()
    keep.wait()
    for half in sums:
        half.sent()
    links.finish()


def exchange_last(
    w_qkv,
    hidden,
    grad_middle,
    gain,
    normed,
    grad_qkv,
    heads,
    all_low,
    head_terms,
    out_parts,
    middle,
):
    n_dp, _, n_uly = (lax.axis_size(a) for a in EVERY)
    n_blk, tokens, width = out_parts.shape
    columns = grad_qkv.shape[1]
    depth = width // (n_dp * n_blk * n_uly)
    out_depth = heads.shape[1] // (n_dp * n_uly)
    small = head_terms.shape
    return pl.pallas_call(
        last_kernel,
        out_shape=[
            jax.ShapeDtypeStruct((tokens, width), jnp.float32),
            jax.ShapeDtypeStruct((n_blk, depth, columns), jnp.bfloat16),
            jax.ShapeDtypeStruct((1, out_depth, width), jnp.float32),
            jax.ShapeDtypeStruct(small, jnp.float32),
            jax.ShapeDtypeStruct((tokens // 2, width), jnp.bfloat16),
        ],
        in_specs=[VMEM] * 11,
        out_specs=[VMEM, HBM, VMEM, VMEM, VMEM],
        scratch_shapes=[pltpu.VMEM((n_blk, tokens, width), jnp.bfloat16)]
        + line_scratch(n_blk, tokens, width)
        + plane_scratch(n_dp, n_blk, n_uly, depth, columns)
        + plane_scratch(n_dp, 1, n_uly, out_depth, width)
        + [
            pltpu.VMEM((n_blk, depth, columns), jnp.bfloat16),
            pltpu.VMEM((n_blk + 3,) + small, jnp.float32),
            pltpu.VMEM((3,) + small, jnp.float32),
        ]
        + output_scratch(n_blk, tokens, width)
        + semaphores(64),
        compiler_params=kernel_params(4),
    )(
        w_qkv,
        hidden,
        grad_middle,
        gain,
        normed,
        grad_qkv,
        heads,
        all_low,
        head_terms,
        out_parts,
        middle,
    )


def finish_kernel(
    gate,
    up,
    qkv,
    wo,
    wd,
    hidden,
    out_0,
    out_1,
    w_gate,
    w_up,
    w_query,
    key_weight,
    value_weight,
    attn_gain,
    mlp_gain,
    small,
    f_gate,
    f_up,
    f_q,
    f_k,
    f_v,
    f_wo,
    f_wd,
    f_hidden,
    f_out,
    f_attn,
    f_mlp,
    f_q_gain,
    f_k_gain,
):
    n_blk, depth, _ = gate.shape

    def place(source, offset, target):
        width = target.shape[1] // (n_blk * 2)
        for blk in range(n_blk):
            for group in range(2):
                to = (group * n_blk + blk) * width
                at = offset + group * width
                target[:, to : to + width] = source[blk, :, at : at + width].astype(jnp.float32)

    def gain_back(pairs, gain):
        total = jnp.zeros((depth, 128), jnp.float32)
        for weight, grad in pairs:
            for column in range(0, weight.shape[1], 128):
                at = slice(column, column + 128)
                total = total + weight[:, at].astype(jnp.float32) * grad[:, at]
        column = jnp.sum(total, axis=1, keepdims=True)
        square = (depth, depth)
        same = lax.broadcasted_iota(jnp.int32, square, 0) == lax.broadcasted_iota(
            jnp.int32, square, 1
        )
        return jnp.sum(jnp.where(same, column, 0.0), axis=0, keepdims=True) / gain[
            ...
        ].astype(jnp.float32)

    place(gate, 0, f_gate)
    place(up, 0, f_up)
    q_width = f_q.shape[1] // n_blk
    k_width = f_k.shape[1] // n_blk
    place(qkv, 0, f_q)
    place(qkv, q_width, f_k)
    place(qkv, q_width + k_width, f_v)
    f_q_gain[...] = small[0:1, :]
    f_k_gain[...] = small[1:2, :]
    f_wo[...] = wo[0]
    f_wd[...] = wd[0]
    f_hidden[...] = hidden[...]
    half = out_0.shape[0]
    f_out[:half, :] = out_0[...]
    f_out[half:, :] = out_1[...]
    f_attn[...] = gain_back(((w_query, f_q), (key_weight, f_k), (value_weight, f_v)), attn_gain)
    f_mlp[...] = gain_back(((w_gate, f_gate), (w_up, f_up)), mlp_gain)


def finish(gate, up, qkv, wo, wd, hidden, out_0, out_1, weights, gains, small):
    return pl.pallas_call(
        finish_kernel,
        out_shape=[jax.ShapeDtypeStruct(w.shape, jnp.float32) for w in weights]
        + [
            jax.ShapeDtypeStruct(wo.shape[1:], jnp.float32),
            jax.ShapeDtypeStruct(wd.shape[1:], jnp.float32),
            jax.ShapeDtypeStruct(hidden.shape, jnp.float32),
            jax.ShapeDtypeStruct(hidden.shape, jnp.bfloat16),
        ]
        + [jax.ShapeDtypeStruct(gain.shape, jnp.float32) for gain in gains]
        + [jax.ShapeDtypeStruct((1, small.shape[1]), jnp.float32)] * 2,
        in_specs=[VMEM] * 16,
        out_specs=[VMEM] * 13,
        compiler_params=pltpu.CompilerParams(vmem_limit_bytes=62 * MIB),
    )(gate, up, qkv, wo, wd, hidden, out_0, out_1, *weights, *gains, small)


def product(left, right):
    return jnp.dot(left, right, preferred_element_type=jnp.float32)


def shards(
    hidden,
    span_order,
    attn_gain,
    w_query,
    key_weight,
    value_weight,
    w_out,
    q_gain,
    k_gain,
    mlp_gain,
    w_gate,
    w_up,
    w_down,
    cotangent,
):
    seqs, toks, width = hidden.shape
    n_dp, n_blk, n_uly = (lax.axis_size(a) for a in EVERY)
    rows = n_blk * seqs * toks
    bf16 = jnp.bfloat16
    own_hidden = hidden.reshape(seqs * toks, width)
    own_cotangent = cotangent.reshape(seqs * toks, width)

    gain_q, gain_k = q_gain[None, :], k_gain[None, :]
    gain_rows = attn_gain.shape[0]
    own_gains = jnp.pad(jnp.stack([attn_gain, mlp_gain]), ((0, 30), (0, 128 - gain_rows)))
    (
        w_qkv,
        wo,
        all_wg,
        all_wu,
        all_wd,
        cot,
        g_attn,
        g_mlp,
        cosine,
        sine,
        query_pos,
        key_pos,
        heads_flat,
        normed,
        qkv,
        queries,
        key_values,
        lse,
        middle,
        normed2,
    ) = forward(
        span_order,
        own_hidden,
        w_query,
        key_weight,
        value_weight,
        w_out,
        w_gate,
        w_up,
        w_down,
        own_cotangent,
        own_gains,
        gain_q,
        gain_k,
        seqs,
        gain_rows,
    )
    w_qkv = w_qkv.reshape(width, -1)
    wo = wo.reshape(-1, width)
    wg, wu = all_wg.reshape(width, -1), all_wu.reshape(width, -1)
    wd = all_wd.reshape(-1, width)
    cot = cot.reshape(rows, width)
    normed2 = normed2.reshape(rows, width)
    gate_pre = product(normed2, wg)
    up_pre = product(normed2, wu)
    sigmoid_gate = jax.nn.sigmoid(gate_pre)
    activated = (gate_pre * sigmoid_gate * up_pre).astype(bf16)
    out_parts = product(activated, wd).astype(bf16)
    grad_act = product_right(cot, wd)
    grad_gate_pre = (
        grad_act * up_pre * sigmoid_gate * (1.0 + gate_pre * (1.0 - sigmoid_gate))
    ).astype(bf16)
    grad_up_pre = (grad_act * gate_pre * sigmoid_gate).astype(bf16)
    grad_parts = (product_right(grad_gate_pre, wg) + product_right(grad_up_pre, wu)).astype(bf16)
    blocks = (n_blk, seqs * toks, width)
    out_parts = out_parts.reshape(blocks)
    output_0, grad_middle, middle_low, grad_gate, grad_up, part_down = exchange_back(
        grad_parts.reshape(blocks),
        out_parts,
        middle,
        own_cotangent,
        g_mlp,
        normed2,
        grad_gate_pre,
        grad_up_pre,
        activated,
        cot,
    )
    middle_low = middle_low.reshape(rows, width)
    grad_qkv, head_terms, grad_down, grad_gate, grad_up = attend_back(
        middle_low,
        wo,
        queries,
        key_values,
        lse,
        qkv,
        gain_q,
        gain_k,
        cosine,
        sine,
        query_pos,
        key_pos,
        grad_gate,
        grad_up,
        part_down,
    )
    grad_hidden, grad_w_qkv, grad_out, small, output_1 = exchange_last(
        w_qkv,
        own_hidden,
        grad_middle,
        g_attn,
        normed,
        grad_qkv,
        heads_flat,
        middle_low,
        head_terms,
        out_parts,
        middle,
    )
    (
        grad_gate,
        grad_up,
        grad_query,
        grad_key,
        grad_value,
        grad_out,
        grad_down,
        grad_hidden,
        output,
        grad_attn_gain,
        grad_mlp_gain,
        grad_q_gain,
        grad_k_gain,
    ) = finish(
        grad_gate,
        grad_up,
        grad_w_qkv,
        grad_out,
        grad_down,
        grad_hidden,
        output_0,
        output_1,
        (w_gate, w_up, w_query, key_weight, value_weight),
        [g[None, :] for g in (attn_gain, mlp_gain)],
        small,
    )
    return (
        output.reshape(hidden.shape),
        grad_hidden.reshape(hidden.shape),
        grad_attn_gain.reshape(gain_rows),
        grad_query,
        grad_key,
        grad_value,
        grad_out,
        grad_q_gain[0],
        grad_k_gain[0],
        grad_mlp_gain.reshape(gain_rows),
        grad_gate,
        grad_up,
        grad_down,
    )


def solution(mesh):
    n_dp, n_blk, n_uly = (mesh.shape[a] for a in EVERY)
    aligned = (n_dp, n_uly) == (2, 4) and KEY_VALUE_HEADS % (n_dp * n_blk) == 0
    in_specs = (
        TOKENS,
        P(),
        P(EVERY),
        P(EVERY, None),
        P(EVERY, None),
        P(EVERY, None),
        P(EVERY, None),
        P(),
        P(),
        P(EVERY),
        P(EVERY, None),
        P(EVERY, None),
        P(EVERY, None),
        TOKENS,
    )
    out_specs = (
        TOKENS,
        TOKENS,
        P(EVERY),
        P(EVERY, None),
        P(EVERY, None),
        P(EVERY, None),
        P(EVERY, None),
        P(),
        P(),
        P(EVERY),
        P(EVERY, None),
        P(EVERY, None),
        P(EVERY, None),
    )
    return jax.shard_map(
        shards if aligned else shards_general,
        mesh=mesh, in_specs=in_specs, out_specs=out_specs, check_vma=False)
```

```python
import functools
import math

import jax
import jax.numpy as jnp
from jax import lax
from jax.experimental import pallas as pl
from jax.experimental.pallas import tpu as pltpu
from jax.sharding import PartitionSpec as P

QUERY_HEADS = 16
KEY_VALUE_HEADS = 8
HEAD_SIZE = 128


DP, BLK, ULY = "dp", "blk", "uly"
EVERY = (DP, BLK, ULY)
PLANE = (DP, ULY)
TOKENS = P(DP, (BLK, ULY), None)
EQ_KGQD_NKD_TO_KGQN = "kgqd,nkd->kgqn"
EQ_KGQN_KGQD_TO_NKD = "kgqn,kgqd->nkd"
EQ_KGQN_NKD_TO_KGQD = "kgqn,nkd->kgqd"
EQ_KGQN_QKGD_TO_NKD = "kgqn,qkgd->nkd"
EQ_QKGD_NKD_TO_KGQN = "qkgd,nkd->kgqn"
EQ_STD_DE_TO_STE = "std,de->ste"
EQ_STD_DF_TO_STF = "std,df->stf"
EQ_STD_ED_TO_STE = "std,ed->ste"
EQ_STD_FD_TO_STF = "std,fd->stf"
EQ_STD_STE_TO_DE = "std,ste->de"
EQ_STD_STF_TO_DF = "std,stf->df"
EQ_STE_DE_TO_STD = "ste,de->std"
EQ_STE_ED_TO_STD = "ste,ed->std"
EQ_STE_STD_TO_ED = "ste,std->ed"
EQ_STF_DF_TO_STD = "stf,df->std"
EQ_STF_FD_TO_STD = "stf,fd->std"
EQ_STF_STD_TO_FD = "stf,std->fd"

EPSILON = 1e-06
ROPE_BASE = 1000000.0


def rms_scale(source):
    return lax.rsqrt(jnp.mean(source * source, axis=-1, keepdims=True) + EPSILON)


def norm_back(grad_normed, source, norm_scale, gain):
    unit_rows = source * norm_scale
    scaled = grad_normed * gain
    return norm_scale * (scaled - unit_rows * jnp.mean(scaled * unit_rows, axis=-1, keepdims=True))


def angles_of(positions, head_dim):
    freq_steps = jnp.arange(head_dim // 2, dtype=jnp.float32)
    inverse = jnp.exp(freq_steps * (-2.0 * math.log(ROPE_BASE) / head_dim))
    return positions.astype(jnp.float32)[:, None] * inverse[None, :]


def rotate(source, angles, direction):
    half_dim = source.shape[-1] // 2
    cosine = jnp.cos(angles)[:, None, :]
    sine_part = direction * jnp.sin(angles)[:, None, :]
    first_half = source[..., :half_dim]
    second_half = source[..., half_dim:]
    return jnp.concatenate(
        [
            first_half * cosine - second_half * sine_part,
            second_half * cosine + first_half * sine_part,
        ],
        axis=-1,
    )


def positions_of(places, span_order, half_len):
    blocks_of = places // half_len
    block_ids = jnp.arange(span_order.shape[0], dtype=jnp.int32)
    chosen = jnp.sum(
        jnp.where(blocks_of[:, None] == block_ids[None, :], span_order[None, :], 0), axis=1
    )
    return chosen * half_len + places % half_len


def add_rows(buffer, new_rows):
    return buffer + new_rows


def shards_general(
    hidden,
    span_order,
    attn_gain,
    w_query,
    key_weight,
    value_weight,
    w_out,
    q_gain,
    k_gain,
    mlp_gain,
    w_gate,
    w_up,
    w_down,
    cotangent,
):
    sequence_count = hidden.shape[0]
    token_count = hidden.shape[1]
    ulysses_group_size = lax.axis_size(ULY)
    local_q = QUERY_HEADS // ulysses_group_size
    local_key_value = KEY_VALUE_HEADS // ulysses_group_size
    query_group_width = QUERY_HEADS // KEY_VALUE_HEADS
    block_len = token_count * ulysses_group_size
    half_len = block_len // 2
    score_scale = 1.0 / math.sqrt(HEAD_SIZE)
    blk_index = lax.axis_index(BLK)
    uly_index = lax.axis_index(ULY)
    first_place = (blk_index * ulysses_group_size + uly_index) * token_count
    local_angles = angles_of(
        positions_of(first_place + jnp.arange(token_count, dtype=jnp.int32), span_order, half_len),
        HEAD_SIZE,
    )
    query_pos = positions_of(
        blk_index * block_len + jnp.arange(block_len, dtype=jnp.int32), span_order, half_len
    )
    g_attn, wq_all, wk_all, wv_all, wo_all = (
        lax.all_gather(attn_gain, EVERY, axis=0, tiled=True),
        lax.all_gather(w_query, EVERY, axis=0, tiled=True),
        lax.all_gather(key_weight, EVERY, axis=0, tiled=True),
        lax.all_gather(value_weight, EVERY, axis=0, tiled=True),
        lax.all_gather(w_out, EVERY, axis=0, tiled=True),
    )
    source = hidden.astype(jnp.float32)
    first_scale = rms_scale(source)
    normalized_input = (source * first_scale * g_attn.astype(jnp.float32)).astype(jnp.bfloat16)
    q_pre = jnp.einsum(
        EQ_STD_DE_TO_STE, normalized_input, wq_all, preferred_element_type=jnp.float32
    ).reshape(sequence_count, token_count, QUERY_HEADS, HEAD_SIZE)
    key_before_norm = jnp.einsum(
        EQ_STD_DE_TO_STE, normalized_input, wk_all, preferred_element_type=jnp.float32
    ).reshape(sequence_count, token_count, KEY_VALUE_HEADS, HEAD_SIZE)
    value_before_norm = jnp.einsum(
        EQ_STD_DE_TO_STE, normalized_input, wv_all, preferred_element_type=jnp.float32
    ).reshape(sequence_count, token_count, KEY_VALUE_HEADS, HEAD_SIZE)
    q_scale = rms_scale(q_pre)
    k_scale = rms_scale(key_before_norm)
    gain_q = q_gain.astype(jnp.float32)
    gain_k = k_gain.astype(jnp.float32)
    q_rot = rotate(q_pre * q_scale * gain_q, local_angles, 1.0).astype(jnp.bfloat16)
    k_rot = rotate(key_before_norm * k_scale * gain_k, local_angles, 1.0).astype(jnp.bfloat16)
    v_low = value_before_norm.astype(jnp.bfloat16)
    q_heads, k_heads, v_heads = (
        lax.all_to_all(q_rot, ULY, split_axis=2, concat_axis=1, tiled=True),
        lax.all_to_all(k_rot, ULY, split_axis=2, concat_axis=1, tiled=True),
        lax.all_to_all(v_low, ULY, split_axis=2, concat_axis=1, tiled=True),
    )
    q_group = q_heads.reshape(
        sequence_count, block_len, local_key_value, query_group_width, HEAD_SIZE
    )
    stat_shape = (sequence_count, local_key_value, query_group_width, block_len)
    start_state = (
        jnp.full(stat_shape, -1e30, jnp.float32),
        jnp.zeros(stat_shape, jnp.float32),
        jnp.zeros(stat_shape + (HEAD_SIZE,), jnp.float32),
    )
    key_piece = lax.all_gather(k_heads, BLK, axis=1, tiled=True)
    value_piece = lax.all_gather(v_heads, BLK, axis=1, tiled=True)
    key_pos = positions_of(jnp.arange(key_piece.shape[1], dtype=jnp.int32), span_order, half_len)
    allowed = query_pos[:, None] >= key_pos[None, :]

    def attend_one_sequence(members):
        query_rows, key_rows, value_rows, top_seq, total_seq, accum_seq = members
        scores = (
            jnp.einsum(EQ_QKGD_NKD_TO_KGQN, query_rows, key_rows, preferred_element_type=jnp.float32)
            * score_scale
        )
        scores = jnp.where(allowed, scores, -jnp.inf)
        new_top = jnp.maximum(top_seq, jnp.max(scores, axis=-1))
        fading = jnp.exp(top_seq - new_top)
        weights = jnp.exp(scores - new_top[..., None])
        total_seq = total_seq * fading + jnp.sum(weights, axis=-1)
        accum_seq = accum_seq * fading[..., None] + jnp.einsum(
            EQ_KGQN_NKD_TO_KGQD,
            weights.astype(jnp.bfloat16),
            value_rows,
            preferred_element_type=jnp.float32,
        )
        return (new_top, total_seq, accum_seq)

    row_top, row_total, accum = lax.map(
        attend_one_sequence,
        (q_group, key_piece, value_piece, start_state[0], start_state[1], start_state[2]),
    )
    log_total = row_top + jnp.log(row_total)
    attention_output = jnp.transpose(accum / row_total[..., None], (0, 3, 1, 2, 4)).reshape(
        sequence_count, block_len, local_q, HEAD_SIZE
    )
    heads_seq = lax.all_to_all(
        attention_output.astype(jnp.bfloat16), ULY, split_axis=1, concat_axis=2, tiled=True
    )
    heads_flat = heads_seq.reshape(sequence_count, token_count, QUERY_HEADS * HEAD_SIZE)
    middle = source + jnp.einsum(
        EQ_STE_ED_TO_STD, heads_flat, wo_all, preferred_element_type=jnp.float32
    )
    g_mlp, wg_all, wu_all, wd_all = (
        lax.all_gather(mlp_gain, EVERY, axis=0, tiled=True),
        lax.all_gather(w_gate, EVERY, axis=0, tiled=True),
        lax.all_gather(w_up, EVERY, axis=0, tiled=True),
        lax.all_gather(w_down, EVERY, axis=0, tiled=True),
    )
    second_scale = rms_scale(middle)
    gain_mlp = g_mlp.astype(jnp.float32)
    normed2 = (middle * second_scale * gain_mlp).astype(jnp.bfloat16)
    gate_pre = jnp.einsum(EQ_STD_DF_TO_STF, normed2, wg_all, preferred_element_type=jnp.float32)
    up_pre = jnp.einsum(EQ_STD_DF_TO_STF, normed2, wu_all, preferred_element_type=jnp.float32)
    sigmoid_gate = jax.nn.sigmoid(gate_pre)
    activated = (gate_pre * sigmoid_gate * up_pre).astype(jnp.bfloat16)
    result = middle + jnp.einsum(
        EQ_STF_FD_TO_STD, activated, wd_all, preferred_element_type=jnp.float32
    )
    output = result.astype(jnp.bfloat16)
    g_mlp, wg_all, wu_all, wd_all = (
        lax.all_gather(mlp_gain, EVERY, axis=0, tiled=True),
        lax.all_gather(w_gate, EVERY, axis=0, tiled=True),
        lax.all_gather(w_up, EVERY, axis=0, tiled=True),
        lax.all_gather(w_down, EVERY, axis=0, tiled=True),
    )
    gain_mlp = g_mlp.astype(jnp.float32)
    grad_act = jnp.einsum(EQ_STD_FD_TO_STF, cotangent, wd_all, preferred_element_type=jnp.float32)
    grad_gate_pre = (
        grad_act * up_pre * sigmoid_gate * (1.0 + gate_pre * (1.0 - sigmoid_gate))
    ).astype(jnp.bfloat16)
    grad_up_pre = (grad_act * gate_pre * sigmoid_gate).astype(jnp.bfloat16)
    grad_gate = jnp.einsum(
        EQ_STD_STF_TO_DF, normed2, grad_gate_pre, preferred_element_type=jnp.float32
    )
    grad_up = jnp.einsum(EQ_STD_STF_TO_DF, normed2, grad_up_pre, preferred_element_type=jnp.float32)
    grad_normed2 = jnp.einsum(
        EQ_STF_DF_TO_STD, grad_gate_pre, wg_all, preferred_element_type=jnp.float32
    ) + jnp.einsum(EQ_STF_DF_TO_STD, grad_up_pre, wu_all, preferred_element_type=jnp.float32)
    mlp_gain_term = jnp.sum(grad_normed2 * middle * second_scale, axis=(0, 1))
    grad_middle = cotangent.astype(jnp.float32) + norm_back(
        grad_normed2, middle, second_scale, gain_mlp
    )
    grad_mlp_gain, grad_gate, grad_up = (
        lax.psum_scatter(mlp_gain_term, EVERY, scatter_dimension=0, tiled=True),
        lax.psum_scatter(grad_gate, EVERY, scatter_dimension=0, tiled=True),
        lax.psum_scatter(grad_up, EVERY, scatter_dimension=0, tiled=True),
    )
    g_attn, wq_all, wk_all, wv_all, wo_all = (
        lax.all_gather(attn_gain, EVERY, axis=0, tiled=True),
        lax.all_gather(w_query, EVERY, axis=0, tiled=True),
        lax.all_gather(key_weight, EVERY, axis=0, tiled=True),
        lax.all_gather(value_weight, EVERY, axis=0, tiled=True),
        lax.all_gather(w_out, EVERY, axis=0, tiled=True),
    )
    middle_low = grad_middle.astype(jnp.bfloat16)
    grad_out = jnp.einsum(EQ_STE_STD_TO_ED, heads_flat, middle_low, preferred_element_type=jnp.float32)
    grad_heads = (
        jnp.einsum(EQ_STD_ED_TO_STE, middle_low, wo_all, preferred_element_type=jnp.float32)
        .astype(jnp.bfloat16)
        .reshape(sequence_count, token_count, QUERY_HEADS, HEAD_SIZE)
    )
    grad_heads_local = lax.all_to_all(grad_heads, ULY, split_axis=2, concat_axis=1, tiled=True)
    grad_group = jnp.transpose(
        grad_heads_local.reshape(
            sequence_count, block_len, local_key_value, query_group_width, HEAD_SIZE
        ),
        (0, 2, 3, 1, 4),
    )
    delta = jnp.sum(grad_heads_local.astype(jnp.float32) * attention_output, axis=-1)
    delta = jnp.transpose(
        delta.reshape(sequence_count, block_len, local_key_value, query_group_width), (0, 2, 3, 1)
    )
    seq_length = block_len * lax.axis_size(BLK)
    zero_keys = jnp.zeros((sequence_count, seq_length, local_key_value, HEAD_SIZE), jnp.float32)
    back_state = (jnp.zeros(stat_shape + (HEAD_SIZE,), jnp.float32), zero_keys, zero_keys)
    key_piece = lax.all_gather(k_heads, BLK, axis=1, tiled=True)
    value_piece = lax.all_gather(v_heads, BLK, axis=1, tiled=True)
    key_pos = positions_of(jnp.arange(key_piece.shape[1], dtype=jnp.int32), span_order, half_len)
    back_allowed = query_pos[:, None] >= key_pos[None, :]

    def back_one_sequence(members):
        query_rows, grad_rows, lse_seq, delta_seq, key_rows, value_rows, dq_seq, dk_seq, dv_seq = (
            members
        )
        scores = (
            jnp.einsum(EQ_QKGD_NKD_TO_KGQN, query_rows, key_rows, preferred_element_type=jnp.float32)
            * score_scale
        )
        scores = jnp.where(back_allowed, scores, -jnp.inf)
        probs = jnp.exp(scores - lse_seq[..., None])
        grad_values = jnp.einsum(
            EQ_KGQN_KGQD_TO_NKD,
            probs.astype(jnp.bfloat16),
            grad_rows,
            preferred_element_type=jnp.float32,
        )
        grad_probs = jnp.einsum(
            EQ_KGQD_NKD_TO_KGQN, grad_rows, value_rows, preferred_element_type=jnp.float32
        )
        grad_scores = (probs * (grad_probs - delta_seq[..., None])).astype(jnp.bfloat16)
        dq_seq = dq_seq + score_scale * jnp.einsum(
            EQ_KGQN_NKD_TO_KGQD, grad_scores, key_rows, preferred_element_type=jnp.float32
        )
        grad_keys = score_scale * jnp.einsum(
            EQ_KGQN_QKGD_TO_NKD, grad_scores, query_rows, preferred_element_type=jnp.float32
        )
        return (dq_seq, add_rows(dk_seq, grad_keys), add_rows(dv_seq, grad_values))

    grad_q_group, grad_k_whole, grad_v_whole = lax.map(
        back_one_sequence,
        (
            q_group,
            grad_group,
            log_total,
            delta,
            key_piece,
            value_piece,
            back_state[0],
            back_state[1],
            back_state[2],
        ),
    )
    grad_k_block, grad_v_block = (
        lax.psum_scatter(
            grad_k_whole.astype(jnp.bfloat16), BLK, scatter_dimension=1, tiled=True
        ).astype(jnp.float32),
        lax.psum_scatter(
            grad_v_whole.astype(jnp.bfloat16), BLK, scatter_dimension=1, tiled=True
        ).astype(jnp.float32),
    )
    grad_q_block = jnp.transpose(grad_q_group, (0, 3, 1, 2, 4)).reshape(
        sequence_count, block_len, local_q, HEAD_SIZE
    )
    grad_q_seq, grad_k_seq, value_sequence_gradient = (
        lax.all_to_all(
            grad_q_block.astype(jnp.bfloat16), ULY, split_axis=1, concat_axis=2, tiled=True
        ).astype(grad_q_block.dtype),
        lax.all_to_all(
            grad_k_block.astype(jnp.bfloat16), ULY, split_axis=1, concat_axis=2, tiled=True
        ).astype(grad_k_block.dtype),
        lax.all_to_all(
            grad_v_block.astype(jnp.bfloat16), ULY, split_axis=1, concat_axis=2, tiled=True
        ).astype(grad_v_block.dtype),
    )
    grad_q_normed = rotate(grad_q_seq, local_angles, -1.0)
    grad_k_normed = rotate(grad_k_seq, local_angles, -1.0)
    q_gain_term = jnp.sum(grad_q_normed * q_pre * q_scale, axis=(0, 1, 2))
    k_gain_term = jnp.sum(grad_k_normed * key_before_norm * k_scale, axis=(0, 1, 2))
    grad_q_pre = (
        norm_back(grad_q_normed, q_pre, q_scale, gain_q)
        .astype(jnp.bfloat16)
        .reshape(sequence_count, token_count, QUERY_HEADS * HEAD_SIZE)
    )
    grad_k_pre = (
        norm_back(grad_k_normed, key_before_norm, k_scale, gain_k)
        .astype(jnp.bfloat16)
        .reshape(sequence_count, token_count, KEY_VALUE_HEADS * HEAD_SIZE)
    )
    value_pre_gradient = value_sequence_gradient.astype(jnp.bfloat16).reshape(
        sequence_count, token_count, KEY_VALUE_HEADS * HEAD_SIZE
    )
    grad_query = jnp.einsum(
        EQ_STD_STE_TO_DE, normalized_input, grad_q_pre, preferred_element_type=jnp.float32
    )
    grad_key = jnp.einsum(
        EQ_STD_STE_TO_DE, normalized_input, grad_k_pre, preferred_element_type=jnp.float32
    )
    grad_value = jnp.einsum(
        EQ_STD_STE_TO_DE, normalized_input, value_pre_gradient, preferred_element_type=jnp.float32
    )
    grad_normed = jnp.einsum(EQ_STE_DE_TO_STD, grad_q_pre, wq_all, preferred_element_type=jnp.float32)
    grad_normed = grad_normed + jnp.einsum(
        EQ_STE_DE_TO_STD, grad_k_pre, wk_all, preferred_element_type=jnp.float32
    )
    grad_normed = grad_normed + jnp.einsum(
        EQ_STE_DE_TO_STD, value_pre_gradient, wv_all, preferred_element_type=jnp.float32
    )
    attn_gain_term = jnp.sum(grad_normed * source * first_scale, axis=(0, 1))
    grad_hidden = grad_middle + norm_back(
        grad_normed, source, first_scale, g_attn.astype(jnp.float32)
    )
    grad_down = jnp.einsum(EQ_STF_STD_TO_FD, activated, cotangent, preferred_element_type=jnp.float32)
    grad_attn_gain, grad_query, grad_key, grad_value, grad_out, grad_down = (
        lax.psum_scatter(attn_gain_term, EVERY, scatter_dimension=0, tiled=True),
        lax.psum_scatter(grad_query, EVERY, scatter_dimension=0, tiled=True),
        lax.psum_scatter(grad_key, EVERY, scatter_dimension=0, tiled=True),
        lax.psum_scatter(grad_value, EVERY, scatter_dimension=0, tiled=True),
        lax.psum_scatter(grad_out, EVERY, scatter_dimension=0, tiled=True),
        lax.psum_scatter(grad_down, EVERY, scatter_dimension=0, tiled=True),
    )
    grad_q_gain, grad_k_gain = lax.psum((q_gain_term, k_gain_term), EVERY)
    return (
        output,
        grad_hidden,
        grad_attn_gain,
        grad_query,
        grad_key,
        grad_value,
        grad_out,
        grad_q_gain,
        grad_k_gain,
        grad_mlp_gain,
        grad_gate,
        grad_up,
        grad_down,
    )


MESH = pl.DeviceIdType.MESH
HBM = pl.BlockSpec(memory_space=pltpu.HBM)
VMEM = pl.BlockSpec(memory_space=pltpu.VMEM)
MIB = 1 << 20


def kernel_params(collective_id, vmem_mib=62):
    return pltpu.CompilerParams(
        collective_id=collective_id, has_side_effects=True, vmem_limit_bytes=vmem_mib * MIB
    )


def semaphores(count, local=16):
    return [
        pltpu.SemaphoreType.DMA((count,)),
        pltpu.SemaphoreType.DMA((count,)),
        pltpu.SemaphoreType.DMA((local,)),
    ]


class Copy:
    def __init__(self, descriptor, sends, receives):
        self.descriptor, self.sends, self.receives = descriptor, sends, receives

    def under(self, condition, action):
        if condition is None:
            action()
        else:
            pl.when(condition)(action)

    def start(self):
        self.under(self.sends, lambda: self.descriptor().start())
        return self

    def sent(self):
        self.under(self.sends, lambda: self.descriptor().wait_send())

    def arrived(self):
        self.under(self.receives, lambda: self.descriptor().wait_recv())


class Links:
    def __init__(self, send, recv, here):
        self.send, self.recv, self.here = send, recv, here
        self.used, self.used_here = 0, 0
        self.copies, self.local_copies = [], []
        self.n_dp, self.n_blk, self.n_uly = (lax.axis_size(a) for a in EVERY)
        self.dp, self.blk, self.uly = (lax.axis_index(a) for a in EVERY)
        self.other_dp = 1 - self.dp
        self.across = lax.rem(self.uly + 2, 4)
        self.twin = self.uly + 1 - 2 * lax.rem(self.uly, 2)
        self.x_way = (self.other_dp, self.blk, self.uly)
        self.y_way = (self.dp, self.blk, self.across)
        self.core_way = (self.dp, self.blk, self.twin)

    def peer(self, step):
        return lax.rem(self.blk + step, self.n_blk)

    def peers(self):
        return [(self.dp, self.peer(k), self.uly) for k in range(1, self.n_blk)]

    def greet(self, devices):
        barrier = pltpu.get_barrier_semaphore()
        for device in devices:
            pl.semaphore_signal(barrier, inc=1, device_id=device, device_id_type=MESH)
        pl.semaphore_wait(barrier, len(devices))

    def remote(self, source, target, device, sends=None, receives=None):
        slot = self.used
        self.used += 1

        def descriptor():
            return pltpu.make_async_remote_copy(
                src_ref=source(),
                dst_ref=target(),
                send_sem=self.send.at[slot],
                recv_sem=self.recv.at[slot],
                device_id=device,
                device_id_type=MESH,
            )

        copy = Copy(descriptor, sends, receives)
        self.copies.append(copy)
        return copy.start()

    def to(self, source, target, device):
        return self.remote(lambda: source, lambda: target, device)

    def local(self, source, target):
        copy = pltpu.make_async_copy(source, target, self.here.at[self.used_here])
        self.used_here += 1
        copy.start()
        self.local_copies.append(copy)
        return copy

    def finish(self):
        for copy in self.copies:
            copy.sent()


class LineGather:
    def __init__(self, links, own, whole):
        self.links, self.own, self.whole = links, own, whole
        self.waiting = []

    def send(self, step):
        links, whole = self.links, self.whole
        blk, last = links.blk, links.n_blk - 1

        def block(index):
            if step == 0:
                return lambda: self.own
            return lambda: whole.at[index]

        self.waiting = [
            links.remote(
                block(blk - step),
                lambda: whole.at[blk - step],
                (links.dp, blk + 1, links.uly),
                jnp.logical_and(blk >= step, blk < last),
                blk >= step + 1,
            ),
            links.remote(
                block(blk + step),
                lambda: whole.at[blk + step],
                (links.dp, blk - 1, links.uly),
                jnp.logical_and(blk + step <= last, blk > 0),
                blk + step + 1 <= last,
            ),
        ]

    def arrived(self):
        for copy in self.waiting:
            copy.arrived()


def halves(tokens):
    return [pl.ds(0, tokens // 2), pl.ds(tokens // 2, tokens // 2)]


class HalvedLine:
    def __init__(self, links, own, whole):
        self.lines = [
            LineGather(links, None if own is None else own.at[rows], whole.at[:, rows])
            for rows in halves(whole.shape[1])
        ]

    def send(self, step):
        for line in self.lines:
            line.send(step)

    def advance(self, step):
        for line in self.lines:
            line.arrived()
            line.send(step)

    def arrived(self):
        for line in self.lines:
            line.arrived()


class PlaneGather:
    def __init__(self, links, at):
        self.links, self.at = links, at

    def start_x(self, own):
        links = self.links
        mine = self.at(links.dp, links.uly)
        self.from_x = links.to(own, mine, links.x_way)
        self.from_core = [links.to(own, mine, links.core_way)]

    def start_y(self, own):
        links = self.links
        self.from_y = links.to(own, self.at(links.dp, links.uly), links.y_way)

    def start(self, own=None):
        own = self.at(self.links.dp, self.links.uly) if own is None else own
        self.start_x(own)
        self.start_y(own)

    def hand_on(self):
        links, at = self.links, self.at
        self.from_x.arrived()
        half = at(links.other_dp, links.uly, 0)
        self.second_y = links.to(half, half, links.y_way)
        self.from_y.arrived()
        half = at(links.dp, links.across, 1)
        self.second_x = links.to(half, half, links.x_way)
        for chunk in (at(links.other_dp, links.uly), at(links.dp, links.across)):
            self.from_core.append(links.to(chunk, chunk, links.core_way))

    def last(self):
        links = self.links
        self.second_y.arrived()
        self.second_x.arrived()
        chunk = self.at(links.other_dp, links.across)
        self.from_core.append(links.to(chunk, chunk, links.core_way))

    def arrived(self):
        for copy in self.from_core:
            copy.arrived()


def rows_of(whole, blocked):
    def at(dp, uly, half=None):
        part = whole.at[dp, :, uly] if blocked else whole.at[dp, uly]
        if half is None:
            return part
        depth = whole.shape[-2] // 2
        rows = pl.ds(half * depth, depth)
        return part.at[:, rows] if blocked else part.at[rows]

    return at


class ColumnSwap:
    def __init__(self, links, pieces):
        self.links, self.pieces = links, pieces
        self.incoming, self.kept = [], []

    def parts(self, blk):
        links = self.links
        for weight, whole, offset in self.pieces:
            width = weight.shape[-1] // links.n_dp // links.n_blk
            for group in range(links.n_dp):
                start = (group * links.n_blk + blk) * width
                yield (
                    weight.at[:, pl.ds(pl.multiple_of(start, 128), width)],
                    whole.at[links.blk, :, pl.ds(offset + group * width, width)],
                )

    def start(self):
        links = self.links
        for step in range(1, links.n_blk):
            device = (links.dp, links.peer(step), links.uly)
            for source, target in self.parts(links.peer(step)):
                self.incoming.append(links.to(source, target, device))
        for source, target in self.parts(links.blk):
            self.kept.append(links.local(source, target))

    def arrived(self):
        for copy in self.kept:
            copy.wait()
        for copy in self.incoming:
            copy.arrived()


def write_positions(links, span_order, toks, cosine, sine, query_pos, key_pos):
    half_len = toks * links.n_uly // 2

    def first(blk, uly):
        chunk = span_order[2 * blk + lax.div(uly, links.n_uly // 2)]
        return chunk * half_len + lax.rem(uly, links.n_uly // 2) * toks

    lane = lax.broadcasted_iota(jnp.int32, (toks, HEAD_SIZE), 1)
    row = lax.broadcasted_iota(jnp.int32, (toks, HEAD_SIZE), 0)
    upper = lane >= HEAD_SIZE // 2
    step = jnp.where(upper, lane - HEAD_SIZE // 2, lane).astype(jnp.float32)
    inverse = jnp.exp(step * (-2.0 * math.log(ROPE_BASE) / HEAD_SIZE))
    for blk in range(links.n_blk):
        angles = (first(blk, links.uly) + row).astype(jnp.float32) * inverse
        at = slice(blk * toks, (blk + 1) * toks)
        cosine[at, :] = jnp.cos(angles)
        turn = jnp.sin(angles)
        sine[at, :] = jnp.where(upper, turn, -turn)
    lane = lax.broadcasted_iota(jnp.int32, query_pos.shape, 1)
    place = jnp.zeros(query_pos.shape, jnp.int32)
    for start in range(0, query_pos.shape[1], toks):
        blk = start // toks % links.n_blk
        here = jnp.logical_and(lane >= start, lane < start + toks)
        place = jnp.where(here, first(blk, links.uly) + lane - start, place)
    query_pos[...] = place
    row = lax.broadcasted_iota(jnp.int32, (toks, 1), 0)
    for uly in range(links.n_uly):
        for blk in range(links.n_blk):
            start = (uly * links.n_blk + blk) * toks
            key_pos[start : start + toks, :] = row + first(blk, jnp.int32(uly))


def write_gains(links, all_gains, size, targets):
    per_row = 128 // size
    for which, target in enumerate(targets):
        for place in range(target.shape[1] // 128):
            pieces = []
            for part in range(per_row):
                device = place * per_row + part
                plane, uly = device // links.n_uly, device % links.n_uly
                gains = all_gains[plane // links.n_blk, plane % links.n_blk, uly]
                pieces.append(gains.astype(jnp.float32)[which : which + 1, :size])
            target[:, place * 128 : (place + 1) * 128] = jnp.concatenate(pieces, axis=1)


ROWS = 32


def each_block(count, body):
    def step(index, carry):
        body(pl.ds(pl.multiple_of(index * ROWS, ROWS), ROWS))
        return carry

    lax.fori_loop(0, count // ROWS, step, 0)


class LineScatter:
    def __init__(self, links, parts, rightward, leftward):
        self.links, self.parts = links, parts
        self.slots = {1: rightward, -1: leftward}
        self.tokens = parts.shape[1]
        self.number = links.used
        self.last = links.n_blk - 1
        links.used += 2 * self.last

    def target(self, step, way):
        return self.last - step if way == 1 else step

    def slot(self, step, way):
        target = self.target(step, way)
        return self.slots[way].at[target - 1 if way == 1 else target]

    def place(self, way):
        return self.links.blk if way == 1 else self.last - self.links.blk

    def copy(self, step, way, source=None):
        links, slot = self.links, self.slot(step, way)
        number = self.number + 2 * step + (1 if way == 1 else 0)
        return pltpu.make_async_remote_copy(
            src_ref=slot if source is None else source,
            dst_ref=slot,
            send_sem=links.send.at[number],
            recv_sem=links.recv.at[number],
            device_id=(links.dp, links.blk + way, links.uly),
            device_id_type=MESH,
        )

    def start(self):
        for step in range(self.last):
            for way in (1, -1):

                @pl.when(self.place(way) == 0)
                def _(step=step, way=way):
                    self.copy(step, way, self.parts.at[self.target(step, way)]).start()

    def tick(self, tick):
        for way in (1, -1):

            @pl.when(jnp.logical_and(self.place(way) >= 1, self.place(way) <= tick))
            def _(way=way):
                step = tick - self.place(way)
                self.copy(step, way).wait_recv()
                slot, target = self.slot(step, way), self.target(step, way)

                def body(rows):
                    slot[rows, :] = slot[rows, :] + self.parts[target, rows, :]

                each_block(self.tokens, body)
                self.copy(step, way).start()

    def finish(self, total):
        blk, last = self.links.blk, self.last

        def start(rows):
            total[rows, :] = self.parts[blk, rows, :].astype(jnp.float32)

        each_block(self.tokens, start)
        for way in (1, -1):

            @pl.when(self.place(way) >= 1)
            def _(way=way):
                step = last - self.place(way)
                self.copy(step, way).wait_recv()
                slot = self.slot(step, way)

                def body(rows):
                    total[rows, :] = total[rows, :] + slot[rows, :].astype(jnp.float32)

                each_block(self.tokens, body)

    def sent(self):
        for step in range(self.last):
            for way in (1, -1):
                beyond = self.place(way) + step < self.last
                pl.when(beyond)(lambda step=step, way=way: self.copy(step, way).wait_send())


def halved_sums(links, parts, rightward, leftward):
    return [
        LineScatter(links, parts.at[:, rows], rightward.at[:, rows], leftward.at[:, rows])
        for rows in halves(parts.shape[1])
    ]


class OutputHalf:
    def __init__(self, links, which, parts, middle, rightward, leftward, total):
        rows = halves(middle.shape[0])[which]
        self.middle, self.total = middle.at[rows], total
        self.sum = LineScatter(links, parts.at[:, rows], rightward, leftward)

    def write(self, output):
        self.sum.finish(self.total)

        def body(rows):
            output[rows, :] = (self.middle[rows, :] + self.total[rows, :]).astype(jnp.bfloat16)

        each_block(self.middle.shape[0], body)


def output_scratch(n_blk, tokens, width):
    return line_scratch(n_blk, tokens // 2, width) + [
        pltpu.VMEM((tokens // 2, width), jnp.float32)
    ]


def line_scratch(n_blk, tokens, width):
    return [pltpu.VMEM((n_blk - 1, tokens, width), jnp.bfloat16)] * 2


class PlaneScatter:
    def __init__(self, links, parts, from_core, from_x, from_y, last_x, last_y):
        self.links, self.parts = links, parts
        self.own_core_only = from_core is None
        self.from_core, self.from_x, self.from_y = from_core, from_x, from_y
        self.last_x, self.last_y = last_x, last_y
        self.core = lax.rem(links.uly, 2)
        self.row = lax.div(links.uly, 2)
        self.depth = parts.shape[3]
        self.core_copies = {}

    def chunk(self, dp, row, core, half=None):
        if self.own_core_only:
            part = self.parts.at[dp, row]
        else:
            part = self.parts.at[dp, :, row * 2 + core]
        if half is None:
            return part
        depth = self.depth // 2
        return part.at[:, pl.ds(half * depth, depth)]

    def add(self, target, source):
        blocks, depth, _ = target.shape
        rows = 32 if depth % 32 == 0 else 16

        def body(index, carry):
            block = lax.div(index, depth // rows)
            at = pl.ds(pl.multiple_of(lax.rem(index, depth // rows) * rows, rows), rows)
            target[block, at, :] = target[block, at, :] + source[block, at, :]
            return carry

        lax.fori_loop(0, blocks * (depth // rows), body, 0)

    def between_cores(self, which):
        links = self.links
        dp = links.dp if which == 1 else links.other_dp
        self.core_copies[which] = [
            links.to(
                self.chunk(dp, row, 1 - self.core), self.from_core.at[which, row], links.core_way
            )
            for row in range(2)
        ]

    def core_sums(self, which):
        links = self.links
        dp = links.dp if which == 1 else links.other_dp
        for row in range(2):
            self.core_copies[which][row].arrived()
            self.add(self.chunk(dp, row, self.core), self.from_core.at[which, row])

    def across_chips(self):
        links = self.links
        if not self.own_core_only:
            self.core_sums(0)
        self.x_copies = [
            links.to(
                self.chunk(links.other_dp, row, self.core, 0), self.from_x.at[row], links.x_way
            )
            for row in range(2)
        ]
        if not self.own_core_only:
            self.core_sums(1)
        self.y_copies = [
            links.to(
                self.chunk(group, 1 - self.row, self.core, 1),
                self.from_y.at[group],
                links.y_way,
            )
            for group in range(links.n_dp)
        ]

    def second_way(self):
        links = self.links
        for row in range(2):
            self.x_copies[row].arrived()
            self.add(self.chunk(links.dp, row, self.core, 0), self.from_x.at[row])
        self.y_last = links.to(
            self.chunk(links.dp, 1 - self.row, self.core, 0), self.last_y, links.y_way
        )
        for group in range(links.n_dp):
            self.y_copies[group].arrived()
            self.add(self.chunk(group, self.row, self.core, 1), self.from_y.at[group])
        self.x_last = links.to(
            self.chunk(links.other_dp, self.row, self.core, 1), self.last_x, links.x_way
        )

    def result(self, write):
        links = self.links
        for half, copy, source in ((0, self.y_last, self.last_y), (1, self.x_last, self.last_x)):
            copy.arrived()
            own = self.chunk(links.dp, self.row, self.core, half)
            blocks, depth, _ = source.shape
            rows = 32 if depth % 32 == 0 else 16

            def body(index, carry, own=own, source=source, half=half, depth=depth, rows=rows):
                block = lax.div(index, depth // rows)
                start = pl.multiple_of(lax.rem(index, depth // rows) * rows, rows)
                at = pl.ds(start, rows)
                value = own[block, at, :].astype(jnp.float32)
                value = value + source[block, at, :].astype(jnp.float32)
                write(block, pl.ds(pl.multiple_of(start + half * depth, rows), rows), value)
                return carry

            lax.fori_loop(0, blocks * (depth // rows), body, 0)


def plane_shapes(n_dp, blocks, n_uly, depth, width):
    return [
        (n_dp, blocks, n_uly, depth, width),
        (n_dp, 2, blocks, depth, width),
        (2, blocks, depth // 2, width),
        (n_dp, blocks, depth // 2, width),
        (blocks, depth // 2, width),
        (blocks, depth // 2, width),
    ]


def plane_scratch(*sizes):
    return [pltpu.VMEM(shape, jnp.bfloat16) for shape in plane_shapes(*sizes)]


def weight_grad(rows, right, parts, dp):
    _, blocks, n_uly, depth, width = parts.shape
    columns = 512

    def body(index, carry):
        at = pl.ds(pl.multiple_of(index * columns, columns), columns)
        part = jnp.dot(rows[...], right[:, at], preferred_element_type=jnp.float32)
        parts[dp, :, :, :, at] = part.astype(jnp.bfloat16).reshape(blocks, n_uly, depth, columns)
        return carry

    lax.fori_loop(0, width // columns, body, 0)


def rows_turned(left, parts, dp):
    count = parts.shape[1] * parts.shape[2] * parts.shape[3]
    return left[:, pl.ds(pl.multiple_of(dp * count, 128), count)].T


def turned(rows, cosine, sine):
    return rows * cosine + pltpu.roll(rows, HEAD_SIZE // 2, axis=1) * sine


def transposed_product(left, right):
    return lax.dot_general(
        left, right, (((0,), (0,)), ((), ())), preferred_element_type=jnp.float32
    )


def product_right(left, right):
    return lax.dot_general(
        left, right, (((1,), (1,)), ((), ())), preferred_element_type=jnp.float32
    )


SCORE_SCALE = 1.0 / math.sqrt(HEAD_SIZE)


def forward_kernel(
    toks,
    gain_rows,
    span_order,
    hidden,
    wq,
    wk,
    wv,
    wo,
    wg,
    wu,
    wd,
    cotangent,
    gains,
    q_gain,
    k_gain,
    all_qkv,
    all_wo,
    all_wg,
    all_wu,
    all_wd,
    all_cot,
    attn_gain,
    mlp_gain,
    cosine,
    sine,
    query_pos,
    key_pos,
    heads,
    normed,
    qkv,
    queries,
    key_values,
    lse,
    middle,
    all_normed,
    all_gains,
    all_hidden,
    near_qkv,
    near_wo,
    parts,
    rightward,
    leftward,
    own_normed,
    send,
    recv,
    here,
):
    links = Links(send, recv, here)
    links.greet(links.peers() + [links.x_way, links.y_way, links.core_way])
    tokens, width = hidden.shape
    spans = halves(tokens)
    q_width, k_width = wq.shape[1] // links.n_blk, wk.shape[1] // links.n_blk
    chunk = all_qkv.at[links.dp, :, links.uly]
    swap = ColumnSwap(
        links, [(wq, chunk, 0), (wk, chunk, q_width), (wv, chunk, q_width + k_width)]
    )
    plane_wo = PlaneGather(links, rows_of(all_wo, False))
    plane_wd = PlaneGather(links, rows_of(all_wd, False))
    plane_qkv = PlaneGather(links, rows_of(all_qkv, True))
    plane_gain = PlaneGather(links, rows_of(all_gains, True))
    swap.start()
    my_gains = all_gains.at[links.dp, links.blk, links.uly]
    gain_swap = [links.to(gains, my_gains, device) for device in links.peers()]
    plane_wo.start(wo)
    line = HalvedLine(links, hidden, all_hidden)
    line.send(0)
    keep = [
        links.local(gains, my_gains),
        links.local(hidden, all_hidden.at[links.blk]),
        links.local(wo, all_wo.at[links.dp, links.uly]),
        links.local(wd, all_wd.at[links.dp, links.uly]),
        links.local(cotangent, all_cot.at[links.blk]),
    ]
    write_positions(links, span_order, toks, cosine, sine, query_pos, key_pos)
    swap.arrived()
    plane_qkv.start()
    keep[0].wait()
    for copy in gain_swap:
        copy.arrived()
    plane_gain.start()
    plane_wd.start(wd)
    plane_wo.hand_on()
    line.advance(1)
    plane_qkv.hand_on()
    plane_gain.hand_on()
    plane_wo.last()
    for step in range(2, links.n_blk - 1):
        line.advance(step)
    pairs = [(wg, all_wg), (wu, all_wu)]
    planes = [PlaneGather(links, rows_of(whole, True)) for _, whole in pairs]
    swaps = [
        ColumnSwap(links, [(weight, whole.at[links.dp, :, links.uly], 0)])
        for weight, whole in pairs
    ]
    for swap in swaps:
        swap.start()
    plane_qkv.last()
    plane_gain.last()
    plane_gain.arrived()
    write_gains(links, all_gains, gain_rows, (attn_gain, mlp_gain))
    for copy in keep[1:]:
        copy.wait()
    plane_wo.arrived()
    plane_qkv.arrived()
    near = [links.local(all_qkv, near_qkv), links.local(all_wo, near_wo)]
    seqs, kv_heads, q_rows, _ = queries.shape
    q_len = key_values.shape[4]
    group = q_rows // q_len
    q_end = kv_heads * group * HEAD_SIZE
    k_end = q_end + kv_heads * HEAD_SIZE

    def norm(seq):
        def body(rows):
            for blk in range(links.n_blk):
                at = pl.ds(pl.multiple_of(seq * toks + rows.start, ROWS), ROWS)
                to = pl.ds(pl.multiple_of(seq * q_len + blk * toks + rows.start, ROWS), ROWS)
                source = all_hidden[blk, at, :].astype(jnp.float32)
                normed[to, :] = (source * rms_scale(source) * attn_gain[...]).astype(
                    jnp.bfloat16
                )

        each_block(toks, body)

    def rotated(seq, column, gain):
        pre = qkv[seq * q_len : (seq + 1) * q_len, column : column + HEAD_SIZE]
        gain = gain[...].astype(jnp.float32)
        return turned(pre * rms_scale(pre) * gain, cosine[...], sine[...]).astype(jnp.bfloat16)

    def project(seq):
        rows = slice(seq * q_len, (seq + 1) * q_len)
        for column in range(0, qkv.shape[1], 512):
            weight = near_qkv[:, :, :, :, column : column + 512].reshape(width, 512)
            qkv[rows, column : column + 512] = jnp.dot(
                normed[rows, :], weight, preferred_element_type=jnp.float32
            )
        for head in range(kv_heads):
            column = head * HEAD_SIZE
            key_values[links.uly, 0, seq, head] = rotated(seq, q_end + column, k_gain)
            key_values[links.uly, 1, seq, head] = qkv[
                rows, k_end + column : k_end + column + HEAD_SIZE
            ].astype(jnp.bfloat16)
        mine = key_values.at[links.uly, :, seq]
        copies = [links.to(mine, mine, way) for way in (links.core_way, links.y_way)]
        for head in range(kv_heads * group):
            at = pl.ds((head % group) * q_len, q_len)
            queries[seq, head // group, at, :] = rotated(seq, head * HEAD_SIZE, q_gain)
        return copies

    def hand_keys(seq, copies):
        copies[1].arrived()
        theirs = key_values.at[links.across, :, seq]
        copies.append(links.to(theirs, theirs, links.core_way))

    def attend(seq, head):
        def over_keys(piece, carry):
            total, mixed = carry
            rows = pl.ds(pl.multiple_of(piece * q_len, q_len), q_len)
            scores = product_right(key_values[piece, 0, seq, head], queries[seq, head])
            weights = jnp.where(
                query_pos[...] >= key_pos[rows, :], jnp.exp(scores * SCORE_SCALE), 0.0
            )
            total = total + jnp.sum(weights, axis=0, keepdims=True)
            mixed = mixed + transposed_product(
                key_values[piece, 1, seq, head], weights.astype(jnp.bfloat16)
            )
            return total, mixed

        total, mixed = lax.fori_loop(
            0,
            links.n_uly,
            over_keys,
            (
                jnp.zeros((1, q_rows), jnp.float32),
                jnp.zeros((HEAD_SIZE, q_rows), jnp.float32),
            ),
        )
        lse[seq * kv_heads + head] = jnp.log(total)
        attended = (mixed / total).T.astype(jnp.bfloat16)
        for member in range(group):
            column = (head * group + member) * HEAD_SIZE
            for blk in range(links.n_blk):
                row = (blk * seqs + seq) * toks
                start = member * q_len + blk * toks
                heads[row : row + toks, column : column + HEAD_SIZE] = attended[
                    start : start + toks, :
                ]

    sums = halved_sums(links, parts, rightward, leftward)
    def out_weight():
        return near_wo[...].reshape(heads.shape[1], width)

    def out_parts(seq):
        mixed = jnp.concatenate(
            [
                heads[(blk * seqs + seq) * toks : (blk * seqs + seq + 1) * toks, :]
                for blk in range(links.n_blk)
            ],
            axis=0,
        )
        for column in range(0, width, 512):
            parts[:, spans[seq], column : column + 512] = (
                jnp.dot(
                    mixed,
                    out_weight()[:, column : column + 512],
                    preferred_element_type=jnp.float32,
                )
                .astype(jnp.bfloat16)
                .reshape(links.n_blk, toks, 512)
            )
        sums[seq].start()

    key_copies = []
    for seq in range(seqs):
        line.lines[seq].arrived()
        norm(seq)
        if seq == 0:
            for copy in near:
                copy.wait()
        key_copies.append(project(seq))
    plane_wd.hand_on()
    hand_keys(0, key_copies[0])
    swaps[0].arrived()
    planes[0].start()
    for copy in (key_copies[0][0], key_copies[0][2]):
        copy.arrived()
    attend(0, 0)
    hand_keys(1, key_copies[1])
    for head in range(1, kv_heads):
        attend(0, head)
    out_parts(0)
    swaps[1].arrived()
    planes[1].start()
    for copy in (key_copies[1][0], key_copies[1][2]):
        copy.arrived()
    attend(1, 0)
    sums[0].tick(1)
    for head in range(1, kv_heads):
        attend(1, head)
    out_parts(1)
    later = range(2, links.n_blk - 1)
    for tick in later:
        sums[0].tick(tick)
    plane_wd.last()
    planes[0].hand_on()
    cot_lines = HalvedLine(links, cotangent, all_cot).lines
    lines = []

    def settle(half, rows_of_half):
        half.finish(middle.at[rows_of_half])

        def body(rows):
            at = pl.ds(pl.multiple_of(rows_of_half.start + rows.start, ROWS), ROWS)
            total = middle[at, :] + all_hidden[links.blk, at, :].astype(jnp.float32)
            middle[at, :] = total
            own_normed[at, :] = (total * rms_scale(total) * mlp_gain[...]).astype(jnp.bfloat16)

        each_block(tokens // 2, body)
        next_line = LineGather(links, own_normed.at[rows_of_half], all_normed.at[:, rows_of_half])
        next_line.send(0)
        lines.append(next_line)

    settle(sums[0], spans[0])
    cot_lines[0].send(0)
    sums[1].tick(1)
    for tick in later:
        sums[1].tick(tick)
    settle(sums[1], spans[1])
    cot_lines[1].send(0)
    last_local = links.local(own_normed, all_normed.at[links.blk])
    planes[1].hand_on()
    planes[0].last()
    for step in range(1, links.n_blk - 1):
        for half in lines + cot_lines:
            half.arrived()
            half.send(step)
    planes[1].last()
    for half in lines + cot_lines:
        half.arrived()
    for plane in [plane_wd] + planes:
        plane.arrived()
    last_local.wait()
    for half in sums:
        half.sent()
    links.finish()


SMEM = pl.BlockSpec(memory_space=pltpu.SMEM)


def forward(
    span_order,
    hidden,
    wq,
    wk,
    wv,
    wo,
    wg,
    wu,
    wd,
    cotangent,
    gains,
    q_gain,
    k_gain,
    seqs,
    gain_rows,
):
    n_dp, n_blk, n_uly = (lax.axis_size(a) for a in EVERY)
    tokens, width = hidden.shape
    toks = tokens // seqs
    rows, q_len = n_blk * tokens, n_blk * toks
    group = QUERY_HEADS // KEY_VALUE_HEADS
    kv_heads = KEY_VALUE_HEADS // n_blk
    q_rows, keys = group * q_len, n_uly * q_len
    columns = (wq.shape[1] + wk.shape[1] + wv.shape[1]) // n_blk
    f32, low, i32 = jnp.float32, jnp.bfloat16, jnp.int32
    ff = wg.shape[1] // n_blk
    far = [
        (n_dp, n_blk, n_uly, wq.shape[0], columns),
        (n_dp, n_uly) + wo.shape,
        (n_dp, n_blk, n_uly, wg.shape[0], ff),
        (n_dp, n_blk, n_uly, wu.shape[0], ff),
        (n_dp, n_uly) + wd.shape,
        (n_blk, tokens, width),
    ]
    near = [
        ((1, width), f32),
        ((1, width), f32),
        ((q_len, HEAD_SIZE), f32),
        ((q_len, HEAD_SIZE), f32),
        ((1, q_rows), i32),
        ((keys, 1), i32),
        ((rows, kv_heads * group * HEAD_SIZE), low),
        ((rows, width), low),
        ((rows, columns), f32),
        ((seqs, kv_heads, q_rows, HEAD_SIZE), low),
        ((n_uly, 2, seqs, kv_heads, q_len, HEAD_SIZE), low),
        ((seqs * kv_heads, 1, q_rows), f32),
        ((tokens, width), f32),
        ((n_blk, tokens, width), low),
    ]
    scratch = [
        ((n_dp, n_blk, n_uly) + gains.shape, low),
        ((n_blk, tokens, width), low),
        (far[0], low),
        (far[1], low),
        ((n_blk, tokens, width), low),
        ((n_blk - 1, tokens, width), low),
        ((n_blk - 1, tokens, width), low),
        ((tokens, width), low),
    ]
    return pl.pallas_call(
        functools.partial(forward_kernel, toks, gain_rows),
        out_shape=[jax.ShapeDtypeStruct(shape, low) for shape in far]
        + [jax.ShapeDtypeStruct(shape, kind) for shape, kind in near],
        in_specs=[SMEM] + [HBM] * 10 + [VMEM] * 2,
        out_specs=[HBM] * len(far) + [VMEM] * len(near),
        scratch_shapes=[pltpu.VMEM(shape, kind) for shape, kind in scratch]
        + semaphores(160, 32),
        compiler_params=kernel_params(0),
    )(span_order, hidden, wq, wk, wv, wo, wg, wu, wd, cotangent, gains, q_gain, k_gain)


def back_rows(grad_normed, source, gain):
    unit = source * rms_scale(source)
    scaled = grad_normed * gain
    return rms_scale(source) * (
        scaled - unit * jnp.mean(scaled * unit, axis=-1, keepdims=True)
    )


def back_kernel(
    grad_parts,
    out_parts,
    middle,
    cotangent,
    gain,
    all_normed,
    grad_gate_pre,
    grad_up_pre,
    activated,
    all_cot,
    output,
    grad_middle,
    all_low,
    grad_gate,
    grad_up,
    part_down,
    rightward,
    leftward,
    out_right,
    out_left,
    out_total,
    low,
    turned_low,
    gate_1,
    gate_2,
    gate_3,
    gate_4,
    gate_5,
    gate_6,
    up_1,
    up_2,
    up_3,
    up_4,
    up_5,
    up_6,
    down_1,
    down_2,
    send,
    recv,
    here,
):
    links = Links(send, recv, here)
    links.greet(links.peers() + [links.x_way, links.y_way, links.core_way])
    sums = halved_sums(links, grad_parts, rightward, leftward)
    for half in sums:
        half.start()
    out = OutputHalf(links, 0, out_parts, middle, out_right, out_left, out_total)
    gate = PlaneScatter(links, gate_1, gate_2, gate_3, gate_4, gate_5, gate_6)
    up = PlaneScatter(links, up_1, up_2, up_3, up_4, up_5, up_6)
    down = PlaneScatter(links, down_1, down_2, None, None, None, None)
    tokens = middle.shape[0]
    spans, lines, keep = halves(tokens), [], []

    def compute(plane, which, rows, right):
        dp = links.dp if which == 1 else links.other_dp
        weight_grad(rows, right, plane.parts, dp)
        plane.between_cores(which)

    def turn(which):
        dp = links.dp if which == 1 else links.other_dp
        turned_low[which] = rows_turned(all_normed, gate_1, dp)

    def compute_down(which):
        dp = links.dp if which == 1 else links.other_dp
        compute(down, which, rows_turned(activated, down_1, dp), all_cot)

    def settle(half, rows_of_half):
        half.finish(grad_middle.at[rows_of_half])

        def body(rows):
            at = pl.ds(pl.multiple_of(rows_of_half.start + rows.start, ROWS), ROWS)
            back = back_rows(grad_middle[at, :], middle[at, :], gain[...])
            grad = cotangent[at, :].astype(jnp.float32) + back
            grad_middle[at, :] = grad
            low[at, :] = grad.astype(jnp.bfloat16)

        each_block(tokens // 2, body)
        line = LineGather(links, low.at[rows_of_half], all_low.at[:, rows_of_half])
        line.send(0)
        lines.append(line)

    later = range(2, links.n_blk - 1)
    turn(0)
    compute(gate, 0, turned_low.at[0], grad_gate_pre)
    sums[0].tick(1)
    turn(1)
    compute(gate, 1, turned_low.at[1], grad_gate_pre)
    for tick in later:
        sums[0].tick(tick)
    gate.across_chips()
    settle(sums[0], spans[0])
    compute(up, 0, turned_low.at[0], grad_up_pre)
    sums[1].tick(1)
    compute(up, 1, turned_low.at[1], grad_up_pre)
    for tick in later:
        sums[1].tick(tick)
    up.across_chips()
    settle(sums[1], spans[1])
    out.sum.start()
    keep.append(links.local(low, all_low.at[links.blk]))
    compute_down(0)
    for step in range(1, links.n_blk - 1):
        for line in lines:
            line.arrived()
            line.send(step)
        if step == 1:
            gate.second_way()
            compute_down(1)
    out.sum.tick(1)
    up.second_way()
    for which in (0, 1):
        down.core_sums(which)
    for dp in range(links.n_dp):
        for row in range(2):
            keep.append(links.local(down.chunk(dp, row, down.core), part_down.at[dp, row]))
    for tick in later:
        out.sum.tick(tick)
    for line in lines:
        line.arrived()

    def into(target):
        def write(block, rows, values):
            target[block, rows, :] = values.astype(target.dtype)

        return write

    gate.result(into(grad_gate))
    up.result(into(grad_up))
    out.write(output)
    out.sum.sent()
    for copy in keep:
        copy.wait()
    for half in sums:
        half.sent()
    links.finish()


def exchange_back(
    grad_parts,
    out_parts,
    middle,
    cotangent,
    gain,
    all_normed,
    grad_gate_pre,
    grad_up_pre,
    activated,
    all_cot,
):
    n_dp, n_blk, n_uly = (lax.axis_size(a) for a in EVERY)
    _, tokens, width = grad_parts.shape
    ff = grad_gate_pre.shape[1]
    depth = width // (n_dp * n_blk * n_uly)
    down_depth = ff // (n_dp * n_uly)
    return pl.pallas_call(
        back_kernel,
        out_shape=[
            jax.ShapeDtypeStruct((tokens // 2, width), jnp.bfloat16),
            jax.ShapeDtypeStruct((tokens, width), jnp.float32),
            jax.ShapeDtypeStruct((n_blk, tokens, width), jnp.bfloat16),
            jax.ShapeDtypeStruct((n_blk, depth, ff), jnp.bfloat16),
            jax.ShapeDtypeStruct((n_blk, depth, ff), jnp.bfloat16),
            jax.ShapeDtypeStruct((n_dp, 2, 1, down_depth, width), jnp.bfloat16),
        ],
        in_specs=[VMEM] * 10,
        out_specs=[VMEM, VMEM, HBM, VMEM, VMEM, HBM],
        scratch_shapes=line_scratch(n_blk, tokens, width)
        + output_scratch(n_blk, tokens, width)
        + [
            pltpu.VMEM((tokens, width), jnp.bfloat16),
            pltpu.VMEM((n_dp, width // n_dp, n_blk * tokens), jnp.bfloat16),
        ]
        + plane_scratch(n_dp, n_blk, n_uly, depth, ff) * 2
        + plane_scratch(n_dp, 1, n_uly, down_depth, width)[:2]
        + semaphores(72),
        compiler_params=kernel_params(3),
    )(
        grad_parts,
        out_parts,
        middle,
        cotangent,
        gain,
        all_normed,
        grad_gate_pre,
        grad_up_pre,
        activated,
        all_cot,
    )


def backward_kernel(
    all_low,
    wo,
    queries,
    key_values,
    lse,
    qkv,
    q_gain,
    k_gain,
    cosine,
    sine,
    query_pos,
    key_pos,
    w_qkv,
    hidden,
    grad_middle,
    gain,
    normed,
    heads,
    out_parts,
    middle,
    grad_gate,
    grad_up,
    part_down,
    grad_hidden,
    grad_wo,
    grad_down,
    small_sum,
    output,
    gate_rows,
    up_rows,
    grad_w_qkv,
    grad_qkv,
    gain_terms,
    grad_heads,
    grad_rows,
    probs,
    grad_probs,
    grad_kv,
    from_core,
    from_across,
    grad_parts,
    rightward,
    leftward,
    summed,
    small_in,
    small_total,
    out_right,
    out_left,
    out_total,
    down_1,
    down_3,
    down_4,
    down_5,
    down_6,
    qkv_1,
    qkv_2,
    qkv_3,
    qkv_4,
    qkv_5,
    qkv_6,
    wo_1,
    wo_2,
    wo_3,
    wo_4,
    wo_5,
    wo_6,
    send,
    recv,
    here,
):
    links = Links(send, recv, here)
    links.greet(links.peers() + [links.x_way, links.y_way, links.core_way])
    tokens = hidden.shape[0]
    spans = halves(tokens)
    output_half = OutputHalf(links, 1, out_parts, middle, out_right, out_left, out_total)
    output_half.sum.start()
    down = PlaneScatter(links, down_1, None, down_3, down_4, down_5, down_6)
    fetch = links.local(part_down, down_1)
    swapped, keep = [], []
    for source, target in ((grad_gate, gate_rows), (grad_up, up_rows)):
        for step in range(1, links.n_blk):
            peer = links.peer(step)
            swapped.append(
                links.to(source.at[peer], target.at[links.blk], (links.dp, peer, links.uly))
            )
        keep.append(links.local(source.at[links.blk], target.at[links.blk]))
    fetch.wait()
    down.across_chips()
    sums = halved_sums(links, grad_parts, rightward, leftward)
    qkv_sums = PlaneScatter(links, qkv_1, qkv_2, qkv_3, qkv_4, qkv_5, qkv_6)
    wo_sums = PlaneScatter(links, wo_1, wo_2, wo_3, wo_4, wo_5, wo_6)
    seqs, kv_heads, q_rows, _ = queries.shape
    q_len = key_values.shape[4]
    group = q_rows // q_len
    toks = q_len // links.n_blk
    q_end = kv_heads * group * HEAD_SIZE
    k_end = q_end + kv_heads * HEAD_SIZE
    gain_terms[...] = jnp.zeros_like(gain_terms)
    later = range(2, links.n_blk - 1)

    def heads_back(seq):
        low = jnp.concatenate(
            [
                all_low[(blk * seqs + seq) * toks : (blk * seqs + seq + 1) * toks, :]
                for blk in range(links.n_blk)
            ],
            axis=0,
        )
        grad_heads[...] = product_right(low, wo[...])
        for head in range(kv_heads * group):
            to = pl.ds((head % group) * q_len, q_len)
            grad_rows[seq, head // group, to, :] = grad_heads[
                :, head * HEAD_SIZE : (head + 1) * HEAD_SIZE
            ].astype(jnp.bfloat16)

    def back_norm(upstream, seq, column, gain, which):
        rows = slice(seq * q_len, (seq + 1) * q_len)
        pre = qkv[rows, column : column + HEAD_SIZE]
        upstream = turned(upstream, cosine[...], -sine[...])
        gain_terms[which : which + 1, :] += jnp.sum(
            upstream * pre * rms_scale(pre), axis=0, keepdims=True
        )
        grad_qkv[rows, column : column + HEAD_SIZE] = back_rows(
            upstream, pre, gain[...].astype(jnp.float32)
        ).astype(jnp.bfloat16)

    def back(seq, head):
        def first(piece, delta):
            rows = pl.ds(pl.multiple_of(piece * q_len, q_len), q_len)
            scores = product_right(key_values[piece, 0, seq, head], queries[seq, head])
            prob = jnp.where(
                query_pos[...] >= key_pos[rows, :],
                jnp.exp(scores * SCORE_SCALE - lse[seq * kv_heads + head]),
                0.0,
            )
            grad_prob = product_right(key_values[piece, 1, seq, head], grad_rows[seq, head])
            probs[rows, :] = prob
            grad_probs[rows, :] = grad_prob
            return delta + jnp.sum(prob * grad_prob, axis=0, keepdims=True)

        delta = lax.fori_loop(0, links.n_uly, first, jnp.zeros((1, q_rows), jnp.float32))

        def second(piece, grad_query):
            rows = pl.ds(pl.multiple_of(piece * q_len, q_len), q_len)
            prob = probs[rows, :]
            grad_score = (prob * (grad_probs[rows, :] - delta)).astype(jnp.bfloat16)
            grad_kv[seq, piece, 0, head] = (
                SCORE_SCALE
                * jnp.dot(grad_score, queries[seq, head], preferred_element_type=jnp.float32)
            ).astype(jnp.bfloat16)
            grad_kv[seq, piece, 1, head] = jnp.dot(
                prob.astype(jnp.bfloat16),
                grad_rows[seq, head],
                preferred_element_type=jnp.float32,
            ).astype(jnp.bfloat16)
            return grad_query + transposed_product(key_values[piece, 0, seq, head], grad_score)

        grad_query = lax.fori_loop(
            0, links.n_uly, second, jnp.zeros((HEAD_SIZE, q_rows), jnp.float32)
        )
        turned_back = (grad_query * SCORE_SCALE).T
        for member in range(group):
            column = (head * group + member) * HEAD_SIZE
            back_norm(
                turned_back[member * q_len : (member + 1) * q_len, :], seq, column, q_gain, 0
            )

    core, line = lax.rem(links.uly, 2), lax.div(links.uly, 2)

    def add(target, source):
        for kind in range(2):
            for head in range(kv_heads):
                target[kind, head] = target[kind, head] + source[kind, head]

    def core_sums(seq):
        return [
            links.to(
                grad_kv.at[seq, row * 2 + 1 - core], from_core.at[seq, row], links.core_way
            )
            for row in range(2)
        ]

    def across_sums(seq, copies):
        for row in range(2):
            copies[row].arrived()
            add(grad_kv.at[seq, row * 2 + core], from_core.at[seq, row])
        return links.to(
            grad_kv.at[seq, (1 - line) * 2 + core], from_across.at[seq], links.y_way
        )

    def own_keys(seq, copy):
        copy.arrived()
        rows = slice(seq * q_len, (seq + 1) * q_len)
        for head in range(kv_heads):
            term = [
                grad_kv[seq, links.uly, kind, head].astype(jnp.float32)
                + from_across[seq, kind, head].astype(jnp.float32)
                for kind in range(2)
            ]
            back_norm(term[0], seq, q_end + head * HEAD_SIZE, k_gain, 1)
            v_at = k_end + head * HEAD_SIZE
            grad_qkv[rows, v_at : v_at + HEAD_SIZE] = term[1].astype(jnp.bfloat16)

    def normed_parts(seq):
        for column in range(0, w_qkv.shape[0], 512):
            grad_parts[:, spans[seq], column : column + 512] = (
                product_right(
                    grad_qkv[seq * q_len : (seq + 1) * q_len, :],
                    w_qkv[column : column + 512, :],
                )
                .astype(jnp.bfloat16)
                .reshape(links.n_blk, toks, 512)
            )
        sums[seq].start()

    def compute(plane, which, left, right):
        dp = links.dp if which == 1 else links.other_dp
        weight_grad(rows_turned(left, plane.parts, dp), right, plane.parts, dp)
        plane.between_cores(which)

    heads_back(0)
    back(0, 0)
    output_half.sum.tick(1)
    for head in range(1, kv_heads):
        back(0, head)
    core_copies = core_sums(0)
    heads_back(1)
    back(1, 0)
    across = across_sums(0, core_copies)
    for tick in later:
        output_half.sum.tick(tick)
    for head in range(1, kv_heads):
        back(1, head)
    core_copies = core_sums(1)
    own_keys(0, across)
    normed_parts(0)
    across = across_sums(1, core_copies)
    down.second_way()
    compute(wo_sums, 0, heads, all_low)
    own_keys(1, across)
    normed_parts(1)
    small_total[0] = gain_terms[...]
    pending = links.to(small_total.at[0], small_in.at[links.n_blk], links.core_way)
    compute(qkv_sums, 0, normed, grad_qkv)
    pending.arrived()
    small_total[1] = small_total[0] + small_in[links.n_blk]
    pending = links.to(small_total.at[1], small_in.at[links.n_blk + 1], links.x_way)
    compute(qkv_sums, 1, normed, grad_qkv)
    pending.arrived()
    small_total[2] = small_total[1] + small_in[links.n_blk + 1]
    pending = links.to(small_total.at[2], small_in.at[links.n_blk + 2], links.y_way)
    sums[0].tick(1)
    qkv_sums.across_chips()
    compute(wo_sums, 1, heads, all_low)
    for tick in later:
        sums[0].tick(tick)
    pending.arrived()
    small_in[links.blk] = small_total[2] + small_in[links.n_blk + 2]
    mine = small_in.at[links.blk]
    small_copies = [links.to(mine, mine, device) for device in links.peers()]
    wo_sums.across_chips()
    sums[1].tick(1)
    qkv_sums.second_way()
    output_half.write(output)

    def settle(seq):
        sums[seq].finish(grad_hidden.at[spans[seq]])

        def body(rows):
            at = pl.ds(pl.multiple_of(spans[seq].start + rows.start, ROWS), ROWS)
            back = back_rows(grad_hidden[at, :], hidden[at, :].astype(jnp.float32), gain[...])
            grad_hidden[at, :] = grad_middle[at, :] + back

        each_block(toks, body)

    def into(target):
        def write(block, rows, values):
            target[block, rows, :] = values.astype(target.dtype)

        return write

    settle(0)
    for tick in later:
        sums[1].tick(tick)
    qkv_sums.result(into(summed))
    for step in range(1, links.n_blk):
        peer = links.peer(step)
        swapped.append(
            links.to(summed.at[peer], grad_w_qkv.at[links.blk], (links.dp, peer, links.uly))
        )
    keep.append(links.local(summed.at[links.blk], grad_w_qkv.at[links.blk]))
    wo_sums.second_way()
    down.result(into(grad_down))
    settle(1)
    wo_sums.result(into(grad_wo))
    for copy in small_copies:
        copy.arrived()
    total = small_in[0]
    for blk in range(1, links.n_blk):
        total = total + small_in[blk]
    small_sum[...] = total
    for copy in swapped:
        copy.arrived()
    for copy in keep:
        copy.wait()
    for half in sums:
        half.sent()
    output_half.sum.sent()
    links.finish()


def backward(
    all_low,
    wo,
    queries,
    key_values,
    lse,
    qkv,
    q_gain,
    k_gain,
    cosine,
    sine,
    query_pos,
    key_pos,
    w_qkv,
    hidden,
    grad_middle,
    gain,
    normed,
    heads,
    out_parts,
    middle,
    grad_gate,
    grad_up,
    part_down,
):
    seqs, kv_heads, q_rows, _ = queries.shape
    n_uly, _, _, _, q_len, _ = key_values.shape
    n_blk, tokens, width = out_parts.shape
    n_dp, _, _, down_depth, _ = part_down.shape
    keys, columns = key_pos.shape[0], qkv.shape[1]
    depth = width // (n_dp * n_blk * n_uly)
    out_depth = heads.shape[1] // (n_dp * n_uly)
    f32, low = jnp.float32, jnp.bfloat16
    small = (8, HEAD_SIZE)
    outs = [
        ((tokens, width), f32),
        ((1, out_depth, width), f32),
        ((1, down_depth, width), f32),
        (small, f32),
        ((tokens // 2, width), low),
        (grad_gate.shape, low),
        (grad_up.shape, low),
        ((n_blk, depth, columns), low),
    ]
    scratch = [
        (qkv.shape, low),
        (small, f32),
        ((q_len, heads.shape[1]), f32),
        (queries.shape, low),
        ((keys, q_rows), f32),
        ((keys, q_rows), f32),
        ((seqs, n_uly, 2, kv_heads, q_len, HEAD_SIZE), low),
        ((seqs, 2, 2, kv_heads, q_len, HEAD_SIZE), low),
        ((seqs, 2, kv_heads, q_len, HEAD_SIZE), low),
        (out_parts.shape, low),
        ((n_blk - 1, tokens, width), low),
        ((n_blk - 1, tokens, width), low),
        ((n_blk, depth, columns), low),
        ((n_blk + 3,) + small, f32),
        ((3,) + small, f32),
    ]
    down = [part_down.shape] + plane_shapes(n_dp, 1, n_uly, down_depth, width)[2:]
    return pl.pallas_call(
        backward_kernel,
        out_shape=[jax.ShapeDtypeStruct(shape, kind) for shape, kind in outs],
        in_specs=[VMEM] * 20 + [HBM] * 3,
        out_specs=[VMEM] * 5 + [HBM] * 3,
        scratch_shapes=[pltpu.VMEM(shape, kind) for shape, kind in scratch]
        + output_scratch(n_blk, tokens, width)
        + [pltpu.VMEM(shape, low) for shape in down]
        + plane_scratch(n_dp, n_blk, n_uly, depth, columns)
        + plane_scratch(n_dp, 1, n_uly, out_depth, width)
        + semaphores(96),
        compiler_params=kernel_params(4),
    )(
        all_low,
        wo,
        queries,
        key_values,
        lse,
        qkv,
        q_gain,
        k_gain,
        cosine,
        sine,
        query_pos,
        key_pos,
        w_qkv,
        hidden,
        grad_middle,
        gain,
        normed,
        heads,
        out_parts,
        middle,
        grad_gate,
        grad_up,
        part_down,
    )


def finish_kernel(
    gate,
    up,
    qkv,
    wo,
    wd,
    hidden,
    out_0,
    out_1,
    w_gate,
    w_up,
    w_query,
    key_weight,
    value_weight,
    attn_gain,
    mlp_gain,
    small,
    f_gate,
    f_up,
    f_q,
    f_k,
    f_v,
    f_wo,
    f_wd,
    f_hidden,
    f_out,
    f_attn,
    f_mlp,
    f_q_gain,
    f_k_gain,
):
    n_blk, depth, _ = gate.shape

    def place(source, offset, target):
        width = target.shape[1] // (n_blk * 2)
        for blk in range(n_blk):
            for group in range(2):
                to = (group * n_blk + blk) * width
                at = offset + group * width
                target[:, to : to + width] = source[blk, :, at : at + width].astype(jnp.float32)

    def gain_back(pairs, gain):
        total = jnp.zeros((depth, 128), jnp.float32)
        for weight, grad in pairs:
            for column in range(0, weight.shape[1], 128):
                at = slice(column, column + 128)
                total = total + weight[:, at].astype(jnp.float32) * grad[:, at]
        column = jnp.sum(total, axis=1, keepdims=True)
        square = (depth, depth)
        same = lax.broadcasted_iota(jnp.int32, square, 0) == lax.broadcasted_iota(
            jnp.int32, square, 1
        )
        return jnp.sum(jnp.where(same, column, 0.0), axis=0, keepdims=True) / gain[
            ...
        ].astype(jnp.float32)

    place(gate, 0, f_gate)
    place(up, 0, f_up)
    q_width = f_q.shape[1] // n_blk
    k_width = f_k.shape[1] // n_blk
    place(qkv, 0, f_q)
    place(qkv, q_width, f_k)
    place(qkv, q_width + k_width, f_v)
    f_q_gain[...] = small[0:1, :]
    f_k_gain[...] = small[1:2, :]
    f_wo[...] = wo[0]
    f_wd[...] = wd[0]
    f_hidden[...] = hidden[...]
    half = out_0.shape[0]
    f_out[:half, :] = out_0[...]
    f_out[half:, :] = out_1[...]
    f_attn[...] = gain_back(((w_query, f_q), (key_weight, f_k), (value_weight, f_v)), attn_gain)
    f_mlp[...] = gain_back(((w_gate, f_gate), (w_up, f_up)), mlp_gain)


def finish(gate, up, qkv, wo, wd, hidden, out_0, out_1, weights, gains, small):
    return pl.pallas_call(
        finish_kernel,
        out_shape=[jax.ShapeDtypeStruct(w.shape, jnp.float32) for w in weights]
        + [
            jax.ShapeDtypeStruct(wo.shape[1:], jnp.float32),
            jax.ShapeDtypeStruct(wd.shape[1:], jnp.float32),
            jax.ShapeDtypeStruct(hidden.shape, jnp.float32),
            jax.ShapeDtypeStruct(hidden.shape, jnp.bfloat16),
        ]
        + [jax.ShapeDtypeStruct(gain.shape, jnp.float32) for gain in gains]
        + [jax.ShapeDtypeStruct((1, small.shape[1]), jnp.float32)] * 2,
        in_specs=[VMEM] * 16,
        out_specs=[VMEM] * 13,
        compiler_params=pltpu.CompilerParams(vmem_limit_bytes=62 * MIB),
    )(gate, up, qkv, wo, wd, hidden, out_0, out_1, *weights, *gains, small)


def product(left, right):
    return jnp.dot(left, right, preferred_element_type=jnp.float32)


def shards(
    hidden,
    span_order,
    attn_gain,
    w_query,
    key_weight,
    value_weight,
    w_out,
    q_gain,
    k_gain,
    mlp_gain,
    w_gate,
    w_up,
    w_down,
    cotangent,
):
    seqs, toks, width = hidden.shape
    n_dp, n_blk, n_uly = (lax.axis_size(a) for a in EVERY)
    rows = n_blk * seqs * toks
    bf16 = jnp.bfloat16
    own_hidden = hidden.reshape(seqs * toks, width)
    own_cotangent = cotangent.reshape(seqs * toks, width)

    gain_q, gain_k = q_gain[None, :], k_gain[None, :]
    gain_rows = attn_gain.shape[0]
    own_gains = jnp.pad(jnp.stack([attn_gain, mlp_gain]), ((0, 30), (0, 128 - gain_rows)))
    (
        w_qkv,
        wo,
        all_wg,
        all_wu,
        all_wd,
        cot,
        g_attn,
        g_mlp,
        cosine,
        sine,
        query_pos,
        key_pos,
        heads_flat,
        normed,
        qkv,
        queries,
        key_values,
        lse,
        middle,
        normed2,
    ) = forward(
        span_order,
        own_hidden,
        w_query,
        key_weight,
        value_weight,
        w_out,
        w_gate,
        w_up,
        w_down,
        own_cotangent,
        own_gains,
        gain_q,
        gain_k,
        seqs,
        gain_rows,
    )
    w_qkv = w_qkv.reshape(width, -1)
    wo = wo.reshape(-1, width)
    wg, wu = all_wg.reshape(width, -1), all_wu.reshape(width, -1)
    wd = all_wd.reshape(-1, width)
    cot = cot.reshape(rows, width)
    normed2 = normed2.reshape(rows, width)
    gate_pre = product(normed2, wg)
    up_pre = product(normed2, wu)
    sigmoid_gate = jax.nn.sigmoid(gate_pre)
    activated = (gate_pre * sigmoid_gate * up_pre).astype(bf16)
    out_parts = product(activated, wd).astype(bf16)
    grad_act = product_right(cot, wd)
    grad_gate_pre = (
        grad_act * up_pre * sigmoid_gate * (1.0 + gate_pre * (1.0 - sigmoid_gate))
    ).astype(bf16)
    grad_up_pre = (grad_act * gate_pre * sigmoid_gate).astype(bf16)
    grad_parts = (product_right(grad_gate_pre, wg) + product_right(grad_up_pre, wu)).astype(bf16)
    blocks = (n_blk, seqs * toks, width)
    out_parts = out_parts.reshape(blocks)
    output_0, grad_middle, middle_low, grad_gate, grad_up, part_down = exchange_back(
        grad_parts.reshape(blocks),
        out_parts,
        middle,
        own_cotangent,
        g_mlp,
        normed2,
        grad_gate_pre,
        grad_up_pre,
        activated,
        cot,
    )
    middle_low = middle_low.reshape(rows, width)
    (
        grad_hidden,
        grad_out,
        grad_down,
        small,
        output_1,
        grad_gate,
        grad_up,
        grad_w_qkv,
    ) = backward(
        middle_low,
        wo,
        queries,
        key_values,
        lse,
        qkv,
        gain_q,
        gain_k,
        cosine,
        sine,
        query_pos,
        key_pos,
        w_qkv,
        own_hidden,
        grad_middle,
        g_attn,
        normed,
        heads_flat,
        out_parts,
        middle,
        grad_gate,
        grad_up,
        part_down,
    )
    (
        grad_gate,
        grad_up,
        grad_query,
        grad_key,
        grad_value,
        grad_out,
        grad_down,
        grad_hidden,
        output,
        grad_attn_gain,
        grad_mlp_gain,
        grad_q_gain,
        grad_k_gain,
    ) = finish(
        grad_gate,
        grad_up,
        grad_w_qkv,
        grad_out,
        grad_down,
        grad_hidden,
        output_0,
        output_1,
        (w_gate, w_up, w_query, key_weight, value_weight),
        [g[None, :] for g in (attn_gain, mlp_gain)],
        small,
    )
    return (
        output.reshape(hidden.shape),
        grad_hidden.reshape(hidden.shape),
        grad_attn_gain.reshape(gain_rows),
        grad_query,
        grad_key,
        grad_value,
        grad_out,
        grad_q_gain[0],
        grad_k_gain[0],
        grad_mlp_gain.reshape(gain_rows),
        grad_gate,
        grad_up,
        grad_down,
    )


def solution(mesh):
    n_dp, n_blk, n_uly = (mesh.shape[a] for a in EVERY)
    aligned = (n_dp, n_uly) == (2, 4) and KEY_VALUE_HEADS % (n_dp * n_blk) == 0
    in_specs = (
        TOKENS,
        P(),
        P(EVERY),
        P(EVERY, None),
        P(EVERY, None),
        P(EVERY, None),
        P(EVERY, None),
        P(),
        P(),
        P(EVERY),
        P(EVERY, None),
        P(EVERY, None),
        P(EVERY, None),
        TOKENS,
    )
    out_specs = (
        TOKENS,
        TOKENS,
        P(EVERY),
        P(EVERY, None),
        P(EVERY, None),
        P(EVERY, None),
        P(EVERY, None),
        P(),
        P(),
        P(EVERY),
        P(EVERY, None),
        P(EVERY, None),
        P(EVERY, None),
    )
    return jax.shard_map(
        shards if aligned else shards_general,
        mesh=mesh, in_specs=in_specs, out_specs=out_specs, check_vma=False)
```

```python
import functools
import math

import jax
import jax.numpy as jnp
from jax import lax
from jax.experimental import pallas as pl
from jax.experimental.pallas import tpu as pltpu
from jax.sharding import PartitionSpec as P

QUERY_HEADS = 16
KEY_VALUE_HEADS = 8
HEAD_SIZE = 128


DP, BLK, ULY = "dp", "blk", "uly"
EVERY = (DP, BLK, ULY)
PLANE = (DP, ULY)
TOKENS = P(DP, (BLK, ULY), None)
EQ_KGQD_NKD_TO_KGQN = "kgqd,nkd->kgqn"
EQ_KGQN_KGQD_TO_NKD = "kgqn,kgqd->nkd"
EQ_KGQN_NKD_TO_KGQD = "kgqn,nkd->kgqd"
EQ_KGQN_QKGD_TO_NKD = "kgqn,qkgd->nkd"
EQ_QKGD_NKD_TO_KGQN = "qkgd,nkd->kgqn"
EQ_STD_DE_TO_STE = "std,de->ste"
EQ_STD_DF_TO_STF = "std,df->stf"
EQ_STD_ED_TO_STE = "std,ed->ste"
EQ_STD_FD_TO_STF = "std,fd->stf"
EQ_STD_STE_TO_DE = "std,ste->de"
EQ_STD_STF_TO_DF = "std,stf->df"
EQ_STE_DE_TO_STD = "ste,de->std"
EQ_STE_ED_TO_STD = "ste,ed->std"
EQ_STE_STD_TO_ED = "ste,std->ed"
EQ_STF_DF_TO_STD = "stf,df->std"
EQ_STF_FD_TO_STD = "stf,fd->std"
EQ_STF_STD_TO_FD = "stf,std->fd"

EPSILON = 1e-06
ROPE_BASE = 1000000.0


def rms_scale(source):
    return lax.rsqrt(jnp.mean(source * source, axis=-1, keepdims=True) + EPSILON)


def norm_back(grad_normed, source, norm_scale, gain):
    unit_rows = source * norm_scale
    scaled = grad_normed * gain
    return norm_scale * (scaled - unit_rows * jnp.mean(scaled * unit_rows, axis=-1, keepdims=True))


def angles_of(positions, head_dim):
    freq_steps = jnp.arange(head_dim // 2, dtype=jnp.float32)
    inverse = jnp.exp(freq_steps * (-2.0 * math.log(ROPE_BASE) / head_dim))
    return positions.astype(jnp.float32)[:, None] * inverse[None, :]


def rotate(source, angles, direction):
    half_dim = source.shape[-1] // 2
    cosine = jnp.cos(angles)[:, None, :]
    sine_part = direction * jnp.sin(angles)[:, None, :]
    first_half = source[..., :half_dim]
    second_half = source[..., half_dim:]
    return jnp.concatenate(
        [
            first_half * cosine - second_half * sine_part,
            second_half * cosine + first_half * sine_part,
        ],
        axis=-1,
    )


def positions_of(places, span_order, half_len):
    blocks_of = places // half_len
    block_ids = jnp.arange(span_order.shape[0], dtype=jnp.int32)
    chosen = jnp.sum(
        jnp.where(blocks_of[:, None] == block_ids[None, :], span_order[None, :], 0), axis=1
    )
    return chosen * half_len + places % half_len


def add_rows(buffer, new_rows):
    return buffer + new_rows


def shards_general(
    hidden,
    span_order,
    attn_gain,
    w_query,
    key_weight,
    value_weight,
    w_out,
    q_gain,
    k_gain,
    mlp_gain,
    w_gate,
    w_up,
    w_down,
    cotangent,
):
    sequence_count = hidden.shape[0]
    token_count = hidden.shape[1]
    ulysses_group_size = lax.axis_size(ULY)
    local_q = QUERY_HEADS // ulysses_group_size
    local_key_value = KEY_VALUE_HEADS // ulysses_group_size
    query_group_width = QUERY_HEADS // KEY_VALUE_HEADS
    block_len = token_count * ulysses_group_size
    half_len = block_len // 2
    score_scale = 1.0 / math.sqrt(HEAD_SIZE)
    blk_index = lax.axis_index(BLK)
    uly_index = lax.axis_index(ULY)
    first_place = (blk_index * ulysses_group_size + uly_index) * token_count
    local_angles = angles_of(
        positions_of(first_place + jnp.arange(token_count, dtype=jnp.int32), span_order, half_len),
        HEAD_SIZE,
    )
    query_pos = positions_of(
        blk_index * block_len + jnp.arange(block_len, dtype=jnp.int32), span_order, half_len
    )
    g_attn, wq_all, wk_all, wv_all, wo_all = (
        lax.all_gather(attn_gain, EVERY, axis=0, tiled=True),
        lax.all_gather(w_query, EVERY, axis=0, tiled=True),
        lax.all_gather(key_weight, EVERY, axis=0, tiled=True),
        lax.all_gather(value_weight, EVERY, axis=0, tiled=True),
        lax.all_gather(w_out, EVERY, axis=0, tiled=True),
    )
    source = hidden.astype(jnp.float32)
    first_scale = rms_scale(source)
    normalized_input = (source * first_scale * g_attn.astype(jnp.float32)).astype(jnp.bfloat16)
    q_pre = jnp.einsum(
        EQ_STD_DE_TO_STE, normalized_input, wq_all, preferred_element_type=jnp.float32
    ).reshape(sequence_count, token_count, QUERY_HEADS, HEAD_SIZE)
    key_before_norm = jnp.einsum(
        EQ_STD_DE_TO_STE, normalized_input, wk_all, preferred_element_type=jnp.float32
    ).reshape(sequence_count, token_count, KEY_VALUE_HEADS, HEAD_SIZE)
    value_before_norm = jnp.einsum(
        EQ_STD_DE_TO_STE, normalized_input, wv_all, preferred_element_type=jnp.float32
    ).reshape(sequence_count, token_count, KEY_VALUE_HEADS, HEAD_SIZE)
    q_scale = rms_scale(q_pre)
    k_scale = rms_scale(key_before_norm)
    gain_q = q_gain.astype(jnp.float32)
    gain_k = k_gain.astype(jnp.float32)
    q_rot = rotate(q_pre * q_scale * gain_q, local_angles, 1.0).astype(jnp.bfloat16)
    k_rot = rotate(key_before_norm * k_scale * gain_k, local_angles, 1.0).astype(jnp.bfloat16)
    v_low = value_before_norm.astype(jnp.bfloat16)
    q_heads, k_heads, v_heads = (
        lax.all_to_all(q_rot, ULY, split_axis=2, concat_axis=1, tiled=True),
        lax.all_to_all(k_rot, ULY, split_axis=2, concat_axis=1, tiled=True),
        lax.all_to_all(v_low, ULY, split_axis=2, concat_axis=1, tiled=True),
    )
    q_group = q_heads.reshape(
        sequence_count, block_len, local_key_value, query_group_width, HEAD_SIZE
    )
    stat_shape = (sequence_count, local_key_value, query_group_width, block_len)
    start_state = (
        jnp.full(stat_shape, -1e30, jnp.float32),
        jnp.zeros(stat_shape, jnp.float32),
        jnp.zeros(stat_shape + (HEAD_SIZE,), jnp.float32),
    )
    key_piece = lax.all_gather(k_heads, BLK, axis=1, tiled=True)
    value_piece = lax.all_gather(v_heads, BLK, axis=1, tiled=True)
    key_pos = positions_of(jnp.arange(key_piece.shape[1], dtype=jnp.int32), span_order, half_len)
    allowed = query_pos[:, None] >= key_pos[None, :]

    def attend_one_sequence(members):
        query_rows, key_rows, value_rows, top_seq, total_seq, accum_seq = members
        scores = (
            jnp.einsum(EQ_QKGD_NKD_TO_KGQN, query_rows, key_rows, preferred_element_type=jnp.float32)
            * score_scale
        )
        scores = jnp.where(allowed, scores, -jnp.inf)
        new_top = jnp.maximum(top_seq, jnp.max(scores, axis=-1))
        fading = jnp.exp(top_seq - new_top)
        weights = jnp.exp(scores - new_top[..., None])
        total_seq = total_seq * fading + jnp.sum(weights, axis=-1)
        accum_seq = accum_seq * fading[..., None] + jnp.einsum(
            EQ_KGQN_NKD_TO_KGQD,
            weights.astype(jnp.bfloat16),
            value_rows,
            preferred_element_type=jnp.float32,
        )
        return (new_top, total_seq, accum_seq)

    row_top, row_total, accum = lax.map(
        attend_one_sequence,
        (q_group, key_piece, value_piece, start_state[0], start_state[1], start_state[2]),
    )
    log_total = row_top + jnp.log(row_total)
    attention_output = jnp.transpose(accum / row_total[..., None], (0, 3, 1, 2, 4)).reshape(
        sequence_count, block_len, local_q, HEAD_SIZE
    )
    heads_seq = lax.all_to_all(
        attention_output.astype(jnp.bfloat16), ULY, split_axis=1, concat_axis=2, tiled=True
    )
    heads_flat = heads_seq.reshape(sequence_count, token_count, QUERY_HEADS * HEAD_SIZE)
    middle = source + jnp.einsum(
        EQ_STE_ED_TO_STD, heads_flat, wo_all, preferred_element_type=jnp.float32
    )
    g_mlp, wg_all, wu_all, wd_all = (
        lax.all_gather(mlp_gain, EVERY, axis=0, tiled=True),
        lax.all_gather(w_gate, EVERY, axis=0, tiled=True),
        lax.all_gather(w_up, EVERY, axis=0, tiled=True),
        lax.all_gather(w_down, EVERY, axis=0, tiled=True),
    )
    second_scale = rms_scale(middle)
    gain_mlp = g_mlp.astype(jnp.float32)
    normed2 = (middle * second_scale * gain_mlp).astype(jnp.bfloat16)
    gate_pre = jnp.einsum(EQ_STD_DF_TO_STF, normed2, wg_all, preferred_element_type=jnp.float32)
    up_pre = jnp.einsum(EQ_STD_DF_TO_STF, normed2, wu_all, preferred_element_type=jnp.float32)
    sigmoid_gate = jax.nn.sigmoid(gate_pre)
    activated = (gate_pre * sigmoid_gate * up_pre).astype(jnp.bfloat16)
    result = middle + jnp.einsum(
        EQ_STF_FD_TO_STD, activated, wd_all, preferred_element_type=jnp.float32
    )
    output = result.astype(jnp.bfloat16)
    g_mlp, wg_all, wu_all, wd_all = (
        lax.all_gather(mlp_gain, EVERY, axis=0, tiled=True),
        lax.all_gather(w_gate, EVERY, axis=0, tiled=True),
        lax.all_gather(w_up, EVERY, axis=0, tiled=True),
        lax.all_gather(w_down, EVERY, axis=0, tiled=True),
    )
    gain_mlp = g_mlp.astype(jnp.float32)
    grad_act = jnp.einsum(EQ_STD_FD_TO_STF, cotangent, wd_all, preferred_element_type=jnp.float32)
    grad_gate_pre = (
        grad_act * up_pre * sigmoid_gate * (1.0 + gate_pre * (1.0 - sigmoid_gate))
    ).astype(jnp.bfloat16)
    grad_up_pre = (grad_act * gate_pre * sigmoid_gate).astype(jnp.bfloat16)
    grad_gate = jnp.einsum(
        EQ_STD_STF_TO_DF, normed2, grad_gate_pre, preferred_element_type=jnp.float32
    )
    grad_up = jnp.einsum(EQ_STD_STF_TO_DF, normed2, grad_up_pre, preferred_element_type=jnp.float32)
    grad_normed2 = jnp.einsum(
        EQ_STF_DF_TO_STD, grad_gate_pre, wg_all, preferred_element_type=jnp.float32
    ) + jnp.einsum(EQ_STF_DF_TO_STD, grad_up_pre, wu_all, preferred_element_type=jnp.float32)
    mlp_gain_term = jnp.sum(grad_normed2 * middle * second_scale, axis=(0, 1))
    grad_middle = cotangent.astype(jnp.float32) + norm_back(
        grad_normed2, middle, second_scale, gain_mlp
    )
    grad_mlp_gain, grad_gate, grad_up = (
        lax.psum_scatter(mlp_gain_term, EVERY, scatter_dimension=0, tiled=True),
        lax.psum_scatter(grad_gate, EVERY, scatter_dimension=0, tiled=True),
        lax.psum_scatter(grad_up, EVERY, scatter_dimension=0, tiled=True),
    )
    g_attn, wq_all, wk_all, wv_all, wo_all = (
        lax.all_gather(attn_gain, EVERY, axis=0, tiled=True),
        lax.all_gather(w_query, EVERY, axis=0, tiled=True),
        lax.all_gather(key_weight, EVERY, axis=0, tiled=True),
        lax.all_gather(value_weight, EVERY, axis=0, tiled=True),
        lax.all_gather(w_out, EVERY, axis=0, tiled=True),
    )
    middle_low = grad_middle.astype(jnp.bfloat16)
    grad_out = jnp.einsum(EQ_STE_STD_TO_ED, heads_flat, middle_low, preferred_element_type=jnp.float32)
    grad_heads = (
        jnp.einsum(EQ_STD_ED_TO_STE, middle_low, wo_all, preferred_element_type=jnp.float32)
        .astype(jnp.bfloat16)
        .reshape(sequence_count, token_count, QUERY_HEADS, HEAD_SIZE)
    )
    grad_heads_local = lax.all_to_all(grad_heads, ULY, split_axis=2, concat_axis=1, tiled=True)
    grad_group = jnp.transpose(
        grad_heads_local.reshape(
            sequence_count, block_len, local_key_value, query_group_width, HEAD_SIZE
        ),
        (0, 2, 3, 1, 4),
    )
    delta = jnp.sum(grad_heads_local.astype(jnp.float32) * attention_output, axis=-1)
    delta = jnp.transpose(
        delta.reshape(sequence_count, block_len, local_key_value, query_group_width), (0, 2, 3, 1)
    )
    seq_length = block_len * lax.axis_size(BLK)
    zero_keys = jnp.zeros((sequence_count, seq_length, local_key_value, HEAD_SIZE), jnp.float32)
    back_state = (jnp.zeros(stat_shape + (HEAD_SIZE,), jnp.float32), zero_keys, zero_keys)
    key_piece = lax.all_gather(k_heads, BLK, axis=1, tiled=True)
    value_piece = lax.all_gather(v_heads, BLK, axis=1, tiled=True)
    key_pos = positions_of(jnp.arange(key_piece.shape[1], dtype=jnp.int32), span_order, half_len)
    back_allowed = query_pos[:, None] >= key_pos[None, :]

    def back_one_sequence(members):
        query_rows, grad_rows, lse_seq, delta_seq, key_rows, value_rows, dq_seq, dk_seq, dv_seq = (
            members
        )
        scores = (
            jnp.einsum(EQ_QKGD_NKD_TO_KGQN, query_rows, key_rows, preferred_element_type=jnp.float32)
            * score_scale
        )
        scores = jnp.where(back_allowed, scores, -jnp.inf)
        probs = jnp.exp(scores - lse_seq[..., None])
        grad_values = jnp.einsum(
            EQ_KGQN_KGQD_TO_NKD,
            probs.astype(jnp.bfloat16),
            grad_rows,
            preferred_element_type=jnp.float32,
        )
        grad_probs = jnp.einsum(
            EQ_KGQD_NKD_TO_KGQN, grad_rows, value_rows, preferred_element_type=jnp.float32
        )
        grad_scores = (probs * (grad_probs - delta_seq[..., None])).astype(jnp.bfloat16)
        dq_seq = dq_seq + score_scale * jnp.einsum(
            EQ_KGQN_NKD_TO_KGQD, grad_scores, key_rows, preferred_element_type=jnp.float32
        )
        grad_keys = score_scale * jnp.einsum(
            EQ_KGQN_QKGD_TO_NKD, grad_scores, query_rows, preferred_element_type=jnp.float32
        )
        return (dq_seq, add_rows(dk_seq, grad_keys), add_rows(dv_seq, grad_values))

    grad_q_group, grad_k_whole, grad_v_whole = lax.map(
        back_one_sequence,
        (
            q_group,
            grad_group,
            log_total,
            delta,
            key_piece,
            value_piece,
            back_state[0],
            back_state[1],
            back_state[2],
        ),
    )
    grad_k_block, grad_v_block = (
        lax.psum_scatter(
            grad_k_whole.astype(jnp.bfloat16), BLK, scatter_dimension=1, tiled=True
        ).astype(jnp.float32),
        lax.psum_scatter(
            grad_v_whole.astype(jnp.bfloat16), BLK, scatter_dimension=1, tiled=True
        ).astype(jnp.float32),
    )
    grad_q_block = jnp.transpose(grad_q_group, (0, 3, 1, 2, 4)).reshape(
        sequence_count, block_len, local_q, HEAD_SIZE
    )
    grad_q_seq, grad_k_seq, value_sequence_gradient = (
        lax.all_to_all(
            grad_q_block.astype(jnp.bfloat16), ULY, split_axis=1, concat_axis=2, tiled=True
        ).astype(grad_q_block.dtype),
        lax.all_to_all(
            grad_k_block.astype(jnp.bfloat16), ULY, split_axis=1, concat_axis=2, tiled=True
        ).astype(grad_k_block.dtype),
        lax.all_to_all(
            grad_v_block.astype(jnp.bfloat16), ULY, split_axis=1, concat_axis=2, tiled=True
        ).astype(grad_v_block.dtype),
    )
    grad_q_normed = rotate(grad_q_seq, local_angles, -1.0)
    grad_k_normed = rotate(grad_k_seq, local_angles, -1.0)
    q_gain_term = jnp.sum(grad_q_normed * q_pre * q_scale, axis=(0, 1, 2))
    k_gain_term = jnp.sum(grad_k_normed * key_before_norm * k_scale, axis=(0, 1, 2))
    grad_q_pre = (
        norm_back(grad_q_normed, q_pre, q_scale, gain_q)
        .astype(jnp.bfloat16)
        .reshape(sequence_count, token_count, QUERY_HEADS * HEAD_SIZE)
    )
    grad_k_pre = (
        norm_back(grad_k_normed, key_before_norm, k_scale, gain_k)
        .astype(jnp.bfloat16)
        .reshape(sequence_count, token_count, KEY_VALUE_HEADS * HEAD_SIZE)
    )
    value_pre_gradient = value_sequence_gradient.astype(jnp.bfloat16).reshape(
        sequence_count, token_count, KEY_VALUE_HEADS * HEAD_SIZE
    )
    grad_query = jnp.einsum(
        EQ_STD_STE_TO_DE, normalized_input, grad_q_pre, preferred_element_type=jnp.float32
    )
    grad_key = jnp.einsum(
        EQ_STD_STE_TO_DE, normalized_input, grad_k_pre, preferred_element_type=jnp.float32
    )
    grad_value = jnp.einsum(
        EQ_STD_STE_TO_DE, normalized_input, value_pre_gradient, preferred_element_type=jnp.float32
    )
    grad_normed = jnp.einsum(EQ_STE_DE_TO_STD, grad_q_pre, wq_all, preferred_element_type=jnp.float32)
    grad_normed = grad_normed + jnp.einsum(
        EQ_STE_DE_TO_STD, grad_k_pre, wk_all, preferred_element_type=jnp.float32
    )
    grad_normed = grad_normed + jnp.einsum(
        EQ_STE_DE_TO_STD, value_pre_gradient, wv_all, preferred_element_type=jnp.float32
    )
    attn_gain_term = jnp.sum(grad_normed * source * first_scale, axis=(0, 1))
    grad_hidden = grad_middle + norm_back(
        grad_normed, source, first_scale, g_attn.astype(jnp.float32)
    )
    grad_down = jnp.einsum(EQ_STF_STD_TO_FD, activated, cotangent, preferred_element_type=jnp.float32)
    grad_attn_gain, grad_query, grad_key, grad_value, grad_out, grad_down = (
        lax.psum_scatter(attn_gain_term, EVERY, scatter_dimension=0, tiled=True),
        lax.psum_scatter(grad_query, EVERY, scatter_dimension=0, tiled=True),
        lax.psum_scatter(grad_key, EVERY, scatter_dimension=0, tiled=True),
        lax.psum_scatter(grad_value, EVERY, scatter_dimension=0, tiled=True),
        lax.psum_scatter(grad_out, EVERY, scatter_dimension=0, tiled=True),
        lax.psum_scatter(grad_down, EVERY, scatter_dimension=0, tiled=True),
    )
    grad_q_gain, grad_k_gain = lax.psum((q_gain_term, k_gain_term), EVERY)
    return (
        output,
        grad_hidden,
        grad_attn_gain,
        grad_query,
        grad_key,
        grad_value,
        grad_out,
        grad_q_gain,
        grad_k_gain,
        grad_mlp_gain,
        grad_gate,
        grad_up,
        grad_down,
    )


MESH = pl.DeviceIdType.MESH
HBM = pl.BlockSpec(memory_space=pltpu.HBM)
VMEM = pl.BlockSpec(memory_space=pltpu.VMEM)
MIB = 1 << 20


def kernel_params(collective_id, vmem_mib=62):
    return pltpu.CompilerParams(
        collective_id=collective_id, has_side_effects=True, vmem_limit_bytes=vmem_mib * MIB
    )


def semaphores(count, local=16):
    return [
        pltpu.SemaphoreType.DMA((count,)),
        pltpu.SemaphoreType.DMA((count,)),
        pltpu.SemaphoreType.DMA((local,)),
    ]


class Copy:
    def __init__(self, descriptor, sends, receives):
        self.descriptor, self.sends, self.receives = descriptor, sends, receives

    def under(self, condition, action):
        if condition is None:
            action()
        else:
            pl.when(condition)(action)

    def start(self):
        self.under(self.sends, lambda: self.descriptor().start())
        return self

    def sent(self):
        self.under(self.sends, lambda: self.descriptor().wait_send())

    def arrived(self):
        self.under(self.receives, lambda: self.descriptor().wait_recv())


class Links:
    def __init__(self, send, recv, here):
        self.send, self.recv, self.here = send, recv, here
        self.used, self.used_here = 0, 0
        self.copies, self.local_copies = [], []
        self.n_dp, self.n_blk, self.n_uly = (lax.axis_size(a) for a in EVERY)
        self.dp, self.blk, self.uly = (lax.axis_index(a) for a in EVERY)
        self.other_dp = 1 - self.dp
        self.across = lax.rem(self.uly + 2, 4)
        self.twin = self.uly + 1 - 2 * lax.rem(self.uly, 2)
        self.x_way = (self.other_dp, self.blk, self.uly)
        self.y_way = (self.dp, self.blk, self.across)
        self.core_way = (self.dp, self.blk, self.twin)

    def peer(self, step):
        return lax.rem(self.blk + step, self.n_blk)

    def peers(self):
        return [(self.dp, self.peer(k), self.uly) for k in range(1, self.n_blk)]

    def far_first(self):
        last = self.n_blk - 1
        orders = [
            sorted((p for p in range(self.n_blk) if p != b), key=lambda p, b=b: -abs(p - b))
            for b in range(self.n_blk)
        ]
        for b, order in enumerate(orders):
            ways = [[p for p in order if p > b], [p for p in order if p < b]]
            ways.sort(key=lambda way: -len(way))
            merged = []
            while ways[0] or ways[1]:
                for way in ways:
                    if way:
                        merged.append(way.pop(0))
            orders[b] = merged
        peers = []
        for turn in range(last):
            peer = jnp.int32(0)
            for b, order in enumerate(orders):
                peer = jnp.where(self.blk == b, order[turn], peer)
            peers.append(peer)
        return peers

    def swap(self, pieces_for):
        base, count = self.used, 0
        for peer in self.far_first():
            pieces = pieces_for(peer)
            count = len(pieces)
            distance = lax.rem(peer - self.blk + self.n_blk, self.n_blk) - 1
            for number, (source, target) in enumerate(pieces):
                self.swap_copy(base + distance * count + number, source, target, peer).start()
        self.used = base + (self.n_blk - 1) * count
        waits = []
        for slot in range(base, self.used):
            source, target = pieces_for(self.blk)[(slot - base) % count]

            def descriptor(slot=slot, source=source, target=target):
                return self.swap_copy(slot, source, target, self.peer(1))

            copy = Copy(descriptor, None, None)
            self.copies.append(copy)
            waits.append(copy)
        return waits

    def swap_copy(self, slot, source, target, peer):
        return pltpu.make_async_remote_copy(
            src_ref=source,
            dst_ref=target,
            send_sem=self.send.at[slot],
            recv_sem=self.recv.at[slot],
            device_id=(self.dp, peer, self.uly),
            device_id_type=MESH,
        )

    def greet(self, devices):
        barrier = pltpu.get_barrier_semaphore()
        for device in devices:
            pl.semaphore_signal(barrier, inc=1, device_id=device, device_id_type=MESH)
        pl.semaphore_wait(barrier, len(devices))

    def remote(self, source, target, device, sends=None, receives=None):
        slot = self.used
        self.used += 1

        def descriptor():
            return pltpu.make_async_remote_copy(
                src_ref=source(),
                dst_ref=target(),
                send_sem=self.send.at[slot],
                recv_sem=self.recv.at[slot],
                device_id=device,
                device_id_type=MESH,
            )

        copy = Copy(descriptor, sends, receives)
        self.copies.append(copy)
        return copy.start()

    def to(self, source, target, device):
        return self.remote(lambda: source, lambda: target, device)

    def local(self, source, target):
        copy = pltpu.make_async_copy(source, target, self.here.at[self.used_here])
        self.used_here += 1
        copy.start()
        self.local_copies.append(copy)
        return copy

    def finish(self):
        for copy in self.copies:
            copy.sent()


class LineGather:
    def __init__(self, links, own, whole):
        self.links, self.own, self.whole = links, own, whole
        self.waiting = []

    def send(self, step):
        links, whole = self.links, self.whole
        blk, last = links.blk, links.n_blk - 1

        def block(index):
            if step == 0:
                return lambda: self.own
            return lambda: whole.at[index]

        self.waiting = [
            links.remote(
                block(blk - step),
                lambda: whole.at[blk - step],
                (links.dp, blk + 1, links.uly),
                jnp.logical_and(blk >= step, blk < last),
                blk >= step + 1,
            ),
            links.remote(
                block(blk + step),
                lambda: whole.at[blk + step],
                (links.dp, blk - 1, links.uly),
                jnp.logical_and(blk + step <= last, blk > 0),
                blk + step + 1 <= last,
            ),
        ]

    def arrived(self):
        for copy in self.waiting:
            copy.arrived()


def halves(tokens):
    return [pl.ds(0, tokens // 2), pl.ds(tokens // 2, tokens // 2)]


class HalvedLine:
    def __init__(self, links, own, whole):
        self.lines = [
            LineGather(links, None if own is None else own.at[rows], whole.at[:, rows])
            for rows in halves(whole.shape[1])
        ]

    def send(self, step):
        for line in self.lines:
            line.send(step)

    def advance(self, step):
        for line in self.lines:
            line.arrived()
            line.send(step)

    def arrived(self):
        for line in self.lines:
            line.arrived()


class PlaneGather:
    def __init__(self, links, at):
        self.links, self.at = links, at

    def start_x(self, own):
        links = self.links
        mine = self.at(links.dp, links.uly)
        self.from_x = links.to(own, mine, links.x_way)
        self.from_core = [links.to(own, mine, links.core_way)]

    def start_y(self, own):
        links = self.links
        self.from_y = links.to(own, self.at(links.dp, links.uly), links.y_way)

    def start(self, own=None):
        own = self.at(self.links.dp, self.links.uly) if own is None else own
        self.start_x(own)
        self.start_y(own)

    def hand_on(self):
        links, at = self.links, self.at
        self.from_x.arrived()
        half = at(links.other_dp, links.uly, 0)
        self.second_y = links.to(half, half, links.y_way)
        self.from_y.arrived()
        half = at(links.dp, links.across, 1)
        self.second_x = links.to(half, half, links.x_way)
        for chunk in (at(links.other_dp, links.uly), at(links.dp, links.across)):
            self.from_core.append(links.to(chunk, chunk, links.core_way))

    def last(self):
        links = self.links
        self.second_y.arrived()
        self.second_x.arrived()
        chunk = self.at(links.other_dp, links.across)
        self.from_core.append(links.to(chunk, chunk, links.core_way))

    def arrived(self):
        for copy in self.from_core:
            copy.arrived()


def rows_of(whole, blocked):
    def at(dp, uly, half=None):
        part = whole.at[dp, :, uly] if blocked else whole.at[dp, uly]
        if half is None:
            return part
        depth = whole.shape[-2] // 2
        rows = pl.ds(half * depth, depth)
        return part.at[:, rows] if blocked else part.at[rows]

    return at


class ColumnSwap:
    def __init__(self, links, pieces):
        self.links, self.pieces = links, pieces
        self.incoming, self.kept = [], []

    def parts(self, blk):
        links = self.links
        for weight, whole, offset in self.pieces:
            width = weight.shape[-1] // links.n_dp // links.n_blk
            for group in range(links.n_dp):
                start = (group * links.n_blk + blk) * width
                yield (
                    weight.at[:, pl.ds(pl.multiple_of(start, 128), width)],
                    whole.at[links.blk, :, pl.ds(offset + group * width, width)],
                )

    def start(self):
        links = self.links
        self.incoming = links.swap(lambda peer: list(self.parts(peer)))
        for source, target in self.parts(links.blk):
            self.kept.append(links.local(source, target))

    def arrived(self):
        for copy in self.kept:
            copy.wait()
        for copy in self.incoming:
            copy.arrived()


def write_positions(links, span_order, toks, cosine, sine, query_pos, key_pos):
    half_len = toks * links.n_uly // 2

    def first(blk, uly):
        chunk = span_order[2 * blk + lax.div(uly, links.n_uly // 2)]
        return chunk * half_len + lax.rem(uly, links.n_uly // 2) * toks

    lane = lax.broadcasted_iota(jnp.int32, (toks, HEAD_SIZE), 1)
    row = lax.broadcasted_iota(jnp.int32, (toks, HEAD_SIZE), 0)
    upper = lane >= HEAD_SIZE // 2
    step = jnp.where(upper, lane - HEAD_SIZE // 2, lane).astype(jnp.float32)
    inverse = jnp.exp(step * (-2.0 * math.log(ROPE_BASE) / HEAD_SIZE))
    for blk in range(links.n_blk):
        angles = (first(blk, links.uly) + row).astype(jnp.float32) * inverse
        at = slice(blk * toks, (blk + 1) * toks)
        cosine[at, :] = jnp.cos(angles)
        turn = jnp.sin(angles)
        sine[at, :] = jnp.where(upper, turn, -turn)
    lane = lax.broadcasted_iota(jnp.int32, query_pos.shape, 1)
    place = jnp.zeros(query_pos.shape, jnp.int32)
    for start in range(0, query_pos.shape[1], toks):
        blk = start // toks % links.n_blk
        here = jnp.logical_and(lane >= start, lane < start + toks)
        place = jnp.where(here, first(blk, links.uly) + lane - start, place)
    query_pos[...] = place
    row = lax.broadcasted_iota(jnp.int32, (toks, 1), 0)
    for uly in range(links.n_uly):
        for blk in range(links.n_blk):
            start = (uly * links.n_blk + blk) * toks
            key_pos[start : start + toks, :] = row + first(blk, jnp.int32(uly))


def write_gains(links, all_gains, size, targets):
    per_row = 128 // size
    for which, target in enumerate(targets):
        for place in range(target.shape[1] // 128):
            pieces = []
            for part in range(per_row):
                device = place * per_row + part
                plane, uly = device // links.n_uly, device % links.n_uly
                gains = all_gains[plane // links.n_blk, plane % links.n_blk, uly]
                pieces.append(gains.astype(jnp.float32)[which : which + 1, :size])
            target[:, place * 128 : (place + 1) * 128] = jnp.concatenate(pieces, axis=1)


ROWS = 32


def each_block(count, body):
    def step(index, carry):
        body(pl.ds(pl.multiple_of(index * ROWS, ROWS), ROWS))
        return carry

    lax.fori_loop(0, count // ROWS, step, 0)


class LineScatter:
    def __init__(self, links, parts, rightward, leftward):
        self.links, self.parts = links, parts
        self.slots = {1: rightward, -1: leftward}
        self.tokens = parts.shape[1]
        self.number = links.used
        self.last = links.n_blk - 1
        links.used += 2 * self.last

    def target(self, step, way):
        return self.last - step if way == 1 else step

    def slot(self, step, way):
        target = self.target(step, way)
        return self.slots[way].at[target - 1 if way == 1 else target]

    def place(self, way):
        return self.links.blk if way == 1 else self.last - self.links.blk

    def copy(self, step, way, source=None):
        links, slot = self.links, self.slot(step, way)
        number = self.number + 2 * step + (1 if way == 1 else 0)
        return pltpu.make_async_remote_copy(
            src_ref=slot if source is None else source,
            dst_ref=slot,
            send_sem=links.send.at[number],
            recv_sem=links.recv.at[number],
            device_id=(links.dp, links.blk + way, links.uly),
            device_id_type=MESH,
        )

    def start(self):
        for step in range(self.last):
            for way in (1, -1):

                @pl.when(self.place(way) == 0)
                def _(step=step, way=way):
                    self.copy(step, way, self.parts.at[self.target(step, way)]).start()

    def tick(self, tick):
        for way in (1, -1):

            @pl.when(jnp.logical_and(self.place(way) >= 1, self.place(way) <= tick))
            def _(way=way):
                step = tick - self.place(way)
                self.copy(step, way).wait_recv()
                slot, target = self.slot(step, way), self.target(step, way)

                def body(rows):
                    slot[rows, :] = slot[rows, :] + self.parts[target, rows, :]

                each_block(self.tokens, body)
                self.copy(step, way).start()

    def finish(self, total):
        blk, last = self.links.blk, self.last

        def start(rows):
            total[rows, :] = self.parts[blk, rows, :].astype(jnp.float32)

        each_block(self.tokens, start)
        for way in (1, -1):

            @pl.when(self.place(way) >= 1)
            def _(way=way):
                step = last - self.place(way)
                self.copy(step, way).wait_recv()
                slot = self.slot(step, way)

                def body(rows):
                    total[rows, :] = total[rows, :] + slot[rows, :].astype(jnp.float32)

                each_block(self.tokens, body)

    def sent(self):
        for step in range(self.last):
            for way in (1, -1):
                beyond = self.place(way) + step < self.last
                pl.when(beyond)(lambda step=step, way=way: self.copy(step, way).wait_send())


def halved_sums(links, parts, rightward, leftward):
    return [
        LineScatter(links, parts.at[:, rows], rightward.at[:, rows], leftward.at[:, rows])
        for rows in halves(parts.shape[1])
    ]


class OutputHalf:
    def __init__(self, links, which, parts, middle, rightward, leftward, total):
        rows = halves(middle.shape[0])[which]
        self.middle, self.total = middle.at[rows], total
        self.sum = LineScatter(links, parts.at[:, rows], rightward, leftward)

    def write(self, output):
        self.sum.finish(self.total)

        def body(rows):
            output[rows, :] = (self.middle[rows, :] + self.total[rows, :]).astype(jnp.bfloat16)

        each_block(self.middle.shape[0], body)


def output_scratch(n_blk, tokens, width):
    return line_scratch(n_blk, tokens // 2, width) + [
        pltpu.VMEM((tokens // 2, width), jnp.float32)
    ]


def line_scratch(n_blk, tokens, width):
    return [pltpu.VMEM((n_blk - 1, tokens, width), jnp.bfloat16)] * 2


class PlaneScatter:
    def __init__(self, links, parts, from_core, from_x, from_y, last_x, last_y):
        self.links, self.parts = links, parts
        self.own_core_only = from_core is None
        self.from_core, self.from_x, self.from_y = from_core, from_x, from_y
        self.last_x, self.last_y = last_x, last_y
        self.core = lax.rem(links.uly, 2)
        self.row = lax.div(links.uly, 2)
        self.depth = parts.shape[3]
        self.core_copies = {}

    def chunk(self, dp, row, core, half=None):
        if self.own_core_only:
            part = self.parts.at[dp, row]
        else:
            part = self.parts.at[dp, :, row * 2 + core]
        if half is None:
            return part
        depth = self.depth // 2
        return part.at[:, pl.ds(half * depth, depth)]

    def add(self, target, source):
        blocks, depth, _ = target.shape
        rows = 32 if depth % 32 == 0 else 16

        def body(index, carry):
            block = lax.div(index, depth // rows)
            at = pl.ds(pl.multiple_of(lax.rem(index, depth // rows) * rows, rows), rows)
            target[block, at, :] = target[block, at, :] + source[block, at, :]
            return carry

        lax.fori_loop(0, blocks * (depth // rows), body, 0)

    def between_cores(self, which):
        links = self.links
        dp = links.dp if which == 1 else links.other_dp
        self.core_copies[which] = [
            links.to(
                self.chunk(dp, row, 1 - self.core), self.from_core.at[which, row], links.core_way
            )
            for row in range(2)
        ]

    def core_sums(self, which):
        links = self.links
        dp = links.dp if which == 1 else links.other_dp
        for row in range(2):
            self.core_copies[which][row].arrived()
            self.add(self.chunk(dp, row, self.core), self.from_core.at[which, row])

    def across_chips(self):
        links = self.links
        if not self.own_core_only:
            self.core_sums(0)
        self.x_copies = [
            links.to(
                self.chunk(links.other_dp, row, self.core, 0), self.from_x.at[row], links.x_way
            )
            for row in range(2)
        ]
        if not self.own_core_only:
            self.core_sums(1)
        self.y_copies = [
            links.to(
                self.chunk(group, 1 - self.row, self.core, 1),
                self.from_y.at[group],
                links.y_way,
            )
            for group in range(links.n_dp)
        ]

    def second_way(self):
        links = self.links
        for row in range(2):
            self.x_copies[row].arrived()
            self.add(self.chunk(links.dp, row, self.core, 0), self.from_x.at[row])
        self.y_last = links.to(
            self.chunk(links.dp, 1 - self.row, self.core, 0), self.last_y, links.y_way
        )
        for group in range(links.n_dp):
            self.y_copies[group].arrived()
            self.add(self.chunk(group, self.row, self.core, 1), self.from_y.at[group])
        self.x_last = links.to(
            self.chunk(links.other_dp, self.row, self.core, 1), self.last_x, links.x_way
        )

    def result(self, write):
        links = self.links
        for half, copy, source in ((0, self.y_last, self.last_y), (1, self.x_last, self.last_x)):
            copy.arrived()
            own = self.chunk(links.dp, self.row, self.core, half)
            blocks, depth, _ = source.shape
            rows = 32 if depth % 32 == 0 else 16

            def body(index, carry, own=own, source=source, half=half, depth=depth, rows=rows):
                block = lax.div(index, depth // rows)
                start = pl.multiple_of(lax.rem(index, depth // rows) * rows, rows)
                at = pl.ds(start, rows)
                value = own[block, at, :].astype(jnp.float32)
                value = value + source[block, at, :].astype(jnp.float32)
                write(block, pl.ds(pl.multiple_of(start + half * depth, rows), rows), value)
                return carry

            lax.fori_loop(0, blocks * (depth // rows), body, 0)


def plane_shapes(n_dp, blocks, n_uly, depth, width):
    return [
        (n_dp, blocks, n_uly, depth, width),
        (n_dp, 2, blocks, depth, width),
        (2, blocks, depth // 2, width),
        (n_dp, blocks, depth // 2, width),
        (blocks, depth // 2, width),
        (blocks, depth // 2, width),
    ]


def plane_scratch(*sizes):
    return [pltpu.VMEM(shape, jnp.bfloat16) for shape in plane_shapes(*sizes)]


def weight_grad(rows, right, parts, dp):
    _, blocks, n_uly, depth, width = parts.shape
    columns = 512

    def body(index, carry):
        at = pl.ds(pl.multiple_of(index * columns, columns), columns)
        part = jnp.dot(rows[...], right[:, at], preferred_element_type=jnp.float32)
        parts[dp, :, :, :, at] = part.astype(jnp.bfloat16).reshape(blocks, n_uly, depth, columns)
        return carry

    lax.fori_loop(0, width // columns, body, 0)


def rows_turned(left, parts, dp):
    count = parts.shape[1] * parts.shape[2] * parts.shape[3]
    return left[:, pl.ds(pl.multiple_of(dp * count, 128), count)].T


def turned(rows, cosine, sine):
    return rows * cosine + pltpu.roll(rows, HEAD_SIZE // 2, axis=1) * sine


def transposed_product(left, right):
    return lax.dot_general(
        left, right, (((0,), (0,)), ((), ())), preferred_element_type=jnp.float32
    )


def product_right(left, right):
    return lax.dot_general(
        left, right, (((1,), (1,)), ((), ())), preferred_element_type=jnp.float32
    )


SCORE_SCALE = 1.0 / math.sqrt(HEAD_SIZE)


def forward_kernel(
    toks,
    gain_rows,
    span_order,
    hidden,
    wq,
    wk,
    wv,
    wo,
    wg,
    wu,
    wd,
    cotangent,
    gains,
    q_gain,
    k_gain,
    all_qkv,
    all_wo,
    all_wg,
    all_wu,
    all_wd,
    all_cot,
    attn_gain,
    mlp_gain,
    cosine,
    sine,
    query_pos,
    key_pos,
    heads,
    normed,
    qkv,
    queries,
    key_values,
    lse,
    middle,
    all_normed,
    all_gains,
    all_hidden,
    near_qkv,
    near_wo,
    parts,
    rightward,
    leftward,
    own_normed,
    send,
    recv,
    here,
):
    links = Links(send, recv, here)
    links.greet(links.peers() + [links.x_way, links.y_way, links.core_way])
    tokens, width = hidden.shape
    spans = halves(tokens)
    q_width, k_width = wq.shape[1] // links.n_blk, wk.shape[1] // links.n_blk
    chunk = all_qkv.at[links.dp, :, links.uly]
    swap = ColumnSwap(
        links, [(wq, chunk, 0), (wk, chunk, q_width), (wv, chunk, q_width + k_width)]
    )
    plane_wo = PlaneGather(links, rows_of(all_wo, False))
    plane_wd = PlaneGather(links, rows_of(all_wd, False))
    plane_qkv = PlaneGather(links, rows_of(all_qkv, True))
    plane_gain = PlaneGather(links, rows_of(all_gains, True))
    swap.start()
    my_gains = all_gains.at[links.dp, links.blk, links.uly]
    gain_swap = [links.to(gains, my_gains, device) for device in links.peers()]
    plane_wo.start(wo)
    line = HalvedLine(links, hidden, all_hidden)
    line.send(0)
    keep = [
        links.local(gains, my_gains),
        links.local(hidden, all_hidden.at[links.blk]),
        links.local(wo, all_wo.at[links.dp, links.uly]),
        links.local(wd, all_wd.at[links.dp, links.uly]),
        links.local(cotangent, all_cot.at[links.blk]),
    ]
    write_positions(links, span_order, toks, cosine, sine, query_pos, key_pos)
    swap.arrived()
    plane_qkv.start()
    keep[0].wait()
    for copy in gain_swap:
        copy.arrived()
    plane_gain.start()
    plane_wd.start(wd)
    plane_wo.hand_on()
    line.advance(1)
    plane_qkv.hand_on()
    plane_gain.hand_on()
    plane_wo.last()
    for step in range(2, links.n_blk - 1):
        line.advance(step)
    pairs = [(wg, all_wg), (wu, all_wu)]
    planes = [PlaneGather(links, rows_of(whole, True)) for _, whole in pairs]
    swaps = [
        ColumnSwap(links, [(weight, whole.at[links.dp, :, links.uly], 0)])
        for weight, whole in pairs
    ]
    for swap in swaps:
        swap.start()
    cot_lines = HalvedLine(links, cotangent, all_cot).lines
    for half in cot_lines:
        half.send(0)
    plane_qkv.last()
    plane_gain.last()
    plane_gain.arrived()
    write_gains(links, all_gains, gain_rows, (attn_gain, mlp_gain))
    for copy in keep[1:]:
        copy.wait()
    plane_wo.arrived()
    plane_qkv.arrived()
    near = [links.local(all_qkv, near_qkv), links.local(all_wo, near_wo)]
    seqs, kv_heads, q_rows, _ = queries.shape
    q_len = key_values.shape[4]
    group = q_rows // q_len
    q_end = kv_heads * group * HEAD_SIZE
    k_end = q_end + kv_heads * HEAD_SIZE

    def norm(seq):
        def body(rows):
            for blk in range(links.n_blk):
                at = pl.ds(pl.multiple_of(seq * toks + rows.start, ROWS), ROWS)
                to = pl.ds(pl.multiple_of(seq * q_len + blk * toks + rows.start, ROWS), ROWS)
                source = all_hidden[blk, at, :].astype(jnp.float32)
                normed[to, :] = (source * rms_scale(source) * attn_gain[...]).astype(
                    jnp.bfloat16
                )

        each_block(toks, body)

    def rotated(seq, column, gain):
        pre = qkv[seq * q_len : (seq + 1) * q_len, column : column + HEAD_SIZE]
        gain = gain[...].astype(jnp.float32)
        return turned(pre * rms_scale(pre) * gain, cosine[...], sine[...]).astype(jnp.bfloat16)

    def project(seq):
        rows = slice(seq * q_len, (seq + 1) * q_len)
        for column in range(0, qkv.shape[1], 512):
            weight = near_qkv[:, :, :, :, column : column + 512].reshape(width, 512)
            qkv[rows, column : column + 512] = jnp.dot(
                normed[rows, :], weight, preferred_element_type=jnp.float32
            )
        for head in range(kv_heads):
            column = head * HEAD_SIZE
            key_values[links.uly, 0, seq, head] = rotated(seq, q_end + column, k_gain)
            key_values[links.uly, 1, seq, head] = qkv[
                rows, k_end + column : k_end + column + HEAD_SIZE
            ].astype(jnp.bfloat16)
        mine = key_values.at[links.uly, :, seq]
        copies = [links.to(mine, mine, way) for way in (links.core_way, links.y_way)]
        for head in range(kv_heads * group):
            at = pl.ds((head % group) * q_len, q_len)
            queries[seq, head // group, at, :] = rotated(seq, head * HEAD_SIZE, q_gain)
        return copies

    def hand_keys(seq, copies):
        copies[1].arrived()
        theirs = key_values.at[links.across, :, seq]
        copies.append(links.to(theirs, theirs, links.core_way))

    def attend(seq, head):
        def over_keys(piece, carry):
            total, mixed = carry
            rows = pl.ds(pl.multiple_of(piece * q_len, q_len), q_len)
            scores = product_right(key_values[piece, 0, seq, head], queries[seq, head])
            weights = jnp.where(
                query_pos[...] >= key_pos[rows, :], jnp.exp(scores * SCORE_SCALE), 0.0
            )
            total = total + jnp.sum(weights, axis=0, keepdims=True)
            mixed = mixed + transposed_product(
                key_values[piece, 1, seq, head], weights.astype(jnp.bfloat16)
            )
            return total, mixed

        total, mixed = lax.fori_loop(
            0,
            links.n_uly,
            over_keys,
            (
                jnp.zeros((1, q_rows), jnp.float32),
                jnp.zeros((HEAD_SIZE, q_rows), jnp.float32),
            ),
        )
        lse[seq * kv_heads + head] = jnp.log(total)
        attended = (mixed / total).T.astype(jnp.bfloat16)
        for member in range(group):
            column = (head * group + member) * HEAD_SIZE
            for blk in range(links.n_blk):
                row = (blk * seqs + seq) * toks
                start = member * q_len + blk * toks
                heads[row : row + toks, column : column + HEAD_SIZE] = attended[
                    start : start + toks, :
                ]

    sums = halved_sums(links, parts, rightward, leftward)
    def out_weight():
        return near_wo[...].reshape(heads.shape[1], width)

    def out_parts(seq):
        mixed = jnp.concatenate(
            [
                heads[(blk * seqs + seq) * toks : (blk * seqs + seq + 1) * toks, :]
                for blk in range(links.n_blk)
            ],
            axis=0,
        )
        for column in range(0, width, 512):
            parts[:, spans[seq], column : column + 512] = (
                jnp.dot(
                    mixed,
                    out_weight()[:, column : column + 512],
                    preferred_element_type=jnp.float32,
                )
                .astype(jnp.bfloat16)
                .reshape(links.n_blk, toks, 512)
            )
        sums[seq].start()

    key_copies = []
    for seq in range(seqs):
        line.lines[seq].arrived()
        norm(seq)
        if seq == 0:
            for copy in near:
                copy.wait()
        key_copies.append(project(seq))
    plane_wd.hand_on()
    hand_keys(0, key_copies[0])
    swaps[0].arrived()
    planes[0].start()
    for copy in (key_copies[0][0], key_copies[0][2]):
        copy.arrived()
    attend(0, 0)
    hand_keys(1, key_copies[1])
    for head in range(1, kv_heads):
        attend(0, head)
    out_parts(0)
    swaps[1].arrived()
    planes[1].start()
    for copy in (key_copies[1][0], key_copies[1][2]):
        copy.arrived()
    attend(1, 0)
    sums[0].tick(1)
    for head in range(1, kv_heads):
        attend(1, head)
    out_parts(1)
    later = range(2, links.n_blk - 1)
    for tick in later:
        sums[0].tick(tick)
    for half in cot_lines:
        half.arrived()
        half.send(1)
    plane_wd.last()
    planes[0].hand_on()
    lines = []

    def settle(half, rows_of_half):
        half.finish(middle.at[rows_of_half])

        def body(rows):
            at = pl.ds(pl.multiple_of(rows_of_half.start + rows.start, ROWS), ROWS)
            total = middle[at, :] + all_hidden[links.blk, at, :].astype(jnp.float32)
            middle[at, :] = total
            own_normed[at, :] = (total * rms_scale(total) * mlp_gain[...]).astype(jnp.bfloat16)

        each_block(tokens // 2, body)
        next_line = LineGather(links, own_normed.at[rows_of_half], all_normed.at[:, rows_of_half])
        next_line.send(0)
        lines.append(next_line)

    settle(sums[0], spans[0])
    sums[1].tick(1)
    for tick in later:
        sums[1].tick(tick)
    settle(sums[1], spans[1])
    for step in range(2, links.n_blk - 1):
        for half in cot_lines:
            half.arrived()
            half.send(step)
    last_local = links.local(own_normed, all_normed.at[links.blk])
    planes[1].hand_on()
    planes[0].last()
    for step in range(1, links.n_blk - 1):
        for half in lines:
            half.arrived()
            half.send(step)
    planes[1].last()
    for half in lines + cot_lines:
        half.arrived()
    for plane in [plane_wd] + planes:
        plane.arrived()
    last_local.wait()
    for half in sums:
        half.sent()
    links.finish()


SMEM = pl.BlockSpec(memory_space=pltpu.SMEM)


def forward(
    span_order,
    hidden,
    wq,
    wk,
    wv,
    wo,
    wg,
    wu,
    wd,
    cotangent,
    gains,
    q_gain,
    k_gain,
    seqs,
    gain_rows,
):
    n_dp, n_blk, n_uly = (lax.axis_size(a) for a in EVERY)
    tokens, width = hidden.shape
    toks = tokens // seqs
    rows, q_len = n_blk * tokens, n_blk * toks
    group = QUERY_HEADS // KEY_VALUE_HEADS
    kv_heads = KEY_VALUE_HEADS // n_blk
    q_rows, keys = group * q_len, n_uly * q_len
    columns = (wq.shape[1] + wk.shape[1] + wv.shape[1]) // n_blk
    f32, low, i32 = jnp.float32, jnp.bfloat16, jnp.int32
    ff = wg.shape[1] // n_blk
    far = [
        (n_dp, n_blk, n_uly, wq.shape[0], columns),
        (n_dp, n_uly) + wo.shape,
        (n_dp, n_blk, n_uly, wg.shape[0], ff),
        (n_dp, n_blk, n_uly, wu.shape[0], ff),
        (n_dp, n_uly) + wd.shape,
        (n_blk, tokens, width),
    ]
    near = [
        ((1, width), f32),
        ((1, width), f32),
        ((q_len, HEAD_SIZE), f32),
        ((q_len, HEAD_SIZE), f32),
        ((1, q_rows), i32),
        ((keys, 1), i32),
        ((rows, kv_heads * group * HEAD_SIZE), low),
        ((rows, width), low),
        ((rows, columns), f32),
        ((seqs, kv_heads, q_rows, HEAD_SIZE), low),
        ((n_uly, 2, seqs, kv_heads, q_len, HEAD_SIZE), low),
        ((seqs * kv_heads, 1, q_rows), f32),
        ((tokens, width), f32),
        ((n_blk, tokens, width), low),
    ]
    scratch = [
        ((n_dp, n_blk, n_uly) + gains.shape, low),
        ((n_blk, tokens, width), low),
        (far[0], low),
        (far[1], low),
        ((n_blk, tokens, width), low),
        ((n_blk - 1, tokens, width), low),
        ((n_blk - 1, tokens, width), low),
        ((tokens, width), low),
    ]
    return pl.pallas_call(
        functools.partial(forward_kernel, toks, gain_rows),
        out_shape=[jax.ShapeDtypeStruct(shape, low) for shape in far]
        + [jax.ShapeDtypeStruct(shape, kind) for shape, kind in near],
        in_specs=[SMEM] + [HBM] * 10 + [VMEM] * 2,
        out_specs=[HBM] * len(far) + [VMEM] * len(near),
        scratch_shapes=[pltpu.VMEM(shape, kind) for shape, kind in scratch]
        + semaphores(160, 32),
        compiler_params=kernel_params(0),
    )(span_order, hidden, wq, wk, wv, wo, wg, wu, wd, cotangent, gains, q_gain, k_gain)


def back_rows(grad_normed, source, gain):
    unit = source * rms_scale(source)
    scaled = grad_normed * gain
    return rms_scale(source) * (
        scaled - unit * jnp.mean(scaled * unit, axis=-1, keepdims=True)
    )


def back_kernel(
    grad_parts,
    out_parts,
    middle,
    cotangent,
    gain,
    all_normed,
    grad_gate_pre,
    grad_up_pre,
    activated,
    all_cot,
    output,
    grad_middle,
    all_low,
    grad_gate,
    grad_up,
    part_down,
    rightward,
    leftward,
    out_right,
    out_left,
    out_total,
    low,
    turned_low,
    gate_1,
    gate_2,
    gate_3,
    gate_4,
    gate_5,
    gate_6,
    up_1,
    up_2,
    up_3,
    up_4,
    up_5,
    up_6,
    down_1,
    down_2,
    send,
    recv,
    here,
):
    links = Links(send, recv, here)
    links.greet(links.peers() + [links.x_way, links.y_way, links.core_way])
    sums = halved_sums(links, grad_parts, rightward, leftward)
    for half in sums:
        half.start()
    out = OutputHalf(links, 0, out_parts, middle, out_right, out_left, out_total)
    gate = PlaneScatter(links, gate_1, gate_2, gate_3, gate_4, gate_5, gate_6)
    up = PlaneScatter(links, up_1, up_2, up_3, up_4, up_5, up_6)
    down = PlaneScatter(links, down_1, down_2, None, None, None, None)
    tokens = middle.shape[0]
    spans, lines, keep = halves(tokens), [], []

    def compute(plane, which, rows, right):
        dp = links.dp if which == 1 else links.other_dp
        weight_grad(rows, right, plane.parts, dp)
        plane.between_cores(which)

    def turn(which):
        dp = links.dp if which == 1 else links.other_dp
        turned_low[which] = rows_turned(all_normed, gate_1, dp)

    def compute_down(which):
        dp = links.dp if which == 1 else links.other_dp
        compute(down, which, rows_turned(activated, down_1, dp), all_cot)

    def settle(half, rows_of_half):
        half.finish(grad_middle.at[rows_of_half])

        def body(rows):
            at = pl.ds(pl.multiple_of(rows_of_half.start + rows.start, ROWS), ROWS)
            back = back_rows(grad_middle[at, :], middle[at, :], gain[...])
            grad = cotangent[at, :].astype(jnp.float32) + back
            grad_middle[at, :] = grad
            low[at, :] = grad.astype(jnp.bfloat16)

        each_block(tokens // 2, body)
        line = LineGather(links, low.at[rows_of_half], all_low.at[:, rows_of_half])
        line.send(0)
        lines.append(line)

    later = range(2, links.n_blk - 1)
    turn(0)
    compute(gate, 0, turned_low.at[0], grad_gate_pre)
    sums[0].tick(1)
    turn(1)
    compute(gate, 1, turned_low.at[1], grad_gate_pre)
    for tick in later:
        sums[0].tick(tick)
    gate.across_chips()
    settle(sums[0], spans[0])
    compute(up, 0, turned_low.at[0], grad_up_pre)
    sums[1].tick(1)
    compute(up, 1, turned_low.at[1], grad_up_pre)
    for tick in later:
        sums[1].tick(tick)
    up.across_chips()
    settle(sums[1], spans[1])
    out.sum.start()
    keep.append(links.local(low, all_low.at[links.blk]))
    compute_down(0)
    for step in range(1, links.n_blk - 1):
        for line in lines:
            line.arrived()
            line.send(step)
        if step == 1:
            gate.second_way()
            compute_down(1)
    out.sum.tick(1)
    up.second_way()
    for which in (0, 1):
        down.core_sums(which)
    for dp in range(links.n_dp):
        for row in range(2):
            keep.append(links.local(down.chunk(dp, row, down.core), part_down.at[dp, row]))
    for tick in later:
        out.sum.tick(tick)
    for line in lines:
        line.arrived()

    def into(target):
        def write(block, rows, values):
            target[block, rows, :] = values.astype(target.dtype)

        return write

    gate.result(into(grad_gate))
    up.result(into(grad_up))
    out.write(output)
    out.sum.sent()
    for copy in keep:
        copy.wait()
    for half in sums:
        half.sent()
    links.finish()


def exchange_back(
    grad_parts,
    out_parts,
    middle,
    cotangent,
    gain,
    all_normed,
    grad_gate_pre,
    grad_up_pre,
    activated,
    all_cot,
):
    n_dp, n_blk, n_uly = (lax.axis_size(a) for a in EVERY)
    _, tokens, width = grad_parts.shape
    ff = grad_gate_pre.shape[1]
    depth = width // (n_dp * n_blk * n_uly)
    down_depth = ff // (n_dp * n_uly)
    return pl.pallas_call(
        back_kernel,
        out_shape=[
            jax.ShapeDtypeStruct((tokens // 2, width), jnp.bfloat16),
            jax.ShapeDtypeStruct((tokens, width), jnp.float32),
            jax.ShapeDtypeStruct((n_blk, tokens, width), jnp.bfloat16),
            jax.ShapeDtypeStruct((n_blk, depth, ff), jnp.bfloat16),
            jax.ShapeDtypeStruct((n_blk, depth, ff), jnp.bfloat16),
            jax.ShapeDtypeStruct((n_dp, 2, 1, down_depth, width), jnp.bfloat16),
        ],
        in_specs=[VMEM] * 10,
        out_specs=[VMEM, VMEM, HBM, VMEM, VMEM, HBM],
        scratch_shapes=line_scratch(n_blk, tokens, width)
        + output_scratch(n_blk, tokens, width)
        + [
            pltpu.VMEM((tokens, width), jnp.bfloat16),
            pltpu.VMEM((n_dp, width // n_dp, n_blk * tokens), jnp.bfloat16),
        ]
        + plane_scratch(n_dp, n_blk, n_uly, depth, ff) * 2
        + plane_scratch(n_dp, 1, n_uly, down_depth, width)[:2]
        + semaphores(72),
        compiler_params=kernel_params(3),
    )(
        grad_parts,
        out_parts,
        middle,
        cotangent,
        gain,
        all_normed,
        grad_gate_pre,
        grad_up_pre,
        activated,
        all_cot,
    )


def backward_kernel(
    all_low,
    wo,
    queries,
    key_values,
    lse,
    qkv,
    q_gain,
    k_gain,
    cosine,
    sine,
    query_pos,
    key_pos,
    w_qkv,
    hidden,
    grad_middle,
    gain,
    normed,
    heads,
    out_parts,
    middle,
    grad_gate,
    grad_up,
    part_down,
    grad_hidden,
    grad_wo,
    grad_down,
    small_sum,
    output,
    gate_rows,
    up_rows,
    grad_w_qkv,
    grad_qkv,
    gain_terms,
    grad_heads,
    grad_rows,
    probs,
    grad_probs,
    grad_kv,
    from_core,
    from_across,
    grad_parts,
    rightward,
    leftward,
    summed,
    small_in,
    small_total,
    out_right,
    out_left,
    out_total,
    down_1,
    down_3,
    down_4,
    down_5,
    down_6,
    qkv_1,
    qkv_2,
    qkv_3,
    qkv_4,
    qkv_5,
    qkv_6,
    wo_1,
    wo_2,
    wo_3,
    wo_4,
    wo_5,
    wo_6,
    send,
    recv,
    here,
):
    links = Links(send, recv, here)
    links.greet(links.peers() + [links.x_way, links.y_way, links.core_way])
    tokens = hidden.shape[0]
    spans = halves(tokens)
    output_half = OutputHalf(links, 1, out_parts, middle, out_right, out_left, out_total)
    output_half.sum.start()
    down = PlaneScatter(links, down_1, None, down_3, down_4, down_5, down_6)
    fetch = links.local(part_down, down_1)
    swapped, keep = [], []
    for source, target in ((grad_gate, gate_rows), (grad_up, up_rows)):
        swapped += links.swap(
            lambda peer, source=source, target=target: [(source.at[peer], target.at[links.blk])]
        )
        keep.append(links.local(source.at[links.blk], target.at[links.blk]))
    fetch.wait()
    down.across_chips()
    sums = halved_sums(links, grad_parts, rightward, leftward)
    qkv_sums = PlaneScatter(links, qkv_1, qkv_2, qkv_3, qkv_4, qkv_5, qkv_6)
    wo_sums = PlaneScatter(links, wo_1, wo_2, wo_3, wo_4, wo_5, wo_6)
    seqs, kv_heads, q_rows, _ = queries.shape
    q_len = key_values.shape[4]
    group = q_rows // q_len
    toks = q_len // links.n_blk
    q_end = kv_heads * group * HEAD_SIZE
    k_end = q_end + kv_heads * HEAD_SIZE
    gain_terms[...] = jnp.zeros_like(gain_terms)
    later = range(2, links.n_blk - 1)

    def heads_back(seq):
        low = jnp.concatenate(
            [
                all_low[(blk * seqs + seq) * toks : (blk * seqs + seq + 1) * toks, :]
                for blk in range(links.n_blk)
            ],
            axis=0,
        )
        grad_heads[...] = product_right(low, wo[...])
        for head in range(kv_heads * group):
            to = pl.ds((head % group) * q_len, q_len)
            grad_rows[seq, head // group, to, :] = grad_heads[
                :, head * HEAD_SIZE : (head + 1) * HEAD_SIZE
            ].astype(jnp.bfloat16)

    def back_norm(upstream, seq, column, gain, which):
        rows = slice(seq * q_len, (seq + 1) * q_len)
        pre = qkv[rows, column : column + HEAD_SIZE]
        upstream = turned(upstream, cosine[...], -sine[...])
        gain_terms[which : which + 1, :] += jnp.sum(
            upstream * pre * rms_scale(pre), axis=0, keepdims=True
        )
        grad_qkv[rows, column : column + HEAD_SIZE] = back_rows(
            upstream, pre, gain[...].astype(jnp.float32)
        ).astype(jnp.bfloat16)

    def back(seq, head):
        def first(piece, delta):
            rows = pl.ds(pl.multiple_of(piece * q_len, q_len), q_len)
            scores = product_right(key_values[piece, 0, seq, head], queries[seq, head])
            prob = jnp.where(
                query_pos[...] >= key_pos[rows, :],
                jnp.exp(scores * SCORE_SCALE - lse[seq * kv_heads + head]),
                0.0,
            )
            grad_prob = product_right(key_values[piece, 1, seq, head], grad_rows[seq, head])
            probs[rows, :] = prob
            grad_probs[rows, :] = grad_prob
            return delta + jnp.sum(prob * grad_prob, axis=0, keepdims=True)

        delta = lax.fori_loop(0, links.n_uly, first, jnp.zeros((1, q_rows), jnp.float32))

        def second(piece, grad_query):
            rows = pl.ds(pl.multiple_of(piece * q_len, q_len), q_len)
            prob = probs[rows, :]
            grad_score = (prob * (grad_probs[rows, :] - delta)).astype(jnp.bfloat16)
            grad_kv[seq, piece, 0, head] = (
                SCORE_SCALE
                * jnp.dot(grad_score, queries[seq, head], preferred_element_type=jnp.float32)
            ).astype(jnp.bfloat16)
            grad_kv[seq, piece, 1, head] = jnp.dot(
                prob.astype(jnp.bfloat16),
                grad_rows[seq, head],
                preferred_element_type=jnp.float32,
            ).astype(jnp.bfloat16)
            return grad_query + transposed_product(key_values[piece, 0, seq, head], grad_score)

        grad_query = lax.fori_loop(
            0, links.n_uly, second, jnp.zeros((HEAD_SIZE, q_rows), jnp.float32)
        )
        turned_back = (grad_query * SCORE_SCALE).T
        for member in range(group):
            column = (head * group + member) * HEAD_SIZE
            back_norm(
                turned_back[member * q_len : (member + 1) * q_len, :], seq, column, q_gain, 0
            )

    core, line = lax.rem(links.uly, 2), lax.div(links.uly, 2)

    def add(target, source):
        for kind in range(2):
            for head in range(kv_heads):
                target[kind, head] = target[kind, head] + source[kind, head]

    def core_sums(seq):
        return [
            links.to(
                grad_kv.at[seq, row * 2 + 1 - core], from_core.at[seq, row], links.core_way
            )
            for row in range(2)
        ]

    def across_sums(seq, copies):
        for row in range(2):
            copies[row].arrived()
            add(grad_kv.at[seq, row * 2 + core], from_core.at[seq, row])
        return links.to(
            grad_kv.at[seq, (1 - line) * 2 + core], from_across.at[seq], links.y_way
        )

    def own_keys(seq, copy):
        copy.arrived()
        rows = slice(seq * q_len, (seq + 1) * q_len)
        for head in range(kv_heads):
            term = [
                grad_kv[seq, links.uly, kind, head].astype(jnp.float32)
                + from_across[seq, kind, head].astype(jnp.float32)
                for kind in range(2)
            ]
            back_norm(term[0], seq, q_end + head * HEAD_SIZE, k_gain, 1)
            v_at = k_end + head * HEAD_SIZE
            grad_qkv[rows, v_at : v_at + HEAD_SIZE] = term[1].astype(jnp.bfloat16)

    def normed_parts(seq):
        for column in range(0, w_qkv.shape[0], 512):
            grad_parts[:, spans[seq], column : column + 512] = (
                product_right(
                    grad_qkv[seq * q_len : (seq + 1) * q_len, :],
                    w_qkv[column : column + 512, :],
                )
                .astype(jnp.bfloat16)
                .reshape(links.n_blk, toks, 512)
            )
        sums[seq].start()

    def compute(plane, which, left, right):
        dp = links.dp if which == 1 else links.other_dp
        weight_grad(rows_turned(left, plane.parts, dp), right, plane.parts, dp)
        plane.between_cores(which)

    heads_back(0)
    back(0, 0)
    output_half.sum.tick(1)
    for head in range(1, kv_heads):
        back(0, head)
    core_copies = core_sums(0)
    heads_back(1)
    back(1, 0)
    across = across_sums(0, core_copies)
    for tick in later:
        output_half.sum.tick(tick)
    for head in range(1, kv_heads):
        back(1, head)
    core_copies = core_sums(1)
    own_keys(0, across)
    across = across_sums(1, core_copies)
    normed_parts(0)
    down.second_way()
    compute(wo_sums, 0, heads, all_low)
    own_keys(1, across)
    small_total[0] = gain_terms[...]
    pending = links.to(small_total.at[0], small_in.at[links.n_blk], links.core_way)
    compute(qkv_sums, 0, normed, grad_qkv)
    pending.arrived()
    small_total[1] = small_total[0] + small_in[links.n_blk]
    pending = links.to(small_total.at[1], small_in.at[links.n_blk + 1], links.x_way)
    compute(qkv_sums, 1, normed, grad_qkv)
    normed_parts(1)
    pending.arrived()
    small_total[2] = small_total[1] + small_in[links.n_blk + 1]
    pending = links.to(small_total.at[2], small_in.at[links.n_blk + 2], links.y_way)
    qkv_sums.across_chips()
    sums[0].tick(1)
    compute(wo_sums, 1, heads, all_low)
    for tick in later:
        sums[0].tick(tick)
    pending.arrived()
    small_in[links.blk] = small_total[2] + small_in[links.n_blk + 2]
    mine = small_in.at[links.blk]
    small_copies = [links.to(mine, mine, device) for device in links.peers()]
    wo_sums.across_chips()
    output_half.write(output)
    qkv_sums.second_way()
    sums[1].tick(1)

    def settle(seq):
        sums[seq].finish(grad_hidden.at[spans[seq]])

        def body(rows):
            at = pl.ds(pl.multiple_of(spans[seq].start + rows.start, ROWS), ROWS)
            back = back_rows(grad_hidden[at, :], hidden[at, :].astype(jnp.float32), gain[...])
            grad_hidden[at, :] = grad_middle[at, :] + back

        each_block(toks, body)

    def into(target):
        def write(block, rows, values):
            target[block, rows, :] = values.astype(target.dtype)

        return write

    settle(0)
    qkv_sums.result(into(summed))
    swapped += links.swap(lambda peer: [(summed.at[peer], grad_w_qkv.at[links.blk])])
    keep.append(links.local(summed.at[links.blk], grad_w_qkv.at[links.blk]))
    for tick in later:
        sums[1].tick(tick)
    wo_sums.second_way()
    down.result(into(grad_down))
    settle(1)
    wo_sums.result(into(grad_wo))
    for copy in small_copies:
        copy.arrived()
    total = small_in[0]
    for blk in range(1, links.n_blk):
        total = total + small_in[blk]
    small_sum[...] = total
    for copy in swapped:
        copy.arrived()
    for copy in keep:
        copy.wait()
    for half in sums:
        half.sent()
    output_half.sum.sent()
    links.finish()


def backward(
    all_low,
    wo,
    queries,
    key_values,
    lse,
    qkv,
    q_gain,
    k_gain,
    cosine,
    sine,
    query_pos,
    key_pos,
    w_qkv,
    hidden,
    grad_middle,
    gain,
    normed,
    heads,
    out_parts,
    middle,
    grad_gate,
    grad_up,
    part_down,
):
    seqs, kv_heads, q_rows, _ = queries.shape
    n_uly, _, _, _, q_len, _ = key_values.shape
    n_blk, tokens, width = out_parts.shape
    n_dp, _, _, down_depth, _ = part_down.shape
    keys, columns = key_pos.shape[0], qkv.shape[1]
    depth = width // (n_dp * n_blk * n_uly)
    out_depth = heads.shape[1] // (n_dp * n_uly)
    f32, low = jnp.float32, jnp.bfloat16
    small = (8, HEAD_SIZE)
    outs = [
        ((tokens, width), f32),
        ((1, out_depth, width), f32),
        ((1, down_depth, width), f32),
        (small, f32),
        ((tokens // 2, width), low),
        (grad_gate.shape, low),
        (grad_up.shape, low),
        ((n_blk, depth, columns), low),
    ]
    scratch = [
        (qkv.shape, low),
        (small, f32),
        ((q_len, heads.shape[1]), f32),
        (queries.shape, low),
        ((keys, q_rows), f32),
        ((keys, q_rows), f32),
        ((seqs, n_uly, 2, kv_heads, q_len, HEAD_SIZE), low),
        ((seqs, 2, 2, kv_heads, q_len, HEAD_SIZE), low),
        ((seqs, 2, kv_heads, q_len, HEAD_SIZE), low),
        (out_parts.shape, low),
        ((n_blk - 1, tokens, width), low),
        ((n_blk - 1, tokens, width), low),
        ((n_blk, depth, columns), low),
        ((n_blk + 3,) + small, f32),
        ((3,) + small, f32),
    ]
    down = [part_down.shape] + plane_shapes(n_dp, 1, n_uly, down_depth, width)[2:]
    return pl.pallas_call(
        backward_kernel,
        out_shape=[jax.ShapeDtypeStruct(shape, kind) for shape, kind in outs],
        in_specs=[VMEM] * 20 + [HBM] * 3,
        out_specs=[VMEM] * 5 + [HBM] * 3,
        scratch_shapes=[pltpu.VMEM(shape, kind) for shape, kind in scratch]
        + output_scratch(n_blk, tokens, width)
        + [pltpu.VMEM(shape, low) for shape in down]
        + plane_scratch(n_dp, n_blk, n_uly, depth, columns)
        + plane_scratch(n_dp, 1, n_uly, out_depth, width)
        + semaphores(96),
        compiler_params=kernel_params(4),
    )(
        all_low,
        wo,
        queries,
        key_values,
        lse,
        qkv,
        q_gain,
        k_gain,
        cosine,
        sine,
        query_pos,
        key_pos,
        w_qkv,
        hidden,
        grad_middle,
        gain,
        normed,
        heads,
        out_parts,
        middle,
        grad_gate,
        grad_up,
        part_down,
    )


def finish_kernel(
    gate,
    up,
    qkv,
    wo,
    wd,
    hidden,
    out_0,
    out_1,
    w_gate,
    w_up,
    w_query,
    key_weight,
    value_weight,
    attn_gain,
    mlp_gain,
    small,
    f_gate,
    f_up,
    f_q,
    f_k,
    f_v,
    f_wo,
    f_wd,
    f_hidden,
    f_out,
    f_attn,
    f_mlp,
    f_q_gain,
    f_k_gain,
):
    n_blk, depth, _ = gate.shape

    def place(source, offset, target):
        width = target.shape[1] // (n_blk * 2)
        for blk in range(n_blk):
            for group in range(2):
                to = (group * n_blk + blk) * width
                at = offset + group * width
                target[:, to : to + width] = source[blk, :, at : at + width].astype(jnp.float32)

    def gain_back(pairs, gain):
        total = jnp.zeros((depth, 128), jnp.float32)
        for weight, grad in pairs:
            for column in range(0, weight.shape[1], 128):
                at = slice(column, column + 128)
                total = total + weight[:, at].astype(jnp.float32) * grad[:, at]
        column = jnp.sum(total, axis=1, keepdims=True)
        square = (depth, depth)
        same = lax.broadcasted_iota(jnp.int32, square, 0) == lax.broadcasted_iota(
            jnp.int32, square, 1
        )
        return jnp.sum(jnp.where(same, column, 0.0), axis=0, keepdims=True) / gain[
            ...
        ].astype(jnp.float32)

    place(gate, 0, f_gate)
    place(up, 0, f_up)
    q_width = f_q.shape[1] // n_blk
    k_width = f_k.shape[1] // n_blk
    place(qkv, 0, f_q)
    place(qkv, q_width, f_k)
    place(qkv, q_width + k_width, f_v)
    f_q_gain[...] = small[0:1, :]
    f_k_gain[...] = small[1:2, :]
    f_wo[...] = wo[0]
    f_wd[...] = wd[0]
    f_hidden[...] = hidden[...]
    half = out_0.shape[0]
    f_out[:half, :] = out_0[...]
    f_out[half:, :] = out_1[...]
    f_attn[...] = gain_back(((w_query, f_q), (key_weight, f_k), (value_weight, f_v)), attn_gain)
    f_mlp[...] = gain_back(((w_gate, f_gate), (w_up, f_up)), mlp_gain)


def finish(gate, up, qkv, wo, wd, hidden, out_0, out_1, weights, gains, small):
    return pl.pallas_call(
        finish_kernel,
        out_shape=[jax.ShapeDtypeStruct(w.shape, jnp.float32) for w in weights]
        + [
            jax.ShapeDtypeStruct(wo.shape[1:], jnp.float32),
            jax.ShapeDtypeStruct(wd.shape[1:], jnp.float32),
            jax.ShapeDtypeStruct(hidden.shape, jnp.float32),
            jax.ShapeDtypeStruct(hidden.shape, jnp.bfloat16),
        ]
        + [jax.ShapeDtypeStruct(gain.shape, jnp.float32) for gain in gains]
        + [jax.ShapeDtypeStruct((1, small.shape[1]), jnp.float32)] * 2,
        in_specs=[VMEM] * 16,
        out_specs=[VMEM] * 13,
        compiler_params=pltpu.CompilerParams(vmem_limit_bytes=62 * MIB),
    )(gate, up, qkv, wo, wd, hidden, out_0, out_1, *weights, *gains, small)


def product(left, right):
    return jnp.dot(left, right, preferred_element_type=jnp.float32)


def shards(
    hidden,
    span_order,
    attn_gain,
    w_query,
    key_weight,
    value_weight,
    w_out,
    q_gain,
    k_gain,
    mlp_gain,
    w_gate,
    w_up,
    w_down,
    cotangent,
):
    seqs, toks, width = hidden.shape
    n_dp, n_blk, n_uly = (lax.axis_size(a) for a in EVERY)
    rows = n_blk * seqs * toks
    bf16 = jnp.bfloat16
    own_hidden = hidden.reshape(seqs * toks, width)
    own_cotangent = cotangent.reshape(seqs * toks, width)

    gain_q, gain_k = q_gain[None, :], k_gain[None, :]
    gain_rows = attn_gain.shape[0]
    own_gains = jnp.pad(jnp.stack([attn_gain, mlp_gain]), ((0, 30), (0, 128 - gain_rows)))
    (
        w_qkv,
        wo,
        all_wg,
        all_wu,
        all_wd,
        cot,
        g_attn,
        g_mlp,
        cosine,
        sine,
        query_pos,
        key_pos,
        heads_flat,
        normed,
        qkv,
        queries,
        key_values,
        lse,
        middle,
        normed2,
    ) = forward(
        span_order,
        own_hidden,
        w_query,
        key_weight,
        value_weight,
        w_out,
        w_gate,
        w_up,
        w_down,
        own_cotangent,
        own_gains,
        gain_q,
        gain_k,
        seqs,
        gain_rows,
    )
    w_qkv = w_qkv.reshape(width, -1)
    wo = wo.reshape(-1, width)
    wg, wu = all_wg.reshape(width, -1), all_wu.reshape(width, -1)
    wd = all_wd.reshape(-1, width)
    cot = cot.reshape(rows, width)
    normed2 = normed2.reshape(rows, width)
    gate_pre = product(normed2, wg)
    up_pre = product(normed2, wu)
    sigmoid_gate = jax.nn.sigmoid(gate_pre)
    activated = (gate_pre * sigmoid_gate * up_pre).astype(bf16)
    out_parts = product(activated, wd).astype(bf16)
    grad_act = product_right(cot, wd)
    grad_gate_pre = (
        grad_act * up_pre * sigmoid_gate * (1.0 + gate_pre * (1.0 - sigmoid_gate))
    ).astype(bf16)
    grad_up_pre = (grad_act * gate_pre * sigmoid_gate).astype(bf16)
    grad_parts = (product_right(grad_gate_pre, wg) + product_right(grad_up_pre, wu)).astype(bf16)
    blocks = (n_blk, seqs * toks, width)
    out_parts = out_parts.reshape(blocks)
    output_0, grad_middle, middle_low, grad_gate, grad_up, part_down = exchange_back(
        grad_parts.reshape(blocks),
        out_parts,
        middle,
        own_cotangent,
        g_mlp,
        normed2,
        grad_gate_pre,
        grad_up_pre,
        activated,
        cot,
    )
    middle_low = middle_low.reshape(rows, width)
    (
        grad_hidden,
        grad_out,
        grad_down,
        small,
        output_1,
        grad_gate,
        grad_up,
        grad_w_qkv,
    ) = backward(
        middle_low,
        wo,
        queries,
        key_values,
        lse,
        qkv,
        gain_q,
        gain_k,
        cosine,
        sine,
        query_pos,
        key_pos,
        w_qkv,
        own_hidden,
        grad_middle,
        g_attn,
        normed,
        heads_flat,
        out_parts,
        middle,
        grad_gate,
        grad_up,
        part_down,
    )
    (
        grad_gate,
        grad_up,
        grad_query,
        grad_key,
        grad_value,
        grad_out,
        grad_down,
        grad_hidden,
        output,
        grad_attn_gain,
        grad_mlp_gain,
        grad_q_gain,
        grad_k_gain,
    ) = finish(
        grad_gate,
        grad_up,
        grad_w_qkv,
        grad_out,
        grad_down,
        grad_hidden,
        output_0,
        output_1,
        (w_gate, w_up, w_query, key_weight, value_weight),
        [g[None, :] for g in (attn_gain, mlp_gain)],
        small,
    )
    return (
        output.reshape(hidden.shape),
        grad_hidden.reshape(hidden.shape),
        grad_attn_gain.reshape(gain_rows),
        grad_query,
        grad_key,
        grad_value,
        grad_out,
        grad_q_gain[0],
        grad_k_gain[0],
        grad_mlp_gain.reshape(gain_rows),
        grad_gate,
        grad_up,
        grad_down,
    )


def solution(mesh):
    n_dp, n_blk, n_uly = (mesh.shape[a] for a in EVERY)
    aligned = (n_dp, n_uly) == (2, 4) and KEY_VALUE_HEADS % (n_dp * n_blk) == 0
    in_specs = (
        TOKENS,
        P(),
        P(EVERY),
        P(EVERY, None),
        P(EVERY, None),
        P(EVERY, None),
        P(EVERY, None),
        P(),
        P(),
        P(EVERY),
        P(EVERY, None),
        P(EVERY, None),
        P(EVERY, None),
        TOKENS,
    )
    out_specs = (
        TOKENS,
        TOKENS,
        P(EVERY),
        P(EVERY, None),
        P(EVERY, None),
        P(EVERY, None),
        P(EVERY, None),
        P(),
        P(),
        P(EVERY),
        P(EVERY, None),
        P(EVERY, None),
        P(EVERY, None),
    )
    return jax.shard_map(
        shards if aligned else shards_general,
        mesh=mesh, in_specs=in_specs, out_specs=out_specs, check_vma=False)
```

```python
import functools
import math

import jax
import jax.numpy as jnp
from jax import lax
from jax.experimental import pallas as pl
from jax.experimental.pallas import tpu as pltpu
from jax.sharding import PartitionSpec as P

QUERY_HEADS = 16
KEY_VALUE_HEADS = 8
HEAD_SIZE = 128


DP, BLK, ULY = "dp", "blk", "uly"
EVERY = (DP, BLK, ULY)
PLANE = (DP, ULY)
TOKENS = P(DP, (BLK, ULY), None)
EQ_KGQD_NKD_TO_KGQN = "kgqd,nkd->kgqn"
EQ_KGQN_KGQD_TO_NKD = "kgqn,kgqd->nkd"
EQ_KGQN_NKD_TO_KGQD = "kgqn,nkd->kgqd"
EQ_KGQN_QKGD_TO_NKD = "kgqn,qkgd->nkd"
EQ_QKGD_NKD_TO_KGQN = "qkgd,nkd->kgqn"
EQ_STD_DE_TO_STE = "std,de->ste"
EQ_STD_DF_TO_STF = "std,df->stf"
EQ_STD_ED_TO_STE = "std,ed->ste"
EQ_STD_FD_TO_STF = "std,fd->stf"
EQ_STD_STE_TO_DE = "std,ste->de"
EQ_STD_STF_TO_DF = "std,stf->df"
EQ_STE_DE_TO_STD = "ste,de->std"
EQ_STE_ED_TO_STD = "ste,ed->std"
EQ_STE_STD_TO_ED = "ste,std->ed"
EQ_STF_DF_TO_STD = "stf,df->std"
EQ_STF_FD_TO_STD = "stf,fd->std"
EQ_STF_STD_TO_FD = "stf,std->fd"

EPSILON = 1e-06
ROPE_BASE = 1000000.0


def rms_scale(source):
    return lax.rsqrt(jnp.mean(source * source, axis=-1, keepdims=True) + EPSILON)


def norm_back(grad_normed, source, norm_scale, gain):
    unit_rows = source * norm_scale
    scaled = grad_normed * gain
    return norm_scale * (scaled - unit_rows * jnp.mean(scaled * unit_rows, axis=-1, keepdims=True))


def angles_of(positions, head_dim):
    freq_steps = jnp.arange(head_dim // 2, dtype=jnp.float32)
    inverse = jnp.exp(freq_steps * (-2.0 * math.log(ROPE_BASE) / head_dim))
    return positions.astype(jnp.float32)[:, None] * inverse[None, :]


def rotate(source, angles, direction):
    half_dim = source.shape[-1] // 2
    cosine = jnp.cos(angles)[:, None, :]
    sine_part = direction * jnp.sin(angles)[:, None, :]
    first_half = source[..., :half_dim]
    second_half = source[..., half_dim:]
    return jnp.concatenate(
        [
            first_half * cosine - second_half * sine_part,
            second_half * cosine + first_half * sine_part,
        ],
        axis=-1,
    )


def positions_of(places, span_order, half_len):
    blocks_of = places // half_len
    block_ids = jnp.arange(span_order.shape[0], dtype=jnp.int32)
    chosen = jnp.sum(
        jnp.where(blocks_of[:, None] == block_ids[None, :], span_order[None, :], 0), axis=1
    )
    return chosen * half_len + places % half_len


def add_rows(buffer, new_rows):
    return buffer + new_rows


def shards_general(
    hidden,
    span_order,
    attn_gain,
    w_query,
    key_weight,
    value_weight,
    w_out,
    q_gain,
    k_gain,
    mlp_gain,
    w_gate,
    w_up,
    w_down,
    cotangent,
):
    sequence_count = hidden.shape[0]
    token_count = hidden.shape[1]
    ulysses_group_size = lax.axis_size(ULY)
    local_q = QUERY_HEADS // ulysses_group_size
    local_key_value = KEY_VALUE_HEADS // ulysses_group_size
    query_group_width = QUERY_HEADS // KEY_VALUE_HEADS
    block_len = token_count * ulysses_group_size
    half_len = block_len // 2
    score_scale = 1.0 / math.sqrt(HEAD_SIZE)
    blk_index = lax.axis_index(BLK)
    uly_index = lax.axis_index(ULY)
    first_place = (blk_index * ulysses_group_size + uly_index) * token_count
    local_angles = angles_of(
        positions_of(first_place + jnp.arange(token_count, dtype=jnp.int32), span_order, half_len),
        HEAD_SIZE,
    )
    query_pos = positions_of(
        blk_index * block_len + jnp.arange(block_len, dtype=jnp.int32), span_order, half_len
    )
    g_attn, wq_all, wk_all, wv_all, wo_all = (
        lax.all_gather(attn_gain, EVERY, axis=0, tiled=True),
        lax.all_gather(w_query, EVERY, axis=0, tiled=True),
        lax.all_gather(key_weight, EVERY, axis=0, tiled=True),
        lax.all_gather(value_weight, EVERY, axis=0, tiled=True),
        lax.all_gather(w_out, EVERY, axis=0, tiled=True),
    )
    source = hidden.astype(jnp.float32)
    first_scale = rms_scale(source)
    normalized_input = (source * first_scale * g_attn.astype(jnp.float32)).astype(jnp.bfloat16)
    q_pre = jnp.einsum(
        EQ_STD_DE_TO_STE, normalized_input, wq_all, preferred_element_type=jnp.float32
    ).reshape(sequence_count, token_count, QUERY_HEADS, HEAD_SIZE)
    key_before_norm = jnp.einsum(
        EQ_STD_DE_TO_STE, normalized_input, wk_all, preferred_element_type=jnp.float32
    ).reshape(sequence_count, token_count, KEY_VALUE_HEADS, HEAD_SIZE)
    value_before_norm = jnp.einsum(
        EQ_STD_DE_TO_STE, normalized_input, wv_all, preferred_element_type=jnp.float32
    ).reshape(sequence_count, token_count, KEY_VALUE_HEADS, HEAD_SIZE)
    q_scale = rms_scale(q_pre)
    k_scale = rms_scale(key_before_norm)
    gain_q = q_gain.astype(jnp.float32)
    gain_k = k_gain.astype(jnp.float32)
    q_rot = rotate(q_pre * q_scale * gain_q, local_angles, 1.0).astype(jnp.bfloat16)
    k_rot = rotate(key_before_norm * k_scale * gain_k, local_angles, 1.0).astype(jnp.bfloat16)
    v_low = value_before_norm.astype(jnp.bfloat16)
    q_heads, k_heads, v_heads = (
        lax.all_to_all(q_rot, ULY, split_axis=2, concat_axis=1, tiled=True),
        lax.all_to_all(k_rot, ULY, split_axis=2, concat_axis=1, tiled=True),
        lax.all_to_all(v_low, ULY, split_axis=2, concat_axis=1, tiled=True),
    )
    q_group = q_heads.reshape(
        sequence_count, block_len, local_key_value, query_group_width, HEAD_SIZE
    )
    stat_shape = (sequence_count, local_key_value, query_group_width, block_len)
    start_state = (
        jnp.full(stat_shape, -1e30, jnp.float32),
        jnp.zeros(stat_shape, jnp.float32),
        jnp.zeros(stat_shape + (HEAD_SIZE,), jnp.float32),
    )
    key_piece = lax.all_gather(k_heads, BLK, axis=1, tiled=True)
    value_piece = lax.all_gather(v_heads, BLK, axis=1, tiled=True)
    key_pos = positions_of(jnp.arange(key_piece.shape[1], dtype=jnp.int32), span_order, half_len)
    allowed = query_pos[:, None] >= key_pos[None, :]

    def attend_one_sequence(members):
        query_rows, key_rows, value_rows, top_seq, total_seq, accum_seq = members
        scores = (
            jnp.einsum(EQ_QKGD_NKD_TO_KGQN, query_rows, key_rows, preferred_element_type=jnp.float32)
            * score_scale
        )
        scores = jnp.where(allowed, scores, -jnp.inf)
        new_top = jnp.maximum(top_seq, jnp.max(scores, axis=-1))
        fading = jnp.exp(top_seq - new_top)
        weights = jnp.exp(scores - new_top[..., None])
        total_seq = total_seq * fading + jnp.sum(weights, axis=-1)
        accum_seq = accum_seq * fading[..., None] + jnp.einsum(
            EQ_KGQN_NKD_TO_KGQD,
            weights.astype(jnp.bfloat16),
            value_rows,
            preferred_element_type=jnp.float32,
        )
        return (new_top, total_seq, accum_seq)

    row_top, row_total, accum = lax.map(
        attend_one_sequence,
        (q_group, key_piece, value_piece, start_state[0], start_state[1], start_state[2]),
    )
    log_total = row_top + jnp.log(row_total)
    attention_output = jnp.transpose(accum / row_total[..., None], (0, 3, 1, 2, 4)).reshape(
        sequence_count, block_len, local_q, HEAD_SIZE
    )
    heads_seq = lax.all_to_all(
        attention_output.astype(jnp.bfloat16), ULY, split_axis=1, concat_axis=2, tiled=True
    )
    heads_flat = heads_seq.reshape(sequence_count, token_count, QUERY_HEADS * HEAD_SIZE)
    middle = source + jnp.einsum(
        EQ_STE_ED_TO_STD, heads_flat, wo_all, preferred_element_type=jnp.float32
    )
    g_mlp, wg_all, wu_all, wd_all = (
        lax.all_gather(mlp_gain, EVERY, axis=0, tiled=True),
        lax.all_gather(w_gate, EVERY, axis=0, tiled=True),
        lax.all_gather(w_up, EVERY, axis=0, tiled=True),
        lax.all_gather(w_down, EVERY, axis=0, tiled=True),
    )
    second_scale = rms_scale(middle)
    gain_mlp = g_mlp.astype(jnp.float32)
    normed2 = (middle * second_scale * gain_mlp).astype(jnp.bfloat16)
    gate_pre = jnp.einsum(EQ_STD_DF_TO_STF, normed2, wg_all, preferred_element_type=jnp.float32)
    up_pre = jnp.einsum(EQ_STD_DF_TO_STF, normed2, wu_all, preferred_element_type=jnp.float32)
    sigmoid_gate = jax.nn.sigmoid(gate_pre)
    activated = (gate_pre * sigmoid_gate * up_pre).astype(jnp.bfloat16)
    result = middle + jnp.einsum(
        EQ_STF_FD_TO_STD, activated, wd_all, preferred_element_type=jnp.float32
    )
    output = result.astype(jnp.bfloat16)
    g_mlp, wg_all, wu_all, wd_all = (
        lax.all_gather(mlp_gain, EVERY, axis=0, tiled=True),
        lax.all_gather(w_gate, EVERY, axis=0, tiled=True),
        lax.all_gather(w_up, EVERY, axis=0, tiled=True),
        lax.all_gather(w_down, EVERY, axis=0, tiled=True),
    )
    gain_mlp = g_mlp.astype(jnp.float32)
    grad_act = jnp.einsum(EQ_STD_FD_TO_STF, cotangent, wd_all, preferred_element_type=jnp.float32)
    grad_gate_pre = (
        grad_act * up_pre * sigmoid_gate * (1.0 + gate_pre * (1.0 - sigmoid_gate))
    ).astype(jnp.bfloat16)
    grad_up_pre = (grad_act * gate_pre * sigmoid_gate).astype(jnp.bfloat16)
    grad_gate = jnp.einsum(
        EQ_STD_STF_TO_DF, normed2, grad_gate_pre, preferred_element_type=jnp.float32
    )
    grad_up = jnp.einsum(EQ_STD_STF_TO_DF, normed2, grad_up_pre, preferred_element_type=jnp.float32)
    grad_normed2 = jnp.einsum(
        EQ_STF_DF_TO_STD, grad_gate_pre, wg_all, preferred_element_type=jnp.float32
    ) + jnp.einsum(EQ_STF_DF_TO_STD, grad_up_pre, wu_all, preferred_element_type=jnp.float32)
    mlp_gain_term = jnp.sum(grad_normed2 * middle * second_scale, axis=(0, 1))
    grad_middle = cotangent.astype(jnp.float32) + norm_back(
        grad_normed2, middle, second_scale, gain_mlp
    )
    grad_mlp_gain, grad_gate, grad_up = (
        lax.psum_scatter(mlp_gain_term, EVERY, scatter_dimension=0, tiled=True),
        lax.psum_scatter(grad_gate, EVERY, scatter_dimension=0, tiled=True),
        lax.psum_scatter(grad_up, EVERY, scatter_dimension=0, tiled=True),
    )
    g_attn, wq_all, wk_all, wv_all, wo_all = (
        lax.all_gather(attn_gain, EVERY, axis=0, tiled=True),
        lax.all_gather(w_query, EVERY, axis=0, tiled=True),
        lax.all_gather(key_weight, EVERY, axis=0, tiled=True),
        lax.all_gather(value_weight, EVERY, axis=0, tiled=True),
        lax.all_gather(w_out, EVERY, axis=0, tiled=True),
    )
    middle_low = grad_middle.astype(jnp.bfloat16)
    grad_out = jnp.einsum(EQ_STE_STD_TO_ED, heads_flat, middle_low, preferred_element_type=jnp.float32)
    grad_heads = (
        jnp.einsum(EQ_STD_ED_TO_STE, middle_low, wo_all, preferred_element_type=jnp.float32)
        .astype(jnp.bfloat16)
        .reshape(sequence_count, token_count, QUERY_HEADS, HEAD_SIZE)
    )
    grad_heads_local = lax.all_to_all(grad_heads, ULY, split_axis=2, concat_axis=1, tiled=True)
    grad_group = jnp.transpose(
        grad_heads_local.reshape(
            sequence_count, block_len, local_key_value, query_group_width, HEAD_SIZE
        ),
        (0, 2, 3, 1, 4),
    )
    delta = jnp.sum(grad_heads_local.astype(jnp.float32) * attention_output, axis=-1)
    delta = jnp.transpose(
        delta.reshape(sequence_count, block_len, local_key_value, query_group_width), (0, 2, 3, 1)
    )
    seq_length = block_len * lax.axis_size(BLK)
    zero_keys = jnp.zeros((sequence_count, seq_length, local_key_value, HEAD_SIZE), jnp.float32)
    back_state = (jnp.zeros(stat_shape + (HEAD_SIZE,), jnp.float32), zero_keys, zero_keys)
    key_piece = lax.all_gather(k_heads, BLK, axis=1, tiled=True)
    value_piece = lax.all_gather(v_heads, BLK, axis=1, tiled=True)
    key_pos = positions_of(jnp.arange(key_piece.shape[1], dtype=jnp.int32), span_order, half_len)
    back_allowed = query_pos[:, None] >= key_pos[None, :]

    def back_one_sequence(members):
        query_rows, grad_rows, lse_seq, delta_seq, key_rows, value_rows, dq_seq, dk_seq, dv_seq = (
            members
        )
        scores = (
            jnp.einsum(EQ_QKGD_NKD_TO_KGQN, query_rows, key_rows, preferred_element_type=jnp.float32)
            * score_scale
        )
        scores = jnp.where(back_allowed, scores, -jnp.inf)
        probs = jnp.exp(scores - lse_seq[..., None])
        grad_values = jnp.einsum(
            EQ_KGQN_KGQD_TO_NKD,
            probs.astype(jnp.bfloat16),
            grad_rows,
            preferred_element_type=jnp.float32,
        )
        grad_probs = jnp.einsum(
            EQ_KGQD_NKD_TO_KGQN, grad_rows, value_rows, preferred_element_type=jnp.float32
        )
        grad_scores = (probs * (grad_probs - delta_seq[..., None])).astype(jnp.bfloat16)
        dq_seq = dq_seq + score_scale * jnp.einsum(
            EQ_KGQN_NKD_TO_KGQD, grad_scores, key_rows, preferred_element_type=jnp.float32
        )
        grad_keys = score_scale * jnp.einsum(
            EQ_KGQN_QKGD_TO_NKD, grad_scores, query_rows, preferred_element_type=jnp.float32
        )
        return (dq_seq, add_rows(dk_seq, grad_keys), add_rows(dv_seq, grad_values))

    grad_q_group, grad_k_whole, grad_v_whole = lax.map(
        back_one_sequence,
        (
            q_group,
            grad_group,
            log_total,
            delta,
            key_piece,
            value_piece,
            back_state[0],
            back_state[1],
            back_state[2],
        ),
    )
    grad_k_block, grad_v_block = (
        lax.psum_scatter(
            grad_k_whole.astype(jnp.bfloat16), BLK, scatter_dimension=1, tiled=True
        ).astype(jnp.float32),
        lax.psum_scatter(
            grad_v_whole.astype(jnp.bfloat16), BLK, scatter_dimension=1, tiled=True
        ).astype(jnp.float32),
    )
    grad_q_block = jnp.transpose(grad_q_group, (0, 3, 1, 2, 4)).reshape(
        sequence_count, block_len, local_q, HEAD_SIZE
    )
    grad_q_seq, grad_k_seq, value_sequence_gradient = (
        lax.all_to_all(
            grad_q_block.astype(jnp.bfloat16), ULY, split_axis=1, concat_axis=2, tiled=True
        ).astype(grad_q_block.dtype),
        lax.all_to_all(
            grad_k_block.astype(jnp.bfloat16), ULY, split_axis=1, concat_axis=2, tiled=True
        ).astype(grad_k_block.dtype),
        lax.all_to_all(
            grad_v_block.astype(jnp.bfloat16), ULY, split_axis=1, concat_axis=2, tiled=True
        ).astype(grad_v_block.dtype),
    )
    grad_q_normed = rotate(grad_q_seq, local_angles, -1.0)
    grad_k_normed = rotate(grad_k_seq, local_angles, -1.0)
    q_gain_term = jnp.sum(grad_q_normed * q_pre * q_scale, axis=(0, 1, 2))
    k_gain_term = jnp.sum(grad_k_normed * key_before_norm * k_scale, axis=(0, 1, 2))
    grad_q_pre = (
        norm_back(grad_q_normed, q_pre, q_scale, gain_q)
        .astype(jnp.bfloat16)
        .reshape(sequence_count, token_count, QUERY_HEADS * HEAD_SIZE)
    )
    grad_k_pre = (
        norm_back(grad_k_normed, key_before_norm, k_scale, gain_k)
        .astype(jnp.bfloat16)
        .reshape(sequence_count, token_count, KEY_VALUE_HEADS * HEAD_SIZE)
    )
    value_pre_gradient = value_sequence_gradient.astype(jnp.bfloat16).reshape(
        sequence_count, token_count, KEY_VALUE_HEADS * HEAD_SIZE
    )
    grad_query = jnp.einsum(
        EQ_STD_STE_TO_DE, normalized_input, grad_q_pre, preferred_element_type=jnp.float32
    )
    grad_key = jnp.einsum(
        EQ_STD_STE_TO_DE, normalized_input, grad_k_pre, preferred_element_type=jnp.float32
    )
    grad_value = jnp.einsum(
        EQ_STD_STE_TO_DE, normalized_input, value_pre_gradient, preferred_element_type=jnp.float32
    )
    grad_normed = jnp.einsum(EQ_STE_DE_TO_STD, grad_q_pre, wq_all, preferred_element_type=jnp.float32)
    grad_normed = grad_normed + jnp.einsum(
        EQ_STE_DE_TO_STD, grad_k_pre, wk_all, preferred_element_type=jnp.float32
    )
    grad_normed = grad_normed + jnp.einsum(
        EQ_STE_DE_TO_STD, value_pre_gradient, wv_all, preferred_element_type=jnp.float32
    )
    attn_gain_term = jnp.sum(grad_normed * source * first_scale, axis=(0, 1))
    grad_hidden = grad_middle + norm_back(
        grad_normed, source, first_scale, g_attn.astype(jnp.float32)
    )
    grad_down = jnp.einsum(EQ_STF_STD_TO_FD, activated, cotangent, preferred_element_type=jnp.float32)
    grad_attn_gain, grad_query, grad_key, grad_value, grad_out, grad_down = (
        lax.psum_scatter(attn_gain_term, EVERY, scatter_dimension=0, tiled=True),
        lax.psum_scatter(grad_query, EVERY, scatter_dimension=0, tiled=True),
        lax.psum_scatter(grad_key, EVERY, scatter_dimension=0, tiled=True),
        lax.psum_scatter(grad_value, EVERY, scatter_dimension=0, tiled=True),
        lax.psum_scatter(grad_out, EVERY, scatter_dimension=0, tiled=True),
        lax.psum_scatter(grad_down, EVERY, scatter_dimension=0, tiled=True),
    )
    grad_q_gain, grad_k_gain = lax.psum((q_gain_term, k_gain_term), EVERY)
    return (
        output,
        grad_hidden,
        grad_attn_gain,
        grad_query,
        grad_key,
        grad_value,
        grad_out,
        grad_q_gain,
        grad_k_gain,
        grad_mlp_gain,
        grad_gate,
        grad_up,
        grad_down,
    )


MESH = pl.DeviceIdType.MESH
HBM = pl.BlockSpec(memory_space=pltpu.HBM)
VMEM = pl.BlockSpec(memory_space=pltpu.VMEM)
MIB = 1 << 20


def kernel_params(collective_id, vmem_mib=62):
    return pltpu.CompilerParams(
        collective_id=collective_id, has_side_effects=True, vmem_limit_bytes=vmem_mib * MIB
    )


def semaphores(count, local=16):
    return [
        pltpu.SemaphoreType.DMA((count,)),
        pltpu.SemaphoreType.DMA((count,)),
        pltpu.SemaphoreType.DMA((local,)),
    ]


class Copy:
    def __init__(self, descriptor, sends, receives):
        self.descriptor, self.sends, self.receives = descriptor, sends, receives

    def under(self, condition, action):
        if condition is None:
            action()
        else:
            pl.when(condition)(action)

    def start(self):
        self.under(self.sends, lambda: self.descriptor().start())
        return self

    def sent(self):
        self.under(self.sends, lambda: self.descriptor().wait_send())

    def arrived(self):
        self.under(self.receives, lambda: self.descriptor().wait_recv())


class Links:
    def __init__(self, send, recv, here):
        self.send, self.recv, self.here = send, recv, here
        self.used, self.used_here = 0, 0
        self.copies, self.local_copies = [], []
        self.n_dp, self.n_blk, self.n_uly = (lax.axis_size(a) for a in EVERY)
        self.dp, self.blk, self.uly = (lax.axis_index(a) for a in EVERY)
        self.other_dp = 1 - self.dp
        self.across = lax.rem(self.uly + 2, 4)
        self.twin = self.uly + 1 - 2 * lax.rem(self.uly, 2)
        self.x_way = (self.other_dp, self.blk, self.uly)
        self.y_way = (self.dp, self.blk, self.across)
        self.core_way = (self.dp, self.blk, self.twin)

    def peer(self, step):
        return lax.rem(self.blk + step, self.n_blk)

    def peers(self):
        return [(self.dp, self.peer(k), self.uly) for k in range(1, self.n_blk)]

    def far_first(self):
        last = self.n_blk - 1
        orders = [
            sorted((p for p in range(self.n_blk) if p != b), key=lambda p, b=b: -abs(p - b))
            for b in range(self.n_blk)
        ]
        for b, order in enumerate(orders):
            ways = [[p for p in order if p > b], [p for p in order if p < b]]
            ways.sort(key=lambda way: -len(way))
            merged = []
            while ways[0] or ways[1]:
                for way in ways:
                    if way:
                        merged.append(way.pop(0))
            orders[b] = merged
        peers = []
        for turn in range(last):
            peer = jnp.int32(0)
            for b, order in enumerate(orders):
                peer = jnp.where(self.blk == b, order[turn], peer)
            peers.append(peer)
        return peers

    def swap(self, pieces_for):
        base, count = self.used, 0
        for peer in self.far_first():
            pieces = pieces_for(peer)
            count = len(pieces)
            distance = lax.rem(peer - self.blk + self.n_blk, self.n_blk) - 1
            for number, (source, target) in enumerate(pieces):
                self.swap_copy(base + distance * count + number, source, target, peer).start()
        self.used = base + (self.n_blk - 1) * count
        waits = []
        for slot in range(base, self.used):
            source, target = pieces_for(self.blk)[(slot - base) % count]

            def descriptor(slot=slot, source=source, target=target):
                return self.swap_copy(slot, source, target, self.peer(1))

            copy = Copy(descriptor, None, None)
            self.copies.append(copy)
            waits.append(copy)
        return waits

    def swap_copy(self, slot, source, target, peer):
        return pltpu.make_async_remote_copy(
            src_ref=source,
            dst_ref=target,
            send_sem=self.send.at[slot],
            recv_sem=self.recv.at[slot],
            device_id=(self.dp, peer, self.uly),
            device_id_type=MESH,
        )

    def greet(self, devices):
        barrier = pltpu.get_barrier_semaphore()
        for device in devices:
            pl.semaphore_signal(barrier, inc=1, device_id=device, device_id_type=MESH)
        pl.semaphore_wait(barrier, len(devices))

    def remote(self, source, target, device, sends=None, receives=None):
        slot = self.used
        self.used += 1

        def descriptor():
            return pltpu.make_async_remote_copy(
                src_ref=source(),
                dst_ref=target(),
                send_sem=self.send.at[slot],
                recv_sem=self.recv.at[slot],
                device_id=device,
                device_id_type=MESH,
            )

        copy = Copy(descriptor, sends, receives)
        self.copies.append(copy)
        return copy.start()

    def to(self, source, target, device):
        return self.remote(lambda: source, lambda: target, device)

    def local(self, source, target):
        copy = pltpu.make_async_copy(source, target, self.here.at[self.used_here])
        self.used_here += 1
        copy.start()
        self.local_copies.append(copy)
        return copy

    def finish(self):
        for copy in self.copies:
            copy.sent()


class LineGather:
    def __init__(self, links, own, whole):
        self.links, self.own, self.whole = links, own, whole
        self.waiting = []

    def send(self, step):
        links, whole = self.links, self.whole
        blk, last = links.blk, links.n_blk - 1

        def block(index):
            if step == 0:
                return lambda: self.own
            return lambda: whole.at[index]

        self.waiting = [
            links.remote(
                block(blk - step),
                lambda: whole.at[blk - step],
                (links.dp, blk + 1, links.uly),
                jnp.logical_and(blk >= step, blk < last),
                blk >= step + 1,
            ),
            links.remote(
                block(blk + step),
                lambda: whole.at[blk + step],
                (links.dp, blk - 1, links.uly),
                jnp.logical_and(blk + step <= last, blk > 0),
                blk + step + 1 <= last,
            ),
        ]

    def arrived(self):
        for copy in self.waiting:
            copy.arrived()


def halves(tokens):
    return [pl.ds(0, tokens // 2), pl.ds(tokens // 2, tokens // 2)]


class HalvedLine:
    def __init__(self, links, own, whole):
        self.lines = [
            LineGather(links, None if own is None else own.at[rows], whole.at[:, rows])
            for rows in halves(whole.shape[1])
        ]

    def send(self, step):
        for line in self.lines:
            line.send(step)

    def advance(self, step):
        for line in self.lines:
            line.arrived()
            line.send(step)

    def arrived(self):
        for line in self.lines:
            line.arrived()


class PlaneGather:
    def __init__(self, links, at):
        self.links, self.at = links, at

    def start_x(self, own):
        links = self.links
        mine = self.at(links.dp, links.uly)
        self.from_x = links.to(own, mine, links.x_way)
        self.from_core = [links.to(own, mine, links.core_way)]

    def start_y(self, own):
        links = self.links
        self.from_y = links.to(own, self.at(links.dp, links.uly), links.y_way)

    def start(self, own=None):
        own = self.at(self.links.dp, self.links.uly) if own is None else own
        self.start_x(own)
        self.start_y(own)

    def hand_on(self):
        links, at = self.links, self.at
        self.from_x.arrived()
        half = at(links.other_dp, links.uly, 0)
        self.second_y = links.to(half, half, links.y_way)
        self.from_y.arrived()
        half = at(links.dp, links.across, 1)
        self.second_x = links.to(half, half, links.x_way)
        for chunk in (at(links.other_dp, links.uly), at(links.dp, links.across)):
            self.from_core.append(links.to(chunk, chunk, links.core_way))

    def last(self):
        links = self.links
        self.second_y.arrived()
        self.second_x.arrived()
        chunk = self.at(links.other_dp, links.across)
        self.from_core.append(links.to(chunk, chunk, links.core_way))

    def arrived(self):
        for copy in self.from_core:
            copy.arrived()


def rows_of(whole, blocked):
    def at(dp, uly, half=None):
        part = whole.at[dp, :, uly] if blocked else whole.at[dp, uly]
        if half is None:
            return part
        depth = whole.shape[-2] // 2
        rows = pl.ds(half * depth, depth)
        return part.at[:, rows] if blocked else part.at[rows]

    return at


class ColumnSwap:
    def __init__(self, links, pieces):
        self.links, self.pieces = links, pieces
        self.incoming, self.kept = [], []

    def parts(self, blk):
        links = self.links
        for weight, whole, offset in self.pieces:
            width = weight.shape[-1] // links.n_dp // links.n_blk
            for group in range(links.n_dp):
                start = (group * links.n_blk + blk) * width
                yield (
                    weight.at[:, pl.ds(pl.multiple_of(start, 128), width)],
                    whole.at[links.blk, :, pl.ds(offset + group * width, width)],
                )

    def start(self):
        links = self.links
        self.incoming = links.swap(lambda peer: list(self.parts(peer)))
        for source, target in self.parts(links.blk):
            self.kept.append(links.local(source, target))

    def arrived(self):
        for copy in self.kept:
            copy.wait()
        for copy in self.incoming:
            copy.arrived()


def write_positions(links, span_order, toks, cosine, sine, query_pos, key_pos):
    half_len = toks * links.n_uly // 2

    def first(blk, uly):
        chunk = span_order[2 * blk + lax.div(uly, links.n_uly // 2)]
        return chunk * half_len + lax.rem(uly, links.n_uly // 2) * toks

    lane = lax.broadcasted_iota(jnp.int32, (toks, HEAD_SIZE), 1)
    row = lax.broadcasted_iota(jnp.int32, (toks, HEAD_SIZE), 0)
    upper = lane >= HEAD_SIZE // 2
    step = jnp.where(upper, lane - HEAD_SIZE // 2, lane).astype(jnp.float32)
    inverse = jnp.exp(step * (-2.0 * math.log(ROPE_BASE) / HEAD_SIZE))
    for blk in range(links.n_blk):
        angles = (first(blk, links.uly) + row).astype(jnp.float32) * inverse
        at = slice(blk * toks, (blk + 1) * toks)
        cosine[at, :] = jnp.cos(angles)
        turn = jnp.sin(angles)
        sine[at, :] = jnp.where(upper, turn, -turn)
    lane = lax.broadcasted_iota(jnp.int32, query_pos.shape, 1)
    place = jnp.zeros(query_pos.shape, jnp.int32)
    for start in range(0, query_pos.shape[1], toks):
        blk = start // toks % links.n_blk
        here = jnp.logical_and(lane >= start, lane < start + toks)
        place = jnp.where(here, first(blk, links.uly) + lane - start, place)
    query_pos[...] = place
    row = lax.broadcasted_iota(jnp.int32, (toks, 1), 0)
    for uly in range(links.n_uly):
        for blk in range(links.n_blk):
            start = (uly * links.n_blk + blk) * toks
            key_pos[start : start + toks, :] = row + first(blk, jnp.int32(uly))


def write_gains(links, all_gains, size, targets):
    per_row = 128 // size
    for which, target in enumerate(targets):
        for place in range(target.shape[1] // 128):
            pieces = []
            for part in range(per_row):
                device = place * per_row + part
                plane, uly = device // links.n_uly, device % links.n_uly
                gains = all_gains[plane // links.n_blk, plane % links.n_blk, uly]
                pieces.append(gains.astype(jnp.float32)[which : which + 1, :size])
            target[:, place * 128 : (place + 1) * 128] = jnp.concatenate(pieces, axis=1)


ROWS = 32


def each_block(count, body):
    def step(index, carry):
        body(pl.ds(pl.multiple_of(index * ROWS, ROWS), ROWS))
        return carry

    lax.fori_loop(0, count // ROWS, step, 0)


class LineScatter:
    def __init__(self, links, parts, rightward, leftward):
        self.links, self.parts = links, parts
        self.slots = {1: rightward, -1: leftward}
        self.tokens = parts.shape[1]
        self.number = links.used
        self.last = links.n_blk - 1
        links.used += 2 * self.last

    def target(self, step, way):
        return self.last - step if way == 1 else step

    def slot(self, step, way):
        target = self.target(step, way)
        return self.slots[way].at[target - 1 if way == 1 else target]

    def place(self, way):
        return self.links.blk if way == 1 else self.last - self.links.blk

    def copy(self, step, way, source=None):
        links, slot = self.links, self.slot(step, way)
        number = self.number + 2 * step + (1 if way == 1 else 0)
        return pltpu.make_async_remote_copy(
            src_ref=slot if source is None else source,
            dst_ref=slot,
            send_sem=links.send.at[number],
            recv_sem=links.recv.at[number],
            device_id=(links.dp, links.blk + way, links.uly),
            device_id_type=MESH,
        )

    def start(self):
        for step in range(self.last):
            for way in (1, -1):

                @pl.when(self.place(way) == 0)
                def _(step=step, way=way):
                    self.copy(step, way, self.parts.at[self.target(step, way)]).start()

    def tick(self, tick):
        for way in (1, -1):

            @pl.when(jnp.logical_and(self.place(way) >= 1, self.place(way) <= tick))
            def _(way=way):
                step = tick - self.place(way)
                self.copy(step, way).wait_recv()
                slot, target = self.slot(step, way), self.target(step, way)

                def body(rows):
                    slot[rows, :] = slot[rows, :] + self.parts[target, rows, :]

                each_block(self.tokens, body)
                self.copy(step, way).start()

    def finish(self, total):
        blk, last = self.links.blk, self.last

        def start(rows):
            total[rows, :] = self.parts[blk, rows, :].astype(jnp.float32)

        each_block(self.tokens, start)
        for way in (1, -1):

            @pl.when(self.place(way) >= 1)
            def _(way=way):
                step = last - self.place(way)
                self.copy(step, way).wait_recv()
                slot = self.slot(step, way)

                def body(rows):
                    total[rows, :] = total[rows, :] + slot[rows, :].astype(jnp.float32)

                each_block(self.tokens, body)

    def sent(self):
        for step in range(self.last):
            for way in (1, -1):
                beyond = self.place(way) + step < self.last
                pl.when(beyond)(lambda step=step, way=way: self.copy(step, way).wait_send())


def halved_sums(links, parts, rightward, leftward):
    return [
        LineScatter(links, parts.at[:, rows], rightward.at[:, rows], leftward.at[:, rows])
        for rows in halves(parts.shape[1])
    ]


class OutputHalf:
    def __init__(self, links, which, parts, middle, rightward, leftward, total):
        rows = halves(middle.shape[0])[which]
        self.middle, self.total = middle.at[rows], total
        self.sum = LineScatter(links, parts.at[:, rows], rightward, leftward)

    def write(self, output):
        self.sum.finish(self.total)

        def body(rows):
            output[rows, :] = (self.middle[rows, :] + self.total[rows, :]).astype(jnp.bfloat16)

        each_block(self.middle.shape[0], body)


def output_scratch(n_blk, tokens, width):
    return line_scratch(n_blk, tokens // 2, width) + [
        pltpu.VMEM((tokens // 2, width), jnp.float32)
    ]


def line_scratch(n_blk, tokens, width):
    return [pltpu.VMEM((n_blk - 1, tokens, width), jnp.bfloat16)] * 2


class PlaneScatter:
    def __init__(self, links, parts, from_core, from_x, from_y, last_x, last_y):
        self.links, self.parts = links, parts
        self.own_core_only = from_core is None
        self.from_core, self.from_x, self.from_y = from_core, from_x, from_y
        self.last_x, self.last_y = last_x, last_y
        self.core = lax.rem(links.uly, 2)
        self.row = lax.div(links.uly, 2)
        self.depth = parts.shape[3]
        self.core_copies = {}

    def chunk(self, dp, row, core, half=None):
        if self.own_core_only:
            part = self.parts.at[dp, row]
        else:
            part = self.parts.at[dp, :, row * 2 + core]
        if half is None:
            return part
        depth = self.depth // 2
        return part.at[:, pl.ds(half * depth, depth)]

    def add(self, target, source):
        blocks, depth, _ = target.shape
        rows = 32 if depth % 32 == 0 else 16

        def body(index, carry):
            block = lax.div(index, depth // rows)
            at = pl.ds(pl.multiple_of(lax.rem(index, depth // rows) * rows, rows), rows)
            target[block, at, :] = target[block, at, :] + source[block, at, :]
            return carry

        lax.fori_loop(0, blocks * (depth // rows), body, 0)

    def between_cores(self, which):
        links = self.links
        dp = links.dp if which == 1 else links.other_dp
        self.core_copies[which] = [
            links.to(
                self.chunk(dp, row, 1 - self.core), self.from_core.at[which, row], links.core_way
            )
            for row in range(2)
        ]

    def core_sums(self, which):
        links = self.links
        dp = links.dp if which == 1 else links.other_dp
        for row in range(2):
            self.core_copies[which][row].arrived()
            self.add(self.chunk(dp, row, self.core), self.from_core.at[which, row])

    def across_chips(self):
        links = self.links
        if not self.own_core_only:
            self.core_sums(0)
        self.x_copies = [
            links.to(
                self.chunk(links.other_dp, row, self.core, 0), self.from_x.at[row], links.x_way
            )
            for row in range(2)
        ]
        if not self.own_core_only:
            self.core_sums(1)
        self.y_copies = [
            links.to(
                self.chunk(group, 1 - self.row, self.core, 1),
                self.from_y.at[group],
                links.y_way,
            )
            for group in range(links.n_dp)
        ]

    def second_way(self):
        links = self.links
        for row in range(2):
            self.x_copies[row].arrived()
            self.add(self.chunk(links.dp, row, self.core, 0), self.from_x.at[row])
        self.y_last = links.to(
            self.chunk(links.dp, 1 - self.row, self.core, 0), self.last_y, links.y_way
        )
        for group in range(links.n_dp):
            self.y_copies[group].arrived()
            self.add(self.chunk(group, self.row, self.core, 1), self.from_y.at[group])
        self.x_last = links.to(
            self.chunk(links.other_dp, self.row, self.core, 1), self.last_x, links.x_way
        )

    def result(self, write):
        links = self.links
        for half, copy, source in ((0, self.y_last, self.last_y), (1, self.x_last, self.last_x)):
            copy.arrived()
            own = self.chunk(links.dp, self.row, self.core, half)
            blocks, depth, _ = source.shape
            rows = 32 if depth % 32 == 0 else 16

            def body(index, carry, own=own, source=source, half=half, depth=depth, rows=rows):
                block = lax.div(index, depth // rows)
                start = pl.multiple_of(lax.rem(index, depth // rows) * rows, rows)
                at = pl.ds(start, rows)
                value = own[block, at, :].astype(jnp.float32)
                value = value + source[block, at, :].astype(jnp.float32)
                write(block, pl.ds(pl.multiple_of(start + half * depth, rows), rows), value)
                return carry

            lax.fori_loop(0, blocks * (depth // rows), body, 0)


def plane_shapes(n_dp, blocks, n_uly, depth, width):
    return [
        (n_dp, blocks, n_uly, depth, width),
        (n_dp, 2, blocks, depth, width),
        (2, blocks, depth // 2, width),
        (n_dp, blocks, depth // 2, width),
        (blocks, depth // 2, width),
        (blocks, depth // 2, width),
    ]


def plane_scratch(*sizes):
    return [pltpu.VMEM(shape, jnp.bfloat16) for shape in plane_shapes(*sizes)]


def weight_grad(rows, right, parts, dp):
    _, blocks, n_uly, depth, width = parts.shape
    columns = 512

    def body(index, carry):
        at = pl.ds(pl.multiple_of(index * columns, columns), columns)
        part = jnp.dot(rows[...], right[:, at], preferred_element_type=jnp.float32)
        parts[dp, :, :, :, at] = part.astype(jnp.bfloat16).reshape(blocks, n_uly, depth, columns)
        return carry

    lax.fori_loop(0, width // columns, body, 0)


def rows_turned(left, parts, dp):
    count = parts.shape[1] * parts.shape[2] * parts.shape[3]
    return left[:, pl.ds(pl.multiple_of(dp * count, 128), count)].T


def turned(rows, cosine, sine):
    return rows * cosine + pltpu.roll(rows, HEAD_SIZE // 2, axis=1) * sine


def transposed_product(left, right):
    return lax.dot_general(
        left, right, (((0,), (0,)), ((), ())), preferred_element_type=jnp.float32
    )


def product_right(left, right):
    return lax.dot_general(
        left, right, (((1,), (1,)), ((), ())), preferred_element_type=jnp.float32
    )


SCORE_SCALE = 1.0 / math.sqrt(HEAD_SIZE)


def forward_kernel(
    toks,
    gain_rows,
    span_order,
    hidden,
    wq,
    wk,
    wv,
    wo,
    wg,
    wu,
    wd,
    cotangent,
    gains,
    q_gain,
    k_gain,
    all_qkv,
    all_wo,
    all_wg,
    all_wu,
    all_wd,
    all_cot,
    attn_gain,
    mlp_gain,
    cosine,
    sine,
    query_pos,
    key_pos,
    heads,
    normed,
    qkv,
    queries,
    key_values,
    lse,
    middle,
    all_normed,
    all_gains,
    all_hidden,
    near_qkv,
    near_wo,
    parts,
    rightward,
    leftward,
    own_normed,
    send,
    recv,
    here,
):
    links = Links(send, recv, here)
    links.greet(links.peers() + [links.x_way, links.y_way, links.core_way])
    tokens, width = hidden.shape
    spans = halves(tokens)
    q_width, k_width = wq.shape[1] // links.n_blk, wk.shape[1] // links.n_blk
    chunk = all_qkv.at[links.dp, :, links.uly]
    swap = ColumnSwap(
        links, [(wq, chunk, 0), (wk, chunk, q_width), (wv, chunk, q_width + k_width)]
    )
    plane_wo = PlaneGather(links, rows_of(all_wo, False))
    plane_wd = PlaneGather(links, rows_of(all_wd, False))
    plane_qkv = PlaneGather(links, rows_of(all_qkv, True))
    plane_gain = PlaneGather(links, rows_of(all_gains, True))
    swap.start()
    my_gains = all_gains.at[links.dp, links.blk, links.uly]
    gain_swap = [links.to(gains, my_gains, device) for device in links.peers()]
    plane_wo.start(wo)
    line = HalvedLine(links, hidden, all_hidden)
    line.send(0)
    keep = [
        links.local(gains, my_gains),
        links.local(hidden, all_hidden.at[links.blk]),
        links.local(wo, all_wo.at[links.dp, links.uly]),
        links.local(wd, all_wd.at[links.dp, links.uly]),
        links.local(cotangent, all_cot.at[links.blk]),
    ]
    write_positions(links, span_order, toks, cosine, sine, query_pos, key_pos)
    swap.arrived()
    plane_qkv.start()
    keep[0].wait()
    for copy in gain_swap:
        copy.arrived()
    plane_gain.start()
    plane_wd.start(wd)
    plane_wo.hand_on()
    line.advance(1)
    plane_qkv.hand_on()
    plane_gain.hand_on()
    plane_wo.last()
    for step in range(2, links.n_blk - 1):
        line.advance(step)
    pairs = [(wg, all_wg), (wu, all_wu)]
    planes = [PlaneGather(links, rows_of(whole, True)) for _, whole in pairs]
    swaps = [
        ColumnSwap(links, [(weight, whole.at[links.dp, :, links.uly], 0)])
        for weight, whole in pairs
    ]
    for swap in swaps:
        swap.start()
    plane_qkv.last()
    plane_gain.last()
    plane_gain.arrived()
    write_gains(links, all_gains, gain_rows, (attn_gain, mlp_gain))
    for copy in keep[1:]:
        copy.wait()
    plane_wo.arrived()
    plane_qkv.arrived()
    near = [links.local(all_qkv, near_qkv), links.local(all_wo, near_wo)]
    seqs, kv_heads, q_rows, _ = queries.shape
    q_len = key_values.shape[4]
    group = q_rows // q_len
    q_end = kv_heads * group * HEAD_SIZE
    k_end = q_end + kv_heads * HEAD_SIZE

    def norm(seq):
        def body(rows):
            for blk in range(links.n_blk):
                at = pl.ds(pl.multiple_of(seq * toks + rows.start, ROWS), ROWS)
                to = pl.ds(pl.multiple_of(seq * q_len + blk * toks + rows.start, ROWS), ROWS)
                source = all_hidden[blk, at, :].astype(jnp.float32)
                normed[to, :] = (source * rms_scale(source) * attn_gain[...]).astype(
                    jnp.bfloat16
                )

        each_block(toks, body)

    def rotated(seq, column, gain):
        pre = qkv[seq * q_len : (seq + 1) * q_len, column : column + HEAD_SIZE]
        gain = gain[...].astype(jnp.float32)
        return turned(pre * rms_scale(pre) * gain, cosine[...], sine[...]).astype(jnp.bfloat16)

    def project(seq):
        rows = slice(seq * q_len, (seq + 1) * q_len)
        for column in range(0, qkv.shape[1], 512):
            weight = near_qkv[:, :, :, :, column : column + 512].reshape(width, 512)
            qkv[rows, column : column + 512] = jnp.dot(
                normed[rows, :], weight, preferred_element_type=jnp.float32
            )
        for head in range(kv_heads):
            column = head * HEAD_SIZE
            key_values[links.uly, 0, seq, head] = rotated(seq, q_end + column, k_gain)
            key_values[links.uly, 1, seq, head] = qkv[
                rows, k_end + column : k_end + column + HEAD_SIZE
            ].astype(jnp.bfloat16)
        mine = key_values.at[links.uly, :, seq]
        copies = [links.to(mine, mine, way) for way in (links.core_way, links.y_way)]
        for head in range(kv_heads * group):
            at = pl.ds((head % group) * q_len, q_len)
            queries[seq, head // group, at, :] = rotated(seq, head * HEAD_SIZE, q_gain)
        return copies

    def hand_keys(seq, copies):
        copies[1].arrived()
        theirs = key_values.at[links.across, :, seq]
        copies.append(links.to(theirs, theirs, links.core_way))

    def attend(seq, head):
        def over_keys(piece, carry):
            total, mixed = carry
            rows = pl.ds(pl.multiple_of(piece * q_len, q_len), q_len)
            scores = product_right(key_values[piece, 0, seq, head], queries[seq, head])
            weights = jnp.where(
                query_pos[...] >= key_pos[rows, :], jnp.exp(scores * SCORE_SCALE), 0.0
            )
            total = total + jnp.sum(weights, axis=0, keepdims=True)
            mixed = mixed + transposed_product(
                key_values[piece, 1, seq, head], weights.astype(jnp.bfloat16)
            )
            return total, mixed

        total, mixed = lax.fori_loop(
            0,
            links.n_uly,
            over_keys,
            (
                jnp.zeros((1, q_rows), jnp.float32),
                jnp.zeros((HEAD_SIZE, q_rows), jnp.float32),
            ),
        )
        lse[seq * kv_heads + head] = jnp.log(total)
        attended = (mixed / total).T.astype(jnp.bfloat16)
        for member in range(group):
            column = (head * group + member) * HEAD_SIZE
            for blk in range(links.n_blk):
                row = (blk * seqs + seq) * toks
                start = member * q_len + blk * toks
                heads[row : row + toks, column : column + HEAD_SIZE] = attended[
                    start : start + toks, :
                ]

    sums = halved_sums(links, parts, rightward, leftward)
    def out_weight():
        return near_wo[...].reshape(heads.shape[1], width)

    def out_parts(seq):
        mixed = jnp.concatenate(
            [
                heads[(blk * seqs + seq) * toks : (blk * seqs + seq + 1) * toks, :]
                for blk in range(links.n_blk)
            ],
            axis=0,
        )
        for column in range(0, width, 512):
            parts[:, spans[seq], column : column + 512] = (
                jnp.dot(
                    mixed,
                    out_weight()[:, column : column + 512],
                    preferred_element_type=jnp.float32,
                )
                .astype(jnp.bfloat16)
                .reshape(links.n_blk, toks, 512)
            )
        sums[seq].start()

    key_copies = []
    for seq in range(seqs):
        line.lines[seq].arrived()
        norm(seq)
        if seq == 0:
            for copy in near:
                copy.wait()
        key_copies.append(project(seq))
    plane_wd.hand_on()
    hand_keys(0, key_copies[0])
    for copy in (key_copies[0][0], key_copies[0][2]):
        copy.arrived()
    attend(0, 0)
    hand_keys(1, key_copies[1])
    for head in range(1, kv_heads):
        attend(0, head)
    out_parts(0)
    swaps[0].arrived()
    planes[0].start()
    for copy in (key_copies[1][0], key_copies[1][2]):
        copy.arrived()
    attend(1, 0)
    for head in range(1, kv_heads):
        attend(1, head)
    out_parts(1)
    cot_lines = HalvedLine(links, cotangent, all_cot).lines
    for half in cot_lines:
        half.send(0)
    sums[0].tick(1)
    swaps[1].arrived()
    planes[1].start()
    later = range(2, links.n_blk - 1)
    for tick in later:
        sums[0].tick(tick)
    plane_wd.last()
    planes[0].hand_on()
    lines = []

    def settle(half, rows_of_half):
        half.finish(middle.at[rows_of_half])

        def body(rows):
            at = pl.ds(pl.multiple_of(rows_of_half.start + rows.start, ROWS), ROWS)
            total = middle[at, :] + all_hidden[links.blk, at, :].astype(jnp.float32)
            middle[at, :] = total
            own_normed[at, :] = (total * rms_scale(total) * mlp_gain[...]).astype(jnp.bfloat16)

        each_block(tokens // 2, body)
        next_line = LineGather(links, own_normed.at[rows_of_half], all_normed.at[:, rows_of_half])
        next_line.send(0)
        lines.append(next_line)

    settle(sums[0], spans[0])
    for half in cot_lines:
        half.arrived()
        half.send(1)
    sums[1].tick(1)
    for tick in later:
        sums[1].tick(tick)
    settle(sums[1], spans[1])
    for step in range(2, links.n_blk - 1):
        for half in cot_lines:
            half.arrived()
            half.send(step)
    last_local = links.local(own_normed, all_normed.at[links.blk])
    planes[1].hand_on()
    planes[0].last()
    for step in range(1, links.n_blk - 1):
        for half in lines:
            half.arrived()
            half.send(step)
    planes[1].last()
    for half in lines + cot_lines:
        half.arrived()
    for plane in [plane_wd] + planes:
        plane.arrived()
    last_local.wait()
    for half in sums:
        half.sent()
    links.finish()


SMEM = pl.BlockSpec(memory_space=pltpu.SMEM)


def forward(
    span_order,
    hidden,
    wq,
    wk,
    wv,
    wo,
    wg,
    wu,
    wd,
    cotangent,
    gains,
    q_gain,
    k_gain,
    seqs,
    gain_rows,
):
    n_dp, n_blk, n_uly = (lax.axis_size(a) for a in EVERY)
    tokens, width = hidden.shape
    toks = tokens // seqs
    rows, q_len = n_blk * tokens, n_blk * toks
    group = QUERY_HEADS // KEY_VALUE_HEADS
    kv_heads = KEY_VALUE_HEADS // n_blk
    q_rows, keys = group * q_len, n_uly * q_len
    columns = (wq.shape[1] + wk.shape[1] + wv.shape[1]) // n_blk
    f32, low, i32 = jnp.float32, jnp.bfloat16, jnp.int32
    ff = wg.shape[1] // n_blk
    far = [
        (n_dp, n_blk, n_uly, wq.shape[0], columns),
        (n_dp, n_uly) + wo.shape,
        (n_dp, n_blk, n_uly, wg.shape[0], ff),
        (n_dp, n_blk, n_uly, wu.shape[0], ff),
        (n_dp, n_uly) + wd.shape,
        (n_blk, tokens, width),
    ]
    near = [
        ((1, width), f32),
        ((1, width), f32),
        ((q_len, HEAD_SIZE), f32),
        ((q_len, HEAD_SIZE), f32),
        ((1, q_rows), i32),
        ((keys, 1), i32),
        ((rows, kv_heads * group * HEAD_SIZE), low),
        ((rows, width), low),
        ((rows, columns), f32),
        ((seqs, kv_heads, q_rows, HEAD_SIZE), low),
        ((n_uly, 2, seqs, kv_heads, q_len, HEAD_SIZE), low),
        ((seqs * kv_heads, 1, q_rows), f32),
        ((tokens, width), f32),
        ((n_blk, tokens, width), low),
    ]
    scratch = [
        ((n_dp, n_blk, n_uly) + gains.shape, low),
        ((n_blk, tokens, width), low),
        (far[0], low),
        (far[1], low),
        ((n_blk, tokens, width), low),
        ((n_blk - 1, tokens, width), low),
        ((n_blk - 1, tokens, width), low),
        ((tokens, width), low),
    ]
    return pl.pallas_call(
        functools.partial(forward_kernel, toks, gain_rows),
        out_shape=[jax.ShapeDtypeStruct(shape, low) for shape in far]
        + [jax.ShapeDtypeStruct(shape, kind) for shape, kind in near],
        in_specs=[SMEM] + [HBM] * 10 + [VMEM] * 2,
        out_specs=[HBM] * len(far) + [VMEM] * len(near),
        scratch_shapes=[pltpu.VMEM(shape, kind) for shape, kind in scratch]
        + semaphores(160, 32),
        compiler_params=kernel_params(0),
    )(span_order, hidden, wq, wk, wv, wo, wg, wu, wd, cotangent, gains, q_gain, k_gain)


def back_rows(grad_normed, source, gain):
    unit = source * rms_scale(source)
    scaled = grad_normed * gain
    return rms_scale(source) * (
        scaled - unit * jnp.mean(scaled * unit, axis=-1, keepdims=True)
    )


def back_kernel(
    grad_parts,
    out_parts,
    middle,
    cotangent,
    gain,
    all_normed,
    grad_gate_pre,
    grad_up_pre,
    activated,
    all_cot,
    output,
    grad_middle,
    all_low,
    grad_gate,
    grad_up,
    part_down,
    rightward,
    leftward,
    out_right,
    out_left,
    out_total,
    low,
    turned_low,
    gate_1,
    gate_2,
    gate_3,
    gate_4,
    gate_5,
    gate_6,
    up_1,
    up_2,
    up_3,
    up_4,
    up_5,
    up_6,
    down_1,
    down_2,
    send,
    recv,
    here,
):
    links = Links(send, recv, here)
    links.greet(links.peers() + [links.x_way, links.y_way, links.core_way])
    sums = halved_sums(links, grad_parts, rightward, leftward)
    for half in sums:
        half.start()
    out = OutputHalf(links, 0, out_parts, middle, out_right, out_left, out_total)
    gate = PlaneScatter(links, gate_1, gate_2, gate_3, gate_4, gate_5, gate_6)
    up = PlaneScatter(links, up_1, up_2, up_3, up_4, up_5, up_6)
    down = PlaneScatter(links, down_1, down_2, None, None, None, None)
    tokens = middle.shape[0]
    spans, lines, keep = halves(tokens), [], []

    def compute(plane, which, rows, right):
        dp = links.dp if which == 1 else links.other_dp
        weight_grad(rows, right, plane.parts, dp)
        plane.between_cores(which)

    def turn(which):
        dp = links.dp if which == 1 else links.other_dp
        turned_low[which] = rows_turned(all_normed, gate_1, dp)

    def compute_down(which):
        dp = links.dp if which == 1 else links.other_dp
        compute(down, which, rows_turned(activated, down_1, dp), all_cot)

    def settle(half, rows_of_half):
        half.finish(grad_middle.at[rows_of_half])

        def body(rows):
            at = pl.ds(pl.multiple_of(rows_of_half.start + rows.start, ROWS), ROWS)
            back = back_rows(grad_middle[at, :], middle[at, :], gain[...])
            grad = cotangent[at, :].astype(jnp.float32) + back
            grad_middle[at, :] = grad
            low[at, :] = grad.astype(jnp.bfloat16)

        each_block(tokens // 2, body)
        line = LineGather(links, low.at[rows_of_half], all_low.at[:, rows_of_half])
        line.send(0)
        lines.append(line)

    later = range(2, links.n_blk - 1)
    turn(0)
    compute(gate, 0, turned_low.at[0], grad_gate_pre)
    sums[0].tick(1)
    turn(1)
    compute(gate, 1, turned_low.at[1], grad_gate_pre)
    for tick in later:
        sums[0].tick(tick)
    gate.across_chips()
    settle(sums[0], spans[0])
    compute(up, 0, turned_low.at[0], grad_up_pre)
    sums[1].tick(1)
    compute(up, 1, turned_low.at[1], grad_up_pre)
    for tick in later:
        sums[1].tick(tick)
    up.across_chips()
    settle(sums[1], spans[1])
    out.sum.start()
    keep.append(links.local(low, all_low.at[links.blk]))
    compute_down(0)
    for step in range(1, links.n_blk - 1):
        for line in lines:
            line.arrived()
            line.send(step)
        if step == 1:
            gate.second_way()
            compute_down(1)
    out.sum.tick(1)
    up.second_way()
    for which in (0, 1):
        down.core_sums(which)
    for dp in range(links.n_dp):
        for row in range(2):
            keep.append(links.local(down.chunk(dp, row, down.core), part_down.at[dp, row]))
    for tick in later:
        out.sum.tick(tick)
    for line in lines:
        line.arrived()

    def into(target):
        def write(block, rows, values):
            target[block, rows, :] = values.astype(target.dtype)

        return write

    gate.result(into(grad_gate))
    up.result(into(grad_up))
    out.write(output)
    out.sum.sent()
    for copy in keep:
        copy.wait()
    for half in sums:
        half.sent()
    links.finish()


def exchange_back(
    grad_parts,
    out_parts,
    middle,
    cotangent,
    gain,
    all_normed,
    grad_gate_pre,
    grad_up_pre,
    activated,
    all_cot,
):
    n_dp, n_blk, n_uly = (lax.axis_size(a) for a in EVERY)
    _, tokens, width = grad_parts.shape
    ff = grad_gate_pre.shape[1]
    depth = width // (n_dp * n_blk * n_uly)
    down_depth = ff // (n_dp * n_uly)
    return pl.pallas_call(
        back_kernel,
        out_shape=[
            jax.ShapeDtypeStruct((tokens // 2, width), jnp.bfloat16),
            jax.ShapeDtypeStruct((tokens, width), jnp.float32),
            jax.ShapeDtypeStruct((n_blk, tokens, width), jnp.bfloat16),
            jax.ShapeDtypeStruct((n_blk, depth, ff), jnp.bfloat16),
            jax.ShapeDtypeStruct((n_blk, depth, ff), jnp.bfloat16),
            jax.ShapeDtypeStruct((n_dp, 2, 1, down_depth, width), jnp.bfloat16),
        ],
        in_specs=[VMEM] * 10,
        out_specs=[VMEM, VMEM, HBM, VMEM, VMEM, HBM],
        scratch_shapes=line_scratch(n_blk, tokens, width)
        + output_scratch(n_blk, tokens, width)
        + [
            pltpu.VMEM((tokens, width), jnp.bfloat16),
            pltpu.VMEM((n_dp, width // n_dp, n_blk * tokens), jnp.bfloat16),
        ]
        + plane_scratch(n_dp, n_blk, n_uly, depth, ff) * 2
        + plane_scratch(n_dp, 1, n_uly, down_depth, width)[:2]
        + semaphores(72),
        compiler_params=kernel_params(3),
    )(
        grad_parts,
        out_parts,
        middle,
        cotangent,
        gain,
        all_normed,
        grad_gate_pre,
        grad_up_pre,
        activated,
        all_cot,
    )


def backward_kernel(
    all_low,
    wo,
    queries,
    key_values,
    lse,
    qkv,
    q_gain,
    k_gain,
    cosine,
    sine,
    query_pos,
    key_pos,
    w_qkv,
    hidden,
    grad_middle,
    gain,
    normed,
    heads,
    out_parts,
    middle,
    grad_gate,
    grad_up,
    part_down,
    grad_hidden,
    grad_wo,
    grad_down,
    small_sum,
    output,
    gate_rows,
    up_rows,
    grad_w_qkv,
    grad_qkv,
    gain_terms,
    grad_heads,
    grad_rows,
    probs,
    grad_probs,
    grad_kv,
    from_core,
    from_across,
    grad_parts,
    rightward,
    leftward,
    summed,
    small_in,
    small_total,
    out_right,
    out_left,
    out_total,
    down_1,
    down_3,
    down_4,
    down_5,
    down_6,
    turned_normed,
    q_1,
    q_2,
    q_3,
    q_4,
    q_5,
    q_6,
    kv_1,
    kv_2,
    kv_3,
    kv_4,
    kv_5,
    kv_6,
    wo_1,
    wo_2,
    wo_3,
    wo_4,
    wo_5,
    wo_6,
    send,
    recv,
    here,
):
    links = Links(send, recv, here)
    links.greet(links.peers() + [links.x_way, links.y_way, links.core_way])
    tokens = hidden.shape[0]
    spans = halves(tokens)
    output_half = OutputHalf(links, 1, out_parts, middle, out_right, out_left, out_total)
    output_half.sum.start()
    down = PlaneScatter(links, down_1, None, down_3, down_4, down_5, down_6)
    fetch = links.local(part_down, down_1)
    swapped, keep = [], []
    for source, target in ((grad_gate, gate_rows), (grad_up, up_rows)):
        swapped += links.swap(
            lambda peer, source=source, target=target: [(source.at[peer], target.at[links.blk])]
        )
        keep.append(links.local(source.at[links.blk], target.at[links.blk]))
    fetch.wait()
    down.across_chips()
    sums = halved_sums(links, grad_parts, rightward, leftward)
    q_sums = PlaneScatter(links, q_1, q_2, q_3, q_4, q_5, q_6)
    kv_sums = PlaneScatter(links, kv_1, kv_2, kv_3, kv_4, kv_5, kv_6)
    wo_sums = PlaneScatter(links, wo_1, wo_2, wo_3, wo_4, wo_5, wo_6)
    seqs, kv_heads, q_rows, _ = queries.shape
    q_len = key_values.shape[4]
    group = q_rows // q_len
    toks = q_len // links.n_blk
    q_end = kv_heads * group * HEAD_SIZE
    k_end = q_end + kv_heads * HEAD_SIZE
    gain_terms[...] = jnp.zeros_like(gain_terms)
    later = range(2, links.n_blk - 1)

    def heads_back(seq):
        low = jnp.concatenate(
            [
                all_low[(blk * seqs + seq) * toks : (blk * seqs + seq + 1) * toks, :]
                for blk in range(links.n_blk)
            ],
            axis=0,
        )
        grad_heads[...] = product_right(low, wo[...])
        for head in range(kv_heads * group):
            to = pl.ds((head % group) * q_len, q_len)
            grad_rows[seq, head // group, to, :] = grad_heads[
                :, head * HEAD_SIZE : (head + 1) * HEAD_SIZE
            ].astype(jnp.bfloat16)

    def back_norm(upstream, seq, column, gain, which):
        rows = slice(seq * q_len, (seq + 1) * q_len)
        pre = qkv[rows, column : column + HEAD_SIZE]
        upstream = turned(upstream, cosine[...], -sine[...])
        gain_terms[which : which + 1, :] += jnp.sum(
            upstream * pre * rms_scale(pre), axis=0, keepdims=True
        )
        grad_qkv[rows, column : column + HEAD_SIZE] = back_rows(
            upstream, pre, gain[...].astype(jnp.float32)
        ).astype(jnp.bfloat16)

    def back(seq, head):
        def first(piece, delta):
            rows = pl.ds(pl.multiple_of(piece * q_len, q_len), q_len)
            scores = product_right(key_values[piece, 0, seq, head], queries[seq, head])
            prob = jnp.where(
                query_pos[...] >= key_pos[rows, :],
                jnp.exp(scores * SCORE_SCALE - lse[seq * kv_heads + head]),
                0.0,
            )
            grad_prob = product_right(key_values[piece, 1, seq, head], grad_rows[seq, head])
            probs[rows, :] = prob
            grad_probs[rows, :] = grad_prob
            return delta + jnp.sum(prob * grad_prob, axis=0, keepdims=True)

        delta = lax.fori_loop(0, links.n_uly, first, jnp.zeros((1, q_rows), jnp.float32))

        def second(piece, grad_query):
            rows = pl.ds(pl.multiple_of(piece * q_len, q_len), q_len)
            prob = probs[rows, :]
            grad_score = (prob * (grad_probs[rows, :] - delta)).astype(jnp.bfloat16)
            grad_kv[seq, piece, 0, head] = (
                SCORE_SCALE
                * jnp.dot(grad_score, queries[seq, head], preferred_element_type=jnp.float32)
            ).astype(jnp.bfloat16)
            grad_kv[seq, piece, 1, head] = jnp.dot(
                prob.astype(jnp.bfloat16),
                grad_rows[seq, head],
                preferred_element_type=jnp.float32,
            ).astype(jnp.bfloat16)
            return grad_query + transposed_product(key_values[piece, 0, seq, head], grad_score)

        grad_query = lax.fori_loop(
            0, links.n_uly, second, jnp.zeros((HEAD_SIZE, q_rows), jnp.float32)
        )
        turned_back = (grad_query * SCORE_SCALE).T
        for member in range(group):
            column = (head * group + member) * HEAD_SIZE
            back_norm(
                turned_back[member * q_len : (member + 1) * q_len, :], seq, column, q_gain, 0
            )

    core, line = lax.rem(links.uly, 2), lax.div(links.uly, 2)

    def add(target, source):
        for kind in range(2):
            for head in range(kv_heads):
                target[kind, head] = target[kind, head] + source[kind, head]

    def core_sums(seq):
        return [
            links.to(
                grad_kv.at[seq, row * 2 + 1 - core], from_core.at[seq, row], links.core_way
            )
            for row in range(2)
        ]

    def across_sums(seq, copies):
        for row in range(2):
            copies[row].arrived()
            add(grad_kv.at[seq, row * 2 + core], from_core.at[seq, row])
        return links.to(
            grad_kv.at[seq, (1 - line) * 2 + core], from_across.at[seq], links.y_way
        )

    def own_keys(seq, copy):
        copy.arrived()
        rows = slice(seq * q_len, (seq + 1) * q_len)
        for head in range(kv_heads):
            term = [
                grad_kv[seq, links.uly, kind, head].astype(jnp.float32)
                + from_across[seq, kind, head].astype(jnp.float32)
                for kind in range(2)
            ]
            back_norm(term[0], seq, q_end + head * HEAD_SIZE, k_gain, 1)
            v_at = k_end + head * HEAD_SIZE
            grad_qkv[rows, v_at : v_at + HEAD_SIZE] = term[1].astype(jnp.bfloat16)

    def normed_parts(seq):
        for column in range(0, w_qkv.shape[0], 512):
            grad_parts[:, spans[seq], column : column + 512] = (
                product_right(
                    grad_qkv[seq * q_len : (seq + 1) * q_len, :],
                    w_qkv[column : column + 512, :],
                )
                .astype(jnp.bfloat16)
                .reshape(links.n_blk, toks, 512)
            )
        sums[seq].start()

    def dp_of(which):
        return links.dp if which == 1 else links.other_dp

    def compute_wo(which):
        dp = dp_of(which)
        weight_grad(rows_turned(heads, wo_1, dp), all_low, wo_1, dp)
        wo_sums.between_cores(which)

    def compute_qkv(plane, which, columns):
        weight_grad(
            turned_normed.at[which], grad_qkv.at[:, columns], plane.parts, dp_of(which)
        )
        plane.between_cores(which)

    q_columns, kv_columns = pl.ds(0, q_end), pl.ds(q_end, grad_qkv.shape[1] - q_end)
    heads_back(0)
    back(0, 0)
    output_half.sum.tick(1)
    for head in range(1, kv_heads):
        back(0, head)
    core_copies = core_sums(0)
    heads_back(1)
    down.second_way()
    for which in range(2):
        turned_normed[which] = rows_turned(normed, q_1, dp_of(which))
    back(1, 0)
    across = across_sums(0, core_copies)
    for tick in later:
        output_half.sum.tick(tick)
    for head in range(1, kv_heads):
        back(1, head)
    core_copies = core_sums(1)
    own_keys(0, across)
    across = across_sums(1, core_copies)
    normed_parts(0)
    compute_qkv(q_sums, 0, q_columns)
    compute_qkv(q_sums, 1, q_columns)
    own_keys(1, across)
    small_total[0] = gain_terms[...]
    pending = links.to(small_total.at[0], small_in.at[links.n_blk], links.core_way)
    compute_qkv(kv_sums, 0, kv_columns)
    sums[0].tick(1)
    compute_qkv(kv_sums, 1, kv_columns)
    q_sums.across_chips()
    normed_parts(1)
    for tick in later:
        sums[0].tick(tick)
    pending.arrived()
    small_total[1] = small_total[0] + small_in[links.n_blk]
    pending = links.to(small_total.at[1], small_in.at[links.n_blk + 1], links.x_way)
    kv_sums.across_chips()
    compute_wo(0)
    compute_wo(1)
    q_sums.second_way()
    pending.arrived()
    small_total[2] = small_total[1] + small_in[links.n_blk + 1]
    pending = links.to(small_total.at[2], small_in.at[links.n_blk + 2], links.y_way)
    sums[1].tick(1)
    kv_sums.second_way()
    wo_sums.across_chips()

    def into(target):
        def write(block, rows, values):
            target[block, rows, :] = values.astype(target.dtype)

        return write

    def give_home(plane, columns):
        here, there = summed.at[:, :, columns], grad_w_qkv.at[links.blk, :, columns]
        plane.result(into(here))
        keep.append(links.local(here.at[links.blk], there))
        return links.swap(lambda peer: [(here.at[peer], there)])

    swapped += give_home(q_sums, q_columns)
    for tick in later:
        sums[1].tick(tick)
    pending.arrived()
    small_in[links.blk] = small_total[2] + small_in[links.n_blk + 2]
    mine = small_in.at[links.blk]
    small_copies = [links.to(mine, mine, device) for device in links.peers()]
    swapped += give_home(kv_sums, kv_columns)
    output_half.write(output)

    def settle(seq):
        sums[seq].finish(grad_hidden.at[spans[seq]])

        def body(rows):
            at = pl.ds(pl.multiple_of(spans[seq].start + rows.start, ROWS), ROWS)
            back = back_rows(grad_hidden[at, :], hidden[at, :].astype(jnp.float32), gain[...])
            grad_hidden[at, :] = grad_middle[at, :] + back

        each_block(toks, body)

    settle(0)
    wo_sums.second_way()
    down.result(into(grad_down))
    settle(1)
    wo_sums.result(into(grad_wo))
    for copy in small_copies:
        copy.arrived()
    total = small_in[0]
    for blk in range(1, links.n_blk):
        total = total + small_in[blk]
    small_sum[...] = total
    for copy in swapped:
        copy.arrived()
    for copy in keep:
        copy.wait()
    for half in sums:
        half.sent()
    output_half.sum.sent()
    links.finish()


def backward(
    all_low,
    wo,
    queries,
    key_values,
    lse,
    qkv,
    q_gain,
    k_gain,
    cosine,
    sine,
    query_pos,
    key_pos,
    w_qkv,
    hidden,
    grad_middle,
    gain,
    normed,
    heads,
    out_parts,
    middle,
    grad_gate,
    grad_up,
    part_down,
):
    seqs, kv_heads, q_rows, _ = queries.shape
    n_uly, _, _, _, q_len, _ = key_values.shape
    n_blk, tokens, width = out_parts.shape
    n_dp, _, _, down_depth, _ = part_down.shape
    keys, columns = key_pos.shape[0], qkv.shape[1]
    depth = width // (n_dp * n_blk * n_uly)
    out_depth = heads.shape[1] // (n_dp * n_uly)
    f32, low = jnp.float32, jnp.bfloat16
    small = (8, HEAD_SIZE)
    outs = [
        ((tokens, width), f32),
        ((1, out_depth, width), f32),
        ((1, down_depth, width), f32),
        (small, f32),
        ((tokens // 2, width), low),
        (grad_gate.shape, low),
        (grad_up.shape, low),
        ((n_blk, depth, columns), low),
    ]
    scratch = [
        (qkv.shape, low),
        (small, f32),
        ((q_len, heads.shape[1]), f32),
        (queries.shape, low),
        ((keys, q_rows), f32),
        ((keys, q_rows), f32),
        ((seqs, n_uly, 2, kv_heads, q_len, HEAD_SIZE), low),
        ((seqs, 2, 2, kv_heads, q_len, HEAD_SIZE), low),
        ((seqs, 2, kv_heads, q_len, HEAD_SIZE), low),
        (out_parts.shape, low),
        ((n_blk - 1, tokens, width), low),
        ((n_blk - 1, tokens, width), low),
        ((n_blk, depth, columns), low),
        ((n_blk + 3,) + small, f32),
        ((3,) + small, f32),
    ]
    down = [part_down.shape] + plane_shapes(n_dp, 1, n_uly, down_depth, width)[2:]
    return pl.pallas_call(
        backward_kernel,
        out_shape=[jax.ShapeDtypeStruct(shape, kind) for shape, kind in outs],
        in_specs=[VMEM] * 20 + [HBM] * 3,
        out_specs=[VMEM] * 5 + [HBM] * 3,
        scratch_shapes=[pltpu.VMEM(shape, kind) for shape, kind in scratch]
        + output_scratch(n_blk, tokens, width)
        + [pltpu.VMEM(shape, low) for shape in down]
        + [pltpu.VMEM((n_dp, width // n_dp, normed.shape[0]), low)]
        + plane_scratch(n_dp, n_blk, n_uly, depth, heads.shape[1])
        + plane_scratch(n_dp, n_blk, n_uly, depth, columns - heads.shape[1])
        + plane_scratch(n_dp, 1, n_uly, out_depth, width)
        + semaphores(112),
        compiler_params=kernel_params(4),
    )(
        all_low,
        wo,
        queries,
        key_values,
        lse,
        qkv,
        q_gain,
        k_gain,
        cosine,
        sine,
        query_pos,
        key_pos,
        w_qkv,
        hidden,
        grad_middle,
        gain,
        normed,
        heads,
        out_parts,
        middle,
        grad_gate,
        grad_up,
        part_down,
    )


def finish_kernel(
    gate,
    up,
    qkv,
    wo,
    wd,
    hidden,
    out_0,
    out_1,
    w_gate,
    w_up,
    w_query,
    key_weight,
    value_weight,
    attn_gain,
    mlp_gain,
    small,
    f_gate,
    f_up,
    f_q,
    f_k,
    f_v,
    f_wo,
    f_wd,
    f_hidden,
    f_out,
    f_attn,
    f_mlp,
    f_q_gain,
    f_k_gain,
):
    n_blk, depth, _ = gate.shape

    def place(source, offset, target):
        width = target.shape[1] // (n_blk * 2)
        for blk in range(n_blk):
            for group in range(2):
                to = (group * n_blk + blk) * width
                at = offset + group * width
                target[:, to : to + width] = source[blk, :, at : at + width].astype(jnp.float32)

    def gain_back(pairs, gain):
        total = jnp.zeros((depth, 128), jnp.float32)
        for weight, grad in pairs:
            for column in range(0, weight.shape[1], 128):
                at = slice(column, column + 128)
                total = total + weight[:, at].astype(jnp.float32) * grad[:, at]
        column = jnp.sum(total, axis=1, keepdims=True)
        square = (depth, depth)
        same = lax.broadcasted_iota(jnp.int32, square, 0) == lax.broadcasted_iota(
            jnp.int32, square, 1
        )
        return jnp.sum(jnp.where(same, column, 0.0), axis=0, keepdims=True) / gain[
            ...
        ].astype(jnp.float32)

    place(gate, 0, f_gate)
    place(up, 0, f_up)
    q_width = f_q.shape[1] // n_blk
    k_width = f_k.shape[1] // n_blk
    place(qkv, 0, f_q)
    place(qkv, q_width, f_k)
    place(qkv, q_width + k_width, f_v)
    f_q_gain[...] = small[0:1, :]
    f_k_gain[...] = small[1:2, :]
    f_wo[...] = wo[0]
    f_wd[...] = wd[0]
    f_hidden[...] = hidden[...]
    half = out_0.shape[0]
    f_out[:half, :] = out_0[...]
    f_out[half:, :] = out_1[...]
    f_attn[...] = gain_back(((w_query, f_q), (key_weight, f_k), (value_weight, f_v)), attn_gain)
    f_mlp[...] = gain_back(((w_gate, f_gate), (w_up, f_up)), mlp_gain)


def finish(gate, up, qkv, wo, wd, hidden, out_0, out_1, weights, gains, small):
    return pl.pallas_call(
        finish_kernel,
        out_shape=[jax.ShapeDtypeStruct(w.shape, jnp.float32) for w in weights]
        + [
            jax.ShapeDtypeStruct(wo.shape[1:], jnp.float32),
            jax.ShapeDtypeStruct(wd.shape[1:], jnp.float32),
            jax.ShapeDtypeStruct(hidden.shape, jnp.float32),
            jax.ShapeDtypeStruct(hidden.shape, jnp.bfloat16),
        ]
        + [jax.ShapeDtypeStruct(gain.shape, jnp.float32) for gain in gains]
        + [jax.ShapeDtypeStruct((1, small.shape[1]), jnp.float32)] * 2,
        in_specs=[VMEM] * 16,
        out_specs=[VMEM] * 13,
        compiler_params=pltpu.CompilerParams(vmem_limit_bytes=62 * MIB),
    )(gate, up, qkv, wo, wd, hidden, out_0, out_1, *weights, *gains, small)


def product(left, right):
    return jnp.dot(left, right, preferred_element_type=jnp.float32)


def shards(
    hidden,
    span_order,
    attn_gain,
    w_query,
    key_weight,
    value_weight,
    w_out,
    q_gain,
    k_gain,
    mlp_gain,
    w_gate,
    w_up,
    w_down,
    cotangent,
):
    seqs, toks, width = hidden.shape
    n_dp, n_blk, n_uly = (lax.axis_size(a) for a in EVERY)
    rows = n_blk * seqs * toks
    bf16 = jnp.bfloat16
    own_hidden = hidden.reshape(seqs * toks, width)
    own_cotangent = cotangent.reshape(seqs * toks, width)

    gain_q, gain_k = q_gain[None, :], k_gain[None, :]
    gain_rows = attn_gain.shape[0]
    own_gains = jnp.pad(jnp.stack([attn_gain, mlp_gain]), ((0, 30), (0, 128 - gain_rows)))
    (
        w_qkv,
        wo,
        all_wg,
        all_wu,
        all_wd,
        cot,
        g_attn,
        g_mlp,
        cosine,
        sine,
        query_pos,
        key_pos,
        heads_flat,
        normed,
        qkv,
        queries,
        key_values,
        lse,
        middle,
        normed2,
    ) = forward(
        span_order,
        own_hidden,
        w_query,
        key_weight,
        value_weight,
        w_out,
        w_gate,
        w_up,
        w_down,
        own_cotangent,
        own_gains,
        gain_q,
        gain_k,
        seqs,
        gain_rows,
    )
    w_qkv = w_qkv.reshape(width, -1)
    wo = wo.reshape(-1, width)
    wg, wu = all_wg.reshape(width, -1), all_wu.reshape(width, -1)
    wd = all_wd.reshape(-1, width)
    cot = cot.reshape(rows, width)
    normed2 = normed2.reshape(rows, width)
    gate_pre = product(normed2, wg)
    up_pre = product(normed2, wu)
    sigmoid_gate = jax.nn.sigmoid(gate_pre)
    activated = (gate_pre * sigmoid_gate * up_pre).astype(bf16)
    out_parts = product(activated, wd).astype(bf16)
    grad_act = product_right(cot, wd)
    grad_gate_pre = (
        grad_act * up_pre * sigmoid_gate * (1.0 + gate_pre * (1.0 - sigmoid_gate))
    ).astype(bf16)
    grad_up_pre = (grad_act * gate_pre * sigmoid_gate).astype(bf16)
    grad_parts = (product_right(grad_gate_pre, wg) + product_right(grad_up_pre, wu)).astype(bf16)
    blocks = (n_blk, seqs * toks, width)
    out_parts = out_parts.reshape(blocks)
    output_0, grad_middle, middle_low, grad_gate, grad_up, part_down = exchange_back(
        grad_parts.reshape(blocks),
        out_parts,
        middle,
        own_cotangent,
        g_mlp,
        normed2,
        grad_gate_pre,
        grad_up_pre,
        activated,
        cot,
    )
    middle_low = middle_low.reshape(rows, width)
    (
        grad_hidden,
        grad_out,
        grad_down,
        small,
        output_1,
        grad_gate,
        grad_up,
        grad_w_qkv,
    ) = backward(
        middle_low,
        wo,
        queries,
        key_values,
        lse,
        qkv,
        gain_q,
        gain_k,
        cosine,
        sine,
        query_pos,
        key_pos,
        w_qkv,
        own_hidden,
        grad_middle,
        g_attn,
        normed,
        heads_flat,
        out_parts,
        middle,
        grad_gate,
        grad_up,
        part_down,
    )
    (
        grad_gate,
        grad_up,
        grad_query,
        grad_key,
        grad_value,
        grad_out,
        grad_down,
        grad_hidden,
        output,
        grad_attn_gain,
        grad_mlp_gain,
        grad_q_gain,
        grad_k_gain,
    ) = finish(
        grad_gate,
        grad_up,
        grad_w_qkv,
        grad_out,
        grad_down,
        grad_hidden,
        output_0,
        output_1,
        (w_gate, w_up, w_query, key_weight, value_weight),
        [g[None, :] for g in (attn_gain, mlp_gain)],
        small,
    )
    return (
        output.reshape(hidden.shape),
        grad_hidden.reshape(hidden.shape),
        grad_attn_gain.reshape(gain_rows),
        grad_query,
        grad_key,
        grad_value,
        grad_out,
        grad_q_gain[0],
        grad_k_gain[0],
        grad_mlp_gain.reshape(gain_rows),
        grad_gate,
        grad_up,
        grad_down,
    )


def solution(mesh):
    n_dp, n_blk, n_uly = (mesh.shape[a] for a in EVERY)
    aligned = (n_dp, n_uly) == (2, 4) and KEY_VALUE_HEADS % (n_dp * n_blk) == 0
    in_specs = (
        TOKENS,
        P(),
        P(EVERY),
        P(EVERY, None),
        P(EVERY, None),
        P(EVERY, None),
        P(EVERY, None),
        P(),
        P(),
        P(EVERY),
        P(EVERY, None),
        P(EVERY, None),
        P(EVERY, None),
        TOKENS,
    )
    out_specs = (
        TOKENS,
        TOKENS,
        P(EVERY),
        P(EVERY, None),
        P(EVERY, None),
        P(EVERY, None),
        P(EVERY, None),
        P(),
        P(),
        P(EVERY),
        P(EVERY, None),
        P(EVERY, None),
        P(EVERY, None),
    )
    return jax.shard_map(
        shards if aligned else shards_general,
        mesh=mesh, in_specs=in_specs, out_specs=out_specs, check_vma=False)
```

```python
import functools
import math

import jax
import jax.numpy as jnp
from jax import lax
from jax.experimental import pallas as pl
from jax.experimental.pallas import tpu as pltpu
from jax.sharding import PartitionSpec as P

QUERY_HEADS = 16
KEY_VALUE_HEADS = 8
HEAD_SIZE = 128


DP, BLK, ULY = "dp", "blk", "uly"
EVERY = (DP, BLK, ULY)
PLANE = (DP, ULY)
TOKENS = P(DP, (BLK, ULY), None)
EQ_KGQD_NKD_TO_KGQN = "kgqd,nkd->kgqn"
EQ_KGQN_KGQD_TO_NKD = "kgqn,kgqd->nkd"
EQ_KGQN_NKD_TO_KGQD = "kgqn,nkd->kgqd"
EQ_KGQN_QKGD_TO_NKD = "kgqn,qkgd->nkd"
EQ_QKGD_NKD_TO_KGQN = "qkgd,nkd->kgqn"
EQ_STD_DE_TO_STE = "std,de->ste"
EQ_STD_DF_TO_STF = "std,df->stf"
EQ_STD_ED_TO_STE = "std,ed->ste"
EQ_STD_FD_TO_STF = "std,fd->stf"
EQ_STD_STE_TO_DE = "std,ste->de"
EQ_STD_STF_TO_DF = "std,stf->df"
EQ_STE_DE_TO_STD = "ste,de->std"
EQ_STE_ED_TO_STD = "ste,ed->std"
EQ_STE_STD_TO_ED = "ste,std->ed"
EQ_STF_DF_TO_STD = "stf,df->std"
EQ_STF_FD_TO_STD = "stf,fd->std"
EQ_STF_STD_TO_FD = "stf,std->fd"

EPSILON = 1e-06
ROPE_BASE = 1000000.0


def rms_scale(source):
    return lax.rsqrt(jnp.mean(source * source, axis=-1, keepdims=True) + EPSILON)


def norm_back(grad_normed, source, norm_scale, gain):
    unit_rows = source * norm_scale
    scaled = grad_normed * gain
    return norm_scale * (scaled - unit_rows * jnp.mean(scaled * unit_rows, axis=-1, keepdims=True))


def angles_of(positions, head_dim):
    freq_steps = jnp.arange(head_dim // 2, dtype=jnp.float32)
    inverse = jnp.exp(freq_steps * (-2.0 * math.log(ROPE_BASE) / head_dim))
    return positions.astype(jnp.float32)[:, None] * inverse[None, :]


def rotate(source, angles, direction):
    half_dim = source.shape[-1] // 2
    cosine = jnp.cos(angles)[:, None, :]
    sine_part = direction * jnp.sin(angles)[:, None, :]
    first_half = source[..., :half_dim]
    second_half = source[..., half_dim:]
    return jnp.concatenate(
        [
            first_half * cosine - second_half * sine_part,
            second_half * cosine + first_half * sine_part,
        ],
        axis=-1,
    )


def positions_of(places, span_order, half_len):
    blocks_of = places // half_len
    block_ids = jnp.arange(span_order.shape[0], dtype=jnp.int32)
    chosen = jnp.sum(
        jnp.where(blocks_of[:, None] == block_ids[None, :], span_order[None, :], 0), axis=1
    )
    return chosen * half_len + places % half_len


def add_rows(buffer, new_rows):
    return buffer + new_rows


def shards_general(
    hidden,
    span_order,
    attn_gain,
    w_query,
    key_weight,
    value_weight,
    w_out,
    q_gain,
    k_gain,
    mlp_gain,
    w_gate,
    w_up,
    w_down,
    cotangent,
):
    sequence_count = hidden.shape[0]
    token_count = hidden.shape[1]
    ulysses_group_size = lax.axis_size(ULY)
    local_q = QUERY_HEADS // ulysses_group_size
    local_key_value = KEY_VALUE_HEADS // ulysses_group_size
    query_group_width = QUERY_HEADS // KEY_VALUE_HEADS
    block_len = token_count * ulysses_group_size
    half_len = block_len // 2
    score_scale = 1.0 / math.sqrt(HEAD_SIZE)
    blk_index = lax.axis_index(BLK)
    uly_index = lax.axis_index(ULY)
    first_place = (blk_index * ulysses_group_size + uly_index) * token_count
    local_angles = angles_of(
        positions_of(first_place + jnp.arange(token_count, dtype=jnp.int32), span_order, half_len),
        HEAD_SIZE,
    )
    query_pos = positions_of(
        blk_index * block_len + jnp.arange(block_len, dtype=jnp.int32), span_order, half_len
    )
    g_attn, wq_all, wk_all, wv_all, wo_all = (
        lax.all_gather(attn_gain, EVERY, axis=0, tiled=True),
        lax.all_gather(w_query, EVERY, axis=0, tiled=True),
        lax.all_gather(key_weight, EVERY, axis=0, tiled=True),
        lax.all_gather(value_weight, EVERY, axis=0, tiled=True),
        lax.all_gather(w_out, EVERY, axis=0, tiled=True),
    )
    source = hidden.astype(jnp.float32)
    first_scale = rms_scale(source)
    normalized_input = (source * first_scale * g_attn.astype(jnp.float32)).astype(jnp.bfloat16)
    q_pre = jnp.einsum(
        EQ_STD_DE_TO_STE, normalized_input, wq_all, preferred_element_type=jnp.float32
    ).reshape(sequence_count, token_count, QUERY_HEADS, HEAD_SIZE)
    key_before_norm = jnp.einsum(
        EQ_STD_DE_TO_STE, normalized_input, wk_all, preferred_element_type=jnp.float32
    ).reshape(sequence_count, token_count, KEY_VALUE_HEADS, HEAD_SIZE)
    value_before_norm = jnp.einsum(
        EQ_STD_DE_TO_STE, normalized_input, wv_all, preferred_element_type=jnp.float32
    ).reshape(sequence_count, token_count, KEY_VALUE_HEADS, HEAD_SIZE)
    q_scale = rms_scale(q_pre)
    k_scale = rms_scale(key_before_norm)
    gain_q = q_gain.astype(jnp.float32)
    gain_k = k_gain.astype(jnp.float32)
    q_rot = rotate(q_pre * q_scale * gain_q, local_angles, 1.0).astype(jnp.bfloat16)
    k_rot = rotate(key_before_norm * k_scale * gain_k, local_angles, 1.0).astype(jnp.bfloat16)
    v_low = value_before_norm.astype(jnp.bfloat16)
    q_heads, k_heads, v_heads = (
        lax.all_to_all(q_rot, ULY, split_axis=2, concat_axis=1, tiled=True),
        lax.all_to_all(k_rot, ULY, split_axis=2, concat_axis=1, tiled=True),
        lax.all_to_all(v_low, ULY, split_axis=2, concat_axis=1, tiled=True),
    )
    q_group = q_heads.reshape(
        sequence_count, block_len, local_key_value, query_group_width, HEAD_SIZE
    )
    stat_shape = (sequence_count, local_key_value, query_group_width, block_len)
    start_state = (
        jnp.full(stat_shape, -1e30, jnp.float32),
        jnp.zeros(stat_shape, jnp.float32),
        jnp.zeros(stat_shape + (HEAD_SIZE,), jnp.float32),
    )
    key_piece = lax.all_gather(k_heads, BLK, axis=1, tiled=True)
    value_piece = lax.all_gather(v_heads, BLK, axis=1, tiled=True)
    key_pos = positions_of(jnp.arange(key_piece.shape[1], dtype=jnp.int32), span_order, half_len)
    allowed = query_pos[:, None] >= key_pos[None, :]

    def attend_one_sequence(members):
        query_rows, key_rows, value_rows, top_seq, total_seq, accum_seq = members
        scores = (
            jnp.einsum(EQ_QKGD_NKD_TO_KGQN, query_rows, key_rows, preferred_element_type=jnp.float32)
            * score_scale
        )
        scores = jnp.where(allowed, scores, -jnp.inf)
        new_top = jnp.maximum(top_seq, jnp.max(scores, axis=-1))
        fading = jnp.exp(top_seq - new_top)
        weights = jnp.exp(scores - new_top[..., None])
        total_seq = total_seq * fading + jnp.sum(weights, axis=-1)
        accum_seq = accum_seq * fading[..., None] + jnp.einsum(
            EQ_KGQN_NKD_TO_KGQD,
            weights.astype(jnp.bfloat16),
            value_rows,
            preferred_element_type=jnp.float32,
        )
        return (new_top, total_seq, accum_seq)

    row_top, row_total, accum = lax.map(
        attend_one_sequence,
        (q_group, key_piece, value_piece, start_state[0], start_state[1], start_state[2]),
    )
    log_total = row_top + jnp.log(row_total)
    attention_output = jnp.transpose(accum / row_total[..., None], (0, 3, 1, 2, 4)).reshape(
        sequence_count, block_len, local_q, HEAD_SIZE
    )
    heads_seq = lax.all_to_all(
        attention_output.astype(jnp.bfloat16), ULY, split_axis=1, concat_axis=2, tiled=True
    )
    heads_flat = heads_seq.reshape(sequence_count, token_count, QUERY_HEADS * HEAD_SIZE)
    middle = source + jnp.einsum(
        EQ_STE_ED_TO_STD, heads_flat, wo_all, preferred_element_type=jnp.float32
    )
    g_mlp, wg_all, wu_all, wd_all = (
        lax.all_gather(mlp_gain, EVERY, axis=0, tiled=True),
        lax.all_gather(w_gate, EVERY, axis=0, tiled=True),
        lax.all_gather(w_up, EVERY, axis=0, tiled=True),
        lax.all_gather(w_down, EVERY, axis=0, tiled=True),
    )
    second_scale = rms_scale(middle)
    gain_mlp = g_mlp.astype(jnp.float32)
    normed2 = (middle * second_scale * gain_mlp).astype(jnp.bfloat16)
    gate_pre = jnp.einsum(EQ_STD_DF_TO_STF, normed2, wg_all, preferred_element_type=jnp.float32)
    up_pre = jnp.einsum(EQ_STD_DF_TO_STF, normed2, wu_all, preferred_element_type=jnp.float32)
    sigmoid_gate = jax.nn.sigmoid(gate_pre)
    activated = (gate_pre * sigmoid_gate * up_pre).astype(jnp.bfloat16)
    result = middle + jnp.einsum(
        EQ_STF_FD_TO_STD, activated, wd_all, preferred_element_type=jnp.float32
    )
    output = result.astype(jnp.bfloat16)
    g_mlp, wg_all, wu_all, wd_all = (
        lax.all_gather(mlp_gain, EVERY, axis=0, tiled=True),
        lax.all_gather(w_gate, EVERY, axis=0, tiled=True),
        lax.all_gather(w_up, EVERY, axis=0, tiled=True),
        lax.all_gather(w_down, EVERY, axis=0, tiled=True),
    )
    gain_mlp = g_mlp.astype(jnp.float32)
    grad_act = jnp.einsum(EQ_STD_FD_TO_STF, cotangent, wd_all, preferred_element_type=jnp.float32)
    grad_gate_pre = (
        grad_act * up_pre * sigmoid_gate * (1.0 + gate_pre * (1.0 - sigmoid_gate))
    ).astype(jnp.bfloat16)
    grad_up_pre = (grad_act * gate_pre * sigmoid_gate).astype(jnp.bfloat16)
    grad_gate = jnp.einsum(
        EQ_STD_STF_TO_DF, normed2, grad_gate_pre, preferred_element_type=jnp.float32
    )
    grad_up = jnp.einsum(EQ_STD_STF_TO_DF, normed2, grad_up_pre, preferred_element_type=jnp.float32)
    grad_normed2 = jnp.einsum(
        EQ_STF_DF_TO_STD, grad_gate_pre, wg_all, preferred_element_type=jnp.float32
    ) + jnp.einsum(EQ_STF_DF_TO_STD, grad_up_pre, wu_all, preferred_element_type=jnp.float32)
    mlp_gain_term = jnp.sum(grad_normed2 * middle * second_scale, axis=(0, 1))
    grad_middle = cotangent.astype(jnp.float32) + norm_back(
        grad_normed2, middle, second_scale, gain_mlp
    )
    grad_mlp_gain, grad_gate, grad_up = (
        lax.psum_scatter(mlp_gain_term, EVERY, scatter_dimension=0, tiled=True),
        lax.psum_scatter(grad_gate, EVERY, scatter_dimension=0, tiled=True),
        lax.psum_scatter(grad_up, EVERY, scatter_dimension=0, tiled=True),
    )
    g_attn, wq_all, wk_all, wv_all, wo_all = (
        lax.all_gather(attn_gain, EVERY, axis=0, tiled=True),
        lax.all_gather(w_query, EVERY, axis=0, tiled=True),
        lax.all_gather(key_weight, EVERY, axis=0, tiled=True),
        lax.all_gather(value_weight, EVERY, axis=0, tiled=True),
        lax.all_gather(w_out, EVERY, axis=0, tiled=True),
    )
    middle_low = grad_middle.astype(jnp.bfloat16)
    grad_out = jnp.einsum(EQ_STE_STD_TO_ED, heads_flat, middle_low, preferred_element_type=jnp.float32)
    grad_heads = (
        jnp.einsum(EQ_STD_ED_TO_STE, middle_low, wo_all, preferred_element_type=jnp.float32)
        .astype(jnp.bfloat16)
        .reshape(sequence_count, token_count, QUERY_HEADS, HEAD_SIZE)
    )
    grad_heads_local = lax.all_to_all(grad_heads, ULY, split_axis=2, concat_axis=1, tiled=True)
    grad_group = jnp.transpose(
        grad_heads_local.reshape(
            sequence_count, block_len, local_key_value, query_group_width, HEAD_SIZE
        ),
        (0, 2, 3, 1, 4),
    )
    delta = jnp.sum(grad_heads_local.astype(jnp.float32) * attention_output, axis=-1)
    delta = jnp.transpose(
        delta.reshape(sequence_count, block_len, local_key_value, query_group_width), (0, 2, 3, 1)
    )
    seq_length = block_len * lax.axis_size(BLK)
    zero_keys = jnp.zeros((sequence_count, seq_length, local_key_value, HEAD_SIZE), jnp.float32)
    back_state = (jnp.zeros(stat_shape + (HEAD_SIZE,), jnp.float32), zero_keys, zero_keys)
    key_piece = lax.all_gather(k_heads, BLK, axis=1, tiled=True)
    value_piece = lax.all_gather(v_heads, BLK, axis=1, tiled=True)
    key_pos = positions_of(jnp.arange(key_piece.shape[1], dtype=jnp.int32), span_order, half_len)
    back_allowed = query_pos[:, None] >= key_pos[None, :]

    def back_one_sequence(members):
        query_rows, grad_rows, lse_seq, delta_seq, key_rows, value_rows, dq_seq, dk_seq, dv_seq = (
            members
        )
        scores = (
            jnp.einsum(EQ_QKGD_NKD_TO_KGQN, query_rows, key_rows, preferred_element_type=jnp.float32)
            * score_scale
        )
        scores = jnp.where(back_allowed, scores, -jnp.inf)
        probs = jnp.exp(scores - lse_seq[..., None])
        grad_values = jnp.einsum(
            EQ_KGQN_KGQD_TO_NKD,
            probs.astype(jnp.bfloat16),
            grad_rows,
            preferred_element_type=jnp.float32,
        )
        grad_probs = jnp.einsum(
            EQ_KGQD_NKD_TO_KGQN, grad_rows, value_rows, preferred_element_type=jnp.float32
        )
        grad_scores = (probs * (grad_probs - delta_seq[..., None])).astype(jnp.bfloat16)
        dq_seq = dq_seq + score_scale * jnp.einsum(
            EQ_KGQN_NKD_TO_KGQD, grad_scores, key_rows, preferred_element_type=jnp.float32
        )
        grad_keys = score_scale * jnp.einsum(
            EQ_KGQN_QKGD_TO_NKD, grad_scores, query_rows, preferred_element_type=jnp.float32
        )
        return (dq_seq, add_rows(dk_seq, grad_keys), add_rows(dv_seq, grad_values))

    grad_q_group, grad_k_whole, grad_v_whole = lax.map(
        back_one_sequence,
        (
            q_group,
            grad_group,
            log_total,
            delta,
            key_piece,
            value_piece,
            back_state[0],
            back_state[1],
            back_state[2],
        ),
    )
    grad_k_block, grad_v_block = (
        lax.psum_scatter(
            grad_k_whole.astype(jnp.bfloat16), BLK, scatter_dimension=1, tiled=True
        ).astype(jnp.float32),
        lax.psum_scatter(
            grad_v_whole.astype(jnp.bfloat16), BLK, scatter_dimension=1, tiled=True
        ).astype(jnp.float32),
    )
    grad_q_block = jnp.transpose(grad_q_group, (0, 3, 1, 2, 4)).reshape(
        sequence_count, block_len, local_q, HEAD_SIZE
    )
    grad_q_seq, grad_k_seq, value_sequence_gradient = (
        lax.all_to_all(
            grad_q_block.astype(jnp.bfloat16), ULY, split_axis=1, concat_axis=2, tiled=True
        ).astype(grad_q_block.dtype),
        lax.all_to_all(
            grad_k_block.astype(jnp.bfloat16), ULY, split_axis=1, concat_axis=2, tiled=True
        ).astype(grad_k_block.dtype),
        lax.all_to_all(
            grad_v_block.astype(jnp.bfloat16), ULY, split_axis=1, concat_axis=2, tiled=True
        ).astype(grad_v_block.dtype),
    )
    grad_q_normed = rotate(grad_q_seq, local_angles, -1.0)
    grad_k_normed = rotate(grad_k_seq, local_angles, -1.0)
    q_gain_term = jnp.sum(grad_q_normed * q_pre * q_scale, axis=(0, 1, 2))
    k_gain_term = jnp.sum(grad_k_normed * key_before_norm * k_scale, axis=(0, 1, 2))
    grad_q_pre = (
        norm_back(grad_q_normed, q_pre, q_scale, gain_q)
        .astype(jnp.bfloat16)
        .reshape(sequence_count, token_count, QUERY_HEADS * HEAD_SIZE)
    )
    grad_k_pre = (
        norm_back(grad_k_normed, key_before_norm, k_scale, gain_k)
        .astype(jnp.bfloat16)
        .reshape(sequence_count, token_count, KEY_VALUE_HEADS * HEAD_SIZE)
    )
    value_pre_gradient = value_sequence_gradient.astype(jnp.bfloat16).reshape(
        sequence_count, token_count, KEY_VALUE_HEADS * HEAD_SIZE
    )
    grad_query = jnp.einsum(
        EQ_STD_STE_TO_DE, normalized_input, grad_q_pre, preferred_element_type=jnp.float32
    )
    grad_key = jnp.einsum(
        EQ_STD_STE_TO_DE, normalized_input, grad_k_pre, preferred_element_type=jnp.float32
    )
    grad_value = jnp.einsum(
        EQ_STD_STE_TO_DE, normalized_input, value_pre_gradient, preferred_element_type=jnp.float32
    )
    grad_normed = jnp.einsum(EQ_STE_DE_TO_STD, grad_q_pre, wq_all, preferred_element_type=jnp.float32)
    grad_normed = grad_normed + jnp.einsum(
        EQ_STE_DE_TO_STD, grad_k_pre, wk_all, preferred_element_type=jnp.float32
    )
    grad_normed = grad_normed + jnp.einsum(
        EQ_STE_DE_TO_STD, value_pre_gradient, wv_all, preferred_element_type=jnp.float32
    )
    attn_gain_term = jnp.sum(grad_normed * source * first_scale, axis=(0, 1))
    grad_hidden = grad_middle + norm_back(
        grad_normed, source, first_scale, g_attn.astype(jnp.float32)
    )
    grad_down = jnp.einsum(EQ_STF_STD_TO_FD, activated, cotangent, preferred_element_type=jnp.float32)
    grad_attn_gain, grad_query, grad_key, grad_value, grad_out, grad_down = (
        lax.psum_scatter(attn_gain_term, EVERY, scatter_dimension=0, tiled=True),
        lax.psum_scatter(grad_query, EVERY, scatter_dimension=0, tiled=True),
        lax.psum_scatter(grad_key, EVERY, scatter_dimension=0, tiled=True),
        lax.psum_scatter(grad_value, EVERY, scatter_dimension=0, tiled=True),
        lax.psum_scatter(grad_out, EVERY, scatter_dimension=0, tiled=True),
        lax.psum_scatter(grad_down, EVERY, scatter_dimension=0, tiled=True),
    )
    grad_q_gain, grad_k_gain = lax.psum((q_gain_term, k_gain_term), EVERY)
    return (
        output,
        grad_hidden,
        grad_attn_gain,
        grad_query,
        grad_key,
        grad_value,
        grad_out,
        grad_q_gain,
        grad_k_gain,
        grad_mlp_gain,
        grad_gate,
        grad_up,
        grad_down,
    )


MESH = pl.DeviceIdType.MESH
HBM = pl.BlockSpec(memory_space=pltpu.HBM)
VMEM = pl.BlockSpec(memory_space=pltpu.VMEM)
MIB = 1 << 20


def kernel_params(collective_id, vmem_mib=62):
    return pltpu.CompilerParams(
        collective_id=collective_id, has_side_effects=True, vmem_limit_bytes=vmem_mib * MIB
    )


def semaphores(count, local=16):
    return [
        pltpu.SemaphoreType.DMA((count,)),
        pltpu.SemaphoreType.DMA((count,)),
        pltpu.SemaphoreType.DMA((local,)),
    ]


class Copy:
    def __init__(self, descriptor, sends, receives):
        self.descriptor, self.sends, self.receives = descriptor, sends, receives

    def under(self, condition, action):
        if condition is None:
            action()
        else:
            pl.when(condition)(action)

    def start(self):
        self.under(self.sends, lambda: self.descriptor().start())
        return self

    def sent(self):
        self.under(self.sends, lambda: self.descriptor().wait_send())

    def arrived(self):
        self.under(self.receives, lambda: self.descriptor().wait_recv())


class Links:
    def __init__(self, send, recv, here):
        self.send, self.recv, self.here = send, recv, here
        self.used, self.used_here = 0, 0
        self.copies, self.local_copies = [], []
        self.n_dp, self.n_blk, self.n_uly = (lax.axis_size(a) for a in EVERY)
        self.dp, self.blk, self.uly = (lax.axis_index(a) for a in EVERY)
        self.other_dp = 1 - self.dp
        self.across = lax.rem(self.uly + 2, 4)
        self.twin = self.uly + 1 - 2 * lax.rem(self.uly, 2)
        self.x_way = (self.other_dp, self.blk, self.uly)
        self.y_way = (self.dp, self.blk, self.across)
        self.core_way = (self.dp, self.blk, self.twin)

    def peer(self, step):
        return lax.rem(self.blk + step, self.n_blk)

    def peers(self):
        return [(self.dp, self.peer(k), self.uly) for k in range(1, self.n_blk)]

    def far_first(self):
        last = self.n_blk - 1
        orders = [
            sorted((p for p in range(self.n_blk) if p != b), key=lambda p, b=b: -abs(p - b))
            for b in range(self.n_blk)
        ]
        for b, order in enumerate(orders):
            ways = [[p for p in order if p > b], [p for p in order if p < b]]
            ways.sort(key=lambda way: -len(way))
            merged = []
            while ways[0] or ways[1]:
                for way in ways:
                    if way:
                        merged.append(way.pop(0))
            orders[b] = merged
        peers = []
        for turn in range(last):
            peer = jnp.int32(0)
            for b, order in enumerate(orders):
                peer = jnp.where(self.blk == b, order[turn], peer)
            peers.append(peer)
        return peers

    def swap(self, pieces_for):
        base, count = self.used, 0
        for peer in self.far_first():
            pieces = pieces_for(peer)
            count = len(pieces)
            distance = lax.rem(peer - self.blk + self.n_blk, self.n_blk) - 1
            for number, (source, target) in enumerate(pieces):
                self.swap_copy(base + distance * count + number, source, target, peer).start()
        self.used = base + (self.n_blk - 1) * count
        waits = []
        for slot in range(base, self.used):
            source, target = pieces_for(self.blk)[(slot - base) % count]

            def descriptor(slot=slot, source=source, target=target):
                return self.swap_copy(slot, source, target, self.peer(1))

            copy = Copy(descriptor, None, None)
            self.copies.append(copy)
            waits.append(copy)
        return waits

    def swap_copy(self, slot, source, target, peer):
        return pltpu.make_async_remote_copy(
            src_ref=source,
            dst_ref=target,
            send_sem=self.send.at[slot],
            recv_sem=self.recv.at[slot],
            device_id=(self.dp, peer, self.uly),
            device_id_type=MESH,
        )

    def greet(self, devices):
        barrier = pltpu.get_barrier_semaphore()
        for device in devices:
            pl.semaphore_signal(barrier, inc=1, device_id=device, device_id_type=MESH)
        pl.semaphore_wait(barrier, len(devices))

    def remote(self, source, target, device, sends=None, receives=None):
        slot = self.used
        self.used += 1

        def descriptor():
            return pltpu.make_async_remote_copy(
                src_ref=source(),
                dst_ref=target(),
                send_sem=self.send.at[slot],
                recv_sem=self.recv.at[slot],
                device_id=device,
                device_id_type=MESH,
            )

        copy = Copy(descriptor, sends, receives)
        self.copies.append(copy)
        return copy.start()

    def to(self, source, target, device):
        return self.remote(lambda: source, lambda: target, device)

    def local(self, source, target):
        copy = pltpu.make_async_copy(source, target, self.here.at[self.used_here])
        self.used_here += 1
        copy.start()
        self.local_copies.append(copy)
        return copy

    def finish(self):
        for copy in self.copies:
            copy.sent()


class LineGather:
    def __init__(self, links, own, whole):
        self.links, self.own, self.whole = links, own, whole
        self.waiting = []

    def send(self, step):
        links, whole = self.links, self.whole
        blk, last = links.blk, links.n_blk - 1

        def block(index):
            if step == 0:
                return lambda: self.own
            return lambda: whole.at[index]

        self.waiting = [
            links.remote(
                block(blk - step),
                lambda: whole.at[blk - step],
                (links.dp, blk + 1, links.uly),
                jnp.logical_and(blk >= step, blk < last),
                blk >= step + 1,
            ),
            links.remote(
                block(blk + step),
                lambda: whole.at[blk + step],
                (links.dp, blk - 1, links.uly),
                jnp.logical_and(blk + step <= last, blk > 0),
                blk + step + 1 <= last,
            ),
        ]

    def arrived(self):
        for copy in self.waiting:
            copy.arrived()


def halves(tokens):
    return [pl.ds(0, tokens // 2), pl.ds(tokens // 2, tokens // 2)]


class HalvedLine:
    def __init__(self, links, own, whole):
        self.lines = [
            LineGather(links, None if own is None else own.at[rows], whole.at[:, rows])
            for rows in halves(whole.shape[1])
        ]

    def send(self, step):
        for line in self.lines:
            line.send(step)

    def advance(self, step):
        for line in self.lines:
            line.arrived()
            line.send(step)

    def arrived(self):
        for line in self.lines:
            line.arrived()


class PlaneGather:
    def __init__(self, links, at):
        self.links, self.at = links, at

    def start_x(self, own):
        links = self.links
        mine = self.at(links.dp, links.uly)
        self.from_x = links.to(own, mine, links.x_way)
        self.from_core = [links.to(own, mine, links.core_way)]

    def start_y(self, own):
        links = self.links
        self.from_y = links.to(own, self.at(links.dp, links.uly), links.y_way)

    def start(self, own=None):
        own = self.at(self.links.dp, self.links.uly) if own is None else own
        self.start_x(own)
        self.start_y(own)

    def hand_on(self):
        links, at = self.links, self.at
        self.from_x.arrived()
        half = at(links.other_dp, links.uly, 0)
        self.second_y = links.to(half, half, links.y_way)
        self.from_y.arrived()
        half = at(links.dp, links.across, 1)
        self.second_x = links.to(half, half, links.x_way)
        for chunk in (at(links.other_dp, links.uly), at(links.dp, links.across)):
            self.from_core.append(links.to(chunk, chunk, links.core_way))

    def last(self):
        links = self.links
        self.second_y.arrived()
        self.second_x.arrived()
        chunk = self.at(links.other_dp, links.across)
        self.from_core.append(links.to(chunk, chunk, links.core_way))

    def arrived(self):
        for copy in self.from_core:
            copy.arrived()


def rows_of(whole, blocked):
    def at(dp, uly, half=None):
        part = whole.at[dp, :, uly] if blocked else whole.at[dp, uly]
        if half is None:
            return part
        depth = whole.shape[-2] // 2
        rows = pl.ds(half * depth, depth)
        return part.at[:, rows] if blocked else part.at[rows]

    return at


class ColumnSwap:
    def __init__(self, links, pieces):
        self.links, self.pieces = links, pieces
        self.incoming, self.kept = [], []

    def parts(self, blk):
        links = self.links
        for weight, whole, offset in self.pieces:
            width = weight.shape[-1] // links.n_dp // links.n_blk
            for group in range(links.n_dp):
                start = (group * links.n_blk + blk) * width
                yield (
                    weight.at[:, pl.ds(pl.multiple_of(start, 128), width)],
                    whole.at[links.blk, :, pl.ds(offset + group * width, width)],
                )

    def start(self):
        links = self.links
        self.incoming = links.swap(lambda peer: list(self.parts(peer)))
        for source, target in self.parts(links.blk):
            self.kept.append(links.local(source, target))

    def arrived(self):
        for copy in self.kept:
            copy.wait()
        for copy in self.incoming:
            copy.arrived()


def write_positions(links, span_order, toks, cosine, sine, query_pos, key_pos):
    half_len = toks * links.n_uly // 2

    def first(blk, uly):
        chunk = span_order[2 * blk + lax.div(uly, links.n_uly // 2)]
        return chunk * half_len + lax.rem(uly, links.n_uly // 2) * toks

    lane = lax.broadcasted_iota(jnp.int32, (toks, HEAD_SIZE), 1)
    row = lax.broadcasted_iota(jnp.int32, (toks, HEAD_SIZE), 0)
    upper = lane >= HEAD_SIZE // 2
    step = jnp.where(upper, lane - HEAD_SIZE // 2, lane).astype(jnp.float32)
    inverse = jnp.exp(step * (-2.0 * math.log(ROPE_BASE) / HEAD_SIZE))
    for blk in range(links.n_blk):
        angles = (first(blk, links.uly) + row).astype(jnp.float32) * inverse
        at = slice(blk * toks, (blk + 1) * toks)
        cosine[at, :] = jnp.cos(angles)
        turn = jnp.sin(angles)
        sine[at, :] = jnp.where(upper, turn, -turn)
    lane = lax.broadcasted_iota(jnp.int32, query_pos.shape, 1)
    place = jnp.zeros(query_pos.shape, jnp.int32)
    for start in range(0, query_pos.shape[1], toks):
        blk = start // toks % links.n_blk
        here = jnp.logical_and(lane >= start, lane < start + toks)
        place = jnp.where(here, first(blk, links.uly) + lane - start, place)
    query_pos[...] = place
    row = lax.broadcasted_iota(jnp.int32, (toks, 1), 0)
    for uly in range(links.n_uly):
        for blk in range(links.n_blk):
            start = (uly * links.n_blk + blk) * toks
            key_pos[start : start + toks, :] = row + first(blk, jnp.int32(uly))


def write_gains(links, all_gains, size, targets):
    per_row = 128 // size
    for which, target in enumerate(targets):
        for place in range(target.shape[1] // 128):
            pieces = []
            for part in range(per_row):
                device = place * per_row + part
                plane, uly = device // links.n_uly, device % links.n_uly
                gains = all_gains[plane // links.n_blk, plane % links.n_blk, uly]
                pieces.append(gains.astype(jnp.float32)[which : which + 1, :size])
            target[:, place * 128 : (place + 1) * 128] = jnp.concatenate(pieces, axis=1)


ROWS = 32


def each_block(count, body):
    def step(index, carry):
        body(pl.ds(pl.multiple_of(index * ROWS, ROWS), ROWS))
        return carry

    lax.fori_loop(0, count // ROWS, step, 0)


class LineScatter:
    def __init__(self, links, parts, rightward, leftward):
        self.links, self.parts = links, parts
        self.slots = {1: rightward, -1: leftward}
        self.tokens = parts.shape[1]
        self.number = links.used
        self.last = links.n_blk - 1
        links.used += 2 * self.last

    def target(self, step, way):
        return self.last - step if way == 1 else step

    def slot(self, step, way):
        target = self.target(step, way)
        return self.slots[way].at[target - 1 if way == 1 else target]

    def place(self, way):
        return self.links.blk if way == 1 else self.last - self.links.blk

    def copy(self, step, way, source=None):
        links, slot = self.links, self.slot(step, way)
        number = self.number + 2 * step + (1 if way == 1 else 0)
        return pltpu.make_async_remote_copy(
            src_ref=slot if source is None else source,
            dst_ref=slot,
            send_sem=links.send.at[number],
            recv_sem=links.recv.at[number],
            device_id=(links.dp, links.blk + way, links.uly),
            device_id_type=MESH,
        )

    def start(self):
        for step in range(self.last):
            for way in (1, -1):

                @pl.when(self.place(way) == 0)
                def _(step=step, way=way):
                    self.copy(step, way, self.parts.at[self.target(step, way)]).start()

    def tick(self, tick):
        for way in (1, -1):

            @pl.when(jnp.logical_and(self.place(way) >= 1, self.place(way) <= tick))
            def _(way=way):
                step = tick - self.place(way)
                self.copy(step, way).wait_recv()
                slot, target = self.slot(step, way), self.target(step, way)

                def body(rows):
                    slot[rows, :] = slot[rows, :] + self.parts[target, rows, :]

                each_block(self.tokens, body)
                self.copy(step, way).start()

    def finish(self, total):
        blk, last = self.links.blk, self.last

        def start(rows):
            total[rows, :] = self.parts[blk, rows, :].astype(jnp.float32)

        each_block(self.tokens, start)
        for way in (1, -1):

            @pl.when(self.place(way) >= 1)
            def _(way=way):
                step = last - self.place(way)
                self.copy(step, way).wait_recv()
                slot = self.slot(step, way)

                def body(rows):
                    total[rows, :] = total[rows, :] + slot[rows, :].astype(jnp.float32)

                each_block(self.tokens, body)

    def sent(self):
        for step in range(self.last):
            for way in (1, -1):
                beyond = self.place(way) + step < self.last
                pl.when(beyond)(lambda step=step, way=way: self.copy(step, way).wait_send())


def halved_sums(links, parts, rightward, leftward):
    return [
        LineScatter(links, parts.at[:, rows], rightward.at[:, rows], leftward.at[:, rows])
        for rows in halves(parts.shape[1])
    ]


class OutputHalf:
    def __init__(self, links, which, parts, middle, rightward, leftward, total):
        rows = halves(middle.shape[0])[which]
        self.middle, self.total = middle.at[rows], total
        self.sum = LineScatter(links, parts.at[:, rows], rightward, leftward)

    def write(self, output):
        self.sum.finish(self.total)

        def body(rows):
            output[rows, :] = (self.middle[rows, :] + self.total[rows, :]).astype(jnp.bfloat16)

        each_block(self.middle.shape[0], body)


def output_scratch(n_blk, tokens, width):
    return line_scratch(n_blk, tokens // 2, width) + [
        pltpu.VMEM((tokens // 2, width), jnp.float32)
    ]


def line_scratch(n_blk, tokens, width):
    return [pltpu.VMEM((n_blk - 1, tokens, width), jnp.bfloat16)] * 2


class PlaneScatter:
    def __init__(self, links, parts, from_core, from_x, from_y, last_x, last_y):
        self.links, self.parts = links, parts
        self.own_core_only = from_core is None
        self.from_core, self.from_x, self.from_y = from_core, from_x, from_y
        self.last_x, self.last_y = last_x, last_y
        self.core = lax.rem(links.uly, 2)
        self.row = lax.div(links.uly, 2)
        self.depth = parts.shape[3]
        self.core_copies = {}

    def chunk(self, dp, row, core, half=None):
        if self.own_core_only:
            part = self.parts.at[dp, row]
        else:
            part = self.parts.at[dp, :, row * 2 + core]
        if half is None:
            return part
        depth = self.depth // 2
        return part.at[:, pl.ds(half * depth, depth)]

    def add(self, target, source):
        blocks, depth, _ = target.shape
        rows = 32 if depth % 32 == 0 else 16

        def body(index, carry):
            block = lax.div(index, depth // rows)
            at = pl.ds(pl.multiple_of(lax.rem(index, depth // rows) * rows, rows), rows)
            target[block, at, :] = target[block, at, :] + source[block, at, :]
            return carry

        lax.fori_loop(0, blocks * (depth // rows), body, 0)

    def between_cores(self, which):
        links = self.links
        dp = links.dp if which == 1 else links.other_dp
        self.core_copies[which] = [
            links.to(
                self.chunk(dp, row, 1 - self.core), self.from_core.at[which, row], links.core_way
            )
            for row in range(2)
        ]

    def core_sums(self, which):
        links = self.links
        dp = links.dp if which == 1 else links.other_dp
        for row in range(2):
            self.core_copies[which][row].arrived()
            self.add(self.chunk(dp, row, self.core), self.from_core.at[which, row])

    def across_chips(self):
        links = self.links
        if not self.own_core_only:
            self.core_sums(0)
        self.x_copies = [
            links.to(
                self.chunk(links.other_dp, row, self.core, 0), self.from_x.at[row], links.x_way
            )
            for row in range(2)
        ]
        if not self.own_core_only:
            self.core_sums(1)
        self.y_copies = [
            links.to(
                self.chunk(group, 1 - self.row, self.core, 1),
                self.from_y.at[group],
                links.y_way,
            )
            for group in range(links.n_dp)
        ]

    def second_way(self):
        links = self.links
        for row in range(2):
            self.x_copies[row].arrived()
            self.add(self.chunk(links.dp, row, self.core, 0), self.from_x.at[row])
        self.y_last = links.to(
            self.chunk(links.dp, 1 - self.row, self.core, 0), self.last_y, links.y_way
        )
        for group in range(links.n_dp):
            self.y_copies[group].arrived()
            self.add(self.chunk(group, self.row, self.core, 1), self.from_y.at[group])
        self.x_last = links.to(
            self.chunk(links.other_dp, self.row, self.core, 1), self.last_x, links.x_way
        )

    def result(self, write):
        links = self.links
        for half, copy, source in ((0, self.y_last, self.last_y), (1, self.x_last, self.last_x)):
            copy.arrived()
            own = self.chunk(links.dp, self.row, self.core, half)
            blocks, depth, _ = source.shape
            rows = 32 if depth % 32 == 0 else 16

            def body(index, carry, own=own, source=source, half=half, depth=depth, rows=rows):
                block = lax.div(index, depth // rows)
                start = pl.multiple_of(lax.rem(index, depth // rows) * rows, rows)
                at = pl.ds(start, rows)
                value = own[block, at, :].astype(jnp.float32)
                value = value + source[block, at, :].astype(jnp.float32)
                write(block, pl.ds(pl.multiple_of(start + half * depth, rows), rows), value)
                return carry

            lax.fori_loop(0, blocks * (depth // rows), body, 0)


def plane_shapes(n_dp, blocks, n_uly, depth, width):
    return [
        (n_dp, blocks, n_uly, depth, width),
        (n_dp, 2, blocks, depth, width),
        (2, blocks, depth // 2, width),
        (n_dp, blocks, depth // 2, width),
        (blocks, depth // 2, width),
        (blocks, depth // 2, width),
    ]


def plane_scratch(*sizes):
    return [pltpu.VMEM(shape, jnp.bfloat16) for shape in plane_shapes(*sizes)]


def weight_grad(rows, right, parts, dp):
    _, blocks, n_uly, depth, width = parts.shape
    columns = 512

    def body(index, carry):
        at = pl.ds(pl.multiple_of(index * columns, columns), columns)
        part = jnp.dot(rows[...], right[:, at], preferred_element_type=jnp.float32)
        parts[dp, :, :, :, at] = part.astype(jnp.bfloat16).reshape(blocks, n_uly, depth, columns)
        return carry

    lax.fori_loop(0, width // columns, body, 0)


def rows_turned(left, parts, dp):
    count = parts.shape[1] * parts.shape[2] * parts.shape[3]
    return left[:, pl.ds(pl.multiple_of(dp * count, 128), count)].T


def turned(rows, cosine, sine):
    return rows * cosine + pltpu.roll(rows, HEAD_SIZE // 2, axis=1) * sine


def transposed_product(left, right):
    return lax.dot_general(
        left, right, (((0,), (0,)), ((), ())), preferred_element_type=jnp.float32
    )


def product_right(left, right):
    return lax.dot_general(
        left, right, (((1,), (1,)), ((), ())), preferred_element_type=jnp.float32
    )


SCORE_SCALE = 1.0 / math.sqrt(HEAD_SIZE)


def forward_kernel(
    toks,
    gain_rows,
    span_order,
    hidden,
    wq,
    wk,
    wv,
    wo,
    wg,
    wu,
    wd,
    cotangent,
    gains,
    q_gain,
    k_gain,
    all_qkv,
    all_wo,
    all_wg,
    all_wu,
    all_wd,
    all_cot,
    attn_gain,
    mlp_gain,
    cosine,
    sine,
    query_pos,
    key_pos,
    heads,
    normed,
    qkv,
    queries,
    key_values,
    lse,
    middle,
    all_normed,
    all_gains,
    all_hidden,
    near_qkv,
    near_wo,
    parts,
    rightward,
    leftward,
    own_normed,
    send,
    recv,
    here,
):
    links = Links(send, recv, here)
    links.greet(links.peers() + [links.x_way, links.y_way, links.core_way])
    tokens, width = hidden.shape
    spans = halves(tokens)
    q_width, k_width = wq.shape[1] // links.n_blk, wk.shape[1] // links.n_blk
    chunk = all_qkv.at[links.dp, :, links.uly]
    swap = ColumnSwap(
        links, [(wq, chunk, 0), (wk, chunk, q_width), (wv, chunk, q_width + k_width)]
    )
    plane_wo = PlaneGather(links, rows_of(all_wo, False))
    plane_wd = PlaneGather(links, rows_of(all_wd, False))
    plane_qkv = PlaneGather(links, rows_of(all_qkv, True))
    plane_gain = PlaneGather(links, rows_of(all_gains, True))
    swap.start()
    my_gains = all_gains.at[links.dp, links.blk, links.uly]
    gain_swap = [links.to(gains, my_gains, device) for device in links.peers()]
    plane_wo.start(wo)
    line = HalvedLine(links, hidden, all_hidden)
    line.send(0)
    keep = [
        links.local(gains, my_gains),
        links.local(hidden, all_hidden.at[links.blk]),
        links.local(wo, all_wo.at[links.dp, links.uly]),
        links.local(wd, all_wd.at[links.dp, links.uly]),
        links.local(cotangent, all_cot.at[links.blk]),
    ]
    write_positions(links, span_order, toks, cosine, sine, query_pos, key_pos)
    swap.arrived()
    plane_qkv.start()
    keep[0].wait()
    for copy in gain_swap:
        copy.arrived()
    plane_gain.start()
    plane_wd.start(wd)
    plane_wo.hand_on()
    line.advance(1)
    plane_qkv.hand_on()
    plane_gain.hand_on()
    plane_wo.last()
    for step in range(2, links.n_blk - 1):
        line.advance(step)
    pairs = [(wg, all_wg), (wu, all_wu)]
    planes = [PlaneGather(links, rows_of(whole, True)) for _, whole in pairs]
    swaps = [
        ColumnSwap(links, [(weight, whole.at[links.dp, :, links.uly], 0)])
        for weight, whole in pairs
    ]
    for swap in swaps:
        swap.start()
    cot_lines = HalvedLine(links, cotangent, all_cot).lines
    for half in cot_lines:
        half.send(0)
    plane_qkv.last()
    plane_gain.last()
    plane_gain.arrived()
    write_gains(links, all_gains, gain_rows, (attn_gain, mlp_gain))
    for copy in keep[1:]:
        copy.wait()
    plane_wo.arrived()
    plane_qkv.arrived()
    near = [links.local(all_qkv, near_qkv), links.local(all_wo, near_wo)]
    seqs, kv_heads, q_rows, _ = queries.shape
    q_len = key_values.shape[4]
    group = q_rows // q_len
    q_end = kv_heads * group * HEAD_SIZE
    k_end = q_end + kv_heads * HEAD_SIZE

    def norm(seq):
        def body(rows):
            for blk in range(links.n_blk):
                at = pl.ds(pl.multiple_of(seq * toks + rows.start, ROWS), ROWS)
                to = pl.ds(pl.multiple_of(seq * q_len + blk * toks + rows.start, ROWS), ROWS)
                source = all_hidden[blk, at, :].astype(jnp.float32)
                normed[to, :] = (source * rms_scale(source) * attn_gain[...]).astype(
                    jnp.bfloat16
                )

        each_block(toks, body)

    def rotated(seq, column, gain):
        pre = qkv[seq * q_len : (seq + 1) * q_len, column : column + HEAD_SIZE]
        gain = gain[...].astype(jnp.float32)
        return turned(pre * rms_scale(pre) * gain, cosine[...], sine[...]).astype(jnp.bfloat16)

    def project(seq):
        rows = slice(seq * q_len, (seq + 1) * q_len)
        for column in range(0, qkv.shape[1], 512):
            weight = near_qkv[:, :, :, :, column : column + 512].reshape(width, 512)
            qkv[rows, column : column + 512] = jnp.dot(
                normed[rows, :], weight, preferred_element_type=jnp.float32
            )
        for head in range(kv_heads):
            column = head * HEAD_SIZE
            key_values[links.uly, 0, seq, head] = rotated(seq, q_end + column, k_gain)
            key_values[links.uly, 1, seq, head] = qkv[
                rows, k_end + column : k_end + column + HEAD_SIZE
            ].astype(jnp.bfloat16)
        mine = key_values.at[links.uly, :, seq]
        copies = [links.to(mine, mine, way) for way in (links.core_way, links.y_way)]
        for head in range(kv_heads * group):
            at = pl.ds((head % group) * q_len, q_len)
            queries[seq, head // group, at, :] = rotated(seq, head * HEAD_SIZE, q_gain)
        return copies

    def hand_keys(seq, copies):
        copies[1].arrived()
        theirs = key_values.at[links.across, :, seq]
        copies.append(links.to(theirs, theirs, links.core_way))

    def attend(seq, head):
        def over_keys(piece, carry):
            total, mixed = carry
            rows = pl.ds(pl.multiple_of(piece * q_len, q_len), q_len)
            scores = product_right(key_values[piece, 0, seq, head], queries[seq, head])
            weights = jnp.where(
                query_pos[...] >= key_pos[rows, :], jnp.exp(scores * SCORE_SCALE), 0.0
            )
            total = total + jnp.sum(weights, axis=0, keepdims=True)
            mixed = mixed + transposed_product(
                key_values[piece, 1, seq, head], weights.astype(jnp.bfloat16)
            )
            return total, mixed

        total, mixed = lax.fori_loop(
            0,
            links.n_uly,
            over_keys,
            (
                jnp.zeros((1, q_rows), jnp.float32),
                jnp.zeros((HEAD_SIZE, q_rows), jnp.float32),
            ),
        )
        lse[seq * kv_heads + head] = jnp.log(total)
        attended = (mixed / total).T.astype(jnp.bfloat16)
        for member in range(group):
            column = (head * group + member) * HEAD_SIZE
            for blk in range(links.n_blk):
                row = (blk * seqs + seq) * toks
                start = member * q_len + blk * toks
                heads[row : row + toks, column : column + HEAD_SIZE] = attended[
                    start : start + toks, :
                ]

    sums = halved_sums(links, parts, rightward, leftward)
    def out_weight():
        return near_wo[...].reshape(heads.shape[1], width)

    def out_parts(seq):
        mixed = jnp.concatenate(
            [
                heads[(blk * seqs + seq) * toks : (blk * seqs + seq + 1) * toks, :]
                for blk in range(links.n_blk)
            ],
            axis=0,
        )
        for column in range(0, width, 512):
            parts[:, spans[seq], column : column + 512] = (
                jnp.dot(
                    mixed,
                    out_weight()[:, column : column + 512],
                    preferred_element_type=jnp.float32,
                )
                .astype(jnp.bfloat16)
                .reshape(links.n_blk, toks, 512)
            )
        sums[seq].start()

    key_copies = []
    for seq in range(seqs):
        line.lines[seq].arrived()
        norm(seq)
        if seq == 0:
            for copy in near:
                copy.wait()
        key_copies.append(project(seq))
    plane_wd.hand_on()
    hand_keys(0, key_copies[0])
    for copy in (key_copies[0][0], key_copies[0][2]):
        copy.arrived()
    attend(0, 0)
    hand_keys(1, key_copies[1])
    for head in range(1, kv_heads):
        attend(0, head)
    out_parts(0)
    swaps[0].arrived()
    planes[0].start()
    for copy in (key_copies[1][0], key_copies[1][2]):
        copy.arrived()
    attend(1, 0)
    sums[0].tick(1)
    for head in range(1, kv_heads):
        attend(1, head)
    out_parts(1)
    swaps[1].arrived()
    planes[1].start()
    later = range(2, links.n_blk - 1)
    for tick in later:
        sums[0].tick(tick)
    for half in cot_lines:
        half.arrived()
        half.send(1)
    plane_wd.last()
    planes[0].hand_on()
    lines = []

    def settle(half, rows_of_half):
        half.finish(middle.at[rows_of_half])

        def body(rows):
            at = pl.ds(pl.multiple_of(rows_of_half.start + rows.start, ROWS), ROWS)
            total = middle[at, :] + all_hidden[links.blk, at, :].astype(jnp.float32)
            middle[at, :] = total
            own_normed[at, :] = (total * rms_scale(total) * mlp_gain[...]).astype(jnp.bfloat16)

        each_block(tokens // 2, body)
        next_line = LineGather(links, own_normed.at[rows_of_half], all_normed.at[:, rows_of_half])
        next_line.send(0)
        lines.append(next_line)

    settle(sums[0], spans[0])
    sums[1].tick(1)
    for tick in later:
        sums[1].tick(tick)
    settle(sums[1], spans[1])
    for step in range(2, links.n_blk - 1):
        for half in cot_lines:
            half.arrived()
            half.send(step)
    last_local = links.local(own_normed, all_normed.at[links.blk])
    planes[1].hand_on()
    planes[0].last()
    for step in range(1, links.n_blk - 1):
        for half in lines:
            half.arrived()
            half.send(step)
    planes[1].last()
    for half in lines + cot_lines:
        half.arrived()
    for plane in [plane_wd] + planes:
        plane.arrived()
    last_local.wait()
    for half in sums:
        half.sent()
    links.finish()


SMEM = pl.BlockSpec(memory_space=pltpu.SMEM)


def forward(
    span_order,
    hidden,
    wq,
    wk,
    wv,
    wo,
    wg,
    wu,
    wd,
    cotangent,
    gains,
    q_gain,
    k_gain,
    seqs,
    gain_rows,
):
    n_dp, n_blk, n_uly = (lax.axis_size(a) for a in EVERY)
    tokens, width = hidden.shape
    toks = tokens // seqs
    rows, q_len = n_blk * tokens, n_blk * toks
    group = QUERY_HEADS // KEY_VALUE_HEADS
    kv_heads = KEY_VALUE_HEADS // n_blk
    q_rows, keys = group * q_len, n_uly * q_len
    columns = (wq.shape[1] + wk.shape[1] + wv.shape[1]) // n_blk
    f32, low, i32 = jnp.float32, jnp.bfloat16, jnp.int32
    ff = wg.shape[1] // n_blk
    far = [
        (n_dp, n_blk, n_uly, wq.shape[0], columns),
        (n_dp, n_uly) + wo.shape,
        (n_dp, n_blk, n_uly, wg.shape[0], ff),
        (n_dp, n_blk, n_uly, wu.shape[0], ff),
        (n_dp, n_uly) + wd.shape,
        (n_blk, tokens, width),
    ]
    near = [
        ((1, width), f32),
        ((1, width), f32),
        ((q_len, HEAD_SIZE), f32),
        ((q_len, HEAD_SIZE), f32),
        ((1, q_rows), i32),
        ((keys, 1), i32),
        ((rows, kv_heads * group * HEAD_SIZE), low),
        ((rows, width), low),
        ((rows, columns), f32),
        ((seqs, kv_heads, q_rows, HEAD_SIZE), low),
        ((n_uly, 2, seqs, kv_heads, q_len, HEAD_SIZE), low),
        ((seqs * kv_heads, 1, q_rows), f32),
        ((tokens, width), f32),
        ((n_blk, tokens, width), low),
    ]
    scratch = [
        ((n_dp, n_blk, n_uly) + gains.shape, low),
        ((n_blk, tokens, width), low),
        (far[0], low),
        (far[1], low),
        ((n_blk, tokens, width), low),
        ((n_blk - 1, tokens, width), low),
        ((n_blk - 1, tokens, width), low),
        ((tokens, width), low),
    ]
    return pl.pallas_call(
        functools.partial(forward_kernel, toks, gain_rows),
        out_shape=[jax.ShapeDtypeStruct(shape, low) for shape in far]
        + [jax.ShapeDtypeStruct(shape, kind) for shape, kind in near],
        in_specs=[SMEM] + [HBM] * 10 + [VMEM] * 2,
        out_specs=[HBM] * len(far) + [VMEM] * len(near),
        scratch_shapes=[pltpu.VMEM(shape, kind) for shape, kind in scratch]
        + semaphores(160, 32),
        compiler_params=kernel_params(0),
    )(span_order, hidden, wq, wk, wv, wo, wg, wu, wd, cotangent, gains, q_gain, k_gain)


def back_rows(grad_normed, source, gain):
    unit = source * rms_scale(source)
    scaled = grad_normed * gain
    return rms_scale(source) * (
        scaled - unit * jnp.mean(scaled * unit, axis=-1, keepdims=True)
    )


def back_kernel(
    grad_parts,
    out_parts,
    middle,
    cotangent,
    gain,
    all_normed,
    grad_gate_pre,
    grad_up_pre,
    activated,
    all_cot,
    output,
    grad_middle,
    all_low,
    grad_gate,
    grad_up,
    part_down,
    rightward,
    leftward,
    out_right,
    out_left,
    out_total,
    low,
    turned_low,
    gate_1,
    gate_2,
    gate_3,
    gate_4,
    gate_5,
    gate_6,
    up_1,
    up_2,
    up_3,
    up_4,
    up_5,
    up_6,
    down_1,
    down_2,
    send,
    recv,
    here,
):
    links = Links(send, recv, here)
    links.greet(links.peers() + [links.x_way, links.y_way, links.core_way])
    sums = halved_sums(links, grad_parts, rightward, leftward)
    for half in sums:
        half.start()
    out = OutputHalf(links, 0, out_parts, middle, out_right, out_left, out_total)
    gate = PlaneScatter(links, gate_1, gate_2, gate_3, gate_4, gate_5, gate_6)
    up = PlaneScatter(links, up_1, up_2, up_3, up_4, up_5, up_6)
    down = PlaneScatter(links, down_1, down_2, None, None, None, None)
    tokens = middle.shape[0]
    spans, lines, keep = halves(tokens), [], []

    def compute(plane, which, rows, right):
        dp = links.dp if which == 1 else links.other_dp
        weight_grad(rows, right, plane.parts, dp)
        plane.between_cores(which)

    def turn(which):
        dp = links.dp if which == 1 else links.other_dp
        turned_low[which] = rows_turned(all_normed, gate_1, dp)

    def compute_down(which):
        dp = links.dp if which == 1 else links.other_dp
        compute(down, which, rows_turned(activated, down_1, dp), all_cot)

    def settle(half, rows_of_half):
        half.finish(grad_middle.at[rows_of_half])

        def body(rows):
            at = pl.ds(pl.multiple_of(rows_of_half.start + rows.start, ROWS), ROWS)
            back = back_rows(grad_middle[at, :], middle[at, :], gain[...])
            grad = cotangent[at, :].astype(jnp.float32) + back
            grad_middle[at, :] = grad
            low[at, :] = grad.astype(jnp.bfloat16)

        each_block(tokens // 2, body)
        line = LineGather(links, low.at[rows_of_half], all_low.at[:, rows_of_half])
        line.send(0)
        lines.append(line)

    later = range(2, links.n_blk - 1)
    turn(0)
    compute(gate, 0, turned_low.at[0], grad_gate_pre)
    sums[0].tick(1)
    turn(1)
    compute(gate, 1, turned_low.at[1], grad_gate_pre)
    for tick in later:
        sums[0].tick(tick)
    gate.across_chips()
    settle(sums[0], spans[0])
    compute(up, 0, turned_low.at[0], grad_up_pre)
    sums[1].tick(1)
    compute(up, 1, turned_low.at[1], grad_up_pre)
    for tick in later:
        sums[1].tick(tick)
    up.across_chips()
    settle(sums[1], spans[1])
    out.sum.start()
    keep.append(links.local(low, all_low.at[links.blk]))
    compute_down(0)
    for step in range(1, links.n_blk - 1):
        for line in lines:
            line.arrived()
            line.send(step)
        if step == 1:
            gate.second_way()
            compute_down(1)
    out.sum.tick(1)
    up.second_way()
    for which in (0, 1):
        down.core_sums(which)
    for dp in range(links.n_dp):
        for row in range(2):
            keep.append(links.local(down.chunk(dp, row, down.core), part_down.at[dp, row]))
    for tick in later:
        out.sum.tick(tick)
    for line in lines:
        line.arrived()

    def into(target):
        def write(block, rows, values):
            target[block, rows, :] = values.astype(target.dtype)

        return write

    gate.result(into(grad_gate))
    up.result(into(grad_up))
    out.write(output)
    out.sum.sent()
    for copy in keep:
        copy.wait()
    for half in sums:
        half.sent()
    links.finish()


def exchange_back(
    grad_parts,
    out_parts,
    middle,
    cotangent,
    gain,
    all_normed,
    grad_gate_pre,
    grad_up_pre,
    activated,
    all_cot,
):
    n_dp, n_blk, n_uly = (lax.axis_size(a) for a in EVERY)
    _, tokens, width = grad_parts.shape
    ff = grad_gate_pre.shape[1]
    depth = width // (n_dp * n_blk * n_uly)
    down_depth = ff // (n_dp * n_uly)
    return pl.pallas_call(
        back_kernel,
        out_shape=[
            jax.ShapeDtypeStruct((tokens // 2, width), jnp.bfloat16),
            jax.ShapeDtypeStruct((tokens, width), jnp.float32),
            jax.ShapeDtypeStruct((n_blk, tokens, width), jnp.bfloat16),
            jax.ShapeDtypeStruct((n_blk, depth, ff), jnp.bfloat16),
            jax.ShapeDtypeStruct((n_blk, depth, ff), jnp.bfloat16),
            jax.ShapeDtypeStruct((n_dp, 2, 1, down_depth, width), jnp.bfloat16),
        ],
        in_specs=[VMEM] * 10,
        out_specs=[VMEM, VMEM, HBM, VMEM, VMEM, HBM],
        scratch_shapes=line_scratch(n_blk, tokens, width)
        + output_scratch(n_blk, tokens, width)
        + [
            pltpu.VMEM((tokens, width), jnp.bfloat16),
            pltpu.VMEM((n_dp, width // n_dp, n_blk * tokens), jnp.bfloat16),
        ]
        + plane_scratch(n_dp, n_blk, n_uly, depth, ff) * 2
        + plane_scratch(n_dp, 1, n_uly, down_depth, width)[:2]
        + semaphores(72),
        compiler_params=kernel_params(3),
    )(
        grad_parts,
        out_parts,
        middle,
        cotangent,
        gain,
        all_normed,
        grad_gate_pre,
        grad_up_pre,
        activated,
        all_cot,
    )


def backward_kernel(
    all_low,
    wo,
    queries,
    key_values,
    lse,
    qkv,
    q_gain,
    k_gain,
    cosine,
    sine,
    query_pos,
    key_pos,
    w_qkv,
    hidden,
    grad_middle,
    gain,
    normed,
    heads,
    out_parts,
    middle,
    grad_gate,
    grad_up,
    part_down,
    grad_hidden,
    grad_wo,
    grad_down,
    small_sum,
    output,
    gate_rows,
    up_rows,
    grad_w_qkv,
    grad_qkv,
    gain_terms,
    grad_heads,
    grad_rows,
    grad_kv,
    from_core,
    from_across,
    grad_parts,
    rightward,
    leftward,
    summed,
    small_in,
    small_total,
    out_right,
    out_left,
    out_total,
    down_1,
    down_3,
    down_4,
    down_5,
    down_6,
    turned_normed,
    q_1,
    q_2,
    q_3,
    q_4,
    q_5,
    q_6,
    kv_1,
    kv_2,
    kv_3,
    kv_4,
    kv_5,
    kv_6,
    wo_1,
    wo_2,
    wo_3,
    wo_4,
    wo_5,
    wo_6,
    send,
    recv,
    here,
):
    links = Links(send, recv, here)
    links.greet(links.peers() + [links.x_way, links.y_way, links.core_way])
    tokens = hidden.shape[0]
    spans = halves(tokens)
    output_half = OutputHalf(links, 1, out_parts, middle, out_right, out_left, out_total)
    output_half.sum.start()
    down = PlaneScatter(links, down_1, None, down_3, down_4, down_5, down_6)
    fetch = links.local(part_down, down_1)
    swapped, keep = [], []
    for source, target in ((grad_gate, gate_rows), (grad_up, up_rows)):
        swapped += links.swap(
            lambda peer, source=source, target=target: [(source.at[peer], target.at[links.blk])]
        )
        keep.append(links.local(source.at[links.blk], target.at[links.blk]))
    fetch.wait()
    down.across_chips()
    sums = halved_sums(links, grad_parts, rightward, leftward)
    q_sums = PlaneScatter(links, q_1, q_2, q_3, q_4, q_5, q_6)
    kv_sums = PlaneScatter(links, kv_1, kv_2, kv_3, kv_4, kv_5, kv_6)
    wo_sums = PlaneScatter(links, wo_1, wo_2, wo_3, wo_4, wo_5, wo_6)
    seqs, kv_heads, q_rows, _ = queries.shape
    q_len = key_values.shape[4]
    group = q_rows // q_len
    toks = q_len // links.n_blk
    q_end = kv_heads * group * HEAD_SIZE
    k_end = q_end + kv_heads * HEAD_SIZE
    gain_terms[...] = jnp.zeros_like(gain_terms)
    later = range(2, links.n_blk - 1)

    def heads_back(seq):
        low = jnp.concatenate(
            [
                all_low[(blk * seqs + seq) * toks : (blk * seqs + seq + 1) * toks, :]
                for blk in range(links.n_blk)
            ],
            axis=0,
        )
        grad_heads[...] = product_right(low, wo[...])
        for head in range(kv_heads * group):
            to = pl.ds((head % group) * q_len, q_len)
            grad_rows[seq, head // group, to, :] = grad_heads[
                :, head * HEAD_SIZE : (head + 1) * HEAD_SIZE
            ].astype(jnp.bfloat16)

    def back_norm(upstream, seq, column, gain, which):
        rows = slice(seq * q_len, (seq + 1) * q_len)
        pre = qkv[rows, column : column + HEAD_SIZE]
        upstream = turned(upstream, cosine[...], -sine[...])
        gain_terms[which : which + 1, :] += jnp.sum(
            upstream * pre * rms_scale(pre), axis=0, keepdims=True
        )
        grad_qkv[rows, column : column + HEAD_SIZE] = back_rows(
            upstream, pre, gain[...].astype(jnp.float32)
        ).astype(jnp.bfloat16)

    def deltas(seq, head):
        sums_of = []
        for member in range(group):
            column = (head * group + member) * HEAD_SIZE
            attended = jnp.concatenate(
                [
                    heads[row : row + toks, column : column + HEAD_SIZE]
                    for row in ((blk * seqs + seq) * toks for blk in range(links.n_blk))
                ],
                axis=0,
            )
            upstream = grad_rows[seq, head, member * q_len : (member + 1) * q_len, :]
            sums_of.append(attended.astype(jnp.float32) * upstream.astype(jnp.float32))
        terms = jnp.concatenate(sums_of, axis=0)
        high = terms.astype(jnp.bfloat16)
        rest = (terms - high.astype(jnp.float32)).astype(jnp.bfloat16)
        ones = jnp.ones((16, HEAD_SIZE), jnp.bfloat16)
        return (product_right(ones, high) + product_right(ones, rest))[:1, :]

    def back(seq, head):
        delta = deltas(seq, head)

        def over_keys(piece, grad_query):
            rows = pl.ds(pl.multiple_of(piece * q_len, q_len), q_len)
            scores = product_right(key_values[piece, 0, seq, head], queries[seq, head])
            prob = jnp.where(
                query_pos[...] >= key_pos[rows, :],
                jnp.exp(scores * SCORE_SCALE - lse[seq * kv_heads + head]),
                0.0,
            )
            grad_prob = product_right(key_values[piece, 1, seq, head], grad_rows[seq, head])
            grad_score = (prob * (grad_prob - delta)).astype(jnp.bfloat16)
            grad_kv[seq, piece, 0, head] = (
                SCORE_SCALE
                * jnp.dot(grad_score, queries[seq, head], preferred_element_type=jnp.float32)
            ).astype(jnp.bfloat16)
            grad_kv[seq, piece, 1, head] = jnp.dot(
                prob.astype(jnp.bfloat16),
                grad_rows[seq, head],
                preferred_element_type=jnp.float32,
            ).astype(jnp.bfloat16)
            return grad_query + transposed_product(key_values[piece, 0, seq, head], grad_score)

        grad_query = lax.fori_loop(
            0, links.n_uly, over_keys, jnp.zeros((HEAD_SIZE, q_rows), jnp.float32)
        )
        turned_back = (grad_query * SCORE_SCALE).T
        for member in range(group):
            column = (head * group + member) * HEAD_SIZE
            back_norm(
                turned_back[member * q_len : (member + 1) * q_len, :], seq, column, q_gain, 0
            )

    core, line = lax.rem(links.uly, 2), lax.div(links.uly, 2)

    def add(target, source):
        for kind in range(2):
            for head in range(kv_heads):
                target[kind, head] = target[kind, head] + source[kind, head]

    def core_sums(seq):
        return [
            links.to(
                grad_kv.at[seq, row * 2 + 1 - core], from_core.at[seq, row], links.core_way
            )
            for row in range(2)
        ]

    def across_sums(seq, copies):
        for row in range(2):
            copies[row].arrived()
            add(grad_kv.at[seq, row * 2 + core], from_core.at[seq, row])
        return links.to(
            grad_kv.at[seq, (1 - line) * 2 + core], from_across.at[seq], links.y_way
        )

    def own_keys(seq, copy):
        copy.arrived()
        rows = slice(seq * q_len, (seq + 1) * q_len)
        for head in range(kv_heads):
            term = [
                grad_kv[seq, links.uly, kind, head].astype(jnp.float32)
                + from_across[seq, kind, head].astype(jnp.float32)
                for kind in range(2)
            ]
            back_norm(term[0], seq, q_end + head * HEAD_SIZE, k_gain, 1)
            v_at = k_end + head * HEAD_SIZE
            grad_qkv[rows, v_at : v_at + HEAD_SIZE] = term[1].astype(jnp.bfloat16)

    def normed_parts(seq):
        for column in range(0, w_qkv.shape[0], 512):
            grad_parts[:, spans[seq], column : column + 512] = (
                product_right(
                    grad_qkv[seq * q_len : (seq + 1) * q_len, :],
                    w_qkv[column : column + 512, :],
                )
                .astype(jnp.bfloat16)
                .reshape(links.n_blk, toks, 512)
            )
        sums[seq].start()

    def dp_of(which):
        return links.dp if which == 1 else links.other_dp

    def compute_wo(which):
        dp = dp_of(which)
        weight_grad(rows_turned(heads, wo_1, dp), all_low, wo_1, dp)
        wo_sums.between_cores(which)

    def compute_qkv(plane, which, columns):
        weight_grad(
            turned_normed.at[which], grad_qkv.at[:, columns], plane.parts, dp_of(which)
        )
        plane.between_cores(which)

    q_columns, kv_columns = pl.ds(0, q_end), pl.ds(q_end, grad_qkv.shape[1] - q_end)
    heads_back(0)
    back(0, 0)
    output_half.sum.tick(1)
    for head in range(1, kv_heads):
        back(0, head)
    core_copies = core_sums(0)
    heads_back(1)
    down.second_way()
    for which in range(2):
        turned_normed[which] = rows_turned(normed, q_1, dp_of(which))
    back(1, 0)
    across = across_sums(0, core_copies)
    for tick in later:
        output_half.sum.tick(tick)
    for head in range(1, kv_heads):
        back(1, head)
    core_copies = core_sums(1)
    own_keys(0, across)
    across = across_sums(1, core_copies)
    normed_parts(0)
    compute_qkv(q_sums, 0, q_columns)
    compute_qkv(q_sums, 1, q_columns)
    own_keys(1, across)
    small_total[0] = gain_terms[...]
    pending = links.to(small_total.at[0], small_in.at[links.n_blk], links.core_way)
    q_sums.across_chips()
    normed_parts(1)
    sums[0].tick(1)
    compute_qkv(kv_sums, 0, kv_columns)
    compute_qkv(kv_sums, 1, kv_columns)
    for tick in later:
        sums[0].tick(tick)
    pending.arrived()
    small_total[1] = small_total[0] + small_in[links.n_blk]
    pending = links.to(small_total.at[1], small_in.at[links.n_blk + 1], links.x_way)
    kv_sums.across_chips()
    q_sums.second_way()
    compute_wo(0)
    compute_wo(1)
    pending.arrived()
    small_total[2] = small_total[1] + small_in[links.n_blk + 1]
    pending = links.to(small_total.at[2], small_in.at[links.n_blk + 2], links.y_way)
    sums[1].tick(1)
    kv_sums.second_way()
    wo_sums.across_chips()

    def into(target):
        def write(block, rows, values):
            target[block, rows, :] = values.astype(target.dtype)

        return write

    def give_home(plane, columns):
        here, there = summed.at[:, :, columns], grad_w_qkv.at[links.blk, :, columns]
        plane.result(into(here))
        keep.append(links.local(here.at[links.blk], there))
        return links.swap(lambda peer: [(here.at[peer], there)])

    swapped += give_home(q_sums, q_columns)
    for tick in later:
        sums[1].tick(tick)
    pending.arrived()
    small_in[links.blk] = small_total[2] + small_in[links.n_blk + 2]
    mine = small_in.at[links.blk]
    small_copies = [links.to(mine, mine, device) for device in links.peers()]
    swapped += give_home(kv_sums, kv_columns)
    output_half.write(output)

    def settle(seq):
        sums[seq].finish(grad_hidden.at[spans[seq]])

        def body(rows):
            at = pl.ds(pl.multiple_of(spans[seq].start + rows.start, ROWS), ROWS)
            back = back_rows(grad_hidden[at, :], hidden[at, :].astype(jnp.float32), gain[...])
            grad_hidden[at, :] = grad_middle[at, :] + back

        each_block(toks, body)

    settle(0)
    wo_sums.second_way()
    down.result(into(grad_down))
    settle(1)
    wo_sums.result(into(grad_wo))
    for copy in small_copies:
        copy.arrived()
    total = small_in[0]
    for blk in range(1, links.n_blk):
        total = total + small_in[blk]
    small_sum[...] = total
    for copy in swapped:
        copy.arrived()
    for copy in keep:
        copy.wait()
    for half in sums:
        half.sent()
    output_half.sum.sent()
    links.finish()


def backward(
    all_low,
    wo,
    queries,
    key_values,
    lse,
    qkv,
    q_gain,
    k_gain,
    cosine,
    sine,
    query_pos,
    key_pos,
    w_qkv,
    hidden,
    grad_middle,
    gain,
    normed,
    heads,
    out_parts,
    middle,
    grad_gate,
    grad_up,
    part_down,
):
    seqs, kv_heads, q_rows, _ = queries.shape
    n_uly, _, _, _, q_len, _ = key_values.shape
    n_blk, tokens, width = out_parts.shape
    n_dp, _, _, down_depth, _ = part_down.shape
    columns = qkv.shape[1]
    depth = width // (n_dp * n_blk * n_uly)
    out_depth = heads.shape[1] // (n_dp * n_uly)
    f32, low = jnp.float32, jnp.bfloat16
    small = (8, HEAD_SIZE)
    outs = [
        ((tokens, width), f32),
        ((1, out_depth, width), f32),
        ((1, down_depth, width), f32),
        (small, f32),
        ((tokens // 2, width), low),
        (grad_gate.shape, low),
        (grad_up.shape, low),
        ((n_blk, depth, columns), low),
    ]
    scratch = [
        (qkv.shape, low),
        (small, f32),
        ((q_len, heads.shape[1]), f32),
        (queries.shape, low),
        ((seqs, n_uly, 2, kv_heads, q_len, HEAD_SIZE), low),
        ((seqs, 2, 2, kv_heads, q_len, HEAD_SIZE), low),
        ((seqs, 2, kv_heads, q_len, HEAD_SIZE), low),
        (out_parts.shape, low),
        ((n_blk - 1, tokens, width), low),
        ((n_blk - 1, tokens, width), low),
        ((n_blk, depth, columns), low),
        ((n_blk + 3,) + small, f32),
        ((3,) + small, f32),
    ]
    down = [part_down.shape] + plane_shapes(n_dp, 1, n_uly, down_depth, width)[2:]
    return pl.pallas_call(
        backward_kernel,
        out_shape=[jax.ShapeDtypeStruct(shape, kind) for shape, kind in outs],
        in_specs=[VMEM] * 20 + [HBM] * 3,
        out_specs=[VMEM] * 5 + [HBM] * 3,
        scratch_shapes=[pltpu.VMEM(shape, kind) for shape, kind in scratch]
        + output_scratch(n_blk, tokens, width)
        + [pltpu.VMEM(shape, low) for shape in down]
        + [pltpu.VMEM((n_dp, width // n_dp, normed.shape[0]), low)]
        + plane_scratch(n_dp, n_blk, n_uly, depth, heads.shape[1])
        + plane_scratch(n_dp, n_blk, n_uly, depth, columns - heads.shape[1])
        + plane_scratch(n_dp, 1, n_uly, out_depth, width)
        + semaphores(112),
        compiler_params=kernel_params(4),
    )(
        all_low,
        wo,
        queries,
        key_values,
        lse,
        qkv,
        q_gain,
        k_gain,
        cosine,
        sine,
        query_pos,
        key_pos,
        w_qkv,
        hidden,
        grad_middle,
        gain,
        normed,
        heads,
        out_parts,
        middle,
        grad_gate,
        grad_up,
        part_down,
    )


def finish_kernel(
    gate,
    up,
    qkv,
    wo,
    wd,
    hidden,
    out_0,
    out_1,
    w_gate,
    w_up,
    w_query,
    key_weight,
    value_weight,
    attn_gain,
    mlp_gain,
    small,
    f_gate,
    f_up,
    f_q,
    f_k,
    f_v,
    f_wo,
    f_wd,
    f_hidden,
    f_out,
    f_attn,
    f_mlp,
    f_q_gain,
    f_k_gain,
):
    n_blk, depth, _ = gate.shape

    def place(source, offset, target):
        width = target.shape[1] // (n_blk * 2)
        for blk in range(n_blk):
            for group in range(2):
                to = (group * n_blk + blk) * width
                at = offset + group * width
                target[:, to : to + width] = source[blk, :, at : at + width].astype(jnp.float32)

    def gain_back(pairs, gain):
        total = jnp.zeros((depth, 128), jnp.float32)
        for weight, grad in pairs:
            for column in range(0, weight.shape[1], 128):
                at = slice(column, column + 128)
                total = total + weight[:, at].astype(jnp.float32) * grad[:, at]
        column = jnp.sum(total, axis=1, keepdims=True)
        square = (depth, depth)
        same = lax.broadcasted_iota(jnp.int32, square, 0) == lax.broadcasted_iota(
            jnp.int32, square, 1
        )
        return jnp.sum(jnp.where(same, column, 0.0), axis=0, keepdims=True) / gain[
            ...
        ].astype(jnp.float32)

    place(gate, 0, f_gate)
    place(up, 0, f_up)
    q_width = f_q.shape[1] // n_blk
    k_width = f_k.shape[1] // n_blk
    place(qkv, 0, f_q)
    place(qkv, q_width, f_k)
    place(qkv, q_width + k_width, f_v)
    f_q_gain[...] = small[0:1, :]
    f_k_gain[...] = small[1:2, :]
    f_wo[...] = wo[0]
    f_wd[...] = wd[0]
    f_hidden[...] = hidden[...]
    half = out_0.shape[0]
    f_out[:half, :] = out_0[...]
    f_out[half:, :] = out_1[...]
    f_attn[...] = gain_back(((w_query, f_q), (key_weight, f_k), (value_weight, f_v)), attn_gain)
    f_mlp[...] = gain_back(((w_gate, f_gate), (w_up, f_up)), mlp_gain)


def finish(gate, up, qkv, wo, wd, hidden, out_0, out_1, weights, gains, small):
    return pl.pallas_call(
        finish_kernel,
        out_shape=[jax.ShapeDtypeStruct(w.shape, jnp.float32) for w in weights]
        + [
            jax.ShapeDtypeStruct(wo.shape[1:], jnp.float32),
            jax.ShapeDtypeStruct(wd.shape[1:], jnp.float32),
            jax.ShapeDtypeStruct(hidden.shape, jnp.float32),
            jax.ShapeDtypeStruct(hidden.shape, jnp.bfloat16),
        ]
        + [jax.ShapeDtypeStruct(gain.shape, jnp.float32) for gain in gains]
        + [jax.ShapeDtypeStruct((1, small.shape[1]), jnp.float32)] * 2,
        in_specs=[VMEM] * 16,
        out_specs=[VMEM] * 13,
        compiler_params=pltpu.CompilerParams(vmem_limit_bytes=62 * MIB),
    )(gate, up, qkv, wo, wd, hidden, out_0, out_1, *weights, *gains, small)


def product(left, right):
    return jnp.dot(left, right, preferred_element_type=jnp.float32)


def shards(
    hidden,
    span_order,
    attn_gain,
    w_query,
    key_weight,
    value_weight,
    w_out,
    q_gain,
    k_gain,
    mlp_gain,
    w_gate,
    w_up,
    w_down,
    cotangent,
):
    seqs, toks, width = hidden.shape
    n_dp, n_blk, n_uly = (lax.axis_size(a) for a in EVERY)
    rows = n_blk * seqs * toks
    bf16 = jnp.bfloat16
    own_hidden = hidden.reshape(seqs * toks, width)
    own_cotangent = cotangent.reshape(seqs * toks, width)

    gain_q, gain_k = q_gain[None, :], k_gain[None, :]
    gain_rows = attn_gain.shape[0]
    own_gains = jnp.pad(jnp.stack([attn_gain, mlp_gain]), ((0, 30), (0, 128 - gain_rows)))
    (
        w_qkv,
        wo,
        all_wg,
        all_wu,
        all_wd,
        cot,
        g_attn,
        g_mlp,
        cosine,
        sine,
        query_pos,
        key_pos,
        heads_flat,
        normed,
        qkv,
        queries,
        key_values,
        lse,
        middle,
        normed2,
    ) = forward(
        span_order,
        own_hidden,
        w_query,
        key_weight,
        value_weight,
        w_out,
        w_gate,
        w_up,
        w_down,
        own_cotangent,
        own_gains,
        gain_q,
        gain_k,
        seqs,
        gain_rows,
    )
    w_qkv = w_qkv.reshape(width, -1)
    wo = wo.reshape(-1, width)
    wg, wu = all_wg.reshape(width, -1), all_wu.reshape(width, -1)
    wd = all_wd.reshape(-1, width)
    cot = cot.reshape(rows, width)
    normed2 = normed2.reshape(rows, width)
    gate_pre = product(normed2, wg)
    up_pre = product(normed2, wu)
    sigmoid_gate = jax.nn.sigmoid(gate_pre)
    activated = (gate_pre * sigmoid_gate * up_pre).astype(bf16)
    out_parts = product(activated, wd).astype(bf16)
    grad_act = product_right(cot, wd)
    grad_gate_pre = (
        grad_act * up_pre * sigmoid_gate * (1.0 + gate_pre * (1.0 - sigmoid_gate))
    ).astype(bf16)
    grad_up_pre = (grad_act * gate_pre * sigmoid_gate).astype(bf16)
    grad_parts = (product_right(grad_gate_pre, wg) + product_right(grad_up_pre, wu)).astype(bf16)
    blocks = (n_blk, seqs * toks, width)
    out_parts = out_parts.reshape(blocks)
    output_0, grad_middle, middle_low, grad_gate, grad_up, part_down = exchange_back(
        grad_parts.reshape(blocks),
        out_parts,
        middle,
        own_cotangent,
        g_mlp,
        normed2,
        grad_gate_pre,
        grad_up_pre,
        activated,
        cot,
    )
    middle_low = middle_low.reshape(rows, width)
    (
        grad_hidden,
        grad_out,
        grad_down,
        small,
        output_1,
        grad_gate,
        grad_up,
        grad_w_qkv,
    ) = backward(
        middle_low,
        wo,
        queries,
        key_values,
        lse,
        qkv,
        gain_q,
        gain_k,
        cosine,
        sine,
        query_pos,
        key_pos,
        w_qkv,
        own_hidden,
        grad_middle,
        g_attn,
        normed,
        heads_flat,
        out_parts,
        middle,
        grad_gate,
        grad_up,
        part_down,
    )
    (
        grad_gate,
        grad_up,
        grad_query,
        grad_key,
        grad_value,
        grad_out,
        grad_down,
        grad_hidden,
        output,
        grad_attn_gain,
        grad_mlp_gain,
        grad_q_gain,
        grad_k_gain,
    ) = finish(
        grad_gate,
        grad_up,
        grad_w_qkv,
        grad_out,
        grad_down,
        grad_hidden,
        output_0,
        output_1,
        (w_gate, w_up, w_query, key_weight, value_weight),
        [g[None, :] for g in (attn_gain, mlp_gain)],
        small,
    )
    return (
        output.reshape(hidden.shape),
        grad_hidden.reshape(hidden.shape),
        grad_attn_gain.reshape(gain_rows),
        grad_query,
        grad_key,
        grad_value,
        grad_out,
        grad_q_gain[0],
        grad_k_gain[0],
        grad_mlp_gain.reshape(gain_rows),
        grad_gate,
        grad_up,
        grad_down,
    )


def solution(mesh):
    n_dp, n_blk, n_uly = (mesh.shape[a] for a in EVERY)
    aligned = (n_dp, n_uly) == (2, 4) and KEY_VALUE_HEADS % (n_dp * n_blk) == 0
    in_specs = (
        TOKENS,
        P(),
        P(EVERY),
        P(EVERY, None),
        P(EVERY, None),
        P(EVERY, None),
        P(EVERY, None),
        P(),
        P(),
        P(EVERY),
        P(EVERY, None),
        P(EVERY, None),
        P(EVERY, None),
        TOKENS,
    )
    out_specs = (
        TOKENS,
        TOKENS,
        P(EVERY),
        P(EVERY, None),
        P(EVERY, None),
        P(EVERY, None),
        P(EVERY, None),
        P(),
        P(),
        P(EVERY),
        P(EVERY, None),
        P(EVERY, None),
        P(EVERY, None),
    )
    return jax.shard_map(
        shards if aligned else shards_general,
        mesh=mesh, in_specs=in_specs, out_specs=out_specs, check_vma=False)
```

```python
import functools
import math

import jax
import jax.numpy as jnp
from jax import lax
from jax.experimental import pallas as pl
from jax.experimental.pallas import tpu as pltpu
from jax.sharding import PartitionSpec as P

QUERY_HEADS = 16
KEY_VALUE_HEADS = 8
HEAD_SIZE = 128


DP, BLK, ULY = "dp", "blk", "uly"
EVERY = (DP, BLK, ULY)
PLANE = (DP, ULY)
TOKENS = P(DP, (BLK, ULY), None)
EQ_KGQD_NKD_TO_KGQN = "kgqd,nkd->kgqn"
EQ_KGQN_KGQD_TO_NKD = "kgqn,kgqd->nkd"
EQ_KGQN_NKD_TO_KGQD = "kgqn,nkd->kgqd"
EQ_KGQN_QKGD_TO_NKD = "kgqn,qkgd->nkd"
EQ_QKGD_NKD_TO_KGQN = "qkgd,nkd->kgqn"
EQ_STD_DE_TO_STE = "std,de->ste"
EQ_STD_DF_TO_STF = "std,df->stf"
EQ_STD_ED_TO_STE = "std,ed->ste"
EQ_STD_FD_TO_STF = "std,fd->stf"
EQ_STD_STE_TO_DE = "std,ste->de"
EQ_STD_STF_TO_DF = "std,stf->df"
EQ_STE_DE_TO_STD = "ste,de->std"
EQ_STE_ED_TO_STD = "ste,ed->std"
EQ_STE_STD_TO_ED = "ste,std->ed"
EQ_STF_DF_TO_STD = "stf,df->std"
EQ_STF_FD_TO_STD = "stf,fd->std"
EQ_STF_STD_TO_FD = "stf,std->fd"

EPSILON = 1e-06
ROPE_BASE = 1000000.0


def rms_scale(source):
    return lax.rsqrt(jnp.mean(source * source, axis=-1, keepdims=True) + EPSILON)


def norm_back(grad_normed, source, norm_scale, gain):
    unit_rows = source * norm_scale
    scaled = grad_normed * gain
    return norm_scale * (scaled - unit_rows * jnp.mean(scaled * unit_rows, axis=-1, keepdims=True))


def angles_of(positions, head_dim):
    freq_steps = jnp.arange(head_dim // 2, dtype=jnp.float32)
    inverse = jnp.exp(freq_steps * (-2.0 * math.log(ROPE_BASE) / head_dim))
    return positions.astype(jnp.float32)[:, None] * inverse[None, :]


def rotate(source, angles, direction):
    half_dim = source.shape[-1] // 2
    cosine = jnp.cos(angles)[:, None, :]
    sine_part = direction * jnp.sin(angles)[:, None, :]
    first_half = source[..., :half_dim]
    second_half = source[..., half_dim:]
    return jnp.concatenate(
        [
            first_half * cosine - second_half * sine_part,
            second_half * cosine + first_half * sine_part,
        ],
        axis=-1,
    )


def positions_of(places, span_order, half_len):
    blocks_of = places // half_len
    block_ids = jnp.arange(span_order.shape[0], dtype=jnp.int32)
    chosen = jnp.sum(
        jnp.where(blocks_of[:, None] == block_ids[None, :], span_order[None, :], 0), axis=1
    )
    return chosen * half_len + places % half_len


def add_rows(buffer, new_rows):
    return buffer + new_rows


def shards_general(
    hidden,
    span_order,
    attn_gain,
    w_query,
    key_weight,
    value_weight,
    w_out,
    q_gain,
    k_gain,
    mlp_gain,
    w_gate,
    w_up,
    w_down,
    cotangent,
):
    sequence_count = hidden.shape[0]
    token_count = hidden.shape[1]
    ulysses_group_size = lax.axis_size(ULY)
    local_q = QUERY_HEADS // ulysses_group_size
    local_key_value = KEY_VALUE_HEADS // ulysses_group_size
    query_group_width = QUERY_HEADS // KEY_VALUE_HEADS
    block_len = token_count * ulysses_group_size
    half_len = block_len // 2
    score_scale = 1.0 / math.sqrt(HEAD_SIZE)
    blk_index = lax.axis_index(BLK)
    uly_index = lax.axis_index(ULY)
    first_place = (blk_index * ulysses_group_size + uly_index) * token_count
    local_angles = angles_of(
        positions_of(first_place + jnp.arange(token_count, dtype=jnp.int32), span_order, half_len),
        HEAD_SIZE,
    )
    query_pos = positions_of(
        blk_index * block_len + jnp.arange(block_len, dtype=jnp.int32), span_order, half_len
    )
    g_attn, wq_all, wk_all, wv_all, wo_all = (
        lax.all_gather(attn_gain, EVERY, axis=0, tiled=True),
        lax.all_gather(w_query, EVERY, axis=0, tiled=True),
        lax.all_gather(key_weight, EVERY, axis=0, tiled=True),
        lax.all_gather(value_weight, EVERY, axis=0, tiled=True),
        lax.all_gather(w_out, EVERY, axis=0, tiled=True),
    )
    source = hidden.astype(jnp.float32)
    first_scale = rms_scale(source)
    normalized_input = (source * first_scale * g_attn.astype(jnp.float32)).astype(jnp.bfloat16)
    q_pre = jnp.einsum(
        EQ_STD_DE_TO_STE, normalized_input, wq_all, preferred_element_type=jnp.float32
    ).reshape(sequence_count, token_count, QUERY_HEADS, HEAD_SIZE)
    key_before_norm = jnp.einsum(
        EQ_STD_DE_TO_STE, normalized_input, wk_all, preferred_element_type=jnp.float32
    ).reshape(sequence_count, token_count, KEY_VALUE_HEADS, HEAD_SIZE)
    value_before_norm = jnp.einsum(
        EQ_STD_DE_TO_STE, normalized_input, wv_all, preferred_element_type=jnp.float32
    ).reshape(sequence_count, token_count, KEY_VALUE_HEADS, HEAD_SIZE)
    q_scale = rms_scale(q_pre)
    k_scale = rms_scale(key_before_norm)
    gain_q = q_gain.astype(jnp.float32)
    gain_k = k_gain.astype(jnp.float32)
    q_rot = rotate(q_pre * q_scale * gain_q, local_angles, 1.0).astype(jnp.bfloat16)
    k_rot = rotate(key_before_norm * k_scale * gain_k, local_angles, 1.0).astype(jnp.bfloat16)
    v_low = value_before_norm.astype(jnp.bfloat16)
    q_heads, k_heads, v_heads = (
        lax.all_to_all(q_rot, ULY, split_axis=2, concat_axis=1, tiled=True),
        lax.all_to_all(k_rot, ULY, split_axis=2, concat_axis=1, tiled=True),
        lax.all_to_all(v_low, ULY, split_axis=2, concat_axis=1, tiled=True),
    )
    q_group = q_heads.reshape(
        sequence_count, block_len, local_key_value, query_group_width, HEAD_SIZE
    )
    stat_shape = (sequence_count, local_key_value, query_group_width, block_len)
    start_state = (
        jnp.full(stat_shape, -1e30, jnp.float32),
        jnp.zeros(stat_shape, jnp.float32),
        jnp.zeros(stat_shape + (HEAD_SIZE,), jnp.float32),
    )
    key_piece = lax.all_gather(k_heads, BLK, axis=1, tiled=True)
    value_piece = lax.all_gather(v_heads, BLK, axis=1, tiled=True)
    key_pos = positions_of(jnp.arange(key_piece.shape[1], dtype=jnp.int32), span_order, half_len)
    allowed = query_pos[:, None] >= key_pos[None, :]

    def attend_one_sequence(members):
        query_rows, key_rows, value_rows, top_seq, total_seq, accum_seq = members
        scores = (
            jnp.einsum(EQ_QKGD_NKD_TO_KGQN, query_rows, key_rows, preferred_element_type=jnp.float32)
            * score_scale
        )
        scores = jnp.where(allowed, scores, -jnp.inf)
        new_top = jnp.maximum(top_seq, jnp.max(scores, axis=-1))
        fading = jnp.exp(top_seq - new_top)
        weights = jnp.exp(scores - new_top[..., None])
        total_seq = total_seq * fading + jnp.sum(weights, axis=-1)
        accum_seq = accum_seq * fading[..., None] + jnp.einsum(
            EQ_KGQN_NKD_TO_KGQD,
            weights.astype(jnp.bfloat16),
            value_rows,
            preferred_element_type=jnp.float32,
        )
        return (new_top, total_seq, accum_seq)

    row_top, row_total, accum = lax.map(
        attend_one_sequence,
        (q_group, key_piece, value_piece, start_state[0], start_state[1], start_state[2]),
    )
    log_total = row_top + jnp.log(row_total)
    attention_output = jnp.transpose(accum / row_total[..., None], (0, 3, 1, 2, 4)).reshape(
        sequence_count, block_len, local_q, HEAD_SIZE
    )
    heads_seq = lax.all_to_all(
        attention_output.astype(jnp.bfloat16), ULY, split_axis=1, concat_axis=2, tiled=True
    )
    heads_flat = heads_seq.reshape(sequence_count, token_count, QUERY_HEADS * HEAD_SIZE)
    middle = source + jnp.einsum(
        EQ_STE_ED_TO_STD, heads_flat, wo_all, preferred_element_type=jnp.float32
    )
    g_mlp, wg_all, wu_all, wd_all = (
        lax.all_gather(mlp_gain, EVERY, axis=0, tiled=True),
        lax.all_gather(w_gate, EVERY, axis=0, tiled=True),
        lax.all_gather(w_up, EVERY, axis=0, tiled=True),
        lax.all_gather(w_down, EVERY, axis=0, tiled=True),
    )
    second_scale = rms_scale(middle)
    gain_mlp = g_mlp.astype(jnp.float32)
    normed2 = (middle * second_scale * gain_mlp).astype(jnp.bfloat16)
    gate_pre = jnp.einsum(EQ_STD_DF_TO_STF, normed2, wg_all, preferred_element_type=jnp.float32)
    up_pre = jnp.einsum(EQ_STD_DF_TO_STF, normed2, wu_all, preferred_element_type=jnp.float32)
    sigmoid_gate = jax.nn.sigmoid(gate_pre)
    activated = (gate_pre * sigmoid_gate * up_pre).astype(jnp.bfloat16)
    result = middle + jnp.einsum(
        EQ_STF_FD_TO_STD, activated, wd_all, preferred_element_type=jnp.float32
    )
    output = result.astype(jnp.bfloat16)
    g_mlp, wg_all, wu_all, wd_all = (
        lax.all_gather(mlp_gain, EVERY, axis=0, tiled=True),
        lax.all_gather(w_gate, EVERY, axis=0, tiled=True),
        lax.all_gather(w_up, EVERY, axis=0, tiled=True),
        lax.all_gather(w_down, EVERY, axis=0, tiled=True),
    )
    gain_mlp = g_mlp.astype(jnp.float32)
    grad_act = jnp.einsum(EQ_STD_FD_TO_STF, cotangent, wd_all, preferred_element_type=jnp.float32)
    grad_gate_pre = (
        grad_act * up_pre * sigmoid_gate * (1.0 + gate_pre * (1.0 - sigmoid_gate))
    ).astype(jnp.bfloat16)
    grad_up_pre = (grad_act * gate_pre * sigmoid_gate).astype(jnp.bfloat16)
    grad_gate = jnp.einsum(
        EQ_STD_STF_TO_DF, normed2, grad_gate_pre, preferred_element_type=jnp.float32
    )
    grad_up = jnp.einsum(EQ_STD_STF_TO_DF, normed2, grad_up_pre, preferred_element_type=jnp.float32)
    grad_normed2 = jnp.einsum(
        EQ_STF_DF_TO_STD, grad_gate_pre, wg_all, preferred_element_type=jnp.float32
    ) + jnp.einsum(EQ_STF_DF_TO_STD, grad_up_pre, wu_all, preferred_element_type=jnp.float32)
    mlp_gain_term = jnp.sum(grad_normed2 * middle * second_scale, axis=(0, 1))
    grad_middle = cotangent.astype(jnp.float32) + norm_back(
        grad_normed2, middle, second_scale, gain_mlp
    )
    grad_mlp_gain, grad_gate, grad_up = (
        lax.psum_scatter(mlp_gain_term, EVERY, scatter_dimension=0, tiled=True),
        lax.psum_scatter(grad_gate, EVERY, scatter_dimension=0, tiled=True),
        lax.psum_scatter(grad_up, EVERY, scatter_dimension=0, tiled=True),
    )
    g_attn, wq_all, wk_all, wv_all, wo_all = (
        lax.all_gather(attn_gain, EVERY, axis=0, tiled=True),
        lax.all_gather(w_query, EVERY, axis=0, tiled=True),
        lax.all_gather(key_weight, EVERY, axis=0, tiled=True),
        lax.all_gather(value_weight, EVERY, axis=0, tiled=True),
        lax.all_gather(w_out, EVERY, axis=0, tiled=True),
    )
    middle_low = grad_middle.astype(jnp.bfloat16)
    grad_out = jnp.einsum(EQ_STE_STD_TO_ED, heads_flat, middle_low, preferred_element_type=jnp.float32)
    grad_heads = (
        jnp.einsum(EQ_STD_ED_TO_STE, middle_low, wo_all, preferred_element_type=jnp.float32)
        .astype(jnp.bfloat16)
        .reshape(sequence_count, token_count, QUERY_HEADS, HEAD_SIZE)
    )
    grad_heads_local = lax.all_to_all(grad_heads, ULY, split_axis=2, concat_axis=1, tiled=True)
    grad_group = jnp.transpose(
        grad_heads_local.reshape(
            sequence_count, block_len, local_key_value, query_group_width, HEAD_SIZE
        ),
        (0, 2, 3, 1, 4),
    )
    delta = jnp.sum(grad_heads_local.astype(jnp.float32) * attention_output, axis=-1)
    delta = jnp.transpose(
        delta.reshape(sequence_count, block_len, local_key_value, query_group_width), (0, 2, 3, 1)
    )
    seq_length = block_len * lax.axis_size(BLK)
    zero_keys = jnp.zeros((sequence_count, seq_length, local_key_value, HEAD_SIZE), jnp.float32)
    back_state = (jnp.zeros(stat_shape + (HEAD_SIZE,), jnp.float32), zero_keys, zero_keys)
    key_piece = lax.all_gather(k_heads, BLK, axis=1, tiled=True)
    value_piece = lax.all_gather(v_heads, BLK, axis=1, tiled=True)
    key_pos = positions_of(jnp.arange(key_piece.shape[1], dtype=jnp.int32), span_order, half_len)
    back_allowed = query_pos[:, None] >= key_pos[None, :]

    def back_one_sequence(members):
        query_rows, grad_rows, lse_seq, delta_seq, key_rows, value_rows, dq_seq, dk_seq, dv_seq = (
            members
        )
        scores = (
            jnp.einsum(EQ_QKGD_NKD_TO_KGQN, query_rows, key_rows, preferred_element_type=jnp.float32)
            * score_scale
        )
        scores = jnp.where(back_allowed, scores, -jnp.inf)
        probs = jnp.exp(scores - lse_seq[..., None])
        grad_values = jnp.einsum(
            EQ_KGQN_KGQD_TO_NKD,
            probs.astype(jnp.bfloat16),
            grad_rows,
            preferred_element_type=jnp.float32,
        )
        grad_probs = jnp.einsum(
            EQ_KGQD_NKD_TO_KGQN, grad_rows, value_rows, preferred_element_type=jnp.float32
        )
        grad_scores = (probs * (grad_probs - delta_seq[..., None])).astype(jnp.bfloat16)
        dq_seq = dq_seq + score_scale * jnp.einsum(
            EQ_KGQN_NKD_TO_KGQD, grad_scores, key_rows, preferred_element_type=jnp.float32
        )
        grad_keys = score_scale * jnp.einsum(
            EQ_KGQN_QKGD_TO_NKD, grad_scores, query_rows, preferred_element_type=jnp.float32
        )
        return (dq_seq, add_rows(dk_seq, grad_keys), add_rows(dv_seq, grad_values))

    grad_q_group, grad_k_whole, grad_v_whole = lax.map(
        back_one_sequence,
        (
            q_group,
            grad_group,
            log_total,
            delta,
            key_piece,
            value_piece,
            back_state[0],
            back_state[1],
            back_state[2],
        ),
    )
    grad_k_block, grad_v_block = (
        lax.psum_scatter(
            grad_k_whole.astype(jnp.bfloat16), BLK, scatter_dimension=1, tiled=True
        ).astype(jnp.float32),
        lax.psum_scatter(
            grad_v_whole.astype(jnp.bfloat16), BLK, scatter_dimension=1, tiled=True
        ).astype(jnp.float32),
    )
    grad_q_block = jnp.transpose(grad_q_group, (0, 3, 1, 2, 4)).reshape(
        sequence_count, block_len, local_q, HEAD_SIZE
    )
    grad_q_seq, grad_k_seq, value_sequence_gradient = (
        lax.all_to_all(
            grad_q_block.astype(jnp.bfloat16), ULY, split_axis=1, concat_axis=2, tiled=True
        ).astype(grad_q_block.dtype),
        lax.all_to_all(
            grad_k_block.astype(jnp.bfloat16), ULY, split_axis=1, concat_axis=2, tiled=True
        ).astype(grad_k_block.dtype),
        lax.all_to_all(
            grad_v_block.astype(jnp.bfloat16), ULY, split_axis=1, concat_axis=2, tiled=True
        ).astype(grad_v_block.dtype),
    )
    grad_q_normed = rotate(grad_q_seq, local_angles, -1.0)
    grad_k_normed = rotate(grad_k_seq, local_angles, -1.0)
    q_gain_term = jnp.sum(grad_q_normed * q_pre * q_scale, axis=(0, 1, 2))
    k_gain_term = jnp.sum(grad_k_normed * key_before_norm * k_scale, axis=(0, 1, 2))
    grad_q_pre = (
        norm_back(grad_q_normed, q_pre, q_scale, gain_q)
        .astype(jnp.bfloat16)
        .reshape(sequence_count, token_count, QUERY_HEADS * HEAD_SIZE)
    )
    grad_k_pre = (
        norm_back(grad_k_normed, key_before_norm, k_scale, gain_k)
        .astype(jnp.bfloat16)
        .reshape(sequence_count, token_count, KEY_VALUE_HEADS * HEAD_SIZE)
    )
    value_pre_gradient = value_sequence_gradient.astype(jnp.bfloat16).reshape(
        sequence_count, token_count, KEY_VALUE_HEADS * HEAD_SIZE
    )
    grad_query = jnp.einsum(
        EQ_STD_STE_TO_DE, normalized_input, grad_q_pre, preferred_element_type=jnp.float32
    )
    grad_key = jnp.einsum(
        EQ_STD_STE_TO_DE, normalized_input, grad_k_pre, preferred_element_type=jnp.float32
    )
    grad_value = jnp.einsum(
        EQ_STD_STE_TO_DE, normalized_input, value_pre_gradient, preferred_element_type=jnp.float32
    )
    grad_normed = jnp.einsum(EQ_STE_DE_TO_STD, grad_q_pre, wq_all, preferred_element_type=jnp.float32)
    grad_normed = grad_normed + jnp.einsum(
        EQ_STE_DE_TO_STD, grad_k_pre, wk_all, preferred_element_type=jnp.float32
    )
    grad_normed = grad_normed + jnp.einsum(
        EQ_STE_DE_TO_STD, value_pre_gradient, wv_all, preferred_element_type=jnp.float32
    )
    attn_gain_term = jnp.sum(grad_normed * source * first_scale, axis=(0, 1))
    grad_hidden = grad_middle + norm_back(
        grad_normed, source, first_scale, g_attn.astype(jnp.float32)
    )
    grad_down = jnp.einsum(EQ_STF_STD_TO_FD, activated, cotangent, preferred_element_type=jnp.float32)
    grad_attn_gain, grad_query, grad_key, grad_value, grad_out, grad_down = (
        lax.psum_scatter(attn_gain_term, EVERY, scatter_dimension=0, tiled=True),
        lax.psum_scatter(grad_query, EVERY, scatter_dimension=0, tiled=True),
        lax.psum_scatter(grad_key, EVERY, scatter_dimension=0, tiled=True),
        lax.psum_scatter(grad_value, EVERY, scatter_dimension=0, tiled=True),
        lax.psum_scatter(grad_out, EVERY, scatter_dimension=0, tiled=True),
        lax.psum_scatter(grad_down, EVERY, scatter_dimension=0, tiled=True),
    )
    grad_q_gain, grad_k_gain = lax.psum((q_gain_term, k_gain_term), EVERY)
    return (
        output,
        grad_hidden,
        grad_attn_gain,
        grad_query,
        grad_key,
        grad_value,
        grad_out,
        grad_q_gain,
        grad_k_gain,
        grad_mlp_gain,
        grad_gate,
        grad_up,
        grad_down,
    )


MESH = pl.DeviceIdType.MESH
HBM = pl.BlockSpec(memory_space=pltpu.HBM)
VMEM = pl.BlockSpec(memory_space=pltpu.VMEM)
MIB = 1 << 20


def kernel_params(collective_id, vmem_mib=62):
    return pltpu.CompilerParams(
        collective_id=collective_id, has_side_effects=True, vmem_limit_bytes=vmem_mib * MIB
    )


def semaphores(count, local=16):
    return [
        pltpu.SemaphoreType.DMA((count,)),
        pltpu.SemaphoreType.DMA((count,)),
        pltpu.SemaphoreType.DMA((local,)),
    ]


class Copy:
    def __init__(self, descriptor, sends, receives):
        self.descriptor, self.sends, self.receives = descriptor, sends, receives

    def under(self, condition, action):
        if condition is None:
            action()
        else:
            pl.when(condition)(action)

    def start(self):
        self.under(self.sends, lambda: self.descriptor().start())
        return self

    def sent(self):
        self.under(self.sends, lambda: self.descriptor().wait_send())

    def arrived(self):
        self.under(self.receives, lambda: self.descriptor().wait_recv())


class Links:
    def __init__(self, send, recv, here):
        self.send, self.recv, self.here = send, recv, here
        self.used, self.used_here = 0, 0
        self.copies, self.local_copies = [], []
        self.n_dp, self.n_blk, self.n_uly = (lax.axis_size(a) for a in EVERY)
        self.dp, self.blk, self.uly = (lax.axis_index(a) for a in EVERY)
        self.other_dp = 1 - self.dp
        self.across = lax.rem(self.uly + 2, 4)
        self.twin = self.uly + 1 - 2 * lax.rem(self.uly, 2)
        self.x_way = (self.other_dp, self.blk, self.uly)
        self.y_way = (self.dp, self.blk, self.across)
        self.core_way = (self.dp, self.blk, self.twin)

    def peer(self, step):
        return lax.rem(self.blk + step, self.n_blk)

    def peers(self):
        return [(self.dp, self.peer(k), self.uly) for k in range(1, self.n_blk)]

    def far_first(self):
        last = self.n_blk - 1
        orders = [
            sorted((p for p in range(self.n_blk) if p != b), key=lambda p, b=b: -abs(p - b))
            for b in range(self.n_blk)
        ]
        for b, order in enumerate(orders):
            ways = [[p for p in order if p > b], [p for p in order if p < b]]
            ways.sort(key=lambda way: -len(way))
            merged = []
            while ways[0] or ways[1]:
                for way in ways:
                    if way:
                        merged.append(way.pop(0))
            orders[b] = merged
        peers = []
        for turn in range(last):
            peer = jnp.int32(0)
            for b, order in enumerate(orders):
                peer = jnp.where(self.blk == b, order[turn], peer)
            peers.append(peer)
        return peers

    def swap(self, pieces_for):
        base, count = self.used, 0
        for peer in self.far_first():
            pieces = pieces_for(peer)
            count = len(pieces)
            distance = lax.rem(peer - self.blk + self.n_blk, self.n_blk) - 1
            for number, (source, target) in enumerate(pieces):
                self.swap_copy(base + distance * count + number, source, target, peer).start()
        self.used = base + (self.n_blk - 1) * count
        waits = []
        for slot in range(base, self.used):
            source, target = pieces_for(self.blk)[(slot - base) % count]

            def descriptor(slot=slot, source=source, target=target):
                return self.swap_copy(slot, source, target, self.peer(1))

            copy = Copy(descriptor, None, None)
            self.copies.append(copy)
            waits.append(copy)
        return waits

    def swap_copy(self, slot, source, target, peer):
        return pltpu.make_async_remote_copy(
            src_ref=source,
            dst_ref=target,
            send_sem=self.send.at[slot],
            recv_sem=self.recv.at[slot],
            device_id=(self.dp, peer, self.uly),
            device_id_type=MESH,
        )

    def greet(self, devices):
        barrier = pltpu.get_barrier_semaphore()
        for device in devices:
            pl.semaphore_signal(barrier, inc=1, device_id=device, device_id_type=MESH)
        pl.semaphore_wait(barrier, len(devices))

    def remote(self, source, target, device, sends=None, receives=None):
        slot = self.used
        self.used += 1

        def descriptor():
            return pltpu.make_async_remote_copy(
                src_ref=source(),
                dst_ref=target(),
                send_sem=self.send.at[slot],
                recv_sem=self.recv.at[slot],
                device_id=device,
                device_id_type=MESH,
            )

        copy = Copy(descriptor, sends, receives)
        self.copies.append(copy)
        return copy.start()

    def to(self, source, target, device):
        return self.remote(lambda: source, lambda: target, device)

    def local(self, source, target):
        copy = pltpu.make_async_copy(source, target, self.here.at[self.used_here])
        self.used_here += 1
        copy.start()
        self.local_copies.append(copy)
        return copy

    def finish(self):
        for copy in self.copies:
            copy.sent()


class LineGather:
    def __init__(self, links, own, whole):
        self.links, self.own, self.whole = links, own, whole
        self.waiting = []

    def send(self, step):
        links, whole = self.links, self.whole
        blk, last = links.blk, links.n_blk - 1

        def block(index):
            if step == 0:
                return lambda: self.own
            return lambda: whole.at[index]

        self.waiting = [
            links.remote(
                block(blk - step),
                lambda: whole.at[blk - step],
                (links.dp, blk + 1, links.uly),
                jnp.logical_and(blk >= step, blk < last),
                blk >= step + 1,
            ),
            links.remote(
                block(blk + step),
                lambda: whole.at[blk + step],
                (links.dp, blk - 1, links.uly),
                jnp.logical_and(blk + step <= last, blk > 0),
                blk + step + 1 <= last,
            ),
        ]

    def arrived(self):
        for copy in self.waiting:
            copy.arrived()


def halves(tokens):
    return [pl.ds(0, tokens // 2), pl.ds(tokens // 2, tokens // 2)]


class HalvedLine:
    def __init__(self, links, own, whole):
        self.lines = [
            LineGather(links, None if own is None else own.at[rows], whole.at[:, rows])
            for rows in halves(whole.shape[1])
        ]

    def send(self, step):
        for line in self.lines:
            line.send(step)

    def advance(self, step):
        for line in self.lines:
            line.arrived()
            line.send(step)

    def arrived(self):
        for line in self.lines:
            line.arrived()


class PlaneGather:
    def __init__(self, links, at):
        self.links, self.at = links, at

    def start_x(self, own):
        links = self.links
        mine = self.at(links.dp, links.uly)
        self.from_x = links.to(own, mine, links.x_way)
        self.from_core = [links.to(own, mine, links.core_way)]

    def start_y(self, own):
        links = self.links
        self.from_y = links.to(own, self.at(links.dp, links.uly), links.y_way)

    def start(self, own=None):
        own = self.at(self.links.dp, self.links.uly) if own is None else own
        self.start_x(own)
        self.start_y(own)

    def hand_on(self):
        links, at = self.links, self.at
        self.from_x.arrived()
        half = at(links.other_dp, links.uly, 0)
        self.second_y = links.to(half, half, links.y_way)
        self.from_y.arrived()
        half = at(links.dp, links.across, 1)
        self.second_x = links.to(half, half, links.x_way)
        for chunk in (at(links.other_dp, links.uly), at(links.dp, links.across)):
            self.from_core.append(links.to(chunk, chunk, links.core_way))

    def last(self):
        links = self.links
        self.second_y.arrived()
        self.second_x.arrived()
        chunk = self.at(links.other_dp, links.across)
        self.from_core.append(links.to(chunk, chunk, links.core_way))

    def arrived(self):
        for copy in self.from_core:
            copy.arrived()


def rows_of(whole, blocked):
    def at(dp, uly, half=None):
        part = whole.at[dp, :, uly] if blocked else whole.at[dp, uly]
        if half is None:
            return part
        depth = whole.shape[-2] // 2
        rows = pl.ds(half * depth, depth)
        return part.at[:, rows] if blocked else part.at[rows]

    return at


class ColumnSwap:
    def __init__(self, links, pieces):
        self.links, self.pieces = links, pieces
        self.incoming, self.kept = [], []

    def parts(self, blk):
        links = self.links
        for weight, whole, offset in self.pieces:
            width = weight.shape[-1] // links.n_dp // links.n_blk
            for group in range(links.n_dp):
                start = (group * links.n_blk + blk) * width
                yield (
                    weight.at[:, pl.ds(pl.multiple_of(start, 128), width)],
                    whole.at[links.blk, :, pl.ds(offset + group * width, width)],
                )

    def start(self):
        links = self.links
        self.incoming = links.swap(lambda peer: list(self.parts(peer)))
        for source, target in self.parts(links.blk):
            self.kept.append(links.local(source, target))

    def arrived(self):
        for copy in self.kept:
            copy.wait()
        for copy in self.incoming:
            copy.arrived()


def write_positions(links, span_order, toks, cosine, sine, query_pos, key_pos):
    half_len = toks * links.n_uly // 2

    def first(blk, uly):
        chunk = span_order[2 * blk + lax.div(uly, links.n_uly // 2)]
        return chunk * half_len + lax.rem(uly, links.n_uly // 2) * toks

    lane = lax.broadcasted_iota(jnp.int32, (toks, HEAD_SIZE), 1)
    row = lax.broadcasted_iota(jnp.int32, (toks, HEAD_SIZE), 0)
    upper = lane >= HEAD_SIZE // 2
    step = jnp.where(upper, lane - HEAD_SIZE // 2, lane).astype(jnp.float32)
    inverse = jnp.exp(step * (-2.0 * math.log(ROPE_BASE) / HEAD_SIZE))
    for blk in range(links.n_blk):
        angles = (first(blk, links.uly) + row).astype(jnp.float32) * inverse
        at = slice(blk * toks, (blk + 1) * toks)
        cosine[at, :] = jnp.cos(angles)
        turn = jnp.sin(angles)
        sine[at, :] = jnp.where(upper, turn, -turn)
    lane = lax.broadcasted_iota(jnp.int32, query_pos.shape, 1)
    place = jnp.zeros(query_pos.shape, jnp.int32)
    for start in range(0, query_pos.shape[1], toks):
        blk = start // toks % links.n_blk
        here = jnp.logical_and(lane >= start, lane < start + toks)
        place = jnp.where(here, first(blk, links.uly) + lane - start, place)
    query_pos[...] = place
    row = lax.broadcasted_iota(jnp.int32, (toks, 1), 0)
    for uly in range(links.n_uly):
        for blk in range(links.n_blk):
            start = (uly * links.n_blk + blk) * toks
            key_pos[start : start + toks, :] = row + first(blk, jnp.int32(uly))


def write_gains(links, all_gains, size, targets):
    per_row = 128 // size
    for which, target in enumerate(targets):
        for place in range(target.shape[1] // 128):
            pieces = []
            for part in range(per_row):
                device = place * per_row + part
                plane, uly = device // links.n_uly, device % links.n_uly
                gains = all_gains[plane // links.n_blk, plane % links.n_blk, uly]
                pieces.append(gains.astype(jnp.float32)[which : which + 1, :size])
            target[:, place * 128 : (place + 1) * 128] = jnp.concatenate(pieces, axis=1)


ROWS = 32


def each_block(count, body):
    def step(index, carry):
        body(pl.ds(pl.multiple_of(index * ROWS, ROWS), ROWS))
        return carry

    lax.fori_loop(0, count // ROWS, step, 0)


class LineScatter:
    def __init__(self, links, parts, rightward, leftward):
        self.links, self.parts = links, parts
        self.slots = {1: rightward, -1: leftward}
        self.tokens = parts.shape[1]
        self.number = links.used
        self.last = links.n_blk - 1
        links.used += 2 * self.last

    def target(self, step, way):
        return self.last - step if way == 1 else step

    def slot(self, step, way):
        target = self.target(step, way)
        return self.slots[way].at[target - 1 if way == 1 else target]

    def place(self, way):
        return self.links.blk if way == 1 else self.last - self.links.blk

    def copy(self, step, way, source=None):
        links, slot = self.links, self.slot(step, way)
        number = self.number + 2 * step + (1 if way == 1 else 0)
        return pltpu.make_async_remote_copy(
            src_ref=slot if source is None else source,
            dst_ref=slot,
            send_sem=links.send.at[number],
            recv_sem=links.recv.at[number],
            device_id=(links.dp, links.blk + way, links.uly),
            device_id_type=MESH,
        )

    def start(self):
        for step in range(self.last):
            for way in (1, -1):

                @pl.when(self.place(way) == 0)
                def _(step=step, way=way):
                    self.copy(step, way, self.parts.at[self.target(step, way)]).start()

    def tick(self, tick):
        for way in (1, -1):

            @pl.when(jnp.logical_and(self.place(way) >= 1, self.place(way) <= tick))
            def _(way=way):
                step = tick - self.place(way)
                self.copy(step, way).wait_recv()
                slot, target = self.slot(step, way), self.target(step, way)

                def body(rows):
                    slot[rows, :] = slot[rows, :] + self.parts[target, rows, :]

                each_block(self.tokens, body)
                self.copy(step, way).start()

    def finish(self, total):
        blk, last = self.links.blk, self.last

        def start(rows):
            total[rows, :] = self.parts[blk, rows, :].astype(jnp.float32)

        each_block(self.tokens, start)
        for way in (1, -1):

            @pl.when(self.place(way) >= 1)
            def _(way=way):
                step = last - self.place(way)
                self.copy(step, way).wait_recv()
                slot = self.slot(step, way)

                def body(rows):
                    total[rows, :] = total[rows, :] + slot[rows, :].astype(jnp.float32)

                each_block(self.tokens, body)

    def sent(self):
        for step in range(self.last):
            for way in (1, -1):
                beyond = self.place(way) + step < self.last
                pl.when(beyond)(lambda step=step, way=way: self.copy(step, way).wait_send())


class ScatterPair:
    def __init__(self, links, parts, rightward, leftward):
        self.spans = halves(parts.shape[1])
        self.sums = [
            LineScatter(links, parts.at[:, rows], rightward.at[:, rows], leftward.at[:, rows])
            for rows in self.spans
        ]

    def start(self):
        for half in self.sums:
            half.start()

    def tick(self, tick):
        for half in self.sums:
            half.tick(tick)

    def finish(self, total):
        for half, rows in zip(self.sums, self.spans):
            half.finish(total.at[rows])

    def sent(self):
        for half in self.sums:
            half.sent()


def halved_sums(links, parts, rightward, leftward):
    return [
        ScatterPair(links, parts.at[:, rows], rightward.at[:, rows], leftward.at[:, rows])
        for rows in halves(parts.shape[1])
    ]


class OutputHalf:
    def __init__(self, links, which, parts, middle, rightward, leftward, total):
        rows = halves(middle.shape[0])[which]
        self.middle, self.total = middle.at[rows], total
        self.sum = LineScatter(links, parts.at[:, rows], rightward, leftward)

    def write(self, output):
        self.sum.finish(self.total)

        def body(rows):
            output[rows, :] = (self.middle[rows, :] + self.total[rows, :]).astype(jnp.bfloat16)

        each_block(self.middle.shape[0], body)


def output_scratch(n_blk, tokens, width):
    return line_scratch(n_blk, tokens // 2, width) + [
        pltpu.VMEM((tokens // 2, width), jnp.float32)
    ]


def line_scratch(n_blk, tokens, width):
    return [pltpu.VMEM((n_blk - 1, tokens, width), jnp.bfloat16)] * 2


class PlaneScatter:
    def __init__(self, links, parts, from_core, from_x, from_y, last_x, last_y):
        self.links, self.parts = links, parts
        self.own_core_only = from_core is None
        self.from_core, self.from_x, self.from_y = from_core, from_x, from_y
        self.last_x, self.last_y = last_x, last_y
        self.core = lax.rem(links.uly, 2)
        self.row = lax.div(links.uly, 2)
        self.depth = parts.shape[3]
        self.core_copies = {}

    def chunk(self, dp, row, core, half=None):
        if self.own_core_only:
            part = self.parts.at[dp, row]
        else:
            part = self.parts.at[dp, :, row * 2 + core]
        if half is None:
            return part
        depth = self.depth // 2
        return part.at[:, pl.ds(half * depth, depth)]

    def add(self, target, source):
        blocks, depth, _ = target.shape
        rows = 32 if depth % 32 == 0 else 16

        def body(index, carry):
            block = lax.div(index, depth // rows)
            at = pl.ds(pl.multiple_of(lax.rem(index, depth // rows) * rows, rows), rows)
            target[block, at, :] = target[block, at, :] + source[block, at, :]
            return carry

        lax.fori_loop(0, blocks * (depth // rows), body, 0)

    def between_cores(self, which):
        links = self.links
        dp = links.dp if which == 1 else links.other_dp
        self.core_copies[which] = [
            links.to(
                self.chunk(dp, row, 1 - self.core), self.from_core.at[which, row], links.core_way
            )
            for row in range(2)
        ]

    def core_sums(self, which):
        links = self.links
        dp = links.dp if which == 1 else links.other_dp
        for row in range(2):
            self.core_copies[which][row].arrived()
            self.add(self.chunk(dp, row, self.core), self.from_core.at[which, row])

    def across_chips(self):
        links = self.links
        if not self.own_core_only:
            self.core_sums(0)
        self.x_copies = [
            links.to(
                self.chunk(links.other_dp, row, self.core, 0), self.from_x.at[row], links.x_way
            )
            for row in range(2)
        ]
        if not self.own_core_only:
            self.core_sums(1)
        self.y_copies = [
            links.to(
                self.chunk(group, 1 - self.row, self.core, 1),
                self.from_y.at[group],
                links.y_way,
            )
            for group in range(links.n_dp)
        ]

    def second_way(self):
        links = self.links
        for row in range(2):
            self.x_copies[row].arrived()
            self.add(self.chunk(links.dp, row, self.core, 0), self.from_x.at[row])
        self.y_last = links.to(
            self.chunk(links.dp, 1 - self.row, self.core, 0), self.last_y, links.y_way
        )
        for group in range(links.n_dp):
            self.y_copies[group].arrived()
            self.add(self.chunk(group, self.row, self.core, 1), self.from_y.at[group])
        self.x_last = links.to(
            self.chunk(links.other_dp, self.row, self.core, 1), self.last_x, links.x_way
        )

    def result(self, write):
        links = self.links
        for half, copy, source in ((0, self.y_last, self.last_y), (1, self.x_last, self.last_x)):
            copy.arrived()
            own = self.chunk(links.dp, self.row, self.core, half)
            blocks, depth, _ = source.shape
            rows = 32 if depth % 32 == 0 else 16

            def body(index, carry, own=own, source=source, half=half, depth=depth, rows=rows):
                block = lax.div(index, depth // rows)
                start = pl.multiple_of(lax.rem(index, depth // rows) * rows, rows)
                at = pl.ds(start, rows)
                value = own[block, at, :].astype(jnp.float32)
                value = value + source[block, at, :].astype(jnp.float32)
                write(block, pl.ds(pl.multiple_of(start + half * depth, rows), rows), value)
                return carry

            lax.fori_loop(0, blocks * (depth // rows), body, 0)


def plane_shapes(n_dp, blocks, n_uly, depth, width):
    return [
        (n_dp, blocks, n_uly, depth, width),
        (n_dp, 2, blocks, depth, width),
        (2, blocks, depth // 2, width),
        (n_dp, blocks, depth // 2, width),
        (blocks, depth // 2, width),
        (blocks, depth // 2, width),
    ]


def plane_scratch(*sizes):
    return [pltpu.VMEM(shape, jnp.bfloat16) for shape in plane_shapes(*sizes)]


def weight_grad(rows, right, parts, dp):
    _, blocks, n_uly, depth, width = parts.shape
    columns = 512

    def body(index, carry):
        at = pl.ds(pl.multiple_of(index * columns, columns), columns)
        part = jnp.dot(rows[...], right[:, at], preferred_element_type=jnp.float32)
        parts[dp, :, :, :, at] = part.astype(jnp.bfloat16).reshape(blocks, n_uly, depth, columns)
        return carry

    lax.fori_loop(0, width // columns, body, 0)


def rows_turned(left, parts, dp):
    count = parts.shape[1] * parts.shape[2] * parts.shape[3]
    return left[:, pl.ds(pl.multiple_of(dp * count, 128), count)].T


def turned(rows, cosine, sine):
    return rows * cosine + pltpu.roll(rows, HEAD_SIZE // 2, axis=1) * sine


def transposed_product(left, right):
    return lax.dot_general(
        left, right, (((0,), (0,)), ((), ())), preferred_element_type=jnp.float32
    )


def product_right(left, right):
    return lax.dot_general(
        left, right, (((1,), (1,)), ((), ())), preferred_element_type=jnp.float32
    )


SCORE_SCALE = 1.0 / math.sqrt(HEAD_SIZE)


def forward_kernel(
    toks,
    gain_rows,
    span_order,
    hidden,
    wq,
    wk,
    wv,
    wo,
    wg,
    wu,
    wd,
    cotangent,
    gains,
    q_gain,
    k_gain,
    all_qkv,
    all_wo,
    all_wg,
    all_wu,
    all_wd,
    all_cot,
    attn_gain,
    mlp_gain,
    cosine,
    sine,
    query_pos,
    key_pos,
    heads,
    normed,
    qkv,
    queries,
    key_values,
    lse,
    middle,
    all_normed,
    all_gains,
    all_hidden,
    near_qkv,
    near_wo,
    parts,
    rightward,
    leftward,
    own_normed,
    send,
    recv,
    here,
):
    links = Links(send, recv, here)
    links.greet(links.peers() + [links.x_way, links.y_way, links.core_way])
    tokens, width = hidden.shape
    spans = halves(tokens)
    q_width, k_width = wq.shape[1] // links.n_blk, wk.shape[1] // links.n_blk
    chunk = all_qkv.at[links.dp, :, links.uly]
    swap = ColumnSwap(
        links, [(wq, chunk, 0), (wk, chunk, q_width), (wv, chunk, q_width + k_width)]
    )
    plane_wo = PlaneGather(links, rows_of(all_wo, False))
    plane_wd = PlaneGather(links, rows_of(all_wd, False))
    plane_qkv = PlaneGather(links, rows_of(all_qkv, True))
    plane_gain = PlaneGather(links, rows_of(all_gains, True))
    swap.start()
    my_gains = all_gains.at[links.dp, links.blk, links.uly]
    gain_swap = [links.to(gains, my_gains, device) for device in links.peers()]
    plane_wo.start(wo)
    line = HalvedLine(links, hidden, all_hidden)
    line.send(0)
    keep = [
        links.local(gains, my_gains),
        links.local(hidden, all_hidden.at[links.blk]),
        links.local(wo, all_wo.at[links.dp, links.uly]),
        links.local(wd, all_wd.at[links.dp, links.uly]),
        links.local(cotangent, all_cot.at[links.blk]),
    ]
    write_positions(links, span_order, toks, cosine, sine, query_pos, key_pos)
    swap.arrived()
    plane_qkv.start()
    keep[0].wait()
    for copy in gain_swap:
        copy.arrived()
    plane_gain.start()
    plane_wd.start(wd)
    plane_wo.hand_on()
    line.advance(1)
    plane_qkv.hand_on()
    plane_gain.hand_on()
    plane_wo.last()
    for step in range(2, links.n_blk - 1):
        line.advance(step)
    pairs = [(wg, all_wg), (wu, all_wu)]
    planes = [PlaneGather(links, rows_of(whole, True)) for _, whole in pairs]
    swaps = [
        ColumnSwap(links, [(weight, whole.at[links.dp, :, links.uly], 0)])
        for weight, whole in pairs
    ]
    for swap in swaps:
        swap.start()
    cot_lines = HalvedLine(links, cotangent, all_cot).lines
    for half in cot_lines:
        half.send(0)
    plane_qkv.last()
    plane_gain.last()
    plane_gain.arrived()
    write_gains(links, all_gains, gain_rows, (attn_gain, mlp_gain))
    for copy in keep[1:]:
        copy.wait()
    plane_wo.arrived()
    plane_qkv.arrived()
    near = [links.local(all_qkv, near_qkv), links.local(all_wo, near_wo)]
    seqs, kv_heads, q_rows, _ = queries.shape
    q_len = key_values.shape[4]
    group = q_rows // q_len
    q_end = kv_heads * group * HEAD_SIZE
    k_end = q_end + kv_heads * HEAD_SIZE

    def norm(seq):
        def body(rows):
            for blk in range(links.n_blk):
                at = pl.ds(pl.multiple_of(seq * toks + rows.start, ROWS), ROWS)
                to = pl.ds(pl.multiple_of(seq * q_len + blk * toks + rows.start, ROWS), ROWS)
                source = all_hidden[blk, at, :].astype(jnp.float32)
                normed[to, :] = (source * rms_scale(source) * attn_gain[...]).astype(
                    jnp.bfloat16
                )

        each_block(toks, body)

    def rotated(seq, column, gain):
        pre = qkv[seq * q_len : (seq + 1) * q_len, column : column + HEAD_SIZE]
        gain = gain[...].astype(jnp.float32)
        return turned(pre * rms_scale(pre) * gain, cosine[...], sine[...]).astype(jnp.bfloat16)

    def project(seq):
        rows = slice(seq * q_len, (seq + 1) * q_len)
        for column in range(0, qkv.shape[1], 512):
            weight = near_qkv[:, :, :, :, column : column + 512].reshape(width, 512)
            qkv[rows, column : column + 512] = jnp.dot(
                normed[rows, :], weight, preferred_element_type=jnp.float32
            )
        for head in range(kv_heads):
            column = head * HEAD_SIZE
            key_values[links.uly, 0, seq, head] = rotated(seq, q_end + column, k_gain)
            key_values[links.uly, 1, seq, head] = qkv[
                rows, k_end + column : k_end + column + HEAD_SIZE
            ].astype(jnp.bfloat16)
        mine = key_values.at[links.uly, :, seq]
        copies = [links.to(mine, mine, way) for way in (links.core_way, links.y_way)]
        for head in range(kv_heads * group):
            at = pl.ds((head % group) * q_len, q_len)
            queries[seq, head // group, at, :] = rotated(seq, head * HEAD_SIZE, q_gain)
        return copies

    def hand_keys(seq, copies):
        copies[1].arrived()
        theirs = key_values.at[links.across, :, seq]
        copies.append(links.to(theirs, theirs, links.core_way))

    def attend(seq, head):
        def over_keys(piece, carry):
            total, mixed = carry
            rows = pl.ds(pl.multiple_of(piece * q_len, q_len), q_len)
            scores = product_right(key_values[piece, 0, seq, head], queries[seq, head])
            weights = jnp.where(
                query_pos[...] >= key_pos[rows, :], jnp.exp(scores * SCORE_SCALE), 0.0
            )
            total = total + jnp.sum(weights, axis=0, keepdims=True)
            mixed = mixed + transposed_product(
                key_values[piece, 1, seq, head], weights.astype(jnp.bfloat16)
            )
            return total, mixed

        total, mixed = lax.fori_loop(
            0,
            links.n_uly,
            over_keys,
            (
                jnp.zeros((1, q_rows), jnp.float32),
                jnp.zeros((HEAD_SIZE, q_rows), jnp.float32),
            ),
        )
        lse[seq * kv_heads + head] = jnp.log(total)
        attended = (mixed / total).T.astype(jnp.bfloat16)
        for member in range(group):
            column = (head * group + member) * HEAD_SIZE
            for blk in range(links.n_blk):
                row = (blk * seqs + seq) * toks
                start = member * q_len + blk * toks
                heads[row : row + toks, column : column + HEAD_SIZE] = attended[
                    start : start + toks, :
                ]

    sums = halved_sums(links, parts, rightward, leftward)
    def out_weight():
        return near_wo[...].reshape(heads.shape[1], width)

    def out_parts(seq):
        mixed = jnp.concatenate(
            [
                heads[(blk * seqs + seq) * toks : (blk * seqs + seq + 1) * toks, :]
                for blk in range(links.n_blk)
            ],
            axis=0,
        )
        for column in range(0, width, 512):
            parts[:, spans[seq], column : column + 512] = (
                jnp.dot(
                    mixed,
                    out_weight()[:, column : column + 512],
                    preferred_element_type=jnp.float32,
                )
                .astype(jnp.bfloat16)
                .reshape(links.n_blk, toks, 512)
            )
        sums[seq].start()

    key_copies = []
    for seq in range(seqs):
        line.lines[seq].arrived()
        norm(seq)
        if seq == 0:
            for copy in near:
                copy.wait()
        key_copies.append(project(seq))
    plane_wd.hand_on()
    hand_keys(0, key_copies[0])
    for copy in (key_copies[0][0], key_copies[0][2]):
        copy.arrived()
    attend(0, 0)
    hand_keys(1, key_copies[1])
    for head in range(1, kv_heads):
        attend(0, head)
    out_parts(0)
    swaps[0].arrived()
    planes[0].start()
    for copy in (key_copies[1][0], key_copies[1][2]):
        copy.arrived()
    attend(1, 0)
    sums[0].tick(1)
    for head in range(1, kv_heads):
        attend(1, head)
    out_parts(1)
    swaps[1].arrived()
    planes[1].start()
    later = range(2, links.n_blk - 1)
    for tick in later:
        sums[0].tick(tick)
    for half in cot_lines:
        half.arrived()
        half.send(1)
    plane_wd.last()
    planes[0].hand_on()
    lines = []

    def settle(half, rows_of_half):
        half.finish(middle.at[rows_of_half])

        def body(rows):
            at = pl.ds(pl.multiple_of(rows_of_half.start + rows.start, ROWS), ROWS)
            total = middle[at, :] + all_hidden[links.blk, at, :].astype(jnp.float32)
            middle[at, :] = total
            own_normed[at, :] = (total * rms_scale(total) * mlp_gain[...]).astype(jnp.bfloat16)

        each_block(tokens // 2, body)
        pair = HalvedLine(links, own_normed.at[rows_of_half], all_normed.at[:, rows_of_half])
        pair.send(0)
        lines.extend(pair.lines)

    settle(sums[0], spans[0])
    sums[1].tick(1)
    for tick in later:
        sums[1].tick(tick)
    settle(sums[1], spans[1])
    for step in range(2, links.n_blk - 1):
        for half in cot_lines:
            half.arrived()
            half.send(step)
    last_local = links.local(own_normed, all_normed.at[links.blk])
    planes[1].hand_on()
    planes[0].last()
    for step in range(1, links.n_blk - 1):
        for half in lines:
            half.arrived()
            half.send(step)
    planes[1].last()
    for half in lines + cot_lines:
        half.arrived()
    for plane in [plane_wd] + planes:
        plane.arrived()
    last_local.wait()
    for half in sums:
        half.sent()
    links.finish()


SMEM = pl.BlockSpec(memory_space=pltpu.SMEM)


def forward(
    span_order,
    hidden,
    wq,
    wk,
    wv,
    wo,
    wg,
    wu,
    wd,
    cotangent,
    gains,
    q_gain,
    k_gain,
    seqs,
    gain_rows,
):
    n_dp, n_blk, n_uly = (lax.axis_size(a) for a in EVERY)
    tokens, width = hidden.shape
    toks = tokens // seqs
    rows, q_len = n_blk * tokens, n_blk * toks
    group = QUERY_HEADS // KEY_VALUE_HEADS
    kv_heads = KEY_VALUE_HEADS // n_blk
    q_rows, keys = group * q_len, n_uly * q_len
    columns = (wq.shape[1] + wk.shape[1] + wv.shape[1]) // n_blk
    f32, low, i32 = jnp.float32, jnp.bfloat16, jnp.int32
    ff = wg.shape[1] // n_blk
    far = [
        (n_dp, n_blk, n_uly, wq.shape[0], columns),
        (n_dp, n_uly) + wo.shape,
        (n_dp, n_blk, n_uly, wg.shape[0], ff),
        (n_dp, n_blk, n_uly, wu.shape[0], ff),
        (n_dp, n_uly) + wd.shape,
        (n_blk, tokens, width),
    ]
    near = [
        ((1, width), f32),
        ((1, width), f32),
        ((q_len, HEAD_SIZE), f32),
        ((q_len, HEAD_SIZE), f32),
        ((1, q_rows), i32),
        ((keys, 1), i32),
        ((rows, kv_heads * group * HEAD_SIZE), low),
        ((rows, width), low),
        ((rows, columns), f32),
        ((seqs, kv_heads, q_rows, HEAD_SIZE), low),
        ((n_uly, 2, seqs, kv_heads, q_len, HEAD_SIZE), low),
        ((seqs * kv_heads, 1, q_rows), f32),
        ((tokens, width), f32),
        ((n_blk, tokens, width), low),
    ]
    scratch = [
        ((n_dp, n_blk, n_uly) + gains.shape, low),
        ((n_blk, tokens, width), low),
        (far[0], low),
        (far[1], low),
        ((n_blk, tokens, width), low),
        ((n_blk - 1, tokens, width), low),
        ((n_blk - 1, tokens, width), low),
        ((tokens, width), low),
    ]
    return pl.pallas_call(
        functools.partial(forward_kernel, toks, gain_rows),
        out_shape=[jax.ShapeDtypeStruct(shape, low) for shape in far]
        + [jax.ShapeDtypeStruct(shape, kind) for shape, kind in near],
        in_specs=[SMEM] + [HBM] * 10 + [VMEM] * 2,
        out_specs=[HBM] * len(far) + [VMEM] * len(near),
        scratch_shapes=[pltpu.VMEM(shape, kind) for shape, kind in scratch]
        + semaphores(184, 32),
        compiler_params=kernel_params(0),
    )(span_order, hidden, wq, wk, wv, wo, wg, wu, wd, cotangent, gains, q_gain, k_gain)


def back_rows(grad_normed, source, gain):
    unit = source * rms_scale(source)
    scaled = grad_normed * gain
    return rms_scale(source) * (
        scaled - unit * jnp.mean(scaled * unit, axis=-1, keepdims=True)
    )


def back_kernel(
    grad_parts,
    out_parts,
    middle,
    cotangent,
    gain,
    all_normed,
    grad_gate_pre,
    grad_up_pre,
    activated,
    all_cot,
    output,
    grad_middle,
    all_low,
    grad_gate,
    grad_up,
    part_down,
    rightward,
    leftward,
    out_right,
    out_left,
    out_total,
    low,
    turned_low,
    gate_1,
    gate_2,
    gate_3,
    gate_4,
    gate_5,
    gate_6,
    up_1,
    up_2,
    up_3,
    up_4,
    up_5,
    up_6,
    down_1,
    down_2,
    send,
    recv,
    here,
):
    links = Links(send, recv, here)
    links.greet(links.peers() + [links.x_way, links.y_way, links.core_way])
    sums = halved_sums(links, grad_parts, rightward, leftward)
    for half in sums:
        half.start()
    out = OutputHalf(links, 0, out_parts, middle, out_right, out_left, out_total)
    gate = PlaneScatter(links, gate_1, gate_2, gate_3, gate_4, gate_5, gate_6)
    up = PlaneScatter(links, up_1, up_2, up_3, up_4, up_5, up_6)
    down = PlaneScatter(links, down_1, down_2, None, None, None, None)
    tokens = middle.shape[0]
    spans, lines, keep = halves(tokens), [], []

    def compute(plane, which, rows, right):
        dp = links.dp if which == 1 else links.other_dp
        weight_grad(rows, right, plane.parts, dp)
        plane.between_cores(which)

    def turn(which):
        dp = links.dp if which == 1 else links.other_dp
        turned_low[which] = rows_turned(all_normed, gate_1, dp)

    def compute_down(which):
        dp = links.dp if which == 1 else links.other_dp
        compute(down, which, rows_turned(activated, down_1, dp), all_cot)

    def settle(half, rows_of_half):
        half.finish(grad_middle.at[rows_of_half])

        def body(rows):
            at = pl.ds(pl.multiple_of(rows_of_half.start + rows.start, ROWS), ROWS)
            back = back_rows(grad_middle[at, :], middle[at, :], gain[...])
            grad = cotangent[at, :].astype(jnp.float32) + back
            grad_middle[at, :] = grad
            low[at, :] = grad.astype(jnp.bfloat16)

        each_block(tokens // 2, body)
        pair = HalvedLine(links, low.at[rows_of_half], all_low.at[:, rows_of_half])
        pair.send(0)
        lines.extend(pair.lines)

    later = range(2, links.n_blk - 1)
    turn(0)
    compute(gate, 0, turned_low.at[0], grad_gate_pre)
    sums[0].tick(1)
    turn(1)
    compute(gate, 1, turned_low.at[1], grad_gate_pre)
    for tick in later:
        sums[0].tick(tick)
    gate.across_chips()
    settle(sums[0], spans[0])
    compute(up, 0, turned_low.at[0], grad_up_pre)
    sums[1].tick(1)
    compute(up, 1, turned_low.at[1], grad_up_pre)
    for tick in later:
        sums[1].tick(tick)
    up.across_chips()
    settle(sums[1], spans[1])
    out.sum.start()
    keep.append(links.local(low, all_low.at[links.blk]))
    compute_down(0)
    for step in range(1, links.n_blk - 1):
        for line in lines:
            line.arrived()
            line.send(step)
        if step == 1:
            gate.second_way()
            compute_down(1)
    out.sum.tick(1)
    up.second_way()
    for which in (0, 1):
        down.core_sums(which)
    for dp in range(links.n_dp):
        for row in range(2):
            keep.append(links.local(down.chunk(dp, row, down.core), part_down.at[dp, row]))
    for tick in later:
        out.sum.tick(tick)
    for line in lines:
        line.arrived()

    def into(target):
        def write(block, rows, values):
            target[block, rows, :] = values.astype(target.dtype)

        return write

    gate.result(into(grad_gate))
    up.result(into(grad_up))
    out.write(output)
    out.sum.sent()
    for copy in keep:
        copy.wait()
    for half in sums:
        half.sent()
    links.finish()


def exchange_back(
    grad_parts,
    out_parts,
    middle,
    cotangent,
    gain,
    all_normed,
    grad_gate_pre,
    grad_up_pre,
    activated,
    all_cot,
):
    n_dp, n_blk, n_uly = (lax.axis_size(a) for a in EVERY)
    _, tokens, width = grad_parts.shape
    ff = grad_gate_pre.shape[1]
    depth = width // (n_dp * n_blk * n_uly)
    down_depth = ff // (n_dp * n_uly)
    return pl.pallas_call(
        back_kernel,
        out_shape=[
            jax.ShapeDtypeStruct((tokens // 2, width), jnp.bfloat16),
            jax.ShapeDtypeStruct((tokens, width), jnp.float32),
            jax.ShapeDtypeStruct((n_blk, tokens, width), jnp.bfloat16),
            jax.ShapeDtypeStruct((n_blk, depth, ff), jnp.bfloat16),
            jax.ShapeDtypeStruct((n_blk, depth, ff), jnp.bfloat16),
            jax.ShapeDtypeStruct((n_dp, 2, 1, down_depth, width), jnp.bfloat16),
        ],
        in_specs=[VMEM] * 10,
        out_specs=[VMEM, VMEM, HBM, VMEM, VMEM, HBM],
        scratch_shapes=line_scratch(n_blk, tokens, width)
        + output_scratch(n_blk, tokens, width)
        + [
            pltpu.VMEM((tokens, width), jnp.bfloat16),
            pltpu.VMEM((n_dp, width // n_dp, n_blk * tokens), jnp.bfloat16),
        ]
        + plane_scratch(n_dp, n_blk, n_uly, depth, ff) * 2
        + plane_scratch(n_dp, 1, n_uly, down_depth, width)[:2]
        + semaphores(112),
        compiler_params=kernel_params(3),
    )(
        grad_parts,
        out_parts,
        middle,
        cotangent,
        gain,
        all_normed,
        grad_gate_pre,
        grad_up_pre,
        activated,
        all_cot,
    )


def backward_kernel(
    all_low,
    wo,
    queries,
    key_values,
    lse,
    qkv,
    q_gain,
    k_gain,
    cosine,
    sine,
    query_pos,
    key_pos,
    w_qkv,
    hidden,
    grad_middle,
    gain,
    normed,
    heads,
    out_parts,
    middle,
    grad_gate,
    grad_up,
    part_down,
    grad_hidden,
    grad_wo,
    grad_down,
    small_sum,
    output,
    gate_rows,
    up_rows,
    grad_w_qkv,
    grad_qkv,
    gain_terms,
    grad_heads,
    grad_rows,
    grad_kv,
    from_core,
    from_across,
    grad_parts,
    rightward,
    leftward,
    summed,
    small_in,
    small_total,
    out_right,
    out_left,
    out_total,
    down_1,
    down_3,
    down_4,
    down_5,
    down_6,
    turned_normed,
    q_1,
    q_2,
    q_3,
    q_4,
    q_5,
    q_6,
    kv_1,
    kv_2,
    kv_3,
    kv_4,
    kv_5,
    kv_6,
    wo_1,
    wo_2,
    wo_3,
    wo_4,
    wo_5,
    wo_6,
    send,
    recv,
    here,
):
    links = Links(send, recv, here)
    links.greet(links.peers() + [links.x_way, links.y_way, links.core_way])
    tokens = hidden.shape[0]
    spans = halves(tokens)
    output_half = OutputHalf(links, 1, out_parts, middle, out_right, out_left, out_total)
    output_half.sum.start()
    down = PlaneScatter(links, down_1, None, down_3, down_4, down_5, down_6)
    fetch = links.local(part_down, down_1)
    swapped, keep = [], []
    for source, target in ((grad_gate, gate_rows), (grad_up, up_rows)):
        swapped += links.swap(
            lambda peer, source=source, target=target: [(source.at[peer], target.at[links.blk])]
        )
        keep.append(links.local(source.at[links.blk], target.at[links.blk]))
    fetch.wait()
    down.across_chips()
    sums = halved_sums(links, grad_parts, rightward, leftward)
    q_sums = PlaneScatter(links, q_1, q_2, q_3, q_4, q_5, q_6)
    kv_sums = PlaneScatter(links, kv_1, kv_2, kv_3, kv_4, kv_5, kv_6)
    wo_sums = PlaneScatter(links, wo_1, wo_2, wo_3, wo_4, wo_5, wo_6)
    seqs, kv_heads, q_rows, _ = queries.shape
    q_len = key_values.shape[4]
    group = q_rows // q_len
    toks = q_len // links.n_blk
    q_end = kv_heads * group * HEAD_SIZE
    k_end = q_end + kv_heads * HEAD_SIZE
    gain_terms[...] = jnp.zeros_like(gain_terms)
    later = range(2, links.n_blk - 1)

    def heads_back(seq):
        low = jnp.concatenate(
            [
                all_low[(blk * seqs + seq) * toks : (blk * seqs + seq + 1) * toks, :]
                for blk in range(links.n_blk)
            ],
            axis=0,
        )
        grad_heads[...] = product_right(low, wo[...])
        for head in range(kv_heads * group):
            to = pl.ds((head % group) * q_len, q_len)
            grad_rows[seq, head // group, to, :] = grad_heads[
                :, head * HEAD_SIZE : (head + 1) * HEAD_SIZE
            ].astype(jnp.bfloat16)

    def back_norm(upstream, seq, column, gain, which):
        rows = slice(seq * q_len, (seq + 1) * q_len)
        pre = qkv[rows, column : column + HEAD_SIZE]
        upstream = turned(upstream, cosine[...], -sine[...])
        gain_terms[which : which + 1, :] += jnp.sum(
            upstream * pre * rms_scale(pre), axis=0, keepdims=True
        )
        grad_qkv[rows, column : column + HEAD_SIZE] = back_rows(
            upstream, pre, gain[...].astype(jnp.float32)
        ).astype(jnp.bfloat16)

    def deltas(seq, head):
        sums_of = []
        for member in range(group):
            column = (head * group + member) * HEAD_SIZE
            attended = jnp.concatenate(
                [
                    heads[row : row + toks, column : column + HEAD_SIZE]
                    for row in ((blk * seqs + seq) * toks for blk in range(links.n_blk))
                ],
                axis=0,
            )
            upstream = grad_rows[seq, head, member * q_len : (member + 1) * q_len, :]
            sums_of.append(attended.astype(jnp.float32) * upstream.astype(jnp.float32))
        terms = jnp.concatenate(sums_of, axis=0)
        high = terms.astype(jnp.bfloat16)
        rest = (terms - high.astype(jnp.float32)).astype(jnp.bfloat16)
        ones = jnp.ones((16, HEAD_SIZE), jnp.bfloat16)
        return (product_right(ones, high) + product_right(ones, rest))[:1, :]

    def back(seq, head):
        delta = deltas(seq, head)

        def over_keys(piece, grad_query):
            rows = pl.ds(pl.multiple_of(piece * q_len, q_len), q_len)
            scores = product_right(key_values[piece, 0, seq, head], queries[seq, head])
            prob = jnp.where(
                query_pos[...] >= key_pos[rows, :],
                jnp.exp(scores * SCORE_SCALE - lse[seq * kv_heads + head]),
                0.0,
            )
            grad_prob = product_right(key_values[piece, 1, seq, head], grad_rows[seq, head])
            grad_score = (prob * (grad_prob - delta)).astype(jnp.bfloat16)
            grad_kv[seq, piece, 0, head] = (
                SCORE_SCALE
                * jnp.dot(grad_score, queries[seq, head], preferred_element_type=jnp.float32)
            ).astype(jnp.bfloat16)
            grad_kv[seq, piece, 1, head] = jnp.dot(
                prob.astype(jnp.bfloat16),
                grad_rows[seq, head],
                preferred_element_type=jnp.float32,
            ).astype(jnp.bfloat16)
            return grad_query + transposed_product(key_values[piece, 0, seq, head], grad_score)

        grad_query = lax.fori_loop(
            0, links.n_uly, over_keys, jnp.zeros((HEAD_SIZE, q_rows), jnp.float32)
        )
        turned_back = (grad_query * SCORE_SCALE).T
        for member in range(group):
            column = (head * group + member) * HEAD_SIZE
            back_norm(
                turned_back[member * q_len : (member + 1) * q_len, :], seq, column, q_gain, 0
            )

    core, line = lax.rem(links.uly, 2), lax.div(links.uly, 2)

    def add(target, source):
        for kind in range(2):
            for head in range(kv_heads):
                target[kind, head] = target[kind, head] + source[kind, head]

    def core_sums(seq):
        return [
            links.to(
                grad_kv.at[seq, row * 2 + 1 - core], from_core.at[seq, row], links.core_way
            )
            for row in range(2)
        ]

    def across_sums(seq, copies):
        for row in range(2):
            copies[row].arrived()
            add(grad_kv.at[seq, row * 2 + core], from_core.at[seq, row])
        return links.to(
            grad_kv.at[seq, (1 - line) * 2 + core], from_across.at[seq], links.y_way
        )

    def own_keys(seq, copy):
        copy.arrived()
        rows = slice(seq * q_len, (seq + 1) * q_len)
        for head in range(kv_heads):
            term = [
                grad_kv[seq, links.uly, kind, head].astype(jnp.float32)
                + from_across[seq, kind, head].astype(jnp.float32)
                for kind in range(2)
            ]
            back_norm(term[0], seq, q_end + head * HEAD_SIZE, k_gain, 1)
            v_at = k_end + head * HEAD_SIZE
            grad_qkv[rows, v_at : v_at + HEAD_SIZE] = term[1].astype(jnp.bfloat16)

    def normed_parts(seq):
        for column in range(0, w_qkv.shape[0], 512):
            grad_parts[:, spans[seq], column : column + 512] = (
                product_right(
                    grad_qkv[seq * q_len : (seq + 1) * q_len, :],
                    w_qkv[column : column + 512, :],
                )
                .astype(jnp.bfloat16)
                .reshape(links.n_blk, toks, 512)
            )
        sums[seq].start()

    def dp_of(which):
        return links.dp if which == 1 else links.other_dp

    def compute_wo(which):
        dp = dp_of(which)
        weight_grad(rows_turned(heads, wo_1, dp), all_low, wo_1, dp)
        wo_sums.between_cores(which)

    def compute_qkv(plane, which, columns):
        weight_grad(
            turned_normed.at[which], grad_qkv.at[:, columns], plane.parts, dp_of(which)
        )
        plane.between_cores(which)

    q_columns, kv_columns = pl.ds(0, q_end), pl.ds(q_end, grad_qkv.shape[1] - q_end)
    heads_back(0)
    back(0, 0)
    output_half.sum.tick(1)
    for head in range(1, kv_heads):
        back(0, head)
    core_copies = core_sums(0)
    heads_back(1)
    down.second_way()
    for which in range(2):
        turned_normed[which] = rows_turned(normed, q_1, dp_of(which))
    back(1, 0)
    across = across_sums(0, core_copies)
    for tick in later:
        output_half.sum.tick(tick)
    for head in range(1, kv_heads):
        back(1, head)
    core_copies = core_sums(1)
    own_keys(0, across)
    across = across_sums(1, core_copies)
    normed_parts(0)
    compute_qkv(q_sums, 0, q_columns)
    compute_qkv(q_sums, 1, q_columns)
    own_keys(1, across)
    small_total[0] = gain_terms[...]
    pending = links.to(small_total.at[0], small_in.at[links.n_blk], links.core_way)
    q_sums.across_chips()
    normed_parts(1)
    sums[0].tick(1)
    compute_qkv(kv_sums, 0, kv_columns)
    compute_qkv(kv_sums, 1, kv_columns)
    for tick in later:
        sums[0].tick(tick)
    pending.arrived()
    small_total[1] = small_total[0] + small_in[links.n_blk]
    pending = links.to(small_total.at[1], small_in.at[links.n_blk + 1], links.x_way)
    kv_sums.across_chips()
    q_sums.second_way()
    compute_wo(0)
    compute_wo(1)
    pending.arrived()
    small_total[2] = small_total[1] + small_in[links.n_blk + 1]
    pending = links.to(small_total.at[2], small_in.at[links.n_blk + 2], links.y_way)
    sums[1].tick(1)
    kv_sums.second_way()
    wo_sums.across_chips()

    def into(target):
        def write(block, rows, values):
            target[block, rows, :] = values.astype(target.dtype)

        return write

    def give_home(plane, columns):
        here, there = summed.at[:, :, columns], grad_w_qkv.at[links.blk, :, columns]
        plane.result(into(here))
        keep.append(links.local(here.at[links.blk], there))
        return links.swap(lambda peer: [(here.at[peer], there)])

    swapped += give_home(q_sums, q_columns)
    for tick in later:
        sums[1].tick(tick)
    pending.arrived()
    small_in[links.blk] = small_total[2] + small_in[links.n_blk + 2]
    mine = small_in.at[links.blk]
    small_copies = [links.to(mine, mine, device) for device in links.peers()]
    swapped += give_home(kv_sums, kv_columns)
    output_half.write(output)

    def settle(seq):
        sums[seq].finish(grad_hidden.at[spans[seq]])

        def body(rows):
            at = pl.ds(pl.multiple_of(spans[seq].start + rows.start, ROWS), ROWS)
            back = back_rows(grad_hidden[at, :], hidden[at, :].astype(jnp.float32), gain[...])
            grad_hidden[at, :] = grad_middle[at, :] + back

        each_block(toks, body)

    settle(0)
    wo_sums.second_way()
    down.result(into(grad_down))
    settle(1)
    wo_sums.result(into(grad_wo))
    for copy in small_copies:
        copy.arrived()
    total = small_in[0]
    for blk in range(1, links.n_blk):
        total = total + small_in[blk]
    small_sum[...] = total
    for copy in swapped:
        copy.arrived()
    for copy in keep:
        copy.wait()
    for half in sums:
        half.sent()
    output_half.sum.sent()
    links.finish()


def backward(
    all_low,
    wo,
    queries,
    key_values,
    lse,
    qkv,
    q_gain,
    k_gain,
    cosine,
    sine,
    query_pos,
    key_pos,
    w_qkv,
    hidden,
    grad_middle,
    gain,
    normed,
    heads,
    out_parts,
    middle,
    grad_gate,
    grad_up,
    part_down,
):
    seqs, kv_heads, q_rows, _ = queries.shape
    n_uly, _, _, _, q_len, _ = key_values.shape
    n_blk, tokens, width = out_parts.shape
    n_dp, _, _, down_depth, _ = part_down.shape
    columns = qkv.shape[1]
    depth = width // (n_dp * n_blk * n_uly)
    out_depth = heads.shape[1] // (n_dp * n_uly)
    f32, low = jnp.float32, jnp.bfloat16
    small = (8, HEAD_SIZE)
    outs = [
        ((tokens, width), f32),
        ((1, out_depth, width), f32),
        ((1, down_depth, width), f32),
        (small, f32),
        ((tokens // 2, width), low),
        (grad_gate.shape, low),
        (grad_up.shape, low),
        ((n_blk, depth, columns), low),
    ]
    scratch = [
        (qkv.shape, low),
        (small, f32),
        ((q_len, heads.shape[1]), f32),
        (queries.shape, low),
        ((seqs, n_uly, 2, kv_heads, q_len, HEAD_SIZE), low),
        ((seqs, 2, 2, kv_heads, q_len, HEAD_SIZE), low),
        ((seqs, 2, kv_heads, q_len, HEAD_SIZE), low),
        (out_parts.shape, low),
        ((n_blk - 1, tokens, width), low),
        ((n_blk - 1, tokens, width), low),
        ((n_blk, depth, columns), low),
        ((n_blk + 3,) + small, f32),
        ((3,) + small, f32),
    ]
    down = [part_down.shape] + plane_shapes(n_dp, 1, n_uly, down_depth, width)[2:]
    return pl.pallas_call(
        backward_kernel,
        out_shape=[jax.ShapeDtypeStruct(shape, kind) for shape, kind in outs],
        in_specs=[VMEM] * 20 + [HBM] * 3,
        out_specs=[VMEM] * 5 + [HBM] * 3,
        scratch_shapes=[pltpu.VMEM(shape, kind) for shape, kind in scratch]
        + output_scratch(n_blk, tokens, width)
        + [pltpu.VMEM(shape, low) for shape in down]
        + [pltpu.VMEM((n_dp, width // n_dp, normed.shape[0]), low)]
        + plane_scratch(n_dp, n_blk, n_uly, depth, heads.shape[1])
        + plane_scratch(n_dp, n_blk, n_uly, depth, columns - heads.shape[1])
        + plane_scratch(n_dp, 1, n_uly, out_depth, width)
        + semaphores(128),
        compiler_params=kernel_params(4),
    )(
        all_low,
        wo,
        queries,
        key_values,
        lse,
        qkv,
        q_gain,
        k_gain,
        cosine,
        sine,
        query_pos,
        key_pos,
        w_qkv,
        hidden,
        grad_middle,
        gain,
        normed,
        heads,
        out_parts,
        middle,
        grad_gate,
        grad_up,
        part_down,
    )


def finish_kernel(
    gate,
    up,
    qkv,
    wo,
    wd,
    hidden,
    out_0,
    out_1,
    w_gate,
    w_up,
    w_query,
    key_weight,
    value_weight,
    attn_gain,
    mlp_gain,
    small,
    f_gate,
    f_up,
    f_q,
    f_k,
    f_v,
    f_wo,
    f_wd,
    f_hidden,
    f_out,
    f_attn,
    f_mlp,
    f_q_gain,
    f_k_gain,
):
    n_blk, depth, _ = gate.shape

    def place(source, offset, target):
        width = target.shape[1] // (n_blk * 2)
        for blk in range(n_blk):
            for group in range(2):
                to = (group * n_blk + blk) * width
                at = offset + group * width
                target[:, to : to + width] = source[blk, :, at : at + width].astype(jnp.float32)

    def gain_back(pairs, gain):
        total = jnp.zeros((depth, 128), jnp.float32)
        for weight, grad in pairs:
            for column in range(0, weight.shape[1], 128):
                at = slice(column, column + 128)
                total = total + weight[:, at].astype(jnp.float32) * grad[:, at]
        column = jnp.sum(total, axis=1, keepdims=True)
        square = (depth, depth)
        same = lax.broadcasted_iota(jnp.int32, square, 0) == lax.broadcasted_iota(
            jnp.int32, square, 1
        )
        return jnp.sum(jnp.where(same, column, 0.0), axis=0, keepdims=True) / gain[
            ...
        ].astype(jnp.float32)

    place(gate, 0, f_gate)
    place(up, 0, f_up)
    q_width = f_q.shape[1] // n_blk
    k_width = f_k.shape[1] // n_blk
    place(qkv, 0, f_q)
    place(qkv, q_width, f_k)
    place(qkv, q_width + k_width, f_v)
    f_q_gain[...] = small[0:1, :]
    f_k_gain[...] = small[1:2, :]
    f_wo[...] = wo[0]
    f_wd[...] = wd[0]
    f_hidden[...] = hidden[...]
    half = out_0.shape[0]
    f_out[:half, :] = out_0[...]
    f_out[half:, :] = out_1[...]
    f_attn[...] = gain_back(((w_query, f_q), (key_weight, f_k), (value_weight, f_v)), attn_gain)
    f_mlp[...] = gain_back(((w_gate, f_gate), (w_up, f_up)), mlp_gain)


def finish(gate, up, qkv, wo, wd, hidden, out_0, out_1, weights, gains, small):
    return pl.pallas_call(
        finish_kernel,
        out_shape=[jax.ShapeDtypeStruct(w.shape, jnp.float32) for w in weights]
        + [
            jax.ShapeDtypeStruct(wo.shape[1:], jnp.float32),
            jax.ShapeDtypeStruct(wd.shape[1:], jnp.float32),
            jax.ShapeDtypeStruct(hidden.shape, jnp.float32),
            jax.ShapeDtypeStruct(hidden.shape, jnp.bfloat16),
        ]
        + [jax.ShapeDtypeStruct(gain.shape, jnp.float32) for gain in gains]
        + [jax.ShapeDtypeStruct((1, small.shape[1]), jnp.float32)] * 2,
        in_specs=[VMEM] * 16,
        out_specs=[VMEM] * 13,
        compiler_params=pltpu.CompilerParams(vmem_limit_bytes=62 * MIB),
    )(gate, up, qkv, wo, wd, hidden, out_0, out_1, *weights, *gains, small)


def product(left, right):
    return jnp.dot(left, right, preferred_element_type=jnp.float32)


def shards(
    hidden,
    span_order,
    attn_gain,
    w_query,
    key_weight,
    value_weight,
    w_out,
    q_gain,
    k_gain,
    mlp_gain,
    w_gate,
    w_up,
    w_down,
    cotangent,
):
    seqs, toks, width = hidden.shape
    n_dp, n_blk, n_uly = (lax.axis_size(a) for a in EVERY)
    rows = n_blk * seqs * toks
    bf16 = jnp.bfloat16
    own_hidden = hidden.reshape(seqs * toks, width)
    own_cotangent = cotangent.reshape(seqs * toks, width)

    gain_q, gain_k = q_gain[None, :], k_gain[None, :]
    gain_rows = attn_gain.shape[0]
    own_gains = jnp.pad(jnp.stack([attn_gain, mlp_gain]), ((0, 30), (0, 128 - gain_rows)))
    (
        w_qkv,
        wo,
        all_wg,
        all_wu,
        all_wd,
        cot,
        g_attn,
        g_mlp,
        cosine,
        sine,
        query_pos,
        key_pos,
        heads_flat,
        normed,
        qkv,
        queries,
        key_values,
        lse,
        middle,
        normed2,
    ) = forward(
        span_order,
        own_hidden,
        w_query,
        key_weight,
        value_weight,
        w_out,
        w_gate,
        w_up,
        w_down,
        own_cotangent,
        own_gains,
        gain_q,
        gain_k,
        seqs,
        gain_rows,
    )
    w_qkv = w_qkv.reshape(width, -1)
    wo = wo.reshape(-1, width)
    wg, wu = all_wg.reshape(width, -1), all_wu.reshape(width, -1)
    wd = all_wd.reshape(-1, width)
    cot = cot.reshape(rows, width)
    normed2 = normed2.reshape(rows, width)
    gate_pre = product(normed2, wg)
    up_pre = product(normed2, wu)
    sigmoid_gate = jax.nn.sigmoid(gate_pre)
    activated = (gate_pre * sigmoid_gate * up_pre).astype(bf16)
    out_parts = product(activated, wd).astype(bf16)
    grad_act = product_right(cot, wd)
    grad_gate_pre = (
        grad_act * up_pre * sigmoid_gate * (1.0 + gate_pre * (1.0 - sigmoid_gate))
    ).astype(bf16)
    grad_up_pre = (grad_act * gate_pre * sigmoid_gate).astype(bf16)
    grad_parts = (product_right(grad_gate_pre, wg) + product_right(grad_up_pre, wu)).astype(bf16)
    blocks = (n_blk, seqs * toks, width)
    out_parts = out_parts.reshape(blocks)
    output_0, grad_middle, middle_low, grad_gate, grad_up, part_down = exchange_back(
        grad_parts.reshape(blocks),
        out_parts,
        middle,
        own_cotangent,
        g_mlp,
        normed2,
        grad_gate_pre,
        grad_up_pre,
        activated,
        cot,
    )
    middle_low = middle_low.reshape(rows, width)
    (
        grad_hidden,
        grad_out,
        grad_down,
        small,
        output_1,
        grad_gate,
        grad_up,
        grad_w_qkv,
    ) = backward(
        middle_low,
        wo,
        queries,
        key_values,
        lse,
        qkv,
        gain_q,
        gain_k,
        cosine,
        sine,
        query_pos,
        key_pos,
        w_qkv,
        own_hidden,
        grad_middle,
        g_attn,
        normed,
        heads_flat,
        out_parts,
        middle,
        grad_gate,
        grad_up,
        part_down,
    )
    (
        grad_gate,
        grad_up,
        grad_query,
        grad_key,
        grad_value,
        grad_out,
        grad_down,
        grad_hidden,
        output,
        grad_attn_gain,
        grad_mlp_gain,
        grad_q_gain,
        grad_k_gain,
    ) = finish(
        grad_gate,
        grad_up,
        grad_w_qkv,
        grad_out,
        grad_down,
        grad_hidden,
        output_0,
        output_1,
        (w_gate, w_up, w_query, key_weight, value_weight),
        [g[None, :] for g in (attn_gain, mlp_gain)],
        small,
    )
    return (
        output.reshape(hidden.shape),
        grad_hidden.reshape(hidden.shape),
        grad_attn_gain.reshape(gain_rows),
        grad_query,
        grad_key,
        grad_value,
        grad_out,
        grad_q_gain[0],
        grad_k_gain[0],
        grad_mlp_gain.reshape(gain_rows),
        grad_gate,
        grad_up,
        grad_down,
    )


def solution(mesh):
    n_dp, n_blk, n_uly = (mesh.shape[a] for a in EVERY)
    aligned = (n_dp, n_uly) == (2, 4) and KEY_VALUE_HEADS % (n_dp * n_blk) == 0
    in_specs = (
        TOKENS,
        P(),
        P(EVERY),
        P(EVERY, None),
        P(EVERY, None),
        P(EVERY, None),
        P(EVERY, None),
        P(),
        P(),
        P(EVERY),
        P(EVERY, None),
        P(EVERY, None),
        P(EVERY, None),
        TOKENS,
    )
    out_specs = (
        TOKENS,
        TOKENS,
        P(EVERY),
        P(EVERY, None),
        P(EVERY, None),
        P(EVERY, None),
        P(EVERY, None),
        P(),
        P(),
        P(EVERY),
        P(EVERY, None),
        P(EVERY, None),
        P(EVERY, None),
    )
    return jax.shard_map(
        shards if aligned else shards_general,
        mesh=mesh, in_specs=in_specs, out_specs=out_specs, check_vma=False)
```

```python
import functools
import math

import jax
import jax.numpy as jnp
from jax import lax
from jax.experimental import pallas as pl
from jax.experimental.pallas import tpu as pltpu
from jax.sharding import PartitionSpec as P

QUERY_HEADS = 16
KEY_VALUE_HEADS = 8
HEAD_SIZE = 128


DP, BLK, ULY = "dp", "blk", "uly"
EVERY = (DP, BLK, ULY)
PLANE = (DP, ULY)
TOKENS = P(DP, (BLK, ULY), None)
EQ_KGQD_NKD_TO_KGQN = "kgqd,nkd->kgqn"
EQ_KGQN_KGQD_TO_NKD = "kgqn,kgqd->nkd"
EQ_KGQN_NKD_TO_KGQD = "kgqn,nkd->kgqd"
EQ_KGQN_QKGD_TO_NKD = "kgqn,qkgd->nkd"
EQ_QKGD_NKD_TO_KGQN = "qkgd,nkd->kgqn"
EQ_STD_DE_TO_STE = "std,de->ste"
EQ_STD_DF_TO_STF = "std,df->stf"
EQ_STD_ED_TO_STE = "std,ed->ste"
EQ_STD_FD_TO_STF = "std,fd->stf"
EQ_STD_STE_TO_DE = "std,ste->de"
EQ_STD_STF_TO_DF = "std,stf->df"
EQ_STE_DE_TO_STD = "ste,de->std"
EQ_STE_ED_TO_STD = "ste,ed->std"
EQ_STE_STD_TO_ED = "ste,std->ed"
EQ_STF_DF_TO_STD = "stf,df->std"
EQ_STF_FD_TO_STD = "stf,fd->std"
EQ_STF_STD_TO_FD = "stf,std->fd"

EPSILON = 1e-06
ROPE_BASE = 1000000.0


def rms_scale(source):
    return lax.rsqrt(jnp.mean(source * source, axis=-1, keepdims=True) + EPSILON)


def norm_back(grad_normed, source, norm_scale, gain):
    unit_rows = source * norm_scale
    scaled = grad_normed * gain
    return norm_scale * (scaled - unit_rows * jnp.mean(scaled * unit_rows, axis=-1, keepdims=True))


def angles_of(positions, head_dim):
    freq_steps = jnp.arange(head_dim // 2, dtype=jnp.float32)
    inverse = jnp.exp(freq_steps * (-2.0 * math.log(ROPE_BASE) / head_dim))
    return positions.astype(jnp.float32)[:, None] * inverse[None, :]


def rotate(source, angles, direction):
    half_dim = source.shape[-1] // 2
    cosine = jnp.cos(angles)[:, None, :]
    sine_part = direction * jnp.sin(angles)[:, None, :]
    first_half = source[..., :half_dim]
    second_half = source[..., half_dim:]
    return jnp.concatenate(
        [
            first_half * cosine - second_half * sine_part,
            second_half * cosine + first_half * sine_part,
        ],
        axis=-1,
    )


def positions_of(places, span_order, half_len):
    blocks_of = places // half_len
    block_ids = jnp.arange(span_order.shape[0], dtype=jnp.int32)
    chosen = jnp.sum(
        jnp.where(blocks_of[:, None] == block_ids[None, :], span_order[None, :], 0), axis=1
    )
    return chosen * half_len + places % half_len


def add_rows(buffer, new_rows):
    return buffer + new_rows


def shards_general(
    hidden,
    span_order,
    attn_gain,
    w_query,
    key_weight,
    value_weight,
    w_out,
    q_gain,
    k_gain,
    mlp_gain,
    w_gate,
    w_up,
    w_down,
    cotangent,
):
    sequence_count = hidden.shape[0]
    token_count = hidden.shape[1]
    ulysses_group_size = lax.axis_size(ULY)
    local_q = QUERY_HEADS // ulysses_group_size
    local_key_value = KEY_VALUE_HEADS // ulysses_group_size
    query_group_width = QUERY_HEADS // KEY_VALUE_HEADS
    block_len = token_count * ulysses_group_size
    half_len = block_len // 2
    score_scale = 1.0 / math.sqrt(HEAD_SIZE)
    blk_index = lax.axis_index(BLK)
    uly_index = lax.axis_index(ULY)
    first_place = (blk_index * ulysses_group_size + uly_index) * token_count
    local_angles = angles_of(
        positions_of(first_place + jnp.arange(token_count, dtype=jnp.int32), span_order, half_len),
        HEAD_SIZE,
    )
    query_pos = positions_of(
        blk_index * block_len + jnp.arange(block_len, dtype=jnp.int32), span_order, half_len
    )
    g_attn, wq_all, wk_all, wv_all, wo_all = (
        lax.all_gather(attn_gain, EVERY, axis=0, tiled=True),
        lax.all_gather(w_query, EVERY, axis=0, tiled=True),
        lax.all_gather(key_weight, EVERY, axis=0, tiled=True),
        lax.all_gather(value_weight, EVERY, axis=0, tiled=True),
        lax.all_gather(w_out, EVERY, axis=0, tiled=True),
    )
    source = hidden.astype(jnp.float32)
    first_scale = rms_scale(source)
    normalized_input = (source * first_scale * g_attn.astype(jnp.float32)).astype(jnp.bfloat16)
    q_pre = jnp.einsum(
        EQ_STD_DE_TO_STE, normalized_input, wq_all, preferred_element_type=jnp.float32
    ).reshape(sequence_count, token_count, QUERY_HEADS, HEAD_SIZE)
    key_before_norm = jnp.einsum(
        EQ_STD_DE_TO_STE, normalized_input, wk_all, preferred_element_type=jnp.float32
    ).reshape(sequence_count, token_count, KEY_VALUE_HEADS, HEAD_SIZE)
    value_before_norm = jnp.einsum(
        EQ_STD_DE_TO_STE, normalized_input, wv_all, preferred_element_type=jnp.float32
    ).reshape(sequence_count, token_count, KEY_VALUE_HEADS, HEAD_SIZE)
    q_scale = rms_scale(q_pre)
    k_scale = rms_scale(key_before_norm)
    gain_q = q_gain.astype(jnp.float32)
    gain_k = k_gain.astype(jnp.float32)
    q_rot = rotate(q_pre * q_scale * gain_q, local_angles, 1.0).astype(jnp.bfloat16)
    k_rot = rotate(key_before_norm * k_scale * gain_k, local_angles, 1.0).astype(jnp.bfloat16)
    v_low = value_before_norm.astype(jnp.bfloat16)
    q_heads, k_heads, v_heads = (
        lax.all_to_all(q_rot, ULY, split_axis=2, concat_axis=1, tiled=True),
        lax.all_to_all(k_rot, ULY, split_axis=2, concat_axis=1, tiled=True),
        lax.all_to_all(v_low, ULY, split_axis=2, concat_axis=1, tiled=True),
    )
    q_group = q_heads.reshape(
        sequence_count, block_len, local_key_value, query_group_width, HEAD_SIZE
    )
    stat_shape = (sequence_count, local_key_value, query_group_width, block_len)
    start_state = (
        jnp.full(stat_shape, -1e30, jnp.float32),
        jnp.zeros(stat_shape, jnp.float32),
        jnp.zeros(stat_shape + (HEAD_SIZE,), jnp.float32),
    )
    key_piece = lax.all_gather(k_heads, BLK, axis=1, tiled=True)
    value_piece = lax.all_gather(v_heads, BLK, axis=1, tiled=True)
    key_pos = positions_of(jnp.arange(key_piece.shape[1], dtype=jnp.int32), span_order, half_len)
    allowed = query_pos[:, None] >= key_pos[None, :]

    def attend_one_sequence(members):
        query_rows, key_rows, value_rows, top_seq, total_seq, accum_seq = members
        scores = (
            jnp.einsum(EQ_QKGD_NKD_TO_KGQN, query_rows, key_rows, preferred_element_type=jnp.float32)
            * score_scale
        )
        scores = jnp.where(allowed, scores, -jnp.inf)
        new_top = jnp.maximum(top_seq, jnp.max(scores, axis=-1))
        fading = jnp.exp(top_seq - new_top)
        weights = jnp.exp(scores - new_top[..., None])
        total_seq = total_seq * fading + jnp.sum(weights, axis=-1)
        accum_seq = accum_seq * fading[..., None] + jnp.einsum(
            EQ_KGQN_NKD_TO_KGQD,
            weights.astype(jnp.bfloat16),
            value_rows,
            preferred_element_type=jnp.float32,
        )
        return (new_top, total_seq, accum_seq)

    row_top, row_total, accum = lax.map(
        attend_one_sequence,
        (q_group, key_piece, value_piece, start_state[0], start_state[1], start_state[2]),
    )
    log_total = row_top + jnp.log(row_total)
    attention_output = jnp.transpose(accum / row_total[..., None], (0, 3, 1, 2, 4)).reshape(
        sequence_count, block_len, local_q, HEAD_SIZE
    )
    heads_seq = lax.all_to_all(
        attention_output.astype(jnp.bfloat16), ULY, split_axis=1, concat_axis=2, tiled=True
    )
    heads_flat = heads_seq.reshape(sequence_count, token_count, QUERY_HEADS * HEAD_SIZE)
    middle = source + jnp.einsum(
        EQ_STE_ED_TO_STD, heads_flat, wo_all, preferred_element_type=jnp.float32
    )
    g_mlp, wg_all, wu_all, wd_all = (
        lax.all_gather(mlp_gain, EVERY, axis=0, tiled=True),
        lax.all_gather(w_gate, EVERY, axis=0, tiled=True),
        lax.all_gather(w_up, EVERY, axis=0, tiled=True),
        lax.all_gather(w_down, EVERY, axis=0, tiled=True),
    )
    second_scale = rms_scale(middle)
    gain_mlp = g_mlp.astype(jnp.float32)
    normed2 = (middle * second_scale * gain_mlp).astype(jnp.bfloat16)
    gate_pre = jnp.einsum(EQ_STD_DF_TO_STF, normed2, wg_all, preferred_element_type=jnp.float32)
    up_pre = jnp.einsum(EQ_STD_DF_TO_STF, normed2, wu_all, preferred_element_type=jnp.float32)
    sigmoid_gate = jax.nn.sigmoid(gate_pre)
    activated = (gate_pre * sigmoid_gate * up_pre).astype(jnp.bfloat16)
    result = middle + jnp.einsum(
        EQ_STF_FD_TO_STD, activated, wd_all, preferred_element_type=jnp.float32
    )
    output = result.astype(jnp.bfloat16)
    g_mlp, wg_all, wu_all, wd_all = (
        lax.all_gather(mlp_gain, EVERY, axis=0, tiled=True),
        lax.all_gather(w_gate, EVERY, axis=0, tiled=True),
        lax.all_gather(w_up, EVERY, axis=0, tiled=True),
        lax.all_gather(w_down, EVERY, axis=0, tiled=True),
    )
    gain_mlp = g_mlp.astype(jnp.float32)
    grad_act = jnp.einsum(EQ_STD_FD_TO_STF, cotangent, wd_all, preferred_element_type=jnp.float32)
    grad_gate_pre = (
        grad_act * up_pre * sigmoid_gate * (1.0 + gate_pre * (1.0 - sigmoid_gate))
    ).astype(jnp.bfloat16)
    grad_up_pre = (grad_act * gate_pre * sigmoid_gate).astype(jnp.bfloat16)
    grad_gate = jnp.einsum(
        EQ_STD_STF_TO_DF, normed2, grad_gate_pre, preferred_element_type=jnp.float32
    )
    grad_up = jnp.einsum(EQ_STD_STF_TO_DF, normed2, grad_up_pre, preferred_element_type=jnp.float32)
    grad_normed2 = jnp.einsum(
        EQ_STF_DF_TO_STD, grad_gate_pre, wg_all, preferred_element_type=jnp.float32
    ) + jnp.einsum(EQ_STF_DF_TO_STD, grad_up_pre, wu_all, preferred_element_type=jnp.float32)
    mlp_gain_term = jnp.sum(grad_normed2 * middle * second_scale, axis=(0, 1))
    grad_middle = cotangent.astype(jnp.float32) + norm_back(
        grad_normed2, middle, second_scale, gain_mlp
    )
    grad_mlp_gain, grad_gate, grad_up = (
        lax.psum_scatter(mlp_gain_term, EVERY, scatter_dimension=0, tiled=True),
        lax.psum_scatter(grad_gate, EVERY, scatter_dimension=0, tiled=True),
        lax.psum_scatter(grad_up, EVERY, scatter_dimension=0, tiled=True),
    )
    g_attn, wq_all, wk_all, wv_all, wo_all = (
        lax.all_gather(attn_gain, EVERY, axis=0, tiled=True),
        lax.all_gather(w_query, EVERY, axis=0, tiled=True),
        lax.all_gather(key_weight, EVERY, axis=0, tiled=True),
        lax.all_gather(value_weight, EVERY, axis=0, tiled=True),
        lax.all_gather(w_out, EVERY, axis=0, tiled=True),
    )
    middle_low = grad_middle.astype(jnp.bfloat16)
    grad_out = jnp.einsum(EQ_STE_STD_TO_ED, heads_flat, middle_low, preferred_element_type=jnp.float32)
    grad_heads = (
        jnp.einsum(EQ_STD_ED_TO_STE, middle_low, wo_all, preferred_element_type=jnp.float32)
        .astype(jnp.bfloat16)
        .reshape(sequence_count, token_count, QUERY_HEADS, HEAD_SIZE)
    )
    grad_heads_local = lax.all_to_all(grad_heads, ULY, split_axis=2, concat_axis=1, tiled=True)
    grad_group = jnp.transpose(
        grad_heads_local.reshape(
            sequence_count, block_len, local_key_value, query_group_width, HEAD_SIZE
        ),
        (0, 2, 3, 1, 4),
    )
    delta = jnp.sum(grad_heads_local.astype(jnp.float32) * attention_output, axis=-1)
    delta = jnp.transpose(
        delta.reshape(sequence_count, block_len, local_key_value, query_group_width), (0, 2, 3, 1)
    )
    seq_length = block_len * lax.axis_size(BLK)
    zero_keys = jnp.zeros((sequence_count, seq_length, local_key_value, HEAD_SIZE), jnp.float32)
    back_state = (jnp.zeros(stat_shape + (HEAD_SIZE,), jnp.float32), zero_keys, zero_keys)
    key_piece = lax.all_gather(k_heads, BLK, axis=1, tiled=True)
    value_piece = lax.all_gather(v_heads, BLK, axis=1, tiled=True)
    key_pos = positions_of(jnp.arange(key_piece.shape[1], dtype=jnp.int32), span_order, half_len)
    back_allowed = query_pos[:, None] >= key_pos[None, :]

    def back_one_sequence(members):
        query_rows, grad_rows, lse_seq, delta_seq, key_rows, value_rows, dq_seq, dk_seq, dv_seq = (
            members
        )
        scores = (
            jnp.einsum(EQ_QKGD_NKD_TO_KGQN, query_rows, key_rows, preferred_element_type=jnp.float32)
            * score_scale
        )
        scores = jnp.where(back_allowed, scores, -jnp.inf)
        probs = jnp.exp(scores - lse_seq[..., None])
        grad_values = jnp.einsum(
            EQ_KGQN_KGQD_TO_NKD,
            probs.astype(jnp.bfloat16),
            grad_rows,
            preferred_element_type=jnp.float32,
        )
        grad_probs = jnp.einsum(
            EQ_KGQD_NKD_TO_KGQN, grad_rows, value_rows, preferred_element_type=jnp.float32
        )
        grad_scores = (probs * (grad_probs - delta_seq[..., None])).astype(jnp.bfloat16)
        dq_seq = dq_seq + score_scale * jnp.einsum(
            EQ_KGQN_NKD_TO_KGQD, grad_scores, key_rows, preferred_element_type=jnp.float32
        )
        grad_keys = score_scale * jnp.einsum(
            EQ_KGQN_QKGD_TO_NKD, grad_scores, query_rows, preferred_element_type=jnp.float32
        )
        return (dq_seq, add_rows(dk_seq, grad_keys), add_rows(dv_seq, grad_values))

    grad_q_group, grad_k_whole, grad_v_whole = lax.map(
        back_one_sequence,
        (
            q_group,
            grad_group,
            log_total,
            delta,
            key_piece,
            value_piece,
            back_state[0],
            back_state[1],
            back_state[2],
        ),
    )
    grad_k_block, grad_v_block = (
        lax.psum_scatter(
            grad_k_whole.astype(jnp.bfloat16), BLK, scatter_dimension=1, tiled=True
        ).astype(jnp.float32),
        lax.psum_scatter(
            grad_v_whole.astype(jnp.bfloat16), BLK, scatter_dimension=1, tiled=True
        ).astype(jnp.float32),
    )
    grad_q_block = jnp.transpose(grad_q_group, (0, 3, 1, 2, 4)).reshape(
        sequence_count, block_len, local_q, HEAD_SIZE
    )
    grad_q_seq, grad_k_seq, value_sequence_gradient = (
        lax.all_to_all(
            grad_q_block.astype(jnp.bfloat16), ULY, split_axis=1, concat_axis=2, tiled=True
        ).astype(grad_q_block.dtype),
        lax.all_to_all(
            grad_k_block.astype(jnp.bfloat16), ULY, split_axis=1, concat_axis=2, tiled=True
        ).astype(grad_k_block.dtype),
        lax.all_to_all(
            grad_v_block.astype(jnp.bfloat16), ULY, split_axis=1, concat_axis=2, tiled=True
        ).astype(grad_v_block.dtype),
    )
    grad_q_normed = rotate(grad_q_seq, local_angles, -1.0)
    grad_k_normed = rotate(grad_k_seq, local_angles, -1.0)
    q_gain_term = jnp.sum(grad_q_normed * q_pre * q_scale, axis=(0, 1, 2))
    k_gain_term = jnp.sum(grad_k_normed * key_before_norm * k_scale, axis=(0, 1, 2))
    grad_q_pre = (
        norm_back(grad_q_normed, q_pre, q_scale, gain_q)
        .astype(jnp.bfloat16)
        .reshape(sequence_count, token_count, QUERY_HEADS * HEAD_SIZE)
    )
    grad_k_pre = (
        norm_back(grad_k_normed, key_before_norm, k_scale, gain_k)
        .astype(jnp.bfloat16)
        .reshape(sequence_count, token_count, KEY_VALUE_HEADS * HEAD_SIZE)
    )
    value_pre_gradient = value_sequence_gradient.astype(jnp.bfloat16).reshape(
        sequence_count, token_count, KEY_VALUE_HEADS * HEAD_SIZE
    )
    grad_query = jnp.einsum(
        EQ_STD_STE_TO_DE, normalized_input, grad_q_pre, preferred_element_type=jnp.float32
    )
    grad_key = jnp.einsum(
        EQ_STD_STE_TO_DE, normalized_input, grad_k_pre, preferred_element_type=jnp.float32
    )
    grad_value = jnp.einsum(
        EQ_STD_STE_TO_DE, normalized_input, value_pre_gradient, preferred_element_type=jnp.float32
    )
    grad_normed = jnp.einsum(EQ_STE_DE_TO_STD, grad_q_pre, wq_all, preferred_element_type=jnp.float32)
    grad_normed = grad_normed + jnp.einsum(
        EQ_STE_DE_TO_STD, grad_k_pre, wk_all, preferred_element_type=jnp.float32
    )
    grad_normed = grad_normed + jnp.einsum(
        EQ_STE_DE_TO_STD, value_pre_gradient, wv_all, preferred_element_type=jnp.float32
    )
    attn_gain_term = jnp.sum(grad_normed * source * first_scale, axis=(0, 1))
    grad_hidden = grad_middle + norm_back(
        grad_normed, source, first_scale, g_attn.astype(jnp.float32)
    )
    grad_down = jnp.einsum(EQ_STF_STD_TO_FD, activated, cotangent, preferred_element_type=jnp.float32)
    grad_attn_gain, grad_query, grad_key, grad_value, grad_out, grad_down = (
        lax.psum_scatter(attn_gain_term, EVERY, scatter_dimension=0, tiled=True),
        lax.psum_scatter(grad_query, EVERY, scatter_dimension=0, tiled=True),
        lax.psum_scatter(grad_key, EVERY, scatter_dimension=0, tiled=True),
        lax.psum_scatter(grad_value, EVERY, scatter_dimension=0, tiled=True),
        lax.psum_scatter(grad_out, EVERY, scatter_dimension=0, tiled=True),
        lax.psum_scatter(grad_down, EVERY, scatter_dimension=0, tiled=True),
    )
    grad_q_gain, grad_k_gain = lax.psum((q_gain_term, k_gain_term), EVERY)
    return (
        output,
        grad_hidden,
        grad_attn_gain,
        grad_query,
        grad_key,
        grad_value,
        grad_out,
        grad_q_gain,
        grad_k_gain,
        grad_mlp_gain,
        grad_gate,
        grad_up,
        grad_down,
    )


MESH = pl.DeviceIdType.MESH
HBM = pl.BlockSpec(memory_space=pltpu.HBM)
VMEM = pl.BlockSpec(memory_space=pltpu.VMEM)
MIB = 1 << 20


def kernel_params(collective_id, vmem_mib=62):
    return pltpu.CompilerParams(
        collective_id=collective_id, has_side_effects=True, vmem_limit_bytes=vmem_mib * MIB
    )


def semaphores(count, local=16):
    return [
        pltpu.SemaphoreType.DMA((count,)),
        pltpu.SemaphoreType.DMA((count,)),
        pltpu.SemaphoreType.DMA((local,)),
    ]


class Copy:
    def __init__(self, descriptor, sends, receives):
        self.descriptor, self.sends, self.receives = descriptor, sends, receives

    def under(self, condition, action):
        if condition is None:
            action()
        else:
            pl.when(condition)(action)

    def start(self):
        self.under(self.sends, lambda: self.descriptor().start())
        return self

    def sent(self):
        self.under(self.sends, lambda: self.descriptor().wait_send())

    def arrived(self):
        self.under(self.receives, lambda: self.descriptor().wait_recv())


class Links:
    def __init__(self, send, recv, here):
        self.send, self.recv, self.here = send, recv, here
        self.used, self.used_here = 0, 0
        self.copies, self.local_copies = [], []
        self.n_dp, self.n_blk, self.n_uly = (lax.axis_size(a) for a in EVERY)
        self.dp, self.blk, self.uly = (lax.axis_index(a) for a in EVERY)
        self.other_dp = 1 - self.dp
        self.across = lax.rem(self.uly + 2, 4)
        self.twin = self.uly + 1 - 2 * lax.rem(self.uly, 2)
        self.x_way = (self.other_dp, self.blk, self.uly)
        self.y_way = (self.dp, self.blk, self.across)
        self.core_way = (self.dp, self.blk, self.twin)

    def peer(self, step):
        return lax.rem(self.blk + step, self.n_blk)

    def peers(self):
        return [(self.dp, self.peer(k), self.uly) for k in range(1, self.n_blk)]

    def far_first(self):
        last = self.n_blk - 1
        orders = [
            sorted((p for p in range(self.n_blk) if p != b), key=lambda p, b=b: -abs(p - b))
            for b in range(self.n_blk)
        ]
        for b, order in enumerate(orders):
            ways = [[p for p in order if p > b], [p for p in order if p < b]]
            ways.sort(key=lambda way: -len(way))
            merged = []
            while ways[0] or ways[1]:
                for way in ways:
                    if way:
                        merged.append(way.pop(0))
            orders[b] = merged
        peers = []
        for turn in range(last):
            peer = jnp.int32(0)
            for b, order in enumerate(orders):
                peer = jnp.where(self.blk == b, order[turn], peer)
            peers.append(peer)
        return peers

    def swap(self, pieces_for):
        base, count = self.used, 0
        for peer in self.far_first():
            pieces = pieces_for(peer)
            count = len(pieces)
            distance = lax.rem(peer - self.blk + self.n_blk, self.n_blk) - 1
            for number, (source, target) in enumerate(pieces):
                self.swap_copy(base + distance * count + number, source, target, peer).start()
        self.used = base + (self.n_blk - 1) * count
        waits = []
        for slot in range(base, self.used):
            source, target = pieces_for(self.blk)[(slot - base) % count]

            def descriptor(slot=slot, source=source, target=target):
                return self.swap_copy(slot, source, target, self.peer(1))

            copy = Copy(descriptor, None, None)
            self.copies.append(copy)
            waits.append(copy)
        return waits

    def swap_copy(self, slot, source, target, peer):
        return pltpu.make_async_remote_copy(
            src_ref=source,
            dst_ref=target,
            send_sem=self.send.at[slot],
            recv_sem=self.recv.at[slot],
            device_id=(self.dp, peer, self.uly),
            device_id_type=MESH,
        )

    def greet(self, devices):
        barrier = pltpu.get_barrier_semaphore()
        for device in devices:
            pl.semaphore_signal(barrier, inc=1, device_id=device, device_id_type=MESH)
        pl.semaphore_wait(barrier, len(devices))

    def remote(self, source, target, device, sends=None, receives=None):
        slot = self.used
        self.used += 1

        def descriptor():
            return pltpu.make_async_remote_copy(
                src_ref=source(),
                dst_ref=target(),
                send_sem=self.send.at[slot],
                recv_sem=self.recv.at[slot],
                device_id=device,
                device_id_type=MESH,
            )

        copy = Copy(descriptor, sends, receives)
        self.copies.append(copy)
        return copy.start()

    def to(self, source, target, device):
        return self.remote(lambda: source, lambda: target, device)

    def local(self, source, target):
        copy = pltpu.make_async_copy(source, target, self.here.at[self.used_here])
        self.used_here += 1
        copy.start()
        self.local_copies.append(copy)
        return copy

    def finish(self):
        for copy in self.copies:
            copy.sent()


class LineGather:
    def __init__(self, links, own, whole):
        self.links, self.own, self.whole = links, own, whole
        self.waiting = []

    def send(self, step):
        links, whole = self.links, self.whole
        blk, last = links.blk, links.n_blk - 1

        def block(index):
            if step == 0:
                return lambda: self.own
            return lambda: whole.at[index]

        self.waiting = [
            links.remote(
                block(blk - step),
                lambda: whole.at[blk - step],
                (links.dp, blk + 1, links.uly),
                jnp.logical_and(blk >= step, blk < last),
                blk >= step + 1,
            ),
            links.remote(
                block(blk + step),
                lambda: whole.at[blk + step],
                (links.dp, blk - 1, links.uly),
                jnp.logical_and(blk + step <= last, blk > 0),
                blk + step + 1 <= last,
            ),
        ]

    def arrived(self):
        for copy in self.waiting:
            copy.arrived()


def halves(tokens):
    return [pl.ds(0, tokens // 2), pl.ds(tokens // 2, tokens // 2)]


def advance(line, step):
    line.arrived()
    line.send(step)


class HalvedLine:
    def __init__(self, links, own, whole):
        self.lines = [
            LineGather(links, None if own is None else own.at[rows], whole.at[:, rows])
            for rows in halves(whole.shape[1])
        ]

    def send(self, step):
        for line in self.lines:
            line.send(step)

    def advance(self, step):
        for line in self.lines:
            line.arrived()
            line.send(step)

    def arrived(self):
        for line in self.lines:
            line.arrived()


class PlaneGather:
    def __init__(self, links, at):
        self.links, self.at = links, at

    def start_x(self, own):
        links = self.links
        mine = self.at(links.dp, links.uly)
        self.from_x = links.to(own, mine, links.x_way)
        self.from_core = [links.to(own, mine, links.core_way)]

    def start_y(self, own):
        links = self.links
        self.from_y = links.to(own, self.at(links.dp, links.uly), links.y_way)

    def start(self, own=None):
        own = self.at(self.links.dp, self.links.uly) if own is None else own
        self.start_x(own)
        self.start_y(own)

    def hand_on(self):
        links, at = self.links, self.at
        self.from_x.arrived()
        half = at(links.other_dp, links.uly, 0)
        self.second_y = links.to(half, half, links.y_way)
        self.from_y.arrived()
        half = at(links.dp, links.across, 1)
        self.second_x = links.to(half, half, links.x_way)
        for chunk in (at(links.other_dp, links.uly), at(links.dp, links.across)):
            self.from_core.append(links.to(chunk, chunk, links.core_way))

    def last(self):
        links = self.links
        self.second_y.arrived()
        self.second_x.arrived()
        chunk = self.at(links.other_dp, links.across)
        self.from_core.append(links.to(chunk, chunk, links.core_way))

    def arrived(self):
        for copy in self.from_core:
            copy.arrived()


def rows_of(whole, blocked):
    def at(dp, uly, half=None):
        part = whole.at[dp, :, uly] if blocked else whole.at[dp, uly]
        if half is None:
            return part
        depth = whole.shape[-2] // 2
        rows = pl.ds(half * depth, depth)
        return part.at[:, rows] if blocked else part.at[rows]

    return at


class ColumnSwap:
    def __init__(self, links, pieces):
        self.links, self.pieces = links, pieces
        self.incoming, self.kept = [], []

    def parts(self, blk):
        links = self.links
        for weight, whole, offset in self.pieces:
            width = weight.shape[-1] // links.n_dp // links.n_blk
            for group in range(links.n_dp):
                start = (group * links.n_blk + blk) * width
                yield (
                    weight.at[:, pl.ds(pl.multiple_of(start, 128), width)],
                    whole.at[links.blk, :, pl.ds(offset + group * width, width)],
                )

    def start(self):
        links = self.links
        self.incoming = links.swap(lambda peer: list(self.parts(peer)))
        for source, target in self.parts(links.blk):
            self.kept.append(links.local(source, target))

    def arrived(self):
        for copy in self.kept:
            copy.wait()
        for copy in self.incoming:
            copy.arrived()


def write_positions(links, span_order, toks, cosine, sine, query_pos, key_pos):
    half_len = toks * links.n_uly // 2

    def first(blk, uly):
        chunk = span_order[2 * blk + lax.div(uly, links.n_uly // 2)]
        return chunk * half_len + lax.rem(uly, links.n_uly // 2) * toks

    lane = lax.broadcasted_iota(jnp.int32, (toks, HEAD_SIZE), 1)
    row = lax.broadcasted_iota(jnp.int32, (toks, HEAD_SIZE), 0)
    upper = lane >= HEAD_SIZE // 2
    step = jnp.where(upper, lane - HEAD_SIZE // 2, lane).astype(jnp.float32)
    inverse = jnp.exp(step * (-2.0 * math.log(ROPE_BASE) / HEAD_SIZE))
    for blk in range(links.n_blk):
        angles = (first(blk, links.uly) + row).astype(jnp.float32) * inverse
        at = slice(blk * toks, (blk + 1) * toks)
        cosine[at, :] = jnp.cos(angles)
        turn = jnp.sin(angles)
        sine[at, :] = jnp.where(upper, turn, -turn)
    lane = lax.broadcasted_iota(jnp.int32, query_pos.shape, 1)
    place = jnp.zeros(query_pos.shape, jnp.int32)
    for start in range(0, query_pos.shape[1], toks):
        blk = start // toks % links.n_blk
        here = jnp.logical_and(lane >= start, lane < start + toks)
        place = jnp.where(here, first(blk, links.uly) + lane - start, place)
    query_pos[...] = place
    row = lax.broadcasted_iota(jnp.int32, (toks, 1), 0)
    for uly in range(links.n_uly):
        for blk in range(links.n_blk):
            start = (uly * links.n_blk + blk) * toks
            key_pos[start : start + toks, :] = row + first(blk, jnp.int32(uly))


def write_gains(links, all_gains, size, targets):
    per_row = 128 // size
    for which, target in enumerate(targets):
        for place in range(target.shape[1] // 128):
            pieces = []
            for part in range(per_row):
                device = place * per_row + part
                plane, uly = device // links.n_uly, device % links.n_uly
                gains = all_gains[plane // links.n_blk, plane % links.n_blk, uly]
                pieces.append(gains.astype(jnp.float32)[which : which + 1, :size])
            target[:, place * 128 : (place + 1) * 128] = jnp.concatenate(pieces, axis=1)


ROWS = 32


def each_block(count, body):
    def step(index, carry):
        body(pl.ds(pl.multiple_of(index * ROWS, ROWS), ROWS))
        return carry

    lax.fori_loop(0, count // ROWS, step, 0)


class LineScatter:
    def __init__(self, links, parts, rightward, leftward):
        self.links, self.parts = links, parts
        self.slots = {1: rightward, -1: leftward}
        self.tokens = parts.shape[1]
        self.number = links.used
        self.last = links.n_blk - 1
        links.used += 2 * self.last

    def target(self, step, way):
        return self.last - step if way == 1 else step

    def slot(self, step, way):
        target = self.target(step, way)
        return self.slots[way].at[target - 1 if way == 1 else target]

    def place(self, way):
        return self.links.blk if way == 1 else self.last - self.links.blk

    def copy(self, step, way, source=None):
        links, slot = self.links, self.slot(step, way)
        number = self.number + 2 * step + (1 if way == 1 else 0)
        return pltpu.make_async_remote_copy(
            src_ref=slot if source is None else source,
            dst_ref=slot,
            send_sem=links.send.at[number],
            recv_sem=links.recv.at[number],
            device_id=(links.dp, links.blk + way, links.uly),
            device_id_type=MESH,
        )

    def start(self):
        for step in range(self.last):
            for way in (1, -1):

                @pl.when(self.place(way) == 0)
                def _(step=step, way=way):
                    self.copy(step, way, self.parts.at[self.target(step, way)]).start()

    def tick(self, tick):
        for way in (1, -1):

            @pl.when(jnp.logical_and(self.place(way) >= 1, self.place(way) <= tick))
            def _(way=way):
                step = tick - self.place(way)
                self.copy(step, way).wait_recv()
                slot, target = self.slot(step, way), self.target(step, way)

                def body(rows):
                    slot[rows, :] = slot[rows, :] + self.parts[target, rows, :]

                each_block(self.tokens, body)
                self.copy(step, way).start()

    def finish(self, total):
        blk, last = self.links.blk, self.last

        def start(rows):
            total[rows, :] = self.parts[blk, rows, :].astype(jnp.float32)

        each_block(self.tokens, start)
        for way in (1, -1):

            @pl.when(self.place(way) >= 1)
            def _(way=way):
                step = last - self.place(way)
                self.copy(step, way).wait_recv()
                slot = self.slot(step, way)

                def body(rows):
                    total[rows, :] = total[rows, :] + slot[rows, :].astype(jnp.float32)

                each_block(self.tokens, body)

    def sent(self):
        for step in range(self.last):
            for way in (1, -1):
                beyond = self.place(way) + step < self.last
                pl.when(beyond)(lambda step=step, way=way: self.copy(step, way).wait_send())


def halved_sums(links, parts, rightward, leftward):
    return [
        LineScatter(links, parts.at[:, rows], rightward.at[:, rows], leftward.at[:, rows])
        for rows in halves(parts.shape[1])
    ]


class OutputHalf:
    def __init__(self, links, which, parts, middle, rightward, leftward, total):
        rows = halves(middle.shape[0])[which]
        self.middle, self.total = middle.at[rows], total
        self.sum = LineScatter(links, parts.at[:, rows], rightward, leftward)

    def write(self, output):
        self.sum.finish(self.total)

        def body(rows):
            output[rows, :] = (self.middle[rows, :] + self.total[rows, :]).astype(jnp.bfloat16)

        each_block(self.middle.shape[0], body)


def output_scratch(n_blk, tokens, width):
    return line_scratch(n_blk, tokens // 2, width) + [
        pltpu.VMEM((tokens // 2, width), jnp.float32)
    ]


def line_scratch(n_blk, tokens, width):
    return [pltpu.VMEM((n_blk - 1, tokens, width), jnp.bfloat16)] * 2


class PlaneScatter:
    def __init__(self, links, parts, from_core, from_x, from_y, last_x, last_y):
        self.links, self.parts = links, parts
        self.own_core_only = from_core is None
        self.from_core, self.from_x, self.from_y = from_core, from_x, from_y
        self.last_x, self.last_y = last_x, last_y
        self.core = lax.rem(links.uly, 2)
        self.row = lax.div(links.uly, 2)
        self.depth = parts.shape[3]
        self.core_copies = {}

    def chunk(self, dp, row, core, half=None):
        if self.own_core_only:
            part = self.parts.at[dp, row]
        else:
            part = self.parts.at[dp, :, row * 2 + core]
        if half is None:
            return part
        depth = self.depth // 2
        return part.at[:, pl.ds(half * depth, depth)]

    def add(self, target, source):
        blocks, depth, _ = target.shape
        rows = 32 if depth % 32 == 0 else 16

        def body(index, carry):
            block = lax.div(index, depth // rows)
            at = pl.ds(pl.multiple_of(lax.rem(index, depth // rows) * rows, rows), rows)
            target[block, at, :] = target[block, at, :] + source[block, at, :]
            return carry

        lax.fori_loop(0, blocks * (depth // rows), body, 0)

    def between_cores(self, which):
        links = self.links
        dp = links.dp if which == 1 else links.other_dp
        self.core_copies[which] = [
            links.to(
                self.chunk(dp, row, 1 - self.core), self.from_core.at[which, row], links.core_way
            )
            for row in range(2)
        ]

    def core_sums(self, which):
        links = self.links
        dp = links.dp if which == 1 else links.other_dp
        for row in range(2):
            self.core_copies[which][row].arrived()
            self.add(self.chunk(dp, row, self.core), self.from_core.at[which, row])

    def across_chips(self):
        links = self.links
        if not self.own_core_only:
            self.core_sums(0)
        self.x_copies = [
            links.to(
                self.chunk(links.other_dp, row, self.core, 0), self.from_x.at[row], links.x_way
            )
            for row in range(2)
        ]
        if not self.own_core_only:
            self.core_sums(1)
        self.y_copies = [
            links.to(
                self.chunk(group, 1 - self.row, self.core, 1),
                self.from_y.at[group],
                links.y_way,
            )
            for group in range(links.n_dp)
        ]

    def second_way(self):
        links = self.links
        for row in range(2):
            self.x_copies[row].arrived()
            self.add(self.chunk(links.dp, row, self.core, 0), self.from_x.at[row])
        self.y_last = links.to(
            self.chunk(links.dp, 1 - self.row, self.core, 0), self.last_y, links.y_way
        )
        for group in range(links.n_dp):
            self.y_copies[group].arrived()
            self.add(self.chunk(group, self.row, self.core, 1), self.from_y.at[group])
        self.x_last = links.to(
            self.chunk(links.other_dp, self.row, self.core, 1), self.last_x, links.x_way
        )

    def result(self, write):
        links = self.links
        for half, copy, source in ((0, self.y_last, self.last_y), (1, self.x_last, self.last_x)):
            copy.arrived()
            own = self.chunk(links.dp, self.row, self.core, half)
            blocks, depth, _ = source.shape
            rows = 32 if depth % 32 == 0 else 16

            def body(index, carry, own=own, source=source, half=half, depth=depth, rows=rows):
                block = lax.div(index, depth // rows)
                start = pl.multiple_of(lax.rem(index, depth // rows) * rows, rows)
                at = pl.ds(start, rows)
                value = own[block, at, :].astype(jnp.float32)
                value = value + source[block, at, :].astype(jnp.float32)
                write(block, pl.ds(pl.multiple_of(start + half * depth, rows), rows), value)
                return carry

            lax.fori_loop(0, blocks * (depth // rows), body, 0)


def plane_shapes(n_dp, blocks, n_uly, depth, width):
    return [
        (n_dp, blocks, n_uly, depth, width),
        (n_dp, 2, blocks, depth, width),
        (2, blocks, depth // 2, width),
        (n_dp, blocks, depth // 2, width),
        (blocks, depth // 2, width),
        (blocks, depth // 2, width),
    ]


def plane_scratch(*sizes):
    return [pltpu.VMEM(shape, jnp.bfloat16) for shape in plane_shapes(*sizes)]


def weight_grad(rows, right, parts, dp):
    _, blocks, n_uly, depth, width = parts.shape
    columns = 512

    def body(index, carry):
        at = pl.ds(pl.multiple_of(index * columns, columns), columns)
        part = jnp.dot(rows[...], right[:, at], preferred_element_type=jnp.float32)
        parts[dp, :, :, :, at] = part.astype(jnp.bfloat16).reshape(blocks, n_uly, depth, columns)
        return carry

    lax.fori_loop(0, width // columns, body, 0)


def rows_turned(left, parts, dp):
    count = parts.shape[1] * parts.shape[2] * parts.shape[3]
    return left[:, pl.ds(pl.multiple_of(dp * count, 128), count)].T


def turned(rows, cosine, sine):
    return rows * cosine + pltpu.roll(rows, HEAD_SIZE // 2, axis=1) * sine


def transposed_product(left, right):
    return lax.dot_general(
        left, right, (((0,), (0,)), ((), ())), preferred_element_type=jnp.float32
    )


def product_right(left, right):
    return lax.dot_general(
        left, right, (((1,), (1,)), ((), ())), preferred_element_type=jnp.float32
    )


SCORE_SCALE = 1.0 / math.sqrt(HEAD_SIZE)


def forward_kernel(
    toks,
    gain_rows,
    span_order,
    hidden,
    wq,
    wk,
    wv,
    wo,
    wg,
    wu,
    wd,
    cotangent,
    gains,
    q_gain,
    k_gain,
    all_qkv,
    all_wo,
    all_wg,
    all_wu,
    all_wd,
    all_cot,
    attn_gain,
    mlp_gain,
    cosine,
    sine,
    query_pos,
    key_pos,
    heads,
    normed,
    qkv,
    queries,
    key_values,
    lse,
    middle,
    all_normed,
    all_gains,
    all_hidden,
    near_qkv,
    near_wo,
    parts,
    rightward,
    leftward,
    own_normed,
    send,
    recv,
    here,
):
    links = Links(send, recv, here)
    links.greet(links.peers() + [links.x_way, links.y_way, links.core_way])
    tokens, width = hidden.shape
    spans = halves(tokens)
    q_width, k_width = wq.shape[1] // links.n_blk, wk.shape[1] // links.n_blk
    chunk = all_qkv.at[links.dp, :, links.uly]
    swap = ColumnSwap(
        links, [(wq, chunk, 0), (wk, chunk, q_width), (wv, chunk, q_width + k_width)]
    )
    plane_wo = PlaneGather(links, rows_of(all_wo, False))
    plane_wd = PlaneGather(links, rows_of(all_wd, False))
    plane_qkv = PlaneGather(links, rows_of(all_qkv, True))
    plane_gain = PlaneGather(links, rows_of(all_gains, True))
    swap.start()
    my_gains = all_gains.at[links.dp, links.blk, links.uly]
    gain_swap = [links.to(gains, my_gains, device) for device in links.peers()]
    plane_wo.start(wo)
    line = HalvedLine(links, hidden, all_hidden)
    line.send(0)
    keep = [
        links.local(gains, my_gains),
        links.local(hidden, all_hidden.at[links.blk]),
        links.local(wo, all_wo.at[links.dp, links.uly]),
        links.local(wd, all_wd.at[links.dp, links.uly]),
        links.local(cotangent, all_cot.at[links.blk]),
    ]
    write_positions(links, span_order, toks, cosine, sine, query_pos, key_pos)
    swap.arrived()
    plane_qkv.start()
    keep[0].wait()
    for copy in gain_swap:
        copy.arrived()
    plane_gain.start()
    plane_wd.start(wd)
    plane_wo.hand_on()
    line.advance(1)
    plane_qkv.hand_on()
    plane_gain.hand_on()
    plane_wo.last()
    for step in range(2, links.n_blk - 1):
        line.advance(step)
    pairs = [(wg, all_wg), (wu, all_wu)]
    planes = [PlaneGather(links, rows_of(whole, True)) for _, whole in pairs]
    swaps = [
        ColumnSwap(links, [(weight, whole.at[links.dp, :, links.uly], 0)])
        for weight, whole in pairs
    ]
    for swap in swaps:
        swap.start()
    cot_lines = HalvedLine(links, cotangent, all_cot).lines
    for half in cot_lines:
        half.send(0)
    plane_qkv.last()
    plane_gain.last()
    plane_gain.arrived()
    write_gains(links, all_gains, gain_rows, (attn_gain, mlp_gain))
    for copy in keep[1:]:
        copy.wait()
    plane_wo.arrived()
    plane_qkv.arrived()
    near = [links.local(all_qkv, near_qkv), links.local(all_wo, near_wo)]
    seqs, kv_heads, q_rows, _ = queries.shape
    q_len = key_values.shape[4]
    group = q_rows // q_len
    q_end = kv_heads * group * HEAD_SIZE
    k_end = q_end + kv_heads * HEAD_SIZE

    def norm(seq):
        def body(rows):
            for blk in range(links.n_blk):
                at = pl.ds(pl.multiple_of(seq * toks + rows.start, ROWS), ROWS)
                to = pl.ds(pl.multiple_of(seq * q_len + blk * toks + rows.start, ROWS), ROWS)
                source = all_hidden[blk, at, :].astype(jnp.float32)
                normed[to, :] = (source * rms_scale(source) * attn_gain[...]).astype(
                    jnp.bfloat16
                )

        each_block(toks, body)

    def rotated(seq, column, gain):
        pre = qkv[seq * q_len : (seq + 1) * q_len, column : column + HEAD_SIZE]
        gain = gain[...].astype(jnp.float32)
        return turned(pre * rms_scale(pre) * gain, cosine[...], sine[...]).astype(jnp.bfloat16)

    def project(seq):
        rows = slice(seq * q_len, (seq + 1) * q_len)
        for column in range(0, qkv.shape[1], 512):
            weight = near_qkv[:, :, :, :, column : column + 512].reshape(width, 512)
            qkv[rows, column : column + 512] = jnp.dot(
                normed[rows, :], weight, preferred_element_type=jnp.float32
            )
        for head in range(kv_heads):
            column = head * HEAD_SIZE
            key_values[links.uly, 0, seq, head] = rotated(seq, q_end + column, k_gain)
            key_values[links.uly, 1, seq, head] = qkv[
                rows, k_end + column : k_end + column + HEAD_SIZE
            ].astype(jnp.bfloat16)
        mine = key_values.at[links.uly, :, seq]
        copies = [links.to(mine, mine, way) for way in (links.core_way, links.y_way)]
        for head in range(kv_heads * group):
            at = pl.ds((head % group) * q_len, q_len)
            queries[seq, head // group, at, :] = rotated(seq, head * HEAD_SIZE, q_gain)
        return copies

    def hand_keys(seq, copies):
        copies[1].arrived()
        theirs = key_values.at[links.across, :, seq]
        copies.append(links.to(theirs, theirs, links.core_way))

    def attend(seq, head):
        def over_keys(piece, carry):
            total, mixed = carry
            rows = pl.ds(pl.multiple_of(piece * q_len, q_len), q_len)
            scores = product_right(key_values[piece, 0, seq, head], queries[seq, head])
            weights = jnp.where(
                query_pos[...] >= key_pos[rows, :], jnp.exp(scores * SCORE_SCALE), 0.0
            )
            total = total + jnp.sum(weights, axis=0, keepdims=True)
            mixed = mixed + transposed_product(
                key_values[piece, 1, seq, head], weights.astype(jnp.bfloat16)
            )
            return total, mixed

        total, mixed = lax.fori_loop(
            0,
            links.n_uly,
            over_keys,
            (
                jnp.zeros((1, q_rows), jnp.float32),
                jnp.zeros((HEAD_SIZE, q_rows), jnp.float32),
            ),
        )
        lse[seq * kv_heads + head] = jnp.log(total)
        attended = (mixed / total).T.astype(jnp.bfloat16)
        for member in range(group):
            column = (head * group + member) * HEAD_SIZE
            for blk in range(links.n_blk):
                row = (blk * seqs + seq) * toks
                start = member * q_len + blk * toks
                heads[row : row + toks, column : column + HEAD_SIZE] = attended[
                    start : start + toks, :
                ]

    sums = halved_sums(links, parts, rightward, leftward)
    def out_weight():
        return near_wo[...].reshape(heads.shape[1], width)

    def out_parts(seq):
        mixed = jnp.concatenate(
            [
                heads[(blk * seqs + seq) * toks : (blk * seqs + seq + 1) * toks, :]
                for blk in range(links.n_blk)
            ],
            axis=0,
        )
        for column in range(0, width, 512):
            parts[:, spans[seq], column : column + 512] = (
                jnp.dot(
                    mixed,
                    out_weight()[:, column : column + 512],
                    preferred_element_type=jnp.float32,
                )
                .astype(jnp.bfloat16)
                .reshape(links.n_blk, toks, 512)
            )
        sums[seq].start()

    key_copies = []
    for seq in range(seqs):
        line.lines[seq].arrived()
        norm(seq)
        if seq == 0:
            for copy in near:
                copy.wait()
        key_copies.append(project(seq))
    plane_wd.hand_on()
    hand_keys(0, key_copies[0])
    for copy in (key_copies[0][0], key_copies[0][2]):
        copy.arrived()
    attend(0, 0)
    hand_keys(1, key_copies[1])
    for head in range(1, kv_heads):
        attend(0, head)
    out_parts(0)
    swaps[0].arrived()
    planes[0].start()
    for copy in (key_copies[1][0], key_copies[1][2]):
        copy.arrived()
    attend(1, 0)
    sums[0].tick(1)
    for head in range(1, kv_heads):
        attend(1, head)
    out_parts(1)
    swaps[1].arrived()
    planes[1].start()
    later = range(2, links.n_blk - 1)
    for tick in later:
        sums[0].tick(tick)
    for half in cot_lines:
        half.arrived()
        half.send(1)
    plane_wd.last()
    planes[0].hand_on()
    lines = []

    def settle(half, rows_of_half):
        half.finish(middle.at[rows_of_half])

        def body(rows):
            at = pl.ds(pl.multiple_of(rows_of_half.start + rows.start, ROWS), ROWS)
            total = middle[at, :] + all_hidden[links.blk, at, :].astype(jnp.float32)
            middle[at, :] = total
            own_normed[at, :] = (total * rms_scale(total) * mlp_gain[...]).astype(jnp.bfloat16)

        each_block(tokens // 2, body)
        next_line = LineGather(links, own_normed.at[rows_of_half], all_normed.at[:, rows_of_half])
        next_line.send(0)
        lines.append(next_line)

    settle(sums[0], spans[0])
    sums[1].tick(1)
    advance(lines[0], 1)
    for tick in later:
        sums[1].tick(tick)
    settle(sums[1], spans[1])
    advance(lines[0], 2)
    last_local = links.local(own_normed, all_normed.at[links.blk])
    planes[0].last()
    advance(lines[1], 1)
    for half in cot_lines:
        advance(half, 2)
    planes[1].hand_on()
    advance(lines[1], 2)
    planes[1].last()
    for half in lines + cot_lines:
        half.arrived()
    for plane in [plane_wd] + planes:
        plane.arrived()
    last_local.wait()
    for half in sums:
        half.sent()
    links.finish()


SMEM = pl.BlockSpec(memory_space=pltpu.SMEM)


def forward(
    span_order,
    hidden,
    wq,
    wk,
    wv,
    wo,
    wg,
    wu,
    wd,
    cotangent,
    gains,
    q_gain,
    k_gain,
    seqs,
    gain_rows,
):
    n_dp, n_blk, n_uly = (lax.axis_size(a) for a in EVERY)
    tokens, width = hidden.shape
    toks = tokens // seqs
    rows, q_len = n_blk * tokens, n_blk * toks
    group = QUERY_HEADS // KEY_VALUE_HEADS
    kv_heads = KEY_VALUE_HEADS // n_blk
    q_rows, keys = group * q_len, n_uly * q_len
    columns = (wq.shape[1] + wk.shape[1] + wv.shape[1]) // n_blk
    f32, low, i32 = jnp.float32, jnp.bfloat16, jnp.int32
    ff = wg.shape[1] // n_blk
    far = [
        (n_dp, n_blk, n_uly, wq.shape[0], columns),
        (n_dp, n_uly) + wo.shape,
        (n_dp, n_blk, n_uly, wg.shape[0], ff),
        (n_dp, n_blk, n_uly, wu.shape[0], ff),
        (n_dp, n_uly) + wd.shape,
        (n_blk, tokens, width),
    ]
    near = [
        ((1, width), f32),
        ((1, width), f32),
        ((q_len, HEAD_SIZE), f32),
        ((q_len, HEAD_SIZE), f32),
        ((1, q_rows), i32),
        ((keys, 1), i32),
        ((rows, kv_heads * group * HEAD_SIZE), low),
        ((rows, width), low),
        ((rows, columns), f32),
        ((seqs, kv_heads, q_rows, HEAD_SIZE), low),
        ((n_uly, 2, seqs, kv_heads, q_len, HEAD_SIZE), low),
        ((seqs * kv_heads, 1, q_rows), f32),
        ((tokens, width), f32),
        ((n_blk, tokens, width), low),
    ]
    scratch = [
        ((n_dp, n_blk, n_uly) + gains.shape, low),
        ((n_blk, tokens, width), low),
        (far[0], low),
        (far[1], low),
        ((n_blk, tokens, width), low),
        ((n_blk - 1, tokens, width), low),
        ((n_blk - 1, tokens, width), low),
        ((tokens, width), low),
    ]
    return pl.pallas_call(
        functools.partial(forward_kernel, toks, gain_rows),
        out_shape=[jax.ShapeDtypeStruct(shape, low) for shape in far]
        + [jax.ShapeDtypeStruct(shape, kind) for shape, kind in near],
        in_specs=[SMEM] + [HBM] * 10 + [VMEM] * 2,
        out_specs=[HBM] * len(far) + [VMEM] * len(near),
        scratch_shapes=[pltpu.VMEM(shape, kind) for shape, kind in scratch]
        + semaphores(160, 32),
        compiler_params=kernel_params(0),
    )(span_order, hidden, wq, wk, wv, wo, wg, wu, wd, cotangent, gains, q_gain, k_gain)


def back_rows(grad_normed, source, gain):
    unit = source * rms_scale(source)
    scaled = grad_normed * gain
    return rms_scale(source) * (
        scaled - unit * jnp.mean(scaled * unit, axis=-1, keepdims=True)
    )


def back_kernel(
    grad_parts,
    out_parts,
    middle,
    cotangent,
    gain,
    all_normed,
    grad_gate_pre,
    grad_up_pre,
    activated,
    all_cot,
    output,
    grad_middle,
    all_low,
    grad_gate,
    grad_up,
    part_down,
    rightward,
    leftward,
    out_right,
    out_left,
    out_total,
    low,
    turned_low,
    gate_1,
    gate_2,
    gate_3,
    gate_4,
    gate_5,
    gate_6,
    up_1,
    up_2,
    up_3,
    up_4,
    up_5,
    up_6,
    down_1,
    down_2,
    send,
    recv,
    here,
):
    links = Links(send, recv, here)
    links.greet(links.peers() + [links.x_way, links.y_way, links.core_way])
    sums = halved_sums(links, grad_parts, rightward, leftward)
    for half in sums:
        half.start()
    out = OutputHalf(links, 0, out_parts, middle, out_right, out_left, out_total)
    gate = PlaneScatter(links, gate_1, gate_2, gate_3, gate_4, gate_5, gate_6)
    up = PlaneScatter(links, up_1, up_2, up_3, up_4, up_5, up_6)
    down = PlaneScatter(links, down_1, down_2, None, None, None, None)
    tokens = middle.shape[0]
    spans, lines, keep = halves(tokens), [], []

    def compute(plane, which, rows, right):
        dp = links.dp if which == 1 else links.other_dp
        weight_grad(rows, right, plane.parts, dp)
        plane.between_cores(which)

    def turn(which):
        dp = links.dp if which == 1 else links.other_dp
        turned_low[which] = rows_turned(all_normed, gate_1, dp)

    def compute_down(which):
        dp = links.dp if which == 1 else links.other_dp
        compute(down, which, rows_turned(activated, down_1, dp), all_cot)

    def settle(half, rows_of_half):
        half.finish(grad_middle.at[rows_of_half])

        def body(rows):
            at = pl.ds(pl.multiple_of(rows_of_half.start + rows.start, ROWS), ROWS)
            back = back_rows(grad_middle[at, :], middle[at, :], gain[...])
            grad = cotangent[at, :].astype(jnp.float32) + back
            grad_middle[at, :] = grad
            low[at, :] = grad.astype(jnp.bfloat16)

        each_block(tokens // 2, body)
        line = LineGather(links, low.at[rows_of_half], all_low.at[:, rows_of_half])
        line.send(0)
        lines.append(line)

    later = range(2, links.n_blk - 1)
    turn(0)
    compute(gate, 0, turned_low.at[0], grad_gate_pre)
    sums[0].tick(1)
    turn(1)
    compute(gate, 1, turned_low.at[1], grad_gate_pre)
    for tick in later:
        sums[0].tick(tick)
    gate.across_chips()
    settle(sums[0], spans[0])
    compute(up, 0, turned_low.at[0], grad_up_pre)
    sums[1].tick(1)
    compute(up, 1, turned_low.at[1], grad_up_pre)
    for tick in later:
        sums[1].tick(tick)
    advance(lines[0], 1)
    up.across_chips()
    settle(sums[1], spans[1])
    out.sum.start()
    advance(lines[0], 2)
    keep.append(links.local(low, all_low.at[links.blk]))
    compute_down(0)
    advance(lines[1], 1)
    gate.second_way()
    compute_down(1)
    advance(lines[1], 2)
    out.sum.tick(1)
    up.second_way()
    for which in (0, 1):
        down.core_sums(which)
    for dp in range(links.n_dp):
        for row in range(2):
            keep.append(links.local(down.chunk(dp, row, down.core), part_down.at[dp, row]))
    for tick in later:
        out.sum.tick(tick)
    for line in lines:
        line.arrived()

    def into(target):
        def write(block, rows, values):
            target[block, rows, :] = values.astype(target.dtype)

        return write

    gate.result(into(grad_gate))
    up.result(into(grad_up))
    out.write(output)
    out.sum.sent()
    for copy in keep:
        copy.wait()
    for half in sums:
        half.sent()
    links.finish()


def exchange_back(
    grad_parts,
    out_parts,
    middle,
    cotangent,
    gain,
    all_normed,
    grad_gate_pre,
    grad_up_pre,
    activated,
    all_cot,
):
    n_dp, n_blk, n_uly = (lax.axis_size(a) for a in EVERY)
    _, tokens, width = grad_parts.shape
    ff = grad_gate_pre.shape[1]
    depth = width // (n_dp * n_blk * n_uly)
    down_depth = ff // (n_dp * n_uly)
    return pl.pallas_call(
        back_kernel,
        out_shape=[
            jax.ShapeDtypeStruct((tokens // 2, width), jnp.bfloat16),
            jax.ShapeDtypeStruct((tokens, width), jnp.float32),
            jax.ShapeDtypeStruct((n_blk, tokens, width), jnp.bfloat16),
            jax.ShapeDtypeStruct((n_blk, depth, ff), jnp.bfloat16),
            jax.ShapeDtypeStruct((n_blk, depth, ff), jnp.bfloat16),
            jax.ShapeDtypeStruct((n_dp, 2, 1, down_depth, width), jnp.bfloat16),
        ],
        in_specs=[VMEM] * 10,
        out_specs=[VMEM, VMEM, HBM, VMEM, VMEM, HBM],
        scratch_shapes=line_scratch(n_blk, tokens, width)
        + output_scratch(n_blk, tokens, width)
        + [
            pltpu.VMEM((tokens, width), jnp.bfloat16),
            pltpu.VMEM((n_dp, width // n_dp, n_blk * tokens), jnp.bfloat16),
        ]
        + plane_scratch(n_dp, n_blk, n_uly, depth, ff) * 2
        + plane_scratch(n_dp, 1, n_uly, down_depth, width)[:2]
        + semaphores(72),
        compiler_params=kernel_params(3),
    )(
        grad_parts,
        out_parts,
        middle,
        cotangent,
        gain,
        all_normed,
        grad_gate_pre,
        grad_up_pre,
        activated,
        all_cot,
    )


def backward_kernel(
    all_low,
    wo,
    queries,
    key_values,
    lse,
    qkv,
    q_gain,
    k_gain,
    cosine,
    sine,
    query_pos,
    key_pos,
    w_qkv,
    hidden,
    grad_middle,
    gain,
    normed,
    heads,
    out_parts,
    middle,
    grad_gate,
    grad_up,
    part_down,
    grad_hidden,
    grad_wo,
    grad_down,
    small_sum,
    output,
    gate_rows,
    up_rows,
    grad_w_qkv,
    grad_qkv,
    gain_terms,
    grad_heads,
    grad_rows,
    grad_kv,
    from_core,
    from_across,
    grad_parts,
    rightward,
    leftward,
    summed,
    small_in,
    small_total,
    out_right,
    out_left,
    out_total,
    down_1,
    down_3,
    down_4,
    down_5,
    down_6,
    turned_normed,
    q_1,
    q_2,
    q_3,
    q_4,
    q_5,
    q_6,
    kv_1,
    kv_2,
    kv_3,
    kv_4,
    kv_5,
    kv_6,
    wo_1,
    wo_2,
    wo_3,
    wo_4,
    wo_5,
    wo_6,
    send,
    recv,
    here,
):
    links = Links(send, recv, here)
    links.greet(links.peers() + [links.x_way, links.y_way, links.core_way])
    tokens = hidden.shape[0]
    spans = halves(tokens)
    output_half = OutputHalf(links, 1, out_parts, middle, out_right, out_left, out_total)
    output_half.sum.start()
    down = PlaneScatter(links, down_1, None, down_3, down_4, down_5, down_6)
    fetch = links.local(part_down, down_1)
    swapped, keep = [], []
    for source, target in ((grad_gate, gate_rows), (grad_up, up_rows)):
        swapped += links.swap(
            lambda peer, source=source, target=target: [(source.at[peer], target.at[links.blk])]
        )
        keep.append(links.local(source.at[links.blk], target.at[links.blk]))
    fetch.wait()
    down.across_chips()
    sums = halved_sums(links, grad_parts, rightward, leftward)
    q_sums = PlaneScatter(links, q_1, q_2, q_3, q_4, q_5, q_6)
    kv_sums = PlaneScatter(links, kv_1, kv_2, kv_3, kv_4, kv_5, kv_6)
    wo_sums = PlaneScatter(links, wo_1, wo_2, wo_3, wo_4, wo_5, wo_6)
    seqs, kv_heads, q_rows, _ = queries.shape
    q_len = key_values.shape[4]
    group = q_rows // q_len
    toks = q_len // links.n_blk
    q_end = kv_heads * group * HEAD_SIZE
    k_end = q_end + kv_heads * HEAD_SIZE
    gain_terms[...] = jnp.zeros_like(gain_terms)
    later = range(2, links.n_blk - 1)

    def heads_back(seq):
        low = jnp.concatenate(
            [
                all_low[(blk * seqs + seq) * toks : (blk * seqs + seq + 1) * toks, :]
                for blk in range(links.n_blk)
            ],
            axis=0,
        )
        grad_heads[...] = product_right(low, wo[...])
        for head in range(kv_heads * group):
            to = pl.ds((head % group) * q_len, q_len)
            grad_rows[seq, head // group, to, :] = grad_heads[
                :, head * HEAD_SIZE : (head + 1) * HEAD_SIZE
            ].astype(jnp.bfloat16)

    def back_norm(upstream, seq, column, gain, which):
        rows = slice(seq * q_len, (seq + 1) * q_len)
        pre = qkv[rows, column : column + HEAD_SIZE]
        upstream = turned(upstream, cosine[...], -sine[...])
        gain_terms[which : which + 1, :] += jnp.sum(
            upstream * pre * rms_scale(pre), axis=0, keepdims=True
        )
        grad_qkv[rows, column : column + HEAD_SIZE] = back_rows(
            upstream, pre, gain[...].astype(jnp.float32)
        ).astype(jnp.bfloat16)

    def deltas(seq, head):
        sums_of = []
        for member in range(group):
            column = (head * group + member) * HEAD_SIZE
            attended = jnp.concatenate(
                [
                    heads[row : row + toks, column : column + HEAD_SIZE]
                    for row in ((blk * seqs + seq) * toks for blk in range(links.n_blk))
                ],
                axis=0,
            )
            upstream = grad_rows[seq, head, member * q_len : (member + 1) * q_len, :]
            sums_of.append(attended.astype(jnp.float32) * upstream.astype(jnp.float32))
        terms = jnp.concatenate(sums_of, axis=0)
        high = terms.astype(jnp.bfloat16)
        rest = (terms - high.astype(jnp.float32)).astype(jnp.bfloat16)
        ones = jnp.ones((16, HEAD_SIZE), jnp.bfloat16)
        return (product_right(ones, high) + product_right(ones, rest))[:1, :]

    def back(seq, head):
        delta = deltas(seq, head)

        def over_keys(piece, grad_query):
            rows = pl.ds(pl.multiple_of(piece * q_len, q_len), q_len)
            scores = product_right(key_values[piece, 0, seq, head], queries[seq, head])
            prob = jnp.where(
                query_pos[...] >= key_pos[rows, :],
                jnp.exp(scores * SCORE_SCALE - lse[seq * kv_heads + head]),
                0.0,
            )
            grad_prob = product_right(key_values[piece, 1, seq, head], grad_rows[seq, head])
            grad_score = (prob * (grad_prob - delta)).astype(jnp.bfloat16)
            grad_kv[seq, piece, 0, head] = (
                SCORE_SCALE
                * jnp.dot(grad_score, queries[seq, head], preferred_element_type=jnp.float32)
            ).astype(jnp.bfloat16)
            grad_kv[seq, piece, 1, head] = jnp.dot(
                prob.astype(jnp.bfloat16),
                grad_rows[seq, head],
                preferred_element_type=jnp.float32,
            ).astype(jnp.bfloat16)
            return grad_query + transposed_product(key_values[piece, 0, seq, head], grad_score)

        grad_query = lax.fori_loop(
            0, links.n_uly, over_keys, jnp.zeros((HEAD_SIZE, q_rows), jnp.float32)
        )
        turned_back = (grad_query * SCORE_SCALE).T
        for member in range(group):
            column = (head * group + member) * HEAD_SIZE
            back_norm(
                turned_back[member * q_len : (member + 1) * q_len, :], seq, column, q_gain, 0
            )

    core, line = lax.rem(links.uly, 2), lax.div(links.uly, 2)

    def add(target, source):
        for kind in range(2):
            for head in range(kv_heads):
                target[kind, head] = target[kind, head] + source[kind, head]

    def core_sums(seq):
        return [
            links.to(
                grad_kv.at[seq, row * 2 + 1 - core], from_core.at[seq, row], links.core_way
            )
            for row in range(2)
        ]

    def across_sums(seq, copies):
        for row in range(2):
            copies[row].arrived()
            add(grad_kv.at[seq, row * 2 + core], from_core.at[seq, row])
        return links.to(
            grad_kv.at[seq, (1 - line) * 2 + core], from_across.at[seq], links.y_way
        )

    def own_keys(seq, copy):
        copy.arrived()
        rows = slice(seq * q_len, (seq + 1) * q_len)
        for head in range(kv_heads):
            term = [
                grad_kv[seq, links.uly, kind, head].astype(jnp.float32)
                + from_across[seq, kind, head].astype(jnp.float32)
                for kind in range(2)
            ]
            back_norm(term[0], seq, q_end + head * HEAD_SIZE, k_gain, 1)
            v_at = k_end + head * HEAD_SIZE
            grad_qkv[rows, v_at : v_at + HEAD_SIZE] = term[1].astype(jnp.bfloat16)

    def normed_parts(seq):
        for column in range(0, w_qkv.shape[0], 512):
            grad_parts[:, spans[seq], column : column + 512] = (
                product_right(
                    grad_qkv[seq * q_len : (seq + 1) * q_len, :],
                    w_qkv[column : column + 512, :],
                )
                .astype(jnp.bfloat16)
                .reshape(links.n_blk, toks, 512)
            )
        sums[seq].start()

    def dp_of(which):
        return links.dp if which == 1 else links.other_dp

    def compute_wo(which):
        dp = dp_of(which)
        weight_grad(rows_turned(heads, wo_1, dp), all_low, wo_1, dp)
        wo_sums.between_cores(which)

    def compute_qkv(plane, which, columns):
        weight_grad(
            turned_normed.at[which], grad_qkv.at[:, columns], plane.parts, dp_of(which)
        )
        plane.between_cores(which)

    q_columns, kv_columns = pl.ds(0, q_end), pl.ds(q_end, grad_qkv.shape[1] - q_end)
    heads_back(0)
    back(0, 0)
    output_half.sum.tick(1)
    for head in range(1, kv_heads):
        back(0, head)
    core_copies = core_sums(0)
    heads_back(1)
    down.second_way()
    for which in range(2):
        turned_normed[which] = rows_turned(normed, q_1, dp_of(which))
    back(1, 0)
    across = across_sums(0, core_copies)
    for tick in later:
        output_half.sum.tick(tick)
    for head in range(1, kv_heads):
        back(1, head)
    core_copies = core_sums(1)
    own_keys(0, across)
    across = across_sums(1, core_copies)
    normed_parts(0)
    compute_qkv(q_sums, 0, q_columns)
    compute_qkv(q_sums, 1, q_columns)
    own_keys(1, across)
    small_total[0] = gain_terms[...]
    pending = links.to(small_total.at[0], small_in.at[links.n_blk], links.core_way)
    q_sums.across_chips()
    normed_parts(1)
    sums[0].tick(1)
    compute_qkv(kv_sums, 0, kv_columns)
    compute_qkv(kv_sums, 1, kv_columns)
    for tick in later:
        sums[0].tick(tick)
    pending.arrived()
    small_total[1] = small_total[0] + small_in[links.n_blk]
    pending = links.to(small_total.at[1], small_in.at[links.n_blk + 1], links.x_way)
    kv_sums.across_chips()
    q_sums.second_way()
    compute_wo(0)
    compute_wo(1)
    pending.arrived()
    small_total[2] = small_total[1] + small_in[links.n_blk + 1]
    pending = links.to(small_total.at[2], small_in.at[links.n_blk + 2], links.y_way)
    sums[1].tick(1)
    kv_sums.second_way()
    wo_sums.across_chips()

    def into(target):
        def write(block, rows, values):
            target[block, rows, :] = values.astype(target.dtype)

        return write

    def give_home(plane, columns):
        here, there = summed.at[:, :, columns], grad_w_qkv.at[links.blk, :, columns]
        plane.result(into(here))
        keep.append(links.local(here.at[links.blk], there))
        return links.swap(lambda peer: [(here.at[peer], there)])

    swapped += give_home(q_sums, q_columns)
    for tick in later:
        sums[1].tick(tick)
    pending.arrived()
    small_in[links.blk] = small_total[2] + small_in[links.n_blk + 2]
    mine = small_in.at[links.blk]
    small_copies = [links.to(mine, mine, device) for device in links.peers()]
    swapped += give_home(kv_sums, kv_columns)
    output_half.write(output)

    def settle(seq):
        sums[seq].finish(grad_hidden.at[spans[seq]])

        def body(rows):
            at = pl.ds(pl.multiple_of(spans[seq].start + rows.start, ROWS), ROWS)
            back = back_rows(grad_hidden[at, :], hidden[at, :].astype(jnp.float32), gain[...])
            grad_hidden[at, :] = grad_middle[at, :] + back

        each_block(toks, body)

    settle(0)
    wo_sums.second_way()
    down.result(into(grad_down))
    settle(1)
    wo_sums.result(into(grad_wo))
    for copy in small_copies:
        copy.arrived()
    total = small_in[0]
    for blk in range(1, links.n_blk):
        total = total + small_in[blk]
    small_sum[...] = total
    for copy in swapped:
        copy.arrived()
    for copy in keep:
        copy.wait()
    for half in sums:
        half.sent()
    output_half.sum.sent()
    links.finish()


def backward(
    all_low,
    wo,
    queries,
    key_values,
    lse,
    qkv,
    q_gain,
    k_gain,
    cosine,
    sine,
    query_pos,
    key_pos,
    w_qkv,
    hidden,
    grad_middle,
    gain,
    normed,
    heads,
    out_parts,
    middle,
    grad_gate,
    grad_up,
    part_down,
):
    seqs, kv_heads, q_rows, _ = queries.shape
    n_uly, _, _, _, q_len, _ = key_values.shape
    n_blk, tokens, width = out_parts.shape
    n_dp, _, _, down_depth, _ = part_down.shape
    columns = qkv.shape[1]
    depth = width // (n_dp * n_blk * n_uly)
    out_depth = heads.shape[1] // (n_dp * n_uly)
    f32, low = jnp.float32, jnp.bfloat16
    small = (8, HEAD_SIZE)
    outs = [
        ((tokens, width), f32),
        ((1, out_depth, width), f32),
        ((1, down_depth, width), f32),
        (small, f32),
        ((tokens // 2, width), low),
        (grad_gate.shape, low),
        (grad_up.shape, low),
        ((n_blk, depth, columns), low),
    ]
    scratch = [
        (qkv.shape, low),
        (small, f32),
        ((q_len, heads.shape[1]), f32),
        (queries.shape, low),
        ((seqs, n_uly, 2, kv_heads, q_len, HEAD_SIZE), low),
        ((seqs, 2, 2, kv_heads, q_len, HEAD_SIZE), low),
        ((seqs, 2, kv_heads, q_len, HEAD_SIZE), low),
        (out_parts.shape, low),
        ((n_blk - 1, tokens, width), low),
        ((n_blk - 1, tokens, width), low),
        ((n_blk, depth, columns), low),
        ((n_blk + 3,) + small, f32),
        ((3,) + small, f32),
    ]
    down = [part_down.shape] + plane_shapes(n_dp, 1, n_uly, down_depth, width)[2:]
    return pl.pallas_call(
        backward_kernel,
        out_shape=[jax.ShapeDtypeStruct(shape, kind) for shape, kind in outs],
        in_specs=[VMEM] * 20 + [HBM] * 3,
        out_specs=[VMEM] * 5 + [HBM] * 3,
        scratch_shapes=[pltpu.VMEM(shape, kind) for shape, kind in scratch]
        + output_scratch(n_blk, tokens, width)
        + [pltpu.VMEM(shape, low) for shape in down]
        + [pltpu.VMEM((n_dp, width // n_dp, normed.shape[0]), low)]
        + plane_scratch(n_dp, n_blk, n_uly, depth, heads.shape[1])
        + plane_scratch(n_dp, n_blk, n_uly, depth, columns - heads.shape[1])
        + plane_scratch(n_dp, 1, n_uly, out_depth, width)
        + semaphores(112),
        compiler_params=kernel_params(4),
    )(
        all_low,
        wo,
        queries,
        key_values,
        lse,
        qkv,
        q_gain,
        k_gain,
        cosine,
        sine,
        query_pos,
        key_pos,
        w_qkv,
        hidden,
        grad_middle,
        gain,
        normed,
        heads,
        out_parts,
        middle,
        grad_gate,
        grad_up,
        part_down,
    )


def finish_kernel(
    gate,
    up,
    qkv,
    wo,
    wd,
    hidden,
    out_0,
    out_1,
    w_gate,
    w_up,
    w_query,
    key_weight,
    value_weight,
    attn_gain,
    mlp_gain,
    small,
    f_gate,
    f_up,
    f_q,
    f_k,
    f_v,
    f_wo,
    f_wd,
    f_hidden,
    f_out,
    f_attn,
    f_mlp,
    f_q_gain,
    f_k_gain,
):
    n_blk, depth, _ = gate.shape

    def place(source, offset, target):
        width = target.shape[1] // (n_blk * 2)
        for blk in range(n_blk):
            for group in range(2):
                to = (group * n_blk + blk) * width
                at = offset + group * width
                target[:, to : to + width] = source[blk, :, at : at + width].astype(jnp.float32)

    def gain_back(pairs, gain):
        total = jnp.zeros((depth, 128), jnp.float32)
        for weight, grad in pairs:
            for column in range(0, weight.shape[1], 128):
                at = slice(column, column + 128)
                total = total + weight[:, at].astype(jnp.float32) * grad[:, at]
        column = jnp.sum(total, axis=1, keepdims=True)
        square = (depth, depth)
        same = lax.broadcasted_iota(jnp.int32, square, 0) == lax.broadcasted_iota(
            jnp.int32, square, 1
        )
        return jnp.sum(jnp.where(same, column, 0.0), axis=0, keepdims=True) / gain[
            ...
        ].astype(jnp.float32)

    place(gate, 0, f_gate)
    place(up, 0, f_up)
    q_width = f_q.shape[1] // n_blk
    k_width = f_k.shape[1] // n_blk
    place(qkv, 0, f_q)
    place(qkv, q_width, f_k)
    place(qkv, q_width + k_width, f_v)
    f_q_gain[...] = small[0:1, :]
    f_k_gain[...] = small[1:2, :]
    f_wo[...] = wo[0]
    f_wd[...] = wd[0]
    f_hidden[...] = hidden[...]
    half = out_0.shape[0]
    f_out[:half, :] = out_0[...]
    f_out[half:, :] = out_1[...]
    f_attn[...] = gain_back(((w_query, f_q), (key_weight, f_k), (value_weight, f_v)), attn_gain)
    f_mlp[...] = gain_back(((w_gate, f_gate), (w_up, f_up)), mlp_gain)


def finish(gate, up, qkv, wo, wd, hidden, out_0, out_1, weights, gains, small):
    return pl.pallas_call(
        finish_kernel,
        out_shape=[jax.ShapeDtypeStruct(w.shape, jnp.float32) for w in weights]
        + [
            jax.ShapeDtypeStruct(wo.shape[1:], jnp.float32),
            jax.ShapeDtypeStruct(wd.shape[1:], jnp.float32),
            jax.ShapeDtypeStruct(hidden.shape, jnp.float32),
            jax.ShapeDtypeStruct(hidden.shape, jnp.bfloat16),
        ]
        + [jax.ShapeDtypeStruct(gain.shape, jnp.float32) for gain in gains]
        + [jax.ShapeDtypeStruct((1, small.shape[1]), jnp.float32)] * 2,
        in_specs=[VMEM] * 16,
        out_specs=[VMEM] * 13,
        compiler_params=pltpu.CompilerParams(vmem_limit_bytes=62 * MIB),
    )(gate, up, qkv, wo, wd, hidden, out_0, out_1, *weights, *gains, small)


def product(left, right):
    return jnp.dot(left, right, preferred_element_type=jnp.float32)


def shards(
    hidden,
    span_order,
    attn_gain,
    w_query,
    key_weight,
    value_weight,
    w_out,
    q_gain,
    k_gain,
    mlp_gain,
    w_gate,
    w_up,
    w_down,
    cotangent,
):
    seqs, toks, width = hidden.shape
    n_dp, n_blk, n_uly = (lax.axis_size(a) for a in EVERY)
    rows = n_blk * seqs * toks
    bf16 = jnp.bfloat16
    own_hidden = hidden.reshape(seqs * toks, width)
    own_cotangent = cotangent.reshape(seqs * toks, width)

    gain_q, gain_k = q_gain[None, :], k_gain[None, :]
    gain_rows = attn_gain.shape[0]
    own_gains = jnp.pad(jnp.stack([attn_gain, mlp_gain]), ((0, 30), (0, 128 - gain_rows)))
    (
        w_qkv,
        wo,
        all_wg,
        all_wu,
        all_wd,
        cot,
        g_attn,
        g_mlp,
        cosine,
        sine,
        query_pos,
        key_pos,
        heads_flat,
        normed,
        qkv,
        queries,
        key_values,
        lse,
        middle,
        normed2,
    ) = forward(
        span_order,
        own_hidden,
        w_query,
        key_weight,
        value_weight,
        w_out,
        w_gate,
        w_up,
        w_down,
        own_cotangent,
        own_gains,
        gain_q,
        gain_k,
        seqs,
        gain_rows,
    )
    w_qkv = w_qkv.reshape(width, -1)
    wo = wo.reshape(-1, width)
    wg, wu = all_wg.reshape(width, -1), all_wu.reshape(width, -1)
    wd = all_wd.reshape(-1, width)
    cot = cot.reshape(rows, width)
    normed2 = normed2.reshape(rows, width)
    gate_pre = product(normed2, wg)
    up_pre = product(normed2, wu)
    sigmoid_gate = jax.nn.sigmoid(gate_pre)
    activated = (gate_pre * sigmoid_gate * up_pre).astype(bf16)
    out_parts = product(activated, wd).astype(bf16)
    grad_act = product_right(cot, wd)
    grad_gate_pre = (
        grad_act * up_pre * sigmoid_gate * (1.0 + gate_pre * (1.0 - sigmoid_gate))
    ).astype(bf16)
    grad_up_pre = (grad_act * gate_pre * sigmoid_gate).astype(bf16)
    grad_parts = (product_right(grad_gate_pre, wg) + product_right(grad_up_pre, wu)).astype(bf16)
    blocks = (n_blk, seqs * toks, width)
    out_parts = out_parts.reshape(blocks)
    output_0, grad_middle, middle_low, grad_gate, grad_up, part_down = exchange_back(
        grad_parts.reshape(blocks),
        out_parts,
        middle,
        own_cotangent,
        g_mlp,
        normed2,
        grad_gate_pre,
        grad_up_pre,
        activated,
        cot,
    )
    middle_low = middle_low.reshape(rows, width)
    (
        grad_hidden,
        grad_out,
        grad_down,
        small,
        output_1,
        grad_gate,
        grad_up,
        grad_w_qkv,
    ) = backward(
        middle_low,
        wo,
        queries,
        key_values,
        lse,
        qkv,
        gain_q,
        gain_k,
        cosine,
        sine,
        query_pos,
        key_pos,
        w_qkv,
        own_hidden,
        grad_middle,
        g_attn,
        normed,
        heads_flat,
        out_parts,
        middle,
        grad_gate,
        grad_up,
        part_down,
    )
    (
        grad_gate,
        grad_up,
        grad_query,
        grad_key,
        grad_value,
        grad_out,
        grad_down,
        grad_hidden,
        output,
        grad_attn_gain,
        grad_mlp_gain,
        grad_q_gain,
        grad_k_gain,
    ) = finish(
        grad_gate,
        grad_up,
        grad_w_qkv,
        grad_out,
        grad_down,
        grad_hidden,
        output_0,
        output_1,
        (w_gate, w_up, w_query, key_weight, value_weight),
        [g[None, :] for g in (attn_gain, mlp_gain)],
        small,
    )
    return (
        output.reshape(hidden.shape),
        grad_hidden.reshape(hidden.shape),
        grad_attn_gain.reshape(gain_rows),
        grad_query,
        grad_key,
        grad_value,
        grad_out,
        grad_q_gain[0],
        grad_k_gain[0],
        grad_mlp_gain.reshape(gain_rows),
        grad_gate,
        grad_up,
        grad_down,
    )


def solution(mesh):
    n_dp, n_blk, n_uly = (mesh.shape[a] for a in EVERY)
    aligned = (n_dp, n_uly) == (2, 4) and KEY_VALUE_HEADS % (n_dp * n_blk) == 0
    in_specs = (
        TOKENS,
        P(),
        P(EVERY),
        P(EVERY, None),
        P(EVERY, None),
        P(EVERY, None),
        P(EVERY, None),
        P(),
        P(),
        P(EVERY),
        P(EVERY, None),
        P(EVERY, None),
        P(EVERY, None),
        TOKENS,
    )
    out_specs = (
        TOKENS,
        TOKENS,
        P(EVERY),
        P(EVERY, None),
        P(EVERY, None),
        P(EVERY, None),
        P(EVERY, None),
        P(),
        P(),
        P(EVERY),
        P(EVERY, None),
        P(EVERY, None),
        P(EVERY, None),
    )
    return jax.shard_map(
        shards if aligned else shards_general,
        mesh=mesh, in_specs=in_specs, out_specs=out_specs, check_vma=False)
```

```python
import functools
import math

import jax
import jax.numpy as jnp
from jax import lax
from jax.experimental import pallas as pl
from jax.experimental.pallas import tpu as pltpu
from jax.sharding import PartitionSpec as P

QUERY_HEADS = 16
KEY_VALUE_HEADS = 8
HEAD_SIZE = 128


DP, BLK, ULY = "dp", "blk", "uly"
EVERY = (DP, BLK, ULY)
PLANE = (DP, ULY)
TOKENS = P(DP, (BLK, ULY), None)
EQ_KGQD_NKD_TO_KGQN = "kgqd,nkd->kgqn"
EQ_KGQN_KGQD_TO_NKD = "kgqn,kgqd->nkd"
EQ_KGQN_NKD_TO_KGQD = "kgqn,nkd->kgqd"
EQ_KGQN_QKGD_TO_NKD = "kgqn,qkgd->nkd"
EQ_QKGD_NKD_TO_KGQN = "qkgd,nkd->kgqn"
EQ_STD_DE_TO_STE = "std,de->ste"
EQ_STD_DF_TO_STF = "std,df->stf"
EQ_STD_ED_TO_STE = "std,ed->ste"
EQ_STD_FD_TO_STF = "std,fd->stf"
EQ_STD_STE_TO_DE = "std,ste->de"
EQ_STD_STF_TO_DF = "std,stf->df"
EQ_STE_DE_TO_STD = "ste,de->std"
EQ_STE_ED_TO_STD = "ste,ed->std"
EQ_STE_STD_TO_ED = "ste,std->ed"
EQ_STF_DF_TO_STD = "stf,df->std"
EQ_STF_FD_TO_STD = "stf,fd->std"
EQ_STF_STD_TO_FD = "stf,std->fd"

EPSILON = 1e-06
ROPE_BASE = 1000000.0


def rms_scale(source):
    return lax.rsqrt(jnp.mean(source * source, axis=-1, keepdims=True) + EPSILON)


def norm_back(grad_normed, source, norm_scale, gain):
    unit_rows = source * norm_scale
    scaled = grad_normed * gain
    return norm_scale * (scaled - unit_rows * jnp.mean(scaled * unit_rows, axis=-1, keepdims=True))


def angles_of(positions, head_dim):
    freq_steps = jnp.arange(head_dim // 2, dtype=jnp.float32)
    inverse = jnp.exp(freq_steps * (-2.0 * math.log(ROPE_BASE) / head_dim))
    return positions.astype(jnp.float32)[:, None] * inverse[None, :]


def rotate(source, angles, direction):
    half_dim = source.shape[-1] // 2
    cosine = jnp.cos(angles)[:, None, :]
    sine_part = direction * jnp.sin(angles)[:, None, :]
    first_half = source[..., :half_dim]
    second_half = source[..., half_dim:]
    return jnp.concatenate(
        [
            first_half * cosine - second_half * sine_part,
            second_half * cosine + first_half * sine_part,
        ],
        axis=-1,
    )


def positions_of(places, span_order, half_len):
    blocks_of = places // half_len
    block_ids = jnp.arange(span_order.shape[0], dtype=jnp.int32)
    chosen = jnp.sum(
        jnp.where(blocks_of[:, None] == block_ids[None, :], span_order[None, :], 0), axis=1
    )
    return chosen * half_len + places % half_len


def add_rows(buffer, new_rows):
    return buffer + new_rows


def shards_general(
    hidden,
    span_order,
    attn_gain,
    w_query,
    key_weight,
    value_weight,
    w_out,
    q_gain,
    k_gain,
    mlp_gain,
    w_gate,
    w_up,
    w_down,
    cotangent,
):
    sequence_count = hidden.shape[0]
    token_count = hidden.shape[1]
    ulysses_group_size = lax.axis_size(ULY)
    local_q = QUERY_HEADS // ulysses_group_size
    local_key_value = KEY_VALUE_HEADS // ulysses_group_size
    query_group_width = QUERY_HEADS // KEY_VALUE_HEADS
    block_len = token_count * ulysses_group_size
    half_len = block_len // 2
    score_scale = 1.0 / math.sqrt(HEAD_SIZE)
    blk_index = lax.axis_index(BLK)
    uly_index = lax.axis_index(ULY)
    first_place = (blk_index * ulysses_group_size + uly_index) * token_count
    local_angles = angles_of(
        positions_of(first_place + jnp.arange(token_count, dtype=jnp.int32), span_order, half_len),
        HEAD_SIZE,
    )
    query_pos = positions_of(
        blk_index * block_len + jnp.arange(block_len, dtype=jnp.int32), span_order, half_len
    )
    g_attn, wq_all, wk_all, wv_all, wo_all = (
        lax.all_gather(attn_gain, EVERY, axis=0, tiled=True),
        lax.all_gather(w_query, EVERY, axis=0, tiled=True),
        lax.all_gather(key_weight, EVERY, axis=0, tiled=True),
        lax.all_gather(value_weight, EVERY, axis=0, tiled=True),
        lax.all_gather(w_out, EVERY, axis=0, tiled=True),
    )
    source = hidden.astype(jnp.float32)
    first_scale = rms_scale(source)
    normalized_input = (source * first_scale * g_attn.astype(jnp.float32)).astype(jnp.bfloat16)
    q_pre = jnp.einsum(
        EQ_STD_DE_TO_STE, normalized_input, wq_all, preferred_element_type=jnp.float32
    ).reshape(sequence_count, token_count, QUERY_HEADS, HEAD_SIZE)
    key_before_norm = jnp.einsum(
        EQ_STD_DE_TO_STE, normalized_input, wk_all, preferred_element_type=jnp.float32
    ).reshape(sequence_count, token_count, KEY_VALUE_HEADS, HEAD_SIZE)
    value_before_norm = jnp.einsum(
        EQ_STD_DE_TO_STE, normalized_input, wv_all, preferred_element_type=jnp.float32
    ).reshape(sequence_count, token_count, KEY_VALUE_HEADS, HEAD_SIZE)
    q_scale = rms_scale(q_pre)
    k_scale = rms_scale(key_before_norm)
    gain_q = q_gain.astype(jnp.float32)
    gain_k = k_gain.astype(jnp.float32)
    q_rot = rotate(q_pre * q_scale * gain_q, local_angles, 1.0).astype(jnp.bfloat16)
    k_rot = rotate(key_before_norm * k_scale * gain_k, local_angles, 1.0).astype(jnp.bfloat16)
    v_low = value_before_norm.astype(jnp.bfloat16)
    q_heads, k_heads, v_heads = (
        lax.all_to_all(q_rot, ULY, split_axis=2, concat_axis=1, tiled=True),
        lax.all_to_all(k_rot, ULY, split_axis=2, concat_axis=1, tiled=True),
        lax.all_to_all(v_low, ULY, split_axis=2, concat_axis=1, tiled=True),
    )
    q_group = q_heads.reshape(
        sequence_count, block_len, local_key_value, query_group_width, HEAD_SIZE
    )
    stat_shape = (sequence_count, local_key_value, query_group_width, block_len)
    start_state = (
        jnp.full(stat_shape, -1e30, jnp.float32),
        jnp.zeros(stat_shape, jnp.float32),
        jnp.zeros(stat_shape + (HEAD_SIZE,), jnp.float32),
    )
    key_piece = lax.all_gather(k_heads, BLK, axis=1, tiled=True)
    value_piece = lax.all_gather(v_heads, BLK, axis=1, tiled=True)
    key_pos = positions_of(jnp.arange(key_piece.shape[1], dtype=jnp.int32), span_order, half_len)
    allowed = query_pos[:, None] >= key_pos[None, :]

    def attend_one_sequence(members):
        query_rows, key_rows, value_rows, top_seq, total_seq, accum_seq = members
        scores = (
            jnp.einsum(EQ_QKGD_NKD_TO_KGQN, query_rows, key_rows, preferred_element_type=jnp.float32)
            * score_scale
        )
        scores = jnp.where(allowed, scores, -jnp.inf)
        new_top = jnp.maximum(top_seq, jnp.max(scores, axis=-1))
        fading = jnp.exp(top_seq - new_top)
        weights = jnp.exp(scores - new_top[..., None])
        total_seq = total_seq * fading + jnp.sum(weights, axis=-1)
        accum_seq = accum_seq * fading[..., None] + jnp.einsum(
            EQ_KGQN_NKD_TO_KGQD,
            weights.astype(jnp.bfloat16),
            value_rows,
            preferred_element_type=jnp.float32,
        )
        return (new_top, total_seq, accum_seq)

    row_top, row_total, accum = lax.map(
        attend_one_sequence,
        (q_group, key_piece, value_piece, start_state[0], start_state[1], start_state[2]),
    )
    log_total = row_top + jnp.log(row_total)
    attention_output = jnp.transpose(accum / row_total[..., None], (0, 3, 1, 2, 4)).reshape(
        sequence_count, block_len, local_q, HEAD_SIZE
    )
    heads_seq = lax.all_to_all(
        attention_output.astype(jnp.bfloat16), ULY, split_axis=1, concat_axis=2, tiled=True
    )
    heads_flat = heads_seq.reshape(sequence_count, token_count, QUERY_HEADS * HEAD_SIZE)
    middle = source + jnp.einsum(
        EQ_STE_ED_TO_STD, heads_flat, wo_all, preferred_element_type=jnp.float32
    )
    g_mlp, wg_all, wu_all, wd_all = (
        lax.all_gather(mlp_gain, EVERY, axis=0, tiled=True),
        lax.all_gather(w_gate, EVERY, axis=0, tiled=True),
        lax.all_gather(w_up, EVERY, axis=0, tiled=True),
        lax.all_gather(w_down, EVERY, axis=0, tiled=True),
    )
    second_scale = rms_scale(middle)
    gain_mlp = g_mlp.astype(jnp.float32)
    normed2 = (middle * second_scale * gain_mlp).astype(jnp.bfloat16)
    gate_pre = jnp.einsum(EQ_STD_DF_TO_STF, normed2, wg_all, preferred_element_type=jnp.float32)
    up_pre = jnp.einsum(EQ_STD_DF_TO_STF, normed2, wu_all, preferred_element_type=jnp.float32)
    sigmoid_gate = jax.nn.sigmoid(gate_pre)
    activated = (gate_pre * sigmoid_gate * up_pre).astype(jnp.bfloat16)
    result = middle + jnp.einsum(
        EQ_STF_FD_TO_STD, activated, wd_all, preferred_element_type=jnp.float32
    )
    output = result.astype(jnp.bfloat16)
    g_mlp, wg_all, wu_all, wd_all = (
        lax.all_gather(mlp_gain, EVERY, axis=0, tiled=True),
        lax.all_gather(w_gate, EVERY, axis=0, tiled=True),
        lax.all_gather(w_up, EVERY, axis=0, tiled=True),
        lax.all_gather(w_down, EVERY, axis=0, tiled=True),
    )
    gain_mlp = g_mlp.astype(jnp.float32)
    grad_act = jnp.einsum(EQ_STD_FD_TO_STF, cotangent, wd_all, preferred_element_type=jnp.float32)
    grad_gate_pre = (
        grad_act * up_pre * sigmoid_gate * (1.0 + gate_pre * (1.0 - sigmoid_gate))
    ).astype(jnp.bfloat16)
    grad_up_pre = (grad_act * gate_pre * sigmoid_gate).astype(jnp.bfloat16)
    grad_gate = jnp.einsum(
        EQ_STD_STF_TO_DF, normed2, grad_gate_pre, preferred_element_type=jnp.float32
    )
    grad_up = jnp.einsum(EQ_STD_STF_TO_DF, normed2, grad_up_pre, preferred_element_type=jnp.float32)
    grad_normed2 = jnp.einsum(
        EQ_STF_DF_TO_STD, grad_gate_pre, wg_all, preferred_element_type=jnp.float32
    ) + jnp.einsum(EQ_STF_DF_TO_STD, grad_up_pre, wu_all, preferred_element_type=jnp.float32)
    mlp_gain_term = jnp.sum(grad_normed2 * middle * second_scale, axis=(0, 1))
    grad_middle = cotangent.astype(jnp.float32) + norm_back(
        grad_normed2, middle, second_scale, gain_mlp
    )
    grad_mlp_gain, grad_gate, grad_up = (
        lax.psum_scatter(mlp_gain_term, EVERY, scatter_dimension=0, tiled=True),
        lax.psum_scatter(grad_gate, EVERY, scatter_dimension=0, tiled=True),
        lax.psum_scatter(grad_up, EVERY, scatter_dimension=0, tiled=True),
    )
    g_attn, wq_all, wk_all, wv_all, wo_all = (
        lax.all_gather(attn_gain, EVERY, axis=0, tiled=True),
        lax.all_gather(w_query, EVERY, axis=0, tiled=True),
        lax.all_gather(key_weight, EVERY, axis=0, tiled=True),
        lax.all_gather(value_weight, EVERY, axis=0, tiled=True),
        lax.all_gather(w_out, EVERY, axis=0, tiled=True),
    )
    middle_low = grad_middle.astype(jnp.bfloat16)
    grad_out = jnp.einsum(EQ_STE_STD_TO_ED, heads_flat, middle_low, preferred_element_type=jnp.float32)
    grad_heads = (
        jnp.einsum(EQ_STD_ED_TO_STE, middle_low, wo_all, preferred_element_type=jnp.float32)
        .astype(jnp.bfloat16)
        .reshape(sequence_count, token_count, QUERY_HEADS, HEAD_SIZE)
    )
    grad_heads_local = lax.all_to_all(grad_heads, ULY, split_axis=2, concat_axis=1, tiled=True)
    grad_group = jnp.transpose(
        grad_heads_local.reshape(
            sequence_count, block_len, local_key_value, query_group_width, HEAD_SIZE
        ),
        (0, 2, 3, 1, 4),
    )
    delta = jnp.sum(grad_heads_local.astype(jnp.float32) * attention_output, axis=-1)
    delta = jnp.transpose(
        delta.reshape(sequence_count, block_len, local_key_value, query_group_width), (0, 2, 3, 1)
    )
    seq_length = block_len * lax.axis_size(BLK)
    zero_keys = jnp.zeros((sequence_count, seq_length, local_key_value, HEAD_SIZE), jnp.float32)
    back_state = (jnp.zeros(stat_shape + (HEAD_SIZE,), jnp.float32), zero_keys, zero_keys)
    key_piece = lax.all_gather(k_heads, BLK, axis=1, tiled=True)
    value_piece = lax.all_gather(v_heads, BLK, axis=1, tiled=True)
    key_pos = positions_of(jnp.arange(key_piece.shape[1], dtype=jnp.int32), span_order, half_len)
    back_allowed = query_pos[:, None] >= key_pos[None, :]

    def back_one_sequence(members):
        query_rows, grad_rows, lse_seq, delta_seq, key_rows, value_rows, dq_seq, dk_seq, dv_seq = (
            members
        )
        scores = (
            jnp.einsum(EQ_QKGD_NKD_TO_KGQN, query_rows, key_rows, preferred_element_type=jnp.float32)
            * score_scale
        )
        scores = jnp.where(back_allowed, scores, -jnp.inf)
        probs = jnp.exp(scores - lse_seq[..., None])
        grad_values = jnp.einsum(
            EQ_KGQN_KGQD_TO_NKD,
            probs.astype(jnp.bfloat16),
            grad_rows,
            preferred_element_type=jnp.float32,
        )
        grad_probs = jnp.einsum(
            EQ_KGQD_NKD_TO_KGQN, grad_rows, value_rows, preferred_element_type=jnp.float32
        )
        grad_scores = (probs * (grad_probs - delta_seq[..., None])).astype(jnp.bfloat16)
        dq_seq = dq_seq + score_scale * jnp.einsum(
            EQ_KGQN_NKD_TO_KGQD, grad_scores, key_rows, preferred_element_type=jnp.float32
        )
        grad_keys = score_scale * jnp.einsum(
            EQ_KGQN_QKGD_TO_NKD, grad_scores, query_rows, preferred_element_type=jnp.float32
        )
        return (dq_seq, add_rows(dk_seq, grad_keys), add_rows(dv_seq, grad_values))

    grad_q_group, grad_k_whole, grad_v_whole = lax.map(
        back_one_sequence,
        (
            q_group,
            grad_group,
            log_total,
            delta,
            key_piece,
            value_piece,
            back_state[0],
            back_state[1],
            back_state[2],
        ),
    )
    grad_k_block, grad_v_block = (
        lax.psum_scatter(
            grad_k_whole.astype(jnp.bfloat16), BLK, scatter_dimension=1, tiled=True
        ).astype(jnp.float32),
        lax.psum_scatter(
            grad_v_whole.astype(jnp.bfloat16), BLK, scatter_dimension=1, tiled=True
        ).astype(jnp.float32),
    )
    grad_q_block = jnp.transpose(grad_q_group, (0, 3, 1, 2, 4)).reshape(
        sequence_count, block_len, local_q, HEAD_SIZE
    )
    grad_q_seq, grad_k_seq, value_sequence_gradient = (
        lax.all_to_all(
            grad_q_block.astype(jnp.bfloat16), ULY, split_axis=1, concat_axis=2, tiled=True
        ).astype(grad_q_block.dtype),
        lax.all_to_all(
            grad_k_block.astype(jnp.bfloat16), ULY, split_axis=1, concat_axis=2, tiled=True
        ).astype(grad_k_block.dtype),
        lax.all_to_all(
            grad_v_block.astype(jnp.bfloat16), ULY, split_axis=1, concat_axis=2, tiled=True
        ).astype(grad_v_block.dtype),
    )
    grad_q_normed = rotate(grad_q_seq, local_angles, -1.0)
    grad_k_normed = rotate(grad_k_seq, local_angles, -1.0)
    q_gain_term = jnp.sum(grad_q_normed * q_pre * q_scale, axis=(0, 1, 2))
    k_gain_term = jnp.sum(grad_k_normed * key_before_norm * k_scale, axis=(0, 1, 2))
    grad_q_pre = (
        norm_back(grad_q_normed, q_pre, q_scale, gain_q)
        .astype(jnp.bfloat16)
        .reshape(sequence_count, token_count, QUERY_HEADS * HEAD_SIZE)
    )
    grad_k_pre = (
        norm_back(grad_k_normed, key_before_norm, k_scale, gain_k)
        .astype(jnp.bfloat16)
        .reshape(sequence_count, token_count, KEY_VALUE_HEADS * HEAD_SIZE)
    )
    value_pre_gradient = value_sequence_gradient.astype(jnp.bfloat16).reshape(
        sequence_count, token_count, KEY_VALUE_HEADS * HEAD_SIZE
    )
    grad_query = jnp.einsum(
        EQ_STD_STE_TO_DE, normalized_input, grad_q_pre, preferred_element_type=jnp.float32
    )
    grad_key = jnp.einsum(
        EQ_STD_STE_TO_DE, normalized_input, grad_k_pre, preferred_element_type=jnp.float32
    )
    grad_value = jnp.einsum(
        EQ_STD_STE_TO_DE, normalized_input, value_pre_gradient, preferred_element_type=jnp.float32
    )
    grad_normed = jnp.einsum(EQ_STE_DE_TO_STD, grad_q_pre, wq_all, preferred_element_type=jnp.float32)
    grad_normed = grad_normed + jnp.einsum(
        EQ_STE_DE_TO_STD, grad_k_pre, wk_all, preferred_element_type=jnp.float32
    )
    grad_normed = grad_normed + jnp.einsum(
        EQ_STE_DE_TO_STD, value_pre_gradient, wv_all, preferred_element_type=jnp.float32
    )
    attn_gain_term = jnp.sum(grad_normed * source * first_scale, axis=(0, 1))
    grad_hidden = grad_middle + norm_back(
        grad_normed, source, first_scale, g_attn.astype(jnp.float32)
    )
    grad_down = jnp.einsum(EQ_STF_STD_TO_FD, activated, cotangent, preferred_element_type=jnp.float32)
    grad_attn_gain, grad_query, grad_key, grad_value, grad_out, grad_down = (
        lax.psum_scatter(attn_gain_term, EVERY, scatter_dimension=0, tiled=True),
        lax.psum_scatter(grad_query, EVERY, scatter_dimension=0, tiled=True),
        lax.psum_scatter(grad_key, EVERY, scatter_dimension=0, tiled=True),
        lax.psum_scatter(grad_value, EVERY, scatter_dimension=0, tiled=True),
        lax.psum_scatter(grad_out, EVERY, scatter_dimension=0, tiled=True),
        lax.psum_scatter(grad_down, EVERY, scatter_dimension=0, tiled=True),
    )
    grad_q_gain, grad_k_gain = lax.psum((q_gain_term, k_gain_term), EVERY)
    return (
        output,
        grad_hidden,
        grad_attn_gain,
        grad_query,
        grad_key,
        grad_value,
        grad_out,
        grad_q_gain,
        grad_k_gain,
        grad_mlp_gain,
        grad_gate,
        grad_up,
        grad_down,
    )


MESH = pl.DeviceIdType.MESH
HBM = pl.BlockSpec(memory_space=pltpu.HBM)
VMEM = pl.BlockSpec(memory_space=pltpu.VMEM)
MIB = 1 << 20


def kernel_params(collective_id, vmem_mib=62):
    return pltpu.CompilerParams(
        collective_id=collective_id, has_side_effects=True, vmem_limit_bytes=vmem_mib * MIB
    )


def semaphores(count, local=16):
    return [
        pltpu.SemaphoreType.DMA((count,)),
        pltpu.SemaphoreType.DMA((count,)),
        pltpu.SemaphoreType.DMA((local,)),
    ]


class Copy:
    def __init__(self, descriptor, sends, receives):
        self.descriptor, self.sends, self.receives = descriptor, sends, receives

    def under(self, condition, action):
        if condition is None:
            action()
        else:
            pl.when(condition)(action)

    def start(self):
        self.under(self.sends, lambda: self.descriptor().start())
        return self

    def sent(self):
        self.under(self.sends, lambda: self.descriptor().wait_send())

    def arrived(self):
        self.under(self.receives, lambda: self.descriptor().wait_recv())


class Links:
    def __init__(self, send, recv, here):
        self.send, self.recv, self.here = send, recv, here
        self.used, self.used_here = 0, 0
        self.copies, self.local_copies = [], []
        self.n_dp, self.n_blk, self.n_uly = (lax.axis_size(a) for a in EVERY)
        self.dp, self.blk, self.uly = (lax.axis_index(a) for a in EVERY)
        self.other_dp = 1 - self.dp
        self.across = lax.rem(self.uly + 2, 4)
        self.twin = self.uly + 1 - 2 * lax.rem(self.uly, 2)
        self.x_way = (self.other_dp, self.blk, self.uly)
        self.y_way = (self.dp, self.blk, self.across)
        self.core_way = (self.dp, self.blk, self.twin)

    def peer(self, step):
        return lax.rem(self.blk + step, self.n_blk)

    def peers(self):
        return [(self.dp, self.peer(k), self.uly) for k in range(1, self.n_blk)]

    def far_first(self):
        last = self.n_blk - 1
        orders = [
            sorted((p for p in range(self.n_blk) if p != b), key=lambda p, b=b: -abs(p - b))
            for b in range(self.n_blk)
        ]
        for b, order in enumerate(orders):
            ways = [[p for p in order if p > b], [p for p in order if p < b]]
            ways.sort(key=lambda way: -len(way))
            merged = []
            while ways[0] or ways[1]:
                for way in ways:
                    if way:
                        merged.append(way.pop(0))
            orders[b] = merged
        peers = []
        for turn in range(last):
            peer = jnp.int32(0)
            for b, order in enumerate(orders):
                peer = jnp.where(self.blk == b, order[turn], peer)
            peers.append(peer)
        return peers

    def swap(self, pieces_for):
        base, count = self.used, 0
        for peer in self.far_first():
            pieces = pieces_for(peer)
            count = len(pieces)
            distance = lax.rem(peer - self.blk + self.n_blk, self.n_blk) - 1
            for number, (source, target) in enumerate(pieces):
                self.swap_copy(base + distance * count + number, source, target, peer).start()
        self.used = base + (self.n_blk - 1) * count
        waits = []
        for slot in range(base, self.used):
            source, target = pieces_for(self.blk)[(slot - base) % count]

            def descriptor(slot=slot, source=source, target=target):
                return self.swap_copy(slot, source, target, self.peer(1))

            copy = Copy(descriptor, None, None)
            self.copies.append(copy)
            waits.append(copy)
        return waits

    def swap_copy(self, slot, source, target, peer):
        return pltpu.make_async_remote_copy(
            src_ref=source,
            dst_ref=target,
            send_sem=self.send.at[slot],
            recv_sem=self.recv.at[slot],
            device_id=(self.dp, peer, self.uly),
            device_id_type=MESH,
        )

    def greet(self, devices):
        barrier = pltpu.get_barrier_semaphore()
        for device in devices:
            pl.semaphore_signal(barrier, inc=1, device_id=device, device_id_type=MESH)
        pl.semaphore_wait(barrier, len(devices))

    def remote(self, source, target, device, sends=None, receives=None):
        slot = self.used
        self.used += 1

        def descriptor():
            return pltpu.make_async_remote_copy(
                src_ref=source(),
                dst_ref=target(),
                send_sem=self.send.at[slot],
                recv_sem=self.recv.at[slot],
                device_id=device,
                device_id_type=MESH,
            )

        copy = Copy(descriptor, sends, receives)
        self.copies.append(copy)
        return copy.start()

    def to(self, source, target, device):
        return self.remote(lambda: source, lambda: target, device)

    def local(self, source, target):
        copy = pltpu.make_async_copy(source, target, self.here.at[self.used_here])
        self.used_here += 1
        copy.start()
        self.local_copies.append(copy)
        return copy

    def finish(self):
        for copy in self.copies:
            copy.sent()


class LineGather:
    def __init__(self, links, own, whole):
        self.links, self.own, self.whole = links, own, whole
        self.waiting = []

    def send(self, step):
        links, whole = self.links, self.whole
        blk, last = links.blk, links.n_blk - 1

        def block(index):
            if step == 0:
                return lambda: self.own
            return lambda: whole.at[index]

        self.waiting = [
            links.remote(
                block(blk - step),
                lambda: whole.at[blk - step],
                (links.dp, blk + 1, links.uly),
                jnp.logical_and(blk >= step, blk < last),
                blk >= step + 1,
            ),
            links.remote(
                block(blk + step),
                lambda: whole.at[blk + step],
                (links.dp, blk - 1, links.uly),
                jnp.logical_and(blk + step <= last, blk > 0),
                blk + step + 1 <= last,
            ),
        ]

    def arrived(self):
        for copy in self.waiting:
            copy.arrived()


def halves(tokens):
    return [pl.ds(0, tokens // 2), pl.ds(tokens // 2, tokens // 2)]


class HalvedLine:
    def __init__(self, links, own, whole):
        self.lines = [
            LineGather(links, None if own is None else own.at[rows], whole.at[:, rows])
            for rows in halves(whole.shape[1])
        ]

    def send(self, step):
        for line in self.lines:
            line.send(step)

    def advance(self, step):
        for line in self.lines:
            line.arrived()
            line.send(step)

    def arrived(self):
        for line in self.lines:
            line.arrived()


class PlaneGather:
    def __init__(self, links, at):
        self.links, self.at = links, at

    def start_x(self, own):
        links = self.links
        mine = self.at(links.dp, links.uly)
        self.from_x = links.to(own, mine, links.x_way)
        self.from_core = [links.to(own, mine, links.core_way)]

    def start_y(self, own):
        links = self.links
        self.from_y = links.to(own, self.at(links.dp, links.uly), links.y_way)

    def start(self, own=None):
        own = self.at(self.links.dp, self.links.uly) if own is None else own
        self.start_x(own)
        self.start_y(own)

    def hand_on(self):
        links, at = self.links, self.at
        self.from_x.arrived()
        half = at(links.other_dp, links.uly, 0)
        self.second_y = links.to(half, half, links.y_way)
        self.from_y.arrived()
        half = at(links.dp, links.across, 1)
        self.second_x = links.to(half, half, links.x_way)
        for chunk in (at(links.other_dp, links.uly), at(links.dp, links.across)):
            self.from_core.append(links.to(chunk, chunk, links.core_way))

    def last(self):
        links = self.links
        self.second_y.arrived()
        self.second_x.arrived()
        chunk = self.at(links.other_dp, links.across)
        self.from_core.append(links.to(chunk, chunk, links.core_way))

    def arrived(self):
        for copy in self.from_core:
            copy.arrived()


def rows_of(whole, blocked):
    def at(dp, uly, half=None):
        part = whole.at[dp, :, uly] if blocked else whole.at[dp, uly]
        if half is None:
            return part
        depth = whole.shape[-2] // 2
        rows = pl.ds(half * depth, depth)
        return part.at[:, rows] if blocked else part.at[rows]

    return at


class ColumnSwap:
    def __init__(self, links, pieces):
        self.links, self.pieces = links, pieces
        self.incoming, self.kept = [], []

    def parts(self, blk):
        links = self.links
        for weight, whole, offset in self.pieces:
            width = weight.shape[-1] // links.n_dp // links.n_blk
            for group in range(links.n_dp):
                start = (group * links.n_blk + blk) * width
                yield (
                    weight.at[:, pl.ds(pl.multiple_of(start, 128), width)],
                    whole.at[links.blk, :, pl.ds(offset + group * width, width)],
                )

    def start(self):
        links = self.links
        self.incoming = links.swap(lambda peer: list(self.parts(peer)))
        for source, target in self.parts(links.blk):
            self.kept.append(links.local(source, target))

    def arrived(self):
        for copy in self.kept:
            copy.wait()
        for copy in self.incoming:
            copy.arrived()


def write_positions(links, span_order, toks, cosine, sine, query_pos, key_pos):
    half_len = toks * links.n_uly // 2

    def first(blk, uly):
        chunk = span_order[2 * blk + lax.div(uly, links.n_uly // 2)]
        return chunk * half_len + lax.rem(uly, links.n_uly // 2) * toks

    lane = lax.broadcasted_iota(jnp.int32, (toks, HEAD_SIZE), 1)
    row = lax.broadcasted_iota(jnp.int32, (toks, HEAD_SIZE), 0)
    upper = lane >= HEAD_SIZE // 2
    step = jnp.where(upper, lane - HEAD_SIZE // 2, lane).astype(jnp.float32)
    inverse = jnp.exp(step * (-2.0 * math.log(ROPE_BASE) / HEAD_SIZE))
    for blk in range(links.n_blk):
        angles = (first(blk, links.uly) + row).astype(jnp.float32) * inverse
        at = slice(blk * toks, (blk + 1) * toks)
        cosine[at, :] = jnp.cos(angles)
        turn = jnp.sin(angles)
        sine[at, :] = jnp.where(upper, turn, -turn)
    lane = lax.broadcasted_iota(jnp.int32, query_pos.shape, 1)
    place = jnp.zeros(query_pos.shape, jnp.int32)
    for start in range(0, query_pos.shape[1], toks):
        blk = start // toks % links.n_blk
        here = jnp.logical_and(lane >= start, lane < start + toks)
        place = jnp.where(here, first(blk, links.uly) + lane - start, place)
    query_pos[...] = place
    row = lax.broadcasted_iota(jnp.int32, (toks, 1), 0)
    for uly in range(links.n_uly):
        for blk in range(links.n_blk):
            start = (uly * links.n_blk + blk) * toks
            key_pos[start : start + toks, :] = row + first(blk, jnp.int32(uly))


def write_gains(links, all_gains, size, targets):
    per_row = 128 // size
    for which, target in enumerate(targets):
        for place in range(target.shape[1] // 128):
            pieces = []
            for part in range(per_row):
                device = place * per_row + part
                plane, uly = device // links.n_uly, device % links.n_uly
                gains = all_gains[plane // links.n_blk, plane % links.n_blk, uly]
                pieces.append(gains.astype(jnp.float32)[which : which + 1, :size])
            target[:, place * 128 : (place + 1) * 128] = jnp.concatenate(pieces, axis=1)


ROWS = 32


def each_block(count, body):
    def step(index, carry):
        body(pl.ds(pl.multiple_of(index * ROWS, ROWS), ROWS))
        return carry

    lax.fori_loop(0, count // ROWS, step, 0)


class LineScatter:
    def __init__(self, links, parts, rightward, leftward):
        self.links, self.parts = links, parts
        self.slots = {1: rightward, -1: leftward}
        self.tokens = parts.shape[1]
        self.number = links.used
        self.last = links.n_blk - 1
        links.used += 2 * self.last

    def target(self, step, way):
        return self.last - step if way == 1 else step

    def slot(self, step, way):
        target = self.target(step, way)
        return self.slots[way].at[target - 1 if way == 1 else target]

    def place(self, way):
        return self.links.blk if way == 1 else self.last - self.links.blk

    def copy(self, step, way, source=None):
        links, slot = self.links, self.slot(step, way)
        number = self.number + 2 * step + (1 if way == 1 else 0)
        return pltpu.make_async_remote_copy(
            src_ref=slot if source is None else source,
            dst_ref=slot,
            send_sem=links.send.at[number],
            recv_sem=links.recv.at[number],
            device_id=(links.dp, links.blk + way, links.uly),
            device_id_type=MESH,
        )

    def start(self):
        for step in range(self.last):
            for way in (1, -1):

                @pl.when(self.place(way) == 0)
                def _(step=step, way=way):
                    self.copy(step, way, self.parts.at[self.target(step, way)]).start()

    def tick(self, tick):
        for way in (1, -1):

            @pl.when(jnp.logical_and(self.place(way) >= 1, self.place(way) <= tick))
            def _(way=way):
                step = tick - self.place(way)
                self.copy(step, way).wait_recv()
                slot, target = self.slot(step, way), self.target(step, way)

                def body(rows):
                    slot[rows, :] = slot[rows, :] + self.parts[target, rows, :]

                each_block(self.tokens, body)
                self.copy(step, way).start()

    def finish(self, total):
        blk, last = self.links.blk, self.last

        def start(rows):
            total[rows, :] = self.parts[blk, rows, :].astype(jnp.float32)

        each_block(self.tokens, start)
        for way in (1, -1):

            @pl.when(self.place(way) >= 1)
            def _(way=way):
                step = last - self.place(way)
                self.copy(step, way).wait_recv()
                slot = self.slot(step, way)

                def body(rows):
                    total[rows, :] = total[rows, :] + slot[rows, :].astype(jnp.float32)

                each_block(self.tokens, body)

    def sent(self):
        for step in range(self.last):
            for way in (1, -1):
                beyond = self.place(way) + step < self.last
                pl.when(beyond)(lambda step=step, way=way: self.copy(step, way).wait_send())


def halved_sums(links, parts, rightward, leftward):
    return [
        LineScatter(links, parts.at[:, rows], rightward.at[:, rows], leftward.at[:, rows])
        for rows in halves(parts.shape[1])
    ]


class DirectSum:
    def __init__(self, links, parts, slots):
        self.links, self.parts, self.slots = links, parts, slots

    def start(self):
        links = self.links
        self.waits = links.swap(lambda peer: [(self.parts.at[peer], self.slots.at[links.blk])])

    def finish(self, total):
        links, parts, slots = self.links, self.parts, self.slots
        for copy in self.waits:
            copy.arrived()

        def body(rows):
            value = parts[links.blk, rows, :].astype(jnp.float32)
            for step in range(1, links.n_blk):
                value = value + slots[links.peer(step), rows, :].astype(jnp.float32)
            total[rows, :] = value

        each_block(parts.shape[1], body)


class OutputHalf:
    def __init__(self, links, which, parts, middle, slots, total):
        rows = halves(middle.shape[0])[which]
        self.middle, self.total = middle.at[rows], total
        if len(slots) == 1:
            self.sum = DirectSum(links, parts.at[:, rows], *slots)
        else:
            self.sum = LineScatter(links, parts.at[:, rows], *slots)

    def write(self, output):
        self.sum.finish(self.total)

        def body(rows):
            output[rows, :] = (self.middle[rows, :] + self.total[rows, :]).astype(jnp.bfloat16)

        each_block(self.middle.shape[0], body)


def output_scratch(n_blk, tokens, width):
    return line_scratch(n_blk, tokens // 2, width) + [
        pltpu.VMEM((tokens // 2, width), jnp.float32)
    ]


def line_scratch(n_blk, tokens, width):
    return [pltpu.VMEM((n_blk - 1, tokens, width), jnp.bfloat16)] * 2


class PlaneScatter:
    def __init__(self, links, parts, from_core, from_x, from_y, last_x, last_y):
        self.links, self.parts = links, parts
        self.own_core_only = from_core is None
        self.from_core, self.from_x, self.from_y = from_core, from_x, from_y
        self.last_x, self.last_y = last_x, last_y
        self.core = lax.rem(links.uly, 2)
        self.row = lax.div(links.uly, 2)
        self.depth = parts.shape[3]
        self.core_copies = {}

    def chunk(self, dp, row, core, half=None):
        if self.own_core_only:
            part = self.parts.at[dp, row]
        else:
            part = self.parts.at[dp, :, row * 2 + core]
        if half is None:
            return part
        depth = self.depth // 2
        return part.at[:, pl.ds(half * depth, depth)]

    def add(self, target, source):
        blocks, depth, _ = target.shape
        rows = 32 if depth % 32 == 0 else 16

        def body(index, carry):
            block = lax.div(index, depth // rows)
            at = pl.ds(pl.multiple_of(lax.rem(index, depth // rows) * rows, rows), rows)
            target[block, at, :] = target[block, at, :] + source[block, at, :]
            return carry

        lax.fori_loop(0, blocks * (depth // rows), body, 0)

    def between_cores(self, which):
        links = self.links
        dp = links.dp if which == 1 else links.other_dp
        self.core_copies[which] = [
            links.to(
                self.chunk(dp, row, 1 - self.core), self.from_core.at[which, row], links.core_way
            )
            for row in range(2)
        ]

    def core_sums(self, which):
        links = self.links
        dp = links.dp if which == 1 else links.other_dp
        for row in range(2):
            self.core_copies[which][row].arrived()
            self.add(self.chunk(dp, row, self.core), self.from_core.at[which, row])

    def across_chips(self):
        links = self.links
        if not self.own_core_only:
            self.core_sums(0)
        self.x_copies = [
            links.to(
                self.chunk(links.other_dp, row, self.core, 0), self.from_x.at[row], links.x_way
            )
            for row in range(2)
        ]
        if not self.own_core_only:
            self.core_sums(1)
        self.y_copies = [
            links.to(
                self.chunk(group, 1 - self.row, self.core, 1),
                self.from_y.at[group],
                links.y_way,
            )
            for group in range(links.n_dp)
        ]

    def second_way(self):
        links = self.links
        for row in range(2):
            self.x_copies[row].arrived()
            self.add(self.chunk(links.dp, row, self.core, 0), self.from_x.at[row])
        self.y_last = links.to(
            self.chunk(links.dp, 1 - self.row, self.core, 0), self.last_y, links.y_way
        )
        for group in range(links.n_dp):
            self.y_copies[group].arrived()
            self.add(self.chunk(group, self.row, self.core, 1), self.from_y.at[group])
        self.x_last = links.to(
            self.chunk(links.other_dp, self.row, self.core, 1), self.last_x, links.x_way
        )

    def result(self, write):
        links = self.links
        for half, copy, source in ((0, self.y_last, self.last_y), (1, self.x_last, self.last_x)):
            copy.arrived()
            own = self.chunk(links.dp, self.row, self.core, half)
            blocks, depth, _ = source.shape
            rows = 32 if depth % 32 == 0 else 16

            def body(index, carry, own=own, source=source, half=half, depth=depth, rows=rows):
                block = lax.div(index, depth // rows)
                start = pl.multiple_of(lax.rem(index, depth // rows) * rows, rows)
                at = pl.ds(start, rows)
                value = own[block, at, :].astype(jnp.float32)
                value = value + source[block, at, :].astype(jnp.float32)
                write(block, pl.ds(pl.multiple_of(start + half * depth, rows), rows), value)
                return carry

            lax.fori_loop(0, blocks * (depth // rows), body, 0)


def plane_shapes(n_dp, blocks, n_uly, depth, width):
    return [
        (n_dp, blocks, n_uly, depth, width),
        (n_dp, 2, blocks, depth, width),
        (2, blocks, depth // 2, width),
        (n_dp, blocks, depth // 2, width),
        (blocks, depth // 2, width),
        (blocks, depth // 2, width),
    ]


def plane_scratch(*sizes):
    return [pltpu.VMEM(shape, jnp.bfloat16) for shape in plane_shapes(*sizes)]


def weight_grad(rows, right, parts, dp):
    _, blocks, n_uly, depth, width = parts.shape
    columns = 512

    def body(index, carry):
        at = pl.ds(pl.multiple_of(index * columns, columns), columns)
        part = jnp.dot(rows[...], right[:, at], preferred_element_type=jnp.float32)
        parts[dp, :, :, :, at] = part.astype(jnp.bfloat16).reshape(blocks, n_uly, depth, columns)
        return carry

    lax.fori_loop(0, width // columns, body, 0)


def rows_turned(left, parts, dp):
    count = parts.shape[1] * parts.shape[2] * parts.shape[3]
    return left[:, pl.ds(pl.multiple_of(dp * count, 128), count)].T


def turned(rows, cosine, sine):
    return rows * cosine + pltpu.roll(rows, HEAD_SIZE // 2, axis=1) * sine


def transposed_product(left, right):
    return lax.dot_general(
        left, right, (((0,), (0,)), ((), ())), preferred_element_type=jnp.float32
    )


def product_right(left, right):
    return lax.dot_general(
        left, right, (((1,), (1,)), ((), ())), preferred_element_type=jnp.float32
    )


SCORE_SCALE = 1.0 / math.sqrt(HEAD_SIZE)


def forward_kernel(
    toks,
    gain_rows,
    span_order,
    hidden,
    wq,
    wk,
    wv,
    wo,
    wg,
    wu,
    wd,
    cotangent,
    gains,
    q_gain,
    k_gain,
    all_qkv,
    all_wo,
    all_wg,
    all_wu,
    all_wd,
    all_cot,
    attn_gain,
    mlp_gain,
    cosine,
    sine,
    query_pos,
    key_pos,
    heads,
    normed,
    qkv,
    queries,
    key_values,
    lse,
    middle,
    all_normed,
    all_gains,
    all_hidden,
    near_qkv,
    near_wo,
    parts,
    rightward,
    leftward,
    own_normed,
    send,
    recv,
    here,
):
    links = Links(send, recv, here)
    links.greet(links.peers() + [links.x_way, links.y_way, links.core_way])
    tokens, width = hidden.shape
    spans = halves(tokens)
    q_width, k_width = wq.shape[1] // links.n_blk, wk.shape[1] // links.n_blk
    chunk = all_qkv.at[links.dp, :, links.uly]
    swap = ColumnSwap(
        links, [(wq, chunk, 0), (wk, chunk, q_width), (wv, chunk, q_width + k_width)]
    )
    plane_wo = PlaneGather(links, rows_of(all_wo, False))
    plane_wd = PlaneGather(links, rows_of(all_wd, False))
    plane_qkv = PlaneGather(links, rows_of(all_qkv, True))
    plane_gain = PlaneGather(links, rows_of(all_gains, True))
    swap.start()
    my_gains = all_gains.at[links.dp, links.blk, links.uly]
    gain_swap = [links.to(gains, my_gains, device) for device in links.peers()]
    plane_wo.start(wo)
    line = HalvedLine(links, hidden, all_hidden)
    line.send(0)
    keep = [
        links.local(gains, my_gains),
        links.local(hidden, all_hidden.at[links.blk]),
        links.local(wo, all_wo.at[links.dp, links.uly]),
        links.local(wd, all_wd.at[links.dp, links.uly]),
        links.local(cotangent, all_cot.at[links.blk]),
    ]
    write_positions(links, span_order, toks, cosine, sine, query_pos, key_pos)
    swap.arrived()
    plane_qkv.start()
    keep[0].wait()
    for copy in gain_swap:
        copy.arrived()
    plane_gain.start()
    plane_wd.start(wd)
    plane_wo.hand_on()
    line.advance(1)
    plane_qkv.hand_on()
    plane_gain.hand_on()
    plane_wo.last()
    for step in range(2, links.n_blk - 1):
        line.advance(step)
    pairs = [(wg, all_wg), (wu, all_wu)]
    planes = [PlaneGather(links, rows_of(whole, True)) for _, whole in pairs]
    swaps = [
        ColumnSwap(links, [(weight, whole.at[links.dp, :, links.uly], 0)])
        for weight, whole in pairs
    ]
    for swap in swaps:
        swap.start()
    cot_lines = HalvedLine(links, cotangent, all_cot).lines
    for half in cot_lines:
        half.send(0)
    plane_qkv.last()
    plane_gain.last()
    plane_gain.arrived()
    write_gains(links, all_gains, gain_rows, (attn_gain, mlp_gain))
    for copy in keep[1:]:
        copy.wait()
    plane_wo.arrived()
    plane_qkv.arrived()
    near = [links.local(all_qkv, near_qkv), links.local(all_wo, near_wo)]
    seqs, kv_heads, q_rows, _ = queries.shape
    q_len = key_values.shape[4]
    group = q_rows // q_len
    q_end = kv_heads * group * HEAD_SIZE
    k_end = q_end + kv_heads * HEAD_SIZE

    def norm(seq):
        def body(rows):
            for blk in range(links.n_blk):
                at = pl.ds(pl.multiple_of(seq * toks + rows.start, ROWS), ROWS)
                to = pl.ds(pl.multiple_of(seq * q_len + blk * toks + rows.start, ROWS), ROWS)
                source = all_hidden[blk, at, :].astype(jnp.float32)
                normed[to, :] = (source * rms_scale(source) * attn_gain[...]).astype(
                    jnp.bfloat16
                )

        each_block(toks, body)

    def rotated(seq, column, gain):
        pre = qkv[seq * q_len : (seq + 1) * q_len, column : column + HEAD_SIZE]
        gain = gain[...].astype(jnp.float32)
        return turned(pre * rms_scale(pre) * gain, cosine[...], sine[...]).astype(jnp.bfloat16)

    def project(seq):
        rows = slice(seq * q_len, (seq + 1) * q_len)
        for column in range(0, qkv.shape[1], 512):
            weight = near_qkv[:, :, :, :, column : column + 512].reshape(width, 512)
            qkv[rows, column : column + 512] = jnp.dot(
                normed[rows, :], weight, preferred_element_type=jnp.float32
            )
        for head in range(kv_heads):
            column = head * HEAD_SIZE
            key_values[links.uly, 0, seq, head] = rotated(seq, q_end + column, k_gain)
            key_values[links.uly, 1, seq, head] = qkv[
                rows, k_end + column : k_end + column + HEAD_SIZE
            ].astype(jnp.bfloat16)
        mine = key_values.at[links.uly, :, seq]
        copies = [links.to(mine, mine, way) for way in (links.core_way, links.y_way)]
        for head in range(kv_heads * group):
            at = pl.ds((head % group) * q_len, q_len)
            queries[seq, head // group, at, :] = rotated(seq, head * HEAD_SIZE, q_gain)
        return copies

    def hand_keys(seq, copies):
        copies[1].arrived()
        theirs = key_values.at[links.across, :, seq]
        copies.append(links.to(theirs, theirs, links.core_way))

    def attend(seq, head):
        def over_keys(piece, carry):
            total, mixed = carry
            rows = pl.ds(pl.multiple_of(piece * q_len, q_len), q_len)
            scores = product_right(key_values[piece, 0, seq, head], queries[seq, head])
            weights = jnp.where(
                query_pos[...] >= key_pos[rows, :], jnp.exp(scores * SCORE_SCALE), 0.0
            )
            total = total + jnp.sum(weights, axis=0, keepdims=True)
            mixed = mixed + transposed_product(
                key_values[piece, 1, seq, head], weights.astype(jnp.bfloat16)
            )
            return total, mixed

        total, mixed = lax.fori_loop(
            0,
            links.n_uly,
            over_keys,
            (
                jnp.zeros((1, q_rows), jnp.float32),
                jnp.zeros((HEAD_SIZE, q_rows), jnp.float32),
            ),
        )
        lse[seq * kv_heads + head] = jnp.log(total)
        attended = (mixed / total).T.astype(jnp.bfloat16)
        for member in range(group):
            column = (head * group + member) * HEAD_SIZE
            for blk in range(links.n_blk):
                row = (blk * seqs + seq) * toks
                start = member * q_len + blk * toks
                heads[row : row + toks, column : column + HEAD_SIZE] = attended[
                    start : start + toks, :
                ]

    sums = halved_sums(links, parts, rightward, leftward)
    def out_weight():
        return near_wo[...].reshape(heads.shape[1], width)

    def out_parts(seq):
        mixed = jnp.concatenate(
            [
                heads[(blk * seqs + seq) * toks : (blk * seqs + seq + 1) * toks, :]
                for blk in range(links.n_blk)
            ],
            axis=0,
        )
        for column in range(0, width, 512):
            parts[:, spans[seq], column : column + 512] = (
                jnp.dot(
                    mixed,
                    out_weight()[:, column : column + 512],
                    preferred_element_type=jnp.float32,
                )
                .astype(jnp.bfloat16)
                .reshape(links.n_blk, toks, 512)
            )
        sums[seq].start()

    key_copies = []
    for seq in range(seqs):
        line.lines[seq].arrived()
        norm(seq)
        if seq == 0:
            for copy in near:
                copy.wait()
        key_copies.append(project(seq))
    plane_wd.hand_on()
    hand_keys(0, key_copies[0])
    for copy in (key_copies[0][0], key_copies[0][2]):
        copy.arrived()
    attend(0, 0)
    hand_keys(1, key_copies[1])
    for head in range(1, kv_heads):
        attend(0, head)
    out_parts(0)
    swaps[0].arrived()
    planes[0].start()
    for copy in (key_copies[1][0], key_copies[1][2]):
        copy.arrived()
    attend(1, 0)
    sums[0].tick(1)
    for head in range(1, kv_heads):
        attend(1, head)
    out_parts(1)
    swaps[1].arrived()
    planes[1].start()
    later = range(2, links.n_blk - 1)
    for tick in later:
        sums[0].tick(tick)
    for half in cot_lines:
        half.arrived()
        half.send(1)
    plane_wd.last()
    planes[0].hand_on()
    lines = []

    def settle(half, rows_of_half):
        half.finish(middle.at[rows_of_half])

        def body(rows):
            at = pl.ds(pl.multiple_of(rows_of_half.start + rows.start, ROWS), ROWS)
            total = middle[at, :] + all_hidden[links.blk, at, :].astype(jnp.float32)
            middle[at, :] = total
            own_normed[at, :] = (total * rms_scale(total) * mlp_gain[...]).astype(jnp.bfloat16)

        each_block(tokens // 2, body)
        next_line = LineGather(links, own_normed.at[rows_of_half], all_normed.at[:, rows_of_half])
        next_line.send(0)
        lines.append(next_line)

    settle(sums[0], spans[0])
    sums[1].tick(1)
    for tick in later:
        sums[1].tick(tick)
    settle(sums[1], spans[1])
    for step in range(2, links.n_blk - 1):
        for half in cot_lines:
            half.arrived()
            half.send(step)
    last_local = links.local(own_normed, all_normed.at[links.blk])
    planes[1].hand_on()
    planes[0].last()
    for step in range(1, links.n_blk - 1):
        for half in lines:
            half.arrived()
            half.send(step)
    planes[1].last()
    for half in lines + cot_lines:
        half.arrived()
    for plane in [plane_wd] + planes:
        plane.arrived()
    last_local.wait()
    for half in sums:
        half.sent()
    links.finish()


SMEM = pl.BlockSpec(memory_space=pltpu.SMEM)


def forward(
    span_order,
    hidden,
    wq,
    wk,
    wv,
    wo,
    wg,
    wu,
    wd,
    cotangent,
    gains,
    q_gain,
    k_gain,
    seqs,
    gain_rows,
):
    n_dp, n_blk, n_uly = (lax.axis_size(a) for a in EVERY)
    tokens, width = hidden.shape
    toks = tokens // seqs
    rows, q_len = n_blk * tokens, n_blk * toks
    group = QUERY_HEADS // KEY_VALUE_HEADS
    kv_heads = KEY_VALUE_HEADS // n_blk
    q_rows, keys = group * q_len, n_uly * q_len
    columns = (wq.shape[1] + wk.shape[1] + wv.shape[1]) // n_blk
    f32, low, i32 = jnp.float32, jnp.bfloat16, jnp.int32
    ff = wg.shape[1] // n_blk
    far = [
        (n_dp, n_blk, n_uly, wq.shape[0], columns),
        (n_dp, n_uly) + wo.shape,
        (n_dp, n_blk, n_uly, wg.shape[0], ff),
        (n_dp, n_blk, n_uly, wu.shape[0], ff),
        (n_dp, n_uly) + wd.shape,
        (n_blk, tokens, width),
    ]
    near = [
        ((1, width), f32),
        ((1, width), f32),
        ((q_len, HEAD_SIZE), f32),
        ((q_len, HEAD_SIZE), f32),
        ((1, q_rows), i32),
        ((keys, 1), i32),
        ((rows, kv_heads * group * HEAD_SIZE), low),
        ((rows, width), low),
        ((rows, columns), f32),
        ((seqs, kv_heads, q_rows, HEAD_SIZE), low),
        ((n_uly, 2, seqs, kv_heads, q_len, HEAD_SIZE), low),
        ((seqs * kv_heads, 1, q_rows), f32),
        ((tokens, width), f32),
        ((n_blk, tokens, width), low),
    ]
    scratch = [
        ((n_dp, n_blk, n_uly) + gains.shape, low),
        ((n_blk, tokens, width), low),
        (far[0], low),
        (far[1], low),
        ((n_blk, tokens, width), low),
        ((n_blk - 1, tokens, width), low),
        ((n_blk - 1, tokens, width), low),
        ((tokens, width), low),
    ]
    return pl.pallas_call(
        functools.partial(forward_kernel, toks, gain_rows),
        out_shape=[jax.ShapeDtypeStruct(shape, low) for shape in far]
        + [jax.ShapeDtypeStruct(shape, kind) for shape, kind in near],
        in_specs=[SMEM] + [HBM] * 10 + [VMEM] * 2,
        out_specs=[HBM] * len(far) + [VMEM] * len(near),
        scratch_shapes=[pltpu.VMEM(shape, kind) for shape, kind in scratch]
        + semaphores(160, 32),
        compiler_params=kernel_params(0),
    )(span_order, hidden, wq, wk, wv, wo, wg, wu, wd, cotangent, gains, q_gain, k_gain)


def back_rows(grad_normed, source, gain):
    unit = source * rms_scale(source)
    scaled = grad_normed * gain
    return rms_scale(source) * (
        scaled - unit * jnp.mean(scaled * unit, axis=-1, keepdims=True)
    )


def back_kernel(
    grad_parts,
    out_parts,
    middle,
    cotangent,
    gain,
    all_normed,
    grad_gate_pre,
    grad_up_pre,
    activated,
    all_cot,
    output,
    grad_middle,
    all_low,
    grad_gate,
    grad_up,
    part_down,
    rightward,
    leftward,
    out_slots,
    out_total,
    low,
    turned_low,
    gate_1,
    gate_2,
    gate_3,
    gate_4,
    gate_5,
    gate_6,
    up_1,
    up_2,
    up_3,
    up_4,
    up_5,
    up_6,
    down_1,
    down_2,
    send,
    recv,
    here,
):
    links = Links(send, recv, here)
    links.greet(links.peers() + [links.x_way, links.y_way, links.core_way])
    sums = halved_sums(links, grad_parts, rightward, leftward)
    for half in sums:
        half.start()
    out = OutputHalf(links, 0, out_parts, middle, [out_slots], out_total)
    gate = PlaneScatter(links, gate_1, gate_2, gate_3, gate_4, gate_5, gate_6)
    up = PlaneScatter(links, up_1, up_2, up_3, up_4, up_5, up_6)
    down = PlaneScatter(links, down_1, down_2, None, None, None, None)
    tokens = middle.shape[0]
    spans, lines, keep = halves(tokens), [], []

    def compute(plane, which, rows, right):
        dp = links.dp if which == 1 else links.other_dp
        weight_grad(rows, right, plane.parts, dp)
        plane.between_cores(which)

    def turn(which):
        dp = links.dp if which == 1 else links.other_dp
        turned_low[which] = rows_turned(all_normed, gate_1, dp)

    def compute_down(which):
        dp = links.dp if which == 1 else links.other_dp
        compute(down, which, rows_turned(activated, down_1, dp), all_cot)

    def settle(half, rows_of_half):
        half.finish(grad_middle.at[rows_of_half])

        def body(rows):
            at = pl.ds(pl.multiple_of(rows_of_half.start + rows.start, ROWS), ROWS)
            back = back_rows(grad_middle[at, :], middle[at, :], gain[...])
            grad = cotangent[at, :].astype(jnp.float32) + back
            grad_middle[at, :] = grad
            low[at, :] = grad.astype(jnp.bfloat16)

        each_block(tokens // 2, body)
        line = LineGather(links, low.at[rows_of_half], all_low.at[:, rows_of_half])
        line.send(0)
        lines.append(line)

    later = range(2, links.n_blk - 1)
    turn(0)
    compute(gate, 0, turned_low.at[0], grad_gate_pre)
    sums[0].tick(1)
    turn(1)
    compute(gate, 1, turned_low.at[1], grad_gate_pre)
    for tick in later:
        sums[0].tick(tick)
    gate.across_chips()
    settle(sums[0], spans[0])
    compute(up, 0, turned_low.at[0], grad_up_pre)
    sums[1].tick(1)
    compute(up, 1, turned_low.at[1], grad_up_pre)
    for tick in later:
        sums[1].tick(tick)
    up.across_chips()
    settle(sums[1], spans[1])
    out.sum.start()
    keep.append(links.local(low, all_low.at[links.blk]))
    compute_down(0)
    for step in range(1, links.n_blk - 1):
        for line in lines:
            line.arrived()
            line.send(step)
        if step == 1:
            gate.second_way()
            compute_down(1)
    up.second_way()
    for which in (0, 1):
        down.core_sums(which)
    for dp in range(links.n_dp):
        for row in range(2):
            keep.append(links.local(down.chunk(dp, row, down.core), part_down.at[dp, row]))
    for line in lines:
        line.arrived()

    def into(target):
        def write(block, rows, values):
            target[block, rows, :] = values.astype(target.dtype)

        return write

    gate.result(into(grad_gate))
    up.result(into(grad_up))
    out.write(output)
    for copy in keep:
        copy.wait()
    for half in sums:
        half.sent()
    links.finish()


def exchange_back(
    grad_parts,
    out_parts,
    middle,
    cotangent,
    gain,
    all_normed,
    grad_gate_pre,
    grad_up_pre,
    activated,
    all_cot,
):
    n_dp, n_blk, n_uly = (lax.axis_size(a) for a in EVERY)
    _, tokens, width = grad_parts.shape
    ff = grad_gate_pre.shape[1]
    depth = width // (n_dp * n_blk * n_uly)
    down_depth = ff // (n_dp * n_uly)
    return pl.pallas_call(
        back_kernel,
        out_shape=[
            jax.ShapeDtypeStruct((tokens // 2, width), jnp.bfloat16),
            jax.ShapeDtypeStruct((tokens, width), jnp.float32),
            jax.ShapeDtypeStruct((n_blk, tokens, width), jnp.bfloat16),
            jax.ShapeDtypeStruct((n_blk, depth, ff), jnp.bfloat16),
            jax.ShapeDtypeStruct((n_blk, depth, ff), jnp.bfloat16),
            jax.ShapeDtypeStruct((n_dp, 2, 1, down_depth, width), jnp.bfloat16),
        ],
        in_specs=[VMEM] * 10,
        out_specs=[VMEM, VMEM, HBM, VMEM, VMEM, HBM],
        scratch_shapes=line_scratch(n_blk, tokens, width)
        + [
            pltpu.VMEM((n_blk, tokens // 2, width), jnp.bfloat16),
            pltpu.VMEM((tokens // 2, width), jnp.float32),
        ]
        + [
            pltpu.VMEM((tokens, width), jnp.bfloat16),
            pltpu.VMEM((n_dp, width // n_dp, n_blk * tokens), jnp.bfloat16),
        ]
        + plane_scratch(n_dp, n_blk, n_uly, depth, ff) * 2
        + plane_scratch(n_dp, 1, n_uly, down_depth, width)[:2]
        + semaphores(72),
        compiler_params=kernel_params(3),
    )(
        grad_parts,
        out_parts,
        middle,
        cotangent,
        gain,
        all_normed,
        grad_gate_pre,
        grad_up_pre,
        activated,
        all_cot,
    )


def backward_kernel(
    all_low,
    wo,
    queries,
    key_values,
    lse,
    qkv,
    q_gain,
    k_gain,
    cosine,
    sine,
    query_pos,
    key_pos,
    w_qkv,
    hidden,
    grad_middle,
    gain,
    normed,
    heads,
    out_parts,
    middle,
    grad_gate,
    grad_up,
    part_down,
    grad_hidden,
    grad_wo,
    grad_down,
    small_sum,
    output,
    gate_rows,
    up_rows,
    grad_w_qkv,
    grad_qkv,
    gain_terms,
    grad_heads,
    grad_rows,
    grad_kv,
    from_core,
    from_across,
    grad_parts,
    rightward,
    leftward,
    direct,
    summed,
    small_in,
    small_total,
    out_right,
    out_left,
    out_total,
    down_1,
    down_3,
    down_4,
    down_5,
    down_6,
    turned_normed,
    q_1,
    q_2,
    q_3,
    q_4,
    q_5,
    q_6,
    kv_1,
    kv_2,
    kv_3,
    kv_4,
    kv_5,
    kv_6,
    wo_1,
    wo_2,
    wo_3,
    wo_4,
    wo_5,
    wo_6,
    send,
    recv,
    here,
):
    links = Links(send, recv, here)
    links.greet(links.peers() + [links.x_way, links.y_way, links.core_way])
    tokens = hidden.shape[0]
    spans = halves(tokens)
    output_half = OutputHalf(
        links, 1, out_parts, middle, [out_right, out_left], out_total
    )
    output_half.sum.start()
    down = PlaneScatter(links, down_1, None, down_3, down_4, down_5, down_6)
    fetch = links.local(part_down, down_1)
    swapped, keep = [], []
    for source, target in ((grad_gate, gate_rows), (grad_up, up_rows)):
        swapped += links.swap(
            lambda peer, source=source, target=target: [(source.at[peer], target.at[links.blk])]
        )
        keep.append(links.local(source.at[links.blk], target.at[links.blk]))
    fetch.wait()
    down.across_chips()
    sums = [
        LineScatter(links, grad_parts.at[:, spans[0]], rightward, leftward),
        DirectSum(links, grad_parts.at[:, spans[1]], direct),
    ]
    q_sums = PlaneScatter(links, q_1, q_2, q_3, q_4, q_5, q_6)
    kv_sums = PlaneScatter(links, kv_1, kv_2, kv_3, kv_4, kv_5, kv_6)
    wo_sums = PlaneScatter(links, wo_1, wo_2, wo_3, wo_4, wo_5, wo_6)
    seqs, kv_heads, q_rows, _ = queries.shape
    q_len = key_values.shape[4]
    group = q_rows // q_len
    toks = q_len // links.n_blk
    q_end = kv_heads * group * HEAD_SIZE
    k_end = q_end + kv_heads * HEAD_SIZE
    gain_terms[...] = jnp.zeros_like(gain_terms)
    later = range(2, links.n_blk - 1)

    def heads_back(seq):
        low = jnp.concatenate(
            [
                all_low[(blk * seqs + seq) * toks : (blk * seqs + seq + 1) * toks, :]
                for blk in range(links.n_blk)
            ],
            axis=0,
        )
        grad_heads[...] = product_right(low, wo[...])
        for head in range(kv_heads * group):
            to = pl.ds((head % group) * q_len, q_len)
            grad_rows[seq, head // group, to, :] = grad_heads[
                :, head * HEAD_SIZE : (head + 1) * HEAD_SIZE
            ].astype(jnp.bfloat16)

    def back_norm(upstream, seq, column, gain, which):
        rows = slice(seq * q_len, (seq + 1) * q_len)
        pre = qkv[rows, column : column + HEAD_SIZE]
        upstream = turned(upstream, cosine[...], -sine[...])
        gain_terms[which : which + 1, :] += jnp.sum(
            upstream * pre * rms_scale(pre), axis=0, keepdims=True
        )
        grad_qkv[rows, column : column + HEAD_SIZE] = back_rows(
            upstream, pre, gain[...].astype(jnp.float32)
        ).astype(jnp.bfloat16)

    def deltas(seq, head):
        sums_of = []
        for member in range(group):
            column = (head * group + member) * HEAD_SIZE
            attended = jnp.concatenate(
                [
                    heads[row : row + toks, column : column + HEAD_SIZE]
                    for row in ((blk * seqs + seq) * toks for blk in range(links.n_blk))
                ],
                axis=0,
            )
            upstream = grad_rows[seq, head, member * q_len : (member + 1) * q_len, :]
            sums_of.append(attended.astype(jnp.float32) * upstream.astype(jnp.float32))
        terms = jnp.concatenate(sums_of, axis=0)
        high = terms.astype(jnp.bfloat16)
        rest = (terms - high.astype(jnp.float32)).astype(jnp.bfloat16)
        ones = jnp.ones((16, HEAD_SIZE), jnp.bfloat16)
        return (product_right(ones, high) + product_right(ones, rest))[:1, :]

    def back(seq, head):
        delta = deltas(seq, head)

        def over_keys(piece, grad_query):
            rows = pl.ds(pl.multiple_of(piece * q_len, q_len), q_len)
            scores = product_right(key_values[piece, 0, seq, head], queries[seq, head])
            prob = jnp.where(
                query_pos[...] >= key_pos[rows, :],
                jnp.exp(scores * SCORE_SCALE - lse[seq * kv_heads + head]),
                0.0,
            )
            grad_prob = product_right(key_values[piece, 1, seq, head], grad_rows[seq, head])
            grad_score = (prob * (grad_prob - delta)).astype(jnp.bfloat16)
            grad_kv[seq, piece, 0, head] = (
                SCORE_SCALE
                * jnp.dot(grad_score, queries[seq, head], preferred_element_type=jnp.float32)
            ).astype(jnp.bfloat16)
            grad_kv[seq, piece, 1, head] = jnp.dot(
                prob.astype(jnp.bfloat16),
                grad_rows[seq, head],
                preferred_element_type=jnp.float32,
            ).astype(jnp.bfloat16)
            return grad_query + transposed_product(key_values[piece, 0, seq, head], grad_score)

        grad_query = lax.fori_loop(
            0, links.n_uly, over_keys, jnp.zeros((HEAD_SIZE, q_rows), jnp.float32)
        )
        turned_back = (grad_query * SCORE_SCALE).T
        for member in range(group):
            column = (head * group + member) * HEAD_SIZE
            back_norm(
                turned_back[member * q_len : (member + 1) * q_len, :], seq, column, q_gain, 0
            )

    core, line = lax.rem(links.uly, 2), lax.div(links.uly, 2)

    def add(target, source):
        for kind in range(2):
            for head in range(kv_heads):
                target[kind, head] = target[kind, head] + source[kind, head]

    def core_sums(seq):
        return [
            links.to(
                grad_kv.at[seq, row * 2 + 1 - core], from_core.at[seq, row], links.core_way
            )
            for row in range(2)
        ]

    def across_sums(seq, copies):
        for row in range(2):
            copies[row].arrived()
            add(grad_kv.at[seq, row * 2 + core], from_core.at[seq, row])
        return links.to(
            grad_kv.at[seq, (1 - line) * 2 + core], from_across.at[seq], links.y_way
        )

    def own_keys(seq, copy):
        copy.arrived()
        rows = slice(seq * q_len, (seq + 1) * q_len)
        for head in range(kv_heads):
            term = [
                grad_kv[seq, links.uly, kind, head].astype(jnp.float32)
                + from_across[seq, kind, head].astype(jnp.float32)
                for kind in range(2)
            ]
            back_norm(term[0], seq, q_end + head * HEAD_SIZE, k_gain, 1)
            v_at = k_end + head * HEAD_SIZE
            grad_qkv[rows, v_at : v_at + HEAD_SIZE] = term[1].astype(jnp.bfloat16)

    def normed_parts(seq):
        for column in range(0, w_qkv.shape[0], 512):
            grad_parts[:, spans[seq], column : column + 512] = (
                product_right(
                    grad_qkv[seq * q_len : (seq + 1) * q_len, :],
                    w_qkv[column : column + 512, :],
                )
                .astype(jnp.bfloat16)
                .reshape(links.n_blk, toks, 512)
            )
        sums[seq].start()

    def dp_of(which):
        return links.dp if which == 1 else links.other_dp

    def compute_wo(which):
        dp = dp_of(which)
        weight_grad(rows_turned(heads, wo_1, dp), all_low, wo_1, dp)
        wo_sums.between_cores(which)

    def compute_qkv(plane, which, columns):
        weight_grad(
            turned_normed.at[which], grad_qkv.at[:, columns], plane.parts, dp_of(which)
        )
        plane.between_cores(which)

    q_columns, kv_columns = pl.ds(0, q_end), pl.ds(q_end, grad_qkv.shape[1] - q_end)
    heads_back(0)
    back(0, 0)
    output_half.sum.tick(1)
    for head in range(1, kv_heads):
        back(0, head)
    core_copies = core_sums(0)
    heads_back(1)
    down.second_way()
    for which in range(2):
        turned_normed[which] = rows_turned(normed, q_1, dp_of(which))
    back(1, 0)
    across = across_sums(0, core_copies)
    for tick in later:
        output_half.sum.tick(tick)
    for head in range(1, kv_heads):
        back(1, head)
    core_copies = core_sums(1)
    own_keys(0, across)
    across = across_sums(1, core_copies)
    normed_parts(0)
    compute_qkv(q_sums, 0, q_columns)
    compute_qkv(q_sums, 1, q_columns)
    own_keys(1, across)
    small_total[0] = gain_terms[...]
    pending = links.to(small_total.at[0], small_in.at[links.n_blk], links.core_way)
    q_sums.across_chips()
    normed_parts(1)
    sums[0].tick(1)
    compute_qkv(kv_sums, 0, kv_columns)
    compute_qkv(kv_sums, 1, kv_columns)
    for tick in later:
        sums[0].tick(tick)
    pending.arrived()
    small_total[1] = small_total[0] + small_in[links.n_blk]
    pending = links.to(small_total.at[1], small_in.at[links.n_blk + 1], links.x_way)
    kv_sums.across_chips()
    q_sums.second_way()
    compute_wo(0)
    compute_wo(1)
    pending.arrived()
    small_total[2] = small_total[1] + small_in[links.n_blk + 1]
    pending = links.to(small_total.at[2], small_in.at[links.n_blk + 2], links.y_way)
    kv_sums.second_way()
    wo_sums.across_chips()

    def into(target):
        def write(block, rows, values):
            target[block, rows, :] = values.astype(target.dtype)

        return write

    def give_home(plane, columns):
        here, there = summed.at[:, :, columns], grad_w_qkv.at[links.blk, :, columns]
        plane.result(into(here))
        keep.append(links.local(here.at[links.blk], there))
        return links.swap(lambda peer: [(here.at[peer], there)])

    swapped += give_home(q_sums, q_columns)
    pending.arrived()
    small_in[links.blk] = small_total[2] + small_in[links.n_blk + 2]
    mine = small_in.at[links.blk]
    small_copies = [links.to(mine, mine, device) for device in links.peers()]
    swapped += give_home(kv_sums, kv_columns)
    output_half.write(output)

    def settle(seq):
        sums[seq].finish(grad_hidden.at[spans[seq]])

        def body(rows):
            at = pl.ds(pl.multiple_of(spans[seq].start + rows.start, ROWS), ROWS)
            back = back_rows(grad_hidden[at, :], hidden[at, :].astype(jnp.float32), gain[...])
            grad_hidden[at, :] = grad_middle[at, :] + back

        each_block(toks, body)

    settle(0)
    wo_sums.second_way()
    down.result(into(grad_down))
    settle(1)
    wo_sums.result(into(grad_wo))
    for copy in small_copies:
        copy.arrived()
    total = small_in[0]
    for blk in range(1, links.n_blk):
        total = total + small_in[blk]
    small_sum[...] = total
    for copy in swapped:
        copy.arrived()
    for copy in keep:
        copy.wait()
    sums[0].sent()
    output_half.sum.sent()
    links.finish()


def backward(
    all_low,
    wo,
    queries,
    key_values,
    lse,
    qkv,
    q_gain,
    k_gain,
    cosine,
    sine,
    query_pos,
    key_pos,
    w_qkv,
    hidden,
    grad_middle,
    gain,
    normed,
    heads,
    out_parts,
    middle,
    grad_gate,
    grad_up,
    part_down,
):
    seqs, kv_heads, q_rows, _ = queries.shape
    n_uly, _, _, _, q_len, _ = key_values.shape
    n_blk, tokens, width = out_parts.shape
    n_dp, _, _, down_depth, _ = part_down.shape
    columns = qkv.shape[1]
    depth = width // (n_dp * n_blk * n_uly)
    out_depth = heads.shape[1] // (n_dp * n_uly)
    f32, low = jnp.float32, jnp.bfloat16
    small = (8, HEAD_SIZE)
    outs = [
        ((tokens, width), f32),
        ((1, out_depth, width), f32),
        ((1, down_depth, width), f32),
        (small, f32),
        ((tokens // 2, width), low),
        (grad_gate.shape, low),
        (grad_up.shape, low),
        ((n_blk, depth, columns), low),
    ]
    scratch = [
        (qkv.shape, low),
        (small, f32),
        ((q_len, heads.shape[1]), f32),
        (queries.shape, low),
        ((seqs, n_uly, 2, kv_heads, q_len, HEAD_SIZE), low),
        ((seqs, 2, 2, kv_heads, q_len, HEAD_SIZE), low),
        ((seqs, 2, kv_heads, q_len, HEAD_SIZE), low),
        (out_parts.shape, low),
        ((n_blk - 1, tokens // 2, width), low),
        ((n_blk - 1, tokens // 2, width), low),
        ((n_blk, tokens // 2, width), low),
        ((n_blk, depth, columns), low),
        ((n_blk + 3,) + small, f32),
        ((3,) + small, f32),
    ]
    down = [part_down.shape] + plane_shapes(n_dp, 1, n_uly, down_depth, width)[2:]
    return pl.pallas_call(
        backward_kernel,
        out_shape=[jax.ShapeDtypeStruct(shape, kind) for shape, kind in outs],
        in_specs=[VMEM] * 20 + [HBM] * 3,
        out_specs=[VMEM] * 5 + [HBM] * 3,
        scratch_shapes=[pltpu.VMEM(shape, kind) for shape, kind in scratch]
        + output_scratch(n_blk, tokens, width)
        + [pltpu.VMEM(shape, low) for shape in down]
        + [pltpu.VMEM((n_dp, width // n_dp, normed.shape[0]), low)]
        + plane_scratch(n_dp, n_blk, n_uly, depth, heads.shape[1])
        + plane_scratch(n_dp, n_blk, n_uly, depth, columns - heads.shape[1])
        + plane_scratch(n_dp, 1, n_uly, out_depth, width)
        + semaphores(112),
        compiler_params=kernel_params(4),
    )(
        all_low,
        wo,
        queries,
        key_values,
        lse,
        qkv,
        q_gain,
        k_gain,
        cosine,
        sine,
        query_pos,
        key_pos,
        w_qkv,
        hidden,
        grad_middle,
        gain,
        normed,
        heads,
        out_parts,
        middle,
        grad_gate,
        grad_up,
        part_down,
    )


def finish_kernel(
    gate,
    up,
    qkv,
    wo,
    wd,
    hidden,
    out_0,
    out_1,
    w_gate,
    w_up,
    w_query,
    key_weight,
    value_weight,
    attn_gain,
    mlp_gain,
    small,
    f_gate,
    f_up,
    f_q,
    f_k,
    f_v,
    f_wo,
    f_wd,
    f_hidden,
    f_out,
    f_attn,
    f_mlp,
    f_q_gain,
    f_k_gain,
):
    n_blk, depth, _ = gate.shape

    def place(source, offset, target):
        width = target.shape[1] // (n_blk * 2)
        for blk in range(n_blk):
            for group in range(2):
                to = (group * n_blk + blk) * width
                at = offset + group * width
                target[:, to : to + width] = source[blk, :, at : at + width].astype(jnp.float32)

    def gain_back(pairs, gain):
        total = jnp.zeros((depth, 128), jnp.float32)
        for weight, grad in pairs:
            for column in range(0, weight.shape[1], 128):
                at = slice(column, column + 128)
                total = total + weight[:, at].astype(jnp.float32) * grad[:, at]
        column = jnp.sum(total, axis=1, keepdims=True)
        square = (depth, depth)
        same = lax.broadcasted_iota(jnp.int32, square, 0) == lax.broadcasted_iota(
            jnp.int32, square, 1
        )
        return jnp.sum(jnp.where(same, column, 0.0), axis=0, keepdims=True) / gain[
            ...
        ].astype(jnp.float32)

    place(gate, 0, f_gate)
    place(up, 0, f_up)
    q_width = f_q.shape[1] // n_blk
    k_width = f_k.shape[1] // n_blk
    place(qkv, 0, f_q)
    place(qkv, q_width, f_k)
    place(qkv, q_width + k_width, f_v)
    f_q_gain[...] = small[0:1, :]
    f_k_gain[...] = small[1:2, :]
    f_wo[...] = wo[0]
    f_wd[...] = wd[0]
    f_hidden[...] = hidden[...]
    half = out_0.shape[0]
    f_out[:half, :] = out_0[...]
    f_out[half:, :] = out_1[...]
    f_attn[...] = gain_back(((w_query, f_q), (key_weight, f_k), (value_weight, f_v)), attn_gain)
    f_mlp[...] = gain_back(((w_gate, f_gate), (w_up, f_up)), mlp_gain)


def finish(gate, up, qkv, wo, wd, hidden, out_0, out_1, weights, gains, small):
    return pl.pallas_call(
        finish_kernel,
        out_shape=[jax.ShapeDtypeStruct(w.shape, jnp.float32) for w in weights]
        + [
            jax.ShapeDtypeStruct(wo.shape[1:], jnp.float32),
            jax.ShapeDtypeStruct(wd.shape[1:], jnp.float32),
            jax.ShapeDtypeStruct(hidden.shape, jnp.float32),
            jax.ShapeDtypeStruct(hidden.shape, jnp.bfloat16),
        ]
        + [jax.ShapeDtypeStruct(gain.shape, jnp.float32) for gain in gains]
        + [jax.ShapeDtypeStruct((1, small.shape[1]), jnp.float32)] * 2,
        in_specs=[VMEM] * 16,
        out_specs=[VMEM] * 13,
        compiler_params=pltpu.CompilerParams(vmem_limit_bytes=62 * MIB),
    )(gate, up, qkv, wo, wd, hidden, out_0, out_1, *weights, *gains, small)


def product(left, right):
    return jnp.dot(left, right, preferred_element_type=jnp.float32)


def shards(
    hidden,
    span_order,
    attn_gain,
    w_query,
    key_weight,
    value_weight,
    w_out,
    q_gain,
    k_gain,
    mlp_gain,
    w_gate,
    w_up,
    w_down,
    cotangent,
):
    seqs, toks, width = hidden.shape
    n_dp, n_blk, n_uly = (lax.axis_size(a) for a in EVERY)
    rows = n_blk * seqs * toks
    bf16 = jnp.bfloat16
    own_hidden = hidden.reshape(seqs * toks, width)
    own_cotangent = cotangent.reshape(seqs * toks, width)

    gain_q, gain_k = q_gain[None, :], k_gain[None, :]
    gain_rows = attn_gain.shape[0]
    own_gains = jnp.pad(jnp.stack([attn_gain, mlp_gain]), ((0, 30), (0, 128 - gain_rows)))
    (
        w_qkv,
        wo,
        all_wg,
        all_wu,
        all_wd,
        cot,
        g_attn,
        g_mlp,
        cosine,
        sine,
        query_pos,
        key_pos,
        heads_flat,
        normed,
        qkv,
        queries,
        key_values,
        lse,
        middle,
        normed2,
    ) = forward(
        span_order,
        own_hidden,
        w_query,
        key_weight,
        value_weight,
        w_out,
        w_gate,
        w_up,
        w_down,
        own_cotangent,
        own_gains,
        gain_q,
        gain_k,
        seqs,
        gain_rows,
    )
    w_qkv = w_qkv.reshape(width, -1)
    wo = wo.reshape(-1, width)
    wg, wu = all_wg.reshape(width, -1), all_wu.reshape(width, -1)
    wd = all_wd.reshape(-1, width)
    cot = cot.reshape(rows, width)
    normed2 = normed2.reshape(rows, width)
    gate_pre = product(normed2, wg)
    up_pre = product(normed2, wu)
    sigmoid_gate = jax.nn.sigmoid(gate_pre)
    activated = (gate_pre * sigmoid_gate * up_pre).astype(bf16)
    out_parts = product(activated, wd).astype(bf16)
    grad_act = product_right(cot, wd)
    grad_gate_pre = (
        grad_act * up_pre * sigmoid_gate * (1.0 + gate_pre * (1.0 - sigmoid_gate))
    ).astype(bf16)
    grad_up_pre = (grad_act * gate_pre * sigmoid_gate).astype(bf16)
    grad_parts = (product_right(grad_gate_pre, wg) + product_right(grad_up_pre, wu)).astype(bf16)
    blocks = (n_blk, seqs * toks, width)
    out_parts = out_parts.reshape(blocks)
    output_0, grad_middle, middle_low, grad_gate, grad_up, part_down = exchange_back(
        grad_parts.reshape(blocks),
        out_parts,
        middle,
        own_cotangent,
        g_mlp,
        normed2,
        grad_gate_pre,
        grad_up_pre,
        activated,
        cot,
    )
    middle_low = middle_low.reshape(rows, width)
    (
        grad_hidden,
        grad_out,
        grad_down,
        small,
        output_1,
        grad_gate,
        grad_up,
        grad_w_qkv,
    ) = backward(
        middle_low,
        wo,
        queries,
        key_values,
        lse,
        qkv,
        gain_q,
        gain_k,
        cosine,
        sine,
        query_pos,
        key_pos,
        w_qkv,
        own_hidden,
        grad_middle,
        g_attn,
        normed,
        heads_flat,
        out_parts,
        middle,
        grad_gate,
        grad_up,
        part_down,
    )
    (
        grad_gate,
        grad_up,
        grad_query,
        grad_key,
        grad_value,
        grad_out,
        grad_down,
        grad_hidden,
        output,
        grad_attn_gain,
        grad_mlp_gain,
        grad_q_gain,
        grad_k_gain,
    ) = finish(
        grad_gate,
        grad_up,
        grad_w_qkv,
        grad_out,
        grad_down,
        grad_hidden,
        output_0,
        output_1,
        (w_gate, w_up, w_query, key_weight, value_weight),
        [g[None, :] for g in (attn_gain, mlp_gain)],
        small,
    )
    return (
        output.reshape(hidden.shape),
        grad_hidden.reshape(hidden.shape),
        grad_attn_gain.reshape(gain_rows),
        grad_query,
        grad_key,
        grad_value,
        grad_out,
        grad_q_gain[0],
        grad_k_gain[0],
        grad_mlp_gain.reshape(gain_rows),
        grad_gate,
        grad_up,
        grad_down,
    )


def solution(mesh):
    n_dp, n_blk, n_uly = (mesh.shape[a] for a in EVERY)
    aligned = (n_dp, n_uly) == (2, 4) and KEY_VALUE_HEADS % (n_dp * n_blk) == 0
    in_specs = (
        TOKENS,
        P(),
        P(EVERY),
        P(EVERY, None),
        P(EVERY, None),
        P(EVERY, None),
        P(EVERY, None),
        P(),
        P(),
        P(EVERY),
        P(EVERY, None),
        P(EVERY, None),
        P(EVERY, None),
        TOKENS,
    )
    out_specs = (
        TOKENS,
        TOKENS,
        P(EVERY),
        P(EVERY, None),
        P(EVERY, None),
        P(EVERY, None),
        P(EVERY, None),
        P(),
        P(),
        P(EVERY),
        P(EVERY, None),
        P(EVERY, None),
        P(EVERY, None),
    )
    return jax.shard_map(
        shards if aligned else shards_general,
        mesh=mesh, in_specs=in_specs, out_specs=out_specs, check_vma=False)
```

```python
import functools
import math

import jax
import jax.numpy as jnp
from jax import lax
from jax.experimental import pallas as pl
from jax.experimental.pallas import tpu as pltpu
from jax.sharding import PartitionSpec as P

QUERY_HEADS = 16
KEY_VALUE_HEADS = 8
HEAD_SIZE = 128


DP, BLK, ULY = "dp", "blk", "uly"
EVERY = (DP, BLK, ULY)
PLANE = (DP, ULY)
TOKENS = P(DP, (BLK, ULY), None)
EQ_KGQD_NKD_TO_KGQN = "kgqd,nkd->kgqn"
EQ_KGQN_KGQD_TO_NKD = "kgqn,kgqd->nkd"
EQ_KGQN_NKD_TO_KGQD = "kgqn,nkd->kgqd"
EQ_KGQN_QKGD_TO_NKD = "kgqn,qkgd->nkd"
EQ_QKGD_NKD_TO_KGQN = "qkgd,nkd->kgqn"
EQ_STD_DE_TO_STE = "std,de->ste"
EQ_STD_DF_TO_STF = "std,df->stf"
EQ_STD_ED_TO_STE = "std,ed->ste"
EQ_STD_FD_TO_STF = "std,fd->stf"
EQ_STD_STE_TO_DE = "std,ste->de"
EQ_STD_STF_TO_DF = "std,stf->df"
EQ_STE_DE_TO_STD = "ste,de->std"
EQ_STE_ED_TO_STD = "ste,ed->std"
EQ_STE_STD_TO_ED = "ste,std->ed"
EQ_STF_DF_TO_STD = "stf,df->std"
EQ_STF_FD_TO_STD = "stf,fd->std"
EQ_STF_STD_TO_FD = "stf,std->fd"

EPSILON = 1e-06
ROPE_BASE = 1000000.0


def rms_scale(source):
    return lax.rsqrt(jnp.mean(source * source, axis=-1, keepdims=True) + EPSILON)


def norm_back(grad_normed, source, norm_scale, gain):
    unit_rows = source * norm_scale
    scaled = grad_normed * gain
    return norm_scale * (scaled - unit_rows * jnp.mean(scaled * unit_rows, axis=-1, keepdims=True))


def angles_of(positions, head_dim):
    freq_steps = jnp.arange(head_dim // 2, dtype=jnp.float32)
    inverse = jnp.exp(freq_steps * (-2.0 * math.log(ROPE_BASE) / head_dim))
    return positions.astype(jnp.float32)[:, None] * inverse[None, :]


def rotate(source, angles, direction):
    half_dim = source.shape[-1] // 2
    cosine = jnp.cos(angles)[:, None, :]
    sine_part = direction * jnp.sin(angles)[:, None, :]
    first_half = source[..., :half_dim]
    second_half = source[..., half_dim:]
    return jnp.concatenate(
        [
            first_half * cosine - second_half * sine_part,
            second_half * cosine + first_half * sine_part,
        ],
        axis=-1,
    )


def positions_of(places, span_order, half_len):
    blocks_of = places // half_len
    block_ids = jnp.arange(span_order.shape[0], dtype=jnp.int32)
    chosen = jnp.sum(
        jnp.where(blocks_of[:, None] == block_ids[None, :], span_order[None, :], 0), axis=1
    )
    return chosen * half_len + places % half_len


def add_rows(buffer, new_rows):
    return buffer + new_rows


def shards_general(
    hidden,
    span_order,
    attn_gain,
    w_query,
    key_weight,
    value_weight,
    w_out,
    q_gain,
    k_gain,
    mlp_gain,
    w_gate,
    w_up,
    w_down,
    cotangent,
):
    sequence_count = hidden.shape[0]
    token_count = hidden.shape[1]
    ulysses_group_size = lax.axis_size(ULY)
    local_q = QUERY_HEADS // ulysses_group_size
    local_key_value = KEY_VALUE_HEADS // ulysses_group_size
    query_group_width = QUERY_HEADS // KEY_VALUE_HEADS
    block_len = token_count * ulysses_group_size
    half_len = block_len // 2
    score_scale = 1.0 / math.sqrt(HEAD_SIZE)
    blk_index = lax.axis_index(BLK)
    uly_index = lax.axis_index(ULY)
    first_place = (blk_index * ulysses_group_size + uly_index) * token_count
    local_angles = angles_of(
        positions_of(first_place + jnp.arange(token_count, dtype=jnp.int32), span_order, half_len),
        HEAD_SIZE,
    )
    query_pos = positions_of(
        blk_index * block_len + jnp.arange(block_len, dtype=jnp.int32), span_order, half_len
    )
    g_attn, wq_all, wk_all, wv_all, wo_all = (
        lax.all_gather(attn_gain, EVERY, axis=0, tiled=True),
        lax.all_gather(w_query, EVERY, axis=0, tiled=True),
        lax.all_gather(key_weight, EVERY, axis=0, tiled=True),
        lax.all_gather(value_weight, EVERY, axis=0, tiled=True),
        lax.all_gather(w_out, EVERY, axis=0, tiled=True),
    )
    source = hidden.astype(jnp.float32)
    first_scale = rms_scale(source)
    normalized_input = (source * first_scale * g_attn.astype(jnp.float32)).astype(jnp.bfloat16)
    q_pre = jnp.einsum(
        EQ_STD_DE_TO_STE, normalized_input, wq_all, preferred_element_type=jnp.float32
    ).reshape(sequence_count, token_count, QUERY_HEADS, HEAD_SIZE)
    key_before_norm = jnp.einsum(
        EQ_STD_DE_TO_STE, normalized_input, wk_all, preferred_element_type=jnp.float32
    ).reshape(sequence_count, token_count, KEY_VALUE_HEADS, HEAD_SIZE)
    value_before_norm = jnp.einsum(
        EQ_STD_DE_TO_STE, normalized_input, wv_all, preferred_element_type=jnp.float32
    ).reshape(sequence_count, token_count, KEY_VALUE_HEADS, HEAD_SIZE)
    q_scale = rms_scale(q_pre)
    k_scale = rms_scale(key_before_norm)
    gain_q = q_gain.astype(jnp.float32)
    gain_k = k_gain.astype(jnp.float32)
    q_rot = rotate(q_pre * q_scale * gain_q, local_angles, 1.0).astype(jnp.bfloat16)
    k_rot = rotate(key_before_norm * k_scale * gain_k, local_angles, 1.0).astype(jnp.bfloat16)
    v_low = value_before_norm.astype(jnp.bfloat16)
    q_heads, k_heads, v_heads = (
        lax.all_to_all(q_rot, ULY, split_axis=2, concat_axis=1, tiled=True),
        lax.all_to_all(k_rot, ULY, split_axis=2, concat_axis=1, tiled=True),
        lax.all_to_all(v_low, ULY, split_axis=2, concat_axis=1, tiled=True),
    )
    q_group = q_heads.reshape(
        sequence_count, block_len, local_key_value, query_group_width, HEAD_SIZE
    )
    stat_shape = (sequence_count, local_key_value, query_group_width, block_len)
    start_state = (
        jnp.full(stat_shape, -1e30, jnp.float32),
        jnp.zeros(stat_shape, jnp.float32),
        jnp.zeros(stat_shape + (HEAD_SIZE,), jnp.float32),
    )
    key_piece = lax.all_gather(k_heads, BLK, axis=1, tiled=True)
    value_piece = lax.all_gather(v_heads, BLK, axis=1, tiled=True)
    key_pos = positions_of(jnp.arange(key_piece.shape[1], dtype=jnp.int32), span_order, half_len)
    allowed = query_pos[:, None] >= key_pos[None, :]

    def attend_one_sequence(members):
        query_rows, key_rows, value_rows, top_seq, total_seq, accum_seq = members
        scores = (
            jnp.einsum(EQ_QKGD_NKD_TO_KGQN, query_rows, key_rows, preferred_element_type=jnp.float32)
            * score_scale
        )
        scores = jnp.where(allowed, scores, -jnp.inf)
        new_top = jnp.maximum(top_seq, jnp.max(scores, axis=-1))
        fading = jnp.exp(top_seq - new_top)
        weights = jnp.exp(scores - new_top[..., None])
        total_seq = total_seq * fading + jnp.sum(weights, axis=-1)
        accum_seq = accum_seq * fading[..., None] + jnp.einsum(
            EQ_KGQN_NKD_TO_KGQD,
            weights.astype(jnp.bfloat16),
            value_rows,
            preferred_element_type=jnp.float32,
        )
        return (new_top, total_seq, accum_seq)

    row_top, row_total, accum = lax.map(
        attend_one_sequence,
        (q_group, key_piece, value_piece, start_state[0], start_state[1], start_state[2]),
    )
    log_total = row_top + jnp.log(row_total)
    attention_output = jnp.transpose(accum / row_total[..., None], (0, 3, 1, 2, 4)).reshape(
        sequence_count, block_len, local_q, HEAD_SIZE
    )
    heads_seq = lax.all_to_all(
        attention_output.astype(jnp.bfloat16), ULY, split_axis=1, concat_axis=2, tiled=True
    )
    heads_flat = heads_seq.reshape(sequence_count, token_count, QUERY_HEADS * HEAD_SIZE)
    middle = source + jnp.einsum(
        EQ_STE_ED_TO_STD, heads_flat, wo_all, preferred_element_type=jnp.float32
    )
    g_mlp, wg_all, wu_all, wd_all = (
        lax.all_gather(mlp_gain, EVERY, axis=0, tiled=True),
        lax.all_gather(w_gate, EVERY, axis=0, tiled=True),
        lax.all_gather(w_up, EVERY, axis=0, tiled=True),
        lax.all_gather(w_down, EVERY, axis=0, tiled=True),
    )
    second_scale = rms_scale(middle)
    gain_mlp = g_mlp.astype(jnp.float32)
    normed2 = (middle * second_scale * gain_mlp).astype(jnp.bfloat16)
    gate_pre = jnp.einsum(EQ_STD_DF_TO_STF, normed2, wg_all, preferred_element_type=jnp.float32)
    up_pre = jnp.einsum(EQ_STD_DF_TO_STF, normed2, wu_all, preferred_element_type=jnp.float32)
    sigmoid_gate = jax.nn.sigmoid(gate_pre)
    activated = (gate_pre * sigmoid_gate * up_pre).astype(jnp.bfloat16)
    result = middle + jnp.einsum(
        EQ_STF_FD_TO_STD, activated, wd_all, preferred_element_type=jnp.float32
    )
    output = result.astype(jnp.bfloat16)
    g_mlp, wg_all, wu_all, wd_all = (
        lax.all_gather(mlp_gain, EVERY, axis=0, tiled=True),
        lax.all_gather(w_gate, EVERY, axis=0, tiled=True),
        lax.all_gather(w_up, EVERY, axis=0, tiled=True),
        lax.all_gather(w_down, EVERY, axis=0, tiled=True),
    )
    gain_mlp = g_mlp.astype(jnp.float32)
    grad_act = jnp.einsum(EQ_STD_FD_TO_STF, cotangent, wd_all, preferred_element_type=jnp.float32)
    grad_gate_pre = (
        grad_act * up_pre * sigmoid_gate * (1.0 + gate_pre * (1.0 - sigmoid_gate))
    ).astype(jnp.bfloat16)
    grad_up_pre = (grad_act * gate_pre * sigmoid_gate).astype(jnp.bfloat16)
    grad_gate = jnp.einsum(
        EQ_STD_STF_TO_DF, normed2, grad_gate_pre, preferred_element_type=jnp.float32
    )
    grad_up = jnp.einsum(EQ_STD_STF_TO_DF, normed2, grad_up_pre, preferred_element_type=jnp.float32)
    grad_normed2 = jnp.einsum(
        EQ_STF_DF_TO_STD, grad_gate_pre, wg_all, preferred_element_type=jnp.float32
    ) + jnp.einsum(EQ_STF_DF_TO_STD, grad_up_pre, wu_all, preferred_element_type=jnp.float32)
    mlp_gain_term = jnp.sum(grad_normed2 * middle * second_scale, axis=(0, 1))
    grad_middle = cotangent.astype(jnp.float32) + norm_back(
        grad_normed2, middle, second_scale, gain_mlp
    )
    grad_mlp_gain, grad_gate, grad_up = (
        lax.psum_scatter(mlp_gain_term, EVERY, scatter_dimension=0, tiled=True),
        lax.psum_scatter(grad_gate, EVERY, scatter_dimension=0, tiled=True),
        lax.psum_scatter(grad_up, EVERY, scatter_dimension=0, tiled=True),
    )
    g_attn, wq_all, wk_all, wv_all, wo_all = (
        lax.all_gather(attn_gain, EVERY, axis=0, tiled=True),
        lax.all_gather(w_query, EVERY, axis=0, tiled=True),
        lax.all_gather(key_weight, EVERY, axis=0, tiled=True),
        lax.all_gather(value_weight, EVERY, axis=0, tiled=True),
        lax.all_gather(w_out, EVERY, axis=0, tiled=True),
    )
    middle_low = grad_middle.astype(jnp.bfloat16)
    grad_out = jnp.einsum(EQ_STE_STD_TO_ED, heads_flat, middle_low, preferred_element_type=jnp.float32)
    grad_heads = (
        jnp.einsum(EQ_STD_ED_TO_STE, middle_low, wo_all, preferred_element_type=jnp.float32)
        .astype(jnp.bfloat16)
        .reshape(sequence_count, token_count, QUERY_HEADS, HEAD_SIZE)
    )
    grad_heads_local = lax.all_to_all(grad_heads, ULY, split_axis=2, concat_axis=1, tiled=True)
    grad_group = jnp.transpose(
        grad_heads_local.reshape(
            sequence_count, block_len, local_key_value, query_group_width, HEAD_SIZE
        ),
        (0, 2, 3, 1, 4),
    )
    delta = jnp.sum(grad_heads_local.astype(jnp.float32) * attention_output, axis=-1)
    delta = jnp.transpose(
        delta.reshape(sequence_count, block_len, local_key_value, query_group_width), (0, 2, 3, 1)
    )
    seq_length = block_len * lax.axis_size(BLK)
    zero_keys = jnp.zeros((sequence_count, seq_length, local_key_value, HEAD_SIZE), jnp.float32)
    back_state = (jnp.zeros(stat_shape + (HEAD_SIZE,), jnp.float32), zero_keys, zero_keys)
    key_piece = lax.all_gather(k_heads, BLK, axis=1, tiled=True)
    value_piece = lax.all_gather(v_heads, BLK, axis=1, tiled=True)
    key_pos = positions_of(jnp.arange(key_piece.shape[1], dtype=jnp.int32), span_order, half_len)
    back_allowed = query_pos[:, None] >= key_pos[None, :]

    def back_one_sequence(members):
        query_rows, grad_rows, lse_seq, delta_seq, key_rows, value_rows, dq_seq, dk_seq, dv_seq = (
            members
        )
        scores = (
            jnp.einsum(EQ_QKGD_NKD_TO_KGQN, query_rows, key_rows, preferred_element_type=jnp.float32)
            * score_scale
        )
        scores = jnp.where(back_allowed, scores, -jnp.inf)
        probs = jnp.exp(scores - lse_seq[..., None])
        grad_values = jnp.einsum(
            EQ_KGQN_KGQD_TO_NKD,
            probs.astype(jnp.bfloat16),
            grad_rows,
            preferred_element_type=jnp.float32,
        )
        grad_probs = jnp.einsum(
            EQ_KGQD_NKD_TO_KGQN, grad_rows, value_rows, preferred_element_type=jnp.float32
        )
        grad_scores = (probs * (grad_probs - delta_seq[..., None])).astype(jnp.bfloat16)
        dq_seq = dq_seq + score_scale * jnp.einsum(
            EQ_KGQN_NKD_TO_KGQD, grad_scores, key_rows, preferred_element_type=jnp.float32
        )
        grad_keys = score_scale * jnp.einsum(
            EQ_KGQN_QKGD_TO_NKD, grad_scores, query_rows, preferred_element_type=jnp.float32
        )
        return (dq_seq, add_rows(dk_seq, grad_keys), add_rows(dv_seq, grad_values))

    grad_q_group, grad_k_whole, grad_v_whole = lax.map(
        back_one_sequence,
        (
            q_group,
            grad_group,
            log_total,
            delta,
            key_piece,
            value_piece,
            back_state[0],
            back_state[1],
            back_state[2],
        ),
    )
    grad_k_block, grad_v_block = (
        lax.psum_scatter(
            grad_k_whole.astype(jnp.bfloat16), BLK, scatter_dimension=1, tiled=True
        ).astype(jnp.float32),
        lax.psum_scatter(
            grad_v_whole.astype(jnp.bfloat16), BLK, scatter_dimension=1, tiled=True
        ).astype(jnp.float32),
    )
    grad_q_block = jnp.transpose(grad_q_group, (0, 3, 1, 2, 4)).reshape(
        sequence_count, block_len, local_q, HEAD_SIZE
    )
    grad_q_seq, grad_k_seq, value_sequence_gradient = (
        lax.all_to_all(
            grad_q_block.astype(jnp.bfloat16), ULY, split_axis=1, concat_axis=2, tiled=True
        ).astype(grad_q_block.dtype),
        lax.all_to_all(
            grad_k_block.astype(jnp.bfloat16), ULY, split_axis=1, concat_axis=2, tiled=True
        ).astype(grad_k_block.dtype),
        lax.all_to_all(
            grad_v_block.astype(jnp.bfloat16), ULY, split_axis=1, concat_axis=2, tiled=True
        ).astype(grad_v_block.dtype),
    )
    grad_q_normed = rotate(grad_q_seq, local_angles, -1.0)
    grad_k_normed = rotate(grad_k_seq, local_angles, -1.0)
    q_gain_term = jnp.sum(grad_q_normed * q_pre * q_scale, axis=(0, 1, 2))
    k_gain_term = jnp.sum(grad_k_normed * key_before_norm * k_scale, axis=(0, 1, 2))
    grad_q_pre = (
        norm_back(grad_q_normed, q_pre, q_scale, gain_q)
        .astype(jnp.bfloat16)
        .reshape(sequence_count, token_count, QUERY_HEADS * HEAD_SIZE)
    )
    grad_k_pre = (
        norm_back(grad_k_normed, key_before_norm, k_scale, gain_k)
        .astype(jnp.bfloat16)
        .reshape(sequence_count, token_count, KEY_VALUE_HEADS * HEAD_SIZE)
    )
    value_pre_gradient = value_sequence_gradient.astype(jnp.bfloat16).reshape(
        sequence_count, token_count, KEY_VALUE_HEADS * HEAD_SIZE
    )
    grad_query = jnp.einsum(
        EQ_STD_STE_TO_DE, normalized_input, grad_q_pre, preferred_element_type=jnp.float32
    )
    grad_key = jnp.einsum(
        EQ_STD_STE_TO_DE, normalized_input, grad_k_pre, preferred_element_type=jnp.float32
    )
    grad_value = jnp.einsum(
        EQ_STD_STE_TO_DE, normalized_input, value_pre_gradient, preferred_element_type=jnp.float32
    )
    grad_normed = jnp.einsum(EQ_STE_DE_TO_STD, grad_q_pre, wq_all, preferred_element_type=jnp.float32)
    grad_normed = grad_normed + jnp.einsum(
        EQ_STE_DE_TO_STD, grad_k_pre, wk_all, preferred_element_type=jnp.float32
    )
    grad_normed = grad_normed + jnp.einsum(
        EQ_STE_DE_TO_STD, value_pre_gradient, wv_all, preferred_element_type=jnp.float32
    )
    attn_gain_term = jnp.sum(grad_normed * source * first_scale, axis=(0, 1))
    grad_hidden = grad_middle + norm_back(
        grad_normed, source, first_scale, g_attn.astype(jnp.float32)
    )
    grad_down = jnp.einsum(EQ_STF_STD_TO_FD, activated, cotangent, preferred_element_type=jnp.float32)
    grad_attn_gain, grad_query, grad_key, grad_value, grad_out, grad_down = (
        lax.psum_scatter(attn_gain_term, EVERY, scatter_dimension=0, tiled=True),
        lax.psum_scatter(grad_query, EVERY, scatter_dimension=0, tiled=True),
        lax.psum_scatter(grad_key, EVERY, scatter_dimension=0, tiled=True),
        lax.psum_scatter(grad_value, EVERY, scatter_dimension=0, tiled=True),
        lax.psum_scatter(grad_out, EVERY, scatter_dimension=0, tiled=True),
        lax.psum_scatter(grad_down, EVERY, scatter_dimension=0, tiled=True),
    )
    grad_q_gain, grad_k_gain = lax.psum((q_gain_term, k_gain_term), EVERY)
    return (
        output,
        grad_hidden,
        grad_attn_gain,
        grad_query,
        grad_key,
        grad_value,
        grad_out,
        grad_q_gain,
        grad_k_gain,
        grad_mlp_gain,
        grad_gate,
        grad_up,
        grad_down,
    )


MESH = pl.DeviceIdType.MESH
HBM = pl.BlockSpec(memory_space=pltpu.HBM)
VMEM = pl.BlockSpec(memory_space=pltpu.VMEM)
MIB = 1 << 20


def kernel_params(collective_id, vmem_mib=62):
    return pltpu.CompilerParams(
        collective_id=collective_id, has_side_effects=True, vmem_limit_bytes=vmem_mib * MIB
    )


def semaphores(count, local=16):
    return [
        pltpu.SemaphoreType.DMA((count,)),
        pltpu.SemaphoreType.DMA((count,)),
        pltpu.SemaphoreType.DMA((local,)),
    ]


class Copy:
    def __init__(self, descriptor, sends, receives):
        self.descriptor, self.sends, self.receives = descriptor, sends, receives

    def under(self, condition, action):
        if condition is None:
            action()
        else:
            pl.when(condition)(action)

    def start(self):
        self.under(self.sends, lambda: self.descriptor().start())
        return self

    def sent(self):
        self.under(self.sends, lambda: self.descriptor().wait_send())

    def arrived(self):
        self.under(self.receives, lambda: self.descriptor().wait_recv())


class Links:
    def __init__(self, send, recv, here):
        self.send, self.recv, self.here = send, recv, here
        self.used, self.used_here = 0, 0
        self.copies, self.local_copies = [], []
        self.n_dp, self.n_blk, self.n_uly = (lax.axis_size(a) for a in EVERY)
        self.dp, self.blk, self.uly = (lax.axis_index(a) for a in EVERY)
        self.other_dp = 1 - self.dp
        self.across = lax.rem(self.uly + 2, 4)
        self.twin = self.uly + 1 - 2 * lax.rem(self.uly, 2)
        self.x_way = (self.other_dp, self.blk, self.uly)
        self.y_way = (self.dp, self.blk, self.across)
        self.core_way = (self.dp, self.blk, self.twin)

    def peer(self, step):
        return lax.rem(self.blk + step, self.n_blk)

    def peers(self):
        return [(self.dp, self.peer(k), self.uly) for k in range(1, self.n_blk)]

    def far_first(self):
        last = self.n_blk - 1
        orders = [
            sorted((p for p in range(self.n_blk) if p != b), key=lambda p, b=b: -abs(p - b))
            for b in range(self.n_blk)
        ]
        for b, order in enumerate(orders):
            ways = [[p for p in order if p > b], [p for p in order if p < b]]
            ways.sort(key=lambda way: -len(way))
            merged = []
            while ways[0] or ways[1]:
                for way in ways:
                    if way:
                        merged.append(way.pop(0))
            orders[b] = merged
        peers = []
        for turn in range(last):
            peer = jnp.int32(0)
            for b, order in enumerate(orders):
                peer = jnp.where(self.blk == b, order[turn], peer)
            peers.append(peer)
        return peers

    def swap(self, pieces_for):
        base, count = self.used, 0
        for peer in self.far_first():
            pieces = pieces_for(peer)
            count = len(pieces)
            distance = lax.rem(peer - self.blk + self.n_blk, self.n_blk) - 1
            for number, (source, target) in enumerate(pieces):
                self.swap_copy(base + distance * count + number, source, target, peer).start()
        self.used = base + (self.n_blk - 1) * count
        waits = []
        for slot in range(base, self.used):
            source, target = pieces_for(self.blk)[(slot - base) % count]

            def descriptor(slot=slot, source=source, target=target):
                return self.swap_copy(slot, source, target, self.peer(1))

            copy = Copy(descriptor, None, None)
            self.copies.append(copy)
            waits.append(copy)
        return waits

    def swap_copy(self, slot, source, target, peer):
        return pltpu.make_async_remote_copy(
            src_ref=source,
            dst_ref=target,
            send_sem=self.send.at[slot],
            recv_sem=self.recv.at[slot],
            device_id=(self.dp, peer, self.uly),
            device_id_type=MESH,
        )

    def greet(self, devices):
        barrier = pltpu.get_barrier_semaphore()
        for device in devices:
            pl.semaphore_signal(barrier, inc=1, device_id=device, device_id_type=MESH)
        pl.semaphore_wait(barrier, len(devices))

    def remote(self, source, target, device, sends=None, receives=None):
        slot = self.used
        self.used += 1

        def descriptor():
            return pltpu.make_async_remote_copy(
                src_ref=source(),
                dst_ref=target(),
                send_sem=self.send.at[slot],
                recv_sem=self.recv.at[slot],
                device_id=device,
                device_id_type=MESH,
            )

        copy = Copy(descriptor, sends, receives)
        self.copies.append(copy)
        return copy.start()

    def to(self, source, target, device):
        return self.remote(lambda: source, lambda: target, device)

    def local(self, source, target):
        copy = pltpu.make_async_copy(source, target, self.here.at[self.used_here])
        self.used_here += 1
        copy.start()
        self.local_copies.append(copy)
        return copy

    def finish(self):
        assert self.used <= self.send.shape[0] and self.used_here <= self.here.shape[0]
        for copy in self.copies:
            copy.sent()


class LineGather:
    def __init__(self, links, own, whole):
        self.links, self.own, self.whole = links, own, whole
        self.waiting = []

    def send(self, step):
        links, whole = self.links, self.whole
        blk, last = links.blk, links.n_blk - 1

        def block(index):
            if step == 0:
                return lambda: self.own
            return lambda: whole.at[index]

        self.waiting = [
            links.remote(
                block(blk - step),
                lambda: whole.at[blk - step],
                (links.dp, blk + 1, links.uly),
                jnp.logical_and(blk >= step, blk < last),
                blk >= step + 1,
            ),
            links.remote(
                block(blk + step),
                lambda: whole.at[blk + step],
                (links.dp, blk - 1, links.uly),
                jnp.logical_and(blk + step <= last, blk > 0),
                blk + step + 1 <= last,
            ),
        ]

    def arrived(self):
        for copy in self.waiting:
            copy.arrived()


def halves(tokens):
    return [pl.ds(0, tokens // 2), pl.ds(tokens // 2, tokens // 2)]


class HalvedLine:
    def __init__(self, links, own, whole):
        self.lines = [
            LineGather(links, None if own is None else own.at[rows], whole.at[:, rows])
            for rows in halves(whole.shape[1])
        ]

    def send(self, step):
        for line in self.lines:
            line.send(step)

    def advance(self, step):
        for line in self.lines:
            line.arrived()
            line.send(step)

    def arrived(self):
        for line in self.lines:
            line.arrived()


class PlaneGather:
    def __init__(self, links, at):
        self.links, self.at = links, at

    def start_x(self, own):
        links = self.links
        mine = self.at(links.dp, links.uly)
        self.from_x = links.to(own, mine, links.x_way)
        self.from_core = [links.to(own, mine, links.core_way)]

    def start_y(self, own):
        links = self.links
        self.from_y = links.to(own, self.at(links.dp, links.uly), links.y_way)

    def start(self, own=None):
        own = self.at(self.links.dp, self.links.uly) if own is None else own
        self.start_x(own)
        self.start_y(own)

    def hand_on(self):
        links, at = self.links, self.at
        self.from_x.arrived()
        half = at(links.other_dp, links.uly, 0)
        self.second_y = links.to(half, half, links.y_way)
        self.from_y.arrived()
        half = at(links.dp, links.across, 1)
        self.second_x = links.to(half, half, links.x_way)
        for chunk in (at(links.other_dp, links.uly), at(links.dp, links.across)):
            self.from_core.append(links.to(chunk, chunk, links.core_way))

    def last(self):
        links = self.links
        self.second_y.arrived()
        self.second_x.arrived()
        chunk = self.at(links.other_dp, links.across)
        self.from_core.append(links.to(chunk, chunk, links.core_way))

    def arrived(self):
        for copy in self.from_core:
            copy.arrived()


def rows_of(whole, blocked):
    def at(dp, uly, half=None):
        part = whole.at[dp, :, uly] if blocked else whole.at[dp, uly]
        if half is None:
            return part
        depth = whole.shape[-2] // 2
        rows = pl.ds(half * depth, depth)
        return part.at[:, rows] if blocked else part.at[rows]

    return at


class LineSwap:
    def __init__(self, links, source, target, relay):
        self.links, self.source, self.target = links, source, target
        self.base, self.last = links.used, links.n_blk - 1
        self.count = len(target(links.blk))
        links.used += 2 * self.last * links.n_blk * self.count
        self.slots = {}
        for way in (1, -1):
            for step in range(self.last):
                for steps_on in range(step + 2, links.n_blk):
                    bound = steps_on if way == 1 else self.last - steps_on
                    self.slots[way, step, bound] = relay.at[len(self.slots)]

    def copies(self, way, step, bound, target):
        links = self.links
        first = ((1 if way == 1 else 0) * self.last + step) * links.n_blk + bound
        if step == 0:
            source = self.source(bound)
        else:
            slot = self.slots.get((way, step - 1, bound))
            source = target if slot is None else [slot.at[n] for n in range(self.count)]
        return [
            pltpu.make_async_remote_copy(
                src_ref=source[number],
                dst_ref=target[number],
                send_sem=links.send.at[self.base + first * self.count + number],
                recv_sem=links.recv.at[self.base + first * self.count + number],
                device_id=(links.dp, links.blk + way, links.uly),
                device_id_type=MESH,
            )
            for number in range(self.count)
        ]

    def bounds(self, way, step):
        ahead = [n for n in range(self.links.n_blk) if n > step]
        return [n if way == 1 else self.last - n for n in reversed(ahead)]

    def sends(self, way, step, bound):
        blk = self.links.blk
        if way == 1:
            return jnp.logical_and(blk >= step, bound > blk)
        return jnp.logical_and(blk + step <= self.last, bound < blk)

    def relayed(self, way, step, bound):
        slot = self.slots.get((way, step, bound))
        return None if slot is None else [slot.at[n] for n in range(self.count)]

    def hand_on(self, step):
        links = self.links
        for near, way in enumerate((1, -1)):
            for bound in self.bounds(way, step):

                @pl.when(self.sends(way, step, bound))
                def _(way=way, bound=bound):
                    if step > 0:
                        for copy in self.copies(
                            way, step - 1, bound, self.relayed(way, step - 1, bound)
                        ):
                            copy.wait_recv()
                    final = links.blk + way == bound

                    @pl.when(final)
                    def _():
                        origin = links.blk - way * step
                        for copy in self.copies(way, step, bound, self.target(origin)):
                            copy.start()

                    onward = self.relayed(way, step, bound)
                    if onward is not None:

                        @pl.when(jnp.logical_not(final))
                        def _():
                            for copy in self.copies(way, step, bound, onward):
                                copy.start()

    def arrived(self):
        links = self.links
        for step in range(self.last):
            for way in (1, -1):
                place = links.blk if way == 1 else self.last - links.blk

                @pl.when(place >= step + 1)
                def _(way=way, step=step):
                    origin = links.blk - way * (step + 1)
                    target = self.target(origin)
                    first = ((1 if way == 1 else 0) * self.last + step) * links.n_blk + links.blk
                    for number in range(self.count):
                        at = self.base + first * self.count + number
                        pltpu.make_async_remote_copy(
                            src_ref=target[number],
                            dst_ref=target[number],
                            send_sem=links.send.at[at],
                            recv_sem=links.recv.at[at],
                            device_id=(links.dp, links.blk - way, links.uly),
                            device_id_type=MESH,
                        ).wait_recv()

    def sent(self):
        for step in range(self.last):
            for way in (1, -1):
                for bound in self.bounds(way, step):

                    @pl.when(self.sends(way, step, bound))
                    def _(way=way, step=step, bound=bound):
                        for copy in self.copies(
                            way, step, bound, self.target(self.links.blk)
                        ):
                            copy.wait_send()


def relay_slots(n_blk):
    return (n_blk - 1) * (n_blk - 2)


class ColumnSwap:
    def __init__(self, links, pieces):
        self.links, self.pieces = links, pieces
        self.incoming, self.kept = [], []

    def parts(self, blk):
        links = self.links
        for weight, whole, offset in self.pieces:
            width = weight.shape[-1] // links.n_dp // links.n_blk
            for group in range(links.n_dp):
                start = (group * links.n_blk + blk) * width
                yield (
                    weight.at[:, pl.ds(pl.multiple_of(start, 128), width)],
                    whole.at[links.blk, :, pl.ds(offset + group * width, width)],
                )

    def start(self):
        links = self.links
        self.incoming = links.swap(lambda peer: list(self.parts(peer)))
        for source, target in self.parts(links.blk):
            self.kept.append(links.local(source, target))

    def arrived(self):
        for copy in self.kept:
            copy.wait()
        for copy in self.incoming:
            copy.arrived()


def write_positions(links, span_order, toks, cosine, sine, query_pos, key_pos):
    half_len = toks * links.n_uly // 2

    def first(blk, uly):
        chunk = span_order[2 * blk + lax.div(uly, links.n_uly // 2)]
        return chunk * half_len + lax.rem(uly, links.n_uly // 2) * toks

    lane = lax.broadcasted_iota(jnp.int32, (toks, HEAD_SIZE), 1)
    row = lax.broadcasted_iota(jnp.int32, (toks, HEAD_SIZE), 0)
    upper = lane >= HEAD_SIZE // 2
    step = jnp.where(upper, lane - HEAD_SIZE // 2, lane).astype(jnp.float32)
    inverse = jnp.exp(step * (-2.0 * math.log(ROPE_BASE) / HEAD_SIZE))
    for blk in range(links.n_blk):
        angles = (first(blk, links.uly) + row).astype(jnp.float32) * inverse
        at = slice(blk * toks, (blk + 1) * toks)
        cosine[at, :] = jnp.cos(angles)
        turn = jnp.sin(angles)
        sine[at, :] = jnp.where(upper, turn, -turn)
    lane = lax.broadcasted_iota(jnp.int32, query_pos.shape, 1)
    place = jnp.zeros(query_pos.shape, jnp.int32)
    for start in range(0, query_pos.shape[1], toks):
        blk = start // toks % links.n_blk
        here = jnp.logical_and(lane >= start, lane < start + toks)
        place = jnp.where(here, first(blk, links.uly) + lane - start, place)
    query_pos[...] = place
    row = lax.broadcasted_iota(jnp.int32, (toks, 1), 0)
    for uly in range(links.n_uly):
        for blk in range(links.n_blk):
            start = (uly * links.n_blk + blk) * toks
            key_pos[start : start + toks, :] = row + first(blk, jnp.int32(uly))


def write_gains(links, all_gains, size, targets):
    per_row = 128 // size
    for which, target in enumerate(targets):
        for place in range(target.shape[1] // 128):
            pieces = []
            for part in range(per_row):
                device = place * per_row + part
                plane, uly = device // links.n_uly, device % links.n_uly
                gains = all_gains[plane // links.n_blk, plane % links.n_blk, uly]
                pieces.append(gains.astype(jnp.float32)[which : which + 1, :size])
            target[:, place * 128 : (place + 1) * 128] = jnp.concatenate(pieces, axis=1)


ROWS = 32


def each_block(count, body):
    def step(index, carry):
        body(pl.ds(pl.multiple_of(index * ROWS, ROWS), ROWS))
        return carry

    lax.fori_loop(0, count // ROWS, step, 0)


class LineScatter:
    def __init__(self, links, parts, rightward, leftward):
        self.links, self.parts = links, parts
        self.slots = {1: rightward, -1: leftward}
        self.tokens = parts.shape[1]
        self.number = links.used
        self.last = links.n_blk - 1
        links.used += 2 * self.last

    def target(self, step, way):
        return self.last - step if way == 1 else step

    def slot(self, step, way):
        target = self.target(step, way)
        return self.slots[way].at[target - 1 if way == 1 else target]

    def place(self, way):
        return self.links.blk if way == 1 else self.last - self.links.blk

    def copy(self, step, way, source=None):
        links, slot = self.links, self.slot(step, way)
        number = self.number + 2 * step + (1 if way == 1 else 0)
        return pltpu.make_async_remote_copy(
            src_ref=slot if source is None else source,
            dst_ref=slot,
            send_sem=links.send.at[number],
            recv_sem=links.recv.at[number],
            device_id=(links.dp, links.blk + way, links.uly),
            device_id_type=MESH,
        )

    def start(self):
        for step in range(self.last):
            for way in (1, -1):

                @pl.when(self.place(way) == 0)
                def _(step=step, way=way):
                    self.copy(step, way, self.parts.at[self.target(step, way)]).start()

    def tick(self, tick):
        for way in (1, -1):

            @pl.when(jnp.logical_and(self.place(way) >= 1, self.place(way) <= tick))
            def _(way=way):
                step = tick - self.place(way)
                self.copy(step, way).wait_recv()
                slot, target = self.slot(step, way), self.target(step, way)

                def body(rows):
                    slot[rows, :] = slot[rows, :] + self.parts[target, rows, :]

                each_block(self.tokens, body)
                self.copy(step, way).start()

    def finish(self, total):
        blk, last = self.links.blk, self.last

        def start(rows):
            total[rows, :] = self.parts[blk, rows, :].astype(jnp.float32)

        each_block(self.tokens, start)
        for way in (1, -1):

            @pl.when(self.place(way) >= 1)
            def _(way=way):
                step = last - self.place(way)
                self.copy(step, way).wait_recv()
                slot = self.slot(step, way)

                def body(rows):
                    total[rows, :] = total[rows, :] + slot[rows, :].astype(jnp.float32)

                each_block(self.tokens, body)

    def sent(self):
        for step in range(self.last):
            for way in (1, -1):
                beyond = self.place(way) + step < self.last
                pl.when(beyond)(lambda step=step, way=way: self.copy(step, way).wait_send())


def halved_sums(links, parts, rightward, leftward):
    return [
        LineScatter(links, parts.at[:, rows], rightward.at[:, rows], leftward.at[:, rows])
        for rows in halves(parts.shape[1])
    ]


class OutputHalf:
    def __init__(self, links, which, parts, middle, rightward, leftward, total):
        rows = halves(middle.shape[0])[which]
        self.middle, self.total = middle.at[rows], total
        self.sum = LineScatter(links, parts.at[:, rows], rightward, leftward)

    def write(self, output):
        self.sum.finish(self.total)

        def body(rows):
            output[rows, :] = (self.middle[rows, :] + self.total[rows, :]).astype(jnp.bfloat16)

        each_block(self.middle.shape[0], body)


def output_scratch(n_blk, tokens, width):
    return line_scratch(n_blk, tokens // 2, width) + [
        pltpu.VMEM((tokens // 2, width), jnp.float32)
    ]


def line_scratch(n_blk, tokens, width):
    return [pltpu.VMEM((n_blk - 1, tokens, width), jnp.bfloat16)] * 2


class PlaneScatter:
    def __init__(self, links, parts, from_core, from_x, from_y, last_x, last_y):
        self.links, self.parts = links, parts
        self.own_core_only = from_core is None
        self.from_core, self.from_x, self.from_y = from_core, from_x, from_y
        self.last_x, self.last_y = last_x, last_y
        self.core = lax.rem(links.uly, 2)
        self.row = lax.div(links.uly, 2)
        self.depth = parts.shape[3]
        self.core_copies = {}

    def chunk(self, dp, row, core, half=None):
        if self.own_core_only:
            part = self.parts.at[dp, row]
        else:
            part = self.parts.at[dp, :, row * 2 + core]
        if half is None:
            return part
        depth = self.depth // 2
        return part.at[:, pl.ds(half * depth, depth)]

    def add(self, target, source):
        blocks, depth, _ = target.shape
        rows = 32 if depth % 32 == 0 else 16

        def body(index, carry):
            block = lax.div(index, depth // rows)
            at = pl.ds(pl.multiple_of(lax.rem(index, depth // rows) * rows, rows), rows)
            target[block, at, :] = target[block, at, :] + source[block, at, :]
            return carry

        lax.fori_loop(0, blocks * (depth // rows), body, 0)

    def between_cores(self, which):
        links = self.links
        dp = links.dp if which == 1 else links.other_dp
        self.core_copies[which] = [
            links.to(
                self.chunk(dp, row, 1 - self.core), self.from_core.at[which, row], links.core_way
            )
            for row in range(2)
        ]

    def core_sums(self, which):
        links = self.links
        dp = links.dp if which == 1 else links.other_dp
        for row in range(2):
            self.core_copies[which][row].arrived()
            self.add(self.chunk(dp, row, self.core), self.from_core.at[which, row])

    def across_chips(self):
        links = self.links
        if not self.own_core_only:
            self.core_sums(0)
        self.x_copies = [
            links.to(
                self.chunk(links.other_dp, row, self.core, 0), self.from_x.at[row], links.x_way
            )
            for row in range(2)
        ]
        if not self.own_core_only:
            self.core_sums(1)
        self.y_copies = [
            links.to(
                self.chunk(group, 1 - self.row, self.core, 1),
                self.from_y.at[group],
                links.y_way,
            )
            for group in range(links.n_dp)
        ]

    def second_way(self):
        links = self.links
        for row in range(2):
            self.x_copies[row].arrived()
            self.add(self.chunk(links.dp, row, self.core, 0), self.from_x.at[row])
        self.y_last = links.to(
            self.chunk(links.dp, 1 - self.row, self.core, 0), self.last_y, links.y_way
        )
        for group in range(links.n_dp):
            self.y_copies[group].arrived()
            self.add(self.chunk(group, self.row, self.core, 1), self.from_y.at[group])
        self.x_last = links.to(
            self.chunk(links.other_dp, self.row, self.core, 1), self.last_x, links.x_way
        )

    def result(self, write):
        links = self.links
        for half, copy, source in ((0, self.y_last, self.last_y), (1, self.x_last, self.last_x)):
            copy.arrived()
            own = self.chunk(links.dp, self.row, self.core, half)
            blocks, depth, _ = source.shape
            rows = 32 if depth % 32 == 0 else 16

            def body(index, carry, own=own, source=source, half=half, depth=depth, rows=rows):
                block = lax.div(index, depth // rows)
                start = pl.multiple_of(lax.rem(index, depth // rows) * rows, rows)
                at = pl.ds(start, rows)
                value = own[block, at, :].astype(jnp.float32)
                value = value + source[block, at, :].astype(jnp.float32)
                write(block, pl.ds(pl.multiple_of(start + half * depth, rows), rows), value)
                return carry

            lax.fori_loop(0, blocks * (depth // rows), body, 0)


def plane_shapes(n_dp, blocks, n_uly, depth, width):
    return [
        (n_dp, blocks, n_uly, depth, width),
        (n_dp, 2, blocks, depth, width),
        (2, blocks, depth // 2, width),
        (n_dp, blocks, depth // 2, width),
        (blocks, depth // 2, width),
        (blocks, depth // 2, width),
    ]


def plane_scratch(*sizes):
    return [pltpu.VMEM(shape, jnp.bfloat16) for shape in plane_shapes(*sizes)]


def weight_grad(rows, right, parts, dp):
    _, blocks, n_uly, depth, width = parts.shape
    columns = 512

    def body(index, carry):
        at = pl.ds(pl.multiple_of(index * columns, columns), columns)
        part = jnp.dot(rows[...], right[:, at], preferred_element_type=jnp.float32)
        parts[dp, :, :, :, at] = part.astype(jnp.bfloat16).reshape(blocks, n_uly, depth, columns)
        return carry

    lax.fori_loop(0, width // columns, body, 0)


def rows_turned(left, parts, dp):
    count = parts.shape[1] * parts.shape[2] * parts.shape[3]
    return left[:, pl.ds(pl.multiple_of(dp * count, 128), count)].T


def turned(rows, cosine, sine):
    return rows * cosine + pltpu.roll(rows, HEAD_SIZE // 2, axis=1) * sine


def transposed_product(left, right):
    return lax.dot_general(
        left, right, (((0,), (0,)), ((), ())), preferred_element_type=jnp.float32
    )


def product_right(left, right):
    return lax.dot_general(
        left, right, (((1,), (1,)), ((), ())), preferred_element_type=jnp.float32
    )


SCORE_SCALE = 1.0 / math.sqrt(HEAD_SIZE)


def forward_kernel(
    toks,
    gain_rows,
    span_order,
    hidden,
    wq,
    wk,
    wv,
    wo,
    wg,
    wu,
    wd,
    cotangent,
    gains,
    q_gain,
    k_gain,
    all_qkv,
    all_wo,
    all_wg,
    all_wu,
    all_wd,
    all_cot,
    attn_gain,
    mlp_gain,
    cosine,
    sine,
    query_pos,
    key_pos,
    heads,
    normed,
    qkv,
    queries,
    key_values,
    lse,
    middle,
    all_normed,
    all_gains,
    all_hidden,
    near_qkv,
    near_wo,
    parts,
    rightward,
    leftward,
    own_normed,
    relay,
    send,
    recv,
    here,
):
    links = Links(send, recv, here)
    links.greet(links.peers() + [links.x_way, links.y_way, links.core_way])
    tokens, width = hidden.shape
    spans = halves(tokens)
    q_width, k_width = wq.shape[1] // links.n_blk, wk.shape[1] // links.n_blk
    chunk = all_qkv.at[links.dp, :, links.uly]
    swap = ColumnSwap(
        links, [(wq, chunk, 0), (wk, chunk, q_width), (wv, chunk, q_width + k_width)]
    )
    plane_wo = PlaneGather(links, rows_of(all_wo, False))
    plane_wd = PlaneGather(links, rows_of(all_wd, False))
    plane_qkv = PlaneGather(links, rows_of(all_qkv, True))
    plane_gain = PlaneGather(links, rows_of(all_gains, True))
    swap.start()
    my_gains = all_gains.at[links.dp, links.blk, links.uly]
    gain_swap = [links.to(gains, my_gains, device) for device in links.peers()]
    plane_wo.start(wo)
    line = HalvedLine(links, hidden, all_hidden)
    line.send(0)
    keep = [
        links.local(gains, my_gains),
        links.local(hidden, all_hidden.at[links.blk]),
        links.local(wo, all_wo.at[links.dp, links.uly]),
        links.local(wd, all_wd.at[links.dp, links.uly]),
        links.local(cotangent, all_cot.at[links.blk]),
    ]
    write_positions(links, span_order, toks, cosine, sine, query_pos, key_pos)
    swap.arrived()
    plane_qkv.start()
    keep[0].wait()
    for copy in gain_swap:
        copy.arrived()
    plane_gain.start()
    plane_wd.start(wd)
    plane_wo.hand_on()
    line.advance(1)
    plane_qkv.hand_on()
    plane_gain.hand_on()
    plane_wo.last()
    for step in range(2, links.n_blk - 1):
        line.advance(step)
    pairs = [(wg, all_wg), (wu, all_wu)]
    planes = [PlaneGather(links, rows_of(whole, True)) for _, whole in pairs]
    swaps = []
    for number, (weight, whole) in enumerate(pairs):
        piece = weight.shape[1] // links.n_dp // links.n_blk

        def source(blk, weight=weight, piece=piece):
            starts = [(group * links.n_blk + blk) * piece for group in range(links.n_dp)]
            if not isinstance(blk, int):
                starts = [pl.multiple_of(start, 128) for start in starts]
            return [weight.at[:, pl.ds(start, piece)] for start in starts]

        def target(origin, whole=whole, piece=piece):
            chunk = whole.at[links.dp, origin, links.uly]
            return [chunk.at[:, pl.ds(group * piece, piece)] for group in range(links.n_dp)]

        swap = LineSwap(links, source, target, relay.at[number])
        swap.hand_on(0)
        for own, place in zip(source(links.blk), target(links.blk)):
            keep.append(links.local(own, place))
        swaps.append(swap)
    cot_lines = HalvedLine(links, cotangent, all_cot).lines
    for half in cot_lines:
        half.send(0)
    plane_qkv.last()
    plane_gain.last()
    plane_gain.arrived()
    write_gains(links, all_gains, gain_rows, (attn_gain, mlp_gain))
    for copy in keep[1:]:
        copy.wait()
    plane_wo.arrived()
    plane_qkv.arrived()
    near = [links.local(all_qkv, near_qkv), links.local(all_wo, near_wo)]
    seqs, kv_heads, q_rows, _ = queries.shape
    q_len = key_values.shape[4]
    group = q_rows // q_len
    q_end = kv_heads * group * HEAD_SIZE
    k_end = q_end + kv_heads * HEAD_SIZE

    def norm(seq):
        def body(rows):
            for blk in range(links.n_blk):
                at = pl.ds(pl.multiple_of(seq * toks + rows.start, ROWS), ROWS)
                to = pl.ds(pl.multiple_of(seq * q_len + blk * toks + rows.start, ROWS), ROWS)
                source = all_hidden[blk, at, :].astype(jnp.float32)
                normed[to, :] = (source * rms_scale(source) * attn_gain[...]).astype(
                    jnp.bfloat16
                )

        each_block(toks, body)

    def rotated(seq, column, gain):
        pre = qkv[seq * q_len : (seq + 1) * q_len, column : column + HEAD_SIZE]
        gain = gain[...].astype(jnp.float32)
        return turned(pre * rms_scale(pre) * gain, cosine[...], sine[...]).astype(jnp.bfloat16)

    def project(seq):
        rows = slice(seq * q_len, (seq + 1) * q_len)
        for column in range(0, qkv.shape[1], 512):
            weight = near_qkv[:, :, :, :, column : column + 512].reshape(width, 512)
            qkv[rows, column : column + 512] = jnp.dot(
                normed[rows, :], weight, preferred_element_type=jnp.float32
            )
        for head in range(kv_heads):
            column = head * HEAD_SIZE
            key_values[links.uly, 0, seq, head] = rotated(seq, q_end + column, k_gain)
            key_values[links.uly, 1, seq, head] = qkv[
                rows, k_end + column : k_end + column + HEAD_SIZE
            ].astype(jnp.bfloat16)
        mine = key_values.at[links.uly, :, seq]
        copies = [links.to(mine, mine, way) for way in (links.core_way, links.y_way)]
        for head in range(kv_heads * group):
            at = pl.ds((head % group) * q_len, q_len)
            queries[seq, head // group, at, :] = rotated(seq, head * HEAD_SIZE, q_gain)
        return copies

    def hand_keys(seq, copies):
        copies[1].arrived()
        theirs = key_values.at[links.across, :, seq]
        copies.append(links.to(theirs, theirs, links.core_way))

    def attend(seq, head):
        def over_keys(piece, carry):
            total, mixed = carry
            rows = pl.ds(pl.multiple_of(piece * q_len, q_len), q_len)
            scores = product_right(key_values[piece, 0, seq, head], queries[seq, head])
            weights = jnp.where(
                query_pos[...] >= key_pos[rows, :], jnp.exp(scores * SCORE_SCALE), 0.0
            )
            total = total + jnp.sum(weights, axis=0, keepdims=True)
            mixed = mixed + transposed_product(
                key_values[piece, 1, seq, head], weights.astype(jnp.bfloat16)
            )
            return total, mixed

        total, mixed = lax.fori_loop(
            0,
            links.n_uly,
            over_keys,
            (
                jnp.zeros((1, q_rows), jnp.float32),
                jnp.zeros((HEAD_SIZE, q_rows), jnp.float32),
            ),
        )
        lse[seq * kv_heads + head] = jnp.log(total)
        attended = (mixed / total).T.astype(jnp.bfloat16)
        for member in range(group):
            column = (head * group + member) * HEAD_SIZE
            for blk in range(links.n_blk):
                row = (blk * seqs + seq) * toks
                start = member * q_len + blk * toks
                heads[row : row + toks, column : column + HEAD_SIZE] = attended[
                    start : start + toks, :
                ]

    sums = halved_sums(links, parts, rightward, leftward)
    def out_weight():
        return near_wo[...].reshape(heads.shape[1], width)

    def out_parts(seq):
        mixed = jnp.concatenate(
            [
                heads[(blk * seqs + seq) * toks : (blk * seqs + seq + 1) * toks, :]
                for blk in range(links.n_blk)
            ],
            axis=0,
        )
        for column in range(0, width, 512):
            parts[:, spans[seq], column : column + 512] = (
                jnp.dot(
                    mixed,
                    out_weight()[:, column : column + 512],
                    preferred_element_type=jnp.float32,
                )
                .astype(jnp.bfloat16)
                .reshape(links.n_blk, toks, 512)
            )
        sums[seq].start()

    key_copies = []
    for seq in range(seqs):
        line.lines[seq].arrived()
        norm(seq)
        if seq == 0:
            for copy in near:
                copy.wait()
        key_copies.append(project(seq))
    swaps[0].hand_on(1)
    plane_wd.hand_on()
    hand_keys(0, key_copies[0])
    for copy in (key_copies[0][0], key_copies[0][2]):
        copy.arrived()
    attend(0, 0)
    hand_keys(1, key_copies[1])
    for step in range(2, links.n_blk - 1):
        swaps[0].hand_on(step)
    for head in range(1, kv_heads):
        attend(0, head)
    out_parts(0)
    swaps[1].hand_on(1)
    swaps[0].arrived()
    planes[0].start()
    for copy in (key_copies[1][0], key_copies[1][2]):
        copy.arrived()
    attend(1, 0)
    sums[0].tick(1)
    for step in range(2, links.n_blk - 1):
        swaps[1].hand_on(step)
    for head in range(1, kv_heads):
        attend(1, head)
    out_parts(1)
    swaps[1].arrived()
    planes[1].start()
    later = range(2, links.n_blk - 1)
    for tick in later:
        sums[0].tick(tick)
    for half in cot_lines:
        half.arrived()
        half.send(1)
    plane_wd.last()
    planes[0].hand_on()
    lines = []

    def settle(half, rows_of_half):
        half.finish(middle.at[rows_of_half])

        def body(rows):
            at = pl.ds(pl.multiple_of(rows_of_half.start + rows.start, ROWS), ROWS)
            total = middle[at, :] + all_hidden[links.blk, at, :].astype(jnp.float32)
            middle[at, :] = total
            own_normed[at, :] = (total * rms_scale(total) * mlp_gain[...]).astype(jnp.bfloat16)

        each_block(tokens // 2, body)
        next_line = LineGather(links, own_normed.at[rows_of_half], all_normed.at[:, rows_of_half])
        next_line.send(0)
        lines.append(next_line)

    settle(sums[0], spans[0])
    sums[1].tick(1)
    for tick in later:
        sums[1].tick(tick)
    settle(sums[1], spans[1])
    for step in range(2, links.n_blk - 1):
        for half in cot_lines:
            half.arrived()
            half.send(step)
    last_local = links.local(own_normed, all_normed.at[links.blk])
    planes[1].hand_on()
    planes[0].last()
    for step in range(1, links.n_blk - 1):
        for half in lines:
            half.arrived()
            half.send(step)
    planes[1].last()
    for half in lines + cot_lines:
        half.arrived()
    for plane in [plane_wd] + planes:
        plane.arrived()
    last_local.wait()
    for half in sums + swaps:
        half.sent()
    links.finish()


SMEM = pl.BlockSpec(memory_space=pltpu.SMEM)


def forward(
    span_order,
    hidden,
    wq,
    wk,
    wv,
    wo,
    wg,
    wu,
    wd,
    cotangent,
    gains,
    q_gain,
    k_gain,
    seqs,
    gain_rows,
):
    n_dp, n_blk, n_uly = (lax.axis_size(a) for a in EVERY)
    tokens, width = hidden.shape
    toks = tokens // seqs
    rows, q_len = n_blk * tokens, n_blk * toks
    group = QUERY_HEADS // KEY_VALUE_HEADS
    kv_heads = KEY_VALUE_HEADS // n_blk
    q_rows, keys = group * q_len, n_uly * q_len
    columns = (wq.shape[1] + wk.shape[1] + wv.shape[1]) // n_blk
    f32, low, i32 = jnp.float32, jnp.bfloat16, jnp.int32
    ff = wg.shape[1] // n_blk
    far = [
        (n_dp, n_blk, n_uly, wq.shape[0], columns),
        (n_dp, n_uly) + wo.shape,
        (n_dp, n_blk, n_uly, wg.shape[0], ff),
        (n_dp, n_blk, n_uly, wu.shape[0], ff),
        (n_dp, n_uly) + wd.shape,
        (n_blk, tokens, width),
    ]
    near = [
        ((1, width), f32),
        ((1, width), f32),
        ((q_len, HEAD_SIZE), f32),
        ((q_len, HEAD_SIZE), f32),
        ((1, q_rows), i32),
        ((keys, 1), i32),
        ((rows, kv_heads * group * HEAD_SIZE), low),
        ((rows, width), low),
        ((rows, columns), f32),
        ((seqs, kv_heads, q_rows, HEAD_SIZE), low),
        ((n_uly, 2, seqs, kv_heads, q_len, HEAD_SIZE), low),
        ((seqs * kv_heads, 1, q_rows), f32),
        ((tokens, width), f32),
        ((n_blk, tokens, width), low),
    ]
    scratch = [
        ((n_dp, n_blk, n_uly) + gains.shape, low),
        ((n_blk, tokens, width), low),
        (far[0], low),
        (far[1], low),
        ((n_blk, tokens, width), low),
        ((n_blk - 1, tokens, width), low),
        ((n_blk - 1, tokens, width), low),
        ((tokens, width), low),
        ((2, relay_slots(n_blk), n_dp, wg.shape[0], ff // n_dp), low),
    ]
    return pl.pallas_call(
        functools.partial(forward_kernel, toks, gain_rows),
        out_shape=[jax.ShapeDtypeStruct(shape, low) for shape in far]
        + [jax.ShapeDtypeStruct(shape, kind) for shape, kind in near],
        in_specs=[SMEM] + [HBM] * 10 + [VMEM] * 2,
        out_specs=[HBM] * len(far) + [VMEM] * len(near),
        scratch_shapes=[pltpu.VMEM(shape, kind) for shape, kind in scratch]
        + semaphores(232, 32),
        compiler_params=kernel_params(0),
    )(span_order, hidden, wq, wk, wv, wo, wg, wu, wd, cotangent, gains, q_gain, k_gain)


def back_rows(grad_normed, source, gain):
    unit = source * rms_scale(source)
    scaled = grad_normed * gain
    return rms_scale(source) * (
        scaled - unit * jnp.mean(scaled * unit, axis=-1, keepdims=True)
    )


def back_kernel(
    grad_parts,
    out_parts,
    middle,
    cotangent,
    gain,
    all_normed,
    grad_gate_pre,
    grad_up_pre,
    activated,
    all_cot,
    output,
    grad_middle,
    all_low,
    grad_gate,
    grad_up,
    part_down,
    rightward,
    leftward,
    out_right,
    out_left,
    out_total,
    low,
    turned_low,
    gate_1,
    gate_2,
    gate_3,
    gate_4,
    gate_5,
    gate_6,
    up_1,
    up_2,
    up_3,
    up_4,
    up_5,
    up_6,
    down_1,
    down_2,
    send,
    recv,
    here,
):
    links = Links(send, recv, here)
    links.greet(links.peers() + [links.x_way, links.y_way, links.core_way])
    sums = halved_sums(links, grad_parts, rightward, leftward)
    for half in sums:
        half.start()
    out = OutputHalf(links, 0, out_parts, middle, out_right, out_left, out_total)
    gate = PlaneScatter(links, gate_1, gate_2, gate_3, gate_4, gate_5, gate_6)
    up = PlaneScatter(links, up_1, up_2, up_3, up_4, up_5, up_6)
    down = PlaneScatter(links, down_1, down_2, None, None, None, None)
    tokens = middle.shape[0]
    spans, lines, keep = halves(tokens), [], []

    def compute(plane, which, rows, right):
        dp = links.dp if which == 1 else links.other_dp
        weight_grad(rows, right, plane.parts, dp)
        plane.between_cores(which)

    def turn(which):
        dp = links.dp if which == 1 else links.other_dp
        turned_low[which] = rows_turned(all_normed, gate_1, dp)

    def compute_down(which):
        dp = links.dp if which == 1 else links.other_dp
        compute(down, which, rows_turned(activated, down_1, dp), all_cot)

    def settle(half, rows_of_half):
        half.finish(grad_middle.at[rows_of_half])

        def body(rows):
            at = pl.ds(pl.multiple_of(rows_of_half.start + rows.start, ROWS), ROWS)
            back = back_rows(grad_middle[at, :], middle[at, :], gain[...])
            grad = cotangent[at, :].astype(jnp.float32) + back
            grad_middle[at, :] = grad
            low[at, :] = grad.astype(jnp.bfloat16)

        each_block(tokens // 2, body)
        line = LineGather(links, low.at[rows_of_half], all_low.at[:, rows_of_half])
        line.send(0)
        lines.append(line)

    later = range(2, links.n_blk - 1)
    turn(0)
    compute(gate, 0, turned_low.at[0], grad_gate_pre)
    sums[0].tick(1)
    turn(1)
    compute(gate, 1, turned_low.at[1], grad_gate_pre)
    for tick in later:
        sums[0].tick(tick)
    gate.across_chips()
    settle(sums[0], spans[0])
    compute(up, 0, turned_low.at[0], grad_up_pre)
    sums[1].tick(1)
    compute(up, 1, turned_low.at[1], grad_up_pre)
    for tick in later:
        sums[1].tick(tick)
    up.across_chips()
    settle(sums[1], spans[1])
    out.sum.start()
    keep.append(links.local(low, all_low.at[links.blk]))
    compute_down(0)
    for step in range(1, links.n_blk - 1):
        for line in lines:
            line.arrived()
            line.send(step)
        if step == 1:
            gate.second_way()
            compute_down(1)
    out.sum.tick(1)
    up.second_way()
    for which in (0, 1):
        down.core_sums(which)
    for dp in range(links.n_dp):
        for row in range(2):
            keep.append(links.local(down.chunk(dp, row, down.core), part_down.at[dp, row]))
    for tick in later:
        out.sum.tick(tick)
    for line in lines:
        line.arrived()

    def into(target):
        def write(block, rows, values):
            target[block, rows, :] = values.astype(target.dtype)

        return write

    gate.result(into(grad_gate))
    up.result(into(grad_up))
    out.write(output)
    out.sum.sent()
    for copy in keep:
        copy.wait()
    for half in sums:
        half.sent()
    links.finish()


def exchange_back(
    grad_parts,
    out_parts,
    middle,
    cotangent,
    gain,
    all_normed,
    grad_gate_pre,
    grad_up_pre,
    activated,
    all_cot,
):
    n_dp, n_blk, n_uly = (lax.axis_size(a) for a in EVERY)
    _, tokens, width = grad_parts.shape
    ff = grad_gate_pre.shape[1]
    depth = width // (n_dp * n_blk * n_uly)
    down_depth = ff // (n_dp * n_uly)
    return pl.pallas_call(
        back_kernel,
        out_shape=[
            jax.ShapeDtypeStruct((tokens // 2, width), jnp.bfloat16),
            jax.ShapeDtypeStruct((tokens, width), jnp.float32),
            jax.ShapeDtypeStruct((n_blk, tokens, width), jnp.bfloat16),
            jax.ShapeDtypeStruct((n_blk, depth, ff), jnp.bfloat16),
            jax.ShapeDtypeStruct((n_blk, depth, ff), jnp.bfloat16),
            jax.ShapeDtypeStruct((n_dp, 2, 1, down_depth, width), jnp.bfloat16),
        ],
        in_specs=[VMEM] * 10,
        out_specs=[VMEM, VMEM, HBM, VMEM, VMEM, HBM],
        scratch_shapes=line_scratch(n_blk, tokens, width)
        + output_scratch(n_blk, tokens, width)
        + [
            pltpu.VMEM((tokens, width), jnp.bfloat16),
            pltpu.VMEM((n_dp, width // n_dp, n_blk * tokens), jnp.bfloat16),
        ]
        + plane_scratch(n_dp, n_blk, n_uly, depth, ff) * 2
        + plane_scratch(n_dp, 1, n_uly, down_depth, width)[:2]
        + semaphores(72),
        compiler_params=kernel_params(3),
    )(
        grad_parts,
        out_parts,
        middle,
        cotangent,
        gain,
        all_normed,
        grad_gate_pre,
        grad_up_pre,
        activated,
        all_cot,
    )


def backward_kernel(
    all_low,
    wo,
    queries,
    key_values,
    lse,
    qkv,
    q_gain,
    k_gain,
    cosine,
    sine,
    query_pos,
    key_pos,
    w_qkv,
    hidden,
    grad_middle,
    gain,
    normed,
    heads,
    out_parts,
    middle,
    grad_gate,
    grad_up,
    part_down,
    grad_hidden,
    grad_wo,
    grad_down,
    small_sum,
    output,
    gate_rows,
    up_rows,
    grad_w_qkv,
    grad_qkv,
    gain_terms,
    grad_heads,
    grad_rows,
    grad_kv,
    from_core,
    from_across,
    grad_parts,
    rightward,
    leftward,
    summed,
    small_in,
    small_total,
    out_right,
    out_left,
    out_total,
    relay,
    down_1,
    down_3,
    down_4,
    down_5,
    down_6,
    turned_normed,
    q_1,
    q_2,
    q_3,
    q_4,
    q_5,
    q_6,
    kv_1,
    kv_2,
    kv_3,
    kv_4,
    kv_5,
    kv_6,
    wo_1,
    wo_2,
    wo_3,
    wo_4,
    wo_5,
    wo_6,
    send,
    recv,
    here,
):
    links = Links(send, recv, here)
    links.greet(links.peers() + [links.x_way, links.y_way, links.core_way])
    tokens = hidden.shape[0]
    spans = halves(tokens)
    output_half = OutputHalf(links, 1, out_parts, middle, out_right, out_left, out_total)
    output_half.sum.start()
    down = PlaneScatter(links, down_1, None, down_3, down_4, down_5, down_6)
    fetch = links.local(part_down, down_1)
    swapped, keep = [], []
    swaps = []
    for number, (source, target) in enumerate(((grad_gate, gate_rows), (grad_up, up_rows))):
        swap = LineSwap(
            links,
            lambda blk, source=source: [source.at[blk]],
            lambda origin, target=target: [target.at[origin]],
            relay.at[number],
        )
        swap.hand_on(0)
        swaps.append(swap)
        keep.append(links.local(source.at[links.blk], target.at[links.blk]))
    fetch.wait()
    down.across_chips()
    sums = halved_sums(links, grad_parts, rightward, leftward)
    q_sums = PlaneScatter(links, q_1, q_2, q_3, q_4, q_5, q_6)
    kv_sums = PlaneScatter(links, kv_1, kv_2, kv_3, kv_4, kv_5, kv_6)
    wo_sums = PlaneScatter(links, wo_1, wo_2, wo_3, wo_4, wo_5, wo_6)
    seqs, kv_heads, q_rows, _ = queries.shape
    q_len = key_values.shape[4]
    group = q_rows // q_len
    toks = q_len // links.n_blk
    q_end = kv_heads * group * HEAD_SIZE
    k_end = q_end + kv_heads * HEAD_SIZE
    gain_terms[...] = jnp.zeros_like(gain_terms)
    later = range(2, links.n_blk - 1)

    def heads_back(seq):
        low = jnp.concatenate(
            [
                all_low[(blk * seqs + seq) * toks : (blk * seqs + seq + 1) * toks, :]
                for blk in range(links.n_blk)
            ],
            axis=0,
        )
        grad_heads[...] = product_right(low, wo[...])
        for head in range(kv_heads * group):
            to = pl.ds((head % group) * q_len, q_len)
            grad_rows[seq, head // group, to, :] = grad_heads[
                :, head * HEAD_SIZE : (head + 1) * HEAD_SIZE
            ].astype(jnp.bfloat16)

    def back_norm(upstream, seq, column, gain, which):
        rows = slice(seq * q_len, (seq + 1) * q_len)
        pre = qkv[rows, column : column + HEAD_SIZE]
        upstream = turned(upstream, cosine[...], -sine[...])
        gain_terms[which : which + 1, :] += jnp.sum(
            upstream * pre * rms_scale(pre), axis=0, keepdims=True
        )
        grad_qkv[rows, column : column + HEAD_SIZE] = back_rows(
            upstream, pre, gain[...].astype(jnp.float32)
        ).astype(jnp.bfloat16)

    def deltas(seq, head):
        sums_of = []
        for member in range(group):
            column = (head * group + member) * HEAD_SIZE
            attended = jnp.concatenate(
                [
                    heads[row : row + toks, column : column + HEAD_SIZE]
                    for row in ((blk * seqs + seq) * toks for blk in range(links.n_blk))
                ],
                axis=0,
            )
            upstream = grad_rows[seq, head, member * q_len : (member + 1) * q_len, :]
            sums_of.append(attended.astype(jnp.float32) * upstream.astype(jnp.float32))
        terms = jnp.concatenate(sums_of, axis=0)
        high = terms.astype(jnp.bfloat16)
        rest = (terms - high.astype(jnp.float32)).astype(jnp.bfloat16)
        ones = jnp.ones((16, HEAD_SIZE), jnp.bfloat16)
        return (product_right(ones, high) + product_right(ones, rest))[:1, :]

    def back(seq, head):
        delta = deltas(seq, head)

        def over_keys(piece, grad_query):
            rows = pl.ds(pl.multiple_of(piece * q_len, q_len), q_len)
            scores = product_right(key_values[piece, 0, seq, head], queries[seq, head])
            prob = jnp.where(
                query_pos[...] >= key_pos[rows, :],
                jnp.exp(scores * SCORE_SCALE - lse[seq * kv_heads + head]),
                0.0,
            )
            grad_prob = product_right(key_values[piece, 1, seq, head], grad_rows[seq, head])
            grad_score = (prob * (grad_prob - delta)).astype(jnp.bfloat16)
            grad_kv[seq, piece, 0, head] = (
                SCORE_SCALE
                * jnp.dot(grad_score, queries[seq, head], preferred_element_type=jnp.float32)
            ).astype(jnp.bfloat16)
            grad_kv[seq, piece, 1, head] = jnp.dot(
                prob.astype(jnp.bfloat16),
                grad_rows[seq, head],
                preferred_element_type=jnp.float32,
            ).astype(jnp.bfloat16)
            return grad_query + transposed_product(key_values[piece, 0, seq, head], grad_score)

        grad_query = lax.fori_loop(
            0, links.n_uly, over_keys, jnp.zeros((HEAD_SIZE, q_rows), jnp.float32)
        )
        turned_back = (grad_query * SCORE_SCALE).T
        for member in range(group):
            column = (head * group + member) * HEAD_SIZE
            back_norm(
                turned_back[member * q_len : (member + 1) * q_len, :], seq, column, q_gain, 0
            )

    core, line = lax.rem(links.uly, 2), lax.div(links.uly, 2)

    def add(target, source):
        for kind in range(2):
            for head in range(kv_heads):
                target[kind, head] = target[kind, head] + source[kind, head]

    def core_sums(seq):
        return [
            links.to(
                grad_kv.at[seq, row * 2 + 1 - core], from_core.at[seq, row], links.core_way
            )
            for row in range(2)
        ]

    def across_sums(seq, copies):
        for row in range(2):
            copies[row].arrived()
            add(grad_kv.at[seq, row * 2 + core], from_core.at[seq, row])
        return links.to(
            grad_kv.at[seq, (1 - line) * 2 + core], from_across.at[seq], links.y_way
        )

    def own_keys(seq, copy):
        copy.arrived()
        rows = slice(seq * q_len, (seq + 1) * q_len)
        for head in range(kv_heads):
            term = [
                grad_kv[seq, links.uly, kind, head].astype(jnp.float32)
                + from_across[seq, kind, head].astype(jnp.float32)
                for kind in range(2)
            ]
            back_norm(term[0], seq, q_end + head * HEAD_SIZE, k_gain, 1)
            v_at = k_end + head * HEAD_SIZE
            grad_qkv[rows, v_at : v_at + HEAD_SIZE] = term[1].astype(jnp.bfloat16)

    def normed_parts(seq):
        for column in range(0, w_qkv.shape[0], 512):
            grad_parts[:, spans[seq], column : column + 512] = (
                product_right(
                    grad_qkv[seq * q_len : (seq + 1) * q_len, :],
                    w_qkv[column : column + 512, :],
                )
                .astype(jnp.bfloat16)
                .reshape(links.n_blk, toks, 512)
            )
        sums[seq].start()

    def dp_of(which):
        return links.dp if which == 1 else links.other_dp

    def compute_wo(which):
        dp = dp_of(which)
        weight_grad(rows_turned(heads, wo_1, dp), all_low, wo_1, dp)
        wo_sums.between_cores(which)

    def compute_qkv(plane, which, columns):
        weight_grad(
            turned_normed.at[which], grad_qkv.at[:, columns], plane.parts, dp_of(which)
        )
        plane.between_cores(which)

    q_columns, kv_columns = pl.ds(0, q_end), pl.ds(q_end, grad_qkv.shape[1] - q_end)
    heads_back(0)
    back(0, 0)
    output_half.sum.tick(1)
    for head in range(1, kv_heads):
        back(0, head)
    core_copies = core_sums(0)
    heads_back(1)
    down.second_way()
    for which in range(2):
        turned_normed[which] = rows_turned(normed, q_1, dp_of(which))
    back(1, 0)
    across = across_sums(0, core_copies)
    swaps[0].hand_on(1)
    for tick in later:
        output_half.sum.tick(tick)
    for head in range(1, kv_heads):
        back(1, head)
    core_copies = core_sums(1)
    own_keys(0, across)
    across = across_sums(1, core_copies)
    swaps[1].hand_on(1)
    for step in later:
        swaps[0].hand_on(step)
    normed_parts(0)
    compute_qkv(q_sums, 0, q_columns)
    compute_qkv(q_sums, 1, q_columns)
    own_keys(1, across)
    for step in later:
        swaps[1].hand_on(step)
    small_total[0] = gain_terms[...]
    pending = links.to(small_total.at[0], small_in.at[links.n_blk], links.core_way)
    q_sums.across_chips()
    normed_parts(1)
    sums[0].tick(1)
    compute_qkv(kv_sums, 0, kv_columns)
    compute_qkv(kv_sums, 1, kv_columns)
    for tick in later:
        sums[0].tick(tick)
    pending.arrived()
    small_total[1] = small_total[0] + small_in[links.n_blk]
    pending = links.to(small_total.at[1], small_in.at[links.n_blk + 1], links.x_way)
    kv_sums.across_chips()
    q_sums.second_way()
    compute_wo(0)
    compute_wo(1)
    pending.arrived()
    small_total[2] = small_total[1] + small_in[links.n_blk + 1]
    pending = links.to(small_total.at[2], small_in.at[links.n_blk + 2], links.y_way)
    sums[1].tick(1)
    kv_sums.second_way()
    wo_sums.across_chips()

    def into(target):
        def write(block, rows, values):
            target[block, rows, :] = values.astype(target.dtype)

        return write

    def give_home(plane, columns):
        here, there = summed.at[:, :, columns], grad_w_qkv.at[links.blk, :, columns]
        plane.result(into(here))
        keep.append(links.local(here.at[links.blk], there))
        return links.swap(lambda peer: [(here.at[peer], there)])

    swapped += give_home(q_sums, q_columns)
    for tick in later:
        sums[1].tick(tick)
    pending.arrived()
    small_in[links.blk] = small_total[2] + small_in[links.n_blk + 2]
    mine = small_in.at[links.blk]
    small_copies = [links.to(mine, mine, device) for device in links.peers()]
    swapped += give_home(kv_sums, kv_columns)
    output_half.write(output)

    def settle(seq):
        sums[seq].finish(grad_hidden.at[spans[seq]])

        def body(rows):
            at = pl.ds(pl.multiple_of(spans[seq].start + rows.start, ROWS), ROWS)
            back = back_rows(grad_hidden[at, :], hidden[at, :].astype(jnp.float32), gain[...])
            grad_hidden[at, :] = grad_middle[at, :] + back

        each_block(toks, body)

    settle(0)
    wo_sums.second_way()
    down.result(into(grad_down))
    settle(1)
    wo_sums.result(into(grad_wo))
    for copy in small_copies:
        copy.arrived()
    total = small_in[0]
    for blk in range(1, links.n_blk):
        total = total + small_in[blk]
    small_sum[...] = total
    for copy in swapped:
        copy.arrived()
    for copy in keep:
        copy.wait()
    for swap in swaps:
        swap.arrived()
    for half in sums + swaps:
        half.sent()
    output_half.sum.sent()
    links.finish()


def backward(
    all_low,
    wo,
    queries,
    key_values,
    lse,
    qkv,
    q_gain,
    k_gain,
    cosine,
    sine,
    query_pos,
    key_pos,
    w_qkv,
    hidden,
    grad_middle,
    gain,
    normed,
    heads,
    out_parts,
    middle,
    grad_gate,
    grad_up,
    part_down,
):
    seqs, kv_heads, q_rows, _ = queries.shape
    n_uly, _, _, _, q_len, _ = key_values.shape
    n_blk, tokens, width = out_parts.shape
    n_dp, _, _, down_depth, _ = part_down.shape
    columns = qkv.shape[1]
    depth = width // (n_dp * n_blk * n_uly)
    out_depth = heads.shape[1] // (n_dp * n_uly)
    f32, low = jnp.float32, jnp.bfloat16
    small = (8, HEAD_SIZE)
    outs = [
        ((tokens, width), f32),
        ((1, out_depth, width), f32),
        ((1, down_depth, width), f32),
        (small, f32),
        ((tokens // 2, width), low),
        (grad_gate.shape, low),
        (grad_up.shape, low),
        ((n_blk, depth, columns), low),
    ]
    scratch = [
        (qkv.shape, low),
        (small, f32),
        ((q_len, heads.shape[1]), f32),
        (queries.shape, low),
        ((seqs, n_uly, 2, kv_heads, q_len, HEAD_SIZE), low),
        ((seqs, 2, 2, kv_heads, q_len, HEAD_SIZE), low),
        ((seqs, 2, kv_heads, q_len, HEAD_SIZE), low),
        (out_parts.shape, low),
        ((n_blk - 1, tokens, width), low),
        ((n_blk - 1, tokens, width), low),
        ((n_blk, depth, columns), low),
        ((n_blk + 3,) + small, f32),
        ((3,) + small, f32),
    ]
    down = [part_down.shape] + plane_shapes(n_dp, 1, n_uly, down_depth, width)[2:]
    return pl.pallas_call(
        backward_kernel,
        out_shape=[jax.ShapeDtypeStruct(shape, kind) for shape, kind in outs],
        in_specs=[VMEM] * 20 + [HBM] * 3,
        out_specs=[VMEM] * 5 + [HBM] * 3,
        scratch_shapes=[pltpu.VMEM(shape, kind) for shape, kind in scratch]
        + output_scratch(n_blk, tokens, width)
        + [pltpu.VMEM((2, relay_slots(n_blk), 1) + grad_gate.shape[1:], low)]
        + [pltpu.VMEM(shape, low) for shape in down]
        + [pltpu.VMEM((n_dp, width // n_dp, normed.shape[0]), low)]
        + plane_scratch(n_dp, n_blk, n_uly, depth, heads.shape[1])
        + plane_scratch(n_dp, n_blk, n_uly, depth, columns - heads.shape[1])
        + plane_scratch(n_dp, 1, n_uly, out_depth, width)
        + semaphores(144),
        compiler_params=kernel_params(4),
    )(
        all_low,
        wo,
        queries,
        key_values,
        lse,
        qkv,
        q_gain,
        k_gain,
        cosine,
        sine,
        query_pos,
        key_pos,
        w_qkv,
        hidden,
        grad_middle,
        gain,
        normed,
        heads,
        out_parts,
        middle,
        grad_gate,
        grad_up,
        part_down,
    )


def finish_kernel(
    gate,
    up,
    qkv,
    wo,
    wd,
    hidden,
    out_0,
    out_1,
    w_gate,
    w_up,
    w_query,
    key_weight,
    value_weight,
    attn_gain,
    mlp_gain,
    small,
    f_gate,
    f_up,
    f_q,
    f_k,
    f_v,
    f_wo,
    f_wd,
    f_hidden,
    f_out,
    f_attn,
    f_mlp,
    f_q_gain,
    f_k_gain,
):
    n_blk, depth, _ = gate.shape

    def place(source, offset, target):
        width = target.shape[1] // (n_blk * 2)
        for blk in range(n_blk):
            for group in range(2):
                to = (group * n_blk + blk) * width
                at = offset + group * width
                target[:, to : to + width] = source[blk, :, at : at + width].astype(jnp.float32)

    def gain_back(pairs, gain):
        total = jnp.zeros((depth, 128), jnp.float32)
        for weight, grad in pairs:
            for column in range(0, weight.shape[1], 128):
                at = slice(column, column + 128)
                total = total + weight[:, at].astype(jnp.float32) * grad[:, at]
        column = jnp.sum(total, axis=1, keepdims=True)
        square = (depth, depth)
        same = lax.broadcasted_iota(jnp.int32, square, 0) == lax.broadcasted_iota(
            jnp.int32, square, 1
        )
        return jnp.sum(jnp.where(same, column, 0.0), axis=0, keepdims=True) / gain[
            ...
        ].astype(jnp.float32)

    place(gate, 0, f_gate)
    place(up, 0, f_up)
    q_width = f_q.shape[1] // n_blk
    k_width = f_k.shape[1] // n_blk
    place(qkv, 0, f_q)
    place(qkv, q_width, f_k)
    place(qkv, q_width + k_width, f_v)
    f_q_gain[...] = small[0:1, :]
    f_k_gain[...] = small[1:2, :]
    f_wo[...] = wo[0]
    f_wd[...] = wd[0]
    f_hidden[...] = hidden[...]
    half = out_0.shape[0]
    f_out[:half, :] = out_0[...]
    f_out[half:, :] = out_1[...]
    f_attn[...] = gain_back(((w_query, f_q), (key_weight, f_k), (value_weight, f_v)), attn_gain)
    f_mlp[...] = gain_back(((w_gate, f_gate), (w_up, f_up)), mlp_gain)


def finish(gate, up, qkv, wo, wd, hidden, out_0, out_1, weights, gains, small):
    return pl.pallas_call(
        finish_kernel,
        out_shape=[jax.ShapeDtypeStruct(w.shape, jnp.float32) for w in weights]
        + [
            jax.ShapeDtypeStruct(wo.shape[1:], jnp.float32),
            jax.ShapeDtypeStruct(wd.shape[1:], jnp.float32),
            jax.ShapeDtypeStruct(hidden.shape, jnp.float32),
            jax.ShapeDtypeStruct(hidden.shape, jnp.bfloat16),
        ]
        + [jax.ShapeDtypeStruct(gain.shape, jnp.float32) for gain in gains]
        + [jax.ShapeDtypeStruct((1, small.shape[1]), jnp.float32)] * 2,
        in_specs=[VMEM] * 16,
        out_specs=[VMEM] * 13,
        compiler_params=pltpu.CompilerParams(vmem_limit_bytes=62 * MIB),
    )(gate, up, qkv, wo, wd, hidden, out_0, out_1, *weights, *gains, small)


def product(left, right):
    return jnp.dot(left, right, preferred_element_type=jnp.float32)


def shards(
    hidden,
    span_order,
    attn_gain,
    w_query,
    key_weight,
    value_weight,
    w_out,
    q_gain,
    k_gain,
    mlp_gain,
    w_gate,
    w_up,
    w_down,
    cotangent,
):
    seqs, toks, width = hidden.shape
    n_dp, n_blk, n_uly = (lax.axis_size(a) for a in EVERY)
    rows = n_blk * seqs * toks
    bf16 = jnp.bfloat16
    own_hidden = hidden.reshape(seqs * toks, width)
    own_cotangent = cotangent.reshape(seqs * toks, width)

    gain_q, gain_k = q_gain[None, :], k_gain[None, :]
    gain_rows = attn_gain.shape[0]
    own_gains = jnp.pad(jnp.stack([attn_gain, mlp_gain]), ((0, 30), (0, 128 - gain_rows)))
    (
        w_qkv,
        wo,
        all_wg,
        all_wu,
        all_wd,
        cot,
        g_attn,
        g_mlp,
        cosine,
        sine,
        query_pos,
        key_pos,
        heads_flat,
        normed,
        qkv,
        queries,
        key_values,
        lse,
        middle,
        normed2,
    ) = forward(
        span_order,
        own_hidden,
        w_query,
        key_weight,
        value_weight,
        w_out,
        w_gate,
        w_up,
        w_down,
        own_cotangent,
        own_gains,
        gain_q,
        gain_k,
        seqs,
        gain_rows,
    )
    w_qkv = w_qkv.reshape(width, -1)
    wo = wo.reshape(-1, width)
    wg, wu = all_wg.reshape(width, -1), all_wu.reshape(width, -1)
    wd = all_wd.reshape(-1, width)
    cot = cot.reshape(rows, width)
    normed2 = normed2.reshape(rows, width)
    gate_pre = product(normed2, wg)
    up_pre = product(normed2, wu)
    sigmoid_gate = jax.nn.sigmoid(gate_pre)
    activated = (gate_pre * sigmoid_gate * up_pre).astype(bf16)
    out_parts = product(activated, wd).astype(bf16)
    grad_act = product_right(cot, wd)
    grad_gate_pre = (
        grad_act * up_pre * sigmoid_gate * (1.0 + gate_pre * (1.0 - sigmoid_gate))
    ).astype(bf16)
    grad_up_pre = (grad_act * gate_pre * sigmoid_gate).astype(bf16)
    grad_parts = (product_right(grad_gate_pre, wg) + product_right(grad_up_pre, wu)).astype(bf16)
    blocks = (n_blk, seqs * toks, width)
    out_parts = out_parts.reshape(blocks)
    output_0, grad_middle, middle_low, grad_gate, grad_up, part_down = exchange_back(
        grad_parts.reshape(blocks),
        out_parts,
        middle,
        own_cotangent,
        g_mlp,
        normed2,
        grad_gate_pre,
        grad_up_pre,
        activated,
        cot,
    )
    middle_low = middle_low.reshape(rows, width)
    (
        grad_hidden,
        grad_out,
        grad_down,
        small,
        output_1,
        grad_gate,
        grad_up,
        grad_w_qkv,
    ) = backward(
        middle_low,
        wo,
        queries,
        key_values,
        lse,
        qkv,
        gain_q,
        gain_k,
        cosine,
        sine,
        query_pos,
        key_pos,
        w_qkv,
        own_hidden,
        grad_middle,
        g_attn,
        normed,
        heads_flat,
        out_parts,
        middle,
        grad_gate,
        grad_up,
        part_down,
    )
    (
        grad_gate,
        grad_up,
        grad_query,
        grad_key,
        grad_value,
        grad_out,
        grad_down,
        grad_hidden,
        output,
        grad_attn_gain,
        grad_mlp_gain,
        grad_q_gain,
        grad_k_gain,
    ) = finish(
        grad_gate,
        grad_up,
        grad_w_qkv,
        grad_out,
        grad_down,
        grad_hidden,
        output_0,
        output_1,
        (w_gate, w_up, w_query, key_weight, value_weight),
        [g[None, :] for g in (attn_gain, mlp_gain)],
        small,
    )
    return (
        output.reshape(hidden.shape),
        grad_hidden.reshape(hidden.shape),
        grad_attn_gain.reshape(gain_rows),
        grad_query,
        grad_key,
        grad_value,
        grad_out,
        grad_q_gain[0],
        grad_k_gain[0],
        grad_mlp_gain.reshape(gain_rows),
        grad_gate,
        grad_up,
        grad_down,
    )


def solution(mesh):
    n_dp, n_blk, n_uly = (mesh.shape[a] for a in EVERY)
    aligned = (n_dp, n_uly) == (2, 4) and KEY_VALUE_HEADS % (n_dp * n_blk) == 0
    in_specs = (
        TOKENS,
        P(),
        P(EVERY),
        P(EVERY, None),
        P(EVERY, None),
        P(EVERY, None),
        P(EVERY, None),
        P(),
        P(),
        P(EVERY),
        P(EVERY, None),
        P(EVERY, None),
        P(EVERY, None),
        TOKENS,
    )
    out_specs = (
        TOKENS,
        TOKENS,
        P(EVERY),
        P(EVERY, None),
        P(EVERY, None),
        P(EVERY, None),
        P(EVERY, None),
        P(),
        P(),
        P(EVERY),
        P(EVERY, None),
        P(EVERY, None),
        P(EVERY, None),
    )
    return jax.shard_map(
        shards if aligned else shards_general,
        mesh=mesh, in_specs=in_specs, out_specs=out_specs, check_vma=False)
```

```python
import functools
import math

import jax
import jax.numpy as jnp
from jax import lax
from jax.experimental import pallas as pl
from jax.experimental.pallas import tpu as pltpu
from jax.sharding import PartitionSpec as P

QUERY_HEADS = 16
KEY_VALUE_HEADS = 8
HEAD_SIZE = 128


DP, BLK, ULY = "dp", "blk", "uly"
EVERY = (DP, BLK, ULY)
PLANE = (DP, ULY)
TOKENS = P(DP, (BLK, ULY), None)
EQ_KGQD_NKD_TO_KGQN = "kgqd,nkd->kgqn"
EQ_KGQN_KGQD_TO_NKD = "kgqn,kgqd->nkd"
EQ_KGQN_NKD_TO_KGQD = "kgqn,nkd->kgqd"
EQ_KGQN_QKGD_TO_NKD = "kgqn,qkgd->nkd"
EQ_QKGD_NKD_TO_KGQN = "qkgd,nkd->kgqn"
EQ_STD_DE_TO_STE = "std,de->ste"
EQ_STD_DF_TO_STF = "std,df->stf"
EQ_STD_ED_TO_STE = "std,ed->ste"
EQ_STD_FD_TO_STF = "std,fd->stf"
EQ_STD_STE_TO_DE = "std,ste->de"
EQ_STD_STF_TO_DF = "std,stf->df"
EQ_STE_DE_TO_STD = "ste,de->std"
EQ_STE_ED_TO_STD = "ste,ed->std"
EQ_STE_STD_TO_ED = "ste,std->ed"
EQ_STF_DF_TO_STD = "stf,df->std"
EQ_STF_FD_TO_STD = "stf,fd->std"
EQ_STF_STD_TO_FD = "stf,std->fd"

EPSILON = 1e-06
ROPE_BASE = 1000000.0


def rms_scale(source):
    return lax.rsqrt(jnp.mean(source * source, axis=-1, keepdims=True) + EPSILON)


def norm_back(grad_normed, source, norm_scale, gain):
    unit_rows = source * norm_scale
    scaled = grad_normed * gain
    return norm_scale * (scaled - unit_rows * jnp.mean(scaled * unit_rows, axis=-1, keepdims=True))


def angles_of(positions, head_dim):
    freq_steps = jnp.arange(head_dim // 2, dtype=jnp.float32)
    inverse = jnp.exp(freq_steps * (-2.0 * math.log(ROPE_BASE) / head_dim))
    return positions.astype(jnp.float32)[:, None] * inverse[None, :]


def rotate(source, angles, direction):
    half_dim = source.shape[-1] // 2
    cosine = jnp.cos(angles)[:, None, :]
    sine_part = direction * jnp.sin(angles)[:, None, :]
    first_half = source[..., :half_dim]
    second_half = source[..., half_dim:]
    return jnp.concatenate(
        [
            first_half * cosine - second_half * sine_part,
            second_half * cosine + first_half * sine_part,
        ],
        axis=-1,
    )


def positions_of(places, span_order, half_len):
    blocks_of = places // half_len
    block_ids = jnp.arange(span_order.shape[0], dtype=jnp.int32)
    chosen = jnp.sum(
        jnp.where(blocks_of[:, None] == block_ids[None, :], span_order[None, :], 0), axis=1
    )
    return chosen * half_len + places % half_len


def add_rows(buffer, new_rows):
    return buffer + new_rows


def shards_general(
    hidden,
    span_order,
    attn_gain,
    w_query,
    key_weight,
    value_weight,
    w_out,
    q_gain,
    k_gain,
    mlp_gain,
    w_gate,
    w_up,
    w_down,
    cotangent,
):
    sequence_count = hidden.shape[0]
    token_count = hidden.shape[1]
    ulysses_group_size = lax.axis_size(ULY)
    local_q = QUERY_HEADS // ulysses_group_size
    local_key_value = KEY_VALUE_HEADS // ulysses_group_size
    query_group_width = QUERY_HEADS // KEY_VALUE_HEADS
    block_len = token_count * ulysses_group_size
    half_len = block_len // 2
    score_scale = 1.0 / math.sqrt(HEAD_SIZE)
    blk_index = lax.axis_index(BLK)
    uly_index = lax.axis_index(ULY)
    first_place = (blk_index * ulysses_group_size + uly_index) * token_count
    local_angles = angles_of(
        positions_of(first_place + jnp.arange(token_count, dtype=jnp.int32), span_order, half_len),
        HEAD_SIZE,
    )
    query_pos = positions_of(
        blk_index * block_len + jnp.arange(block_len, dtype=jnp.int32), span_order, half_len
    )
    g_attn, wq_all, wk_all, wv_all, wo_all = (
        lax.all_gather(attn_gain, EVERY, axis=0, tiled=True),
        lax.all_gather(w_query, EVERY, axis=0, tiled=True),
        lax.all_gather(key_weight, EVERY, axis=0, tiled=True),
        lax.all_gather(value_weight, EVERY, axis=0, tiled=True),
        lax.all_gather(w_out, EVERY, axis=0, tiled=True),
    )
    source = hidden.astype(jnp.float32)
    first_scale = rms_scale(source)
    normalized_input = (source * first_scale * g_attn.astype(jnp.float32)).astype(jnp.bfloat16)
    q_pre = jnp.einsum(
        EQ_STD_DE_TO_STE, normalized_input, wq_all, preferred_element_type=jnp.float32
    ).reshape(sequence_count, token_count, QUERY_HEADS, HEAD_SIZE)
    key_before_norm = jnp.einsum(
        EQ_STD_DE_TO_STE, normalized_input, wk_all, preferred_element_type=jnp.float32
    ).reshape(sequence_count, token_count, KEY_VALUE_HEADS, HEAD_SIZE)
    value_before_norm = jnp.einsum(
        EQ_STD_DE_TO_STE, normalized_input, wv_all, preferred_element_type=jnp.float32
    ).reshape(sequence_count, token_count, KEY_VALUE_HEADS, HEAD_SIZE)
    q_scale = rms_scale(q_pre)
    k_scale = rms_scale(key_before_norm)
    gain_q = q_gain.astype(jnp.float32)
    gain_k = k_gain.astype(jnp.float32)
    q_rot = rotate(q_pre * q_scale * gain_q, local_angles, 1.0).astype(jnp.bfloat16)
    k_rot = rotate(key_before_norm * k_scale * gain_k, local_angles, 1.0).astype(jnp.bfloat16)
    v_low = value_before_norm.astype(jnp.bfloat16)
    q_heads, k_heads, v_heads = (
        lax.all_to_all(q_rot, ULY, split_axis=2, concat_axis=1, tiled=True),
        lax.all_to_all(k_rot, ULY, split_axis=2, concat_axis=1, tiled=True),
        lax.all_to_all(v_low, ULY, split_axis=2, concat_axis=1, tiled=True),
    )
    q_group = q_heads.reshape(
        sequence_count, block_len, local_key_value, query_group_width, HEAD_SIZE
    )
    stat_shape = (sequence_count, local_key_value, query_group_width, block_len)
    start_state = (
        jnp.full(stat_shape, -1e30, jnp.float32),
        jnp.zeros(stat_shape, jnp.float32),
        jnp.zeros(stat_shape + (HEAD_SIZE,), jnp.float32),
    )
    key_piece = lax.all_gather(k_heads, BLK, axis=1, tiled=True)
    value_piece = lax.all_gather(v_heads, BLK, axis=1, tiled=True)
    key_pos = positions_of(jnp.arange(key_piece.shape[1], dtype=jnp.int32), span_order, half_len)
    allowed = query_pos[:, None] >= key_pos[None, :]

    def attend_one_sequence(members):
        query_rows, key_rows, value_rows, top_seq, total_seq, accum_seq = members
        scores = (
            jnp.einsum(EQ_QKGD_NKD_TO_KGQN, query_rows, key_rows, preferred_element_type=jnp.float32)
            * score_scale
        )
        scores = jnp.where(allowed, scores, -jnp.inf)
        new_top = jnp.maximum(top_seq, jnp.max(scores, axis=-1))
        fading = jnp.exp(top_seq - new_top)
        weights = jnp.exp(scores - new_top[..., None])
        total_seq = total_seq * fading + jnp.sum(weights, axis=-1)
        accum_seq = accum_seq * fading[..., None] + jnp.einsum(
            EQ_KGQN_NKD_TO_KGQD,
            weights.astype(jnp.bfloat16),
            value_rows,
            preferred_element_type=jnp.float32,
        )
        return (new_top, total_seq, accum_seq)

    row_top, row_total, accum = lax.map(
        attend_one_sequence,
        (q_group, key_piece, value_piece, start_state[0], start_state[1], start_state[2]),
    )
    log_total = row_top + jnp.log(row_total)
    attention_output = jnp.transpose(accum / row_total[..., None], (0, 3, 1, 2, 4)).reshape(
        sequence_count, block_len, local_q, HEAD_SIZE
    )
    heads_seq = lax.all_to_all(
        attention_output.astype(jnp.bfloat16), ULY, split_axis=1, concat_axis=2, tiled=True
    )
    heads_flat = heads_seq.reshape(sequence_count, token_count, QUERY_HEADS * HEAD_SIZE)
    middle = source + jnp.einsum(
        EQ_STE_ED_TO_STD, heads_flat, wo_all, preferred_element_type=jnp.float32
    )
    g_mlp, wg_all, wu_all, wd_all = (
        lax.all_gather(mlp_gain, EVERY, axis=0, tiled=True),
        lax.all_gather(w_gate, EVERY, axis=0, tiled=True),
        lax.all_gather(w_up, EVERY, axis=0, tiled=True),
        lax.all_gather(w_down, EVERY, axis=0, tiled=True),
    )
    second_scale = rms_scale(middle)
    gain_mlp = g_mlp.astype(jnp.float32)
    normed2 = (middle * second_scale * gain_mlp).astype(jnp.bfloat16)
    gate_pre = jnp.einsum(EQ_STD_DF_TO_STF, normed2, wg_all, preferred_element_type=jnp.float32)
    up_pre = jnp.einsum(EQ_STD_DF_TO_STF, normed2, wu_all, preferred_element_type=jnp.float32)
    sigmoid_gate = jax.nn.sigmoid(gate_pre)
    activated = (gate_pre * sigmoid_gate * up_pre).astype(jnp.bfloat16)
    result = middle + jnp.einsum(
        EQ_STF_FD_TO_STD, activated, wd_all, preferred_element_type=jnp.float32
    )
    output = result.astype(jnp.bfloat16)
    g_mlp, wg_all, wu_all, wd_all = (
        lax.all_gather(mlp_gain, EVERY, axis=0, tiled=True),
        lax.all_gather(w_gate, EVERY, axis=0, tiled=True),
        lax.all_gather(w_up, EVERY, axis=0, tiled=True),
        lax.all_gather(w_down, EVERY, axis=0, tiled=True),
    )
    gain_mlp = g_mlp.astype(jnp.float32)
    grad_act = jnp.einsum(EQ_STD_FD_TO_STF, cotangent, wd_all, preferred_element_type=jnp.float32)
    grad_gate_pre = (
        grad_act * up_pre * sigmoid_gate * (1.0 + gate_pre * (1.0 - sigmoid_gate))
    ).astype(jnp.bfloat16)
    grad_up_pre = (grad_act * gate_pre * sigmoid_gate).astype(jnp.bfloat16)
    grad_gate = jnp.einsum(
        EQ_STD_STF_TO_DF, normed2, grad_gate_pre, preferred_element_type=jnp.float32
    )
    grad_up = jnp.einsum(EQ_STD_STF_TO_DF, normed2, grad_up_pre, preferred_element_type=jnp.float32)
    grad_normed2 = jnp.einsum(
        EQ_STF_DF_TO_STD, grad_gate_pre, wg_all, preferred_element_type=jnp.float32
    ) + jnp.einsum(EQ_STF_DF_TO_STD, grad_up_pre, wu_all, preferred_element_type=jnp.float32)
    mlp_gain_term = jnp.sum(grad_normed2 * middle * second_scale, axis=(0, 1))
    grad_middle = cotangent.astype(jnp.float32) + norm_back(
        grad_normed2, middle, second_scale, gain_mlp
    )
    grad_mlp_gain, grad_gate, grad_up = (
        lax.psum_scatter(mlp_gain_term, EVERY, scatter_dimension=0, tiled=True),
        lax.psum_scatter(grad_gate, EVERY, scatter_dimension=0, tiled=True),
        lax.psum_scatter(grad_up, EVERY, scatter_dimension=0, tiled=True),
    )
    g_attn, wq_all, wk_all, wv_all, wo_all = (
        lax.all_gather(attn_gain, EVERY, axis=0, tiled=True),
        lax.all_gather(w_query, EVERY, axis=0, tiled=True),
        lax.all_gather(key_weight, EVERY, axis=0, tiled=True),
        lax.all_gather(value_weight, EVERY, axis=0, tiled=True),
        lax.all_gather(w_out, EVERY, axis=0, tiled=True),
    )
    middle_low = grad_middle.astype(jnp.bfloat16)
    grad_out = jnp.einsum(EQ_STE_STD_TO_ED, heads_flat, middle_low, preferred_element_type=jnp.float32)
    grad_heads = (
        jnp.einsum(EQ_STD_ED_TO_STE, middle_low, wo_all, preferred_element_type=jnp.float32)
        .astype(jnp.bfloat16)
        .reshape(sequence_count, token_count, QUERY_HEADS, HEAD_SIZE)
    )
    grad_heads_local = lax.all_to_all(grad_heads, ULY, split_axis=2, concat_axis=1, tiled=True)
    grad_group = jnp.transpose(
        grad_heads_local.reshape(
            sequence_count, block_len, local_key_value, query_group_width, HEAD_SIZE
        ),
        (0, 2, 3, 1, 4),
    )
    delta = jnp.sum(grad_heads_local.astype(jnp.float32) * attention_output, axis=-1)
    delta = jnp.transpose(
        delta.reshape(sequence_count, block_len, local_key_value, query_group_width), (0, 2, 3, 1)
    )
    seq_length = block_len * lax.axis_size(BLK)
    zero_keys = jnp.zeros((sequence_count, seq_length, local_key_value, HEAD_SIZE), jnp.float32)
    back_state = (jnp.zeros(stat_shape + (HEAD_SIZE,), jnp.float32), zero_keys, zero_keys)
    key_piece = lax.all_gather(k_heads, BLK, axis=1, tiled=True)
    value_piece = lax.all_gather(v_heads, BLK, axis=1, tiled=True)
    key_pos = positions_of(jnp.arange(key_piece.shape[1], dtype=jnp.int32), span_order, half_len)
    back_allowed = query_pos[:, None] >= key_pos[None, :]

    def back_one_sequence(members):
        query_rows, grad_rows, lse_seq, delta_seq, key_rows, value_rows, dq_seq, dk_seq, dv_seq = (
            members
        )
        scores = (
            jnp.einsum(EQ_QKGD_NKD_TO_KGQN, query_rows, key_rows, preferred_element_type=jnp.float32)
            * score_scale
        )
        scores = jnp.where(back_allowed, scores, -jnp.inf)
        probs = jnp.exp(scores - lse_seq[..., None])
        grad_values = jnp.einsum(
            EQ_KGQN_KGQD_TO_NKD,
            probs.astype(jnp.bfloat16),
            grad_rows,
            preferred_element_type=jnp.float32,
        )
        grad_probs = jnp.einsum(
            EQ_KGQD_NKD_TO_KGQN, grad_rows, value_rows, preferred_element_type=jnp.float32
        )
        grad_scores = (probs * (grad_probs - delta_seq[..., None])).astype(jnp.bfloat16)
        dq_seq = dq_seq + score_scale * jnp.einsum(
            EQ_KGQN_NKD_TO_KGQD, grad_scores, key_rows, preferred_element_type=jnp.float32
        )
        grad_keys = score_scale * jnp.einsum(
            EQ_KGQN_QKGD_TO_NKD, grad_scores, query_rows, preferred_element_type=jnp.float32
        )
        return (dq_seq, add_rows(dk_seq, grad_keys), add_rows(dv_seq, grad_values))

    grad_q_group, grad_k_whole, grad_v_whole = lax.map(
        back_one_sequence,
        (
            q_group,
            grad_group,
            log_total,
            delta,
            key_piece,
            value_piece,
            back_state[0],
            back_state[1],
            back_state[2],
        ),
    )
    grad_k_block, grad_v_block = (
        lax.psum_scatter(
            grad_k_whole.astype(jnp.bfloat16), BLK, scatter_dimension=1, tiled=True
        ).astype(jnp.float32),
        lax.psum_scatter(
            grad_v_whole.astype(jnp.bfloat16), BLK, scatter_dimension=1, tiled=True
        ).astype(jnp.float32),
    )
    grad_q_block = jnp.transpose(grad_q_group, (0, 3, 1, 2, 4)).reshape(
        sequence_count, block_len, local_q, HEAD_SIZE
    )
    grad_q_seq, grad_k_seq, value_sequence_gradient = (
        lax.all_to_all(
            grad_q_block.astype(jnp.bfloat16), ULY, split_axis=1, concat_axis=2, tiled=True
        ).astype(grad_q_block.dtype),
        lax.all_to_all(
            grad_k_block.astype(jnp.bfloat16), ULY, split_axis=1, concat_axis=2, tiled=True
        ).astype(grad_k_block.dtype),
        lax.all_to_all(
            grad_v_block.astype(jnp.bfloat16), ULY, split_axis=1, concat_axis=2, tiled=True
        ).astype(grad_v_block.dtype),
    )
    grad_q_normed = rotate(grad_q_seq, local_angles, -1.0)
    grad_k_normed = rotate(grad_k_seq, local_angles, -1.0)
    q_gain_term = jnp.sum(grad_q_normed * q_pre * q_scale, axis=(0, 1, 2))
    k_gain_term = jnp.sum(grad_k_normed * key_before_norm * k_scale, axis=(0, 1, 2))
    grad_q_pre = (
        norm_back(grad_q_normed, q_pre, q_scale, gain_q)
        .astype(jnp.bfloat16)
        .reshape(sequence_count, token_count, QUERY_HEADS * HEAD_SIZE)
    )
    grad_k_pre = (
        norm_back(grad_k_normed, key_before_norm, k_scale, gain_k)
        .astype(jnp.bfloat16)
        .reshape(sequence_count, token_count, KEY_VALUE_HEADS * HEAD_SIZE)
    )
    value_pre_gradient = value_sequence_gradient.astype(jnp.bfloat16).reshape(
        sequence_count, token_count, KEY_VALUE_HEADS * HEAD_SIZE
    )
    grad_query = jnp.einsum(
        EQ_STD_STE_TO_DE, normalized_input, grad_q_pre, preferred_element_type=jnp.float32
    )
    grad_key = jnp.einsum(
        EQ_STD_STE_TO_DE, normalized_input, grad_k_pre, preferred_element_type=jnp.float32
    )
    grad_value = jnp.einsum(
        EQ_STD_STE_TO_DE, normalized_input, value_pre_gradient, preferred_element_type=jnp.float32
    )
    grad_normed = jnp.einsum(EQ_STE_DE_TO_STD, grad_q_pre, wq_all, preferred_element_type=jnp.float32)
    grad_normed = grad_normed + jnp.einsum(
        EQ_STE_DE_TO_STD, grad_k_pre, wk_all, preferred_element_type=jnp.float32
    )
    grad_normed = grad_normed + jnp.einsum(
        EQ_STE_DE_TO_STD, value_pre_gradient, wv_all, preferred_element_type=jnp.float32
    )
    attn_gain_term = jnp.sum(grad_normed * source * first_scale, axis=(0, 1))
    grad_hidden = grad_middle + norm_back(
        grad_normed, source, first_scale, g_attn.astype(jnp.float32)
    )
    grad_down = jnp.einsum(EQ_STF_STD_TO_FD, activated, cotangent, preferred_element_type=jnp.float32)
    grad_attn_gain, grad_query, grad_key, grad_value, grad_out, grad_down = (
        lax.psum_scatter(attn_gain_term, EVERY, scatter_dimension=0, tiled=True),
        lax.psum_scatter(grad_query, EVERY, scatter_dimension=0, tiled=True),
        lax.psum_scatter(grad_key, EVERY, scatter_dimension=0, tiled=True),
        lax.psum_scatter(grad_value, EVERY, scatter_dimension=0, tiled=True),
        lax.psum_scatter(grad_out, EVERY, scatter_dimension=0, tiled=True),
        lax.psum_scatter(grad_down, EVERY, scatter_dimension=0, tiled=True),
    )
    grad_q_gain, grad_k_gain = lax.psum((q_gain_term, k_gain_term), EVERY)
    return (
        output,
        grad_hidden,
        grad_attn_gain,
        grad_query,
        grad_key,
        grad_value,
        grad_out,
        grad_q_gain,
        grad_k_gain,
        grad_mlp_gain,
        grad_gate,
        grad_up,
        grad_down,
    )


MESH = pl.DeviceIdType.MESH
HBM = pl.BlockSpec(memory_space=pltpu.HBM)
VMEM = pl.BlockSpec(memory_space=pltpu.VMEM)
MIB = 1 << 20


def kernel_params(collective_id, vmem_mib=62):
    return pltpu.CompilerParams(
        collective_id=collective_id, has_side_effects=True, vmem_limit_bytes=vmem_mib * MIB
    )


def semaphores(count, local=16):
    return [
        pltpu.SemaphoreType.DMA((count,)),
        pltpu.SemaphoreType.DMA((count,)),
        pltpu.SemaphoreType.DMA((local,)),
    ]


class Copy:
    def __init__(self, descriptor, sends, receives):
        self.descriptor, self.sends, self.receives = descriptor, sends, receives

    def under(self, condition, action):
        if condition is None:
            action()
        else:
            pl.when(condition)(action)

    def start(self):
        self.under(self.sends, lambda: self.descriptor().start())
        return self

    def sent(self):
        self.under(self.sends, lambda: self.descriptor().wait_send())

    def arrived(self):
        self.under(self.receives, lambda: self.descriptor().wait_recv())


class Links:
    def __init__(self, send, recv, here):
        self.send, self.recv, self.here = send, recv, here
        self.used, self.used_here = 0, 0
        self.copies, self.local_copies = [], []
        self.n_dp, self.n_blk, self.n_uly = (lax.axis_size(a) for a in EVERY)
        self.dp, self.blk, self.uly = (lax.axis_index(a) for a in EVERY)
        self.other_dp = 1 - self.dp
        self.across = lax.rem(self.uly + 2, 4)
        self.twin = self.uly + 1 - 2 * lax.rem(self.uly, 2)
        self.x_way = (self.other_dp, self.blk, self.uly)
        self.y_way = (self.dp, self.blk, self.across)
        self.core_way = (self.dp, self.blk, self.twin)

    def peer(self, step):
        return lax.rem(self.blk + step, self.n_blk)

    def peers(self):
        return [(self.dp, self.peer(k), self.uly) for k in range(1, self.n_blk)]

    def far_first(self):
        last = self.n_blk - 1
        orders = [
            sorted((p for p in range(self.n_blk) if p != b), key=lambda p, b=b: -abs(p - b))
            for b in range(self.n_blk)
        ]
        for b, order in enumerate(orders):
            ways = [[p for p in order if p > b], [p for p in order if p < b]]
            ways.sort(key=lambda way: -len(way))
            merged = []
            while ways[0] or ways[1]:
                for way in ways:
                    if way:
                        merged.append(way.pop(0))
            orders[b] = merged
        peers = []
        for turn in range(last):
            peer = jnp.int32(0)
            for b, order in enumerate(orders):
                peer = jnp.where(self.blk == b, order[turn], peer)
            peers.append(peer)
        return peers

    def swap(self, pieces_for):
        base, count = self.used, 0
        for peer in self.far_first():
            pieces = pieces_for(peer)
            count = len(pieces)
            distance = lax.rem(peer - self.blk + self.n_blk, self.n_blk) - 1
            for number, (source, target) in enumerate(pieces):
                self.swap_copy(base + distance * count + number, source, target, peer).start()
        self.used = base + (self.n_blk - 1) * count
        waits = []
        for slot in range(base, self.used):
            source, target = pieces_for(self.blk)[(slot - base) % count]

            def descriptor(slot=slot, source=source, target=target):
                return self.swap_copy(slot, source, target, self.peer(1))

            copy = Copy(descriptor, None, None)
            self.copies.append(copy)
            waits.append(copy)
        return waits

    def swap_copy(self, slot, source, target, peer):
        return pltpu.make_async_remote_copy(
            src_ref=source,
            dst_ref=target,
            send_sem=self.send.at[slot],
            recv_sem=self.recv.at[slot],
            device_id=(self.dp, peer, self.uly),
            device_id_type=MESH,
        )

    def greet(self, devices):
        barrier = pltpu.get_barrier_semaphore()
        for device in devices:
            pl.semaphore_signal(barrier, inc=1, device_id=device, device_id_type=MESH)
        pl.semaphore_wait(barrier, len(devices))

    def remote(self, source, target, device, sends=None, receives=None):
        slot = self.used
        self.used += 1

        def descriptor():
            return pltpu.make_async_remote_copy(
                src_ref=source(),
                dst_ref=target(),
                send_sem=self.send.at[slot],
                recv_sem=self.recv.at[slot],
                device_id=device,
                device_id_type=MESH,
            )

        copy = Copy(descriptor, sends, receives)
        self.copies.append(copy)
        return copy.start()

    def to(self, source, target, device):
        return self.remote(lambda: source, lambda: target, device)

    def local(self, source, target):
        copy = pltpu.make_async_copy(source, target, self.here.at[self.used_here])
        self.used_here += 1
        copy.start()
        self.local_copies.append(copy)
        return copy

    def finish(self):
        assert self.used <= self.send.shape[0] and self.used_here <= self.here.shape[0]
        for copy in self.copies:
            copy.sent()


class LineGather:
    def __init__(self, links, own, whole):
        self.links, self.own, self.whole = links, own, whole
        self.waiting = []

    def send(self, step):
        links, whole = self.links, self.whole
        blk, last = links.blk, links.n_blk - 1

        def block(index):
            if step == 0:
                return lambda: self.own
            return lambda: whole.at[index]

        self.waiting = [
            links.remote(
                block(blk - step),
                lambda: whole.at[blk - step],
                (links.dp, blk + 1, links.uly),
                jnp.logical_and(blk >= step, blk < last),
                blk >= step + 1,
            ),
            links.remote(
                block(blk + step),
                lambda: whole.at[blk + step],
                (links.dp, blk - 1, links.uly),
                jnp.logical_and(blk + step <= last, blk > 0),
                blk + step + 1 <= last,
            ),
        ]

    def arrived(self):
        for copy in self.waiting:
            copy.arrived()


def halves(tokens):
    return [pl.ds(0, tokens // 2), pl.ds(tokens // 2, tokens // 2)]


class HalvedLine:
    def __init__(self, links, own, whole):
        self.lines = [
            LineGather(links, None if own is None else own.at[rows], whole.at[:, rows])
            for rows in halves(whole.shape[1])
        ]

    def send(self, step):
        for line in self.lines:
            line.send(step)

    def advance(self, step):
        for line in self.lines:
            line.arrived()
            line.send(step)

    def arrived(self):
        for line in self.lines:
            line.arrived()


class PlaneGather:
    def __init__(self, links, at):
        self.links, self.at = links, at

    def start_x(self, own):
        links = self.links
        mine = self.at(links.dp, links.uly)
        self.from_x = links.to(own, mine, links.x_way)
        self.from_core = [links.to(own, mine, links.core_way)]

    def start_y(self, own):
        links = self.links
        self.from_y = links.to(own, self.at(links.dp, links.uly), links.y_way)

    def start(self, own=None):
        own = self.at(self.links.dp, self.links.uly) if own is None else own
        self.start_x(own)
        self.start_y(own)

    def hand_on(self):
        links, at = self.links, self.at
        self.from_x.arrived()
        half = at(links.other_dp, links.uly, 0)
        self.second_y = links.to(half, half, links.y_way)
        self.from_y.arrived()
        half = at(links.dp, links.across, 1)
        self.second_x = links.to(half, half, links.x_way)
        for chunk in (at(links.other_dp, links.uly), at(links.dp, links.across)):
            self.from_core.append(links.to(chunk, chunk, links.core_way))

    def last(self):
        links = self.links
        self.second_y.arrived()
        self.second_x.arrived()
        chunk = self.at(links.other_dp, links.across)
        self.from_core.append(links.to(chunk, chunk, links.core_way))

    def arrived(self):
        for copy in self.from_core:
            copy.arrived()


def rows_of(whole, blocked):
    def at(dp, uly, half=None):
        part = whole.at[dp, :, uly] if blocked else whole.at[dp, uly]
        if half is None:
            return part
        depth = whole.shape[-2] // 2
        rows = pl.ds(half * depth, depth)
        return part.at[:, rows] if blocked else part.at[rows]

    return at


class LineSwap:
    def __init__(self, links, source, target, relay):
        self.links, self.source, self.target = links, source, target
        self.base, self.last = links.used, links.n_blk - 1
        self.count = len(target(links.blk))
        links.used += 2 * self.last * links.n_blk * self.count
        self.slots = {}
        for way in (1, -1):
            for step in range(self.last):
                for steps_on in range(step + 2, links.n_blk):
                    bound = steps_on if way == 1 else self.last - steps_on
                    self.slots[way, step, bound] = relay.at[len(self.slots)]

    def copies(self, way, step, bound, target):
        links = self.links
        first = ((1 if way == 1 else 0) * self.last + step) * links.n_blk + bound
        if step == 0:
            source = self.source(bound)
        else:
            slot = self.slots.get((way, step - 1, bound))
            source = target if slot is None else [slot.at[n] for n in range(self.count)]
        return [
            pltpu.make_async_remote_copy(
                src_ref=source[number],
                dst_ref=target[number],
                send_sem=links.send.at[self.base + first * self.count + number],
                recv_sem=links.recv.at[self.base + first * self.count + number],
                device_id=(links.dp, links.blk + way, links.uly),
                device_id_type=MESH,
            )
            for number in range(self.count)
        ]

    def bounds(self, way, step):
        ahead = [n for n in range(self.links.n_blk) if n > step]
        return [n if way == 1 else self.last - n for n in reversed(ahead)]

    def sends(self, way, step, bound):
        blk = self.links.blk
        if way == 1:
            return jnp.logical_and(blk >= step, bound > blk)
        return jnp.logical_and(blk + step <= self.last, bound < blk)

    def relayed(self, way, step, bound):
        slot = self.slots.get((way, step, bound))
        return None if slot is None else [slot.at[n] for n in range(self.count)]

    def hand_on(self, step):
        links = self.links
        for near, way in enumerate((1, -1)):
            for bound in self.bounds(way, step):

                @pl.when(self.sends(way, step, bound))
                def _(way=way, bound=bound):
                    if step > 0:
                        for copy in self.copies(
                            way, step - 1, bound, self.relayed(way, step - 1, bound)
                        ):
                            copy.wait_recv()
                    final = links.blk + way == bound

                    @pl.when(final)
                    def _():
                        origin = links.blk - way * step
                        for copy in self.copies(way, step, bound, self.target(origin)):
                            copy.start()

                    onward = self.relayed(way, step, bound)
                    if onward is not None:

                        @pl.when(jnp.logical_not(final))
                        def _():
                            for copy in self.copies(way, step, bound, onward):
                                copy.start()

    def arrived(self):
        links = self.links
        for step in range(self.last):
            for way in (1, -1):
                place = links.blk if way == 1 else self.last - links.blk

                @pl.when(place >= step + 1)
                def _(way=way, step=step):
                    origin = links.blk - way * (step + 1)
                    target = self.target(origin)
                    first = ((1 if way == 1 else 0) * self.last + step) * links.n_blk + links.blk
                    for number in range(self.count):
                        at = self.base + first * self.count + number
                        pltpu.make_async_remote_copy(
                            src_ref=target[number],
                            dst_ref=target[number],
                            send_sem=links.send.at[at],
                            recv_sem=links.recv.at[at],
                            device_id=(links.dp, links.blk - way, links.uly),
                            device_id_type=MESH,
                        ).wait_recv()

    def sent(self):
        for step in range(self.last):
            for way in (1, -1):
                for bound in self.bounds(way, step):

                    @pl.when(self.sends(way, step, bound))
                    def _(way=way, step=step, bound=bound):
                        for copy in self.copies(
                            way, step, bound, self.target(self.links.blk)
                        ):
                            copy.wait_send()


def relay_slots(n_blk):
    return (n_blk - 1) * (n_blk - 2)


class ColumnSwap:
    def __init__(self, links, pieces):
        self.links, self.pieces = links, pieces
        self.incoming, self.kept = [], []

    def parts(self, blk):
        links = self.links
        for weight, whole, offset in self.pieces:
            width = weight.shape[-1] // links.n_dp // links.n_blk
            for group in range(links.n_dp):
                start = (group * links.n_blk + blk) * width
                yield (
                    weight.at[:, pl.ds(pl.multiple_of(start, 128), width)],
                    whole.at[links.blk, :, pl.ds(offset + group * width, width)],
                )

    def start(self):
        links = self.links
        self.incoming = links.swap(lambda peer: list(self.parts(peer)))
        for source, target in self.parts(links.blk):
            self.kept.append(links.local(source, target))

    def arrived(self):
        for copy in self.kept:
            copy.wait()
        for copy in self.incoming:
            copy.arrived()


def write_positions(links, span_order, toks, cosine, sine, query_pos, key_pos):
    half_len = toks * links.n_uly // 2

    def first(blk, uly):
        chunk = span_order[2 * blk + lax.div(uly, links.n_uly // 2)]
        return chunk * half_len + lax.rem(uly, links.n_uly // 2) * toks

    lane = lax.broadcasted_iota(jnp.int32, (toks, HEAD_SIZE), 1)
    row = lax.broadcasted_iota(jnp.int32, (toks, HEAD_SIZE), 0)
    upper = lane >= HEAD_SIZE // 2
    step = jnp.where(upper, lane - HEAD_SIZE // 2, lane).astype(jnp.float32)
    inverse = jnp.exp(step * (-2.0 * math.log(ROPE_BASE) / HEAD_SIZE))
    for blk in range(links.n_blk):
        angles = (first(blk, links.uly) + row).astype(jnp.float32) * inverse
        at = slice(blk * toks, (blk + 1) * toks)
        cosine[at, :] = jnp.cos(angles)
        turn = jnp.sin(angles)
        sine[at, :] = jnp.where(upper, turn, -turn)
    lane = lax.broadcasted_iota(jnp.int32, query_pos.shape, 1)
    place = jnp.zeros(query_pos.shape, jnp.int32)
    for start in range(0, query_pos.shape[1], toks):
        blk = start // toks % links.n_blk
        here = jnp.logical_and(lane >= start, lane < start + toks)
        place = jnp.where(here, first(blk, links.uly) + lane - start, place)
    query_pos[...] = place
    row = lax.broadcasted_iota(jnp.int32, (toks, 1), 0)
    for uly in range(links.n_uly):
        for blk in range(links.n_blk):
            start = (uly * links.n_blk + blk) * toks
            key_pos[start : start + toks, :] = row + first(blk, jnp.int32(uly))


def write_gains(links, all_gains, size, targets):
    per_row = 128 // size
    for which, target in enumerate(targets):
        for place in range(target.shape[1] // 128):
            pieces = []
            for part in range(per_row):
                device = place * per_row + part
                plane, uly = device // links.n_uly, device % links.n_uly
                gains = all_gains[plane // links.n_blk, plane % links.n_blk, uly]
                pieces.append(gains.astype(jnp.float32)[which : which + 1, :size])
            target[:, place * 128 : (place + 1) * 128] = jnp.concatenate(pieces, axis=1)


ROWS = 32


def each_block(count, body):
    def step(index, carry):
        body(pl.ds(pl.multiple_of(index * ROWS, ROWS), ROWS))
        return carry

    lax.fori_loop(0, count // ROWS, step, 0)


class LineScatter:
    def __init__(self, links, parts, rightward, leftward):
        self.links, self.parts = links, parts
        self.slots = {1: rightward, -1: leftward}
        self.tokens = parts.shape[1]
        self.number = links.used
        self.last = links.n_blk - 1
        links.used += 2 * self.last

    def target(self, step, way):
        return self.last - step if way == 1 else step

    def slot(self, step, way):
        target = self.target(step, way)
        return self.slots[way].at[target - 1 if way == 1 else target]

    def place(self, way):
        return self.links.blk if way == 1 else self.last - self.links.blk

    def copy(self, step, way, source=None):
        links, slot = self.links, self.slot(step, way)
        number = self.number + 2 * step + (1 if way == 1 else 0)
        return pltpu.make_async_remote_copy(
            src_ref=slot if source is None else source,
            dst_ref=slot,
            send_sem=links.send.at[number],
            recv_sem=links.recv.at[number],
            device_id=(links.dp, links.blk + way, links.uly),
            device_id_type=MESH,
        )

    def start(self):
        for step in range(self.last):
            for way in (1, -1):

                @pl.when(self.place(way) == 0)
                def _(step=step, way=way):
                    self.copy(step, way, self.parts.at[self.target(step, way)]).start()

    def tick(self, tick):
        for way in (1, -1):

            @pl.when(jnp.logical_and(self.place(way) >= 1, self.place(way) <= tick))
            def _(way=way):
                step = tick - self.place(way)
                self.copy(step, way).wait_recv()
                slot, target = self.slot(step, way), self.target(step, way)

                def body(rows):
                    slot[rows, :] = slot[rows, :] + self.parts[target, rows, :]

                each_block(self.tokens, body)
                self.copy(step, way).start()

    def finish(self, total):
        blk, last = self.links.blk, self.last

        def start(rows):
            total[rows, :] = self.parts[blk, rows, :].astype(jnp.float32)

        each_block(self.tokens, start)
        for way in (1, -1):

            @pl.when(self.place(way) >= 1)
            def _(way=way):
                step = last - self.place(way)
                self.copy(step, way).wait_recv()
                slot = self.slot(step, way)

                def body(rows):
                    total[rows, :] = total[rows, :] + slot[rows, :].astype(jnp.float32)

                each_block(self.tokens, body)

    def sent(self):
        for step in range(self.last):
            for way in (1, -1):
                beyond = self.place(way) + step < self.last
                pl.when(beyond)(lambda step=step, way=way: self.copy(step, way).wait_send())


def halved_sums(links, parts, rightward, leftward):
    return [
        LineScatter(links, parts.at[:, rows], rightward.at[:, rows], leftward.at[:, rows])
        for rows in halves(parts.shape[1])
    ]


class OutputHalf:
    def __init__(self, links, which, parts, middle, rightward, leftward, total):
        rows = halves(middle.shape[0])[which]
        self.middle, self.total = middle.at[rows], total
        self.sum = LineScatter(links, parts.at[:, rows], rightward, leftward)

    def write(self, output):
        self.sum.finish(self.total)

        def body(rows):
            output[rows, :] = (self.middle[rows, :] + self.total[rows, :]).astype(jnp.bfloat16)

        each_block(self.middle.shape[0], body)


def output_scratch(n_blk, tokens, width):
    return line_scratch(n_blk, tokens // 2, width) + [
        pltpu.VMEM((tokens // 2, width), jnp.float32)
    ]


def line_scratch(n_blk, tokens, width):
    return [pltpu.VMEM((n_blk - 1, tokens, width), jnp.bfloat16)] * 2


class PlaneScatter:
    def __init__(self, links, parts, from_core, from_x, from_y, last_x, last_y):
        self.links, self.parts = links, parts
        self.own_core_only = from_core is None
        self.from_core, self.from_x, self.from_y = from_core, from_x, from_y
        self.last_x, self.last_y = last_x, last_y
        self.core = lax.rem(links.uly, 2)
        self.row = lax.div(links.uly, 2)
        self.depth = parts.shape[3]
        self.core_copies = {}

    def chunk(self, dp, row, core, half=None):
        if self.own_core_only:
            part = self.parts.at[dp, row]
        else:
            part = self.parts.at[dp, :, row * 2 + core]
        if half is None:
            return part
        depth = self.depth // 2
        return part.at[:, pl.ds(half * depth, depth)]

    def add(self, target, source):
        blocks, depth, _ = target.shape
        rows = 32 if depth % 32 == 0 else 16

        def body(index, carry):
            block = lax.div(index, depth // rows)
            at = pl.ds(pl.multiple_of(lax.rem(index, depth // rows) * rows, rows), rows)
            target[block, at, :] = target[block, at, :] + source[block, at, :]
            return carry

        lax.fori_loop(0, blocks * (depth // rows), body, 0)

    def between_cores(self, which):
        links = self.links
        dp = links.dp if which == 1 else links.other_dp
        self.core_copies[which] = [
            links.to(
                self.chunk(dp, row, 1 - self.core), self.from_core.at[which, row], links.core_way
            )
            for row in range(2)
        ]

    def core_sums(self, which):
        links = self.links
        dp = links.dp if which == 1 else links.other_dp
        for row in range(2):
            self.core_copies[which][row].arrived()
            self.add(self.chunk(dp, row, self.core), self.from_core.at[which, row])

    def across_chips(self):
        links = self.links
        if not self.own_core_only:
            self.core_sums(0)
        self.x_copies = [
            links.to(
                self.chunk(links.other_dp, row, self.core, 0), self.from_x.at[row], links.x_way
            )
            for row in range(2)
        ]
        if not self.own_core_only:
            self.core_sums(1)
        self.y_copies = [
            links.to(
                self.chunk(group, 1 - self.row, self.core, 1),
                self.from_y.at[group],
                links.y_way,
            )
            for group in range(links.n_dp)
        ]

    def second_way(self):
        links = self.links
        for row in range(2):
            self.x_copies[row].arrived()
            self.add(self.chunk(links.dp, row, self.core, 0), self.from_x.at[row])
        self.y_last = links.to(
            self.chunk(links.dp, 1 - self.row, self.core, 0), self.last_y, links.y_way
        )
        for group in range(links.n_dp):
            self.y_copies[group].arrived()
            self.add(self.chunk(group, self.row, self.core, 1), self.from_y.at[group])
        self.x_last = links.to(
            self.chunk(links.other_dp, self.row, self.core, 1), self.last_x, links.x_way
        )

    def result(self, write):
        links = self.links
        for half, copy, source in ((0, self.y_last, self.last_y), (1, self.x_last, self.last_x)):
            copy.arrived()
            own = self.chunk(links.dp, self.row, self.core, half)
            blocks, depth, _ = source.shape
            rows = 32 if depth % 32 == 0 else 16

            def body(index, carry, own=own, source=source, half=half, depth=depth, rows=rows):
                block = lax.div(index, depth // rows)
                start = pl.multiple_of(lax.rem(index, depth // rows) * rows, rows)
                at = pl.ds(start, rows)
                value = own[block, at, :].astype(jnp.float32)
                value = value + source[block, at, :].astype(jnp.float32)
                write(block, pl.ds(pl.multiple_of(start + half * depth, rows), rows), value)
                return carry

            lax.fori_loop(0, blocks * (depth // rows), body, 0)


def plane_shapes(n_dp, blocks, n_uly, depth, width):
    return [
        (n_dp, blocks, n_uly, depth, width),
        (n_dp, 2, blocks, depth, width),
        (2, blocks, depth // 2, width),
        (n_dp, blocks, depth // 2, width),
        (blocks, depth // 2, width),
        (blocks, depth // 2, width),
    ]


def plane_scratch(*sizes):
    return [pltpu.VMEM(shape, jnp.bfloat16) for shape in plane_shapes(*sizes)]


def weight_grad(rows, right, parts, dp):
    _, blocks, n_uly, depth, width = parts.shape
    columns = 512

    def body(index, carry):
        at = pl.ds(pl.multiple_of(index * columns, columns), columns)
        part = jnp.dot(rows[...], right[:, at], preferred_element_type=jnp.float32)
        parts[dp, :, :, :, at] = part.astype(jnp.bfloat16).reshape(blocks, n_uly, depth, columns)
        return carry

    lax.fori_loop(0, width // columns, body, 0)


def rows_turned(left, parts, dp):
    count = parts.shape[1] * parts.shape[2] * parts.shape[3]
    return left[:, pl.ds(pl.multiple_of(dp * count, 128), count)].T


def turned(rows, cosine, sine):
    return rows * cosine + pltpu.roll(rows, HEAD_SIZE // 2, axis=1) * sine


def transposed_product(left, right):
    return lax.dot_general(
        left, right, (((0,), (0,)), ((), ())), preferred_element_type=jnp.float32
    )


def product_right(left, right):
    return lax.dot_general(
        left, right, (((1,), (1,)), ((), ())), preferred_element_type=jnp.float32
    )


SCORE_SCALE = 1.0 / math.sqrt(HEAD_SIZE)


def forward_kernel(
    toks,
    gain_rows,
    span_order,
    hidden,
    wq,
    wk,
    wv,
    wo,
    wg,
    wu,
    wd,
    cotangent,
    gains,
    q_gain,
    k_gain,
    all_qkv,
    all_wo,
    all_wg,
    all_wu,
    all_wd,
    all_cot,
    attn_gain,
    mlp_gain,
    cosine,
    sine,
    query_pos,
    key_pos,
    heads,
    normed,
    qkv,
    queries,
    key_values,
    lse,
    middle,
    all_normed,
    all_gains,
    all_hidden,
    near_qkv,
    near_wo,
    parts,
    rightward,
    leftward,
    own_normed,
    send,
    recv,
    here,
):
    links = Links(send, recv, here)
    links.greet(links.peers() + [links.x_way, links.y_way, links.core_way])
    tokens, width = hidden.shape
    spans = halves(tokens)
    q_width, k_width = wq.shape[1] // links.n_blk, wk.shape[1] // links.n_blk
    chunk = all_qkv.at[links.dp, :, links.uly]
    swap = ColumnSwap(
        links, [(wq, chunk, 0), (wk, chunk, q_width), (wv, chunk, q_width + k_width)]
    )
    plane_wo = PlaneGather(links, rows_of(all_wo, False))
    plane_wd = PlaneGather(links, rows_of(all_wd, False))
    plane_qkv = PlaneGather(links, rows_of(all_qkv, True))
    plane_gain = PlaneGather(links, rows_of(all_gains, True))
    swap.start()
    my_gains = all_gains.at[links.dp, links.blk, links.uly]
    gain_swap = [links.to(gains, my_gains, device) for device in links.peers()]
    plane_wo.start(wo)
    line = HalvedLine(links, hidden, all_hidden)
    line.send(0)
    keep = [
        links.local(gains, my_gains),
        links.local(hidden, all_hidden.at[links.blk]),
        links.local(wo, all_wo.at[links.dp, links.uly]),
        links.local(wd, all_wd.at[links.dp, links.uly]),
        links.local(cotangent, all_cot.at[links.blk]),
    ]
    write_positions(links, span_order, toks, cosine, sine, query_pos, key_pos)
    swap.arrived()
    plane_qkv.start()
    keep[0].wait()
    for copy in gain_swap:
        copy.arrived()
    plane_gain.start()
    plane_wd.start(wd)
    plane_wo.hand_on()
    line.advance(1)
    plane_qkv.hand_on()
    plane_gain.hand_on()
    plane_wo.last()
    for step in range(2, links.n_blk - 1):
        line.advance(step)
    pairs = [(wg, all_wg), (wu, all_wu)]
    planes = [PlaneGather(links, rows_of(whole, True)) for _, whole in pairs]
    swaps = [
        ColumnSwap(links, [(weight, whole.at[links.dp, :, links.uly], 0)])
        for weight, whole in pairs
    ]
    for swap in swaps:
        swap.start()
    cot_lines = HalvedLine(links, cotangent, all_cot).lines
    for half in cot_lines:
        half.send(0)
    plane_qkv.last()
    plane_gain.last()
    plane_gain.arrived()
    write_gains(links, all_gains, gain_rows, (attn_gain, mlp_gain))
    for copy in keep[1:]:
        copy.wait()
    plane_wo.arrived()
    plane_qkv.arrived()
    near = [links.local(all_qkv, near_qkv), links.local(all_wo, near_wo)]
    seqs, kv_heads, q_rows, _ = queries.shape
    q_len = key_values.shape[4]
    group = q_rows // q_len
    q_end = kv_heads * group * HEAD_SIZE
    k_end = q_end + kv_heads * HEAD_SIZE

    def norm(seq):
        def body(rows):
            for blk in range(links.n_blk):
                at = pl.ds(pl.multiple_of(seq * toks + rows.start, ROWS), ROWS)
                to = pl.ds(pl.multiple_of(seq * q_len + blk * toks + rows.start, ROWS), ROWS)
                source = all_hidden[blk, at, :].astype(jnp.float32)
                normed[to, :] = (source * rms_scale(source) * attn_gain[...]).astype(
                    jnp.bfloat16
                )

        each_block(toks, body)

    def rotated(seq, column, gain):
        pre = qkv[seq * q_len : (seq + 1) * q_len, column : column + HEAD_SIZE]
        gain = gain[...].astype(jnp.float32)
        return turned(pre * rms_scale(pre) * gain, cosine[...], sine[...]).astype(jnp.bfloat16)

    def project(seq):
        rows = slice(seq * q_len, (seq + 1) * q_len)
        for column in range(0, qkv.shape[1], 512):
            weight = near_qkv[:, :, :, :, column : column + 512].reshape(width, 512)
            qkv[rows, column : column + 512] = jnp.dot(
                normed[rows, :], weight, preferred_element_type=jnp.float32
            )
        for head in range(kv_heads):
            column = head * HEAD_SIZE
            key_values[links.uly, 0, seq, head] = rotated(seq, q_end + column, k_gain)
            key_values[links.uly, 1, seq, head] = qkv[
                rows, k_end + column : k_end + column + HEAD_SIZE
            ].astype(jnp.bfloat16)
        mine = key_values.at[links.uly, :, seq]
        copies = [links.to(mine, mine, way) for way in (links.core_way, links.y_way)]
        for head in range(kv_heads * group):
            at = pl.ds((head % group) * q_len, q_len)
            queries[seq, head // group, at, :] = rotated(seq, head * HEAD_SIZE, q_gain)
        return copies

    def hand_keys(seq, copies):
        copies[1].arrived()
        theirs = key_values.at[links.across, :, seq]
        copies.append(links.to(theirs, theirs, links.core_way))

    def attend(seq, head):
        def over_keys(piece, carry):
            total, mixed = carry
            rows = pl.ds(pl.multiple_of(piece * q_len, q_len), q_len)
            scores = product_right(key_values[piece, 0, seq, head], queries[seq, head])
            weights = jnp.where(
                query_pos[...] >= key_pos[rows, :], jnp.exp(scores * SCORE_SCALE), 0.0
            )
            total = total + jnp.sum(weights, axis=0, keepdims=True)
            mixed = mixed + transposed_product(
                key_values[piece, 1, seq, head], weights.astype(jnp.bfloat16)
            )
            return total, mixed

        total, mixed = lax.fori_loop(
            0,
            links.n_uly,
            over_keys,
            (
                jnp.zeros((1, q_rows), jnp.float32),
                jnp.zeros((HEAD_SIZE, q_rows), jnp.float32),
            ),
        )
        lse[seq * kv_heads + head] = jnp.log(total)
        attended = (mixed / total).T.astype(jnp.bfloat16)
        for member in range(group):
            column = (head * group + member) * HEAD_SIZE
            for blk in range(links.n_blk):
                row = (blk * seqs + seq) * toks
                start = member * q_len + blk * toks
                heads[row : row + toks, column : column + HEAD_SIZE] = attended[
                    start : start + toks, :
                ]

    sums = halved_sums(links, parts, rightward, leftward)
    def out_weight():
        return near_wo[...].reshape(heads.shape[1], width)

    def out_parts(seq):
        mixed = jnp.concatenate(
            [
                heads[(blk * seqs + seq) * toks : (blk * seqs + seq + 1) * toks, :]
                for blk in range(links.n_blk)
            ],
            axis=0,
        )
        for column in range(0, width, 512):
            parts[:, spans[seq], column : column + 512] = (
                jnp.dot(
                    mixed,
                    out_weight()[:, column : column + 512],
                    preferred_element_type=jnp.float32,
                )
                .astype(jnp.bfloat16)
                .reshape(links.n_blk, toks, 512)
            )
        sums[seq].start()

    key_copies = []
    for seq in range(seqs):
        line.lines[seq].arrived()
        norm(seq)
        if seq == 0:
            for copy in near:
                copy.wait()
        key_copies.append(project(seq))
    plane_wd.hand_on()
    hand_keys(0, key_copies[0])
    for copy in (key_copies[0][0], key_copies[0][2]):
        copy.arrived()
    attend(0, 0)
    hand_keys(1, key_copies[1])
    for head in range(1, kv_heads):
        attend(0, head)
    out_parts(0)
    swaps[0].arrived()
    planes[0].start()
    for copy in (key_copies[1][0], key_copies[1][2]):
        copy.arrived()
    attend(1, 0)
    sums[0].tick(1)
    for head in range(1, kv_heads):
        attend(1, head)
    out_parts(1)
    swaps[1].arrived()
    planes[1].start()
    later = range(2, links.n_blk - 1)
    for tick in later:
        sums[0].tick(tick)
    for half in cot_lines:
        half.arrived()
        half.send(1)
    plane_wd.last()
    planes[0].hand_on()
    lines = []

    def settle(half, rows_of_half):
        half.finish(middle.at[rows_of_half])

        def body(rows):
            at = pl.ds(pl.multiple_of(rows_of_half.start + rows.start, ROWS), ROWS)
            total = middle[at, :] + all_hidden[links.blk, at, :].astype(jnp.float32)
            middle[at, :] = total
            own_normed[at, :] = (total * rms_scale(total) * mlp_gain[...]).astype(jnp.bfloat16)

        each_block(tokens // 2, body)
        next_line = LineGather(links, own_normed.at[rows_of_half], all_normed.at[:, rows_of_half])
        next_line.send(0)
        lines.append(next_line)

    settle(sums[0], spans[0])
    sums[1].tick(1)
    for tick in later:
        sums[1].tick(tick)
    settle(sums[1], spans[1])
    for step in range(2, links.n_blk - 1):
        for half in cot_lines:
            half.arrived()
            half.send(step)
    last_local = links.local(own_normed, all_normed.at[links.blk])
    planes[1].hand_on()
    planes[0].last()
    for step in range(1, links.n_blk - 1):
        for half in lines:
            half.arrived()
            half.send(step)
    planes[1].last()
    for half in lines + cot_lines:
        half.arrived()
    for plane in [plane_wd] + planes:
        plane.arrived()
    last_local.wait()
    for half in sums:
        half.sent()
    links.finish()


SMEM = pl.BlockSpec(memory_space=pltpu.SMEM)


def forward(
    span_order,
    hidden,
    wq,
    wk,
    wv,
    wo,
    wg,
    wu,
    wd,
    cotangent,
    gains,
    q_gain,
    k_gain,
    seqs,
    gain_rows,
):
    n_dp, n_blk, n_uly = (lax.axis_size(a) for a in EVERY)
    tokens, width = hidden.shape
    toks = tokens // seqs
    rows, q_len = n_blk * tokens, n_blk * toks
    group = QUERY_HEADS // KEY_VALUE_HEADS
    kv_heads = KEY_VALUE_HEADS // n_blk
    q_rows, keys = group * q_len, n_uly * q_len
    columns = (wq.shape[1] + wk.shape[1] + wv.shape[1]) // n_blk
    f32, low, i32 = jnp.float32, jnp.bfloat16, jnp.int32
    ff = wg.shape[1] // n_blk
    far = [
        (n_dp, n_blk, n_uly, wq.shape[0], columns),
        (n_dp, n_uly) + wo.shape,
        (n_dp, n_blk, n_uly, wg.shape[0], ff),
        (n_dp, n_blk, n_uly, wu.shape[0], ff),
        (n_dp, n_uly) + wd.shape,
        (n_blk, tokens, width),
    ]
    near = [
        ((1, width), f32),
        ((1, width), f32),
        ((q_len, HEAD_SIZE), f32),
        ((q_len, HEAD_SIZE), f32),
        ((1, q_rows), i32),
        ((keys, 1), i32),
        ((rows, kv_heads * group * HEAD_SIZE), low),
        ((rows, width), low),
        ((rows, columns), f32),
        ((seqs, kv_heads, q_rows, HEAD_SIZE), low),
        ((n_uly, 2, seqs, kv_heads, q_len, HEAD_SIZE), low),
        ((seqs * kv_heads, 1, q_rows), f32),
        ((tokens, width), f32),
        ((n_blk, tokens, width), low),
    ]
    scratch = [
        ((n_dp, n_blk, n_uly) + gains.shape, low),
        ((n_blk, tokens, width), low),
        (far[0], low),
        (far[1], low),
        ((n_blk, tokens, width), low),
        ((n_blk - 1, tokens, width), low),
        ((n_blk - 1, tokens, width), low),
        ((tokens, width), low),
    ]
    return pl.pallas_call(
        functools.partial(forward_kernel, toks, gain_rows),
        out_shape=[jax.ShapeDtypeStruct(shape, low) for shape in far]
        + [jax.ShapeDtypeStruct(shape, kind) for shape, kind in near],
        in_specs=[SMEM] + [HBM] * 10 + [VMEM] * 2,
        out_specs=[HBM] * len(far) + [VMEM] * len(near),
        scratch_shapes=[pltpu.VMEM(shape, kind) for shape, kind in scratch]
        + semaphores(160, 32),
        compiler_params=kernel_params(0),
    )(span_order, hidden, wq, wk, wv, wo, wg, wu, wd, cotangent, gains, q_gain, k_gain)


def back_rows(grad_normed, source, gain):
    unit = source * rms_scale(source)
    scaled = grad_normed * gain
    return rms_scale(source) * (
        scaled - unit * jnp.mean(scaled * unit, axis=-1, keepdims=True)
    )


def back_kernel(
    grad_parts,
    out_parts,
    middle,
    cotangent,
    gain,
    all_normed,
    grad_gate_pre,
    grad_up_pre,
    activated,
    all_cot,
    output,
    grad_middle,
    all_low,
    grad_gate,
    grad_up,
    part_down,
    rightward,
    leftward,
    out_right,
    out_left,
    out_total,
    low,
    turned_low,
    gate_1,
    gate_2,
    gate_3,
    gate_4,
    gate_5,
    gate_6,
    up_1,
    up_2,
    up_3,
    up_4,
    up_5,
    up_6,
    down_1,
    down_2,
    send,
    recv,
    here,
):
    links = Links(send, recv, here)
    links.greet(links.peers() + [links.x_way, links.y_way, links.core_way])
    sums = halved_sums(links, grad_parts, rightward, leftward)
    for half in sums:
        half.start()
    out = OutputHalf(links, 0, out_parts, middle, out_right, out_left, out_total)
    gate = PlaneScatter(links, gate_1, gate_2, gate_3, gate_4, gate_5, gate_6)
    up = PlaneScatter(links, up_1, up_2, up_3, up_4, up_5, up_6)
    down = PlaneScatter(links, down_1, down_2, None, None, None, None)
    tokens = middle.shape[0]
    spans, lines, keep = halves(tokens), [], []

    def compute(plane, which, rows, right):
        dp = links.dp if which == 1 else links.other_dp
        weight_grad(rows, right, plane.parts, dp)
        plane.between_cores(which)

    def turn(which):
        dp = links.dp if which == 1 else links.other_dp
        turned_low[which] = rows_turned(all_normed, gate_1, dp)

    def compute_down(which):
        dp = links.dp if which == 1 else links.other_dp
        compute(down, which, rows_turned(activated, down_1, dp), all_cot)

    def settle(half, rows_of_half):
        half.finish(grad_middle.at[rows_of_half])

        def body(rows):
            at = pl.ds(pl.multiple_of(rows_of_half.start + rows.start, ROWS), ROWS)
            back = back_rows(grad_middle[at, :], middle[at, :], gain[...])
            grad = cotangent[at, :].astype(jnp.float32) + back
            grad_middle[at, :] = grad
            low[at, :] = grad.astype(jnp.bfloat16)

        each_block(tokens // 2, body)
        line = LineGather(links, low.at[rows_of_half], all_low.at[:, rows_of_half])
        line.send(0)
        lines.append(line)

    later = range(2, links.n_blk - 1)
    turn(0)
    compute(gate, 0, turned_low.at[0], grad_gate_pre)
    sums[0].tick(1)
    turn(1)
    compute(gate, 1, turned_low.at[1], grad_gate_pre)
    for tick in later:
        sums[0].tick(tick)
    gate.across_chips()
    settle(sums[0], spans[0])
    compute(up, 0, turned_low.at[0], grad_up_pre)
    sums[1].tick(1)
    compute(up, 1, turned_low.at[1], grad_up_pre)
    for tick in later:
        sums[1].tick(tick)
    up.across_chips()
    settle(sums[1], spans[1])
    out.sum.start()
    keep.append(links.local(low, all_low.at[links.blk]))
    compute_down(0)
    for step in range(1, links.n_blk - 1):
        for line in lines:
            line.arrived()
            line.send(step)
        if step == 1:
            gate.second_way()
            compute_down(1)
    out.sum.tick(1)
    up.second_way()
    for which in (0, 1):
        down.core_sums(which)
    for dp in range(links.n_dp):
        for row in range(2):
            keep.append(links.local(down.chunk(dp, row, down.core), part_down.at[dp, row]))
    for tick in later:
        out.sum.tick(tick)
    for line in lines:
        line.arrived()

    def into(target):
        def write(block, rows, values):
            target[block, rows, :] = values.astype(target.dtype)

        return write

    gate.result(into(grad_gate))
    up.result(into(grad_up))
    out.write(output)
    out.sum.sent()
    for copy in keep:
        copy.wait()
    for half in sums:
        half.sent()
    links.finish()


def exchange_back(
    grad_parts,
    out_parts,
    middle,
    cotangent,
    gain,
    all_normed,
    grad_gate_pre,
    grad_up_pre,
    activated,
    all_cot,
):
    n_dp, n_blk, n_uly = (lax.axis_size(a) for a in EVERY)
    _, tokens, width = grad_parts.shape
    ff = grad_gate_pre.shape[1]
    depth = width // (n_dp * n_blk * n_uly)
    down_depth = ff // (n_dp * n_uly)
    return pl.pallas_call(
        back_kernel,
        out_shape=[
            jax.ShapeDtypeStruct((tokens // 2, width), jnp.bfloat16),
            jax.ShapeDtypeStruct((tokens, width), jnp.float32),
            jax.ShapeDtypeStruct((n_blk, tokens, width), jnp.bfloat16),
            jax.ShapeDtypeStruct((n_blk, depth, ff), jnp.bfloat16),
            jax.ShapeDtypeStruct((n_blk, depth, ff), jnp.bfloat16),
            jax.ShapeDtypeStruct((n_dp, 2, 1, down_depth, width), jnp.bfloat16),
        ],
        in_specs=[VMEM] * 10,
        out_specs=[VMEM, VMEM, HBM, VMEM, VMEM, HBM],
        scratch_shapes=line_scratch(n_blk, tokens, width)
        + output_scratch(n_blk, tokens, width)
        + [
            pltpu.VMEM((tokens, width), jnp.bfloat16),
            pltpu.VMEM((n_dp, width // n_dp, n_blk * tokens), jnp.bfloat16),
        ]
        + plane_scratch(n_dp, n_blk, n_uly, depth, ff) * 2
        + plane_scratch(n_dp, 1, n_uly, down_depth, width)[:2]
        + semaphores(72),
        compiler_params=kernel_params(3),
    )(
        grad_parts,
        out_parts,
        middle,
        cotangent,
        gain,
        all_normed,
        grad_gate_pre,
        grad_up_pre,
        activated,
        all_cot,
    )


def backward_kernel(
    all_low,
    wo,
    queries,
    key_values,
    lse,
    qkv,
    q_gain,
    k_gain,
    cosine,
    sine,
    query_pos,
    key_pos,
    w_qkv,
    hidden,
    grad_middle,
    gain,
    normed,
    heads,
    out_parts,
    middle,
    grad_gate,
    grad_up,
    part_down,
    grad_hidden,
    grad_wo,
    grad_down,
    small_sum,
    output,
    gate_rows,
    up_rows,
    grad_w_qkv,
    grad_qkv,
    gain_terms,
    grad_heads,
    grad_rows,
    grad_kv,
    from_core,
    from_across,
    grad_parts,
    rightward,
    leftward,
    summed,
    small_in,
    small_total,
    out_right,
    out_left,
    out_total,
    relay,
    down_1,
    down_3,
    down_4,
    down_5,
    down_6,
    turned_normed,
    q_1,
    q_2,
    q_3,
    q_4,
    q_5,
    q_6,
    kv_1,
    kv_2,
    kv_3,
    kv_4,
    kv_5,
    kv_6,
    wo_1,
    wo_2,
    wo_3,
    wo_4,
    wo_5,
    wo_6,
    send,
    recv,
    here,
):
    links = Links(send, recv, here)
    links.greet(links.peers() + [links.x_way, links.y_way, links.core_way])
    tokens = hidden.shape[0]
    spans = halves(tokens)
    output_half = OutputHalf(links, 1, out_parts, middle, out_right, out_left, out_total)
    output_half.sum.start()
    down = PlaneScatter(links, down_1, None, down_3, down_4, down_5, down_6)
    fetch = links.local(part_down, down_1)
    swapped, keep = [], []
    swaps = []
    for number, (source, target) in enumerate(((grad_gate, gate_rows), (grad_up, up_rows))):
        swap = LineSwap(
            links,
            lambda blk, source=source: [source.at[blk]],
            lambda origin, target=target: [target.at[origin]],
            relay.at[number],
        )
        swap.hand_on(0)
        swaps.append(swap)
        keep.append(links.local(source.at[links.blk], target.at[links.blk]))
    fetch.wait()
    down.across_chips()
    sums = halved_sums(links, grad_parts, rightward, leftward)
    q_sums = PlaneScatter(links, q_1, q_2, q_3, q_4, q_5, q_6)
    kv_sums = PlaneScatter(links, kv_1, kv_2, kv_3, kv_4, kv_5, kv_6)
    wo_sums = PlaneScatter(links, wo_1, wo_2, wo_3, wo_4, wo_5, wo_6)
    seqs, kv_heads, q_rows, _ = queries.shape
    q_len = key_values.shape[4]
    group = q_rows // q_len
    toks = q_len // links.n_blk
    q_end = kv_heads * group * HEAD_SIZE
    k_end = q_end + kv_heads * HEAD_SIZE
    gain_terms[...] = jnp.zeros_like(gain_terms)
    later = range(2, links.n_blk - 1)

    def heads_back(seq):
        low = jnp.concatenate(
            [
                all_low[(blk * seqs + seq) * toks : (blk * seqs + seq + 1) * toks, :]
                for blk in range(links.n_blk)
            ],
            axis=0,
        )
        grad_heads[...] = product_right(low, wo[...])
        for head in range(kv_heads * group):
            to = pl.ds((head % group) * q_len, q_len)
            grad_rows[seq, head // group, to, :] = grad_heads[
                :, head * HEAD_SIZE : (head + 1) * HEAD_SIZE
            ].astype(jnp.bfloat16)

    def back_norm(upstream, seq, column, gain, which):
        rows = slice(seq * q_len, (seq + 1) * q_len)
        pre = qkv[rows, column : column + HEAD_SIZE]
        upstream = turned(upstream, cosine[...], -sine[...])
        gain_terms[which : which + 1, :] += jnp.sum(
            upstream * pre * rms_scale(pre), axis=0, keepdims=True
        )
        grad_qkv[rows, column : column + HEAD_SIZE] = back_rows(
            upstream, pre, gain[...].astype(jnp.float32)
        ).astype(jnp.bfloat16)

    def deltas(seq, head):
        sums_of = []
        for member in range(group):
            column = (head * group + member) * HEAD_SIZE
            attended = jnp.concatenate(
                [
                    heads[row : row + toks, column : column + HEAD_SIZE]
                    for row in ((blk * seqs + seq) * toks for blk in range(links.n_blk))
                ],
                axis=0,
            )
            upstream = grad_rows[seq, head, member * q_len : (member + 1) * q_len, :]
            sums_of.append(attended.astype(jnp.float32) * upstream.astype(jnp.float32))
        terms = jnp.concatenate(sums_of, axis=0)
        high = terms.astype(jnp.bfloat16)
        rest = (terms - high.astype(jnp.float32)).astype(jnp.bfloat16)
        ones = jnp.ones((16, HEAD_SIZE), jnp.bfloat16)
        return (product_right(ones, high) + product_right(ones, rest))[:1, :]

    def back(seq, head):
        delta = deltas(seq, head)

        def over_keys(piece, grad_query):
            rows = pl.ds(pl.multiple_of(piece * q_len, q_len), q_len)
            scores = product_right(key_values[piece, 0, seq, head], queries[seq, head])
            prob = jnp.where(
                query_pos[...] >= key_pos[rows, :],
                jnp.exp(scores * SCORE_SCALE - lse[seq * kv_heads + head]),
                0.0,
            )
            grad_prob = product_right(key_values[piece, 1, seq, head], grad_rows[seq, head])
            grad_score = (prob * (grad_prob - delta)).astype(jnp.bfloat16)
            grad_kv[seq, piece, 0, head] = (
                SCORE_SCALE
                * jnp.dot(grad_score, queries[seq, head], preferred_element_type=jnp.float32)
            ).astype(jnp.bfloat16)
            grad_kv[seq, piece, 1, head] = jnp.dot(
                prob.astype(jnp.bfloat16),
                grad_rows[seq, head],
                preferred_element_type=jnp.float32,
            ).astype(jnp.bfloat16)
            return grad_query + transposed_product(key_values[piece, 0, seq, head], grad_score)

        grad_query = lax.fori_loop(
            0, links.n_uly, over_keys, jnp.zeros((HEAD_SIZE, q_rows), jnp.float32)
        )
        turned_back = (grad_query * SCORE_SCALE).T
        for member in range(group):
            column = (head * group + member) * HEAD_SIZE
            back_norm(
                turned_back[member * q_len : (member + 1) * q_len, :], seq, column, q_gain, 0
            )

    core, line = lax.rem(links.uly, 2), lax.div(links.uly, 2)

    def add(target, source):
        for kind in range(2):
            for head in range(kv_heads):
                target[kind, head] = target[kind, head] + source[kind, head]

    def core_sums(seq):
        return [
            links.to(
                grad_kv.at[seq, row * 2 + 1 - core], from_core.at[seq, row], links.core_way
            )
            for row in range(2)
        ]

    def across_sums(seq, copies):
        for row in range(2):
            copies[row].arrived()
            add(grad_kv.at[seq, row * 2 + core], from_core.at[seq, row])
        return links.to(
            grad_kv.at[seq, (1 - line) * 2 + core], from_across.at[seq], links.y_way
        )

    def own_keys(seq, copy):
        copy.arrived()
        rows = slice(seq * q_len, (seq + 1) * q_len)
        for head in range(kv_heads):
            term = [
                grad_kv[seq, links.uly, kind, head].astype(jnp.float32)
                + from_across[seq, kind, head].astype(jnp.float32)
                for kind in range(2)
            ]
            back_norm(term[0], seq, q_end + head * HEAD_SIZE, k_gain, 1)
            v_at = k_end + head * HEAD_SIZE
            grad_qkv[rows, v_at : v_at + HEAD_SIZE] = term[1].astype(jnp.bfloat16)

    def normed_parts(seq):
        for column in range(0, w_qkv.shape[0], 512):
            grad_parts[:, spans[seq], column : column + 512] = (
                product_right(
                    grad_qkv[seq * q_len : (seq + 1) * q_len, :],
                    w_qkv[column : column + 512, :],
                )
                .astype(jnp.bfloat16)
                .reshape(links.n_blk, toks, 512)
            )
        sums[seq].start()

    def dp_of(which):
        return links.dp if which == 1 else links.other_dp

    def compute_wo(which):
        dp = dp_of(which)
        weight_grad(rows_turned(heads, wo_1, dp), all_low, wo_1, dp)
        wo_sums.between_cores(which)

    def compute_qkv(plane, which, columns):
        weight_grad(
            turned_normed.at[which], grad_qkv.at[:, columns], plane.parts, dp_of(which)
        )
        plane.between_cores(which)

    q_columns, kv_columns = pl.ds(0, q_end), pl.ds(q_end, grad_qkv.shape[1] - q_end)
    heads_back(0)
    back(0, 0)
    output_half.sum.tick(1)
    for head in range(1, kv_heads):
        back(0, head)
    core_copies = core_sums(0)
    heads_back(1)
    down.second_way()
    for which in range(2):
        turned_normed[which] = rows_turned(normed, q_1, dp_of(which))
    back(1, 0)
    across = across_sums(0, core_copies)
    swaps[0].hand_on(1)
    for tick in later:
        output_half.sum.tick(tick)
    for head in range(1, kv_heads):
        back(1, head)
    core_copies = core_sums(1)
    own_keys(0, across)
    across = across_sums(1, core_copies)
    swaps[1].hand_on(1)
    for step in later:
        swaps[0].hand_on(step)
    normed_parts(0)
    compute_qkv(q_sums, 0, q_columns)
    compute_qkv(q_sums, 1, q_columns)
    own_keys(1, across)
    for step in later:
        swaps[1].hand_on(step)
    small_total[0] = gain_terms[...]
    pending = links.to(small_total.at[0], small_in.at[links.n_blk], links.core_way)
    q_sums.across_chips()
    normed_parts(1)
    sums[0].tick(1)
    compute_qkv(kv_sums, 0, kv_columns)
    compute_qkv(kv_sums, 1, kv_columns)
    for tick in later:
        sums[0].tick(tick)
    pending.arrived()
    small_total[1] = small_total[0] + small_in[links.n_blk]
    pending = links.to(small_total.at[1], small_in.at[links.n_blk + 1], links.x_way)
    kv_sums.across_chips()
    q_sums.second_way()
    compute_wo(0)
    compute_wo(1)
    pending.arrived()
    small_total[2] = small_total[1] + small_in[links.n_blk + 1]
    pending = links.to(small_total.at[2], small_in.at[links.n_blk + 2], links.y_way)
    sums[1].tick(1)
    kv_sums.second_way()
    wo_sums.across_chips()

    def into(target):
        def write(block, rows, values):
            target[block, rows, :] = values.astype(target.dtype)

        return write

    def give_home(plane, columns):
        here, there = summed.at[:, :, columns], grad_w_qkv.at[links.blk, :, columns]
        plane.result(into(here))
        keep.append(links.local(here.at[links.blk], there))
        return links.swap(lambda peer: [(here.at[peer], there)])

    swapped += give_home(q_sums, q_columns)
    for tick in later:
        sums[1].tick(tick)
    pending.arrived()
    small_in[links.blk] = small_total[2] + small_in[links.n_blk + 2]
    mine = small_in.at[links.blk]
    small_copies = [links.to(mine, mine, device) for device in links.peers()]
    swapped += give_home(kv_sums, kv_columns)
    output_half.write(output)

    def settle(seq):
        sums[seq].finish(grad_hidden.at[spans[seq]])

        def body(rows):
            at = pl.ds(pl.multiple_of(spans[seq].start + rows.start, ROWS), ROWS)
            back = back_rows(grad_hidden[at, :], hidden[at, :].astype(jnp.float32), gain[...])
            grad_hidden[at, :] = grad_middle[at, :] + back

        each_block(toks, body)

    settle(0)
    wo_sums.second_way()
    down.result(into(grad_down))
    settle(1)
    wo_sums.result(into(grad_wo))
    for copy in small_copies:
        copy.arrived()
    total = small_in[0]
    for blk in range(1, links.n_blk):
        total = total + small_in[blk]
    small_sum[...] = total
    for copy in swapped:
        copy.arrived()
    for copy in keep:
        copy.wait()
    for swap in swaps:
        swap.arrived()
    for half in sums + swaps:
        half.sent()
    output_half.sum.sent()
    links.finish()


def backward(
    all_low,
    wo,
    queries,
    key_values,
    lse,
    qkv,
    q_gain,
    k_gain,
    cosine,
    sine,
    query_pos,
    key_pos,
    w_qkv,
    hidden,
    grad_middle,
    gain,
    normed,
    heads,
    out_parts,
    middle,
    grad_gate,
    grad_up,
    part_down,
):
    seqs, kv_heads, q_rows, _ = queries.shape
    n_uly, _, _, _, q_len, _ = key_values.shape
    n_blk, tokens, width = out_parts.shape
    n_dp, _, _, down_depth, _ = part_down.shape
    columns = qkv.shape[1]
    depth = width // (n_dp * n_blk * n_uly)
    out_depth = heads.shape[1] // (n_dp * n_uly)
    f32, low = jnp.float32, jnp.bfloat16
    small = (8, HEAD_SIZE)
    outs = [
        ((tokens, width), f32),
        ((1, out_depth, width), f32),
        ((1, down_depth, width), f32),
        (small, f32),
        ((tokens // 2, width), low),
        (grad_gate.shape, low),
        (grad_up.shape, low),
        ((n_blk, depth, columns), low),
    ]
    scratch = [
        (qkv.shape, low),
        (small, f32),
        ((q_len, heads.shape[1]), f32),
        (queries.shape, low),
        ((seqs, n_uly, 2, kv_heads, q_len, HEAD_SIZE), low),
        ((seqs, 2, 2, kv_heads, q_len, HEAD_SIZE), low),
        ((seqs, 2, kv_heads, q_len, HEAD_SIZE), low),
        (out_parts.shape, low),
        ((n_blk - 1, tokens, width), low),
        ((n_blk - 1, tokens, width), low),
        ((n_blk, depth, columns), low),
        ((n_blk + 3,) + small, f32),
        ((3,) + small, f32),
    ]
    down = [part_down.shape] + plane_shapes(n_dp, 1, n_uly, down_depth, width)[2:]
    return pl.pallas_call(
        backward_kernel,
        out_shape=[jax.ShapeDtypeStruct(shape, kind) for shape, kind in outs],
        in_specs=[VMEM] * 20 + [HBM] * 3,
        out_specs=[VMEM] * 5 + [HBM] * 3,
        scratch_shapes=[pltpu.VMEM(shape, kind) for shape, kind in scratch]
        + output_scratch(n_blk, tokens, width)
        + [pltpu.VMEM((2, relay_slots(n_blk), 1) + grad_gate.shape[1:], low)]
        + [pltpu.VMEM(shape, low) for shape in down]
        + [pltpu.VMEM((n_dp, width // n_dp, normed.shape[0]), low)]
        + plane_scratch(n_dp, n_blk, n_uly, depth, heads.shape[1])
        + plane_scratch(n_dp, n_blk, n_uly, depth, columns - heads.shape[1])
        + plane_scratch(n_dp, 1, n_uly, out_depth, width)
        + semaphores(144),
        compiler_params=kernel_params(4),
    )(
        all_low,
        wo,
        queries,
        key_values,
        lse,
        qkv,
        q_gain,
        k_gain,
        cosine,
        sine,
        query_pos,
        key_pos,
        w_qkv,
        hidden,
        grad_middle,
        gain,
        normed,
        heads,
        out_parts,
        middle,
        grad_gate,
        grad_up,
        part_down,
    )


def finish_kernel(
    gate,
    up,
    qkv,
    wo,
    wd,
    hidden,
    out_0,
    out_1,
    w_gate,
    w_up,
    w_query,
    key_weight,
    value_weight,
    attn_gain,
    mlp_gain,
    small,
    f_gate,
    f_up,
    f_q,
    f_k,
    f_v,
    f_wo,
    f_wd,
    f_hidden,
    f_out,
    f_attn,
    f_mlp,
    f_q_gain,
    f_k_gain,
):
    n_blk, depth, _ = gate.shape

    def place(source, offset, target):
        width = target.shape[1] // (n_blk * 2)
        for blk in range(n_blk):
            for group in range(2):
                to = (group * n_blk + blk) * width
                at = offset + group * width
                target[:, to : to + width] = source[blk, :, at : at + width].astype(jnp.float32)

    def gain_back(pairs, gain):
        total = jnp.zeros((depth, 128), jnp.float32)
        for weight, grad in pairs:
            for column in range(0, weight.shape[1], 128):
                at = slice(column, column + 128)
                total = total + weight[:, at].astype(jnp.float32) * grad[:, at]
        column = jnp.sum(total, axis=1, keepdims=True)
        square = (depth, depth)
        same = lax.broadcasted_iota(jnp.int32, square, 0) == lax.broadcasted_iota(
            jnp.int32, square, 1
        )
        return jnp.sum(jnp.where(same, column, 0.0), axis=0, keepdims=True) / gain[
            ...
        ].astype(jnp.float32)

    place(gate, 0, f_gate)
    place(up, 0, f_up)
    q_width = f_q.shape[1] // n_blk
    k_width = f_k.shape[1] // n_blk
    place(qkv, 0, f_q)
    place(qkv, q_width, f_k)
    place(qkv, q_width + k_width, f_v)
    f_q_gain[...] = small[0:1, :]
    f_k_gain[...] = small[1:2, :]
    f_wo[...] = wo[0]
    f_wd[...] = wd[0]
    f_hidden[...] = hidden[...]
    half = out_0.shape[0]
    f_out[:half, :] = out_0[...]
    f_out[half:, :] = out_1[...]
    f_attn[...] = gain_back(((w_query, f_q), (key_weight, f_k), (value_weight, f_v)), attn_gain)
    f_mlp[...] = gain_back(((w_gate, f_gate), (w_up, f_up)), mlp_gain)


def finish(gate, up, qkv, wo, wd, hidden, out_0, out_1, weights, gains, small):
    return pl.pallas_call(
        finish_kernel,
        out_shape=[jax.ShapeDtypeStruct(w.shape, jnp.float32) for w in weights]
        + [
            jax.ShapeDtypeStruct(wo.shape[1:], jnp.float32),
            jax.ShapeDtypeStruct(wd.shape[1:], jnp.float32),
            jax.ShapeDtypeStruct(hidden.shape, jnp.float32),
            jax.ShapeDtypeStruct(hidden.shape, jnp.bfloat16),
        ]
        + [jax.ShapeDtypeStruct(gain.shape, jnp.float32) for gain in gains]
        + [jax.ShapeDtypeStruct((1, small.shape[1]), jnp.float32)] * 2,
        in_specs=[VMEM] * 16,
        out_specs=[VMEM] * 13,
        compiler_params=pltpu.CompilerParams(vmem_limit_bytes=62 * MIB),
    )(gate, up, qkv, wo, wd, hidden, out_0, out_1, *weights, *gains, small)


def product(left, right):
    return jnp.dot(left, right, preferred_element_type=jnp.float32)


def shards(
    hidden,
    span_order,
    attn_gain,
    w_query,
    key_weight,
    value_weight,
    w_out,
    q_gain,
    k_gain,
    mlp_gain,
    w_gate,
    w_up,
    w_down,
    cotangent,
):
    seqs, toks, width = hidden.shape
    n_dp, n_blk, n_uly = (lax.axis_size(a) for a in EVERY)
    rows = n_blk * seqs * toks
    bf16 = jnp.bfloat16
    own_hidden = hidden.reshape(seqs * toks, width)
    own_cotangent = cotangent.reshape(seqs * toks, width)

    gain_q, gain_k = q_gain[None, :], k_gain[None, :]
    gain_rows = attn_gain.shape[0]
    own_gains = jnp.pad(jnp.stack([attn_gain, mlp_gain]), ((0, 30), (0, 128 - gain_rows)))
    (
        w_qkv,
        wo,
        all_wg,
        all_wu,
        all_wd,
        cot,
        g_attn,
        g_mlp,
        cosine,
        sine,
        query_pos,
        key_pos,
        heads_flat,
        normed,
        qkv,
        queries,
        key_values,
        lse,
        middle,
        normed2,
    ) = forward(
        span_order,
        own_hidden,
        w_query,
        key_weight,
        value_weight,
        w_out,
        w_gate,
        w_up,
        w_down,
        own_cotangent,
        own_gains,
        gain_q,
        gain_k,
        seqs,
        gain_rows,
    )
    w_qkv = w_qkv.reshape(width, -1)
    wo = wo.reshape(-1, width)
    wg, wu = all_wg.reshape(width, -1), all_wu.reshape(width, -1)
    wd = all_wd.reshape(-1, width)
    cot = cot.reshape(rows, width)
    normed2 = normed2.reshape(rows, width)
    gate_pre = product(normed2, wg)
    up_pre = product(normed2, wu)
    sigmoid_gate = jax.nn.sigmoid(gate_pre)
    activated = (gate_pre * sigmoid_gate * up_pre).astype(bf16)
    out_parts = product(activated, wd).astype(bf16)
    grad_act = product_right(cot, wd)
    grad_gate_pre = (
        grad_act * up_pre * sigmoid_gate * (1.0 + gate_pre * (1.0 - sigmoid_gate))
    ).astype(bf16)
    grad_up_pre = (grad_act * gate_pre * sigmoid_gate).astype(bf16)
    grad_parts = (product_right(grad_gate_pre, wg) + product_right(grad_up_pre, wu)).astype(bf16)
    blocks = (n_blk, seqs * toks, width)
    out_parts = out_parts.reshape(blocks)
    output_0, grad_middle, middle_low, grad_gate, grad_up, part_down = exchange_back(
        grad_parts.reshape(blocks),
        out_parts,
        middle,
        own_cotangent,
        g_mlp,
        normed2,
        grad_gate_pre,
        grad_up_pre,
        activated,
        cot,
    )
    middle_low = middle_low.reshape(rows, width)
    (
        grad_hidden,
        grad_out,
        grad_down,
        small,
        output_1,
        grad_gate,
        grad_up,
        grad_w_qkv,
    ) = backward(
        middle_low,
        wo,
        queries,
        key_values,
        lse,
        qkv,
        gain_q,
        gain_k,
        cosine,
        sine,
        query_pos,
        key_pos,
        w_qkv,
        own_hidden,
        grad_middle,
        g_attn,
        normed,
        heads_flat,
        out_parts,
        middle,
        grad_gate,
        grad_up,
        part_down,
    )
    (
        grad_gate,
        grad_up,
        grad_query,
        grad_key,
        grad_value,
        grad_out,
        grad_down,
        grad_hidden,
        output,
        grad_attn_gain,
        grad_mlp_gain,
        grad_q_gain,
        grad_k_gain,
    ) = finish(
        grad_gate,
        grad_up,
        grad_w_qkv,
        grad_out,
        grad_down,
        grad_hidden,
        output_0,
        output_1,
        (w_gate, w_up, w_query, key_weight, value_weight),
        [g[None, :] for g in (attn_gain, mlp_gain)],
        small,
    )
    return (
        output.reshape(hidden.shape),
        grad_hidden.reshape(hidden.shape),
        grad_attn_gain.reshape(gain_rows),
        grad_query,
        grad_key,
        grad_value,
        grad_out,
        grad_q_gain[0],
        grad_k_gain[0],
        grad_mlp_gain.reshape(gain_rows),
        grad_gate,
        grad_up,
        grad_down,
    )


def solution(mesh):
    n_dp, n_blk, n_uly = (mesh.shape[a] for a in EVERY)
    aligned = (n_dp, n_uly) == (2, 4) and KEY_VALUE_HEADS % (n_dp * n_blk) == 0
    in_specs = (
        TOKENS,
        P(),
        P(EVERY),
        P(EVERY, None),
        P(EVERY, None),
        P(EVERY, None),
        P(EVERY, None),
        P(),
        P(),
        P(EVERY),
        P(EVERY, None),
        P(EVERY, None),
        P(EVERY, None),
        TOKENS,
    )
    out_specs = (
        TOKENS,
        TOKENS,
        P(EVERY),
        P(EVERY, None),
        P(EVERY, None),
        P(EVERY, None),
        P(EVERY, None),
        P(),
        P(),
        P(EVERY),
        P(EVERY, None),
        P(EVERY, None),
        P(EVERY, None),
    )
    return jax.shard_map(
        shards if aligned else shards_general,
        mesh=mesh, in_specs=in_specs, out_specs=out_specs, check_vma=False)
```
